32 devices in a mesh: dp: 8 (over z, core), fsdp: 4 (over y, x).
Axes of the slice: x: 2, y: 2, z: 4, core: 2. Of those that a mesh axis runs over, the one named last changes fastest.
Arguments:
- tokens: bfloat16 [16, 64, 16, 1152], P('dp', 'fsdp'), may hold values from -6 to 6
- conditioning: float32 [16, 1152], P('dp'), may hold values from -6 to 6
- frame_counts: int32 [16], P('dp'), may hold values from 8 to 16
- cotangent: bfloat16 [16, 64, 16, 1152], P('dp', 'fsdp'), may hold values from -6 to 6
- weights: float32 [18, 1152, 1152], P(None, 'dp', 'fsdp')
- biases: float32 [16128], P(('dp', 'fsdp')), may hold values from -1.2 to 1.2
- momentum: float32 [18, 1152, 1152], P(None, 'dp', 'fsdp'), may hold values from -0.17677669 to 0.17677669
- left_stats: float32 [18, 1152, 1152], P(None, 'dp', 'fsdp'), as said below
- right_stats: float32 [18, 1152, 1152], P(None, 'dp', 'fsdp'), as said below
- left_roots: float32 [18, 1152, 1152], P(None, 'dp', 'fsdp'), as said below
- right_roots: float32 [18, 1152, 1152], P(None, 'dp', 'fsdp'), as said below
- bias_moment: float32 [16128], P(('dp', 'fsdp')), may hold values from -3 to 3
- bias_second: float32 [16128], P(('dp', 'fsdp')), may hold values from 4096 to 16384
Outputs:
- block_out: bfloat16 [16, 64, 16, 1152], P('dp', 'fsdp')
- input_grad: bfloat16 [16, 64, 16, 1152], P('dp', 'fsdp')
- left_new: float32 [18, 1152, 1152], P(None, 'dp', 'fsdp')
- right_new: float32 [18, 1152, 1152], P(None, 'dp', 'fsdp')
- momentum_new: float32 [18, 1152, 1152], P(None, 'dp', 'fsdp')
- weights_new: float32 [18, 1152, 1152], P(None, 'dp', 'fsdp')
- weights_copy: bfloat16 [18, 1152, 1152], P(None, 'dp', 'fsdp')
- bias_moment_new: float32 [16128], P(('dp', 'fsdp'))
- bias_second_new: float32 [16128], P(('dp', 'fsdp'))
- biases_new: float32 [16128], P(('dp', 'fsdp'))
The draws below stay inside these ranges and needn't reach their ends.
Inputs may be any that keep to these rules, and one draw needn't show every extreme that they name: `left_stats`: symmetric, with a dominant positive diagonal. `right_stats`: symmetric, with a dominant positive diagonal. `left_roots`: symmetric, with a dominant positive diagonal. `right_roots`: symmetric, with a dominant positive diagonal.
All inputs are finite; a program needn't handle non-finite values.
Results may differ from the reference program's by a relative error of at most 0.02.
Values may be sent and summed in bfloat16 or wider, within the bound.
No kernel may reach another device: no remote copies, remote signals or barrier semaphores. Data moves between devices by JAX's collectives and lax.ppermute only.
A program may use at most 320 MiB of HBM per device.

```python
import math
import jax
import jax.numpy as jnp
from jax import lax

D = 1152
HEADS = 16
HEAD_DIM = 72
FF = 4608
FRAMES = 16
BLOCKS = 18
CLIPS = 16
POSITIONS = 64
TOKENS = 16384
BIAS_LEN = 16128


def symmetric(key, level):
    first, second = jax.random.split(key)
    diagonal = level * jnp.exp(jax.random.uniform(first, (BLOCKS, D), jnp.float32, 0.0, jnp.log(4.0)))
    noise = jax.random.normal(second, (BLOCKS, D, D), jnp.float32)
    noise = (noise + jnp.swapaxes(noise, 1, 2)) * 0.5 ** 0.5
    identity_mask = (jnp.arange(D)[:, None] == jnp.arange(D)[None, :]).astype(jnp.float32)
    return noise * (0.2 * level * D ** (-0.5)) * (1.0 - identity_mask) + identity_mask * diagonal[:, None, :]


def draw_weights(key, part):
    key = jax.random.fold_in(key, 11)
    values = jax.random.normal(key, (BLOCKS, D, D), jnp.float32)
    block_ids = jnp.arange(BLOCKS)
    scale = jnp.where(block_ids == 9, (FRAMES * 0.75 / D) ** 0.5, D ** (-0.5))
    scale = jnp.where(block_ids >= 14, (1.0 * FF) ** (-0.5), scale)
    return jnp.clip(values, -6.0, 6.0) * scale[:, None, None]


def draw_left_stats(key, part):
    key = jax.random.fold_in(key, 21)
    return symmetric(key, D * TOKENS * 0.25)


def draw_right_stats(key, part):
    key = jax.random.fold_in(key, 31)
    return symmetric(key, D * TOKENS * 0.25)


def draw_left_roots(key, part):
    key = jax.random.fold_in(key, 41)
    return symmetric(key, (D * TOKENS * 0.25) ** (-0.25))


def draw_right_roots(key, part):
    key = jax.random.fold_in(key, 51)
    return symmetric(key, (D * TOKENS * 0.25) ** (-0.25))


def set_ends(entries, stream_key, least, high):
    dims = entries.shape
    index_at = [jax.random.randint(jax.random.fold_in(stream_key, axis), (), 0, dims[axis]) for axis in range(len(dims))]
    entries = entries.at[tuple(index_at)].set(least)
    longest = dims.index(max(dims))
    index_at[longest] = (index_at[longest] + 1) % dims[longest]
    return entries.at[tuple(index_at)].set(high)


def block_levels(stream_key, shape, cuts, least, top_value):
    loudness = 1.0
    for axis_at, parts in cuts:
        steps = jax.random.uniform(jax.random.fold_in(jax.random.fold_in(stream_key, 6), axis_at), (parts,), jnp.float32, least / len(cuts), top_value / len(cuts))
        loudness = loudness * jnp.repeat(jnp.exp(steps), shape[axis_at] // parts).reshape((-1,) + (1,) * (len(shape) - 1 - axis_at))
    return loudness


def scatter_about(rng, extent, spread, most, pieces=(), kind=jnp.bfloat16):
    drawn = spread * jax.random.normal(rng, extent, jnp.float32)
    if pieces:
        drawn = drawn * block_levels(rng, extent, pieces, -0.22, 0.18)
    return jnp.clip(drawn, -most, most).astype(kind)


def setup_inputs(seed: int = 0) -> dict:
    splits = jax.random.split(jax.random.key(seed), 14)
    tokens = scatter_about(splits[0], (CLIPS, POSITIONS, FRAMES, D), 1.0, 6.0, ((0, 8), (1, 4)))
    conditioning = scatter_about(splits[1], (CLIPS, D), 1.0, 6.0, ((0, 8),), jnp.float32)
    frame_counts = set_ends(jax.random.randint(splits[2], (CLIPS,), 8, 17), jax.random.fold_in(splits[2], 1), 8, 16).astype(jnp.int32)
    cotangent = scatter_about(splits[3], (CLIPS, POSITIONS, FRAMES, D), 1.0, 6.0, ((0, 8), (1, 4)))
    weights = draw_weights(jax.random.fold_in(splits[13], 71), 0)
    biases = scatter_about(splits[5], (BIAS_LEN,), 0.2, 1.2, ((0, 32),), jnp.float32)
    momentum = scatter_about(splits[6], (BLOCKS, D, D), (D ** -0.5), 0.17677669, ((1, 8), (2, 4)), jnp.float32)
    left_stats = draw_left_stats(jax.random.fold_in(splits[13], 71), 0)
    right_stats = draw_right_stats(jax.random.fold_in(splits[13], 71), 0)
    left_roots = draw_left_roots(jax.random.fold_in(splits[13], 71), 0)
    right_roots = draw_right_roots(jax.random.fold_in(splits[13], 71), 0)
    bias_moment = scatter_about(splits[11], (BIAS_LEN,), 0.5, 3.0, ((0, 32),), jnp.float32)
    bias_second = jnp.clip(jnp.exp(math.log(16384.0) - 1.3862944 * jax.random.uniform(splits[12], (BIAS_LEN,), jnp.float32) ** block_levels(splits[12], (BIAS_LEN,), ((0, 32),), -0.2, 0.2)), 4096.0, 16384.0)
    return dict(tokens=tokens, conditioning=conditioning, frame_counts=frame_counts, cotangent=cotangent, weights=weights, biases=biases, momentum=momentum, left_stats=left_stats, right_stats=right_stats, left_roots=left_roots, right_roots=right_roots, bias_moment=bias_moment, bias_second=bias_second)


@jax.custom_vjp
def low(v):
    return lax.optimization_barrier(v.astype(jnp.bfloat16)).astype(jnp.float32)

@jax.custom_vjp
def low_back(v):
    return v

def low_keep(v):
    return (low(v), None)

def low_pass(kept, grad):
    return (grad,)

def back_keep(v):
    return (v, None)

def back_low(kept, grad):
    return (low(grad),)
low.defvjp(low_keep, low_pass)
low_back.defvjp(back_keep, back_low)
precise = lax.Precision.HIGHEST
norm_epsilon = 1e-06
masked_score = -1e+30
stat_decay = 0.5
moment_decay = 0.9
weight_rate = 0.7
bias_rate = 0.1
diag_epsilon = 1e-08

def layer_norm(values):
    centered = values - lax.optimization_barrier(jnp.mean(values, axis=-1, keepdims=True))
    variance = lax.optimization_barrier(jnp.mean(centered * centered, axis=-1, keepdims=True))
    return centered * lax.rsqrt(variance + norm_epsilon)

def modulate(values, shift, scale):
    return layer_norm(values) * (1.0 + scale) + shift

def clip_forward(weight_all, bias_all, clip_tokens, clip_cond, keep):
    w_low = low(weight_all)
    b_low = low(bias_all)
    cond_low = low(jax.nn.silu(clip_cond))
    mods = jnp.einsum('d,jde->je', cond_low, w_low[0:6], precision=precise) + b_low[0:6 * D].reshape(6, D)
    attn_in = low(modulate(clip_tokens, mods[0], mods[1]))
    qkv_bias = jnp.stack([b_low[6 * D:7 * D], jnp.zeros((D,), jnp.float32), b_low[7 * D:8 * D]])
    qkv = low_back(jnp.einsum('pfd,jde->pfje', attn_in, w_low[6:9], precision=precise) + qkv_bias)
    query_rows = qkv[:, :, 0].reshape(POSITIONS, FRAMES, HEADS, HEAD_DIM)
    key_rows = qkv[:, :, 1].reshape(POSITIONS, FRAMES, HEADS, HEAD_DIM)
    value_rows = qkv[:, :, 2].reshape(POSITIONS, FRAMES, HEADS, HEAD_DIM)
    scores = jnp.einsum('pfhd,pghd->phfg', query_rows, key_rows, precision=precise) * HEAD_DIM ** (-0.5)
    scores = jnp.where(keep[None, None, None, :], scores, masked_score)
    probs = jax.nn.softmax(scores, axis=-1)
    mixed = jnp.einsum('phfg,pghd->pfhd', probs, value_rows, precision=precise).reshape(POSITIONS, FRAMES, D)
    proj = low_back(jnp.einsum('pfd,de->pfe', low(mixed), w_low[9], precision=precise) + b_low[8 * D:9 * D])
    valid = keep.astype(jnp.float32)[:, None]
    resid = clip_tokens + valid * mods[2] * proj
    mlp_in = low(modulate(resid, mods[3], mods[4]))
    pre = low_back(jnp.einsum('pfd,jde->pfje', mlp_in, w_low[10:14], precision=precise) + b_low[9 * D:13 * D].reshape(4, D))
    hidden = low(jax.nn.gelu(pre, approximate=True))
    branch = low_back(jnp.einsum('pfjd,jde->pfe', hidden, w_low[14:18], precision=precise) + b_low[13 * D:14 * D])
    return resid + valid * mods[5] * branch

def reference(tokens, conditioning, frame_counts, cotangent, weights, biases, momentum, left_stats, right_stats, left_roots, right_roots, bias_moment, bias_second):
    frame_ids = jnp.arange(FRAMES, dtype=jnp.int32)

    def one_clip(carry, inputs):
        grad_w, grad_b = carry
        clip_tokens, clip_cond, clip_count, clip_cot = inputs
        keep = frame_ids < clip_count

        def run(weight_all, bias_all, token_all):
            return clip_forward(weight_all, bias_all, token_all, clip_cond, keep)
        result, pull = jax.vjp(run, weights, biases, clip_tokens.astype(jnp.float32))
        step_w, step_b, step_x = pull(clip_cot.astype(jnp.float32))
        return ((grad_w + step_w, grad_b + step_b), (result.astype(jnp.bfloat16), step_x.astype(jnp.bfloat16)))
    start = (jnp.zeros_like(weights), jnp.zeros_like(biases))
    (grad_w, grad_b), (block_out, input_grad) = lax.scan(one_clip, start, (tokens, conditioning, frame_counts, cotangent))
    left_new = stat_decay * left_stats + (1.0 - stat_decay) * jnp.einsum('bik,bjk->bij', grad_w, grad_w, precision=precise)
    right_new = stat_decay * right_stats + (1.0 - stat_decay) * jnp.einsum('bki,bkj->bij', grad_w, grad_w, precision=precise)
    left_side = jnp.einsum('bij,bjk->bik', left_roots, grad_w, precision=precise)
    precond = jnp.einsum('bij,bjk->bik', left_side, right_roots, precision=precise)
    momentum_new = moment_decay * momentum + precond
    weights_new = weights - weight_rate * momentum_new
    weights_copy = weights_new.astype(jnp.bfloat16)
    bias_second_new = stat_decay * bias_second + (1.0 - stat_decay) * grad_b * grad_b
    bias_moment_new = moment_decay * bias_moment + grad_b * lax.rsqrt(bias_second_new + diag_epsilon)
    biases_new = biases - bias_rate * bias_moment_new
    return (block_out, input_grad, left_new, right_new, momentum_new, weights_new, weights_copy, bias_moment_new, bias_second_new, biases_new)
```

```python
import jax
import jax.numpy as jnp
from jax import lax
from jax.sharding import PartitionSpec as P

HEADS = 16


precise = lax.Precision.HIGHEST
norm_epsilon = 1e-06
masked_score = -1e30
stat_decay = 0.5
moment_decay = 0.9
weight_rate = 0.7
bias_rate = 0.1
diag_epsilon = 1e-08


def layer_norm(values):
    centered = values - jnp.mean(values, axis=-1, keepdims=True)
    variance = jnp.mean(centered * centered, axis=-1, keepdims=True)
    return centered * lax.rsqrt(variance + norm_epsilon)


def modulate(values, shift, scale):
    return layer_norm(values) * (1.0 + scale) + shift


def gelu_tanh(values_in):
    return jax.nn.gelu(values_in, approximate=True)


def attention_scores(query_rows, key_rows, key_keep):
    scale = query_rows.shape[-1] ** (-0.5)
    scores = jnp.einsum("sfhd,sghd->shfg", query_rows, key_rows, precision=precise) * scale
    return jnp.where(key_keep[:, None, None, :], scores, masked_score)


def attention_forward(query_rows, key_rows, value_rows, key_keep):
    scores = attention_scores(query_rows, key_rows, key_keep)
    highest = jnp.max(scores, axis=-1, keepdims=True)
    expons = jnp.exp(scores - highest)
    totals = jnp.sum(expons, axis=-1, keepdims=True)
    mixed = jnp.einsum("shfg,sghd->sfhd", expons / totals, value_rows, precision=precise)
    return (mixed, highest + jnp.log(totals))


def attention_backward(query_rows, key_rows, value_rows, key_keep, log_totals, grad_mixed):
    scale = query_rows.shape[-1] ** (-0.5)
    probs = jnp.exp(attention_scores(query_rows, key_rows, key_keep) - log_totals)
    grad_probs = jnp.einsum("sfhd,sghd->shfg", grad_mixed, value_rows, precision=precise)
    grad_values = jnp.einsum("shfg,sfhd->sghd", probs, grad_mixed, precision=precise)
    inner = jnp.sum(grad_probs * probs, axis=-1, keepdims=True)
    grad_scores = probs * (grad_probs - inner) * scale
    grad_query = jnp.einsum("shfg,sghd->sfhd", grad_scores, key_rows, precision=precise)
    grad_keys = jnp.einsum("shfg,sfhd->sghd", grad_scores, query_rows, precision=precise)
    return (grad_query, grad_keys, grad_values)


def narrow(array):
    return array.astype(jnp.bfloat16)


def wide(array):
    return array.astype(jnp.float32)


def packed(arrays, tile):
    flat = jnp.concatenate([array.reshape(-1) for array in arrays])
    return jnp.pad(flat, (0, -flat.shape[0] % (tile * 128))).reshape(-1, 128)


def own_rows(parts, group):
    ranks = lax.axis_size("fsdp")
    shares = ranks // group
    count, row_part, col_part = parts.shape
    chunk = row_part // shares
    split = parts.reshape(count // group, group, shares, chunk, col_part)
    split = split.transpose(1, 2, 0, 3, 4).reshape(ranks, count // group, chunk, col_part)
    moved = lax.all_to_all(split, "fsdp", 0, 0, tiled=True)
    return moved.transpose(1, 2, 0, 3).reshape(count // group, chunk, ranks * col_part)


def shard_rows(rows, group):
    ranks = lax.axis_size("fsdp")
    shares = ranks // group
    count, chunk, total = rows.shape
    col_part = total // ranks
    split = rows.reshape(count, chunk, ranks, col_part).transpose(2, 0, 1, 3)
    moved = lax.all_to_all(split, "fsdp", 0, 0, tiled=True)
    moved = moved.reshape(group, shares, count, chunk, col_part).transpose(2, 0, 1, 3, 4)
    return moved.reshape(count * group, shares * chunk, col_part)


def gather_blocks(rows, group):
    ranks, dp_count = lax.axis_size("fsdp"), lax.axis_size("dp")
    shares = ranks // group
    chunk, total = rows.shape
    all_rows = lax.all_gather(rows, ("fsdp", "dp"), axis=0, tiled=True)
    if shares > 1:
        all_rows = all_rows.reshape(group, shares, dp_count, chunk, total).transpose(0, 2, 1, 3, 4)
    return all_rows.reshape(group, total, total)


def gather_own(rows, group):
    ranks = lax.axis_size("fsdp")
    shares = ranks // group
    chunk, total = rows.shape
    if shares > 1:
        sets = [[share + shares * block for share in range(shares)] for block in range(group)]
        rows = lax.all_gather(rows, "fsdp", axis=0, tiled=True, axis_index_groups=sets)
    return lax.all_gather(rows, "dp", axis=0, tiled=True)


def scatter_blocks(blocks, group):
    ranks, dp_count = lax.axis_size("fsdp"), lax.axis_size("dp")
    shares = ranks // group
    count, total, last = blocks.shape
    if shares > 1:
        chunk = total // (dp_count * shares)
        blocks = blocks.reshape(group, dp_count, shares, chunk, last).transpose(0, 2, 1, 3, 4)
    return lax.psum_scatter(
        blocks.reshape(count * total, last), ("fsdp", "dp"), scatter_dimension=0, tiled=True
    )


def fast_dot(subscripts, left, right):
    return jnp.einsum(subscripts, left, right, preferred_element_type=jnp.float32)


def owned_step(grad_rows, left_root, right_root, group):
    chunk, total = grad_rows.shape
    whole = gather_own(grad_rows, group)
    shares = lax.axis_size("fsdp") // group
    first = lax.axis_index("dp") * (chunk * shares) + lax.axis_index("fsdp") % shares * chunk
    own_columns = lax.dynamic_slice_in_dim(whole, first, chunk, 1)
    outer = fast_dot("rk,jk->rj", grad_rows, whole)
    inner = fast_dot("kr,kj->rj", own_columns, whole)
    side = fast_dot("rk,kj->rj", left_root, whole)
    side_high = narrow(side)
    side_low = narrow(side - wide(side_high))
    precond = fast_dot("rk,kj->rj", side_high, right_root) + fast_dot(
        "rk,kj->rj", side_low, right_root
    )
    return narrow(jnp.stack([precond, outer, inner]))


def per_device(
    tokens,
    conditioning,
    frame_counts,
    cotangent,
    weights,
    biases,
    momentum,
    left_stats,
    right_stats,
    left_roots,
    right_roots,
    bias_moment,
    bias_second,
):
    group = 4
    mod_count = 6
    clip_count, pos_count, frame_count, width = tokens.shape
    row_count = pos_count * frame_count
    token_count = clip_count * row_count
    seq_count = clip_count * pos_count
    head_dim = width // HEADS
    block_count, row_part, col_part = weights.shape
    dp_count, ranks = lax.axis_size("dp"), lax.axis_size("fsdp")
    dp_at, rank_at = lax.axis_index("dp"), lax.axis_index("fsdp")
    all_clips = clip_count * dp_count
    bias_part = biases.shape[0]
    stream = tokens.astype(jnp.float32).reshape(clip_count, row_count, width)
    frame_ids = lax.broadcasted_iota(jnp.int32, (clip_count, frame_count), 1)
    keep = frame_ids < frame_counts[:, None]
    keep_all = jnp.broadcast_to(keep[:, None, :], (clip_count, pos_count, frame_count))
    key_keep = keep_all.reshape(seq_count, frame_count)
    valid = keep_all.astype(jnp.float32).reshape(clip_count, row_count, 1)

    weight_rows = own_rows(narrow(weights[mod_count:]), group)
    attn_w = gather_blocks(weight_rows[0], group)
    one_w = gather_blocks(weight_rows[1], group)
    two_w = gather_blocks(weight_rows[2], group)

    cond_low = jax.nn.silu(conditioning).astype(jnp.bfloat16)
    first_parts = lax.all_gather(
        packed([cond_low, narrow(biases)], 16), "dp", axis=0, tiled=True
    ).reshape(dp_count, -1)
    cond_all = first_parts[:, : clip_count * width].reshape(all_clips, width)
    bias_rows = wide(first_parts[:, clip_count * width : clip_count * width + bias_part])
    cond_rows = lax.dynamic_slice_in_dim(cond_all, dp_at * row_part, row_part, 1)
    cond_cols = wide(lax.dynamic_slice_in_dim(cond_all, rank_at * col_part, col_part, 1))
    mod_parts = fast_dot("cr,jre->cje", cond_rows, narrow(weights[:mod_count]))
    mod_parts = lax.all_to_all(mod_parts, "dp", 0, 0, tiled=True)
    mod_cols = jnp.sum(mod_parts.reshape(dp_count, clip_count, mod_count, col_part), axis=0)
    left_cond = jnp.einsum("jrk,ck->jrc", left_roots[:mod_count], cond_cols, precision=precise)
    mod_size, bias_size = mod_cols.size, dp_count * bias_part
    second_parts = lax.all_gather(
        packed([mod_cols, bias_rows, left_cond], 8), "fsdp", axis=0, tiled=True
    ).reshape(ranks, -1)
    mods = second_parts[:, :mod_size].reshape(ranks, clip_count, mod_count, col_part)
    mods = mods.transpose(1, 2, 0, 3).reshape(clip_count, mod_count, width)
    bias_all = second_parts[:, mod_size : mod_size + bias_size].reshape(ranks, dp_count, bias_part)
    bias_all = bias_all.transpose(1, 0, 2).reshape(-1)
    left_size = mod_size + bias_size + left_cond.size
    left_cond = jnp.sum(second_parts[:, mod_size + bias_size : left_size], axis=0)
    left_cond = left_cond.reshape(mod_count, row_part, all_clips)
    mods = mods + bias_all[0 : 6 * width].reshape(6, width)
    shift_one = mods[:, 0:1]
    scale_one = mods[:, 1:2]
    gate_one = mods[:, 2:3]
    shift_two = mods[:, 3:4]
    scale_two = mods[:, 4:5]
    gate_two = mods[:, 5:6]

    attn_in = (
        modulate(stream, shift_one, scale_one).astype(jnp.bfloat16).reshape(token_count, width)
    )
    qkv_bias = jnp.stack(
        [
            bias_all[6 * width : 7 * width],
            jnp.zeros((width,), jnp.float32),
            bias_all[7 * width : 8 * width],
        ]
    )
    qkv = fast_dot("td,jde->tje", attn_in, attn_w[0:3]) + qkv_bias
    query_rows = qkv[:, 0].reshape(seq_count, frame_count, HEADS, head_dim)
    key_rows = qkv[:, 1].reshape(seq_count, frame_count, HEADS, head_dim)
    value_rows = qkv[:, 2].reshape(seq_count, frame_count, HEADS, head_dim)
    mixed, log_totals = attention_forward(query_rows, key_rows, value_rows, key_keep)
    mixed_low = mixed.reshape(token_count, width).astype(jnp.bfloat16)
    proj = fast_dot("td,de->te", mixed_low, attn_w[3]) + bias_all[8 * width : 9 * width]
    proj_rows = proj.reshape(clip_count, row_count, width)
    resid = stream + valid * gate_one * proj_rows
    mlp_in = modulate(resid, shift_two, scale_two).astype(jnp.bfloat16).reshape(token_count, width)
    pre = fast_dot("td,jde->jte", mlp_in, one_w) + bias_all[9 * width : 13 * width].reshape(
        4, 1, width
    )
    hidden = gelu_tanh(pre).astype(jnp.bfloat16)
    grad_out = cotangent.astype(jnp.float32).reshape(clip_count, row_count, width)
    d_branch = (grad_out * valid * gate_two).astype(jnp.bfloat16).reshape(token_count, width)
    grad_two = narrow(fast_dot("jtd,te->jde", hidden, d_branch))
    rows_two = scatter_blocks(grad_two, group)
    branch = fast_dot("jtd,jde->te", hidden, two_w) + bias_all[13 * width : 14 * width]
    branch_rows = branch.reshape(clip_count, row_count, width)
    block_out = (resid + valid * gate_two * branch_rows).astype(jnp.bfloat16).reshape(tokens.shape)
    d_gate_two = jnp.sum(grad_out * valid * branch_rows, axis=1, keepdims=True)
    grad_b_two = jnp.sum(d_branch.astype(jnp.float32), axis=0)
    d_hidden = fast_dot("te,jde->jtd", d_branch, two_w)
    gelu_value, gelu_pull = jax.vjp(gelu_tanh, pre)
    d_pre = gelu_pull(d_hidden)[0].astype(jnp.bfloat16)
    grad_one = narrow(fast_dot("td,jte->jde", mlp_in, d_pre))
    rows_one = scatter_blocks(grad_one, group)
    grad_b_one = jnp.sum(d_pre.astype(jnp.float32), axis=1).reshape(4 * width)
    d_mlp_in = fast_dot("jte,jde->td", d_pre, one_w).reshape(clip_count, row_count, width)
    mod_value, mod_pull = jax.vjp(modulate, resid, shift_two, scale_two)
    d_resid_norm, d_shift_two, d_scale_two = mod_pull(d_mlp_in)
    d_resid = grad_out + d_resid_norm
    d_proj = (d_resid * valid * gate_one).astype(jnp.bfloat16).reshape(token_count, width)
    d_gate_one = jnp.sum(d_resid * valid * proj_rows, axis=1, keepdims=True)
    grad_b_out = jnp.sum(d_proj.astype(jnp.float32), axis=0)
    grad_out_w = narrow(fast_dot("td,te->de", mixed_low, d_proj))
    d_mixed = fast_dot("te,de->td", d_proj, attn_w[3]).reshape(
        seq_count, frame_count, HEADS, head_dim
    )
    d_query, d_keys, d_values = attention_backward(
        query_rows, key_rows, value_rows, key_keep, log_totals, d_mixed
    )
    d_qkv = jnp.stack(
        [
            d_query.reshape(token_count, width),
            d_keys.reshape(token_count, width),
            d_values.reshape(token_count, width),
        ],
        axis=0,
    ).astype(jnp.bfloat16)
    qkv_sums = jnp.sum(d_qkv.astype(jnp.float32), axis=1)
    grad_qkv = narrow(fast_dot("td,jte->jde", attn_in, d_qkv))
    rows_attn = scatter_blocks(jnp.concatenate([grad_qkv, grad_out_w[None]], axis=0), group)
    d_attn_in = fast_dot("jte,jde->td", d_qkv, attn_w[0:3]).reshape(clip_count, row_count, width)
    first_value, first_pull = jax.vjp(modulate, stream, shift_one, scale_one)
    d_stream_norm, d_shift_one, d_scale_one = first_pull(d_attn_in)
    input_grad = (d_resid + d_stream_norm).astype(jnp.bfloat16).reshape(tokens.shape)

    d_mods = jnp.concatenate(
        [d_shift_one, d_scale_one, d_gate_one, d_shift_two, d_scale_two, d_gate_two], axis=1
    )
    grad_b_ada = jnp.sum(d_mods, axis=0).reshape(6 * width)
    grad_bias = jnp.concatenate(
        [grad_b_ada, qkv_sums[0], qkv_sums[2], grad_b_out, grad_b_one, grad_b_two]
    )
    to_ranks = jnp.concatenate(
        [
            d_mods.reshape(clip_count, mod_count, ranks, col_part)
            .transpose(2, 0, 1, 3)
            .reshape(ranks, mod_size),
            grad_bias.reshape(dp_count, ranks, bias_part)
            .transpose(1, 0, 2)
            .reshape(ranks, bias_size),
        ],
        axis=1,
    )
    rank_sums = jnp.sum(lax.all_to_all(to_ranks, "fsdp", 0, 0, tiled=True), axis=0)
    to_rows = jnp.concatenate(
        [
            jnp.broadcast_to(rank_sums[None, :mod_size], (dp_count, mod_size)),
            rank_sums[mod_size:].reshape(dp_count, bias_part),
        ],
        axis=1,
    )
    from_rows = lax.all_to_all(to_rows, "dp", 0, 0, tiled=True)
    bias_grad = jnp.sum(from_rows[:, mod_size:], axis=0)
    mod_grad_cols = from_rows[:, :mod_size].reshape(all_clips, mod_count, col_part)
    mod_grad = lax.all_gather(mod_grad_cols, "fsdp", axis=2, tiled=True)

    mod_grad_rows = lax.dynamic_slice_in_dim(mod_grad, dp_at * row_part, row_part, 2)
    right_parts = jnp.einsum(
        "cjk,jke->cje", mod_grad_rows, right_roots[:mod_count], precision=precise
    )
    mod_right = jnp.sum(lax.all_gather(right_parts, "dp", axis=0), axis=0)
    ada_pre = jnp.einsum("jrc,cje->jre", left_cond, mod_right, precision=precise)
    cond_wide = wide(cond_all)
    cond_row_wide = wide(cond_rows)
    mod_gram = jnp.einsum("cjk,bjk->jcb", mod_grad, mod_grad, precision=precise)
    cond_gram = jnp.einsum("ck,bk->cb", cond_wide, cond_wide, precision=precise)
    mod_side = jnp.einsum("jcb,be->jce", mod_gram, cond_cols, precision=precise)
    ada_left = jnp.einsum("cr,jce->jre", cond_row_wide, mod_side, precision=precise)
    cond_side = jnp.einsum("cb,bje->jce", cond_gram, mod_grad_cols, precision=precise)
    ada_right = jnp.einsum("cjr,jce->jre", mod_grad_rows, cond_side, precision=precise)

    roots = own_rows(
        narrow(jnp.concatenate([left_roots[mod_count:], right_roots[mod_count:]])), group
    )
    right_wholes = [gather_own(roots[3 + piece], group) for piece in range(3)]
    back_two = shard_rows(owned_step(rows_two, roots[2], right_wholes[2], group), group)
    back_one = shard_rows(owned_step(rows_one, roots[1], right_wholes[1], group), group)
    back_attn = shard_rows(owned_step(rows_attn, roots[0], right_wholes[0], group), group)

    def joined(at, ada):
        span = slice(at * group, (at + 1) * group)
        return jnp.concatenate(
            [ada, wide(back_attn[span]), wide(back_one[span]), wide(back_two[span])]
        )

    precond = joined(0, ada_pre)
    left_new = stat_decay * left_stats + (1.0 - stat_decay) * joined(1, ada_left)
    right_new = stat_decay * right_stats + (1.0 - stat_decay) * joined(2, ada_right)
    momentum_new = moment_decay * momentum + precond
    weights_new = weights - weight_rate * momentum_new
    weights_copy = weights_new.astype(jnp.bfloat16)
    bias_second_new = stat_decay * bias_second + (1.0 - stat_decay) * bias_grad * bias_grad
    bias_moment_new = moment_decay * bias_moment + bias_grad * lax.rsqrt(
        bias_second_new + diag_epsilon
    )
    biases_new = biases - bias_rate * bias_moment_new
    return (
        block_out,
        input_grad,
        left_new,
        right_new,
        momentum_new,
        weights_new,
        weights_copy,
        bias_moment_new,
        bias_second_new,
        biases_new,
    )


def solution(mesh):
    placed = (
        P("dp", "fsdp", None, None),
        P("dp", None),
        P("dp"),
        P("dp", "fsdp", None, None),
        P(None, "dp", "fsdp"),
        P(("dp", "fsdp")),
        P(None, "dp", "fsdp"),
        P(None, "dp", "fsdp"),
        P(None, "dp", "fsdp"),
        P(None, "dp", "fsdp"),
        P(None, "dp", "fsdp"),
        P(("dp", "fsdp")),
        P(("dp", "fsdp")),
    )
    return jax.shard_map(
        per_device,
        mesh=mesh,
        in_specs=placed,
        out_specs=(
            P("dp", "fsdp", None, None),
            P("dp", "fsdp", None, None),
            P(None, "dp", "fsdp"),
            P(None, "dp", "fsdp"),
            P(None, "dp", "fsdp"),
            P(None, "dp", "fsdp"),
            P(None, "dp", "fsdp"),
            P(("dp", "fsdp")),
            P(("dp", "fsdp")),
            P(("dp", "fsdp")),
        ),
        check_vma=False,
    )
```

```python
import jax
import jax.numpy as jnp
from jax import lax
from jax.sharding import PartitionSpec as P

HEADS = 16


precise = lax.Precision.HIGHEST
norm_epsilon = 1e-06
masked_score = -1e30
stat_decay = 0.5
moment_decay = 0.9
weight_rate = 0.7
bias_rate = 0.1
diag_epsilon = 1e-08


def layer_norm(values):
    centered = values - jnp.mean(values, axis=-1, keepdims=True)
    variance = jnp.mean(centered * centered, axis=-1, keepdims=True)
    return centered * lax.rsqrt(variance + norm_epsilon)


def modulate(values, shift, scale):
    return layer_norm(values) * (1.0 + scale) + shift


def gelu_tanh(values_in):
    return jax.nn.gelu(values_in, approximate=True)


def attention_scores(query_rows, key_rows, key_keep):
    scale = query_rows.shape[-1] ** (-0.5)
    scores = jnp.einsum("sfhd,sghd->shfg", query_rows, key_rows, precision=precise) * scale
    return jnp.where(key_keep[:, None, None, :], scores, masked_score)


def attention_forward(query_rows, key_rows, value_rows, key_keep):
    scores = attention_scores(query_rows, key_rows, key_keep)
    highest = jnp.max(scores, axis=-1, keepdims=True)
    expons = jnp.exp(scores - highest)
    totals = jnp.sum(expons, axis=-1, keepdims=True)
    mixed = jnp.einsum("shfg,sghd->sfhd", expons / totals, value_rows, precision=precise)
    return (mixed, highest + jnp.log(totals))


def attention_backward(query_rows, key_rows, value_rows, key_keep, log_totals, grad_mixed):
    scale = query_rows.shape[-1] ** (-0.5)
    probs = jnp.exp(attention_scores(query_rows, key_rows, key_keep) - log_totals)
    grad_probs = jnp.einsum("sfhd,sghd->shfg", grad_mixed, value_rows, precision=precise)
    grad_values = jnp.einsum("shfg,sfhd->sghd", probs, grad_mixed, precision=precise)
    inner = jnp.sum(grad_probs * probs, axis=-1, keepdims=True)
    grad_scores = probs * (grad_probs - inner) * scale
    grad_query = jnp.einsum("shfg,sghd->sfhd", grad_scores, key_rows, precision=precise)
    grad_keys = jnp.einsum("shfg,sfhd->sghd", grad_scores, query_rows, precision=precise)
    return (grad_query, grad_keys, grad_values)


def narrow(array):
    return array.astype(jnp.bfloat16)


def wide(array):
    return array.astype(jnp.float32)


def packed(arrays, tile):
    flat = jnp.concatenate([array.reshape(-1) for array in arrays])
    return jnp.pad(flat, (0, -flat.shape[0] % (tile * 128))).reshape(-1, 128)


def core_swap(array):
    count = lax.axis_size("dp")
    return lax.ppermute(array, "dp", [(at, at ^ 1) for at in range(count)])


def chip_shift(array, step):
    count = lax.axis_size("dp")
    return lax.ppermute(array, "dp", [(at, (at + 2 * step) % count) for at in range(count)])


def rank_swap(array, bits):
    count = lax.axis_size("fsdp")
    return lax.ppermute(array, "fsdp", [(at, at ^ bits) for at in range(count)])


def entry(array, at, axis=0):
    return lax.dynamic_index_in_dim(array, at, axis, keepdims=False)


def put(array, part, *at):
    part = part.reshape((1,) * (array.ndim - part.ndim) + part.shape)
    at = at + (0,) * (array.ndim - len(at))
    return lax.dynamic_update_slice(array, part, at)


def own_rows(parts, group):
    ranks, at = lax.axis_size("fsdp"), lax.axis_index("fsdp")
    shares = ranks // group
    row_part, col_part = parts.shape[1:]
    chunk = row_part // shares
    split = parts.reshape(ranks, chunk, col_part)
    panels = [entry(split, at)]
    panels += [rank_swap(entry(split, at ^ bits), bits) for bits in range(1, ranks)]
    placed = [
        lax.select_n(at, *[panels[panel ^ index] for index in range(ranks)])
        for panel in range(ranks)
    ]
    return jnp.concatenate(placed, axis=1)


def shard_rows(rows, group):
    ranks = lax.axis_size("fsdp")
    shares = ranks // group
    count, chunk, total = rows.shape
    col_part = total // ranks
    split = rows.reshape(count, chunk, ranks, col_part).transpose(2, 0, 1, 3)
    moved = lax.all_to_all(split, "fsdp", 0, 0, tiled=True)
    moved = moved.reshape(group, shares, count, chunk, col_part).transpose(2, 0, 1, 3, 4)
    return moved.reshape(count * group, shares * chunk, col_part)


def gather_blocks(rows, group):
    ranks, dp_count = lax.axis_size("fsdp"), lax.axis_size("dp")
    shares = ranks // group
    chunk, total = rows.shape
    all_rows = lax.all_gather(rows, ("fsdp", "dp"), axis=0, tiled=True)
    if shares > 1:
        all_rows = all_rows.reshape(group, shares, dp_count, chunk, total).transpose(0, 2, 1, 3, 4)
    return all_rows.reshape(group, total, total)


def gather_pieces(rows, group):
    ranks, at = lax.axis_size("fsdp"), lax.axis_index("fsdp")
    if ranks != group:
        return gather_blocks(rows, group)
    chips = lax.axis_size("dp") // 2
    core, chip = lax.axis_index("dp") % 2, lax.axis_index("dp") // 2
    chunk, total = rows.shape
    line = put(jnp.zeros((chips, chunk, total), rows.dtype), rows, chip)
    for step in range(1, chips):
        line = put(line, chip_shift(rows, step), (chip - step) % chips)
    own = jnp.zeros((chips, 2, chunk, total), rows.dtype)
    own = put(own, line[:, None], 0, core)
    own = put(own, core_swap(line)[:, None], 0, 1 - core)
    own = own.reshape(2, total // 2, total)
    half = entry(own, core)
    found = put(jnp.zeros((ranks, 2, total // 2, total), rows.dtype), own, at)
    for bits in range(1, ranks):
        mine = rank_swap(half, bits)
        found = put(found, mine, at ^ bits, core)
        found = put(found, core_swap(mine), at ^ bits, 1 - core)
    return found.reshape(group, total, total)


def gather_own(rows, group):
    ranks = lax.axis_size("fsdp")
    shares = ranks // group
    chunk, total = rows.shape
    if shares > 1:
        sets = [[share + shares * block for share in range(shares)] for block in range(group)]
        rows = lax.all_gather(rows, "fsdp", axis=0, tiled=True, axis_index_groups=sets)
    return lax.all_gather(rows, "dp", axis=0, tiled=True)


def scatter_blocks(product, left, group):
    ranks, dp_count = lax.axis_size("fsdp"), lax.axis_size("dp")
    shares = ranks // group
    total = left.shape[-1]
    if shares > 1:
        blocks = narrow(product(left))
        chunk = total // (dp_count * shares)
        blocks = blocks.reshape(group, dp_count, shares, chunk, -1).transpose(0, 2, 1, 3, 4)
        rows = lax.psum_scatter(
            blocks.reshape(group * total, -1), ("fsdp", "dp"), scatter_dimension=0, tiled=True
        )
        return gather_own(rows, group)
    chips, half = dp_count // 2, total // 2
    chunk = half // chips
    core, chip = lax.axis_index("dp") % 2, lax.axis_index("dp") // 2
    low_bit, high_bit = lax.axis_index("fsdp") % 2, lax.axis_index("fsdp") // 2
    away = narrow(product(lax.dynamic_slice_in_dim(left, (1 - core) * half, half, left.ndim - 1)))
    here = product(lax.dynamic_slice_in_dim(left, core * half, half, left.ndim - 1))
    here = narrow(here + wide(core_swap(away)))
    here = here.reshape(2, 2, chips, chunk, -1)
    cut = chips // 2
    first, second = here[:, :, :cut], here[:, :, cut:]
    first_in = rank_swap(entry(first, 1 - low_bit, 1), 1)
    second_in = rank_swap(entry(second, 1 - high_bit, 0), 2)
    first = narrow(wide(entry(first, low_bit, 1)) + wide(first_in))
    second = narrow(wide(entry(second, high_bit, 0)) + wide(second_in))
    first_in = rank_swap(entry(first, 1 - high_bit), 2)
    second_in = rank_swap(entry(second, 1 - low_bit), 1)
    first = narrow(wide(entry(first, high_bit)) + wide(first_in))
    second = narrow(wide(entry(second, low_bit)) + wide(second_in))
    line = jnp.concatenate([first, second])
    rows = wide(entry(line, chip))
    for step in range(1, chips):
        rows = rows + wide(chip_shift(entry(line, (chip + step) % chips), step))
    found = lax.all_gather(narrow(rows), "dp", axis=0, tiled=True)
    return found.reshape(chips, 2, chunk, -1).transpose(1, 0, 2, 3).reshape(total, -1)


def fast_dot(subscripts, left, right):
    return jnp.einsum(subscripts, left, right, preferred_element_type=jnp.float32)


def owned_step(whole, left_root, right_root, group):
    chunk = left_root.shape[0]
    shares = lax.axis_size("fsdp") // group
    first = lax.axis_index("dp") * (chunk * shares) + lax.axis_index("fsdp") % shares * chunk
    grad_rows = lax.dynamic_slice_in_dim(whole, first, chunk, 0)
    own_columns = lax.dynamic_slice_in_dim(whole, first, chunk, 1)
    outer = fast_dot("rk,jk->rj", grad_rows, whole)
    inner = fast_dot("kr,kj->rj", own_columns, whole)
    side = fast_dot("rk,kj->rj", left_root, whole)
    side_high = narrow(side)
    side_low = narrow(side - wide(side_high))
    precond = fast_dot("rk,kj->rj", side_high, right_root) + fast_dot(
        "rk,kj->rj", side_low, right_root
    )
    return narrow(jnp.stack([precond, outer, inner]))


def per_device(
    tokens,
    conditioning,
    frame_counts,
    cotangent,
    weights,
    biases,
    momentum,
    left_stats,
    right_stats,
    left_roots,
    right_roots,
    bias_moment,
    bias_second,
):
    group = 4
    mod_count = 6
    clip_count, pos_count, frame_count, width = tokens.shape
    row_count = pos_count * frame_count
    token_count = clip_count * row_count
    seq_count = clip_count * pos_count
    head_dim = width // HEADS
    block_count, row_part, col_part = weights.shape
    dp_count, ranks = lax.axis_size("dp"), lax.axis_size("fsdp")
    dp_at, rank_at = lax.axis_index("dp"), lax.axis_index("fsdp")
    all_clips = clip_count * dp_count
    bias_part = biases.shape[0]
    stream = tokens.astype(jnp.float32).reshape(clip_count, row_count, width)
    frame_ids = lax.broadcasted_iota(jnp.int32, (clip_count, frame_count), 1)
    keep = frame_ids < frame_counts[:, None]
    keep_all = jnp.broadcast_to(keep[:, None, :], (clip_count, pos_count, frame_count))
    key_keep = keep_all.reshape(seq_count, frame_count)
    valid = keep_all.astype(jnp.float32).reshape(clip_count, row_count, 1)

    pieces = [slice(mod_count + group * piece, mod_count + group * (piece + 1)) for piece in range(3)]
    attn_w = gather_blocks(own_rows(narrow(weights[pieces[0]]), group), group)
    one_w = gather_pieces(own_rows(narrow(weights[pieces[1]]), group), group)
    two_w = gather_blocks(own_rows(narrow(weights[pieces[2]]), group), group)
    left_rows = [own_rows(narrow(left_roots[piece]), group) for piece in pieces]
    right_wholes = [gather_own(own_rows(narrow(right_roots[piece]), group), group) for piece in pieces]

    cond_low = jax.nn.silu(conditioning).astype(jnp.bfloat16)
    first_parts = lax.all_gather(
        packed([cond_low, narrow(biases)], 16), "dp", axis=0, tiled=True
    ).reshape(dp_count, -1)
    cond_all = first_parts[:, : clip_count * width].reshape(all_clips, width)
    bias_rows = wide(first_parts[:, clip_count * width : clip_count * width + bias_part])
    cond_rows = lax.dynamic_slice_in_dim(cond_all, dp_at * row_part, row_part, 1)
    cond_cols = wide(lax.dynamic_slice_in_dim(cond_all, rank_at * col_part, col_part, 1))
    mod_parts = fast_dot("cr,jre->cje", cond_rows, narrow(weights[:mod_count]))
    mod_parts = lax.all_to_all(mod_parts, "dp", 0, 0, tiled=True)
    mod_cols = jnp.sum(mod_parts.reshape(dp_count, clip_count, mod_count, col_part), axis=0)
    left_cond = jnp.einsum("jrk,ck->jrc", left_roots[:mod_count], cond_cols, precision=precise)
    mod_size, bias_size = mod_cols.size, dp_count * bias_part
    second_parts = lax.all_gather(
        packed([mod_cols, bias_rows, left_cond], 8), "fsdp", axis=0, tiled=True
    ).reshape(ranks, -1)
    mods = second_parts[:, :mod_size].reshape(ranks, clip_count, mod_count, col_part)
    mods = mods.transpose(1, 2, 0, 3).reshape(clip_count, mod_count, width)
    bias_all = second_parts[:, mod_size : mod_size + bias_size].reshape(ranks, dp_count, bias_part)
    bias_all = bias_all.transpose(1, 0, 2).reshape(-1)
    left_size = mod_size + bias_size + left_cond.size
    left_cond = jnp.sum(second_parts[:, mod_size + bias_size : left_size], axis=0)
    left_cond = left_cond.reshape(mod_count, row_part, all_clips)
    mods = mods + bias_all[0 : 6 * width].reshape(6, width)
    shift_one = mods[:, 0:1]
    scale_one = mods[:, 1:2]
    gate_one = mods[:, 2:3]
    shift_two = mods[:, 3:4]
    scale_two = mods[:, 4:5]
    gate_two = mods[:, 5:6]

    attn_in = (
        modulate(stream, shift_one, scale_one).astype(jnp.bfloat16).reshape(token_count, width)
    )
    qkv_bias = jnp.stack(
        [
            bias_all[6 * width : 7 * width],
            jnp.zeros((width,), jnp.float32),
            bias_all[7 * width : 8 * width],
        ]
    )
    qkv = fast_dot("td,jde->tje", attn_in, attn_w[0:3]) + qkv_bias
    query_rows = qkv[:, 0].reshape(seq_count, frame_count, HEADS, head_dim)
    key_rows = qkv[:, 1].reshape(seq_count, frame_count, HEADS, head_dim)
    value_rows = qkv[:, 2].reshape(seq_count, frame_count, HEADS, head_dim)
    mixed, log_totals = attention_forward(query_rows, key_rows, value_rows, key_keep)
    mixed_low = mixed.reshape(token_count, width).astype(jnp.bfloat16)
    proj = fast_dot("td,de->te", mixed_low, attn_w[3]) + bias_all[8 * width : 9 * width]
    proj_rows = proj.reshape(clip_count, row_count, width)
    resid = stream + valid * gate_one * proj_rows
    mlp_in = modulate(resid, shift_two, scale_two).astype(jnp.bfloat16).reshape(token_count, width)
    pre = fast_dot("td,jde->jte", mlp_in, one_w) + bias_all[9 * width : 13 * width].reshape(
        4, 1, width
    )
    hidden = gelu_tanh(pre).astype(jnp.bfloat16)
    grad_out = cotangent.astype(jnp.float32).reshape(clip_count, row_count, width)
    d_branch = (grad_out * valid * gate_two).astype(jnp.bfloat16).reshape(token_count, width)
    whole_two = scatter_blocks(lambda left: fast_dot("jtd,te->jde", left, d_branch), hidden, group)
    branch = fast_dot("jtd,jde->te", hidden, two_w) + bias_all[13 * width : 14 * width]
    branch_rows = branch.reshape(clip_count, row_count, width)
    block_out = (resid + valid * gate_two * branch_rows).astype(jnp.bfloat16).reshape(tokens.shape)
    d_gate_two = jnp.sum(grad_out * valid * branch_rows, axis=1, keepdims=True)
    grad_b_two = jnp.sum(d_branch.astype(jnp.float32), axis=0)
    d_hidden = fast_dot("te,jde->jtd", d_branch, two_w)
    gelu_value, gelu_pull = jax.vjp(gelu_tanh, pre)
    d_pre = gelu_pull(d_hidden)[0].astype(jnp.bfloat16)
    whole_one = scatter_blocks(lambda left: fast_dot("td,jte->jde", left, d_pre), mlp_in, group)
    grad_b_one = jnp.sum(d_pre.astype(jnp.float32), axis=1).reshape(4 * width)
    d_mlp_in = fast_dot("jte,jde->td", d_pre, one_w).reshape(clip_count, row_count, width)
    mod_value, mod_pull = jax.vjp(modulate, resid, shift_two, scale_two)
    d_resid_norm, d_shift_two, d_scale_two = mod_pull(d_mlp_in)
    d_resid = grad_out + d_resid_norm
    d_proj = (d_resid * valid * gate_one).astype(jnp.bfloat16).reshape(token_count, width)
    d_gate_one = jnp.sum(d_resid * valid * proj_rows, axis=1, keepdims=True)
    grad_b_out = jnp.sum(d_proj.astype(jnp.float32), axis=0)
    d_proj, right_wholes[2] = lax.optimization_barrier((d_proj, right_wholes[2]))
    d_mixed = fast_dot("te,de->td", d_proj, attn_w[3]).reshape(
        seq_count, frame_count, HEADS, head_dim
    )
    d_query, d_keys, d_values = attention_backward(
        query_rows, key_rows, value_rows, key_keep, log_totals, d_mixed
    )
    d_qkv = jnp.stack(
        [
            d_query.reshape(token_count, width),
            d_keys.reshape(token_count, width),
            d_values.reshape(token_count, width),
        ],
        axis=0,
    ).astype(jnp.bfloat16)
    d_qkv, right_wholes[1], right_wholes[0] = lax.optimization_barrier(
        (d_qkv, right_wholes[1], right_wholes[0])
    )
    qkv_sums = jnp.sum(d_qkv.astype(jnp.float32), axis=1)
    whole_attn = scatter_blocks(
        lambda left: jnp.concatenate(
            [
                fast_dot("td,jte->jde", left[0], d_qkv),
                fast_dot("td,te->de", left[1], d_proj)[None],
            ]
        ),
        jnp.stack([attn_in, mixed_low]),
        group,
    )
    d_attn_in = fast_dot("jte,jde->td", d_qkv, attn_w[0:3]).reshape(clip_count, row_count, width)
    first_value, first_pull = jax.vjp(modulate, stream, shift_one, scale_one)
    d_stream_norm, d_shift_one, d_scale_one = first_pull(d_attn_in)
    input_grad = (d_resid + d_stream_norm).astype(jnp.bfloat16).reshape(tokens.shape)

    d_mods = jnp.concatenate(
        [d_shift_one, d_scale_one, d_gate_one, d_shift_two, d_scale_two, d_gate_two], axis=1
    )
    grad_b_ada = jnp.sum(d_mods, axis=0).reshape(6 * width)
    grad_bias = jnp.concatenate(
        [grad_b_ada, qkv_sums[0], qkv_sums[2], grad_b_out, grad_b_one, grad_b_two]
    )
    to_ranks = jnp.concatenate(
        [
            d_mods.reshape(clip_count, mod_count, ranks, col_part)
            .transpose(2, 0, 1, 3)
            .reshape(ranks, mod_size),
            grad_bias.reshape(dp_count, ranks, bias_part)
            .transpose(1, 0, 2)
            .reshape(ranks, bias_size),
        ],
        axis=1,
    )
    rank_sums = jnp.sum(lax.all_to_all(to_ranks, "fsdp", 0, 0, tiled=True), axis=0)
    to_rows = jnp.concatenate(
        [
            jnp.broadcast_to(rank_sums[None, :mod_size], (dp_count, mod_size)),
            rank_sums[mod_size:].reshape(dp_count, bias_part),
        ],
        axis=1,
    )
    from_rows = lax.all_to_all(to_rows, "dp", 0, 0, tiled=True)
    bias_grad = jnp.sum(from_rows[:, mod_size:], axis=0)
    mod_grad_cols = from_rows[:, :mod_size].reshape(all_clips, mod_count, col_part)
    mod_grad = lax.all_gather(mod_grad_cols, "fsdp", axis=2, tiled=True)

    mod_grad_rows = lax.dynamic_slice_in_dim(mod_grad, dp_at * row_part, row_part, 2)
    right_parts = jnp.einsum(
        "cjk,jke->cje", mod_grad_rows, right_roots[:mod_count], precision=precise
    )
    mod_right = jnp.sum(lax.all_gather(right_parts, "dp", axis=0), axis=0)
    ada_pre = jnp.einsum("jrc,cje->jre", left_cond, mod_right, precision=precise)
    cond_wide = wide(cond_all)
    cond_row_wide = wide(cond_rows)
    mod_gram = jnp.einsum("cjk,bjk->jcb", mod_grad, mod_grad, precision=precise)
    cond_gram = jnp.einsum("ck,bk->cb", cond_wide, cond_wide, precision=precise)
    mod_side = jnp.einsum("jcb,be->jce", mod_gram, cond_cols, precision=precise)
    ada_left = jnp.einsum("cr,jce->jre", cond_row_wide, mod_side, precision=precise)
    cond_side = jnp.einsum("cb,bje->jce", cond_gram, mod_grad_cols, precision=precise)
    ada_right = jnp.einsum("cjr,jce->jre", mod_grad_rows, cond_side, precision=precise)

    back_two = shard_rows(owned_step(whole_two, left_rows[2], right_wholes[2], group), group)
    back_one = shard_rows(owned_step(whole_one, left_rows[1], right_wholes[1], group), group)
    back_attn = shard_rows(owned_step(whole_attn, left_rows[0], right_wholes[0], group), group)

    def joined(at, ada):
        span = slice(at * group, (at + 1) * group)
        return jnp.concatenate(
            [ada, wide(back_attn[span]), wide(back_one[span]), wide(back_two[span])]
        )

    precond = joined(0, ada_pre)
    left_new = stat_decay * left_stats + (1.0 - stat_decay) * joined(1, ada_left)
    right_new = stat_decay * right_stats + (1.0 - stat_decay) * joined(2, ada_right)
    momentum_new = moment_decay * momentum + precond
    weights_new = weights - weight_rate * momentum_new
    weights_copy = weights_new.astype(jnp.bfloat16)
    bias_second_new = stat_decay * bias_second + (1.0 - stat_decay) * bias_grad * bias_grad
    bias_moment_new = moment_decay * bias_moment + bias_grad * lax.rsqrt(
        bias_second_new + diag_epsilon
    )
    biases_new = biases - bias_rate * bias_moment_new
    return (
        block_out,
        input_grad,
        left_new,
        right_new,
        momentum_new,
        weights_new,
        weights_copy,
        bias_moment_new,
        bias_second_new,
        biases_new,
    )


def solution(mesh):
    placed = (
        P("dp", "fsdp", None, None),
        P("dp", None),
        P("dp"),
        P("dp", "fsdp", None, None),
        P(None, "dp", "fsdp"),
        P(("dp", "fsdp")),
        P(None, "dp", "fsdp"),
        P(None, "dp", "fsdp"),
        P(None, "dp", "fsdp"),
        P(None, "dp", "fsdp"),
        P(None, "dp", "fsdp"),
        P(("dp", "fsdp")),
        P(("dp", "fsdp")),
    )
    return jax.shard_map(
        per_device,
        mesh=mesh,
        in_specs=placed,
        out_specs=(
            P("dp", "fsdp", None, None),
            P("dp", "fsdp", None, None),
            P(None, "dp", "fsdp"),
            P(None, "dp", "fsdp"),
            P(None, "dp", "fsdp"),
            P(None, "dp", "fsdp"),
            P(None, "dp", "fsdp"),
            P(("dp", "fsdp")),
            P(("dp", "fsdp")),
            P(("dp", "fsdp")),
        ),
        check_vma=False,
    )
```

```python
import jax
import jax.numpy as jnp
from jax import lax
from jax.sharding import PartitionSpec as P

HEADS = 16


precise = lax.Precision.HIGHEST
norm_epsilon = 1e-06
masked_score = -1e30
stat_decay = 0.5
moment_decay = 0.9
weight_rate = 0.7
bias_rate = 0.1
diag_epsilon = 1e-08


def layer_norm(values):
    centered = values - jnp.mean(values, axis=-1, keepdims=True)
    variance = jnp.mean(centered * centered, axis=-1, keepdims=True)
    return centered * lax.rsqrt(variance + norm_epsilon)


def modulate(values, shift, scale):
    return layer_norm(values) * (1.0 + scale) + shift


def gelu_tanh(values_in):
    return jax.nn.gelu(values_in, approximate=True)


def attention_scores(query_rows, key_rows, key_keep):
    scale = query_rows.shape[-1] ** (-0.5)
    scores = jnp.einsum("sfhd,sghd->shfg", query_rows, key_rows, precision=precise) * scale
    return jnp.where(key_keep[:, None, None, :], scores, masked_score)


def attention_forward(query_rows, key_rows, value_rows, key_keep):
    scores = attention_scores(query_rows, key_rows, key_keep)
    highest = jnp.max(scores, axis=-1, keepdims=True)
    expons = jnp.exp(scores - highest)
    totals = jnp.sum(expons, axis=-1, keepdims=True)
    mixed = jnp.einsum("shfg,sghd->sfhd", expons / totals, value_rows, precision=precise)
    return (mixed, highest + jnp.log(totals))


def attention_backward(query_rows, key_rows, value_rows, key_keep, log_totals, grad_mixed):
    scale = query_rows.shape[-1] ** (-0.5)
    probs = jnp.exp(attention_scores(query_rows, key_rows, key_keep) - log_totals)
    grad_probs = jnp.einsum("sfhd,sghd->shfg", grad_mixed, value_rows, precision=precise)
    grad_values = jnp.einsum("shfg,sfhd->sghd", probs, grad_mixed, precision=precise)
    inner = jnp.sum(grad_probs * probs, axis=-1, keepdims=True)
    grad_scores = probs * (grad_probs - inner) * scale
    grad_query = jnp.einsum("shfg,sghd->sfhd", grad_scores, key_rows, precision=precise)
    grad_keys = jnp.einsum("shfg,sfhd->sghd", grad_scores, query_rows, precision=precise)
    return (grad_query, grad_keys, grad_values)


def narrow(array):
    return array.astype(jnp.bfloat16)


def wide(array):
    return array.astype(jnp.float32)


def packed(arrays, tile):
    flat = jnp.concatenate([array.reshape(-1) for array in arrays])
    return jnp.pad(flat, (0, -flat.shape[0] % (tile * 128))).reshape(-1, 128)


def core_swap(array):
    count = lax.axis_size("dp")
    return lax.ppermute(array, "dp", [(at, at ^ 1) for at in range(count)])


def chip_shift(array, step):
    count = lax.axis_size("dp")
    return lax.ppermute(array, "dp", [(at, (at + 2 * step) % count) for at in range(count)])


def rank_swap(array, bits):
    count = lax.axis_size("fsdp")
    return lax.ppermute(array, "fsdp", [(at, at ^ bits) for at in range(count)])


def entry(array, at, axis=0):
    return lax.dynamic_index_in_dim(array, at, axis, keepdims=False)


def put(array, part, *at):
    part = part.reshape((1,) * (array.ndim - part.ndim) + part.shape)
    at = at + (0,) * (array.ndim - len(at))
    return lax.dynamic_update_slice(array, part, at)


def own_rows(parts, group):
    ranks, at = lax.axis_size("fsdp"), lax.axis_index("fsdp")
    shares = ranks // group
    row_part, col_part = parts.shape[1:]
    chunk = row_part // shares
    split = parts.reshape(ranks, chunk, col_part)
    panels = [entry(split, at)]
    panels += [rank_swap(entry(split, at ^ bits), bits) for bits in range(1, ranks)]
    placed = [
        lax.select_n(at, *[panels[panel ^ index] for index in range(ranks)])
        for panel in range(ranks)
    ]
    return jnp.concatenate(placed, axis=1)


def shard_rows(rows, group):
    ranks = lax.axis_size("fsdp")
    shares = ranks // group
    count, chunk, total = rows.shape
    col_part = total // ranks
    split = rows.reshape(count, chunk, ranks, col_part).transpose(2, 0, 1, 3)
    moved = lax.all_to_all(split, "fsdp", 0, 0, tiled=True)
    moved = moved.reshape(group, shares, count, chunk, col_part).transpose(2, 0, 1, 3, 4)
    return moved.reshape(count * group, shares * chunk, col_part)


def gather_blocks(rows, group):
    ranks, dp_count = lax.axis_size("fsdp"), lax.axis_size("dp")
    shares = ranks // group
    chunk, total = rows.shape
    all_rows = lax.all_gather(rows, ("fsdp", "dp"), axis=0, tiled=True)
    if shares > 1:
        all_rows = all_rows.reshape(group, shares, dp_count, chunk, total).transpose(0, 2, 1, 3, 4)
    return all_rows.reshape(group, total, total)


def tie(*values):
    return lax.optimization_barrier(values)


def gather_pieces(rows, group):
    ranks, at = lax.axis_size("fsdp"), lax.axis_index("fsdp")
    if ranks != group:
        blocks = gather_blocks(rows, group)
        (blocks,) = yield (blocks,)
        yield blocks
        return
    chips = lax.axis_size("dp") // 2
    core, chip = lax.axis_index("dp") % 2, lax.axis_index("dp") // 2
    chunk, total = rows.shape
    line = put(jnp.zeros((chips, chunk, total), rows.dtype), rows, chip)
    for step in range(1, chips):
        line = put(line, chip_shift(rows, step), (chip - step) % chips)
    own = jnp.zeros((chips, 2, chunk, total), rows.dtype)
    own = put(own, line[:, None], 0, core)
    own = put(own, core_swap(line)[:, None], 0, 1 - core)
    own = own.reshape(2, total // 2, total)
    half = entry(own, core)
    mine = [rank_swap(half, bits) for bits in range(1, ranks)]
    own, *mine = yield (own, *mine)
    others = [core_swap(part) for part in mine]
    found = put(jnp.zeros((ranks, 2, total // 2, total), rows.dtype), own, at)
    for bits in range(1, ranks):
        found = put(found, mine[bits - 1], at ^ bits, core)
        found = put(found, others[bits - 1], at ^ bits, 1 - core)
    yield found.reshape(group, total, total)


def gather_own(rows, group):
    ranks = lax.axis_size("fsdp")
    shares = ranks // group
    chunk, total = rows.shape
    if shares > 1:
        sets = [[share + shares * block for share in range(shares)] for block in range(group)]
        rows = lax.all_gather(rows, "fsdp", axis=0, tiled=True, axis_index_groups=sets)
    return lax.all_gather(rows, "dp", axis=0, tiled=True)


def sum_blocks(product, left, group):
    ranks, dp_count = lax.axis_size("fsdp"), lax.axis_size("dp")
    shares = ranks // group
    total = left.shape[-1]
    if shares > 1:
        blocks = narrow(product(left))
        chunk = total // (dp_count * shares)
        blocks = blocks.reshape(group, dp_count, shares, chunk, -1).transpose(0, 2, 1, 3, 4)
        rows = lax.psum_scatter(
            blocks.reshape(group * total, -1), ("fsdp", "dp"), scatter_dimension=0, tiled=True
        )
        for _ in range(3):
            (rows,) = yield (rows,)
        yield gather_own(rows, group)
        return
    chips, half = dp_count // 2, total // 2
    chunk = half // chips
    core, chip = lax.axis_index("dp") % 2, lax.axis_index("dp") // 2
    low_bit, high_bit = lax.axis_index("fsdp") % 2, lax.axis_index("fsdp") // 2
    away = narrow(product(lax.dynamic_slice_in_dim(left, (1 - core) * half, half, left.ndim - 1)))
    here = product(lax.dynamic_slice_in_dim(left, core * half, half, left.ndim - 1))
    here = narrow(here + wide(core_swap(away)))
    here = here.reshape(2, 2, chips, chunk, -1)
    cut = chips // 2
    first, second = here[:, :, :cut], here[:, :, cut:]
    first_in = rank_swap(entry(first, 1 - low_bit, 1), 1)
    second_in = rank_swap(entry(second, 1 - high_bit, 0), 2)
    here, first_in, second_in = yield (here, first_in, second_in)
    first, second = here[:, :, :cut], here[:, :, cut:]
    first = narrow(wide(entry(first, low_bit, 1)) + wide(first_in))
    second = narrow(wide(entry(second, high_bit, 0)) + wide(second_in))
    first_in = rank_swap(entry(first, 1 - high_bit), 2)
    second_in = rank_swap(entry(second, 1 - low_bit), 1)
    first, second, first_in, second_in = yield (first, second, first_in, second_in)
    first = narrow(wide(entry(first, high_bit)) + wide(first_in))
    second = narrow(wide(entry(second, low_bit)) + wide(second_in))
    line = jnp.concatenate([first, second])
    parts = [entry(line, chip)]
    parts += [chip_shift(entry(line, (chip + step) % chips), step) for step in range(1, chips)]
    parts = yield tuple(parts)
    rows = sum(wide(part) for part in parts)
    found = lax.all_gather(narrow(rows), "dp", axis=0, tiled=True)
    yield found.reshape(chips, 2, chunk, -1).transpose(1, 0, 2, 3).reshape(total, -1)


def fast_dot(subscripts, left, right):
    return jnp.einsum(subscripts, left, right, preferred_element_type=jnp.float32)


def owned_step(whole, left_root, right_root, group):
    chunk = left_root.shape[0]
    shares = lax.axis_size("fsdp") // group
    first = lax.axis_index("dp") * (chunk * shares) + lax.axis_index("fsdp") % shares * chunk
    grad_rows = lax.dynamic_slice_in_dim(whole, first, chunk, 0)
    own_columns = lax.dynamic_slice_in_dim(whole, first, chunk, 1)
    outer = fast_dot("rk,jk->rj", grad_rows, whole)
    inner = fast_dot("kr,kj->rj", own_columns, whole)
    side = fast_dot("rk,kj->rj", left_root, whole)
    side_high = narrow(side)
    side_low = narrow(side - wide(side_high))
    precond = fast_dot("rk,kj->rj", side_high, right_root) + fast_dot(
        "rk,kj->rj", side_low, right_root
    )
    return narrow(jnp.stack([precond, outer, inner]))


def per_device(
    tokens,
    conditioning,
    frame_counts,
    cotangent,
    weights,
    biases,
    momentum,
    left_stats,
    right_stats,
    left_roots,
    right_roots,
    bias_moment,
    bias_second,
):
    group = 4
    mod_count = 6
    clip_count, pos_count, frame_count, width = tokens.shape
    row_count = pos_count * frame_count
    token_count = clip_count * row_count
    seq_count = clip_count * pos_count
    head_dim = width // HEADS
    block_count, row_part, col_part = weights.shape
    dp_count, ranks = lax.axis_size("dp"), lax.axis_size("fsdp")
    dp_at, rank_at = lax.axis_index("dp"), lax.axis_index("fsdp")
    all_clips = clip_count * dp_count
    bias_part = biases.shape[0]
    stream = tokens.astype(jnp.float32).reshape(clip_count, row_count, width)
    frame_ids = lax.broadcasted_iota(jnp.int32, (clip_count, frame_count), 1)
    keep = frame_ids < frame_counts[:, None]
    keep_all = jnp.broadcast_to(keep[:, None, :], (clip_count, pos_count, frame_count))
    key_keep = keep_all.reshape(seq_count, frame_count)
    valid = keep_all.astype(jnp.float32).reshape(clip_count, row_count, 1)

    pieces = [slice(mod_count + group * piece, mod_count + group * (piece + 1)) for piece in range(3)]
    attn_w = gather_blocks(own_rows(narrow(weights[pieces[0]]), group), group)
    two_w = gather_blocks(own_rows(narrow(weights[pieces[2]]), group), group)
    one_steps = gather_pieces(own_rows(narrow(weights[pieces[1]]), group), group)
    one_parts = next(one_steps)
    left_rows = [own_rows(narrow(left_roots[piece]), group) for piece in pieces]
    right_wholes = [gather_own(own_rows(narrow(right_roots[piece]), group), group) for piece in pieces]

    cond_low = jax.nn.silu(conditioning).astype(jnp.bfloat16)
    first_parts = lax.all_gather(
        packed([cond_low, narrow(biases)], 16), "dp", axis=0, tiled=True
    ).reshape(dp_count, -1)
    cond_all = first_parts[:, : clip_count * width].reshape(all_clips, width)
    bias_rows = wide(first_parts[:, clip_count * width : clip_count * width + bias_part])
    cond_rows = lax.dynamic_slice_in_dim(cond_all, dp_at * row_part, row_part, 1)
    cond_cols = wide(lax.dynamic_slice_in_dim(cond_all, rank_at * col_part, col_part, 1))
    mod_parts = fast_dot("cr,jre->cje", cond_rows, narrow(weights[:mod_count]))
    mod_parts = lax.all_to_all(mod_parts, "dp", 0, 0, tiled=True)
    mod_cols = jnp.sum(mod_parts.reshape(dp_count, clip_count, mod_count, col_part), axis=0)
    left_cond = jnp.einsum("jrk,ck->jrc", left_roots[:mod_count], cond_cols, precision=precise)
    mod_size, bias_size = mod_cols.size, dp_count * bias_part
    second_parts = lax.all_gather(
        packed([mod_cols, bias_rows, left_cond], 8), "fsdp", axis=0, tiled=True
    ).reshape(ranks, -1)
    mods = second_parts[:, :mod_size].reshape(ranks, clip_count, mod_count, col_part)
    mods = mods.transpose(1, 2, 0, 3).reshape(clip_count, mod_count, width)
    bias_all = second_parts[:, mod_size : mod_size + bias_size].reshape(ranks, dp_count, bias_part)
    bias_all = bias_all.transpose(1, 0, 2).reshape(-1)
    left_size = mod_size + bias_size + left_cond.size
    left_cond = jnp.sum(second_parts[:, mod_size + bias_size : left_size], axis=0)
    left_cond = left_cond.reshape(mod_count, row_part, all_clips)
    mods = mods + bias_all[0 : 6 * width].reshape(6, width)
    shift_one = mods[:, 0:1]
    scale_one = mods[:, 1:2]
    gate_one = mods[:, 2:3]
    shift_two = mods[:, 3:4]
    scale_two = mods[:, 4:5]
    gate_two = mods[:, 5:6]

    attn_in = (
        modulate(stream, shift_one, scale_one).astype(jnp.bfloat16).reshape(token_count, width)
    )
    qkv_bias = jnp.stack(
        [
            bias_all[6 * width : 7 * width],
            jnp.zeros((width,), jnp.float32),
            bias_all[7 * width : 8 * width],
        ]
    )
    qkv = fast_dot("td,jde->tje", attn_in, attn_w[0:3]) + qkv_bias
    query_rows = qkv[:, 0].reshape(seq_count, frame_count, HEADS, head_dim)
    key_rows = qkv[:, 1].reshape(seq_count, frame_count, HEADS, head_dim)
    value_rows = qkv[:, 2].reshape(seq_count, frame_count, HEADS, head_dim)
    mixed, log_totals = attention_forward(query_rows, key_rows, value_rows, key_keep)
    mixed_low = mixed.reshape(token_count, width).astype(jnp.bfloat16)
    proj = fast_dot("td,de->te", mixed_low, attn_w[3]) + bias_all[8 * width : 9 * width]
    proj_rows = proj.reshape(clip_count, row_count, width)
    resid = stream + valid * gate_one * proj_rows
    resid, one_parts = tie(resid, one_parts)
    one_w = one_steps.send(one_parts)
    mlp_in = modulate(resid, shift_two, scale_two).astype(jnp.bfloat16).reshape(token_count, width)
    pre = fast_dot("td,jde->jte", mlp_in, one_w) + bias_all[9 * width : 13 * width].reshape(
        4, 1, width
    )
    hidden = gelu_tanh(pre).astype(jnp.bfloat16)
    grad_out = cotangent.astype(jnp.float32).reshape(clip_count, row_count, width)
    d_branch = (grad_out * valid * gate_two).astype(jnp.bfloat16).reshape(token_count, width)
    two_steps = sum_blocks(lambda left: fast_dot("jtd,te->jde", left, d_branch), hidden, group)
    two_parts = next(two_steps)
    branch = fast_dot("jtd,jde->te", hidden, two_w) + bias_all[13 * width : 14 * width]
    branch_rows = branch.reshape(clip_count, row_count, width)
    block_out = (resid + valid * gate_two * branch_rows).astype(jnp.bfloat16).reshape(tokens.shape)
    d_gate_two = jnp.sum(grad_out * valid * branch_rows, axis=1, keepdims=True)
    grad_b_two = jnp.sum(d_branch.astype(jnp.float32), axis=0)
    d_hidden = fast_dot("te,jde->jtd", d_branch, two_w)
    gelu_value, gelu_pull = jax.vjp(gelu_tanh, pre)
    d_pre = gelu_pull(d_hidden)[0].astype(jnp.bfloat16)
    d_pre, block_out, d_gate_two, two_parts = tie(d_pre, block_out, d_gate_two, two_parts)
    two_parts = two_steps.send(two_parts)
    one_steps = sum_blocks(lambda left: fast_dot("td,jte->jde", left, d_pre), mlp_in, group)
    one_parts = list(next(one_steps))
    grad_b_one = jnp.sum(d_pre.astype(jnp.float32), axis=1).reshape(4 * width)
    d_pre, one_parts[0], two_parts = tie(d_pre, one_parts[0], two_parts)
    two_parts = two_steps.send(two_parts)
    d_mlp_in = fast_dot("jte,jde->td", d_pre, one_w).reshape(clip_count, row_count, width)
    mod_value, mod_pull = jax.vjp(modulate, resid, shift_two, scale_two)
    d_resid_norm, d_shift_two, d_scale_two = mod_pull(d_mlp_in)
    d_resid = grad_out + d_resid_norm
    d_proj = (d_resid * valid * gate_one).astype(jnp.bfloat16).reshape(token_count, width)
    d_gate_one = jnp.sum(d_resid * valid * proj_rows, axis=1, keepdims=True)
    grad_b_out = jnp.sum(d_proj.astype(jnp.float32), axis=0)
    d_mixed = fast_dot("te,de->td", d_proj, attn_w[3]).reshape(
        seq_count, frame_count, HEADS, head_dim
    )
    d_mixed, one_parts, two_parts, right_wholes[2] = tie(
        d_mixed, one_parts, two_parts, right_wholes[2]
    )
    one_parts = one_steps.send(one_parts)
    whole_two = two_steps.send(two_parts)
    d_query, d_keys, d_values = attention_backward(
        query_rows, key_rows, value_rows, key_keep, log_totals, d_mixed
    )
    d_qkv = jnp.stack(
        [
            d_query.reshape(token_count, width),
            d_keys.reshape(token_count, width),
            d_values.reshape(token_count, width),
        ],
        axis=0,
    ).astype(jnp.bfloat16)
    d_qkv, one_parts, right_wholes[1], right_wholes[0] = tie(
        d_qkv, one_parts, right_wholes[1], right_wholes[0]
    )
    one_parts = one_steps.send(one_parts)
    qkv_sums = jnp.sum(d_qkv.astype(jnp.float32), axis=1)
    attn_steps = sum_blocks(
        lambda left: jnp.concatenate(
            [
                fast_dot("td,jte->jde", left[0], d_qkv),
                fast_dot("td,te->de", left[1], d_proj)[None],
            ]
        ),
        jnp.stack([attn_in, mixed_low]),
        group,
    )
    attn_parts = list(next(attn_steps))
    d_qkv, attn_parts[0] = tie(d_qkv, attn_parts[0])
    d_attn_in = fast_dot("jte,jde->td", d_qkv, attn_w[0:3]).reshape(clip_count, row_count, width)
    first_value, first_pull = jax.vjp(modulate, stream, shift_one, scale_one)
    d_stream_norm, d_shift_one, d_scale_one = first_pull(d_attn_in)
    input_grad = (d_resid + d_stream_norm).astype(jnp.bfloat16).reshape(tokens.shape)

    d_shift_one, d_scale_one, input_grad, attn_parts, one_parts = tie(
        d_shift_one, d_scale_one, input_grad, attn_parts, one_parts
    )
    attn_parts = attn_steps.send(attn_parts)
    whole_one = one_steps.send(one_parts)

    d_mods = jnp.concatenate(
        [d_shift_one, d_scale_one, d_gate_one, d_shift_two, d_scale_two, d_gate_two], axis=1
    )
    grad_b_ada = jnp.sum(d_mods, axis=0).reshape(6 * width)
    grad_bias = jnp.concatenate(
        [grad_b_ada, qkv_sums[0], qkv_sums[2], grad_b_out, grad_b_one, grad_b_two]
    )
    to_ranks = jnp.concatenate(
        [
            d_mods.reshape(clip_count, mod_count, ranks, col_part)
            .transpose(2, 0, 1, 3)
            .reshape(ranks, mod_size),
            grad_bias.reshape(dp_count, ranks, bias_part)
            .transpose(1, 0, 2)
            .reshape(ranks, bias_size),
        ],
        axis=1,
    )
    rank_sums = jnp.sum(lax.all_to_all(to_ranks, "fsdp", 0, 0, tiled=True), axis=0)
    to_rows = jnp.concatenate(
        [
            jnp.broadcast_to(rank_sums[None, :mod_size], (dp_count, mod_size)),
            rank_sums[mod_size:].reshape(dp_count, bias_part),
        ],
        axis=1,
    )
    from_rows = lax.all_to_all(to_rows, "dp", 0, 0, tiled=True)
    products_two = owned_step(whole_two, left_rows[2], right_wholes[2], group)
    from_rows, products_two, attn_parts = tie(from_rows, products_two, attn_parts)
    attn_parts = attn_steps.send(attn_parts)
    back_two = shard_rows(products_two, group)
    bias_grad = jnp.sum(from_rows[:, mod_size:], axis=0)
    mod_grad_cols = from_rows[:, :mod_size].reshape(all_clips, mod_count, col_part)
    mod_grad = lax.all_gather(mod_grad_cols, "fsdp", axis=2, tiled=True)

    mod_grad_rows = lax.dynamic_slice_in_dim(mod_grad, dp_at * row_part, row_part, 2)
    right_parts = jnp.einsum(
        "cjk,jke->cje", mod_grad_rows, right_roots[:mod_count], precision=precise
    )
    cond_wide = wide(cond_all)
    cond_row_wide = wide(cond_rows)
    mod_gram = jnp.einsum("cjk,bjk->jcb", mod_grad, mod_grad, precision=precise)
    cond_gram = jnp.einsum("ck,bk->cb", cond_wide, cond_wide, precision=precise)
    mod_side = jnp.einsum("jcb,be->jce", mod_gram, cond_cols, precision=precise)
    ada_left = jnp.einsum("cr,jce->jre", cond_row_wide, mod_side, precision=precise)
    cond_side = jnp.einsum("cb,bje->jce", cond_gram, mod_grad_cols, precision=precise)
    ada_right = jnp.einsum("cjr,jce->jre", mod_grad_rows, cond_side, precision=precise)

    products_one = owned_step(whole_one, left_rows[1], right_wholes[1], group)
    products_one, right_parts, attn_parts = tie(products_one, right_parts, attn_parts)
    whole_attn = attn_steps.send(attn_parts)
    back_one = shard_rows(products_one, group)
    mod_right = jnp.sum(lax.all_gather(right_parts, "dp", axis=0), axis=0)
    ada_pre = jnp.einsum("jrc,cje->jre", left_cond, mod_right, precision=precise)
    back_attn = shard_rows(owned_step(whole_attn, left_rows[0], right_wholes[0], group), group)

    def joined(at, ada):
        span = slice(at * group, (at + 1) * group)
        return jnp.concatenate(
            [ada, wide(back_attn[span]), wide(back_one[span]), wide(back_two[span])]
        )

    precond = joined(0, ada_pre)
    left_new = stat_decay * left_stats + (1.0 - stat_decay) * joined(1, ada_left)
    right_new = stat_decay * right_stats + (1.0 - stat_decay) * joined(2, ada_right)
    momentum_new = moment_decay * momentum + precond
    weights_new = weights - weight_rate * momentum_new
    weights_copy = weights_new.astype(jnp.bfloat16)
    bias_second_new = stat_decay * bias_second + (1.0 - stat_decay) * bias_grad * bias_grad
    bias_moment_new = moment_decay * bias_moment + bias_grad * lax.rsqrt(
        bias_second_new + diag_epsilon
    )
    biases_new = biases - bias_rate * bias_moment_new
    return (
        block_out,
        input_grad,
        left_new,
        right_new,
        momentum_new,
        weights_new,
        weights_copy,
        bias_moment_new,
        bias_second_new,
        biases_new,
    )


def solution(mesh):
    placed = (
        P("dp", "fsdp", None, None),
        P("dp", None),
        P("dp"),
        P("dp", "fsdp", None, None),
        P(None, "dp", "fsdp"),
        P(("dp", "fsdp")),
        P(None, "dp", "fsdp"),
        P(None, "dp", "fsdp"),
        P(None, "dp", "fsdp"),
        P(None, "dp", "fsdp"),
        P(None, "dp", "fsdp"),
        P(("dp", "fsdp")),
        P(("dp", "fsdp")),
    )
    return jax.shard_map(
        per_device,
        mesh=mesh,
        in_specs=placed,
        out_specs=(
            P("dp", "fsdp", None, None),
            P("dp", "fsdp", None, None),
            P(None, "dp", "fsdp"),
            P(None, "dp", "fsdp"),
            P(None, "dp", "fsdp"),
            P(None, "dp", "fsdp"),
            P(None, "dp", "fsdp"),
            P(("dp", "fsdp")),
            P(("dp", "fsdp")),
            P(("dp", "fsdp")),
        ),
        check_vma=False,
    )
```

```python
import functools
import math

import jax
import jax.numpy as jnp
from jax import lax
from jax.experimental import pallas as pl
from jax.experimental.pallas import tpu as pltpu
from jax.sharding import PartitionSpec as P

HEADS = 16


precise = lax.Precision.HIGHEST
norm_epsilon = 1e-06
masked_score = -1e30
stat_decay = 0.5
moment_decay = 0.9
weight_rate = 0.7
bias_rate = 0.1
diag_epsilon = 1e-08
vmem_bytes = 50 * 2**20


def narrow(array):
    return array.astype(jnp.bfloat16)


def wide(array):
    return array.astype(jnp.float32)


def spec(shape, index_map, **keywords):
    return pl.BlockSpec(shape, index_map, **keywords)


def held(shape):
    return pl.BlockSpec(shape, lambda step: (0,) * len(shape), pipeline_mode=pl.Buffered(1))


def column_cuts(total):
    cuts, at = [], 0
    while at < total:
        cuts.append((at, min(total, at + 256)))
        at += 256
    return cuts


def dot_nn(left, right):
    return lax.dot_general(left, right, (((1,), (0,)), ((), ())), preferred_element_type=jnp.float32)


def dot_nt(left, right):
    return lax.dot_general(left, right, (((1,), (1,)), ((), ())), preferred_element_type=jnp.float32)


def dot_tn(left, right):
    return lax.dot_general(left, right, (((0,), (0,)), ((), ())), preferred_element_type=jnp.float32)


def split_high(values):
    high = narrow(values)
    return high, narrow(values - wide(high))


def valid_rows(count, rows, frames):
    at = lax.broadcasted_iota(jnp.int32, (rows, 1), 0)
    return (lax.rem(at, frames) < count).astype(jnp.float32)


def score_offset(count, size, frames, key_axis):
    first = lax.broadcasted_iota(jnp.int32, (size, size), 0)
    second = lax.broadcasted_iota(jnp.int32, (size, size), 1)
    key = second if key_axis == 1 else first
    met = (lax.div(first, frames) == lax.div(second, frames)) & (lax.rem(key, frames) < count)
    return jnp.where(met, 0.0, masked_score)


def head_windows(width):
    size = width // HEADS
    windows = []
    for head in range(HEADS):
        low, high = head * size, (head + 1) * size
        start = low // 128 * 128
        stop = min(width, -(-high // 128) * 128)
        windows.append((low - start, high - start, start, stop))
    return windows


def lane_mask(low, high, count, dtype):
    lanes = lax.broadcasted_iota(jnp.int32, (1, count), 1)
    return ((lanes >= low) & (lanes < high)).astype(jnp.float32).astype(dtype)


def norm_parts(values):
    centered = values - jnp.mean(values, axis=-1, keepdims=True)
    variance = jnp.mean(centered * centered, axis=-1, keepdims=True)
    inverse = lax.rsqrt(variance + norm_epsilon)
    return centered * inverse, inverse


def norm_back(grad, normed, inverse):
    first = jnp.mean(grad, axis=-1, keepdims=True)
    second = jnp.mean(grad * normed, axis=-1, keepdims=True)
    return (grad - first - normed * second) * inverse


def column_sum(values):
    return jnp.sum(values, axis=0, keepdims=True)


def attention_kernel(
    frames,
    counts,
    tokens,
    cotangent,
    mods,
    bias,
    blocks,
    attn_in,
    parts,
    mixed_low,
    proj_out,
    resid_out,
    mlp_in,
    d_branch,
    d_branch_sum,
    mixed,
):
    rows, width = tokens.shape
    tile = min(rows, 128)
    count = counts[pl.program_id(0)]
    shift_one, scale_one, gate_one = (mods[0, at : at + 1, :] for at in range(3))
    shift_two, scale_two, gate_two = (mods[0, at : at + 1, :] for at in range(3, 6))
    for first in range(0, rows, tile):
        span = slice(first, first + tile)
        normed, _ = norm_parts(wide(tokens[span]))
        attn_in[span] = narrow(normed * (1.0 + scale_one) + shift_one)
        branch_back = narrow(wide(cotangent[span]) * valid_rows(count, tile, frames) * gate_two)
        d_branch[span] = branch_back
        part_sum = column_sum(wide(branch_back))
        d_branch_sum[0] = part_sum if first == 0 else d_branch_sum[0] + part_sum
    scale = (width // HEADS) ** -0.5
    source = attn_in[...]
    for low, high in column_cuts(width):
        span = slice(low, high)
        query = (dot_nn(source, blocks[0, :, span]) + bias[0:1, span]) * scale
        parts[0, :, span], parts[1, :, span] = split_high(query)
        parts[2, :, span], parts[3, :, span] = split_high(dot_nn(source, blocks[1, :, span]))
        parts[4, :, span] = narrow(dot_nn(source, blocks[2, :, span]) + bias[2:3, span])
    offset = score_offset(count, tile, frames, 1)
    mixed[...] = jnp.zeros_like(mixed)
    for first in range(0, rows, tile):
        span = slice(first, first + tile)
        for low, high, start, stop in head_windows(width):
            lanes = slice(start, stop)
            mask = lane_mask(low, high, stop - start, jnp.bfloat16)
            key_high = parts[2, span, lanes]
            query_high = parts[0, span, lanes] * mask
            scores = dot_nt(query_high, key_high)
            scores += dot_nt(parts[1, span, lanes] * mask, key_high)
            scores += dot_nt(query_high, parts[3, span, lanes]) + offset
            expons = jnp.exp(scores - jnp.max(scores, axis=-1, keepdims=True))
            probs = expons * (1.0 / jnp.sum(expons, axis=-1, keepdims=True))
            out = dot_nn(narrow(probs), parts[4, span, lanes] * mask)
            mixed[span, lanes] += out
    mixed_low[...] = narrow(mixed[...])
    source = mixed_low[...]
    for low, high in column_cuts(width):
        span = slice(low, high)
        proj_out[:, span] = dot_nn(source, blocks[3, :, span]) + bias[3:4, span]
    for first in range(0, rows, tile):
        span = slice(first, first + tile)
        resid = wide(tokens[span]) + valid_rows(count, tile, frames) * gate_one * proj_out[span]
        resid_out[span] = resid
        normed, _ = norm_parts(resid)
        mlp_in[span] = narrow(normed * (1.0 + scale_two) + shift_two)


def run_attention(frames, counts, tokens, cotangent, mods, bias, blocks):
    total, width = tokens.shape
    clips = mods.shape[0]
    rows = total // clips
    clip_rows = spec((rows, width), lambda clip: (clip, 0))
    low = jax.ShapeDtypeStruct((total, width), jnp.bfloat16)
    full = jax.ShapeDtypeStruct((total, width), jnp.float32)
    return pl.pallas_call(
        functools.partial(attention_kernel, frames),
        grid=(clips,),
        in_specs=[
            pl.BlockSpec(memory_space=pltpu.SMEM),
            clip_rows,
            clip_rows,
            spec((1,) + mods.shape[1:], lambda clip: (clip, 0, 0)),
            held(bias.shape),
            held(blocks.shape),
        ],
        out_specs=[
            clip_rows,
            spec((5, rows, width), lambda clip: (0, clip, 0)),
            clip_rows,
            clip_rows,
            clip_rows,
            clip_rows,
            clip_rows,
            spec((1, 1, width), lambda clip: (clip, 0, 0)),
        ],
        out_shape=[
            low,
            jax.ShapeDtypeStruct((5, total, width), jnp.bfloat16),
            low,
            full,
            full,
            low,
            low,
            jax.ShapeDtypeStruct((clips, 1, width), jnp.float32),
        ],
        scratch_shapes=[pltpu.VMEM((rows, width), jnp.float32)],
        compiler_params=pltpu.CompilerParams(vmem_limit_bytes=vmem_bytes),
        cost_estimate=pl.CostEstimate(
            flops=12 * total * width * width, bytes_accessed=40 * total * width, transcendentals=0
        ),
    )(counts, tokens, cotangent, mods, bias, blocks)


def hidden_kernel(mlp_in, block, bias, hidden, slope):
    root = (2.0 / math.pi) ** 0.5
    source = mlp_in[...]
    for low, high in column_cuts(block.shape[-1]):
        span = slice(low, high)
        pre = dot_nn(source, block[0, :, span]) + bias[0, :, span]
        square = pre * pre
        bent = jnp.tanh(root * pre * (1.0 + 0.044715 * square))
        half = 0.5 + 0.5 * bent
        hidden[0, :, span] = narrow(pre * half)
        steep = (0.5 * root) * pre * (1.0 + 3 * 0.044715 * square)
        slope[0, :, span] = narrow(half + steep * (1.0 - bent * bent))


def run_hidden(mlp_in, blocks, bias):
    total, width = mlp_in.shape
    count = blocks.shape[0]
    per_block = spec((1, total, width), lambda at: (at, 0, 0))
    out = jax.ShapeDtypeStruct((count, total, width), jnp.bfloat16)
    return pl.pallas_call(
        hidden_kernel,
        grid=(count,),
        in_specs=[
            held(mlp_in.shape),
            spec((1, width, width), lambda at: (at, 0, 0)),
            spec((1, 1, width), lambda at: (at, 0, 0)),
        ],
        out_specs=[per_block, per_block],
        out_shape=[out, out],
        compiler_params=pltpu.CompilerParams(vmem_limit_bytes=vmem_bytes),
        cost_estimate=pl.CostEstimate(
            flops=8 * total * width * width, bytes_accessed=30 * total * width, transcendentals=0
        ),
    )(mlp_in, blocks, bias)


def branch_kernel(
    frames,
    counts,
    hidden,
    slope,
    block,
    d_branch,
    bias,
    gates,
    resid,
    cotangent,
    d_pre,
    d_pre_sum,
    block_out,
    d_gate,
    branch,
):
    step, steps = pl.program_id(0), pl.num_programs(0)
    total, width = resid.shape
    clips = gates.shape[0]
    rows = total // clips
    source, back = hidden[0], d_branch[...]

    @pl.when(step == 0)
    def _():
        branch[...] = jnp.zeros_like(branch)

    for low, high in column_cuts(width):
        span = slice(low, high)
        d_hidden = dot_nt(back, block[0, span, :])
        low_back = narrow(d_hidden * wide(slope[0, :, span]))
        d_pre[0, :, span] = low_back
        d_pre_sum[0, :, span] = column_sum(wide(low_back))
        branch[:, span] += dot_nn(source, block[0, :, span])

    @pl.when(step == steps - 1)
    def _():
        for clip in range(clips):
            span = slice(clip * rows, (clip + 1) * rows)
            kept = valid_rows(counts[clip], rows, frames) * (branch[span] + bias[...])
            block_out[span] = narrow(resid[span] + gates[clip] * kept)
            d_gate[clip] = column_sum(wide(cotangent[span]) * kept)


def run_branch(frames, counts, hidden, slope, blocks, d_branch, bias, gates, resid, cotangent):
    count, total, width = hidden.shape
    clips = gates.shape[0]
    per_block = spec((1, total, width), lambda at: (at, 0, 0))
    low = jax.ShapeDtypeStruct((total, width), jnp.bfloat16)
    return pl.pallas_call(
        functools.partial(branch_kernel, frames),
        grid=(count,),
        in_specs=[
            pl.BlockSpec(memory_space=pltpu.SMEM),
            per_block,
            per_block,
            spec((1, width, width), lambda at: (at, 0, 0)),
            held((total, width)),
            held(bias.shape),
            held(gates.shape),
            held((total, width)),
            held((total, width)),
        ],
        out_specs=[
            per_block,
            spec((1, 1, width), lambda at: (at, 0, 0)),
            held((total, width)),
            held((clips, 1, width)),
        ],
        out_shape=[
            jax.ShapeDtypeStruct((count, total, width), jnp.bfloat16),
            jax.ShapeDtypeStruct((count, 1, width), jnp.float32),
            low,
            jax.ShapeDtypeStruct((clips, 1, width), jnp.float32),
        ],
        scratch_shapes=[pltpu.VMEM((total, width), jnp.float32)],
        compiler_params=pltpu.CompilerParams(vmem_limit_bytes=vmem_bytes),
        cost_estimate=pl.CostEstimate(
            flops=16 * total * width * width, bytes_accessed=40 * total * width, transcendentals=0
        ),
    )(counts, hidden, slope, blocks, d_branch, bias, gates, resid, cotangent)


def resid_kernel(
    frames,
    counts,
    d_pre,
    block,
    mods,
    resid,
    cotangent,
    proj,
    d_resid_out,
    d_proj,
    sums,
    total_grad,
):
    step, steps = pl.program_id(0), pl.num_programs(0)
    total, width = resid.shape
    clips = mods.shape[0]
    rows = total // clips
    tile = min(rows, 128)
    source = d_pre[0]

    @pl.when(step == 0)
    def _():
        total_grad[...] = jnp.zeros_like(total_grad)

    for low, high in column_cuts(width):
        span = slice(low, high)
        total_grad[:, span] += dot_nt(source, block[0, span, :])

    @pl.when(step == steps - 1)
    def _():
        for clip in range(clips):
            gate_one, scale_two = mods[clip, 2:3, :], mods[clip, 4:5, :]
            found = [0.0] * 4
            for first in range(clip * rows, (clip + 1) * rows, tile):
                span = slice(first, first + tile)
                grad = total_grad[span]
                normed, inverse = norm_parts(resid[span])
                back = norm_back(grad * (1.0 + scale_two), normed, inverse)
                d_resid = wide(cotangent[span]) + back
                d_resid_out[span] = d_resid
                kept = valid_rows(counts[clip], tile, frames) * d_resid
                low_back = narrow(kept * gate_one)
                d_proj[span] = low_back
                terms = (grad, grad * normed, kept * proj[span], wide(low_back))
                found = [old + column_sum(term) for old, term in zip(found, terms)]
            for at in range(4):
                sums[clip, at : at + 1, :] = found[at]


def run_resid(frames, counts, d_pre, blocks, mods, resid, cotangent, proj):
    count, total, width = d_pre.shape
    clips = mods.shape[0]
    return pl.pallas_call(
        functools.partial(resid_kernel, frames),
        grid=(count,),
        in_specs=[
            pl.BlockSpec(memory_space=pltpu.SMEM),
            spec((1, total, width), lambda at: (at, 0, 0)),
            spec((1, width, width), lambda at: (at, 0, 0)),
            held(mods.shape),
            held((total, width)),
            held((total, width)),
            held((total, width)),
        ],
        out_specs=[held((total, width)), held((total, width)), held((clips, 4, width))],
        out_shape=[
            jax.ShapeDtypeStruct((total, width), jnp.float32),
            jax.ShapeDtypeStruct((total, width), jnp.bfloat16),
            jax.ShapeDtypeStruct((clips, 4, width), jnp.float32),
        ],
        scratch_shapes=[pltpu.VMEM((total, width), jnp.float32)],
        compiler_params=pltpu.CompilerParams(vmem_limit_bytes=vmem_bytes),
        cost_estimate=pl.CostEstimate(
            flops=8 * total * width * width, bytes_accessed=40 * total * width, transcendentals=0
        ),
    )(counts, d_pre, blocks, mods, resid, cotangent, proj)


def attention_back_kernel(
    frames, counts, d_proj, parts, block, d_qkv, sums, d_mixed, d_query, d_key, d_value
):
    rows, width = d_proj.shape
    tile = min(rows, 128)
    count = counts[pl.program_id(0)]
    source = d_proj[...]
    for low, high in column_cuts(width):
        d_mixed[:, low:high] = narrow(dot_nt(source, block[0, low:high, :]))
    scale = (width // HEADS) ** -0.5
    offset = score_offset(count, tile, frames, 0)
    for ref in (d_query, d_key, d_value):
        ref[...] = jnp.zeros_like(ref)
    for first in range(0, rows, tile):
        span = slice(first, first + tile)
        for low, high, start, stop in head_windows(width):
            lanes = slice(start, stop)
            mask = lane_mask(low, high, stop - start, jnp.bfloat16)
            query_high = parts[0, span, lanes] * mask
            key_high = parts[2, span, lanes] * mask
            back = d_mixed[span, lanes] * mask
            scores = dot_nt(key_high, query_high)
            scores += dot_nt(key_high, parts[1, span, lanes])
            scores += dot_nt(parts[3, span, lanes], query_high) + offset
            expons = jnp.exp(scores - jnp.max(scores, axis=0, keepdims=True))
            probs = expons * (1.0 / jnp.sum(expons, axis=0, keepdims=True))
            d_probs = dot_nt(parts[4, span, lanes], back)
            inner = jnp.sum(d_probs * probs, axis=0, keepdims=True)
            d_scores = narrow(probs * (d_probs - inner))
            d_value[span, lanes] += dot_nn(narrow(probs), back)
            d_key[span, lanes] += dot_nn(d_scores, query_high)
            d_query[span, lanes] += dot_tn(d_scores, key_high)
    for at, ref in enumerate((d_query, d_key, d_value)):
        low_back = narrow(ref[...] * scale) if at == 0 else narrow(ref[...])
        d_qkv[at] = low_back
        sums[0, at : at + 1, :] = column_sum(wide(low_back))
    d_qkv[3] = source


def run_attention_back(frames, counts, d_proj, parts, block):
    total, width = d_proj.shape
    clips = counts.shape[0]
    rows = total // clips
    return pl.pallas_call(
        functools.partial(attention_back_kernel, frames),
        grid=(clips,),
        in_specs=[
            pl.BlockSpec(memory_space=pltpu.SMEM),
            spec((rows, width), lambda clip: (clip, 0)),
            spec((5, rows, width), lambda clip: (0, clip, 0)),
            spec((1, width, width), lambda clip: (3, 0, 0), pipeline_mode=pl.Buffered(1)),
        ],
        out_specs=[
            spec((4, rows, width), lambda clip: (0, clip, 0)),
            spec((1, 3, width), lambda clip: (clip, 0, 0)),
        ],
        out_shape=[
            jax.ShapeDtypeStruct((4, total, width), jnp.bfloat16),
            jax.ShapeDtypeStruct((clips, 3, width), jnp.float32),
        ],
        scratch_shapes=[pltpu.VMEM((rows, width), jnp.bfloat16)]
        + [pltpu.VMEM((rows, width), jnp.float32)] * 3,
        compiler_params=pltpu.CompilerParams(vmem_limit_bytes=vmem_bytes),
        cost_estimate=pl.CostEstimate(
            flops=12 * total * width * width, bytes_accessed=20 * total * width, transcendentals=0
        ),
    )(counts, d_proj, parts, block)


def input_kernel(d_qkv, block, mods, tokens, d_resid, input_grad, sums, total_grad):
    step, steps = pl.program_id(0), pl.num_programs(0)
    total, width = tokens.shape
    clips = mods.shape[0]
    rows = total // clips
    tile = min(rows, 128)
    source = d_qkv[0]

    @pl.when(step == 0)
    def _():
        total_grad[...] = jnp.zeros_like(total_grad)

    for low, high in column_cuts(width):
        span = slice(low, high)
        total_grad[:, span] += dot_nt(source, block[0, span, :])

    @pl.when(step == steps - 1)
    def _():
        for clip in range(clips):
            scale_one = mods[clip, 1:2, :]
            found = [0.0] * 2
            for first in range(clip * rows, (clip + 1) * rows, tile):
                span = slice(first, first + tile)
                grad = total_grad[span]
                normed, inverse = norm_parts(wide(tokens[span]))
                back = norm_back(grad * (1.0 + scale_one), normed, inverse)
                input_grad[span] = narrow(d_resid[span] + back)
                terms = (grad, grad * normed)
                found = [old + column_sum(term) for old, term in zip(found, terms)]
            for at in range(2):
                sums[clip, at : at + 1, :] = found[at]


def run_input(d_qkv, blocks, mods, tokens, d_resid):
    total, width = tokens.shape
    clips = mods.shape[0]
    return pl.pallas_call(
        input_kernel,
        grid=(3,),
        in_specs=[
            spec((1, total, width), lambda at: (at, 0, 0)),
            spec((1, width, width), lambda at: (at, 0, 0)),
            held(mods.shape),
            held((total, width)),
            held((total, width)),
        ],
        out_specs=[held((total, width)), held((clips, 2, width))],
        out_shape=[
            jax.ShapeDtypeStruct((total, width), jnp.bfloat16),
            jax.ShapeDtypeStruct((clips, 2, width), jnp.float32),
        ],
        scratch_shapes=[pltpu.VMEM((total, width), jnp.float32)],
        compiler_params=pltpu.CompilerParams(vmem_limit_bytes=vmem_bytes),
        cost_estimate=pl.CostEstimate(
            flops=6 * total * width * width, bytes_accessed=30 * total * width, transcendentals=0
        ),
    )(d_qkv, blocks, mods, tokens, d_resid)


def tie(*values):
    return lax.optimization_barrier(values)


def packed(arrays, tile):
    flat = jnp.concatenate([array.reshape(-1) for array in arrays])
    return jnp.pad(flat, (0, -flat.shape[0] % (tile * 128))).reshape(-1, 128)


def core_swap(array):
    count = lax.axis_size("dp")
    return lax.ppermute(array, "dp", [(at, at ^ 1) for at in range(count)])


def chip_shift(array, step):
    count = lax.axis_size("dp")
    return lax.ppermute(array, "dp", [(at, (at + 2 * step) % count) for at in range(count)])


def rank_swap(array, bits):
    count = lax.axis_size("fsdp")
    return lax.ppermute(array, "fsdp", [(at, at ^ bits) for at in range(count)])


def entry(array, at, axis=0):
    return lax.dynamic_index_in_dim(array, at, axis, keepdims=False)


def place_kernel(count, at, *refs):
    parts, whole, semaphores = refs[:count], refs[count], refs[count + 1]
    copies = []
    for index, part in enumerate(parts):
        rows = part.shape[0]
        first = pl.multiple_of(at[index] * 16, 16)
        copies.append(
            pltpu.make_async_copy(part, whole.at[pl.ds(first, rows)], semaphores.at[index])
        )
        copies[-1].start()
    for copy in copies:
        copy.wait()


def place(parts, starts, rows):
    width = parts[0].shape[-1]
    return pl.pallas_call(
        functools.partial(place_kernel, len(parts)),
        in_specs=[pl.BlockSpec(memory_space=pltpu.SMEM)]
        + [pl.BlockSpec(memory_space=pl.ANY)] * len(parts),
        out_specs=pl.BlockSpec(memory_space=pl.ANY),
        out_shape=jax.ShapeDtypeStruct((rows, width), parts[0].dtype),
        scratch_shapes=[pltpu.SemaphoreType.DMA((len(parts),))],
        cost_estimate=pl.CostEstimate(
            flops=0, bytes_accessed=4 * rows * width, transcendentals=0
        ),
    )(jnp.stack([jnp.asarray(start, jnp.int32) for start in starts]), *parts)


def own_rows(parts, group):
    ranks, at = lax.axis_size("fsdp"), lax.axis_index("fsdp")
    shares = ranks // group
    row_part, col_part = parts.shape[1:]
    chunk = row_part // shares
    split = parts.reshape(ranks, chunk, col_part)
    if shares > 1:
        moved = lax.all_to_all(split, "fsdp", 0, 0, tiled=True)
        return moved.transpose(1, 0, 2).reshape(chunk, ranks * col_part)
    panels = [entry(split, at)]
    panels += [rank_swap(entry(split, at ^ bits), bits) for bits in range(1, ranks)]
    placed = [
        lax.select_n(at, *[panels[panel ^ index] for index in range(ranks)])
        for panel in range(ranks)
    ]
    return jnp.concatenate(placed, axis=1)


def shard_rows(rows, group):
    ranks = lax.axis_size("fsdp")
    shares = ranks // group
    count, chunk, total = rows.shape
    col_part = total // ranks
    split = rows.reshape(count, chunk, ranks, col_part).transpose(2, 0, 1, 3)
    moved = lax.all_to_all(split, "fsdp", 0, 0, tiled=True)
    moved = moved.reshape(group, shares, count, chunk, col_part).transpose(2, 0, 1, 3, 4)
    return moved.reshape(count * group, shares * chunk, col_part)


def gather_blocks(rows, group):
    ranks, dp_count = lax.axis_size("fsdp"), lax.axis_size("dp")
    shares = ranks // group
    chunk, total = rows.shape
    all_rows = lax.all_gather(rows, ("fsdp", "dp"), axis=0, tiled=True)
    if shares > 1:
        all_rows = all_rows.reshape(group, shares, dp_count, chunk, total).transpose(0, 2, 1, 3, 4)
    return all_rows.reshape(group, total, total)


def gather_pieces(rows, group):
    ranks, at = lax.axis_size("fsdp"), lax.axis_index("fsdp")
    if ranks != group:
        blocks = gather_blocks(rows, group)
        (blocks,) = yield (blocks,)
        yield blocks
        return
    chips = lax.axis_size("dp") // 2
    core, chip = lax.axis_index("dp") % 2, lax.axis_index("dp") // 2
    chunk, total = rows.shape
    half = total // 2
    unit = chunk // 16
    found = [rows] + [chip_shift(rows, step) for step in range(1, chips)]
    line = place(found, [(chip - step) % chips * unit for step in range(chips)], half)
    other = core_swap(line)
    pairs = [part[step * chunk : (step + 1) * chunk] for part in (line, other) for step in range(chips)]
    starts = [(2 * step + side) * unit for side in (core, 1 - core) for step in range(chips)]
    own = place(pairs, starts, total)
    share = lax.dynamic_slice_in_dim(own, core * half, half, 0)
    mine = [rank_swap(share, bits) for bits in range(1, ranks)]
    own, *mine = yield (own, *mine)
    others = [core_swap(part) for part in mine]
    starts = [at * 2] + [
        (at ^ bits) * 2 + side for side in (core, 1 - core) for bits in range(1, ranks)
    ]
    starts = [start * (half // 16) for start in starts]
    yield place([own] + mine + others, starts, group * total).reshape(group, total, total)


def gather_own(rows, group):
    ranks = lax.axis_size("fsdp")
    shares = ranks // group
    chunk, total = rows.shape
    if shares > 1:
        sets = [[share + shares * block for share in range(shares)] for block in range(group)]
        rows = lax.all_gather(rows, "fsdp", axis=0, tiled=True, axis_index_groups=sets)
    return lax.all_gather(rows, "dp", axis=0, tiled=True)


def sum_blocks(product, cut, total, group):
    ranks, dp_count = lax.axis_size("fsdp"), lax.axis_size("dp")
    shares = ranks // group
    if shares > 1:
        blocks = narrow(product(cut(0, total)))
        chunk = total // (dp_count * shares)
        blocks = blocks.reshape(group, dp_count, shares, chunk, -1).transpose(0, 2, 1, 3, 4)
        rows = lax.psum_scatter(
            blocks.reshape(group * total, -1), ("fsdp", "dp"), scatter_dimension=0, tiled=True
        )
        for _ in range(3):
            (rows,) = yield (rows,)
        yield gather_own(rows, group)
        return
    chips, half = dp_count // 2, total // 2
    chunk = half // chips
    core, chip = lax.axis_index("dp") % 2, lax.axis_index("dp") // 2
    low_bit, high_bit = lax.axis_index("fsdp") % 2, lax.axis_index("fsdp") // 2
    away = narrow(product(cut((1 - core) * half, half)))
    here = product(cut(core * half, half))
    here = narrow(here + wide(core_swap(away)))
    here = here.reshape(2, 2, chips, chunk, -1)
    middle = chips // 2
    first, second = here[:, :, :middle], here[:, :, middle:]
    first_in = rank_swap(entry(first, 1 - low_bit, 1), 1)
    second_in = rank_swap(entry(second, 1 - high_bit, 0), 2)
    here, first_in, second_in = yield (here, first_in, second_in)
    first, second = here[:, :, :middle], here[:, :, middle:]
    first = narrow(wide(entry(first, low_bit, 1)) + wide(first_in))
    second = narrow(wide(entry(second, high_bit, 0)) + wide(second_in))
    first_in = rank_swap(entry(first, 1 - high_bit), 2)
    second_in = rank_swap(entry(second, 1 - low_bit), 1)
    first, second, first_in, second_in = yield (first, second, first_in, second_in)
    first = narrow(wide(entry(first, high_bit)) + wide(first_in))
    second = narrow(wide(entry(second, low_bit)) + wide(second_in))
    line = jnp.concatenate([first, second])
    parts = [entry(line, chip)]
    parts += [chip_shift(entry(line, (chip + step) % chips), step) for step in range(1, chips)]
    parts = yield tuple(parts)
    rows = sum(wide(part) for part in parts)
    found = lax.all_gather(narrow(rows), "dp", axis=0, tiled=True)
    yield found.reshape(chips, 2, chunk, -1).transpose(1, 0, 2, 3).reshape(total, -1)


def fast_dot(subscripts, left, right):
    return jnp.einsum(subscripts, left, right, preferred_element_type=jnp.float32)


def owned_step(whole, left_root, right_root, group):
    chunk = left_root.shape[0]
    shares = lax.axis_size("fsdp") // group
    first = lax.axis_index("dp") * (chunk * shares) + lax.axis_index("fsdp") % shares * chunk
    grad_rows = lax.dynamic_slice_in_dim(whole, first, chunk, 0)
    own_columns = lax.dynamic_slice_in_dim(whole, first, chunk, 1)
    outer = fast_dot("rk,jk->rj", grad_rows, whole)
    inner = fast_dot("kr,kj->rj", own_columns, whole)
    side = fast_dot("rk,kj->rj", left_root, whole)
    side_high = narrow(side)
    side_low = narrow(side - wide(side_high))
    precond = fast_dot("rk,kj->rj", side_high, right_root) + fast_dot(
        "rk,kj->rj", side_low, right_root
    )
    return narrow(jnp.stack([precond, outer, inner]))


def per_device(
    tokens,
    conditioning,
    frame_counts,
    cotangent,
    weights,
    biases,
    momentum,
    left_stats,
    right_stats,
    left_roots,
    right_roots,
    bias_moment,
    bias_second,
):
    group = 4
    mod_count = 6
    clip_count, pos_count, frames, width = tokens.shape
    token_count = clip_count * pos_count * frames
    block_count, row_part, col_part = weights.shape
    dp_count, ranks = lax.axis_size("dp"), lax.axis_size("fsdp")
    dp_at, rank_at = lax.axis_index("dp"), lax.axis_index("fsdp")
    all_clips = clip_count * dp_count
    bias_part = biases.shape[0]
    stream = tokens.reshape(token_count, width)
    grad_out = cotangent.reshape(token_count, width)
    pieces = [slice(mod_count + group * piece, mod_count + group * (piece + 1)) for piece in range(3)]

    attn_rows = own_rows(narrow(weights[pieces[0]]), group)
    cond_low = narrow(jax.nn.silu(conditioning))
    attn_rows, one_shard, two_shard, cond_low = tie(
        attn_rows, weights[pieces[1]], weights[pieces[2]], cond_low
    )
    attn_w = gather_blocks(attn_rows, group)
    two_w = gather_blocks(own_rows(narrow(two_shard), group), group)
    one_steps = gather_pieces(own_rows(narrow(one_shard), group), group)
    one_parts = next(one_steps)

    first_parts = lax.all_gather(
        packed([cond_low, narrow(biases)], 16), "dp", axis=0, tiled=True
    ).reshape(dp_count, -1)
    cond_all = first_parts[:, : clip_count * width].reshape(all_clips, width)
    bias_rows = wide(first_parts[:, clip_count * width : clip_count * width + bias_part])
    cond_rows = lax.dynamic_slice_in_dim(cond_all, dp_at * row_part, row_part, 1)
    cond_cols = wide(lax.dynamic_slice_in_dim(cond_all, rank_at * col_part, col_part, 1))
    mod_parts = fast_dot("cr,jre->cje", cond_rows, narrow(weights[:mod_count]))
    mod_parts = lax.all_to_all(mod_parts, "dp", 0, 0, tiled=True)
    mod_cols = jnp.sum(mod_parts.reshape(dp_count, clip_count, mod_count, col_part), axis=0)
    left_cond = jnp.einsum("jrk,ck->jrc", left_roots[:mod_count], cond_cols, precision=precise)
    mod_size, bias_size = mod_cols.size, dp_count * bias_part
    second_parts = lax.all_gather(
        packed([mod_cols, bias_rows, left_cond], 8), "fsdp", axis=0, tiled=True
    ).reshape(ranks, -1)
    mods = second_parts[:, :mod_size].reshape(ranks, clip_count, mod_count, col_part)
    mods = mods.transpose(1, 2, 0, 3).reshape(clip_count, mod_count, width)
    bias_all = second_parts[:, mod_size : mod_size + bias_size].reshape(ranks, dp_count, bias_part)
    bias_all = bias_all.transpose(1, 0, 2).reshape(-1, width)
    left_size = mod_size + bias_size + left_cond.size
    left_cond = jnp.sum(second_parts[:, mod_size + bias_size : left_size], axis=0)
    left_cond = left_cond.reshape(mod_count, row_part, all_clips)
    mods = mods + bias_all[:mod_count]
    bias_table = jnp.concatenate(
        [bias_all[6:7], jnp.zeros((1, width), jnp.float32), bias_all[7:14]]
    )

    attn_in, parts, mixed, proj, resid, mlp_in, d_branch, d_branch_sums = run_attention(
        frames, frame_counts, stream, grad_out, mods, bias_table, attn_w
    )
    left_rows = [own_rows(narrow(left_roots[piece]), group) for piece in pieces]
    right_wholes = [gather_own(own_rows(narrow(right_roots[piece]), group), group) for piece in pieces]
    mlp_in, one_parts = tie(mlp_in, one_parts)
    one_w = one_steps.send(one_parts)
    hidden, slope = run_hidden(mlp_in, one_w, bias_table[4:8, None])
    two_steps = sum_blocks(
        lambda left: fast_dot("jtd,te->jde", left, d_branch),
        lambda first, size: lax.dynamic_slice_in_dim(hidden, first, size, 2),
        width,
        group,
    )
    two_parts = list(next(two_steps))
    hidden, two_parts[0] = tie(hidden, two_parts[0])

    d_pre, d_pre_sums, block_out, d_gate_two = run_branch(
        frames,
        frame_counts,
        hidden,
        slope,
        two_w,
        d_branch,
        bias_table[8:9],
        mods[:, 5:6],
        resid,
        grad_out,
    )
    d_pre, two_parts = tie(d_pre, two_parts)
    two_parts = list(two_steps.send(two_parts))
    one_steps = sum_blocks(
        lambda left: fast_dot("td,jte->jde", left, d_pre),
        lambda first, size: lax.dynamic_slice_in_dim(mlp_in, first, size, 1),
        width,
        group,
    )
    one_parts = list(next(one_steps))
    d_pre, one_parts[0], two_parts = tie(d_pre, one_parts[0], two_parts)
    two_parts = two_steps.send(two_parts)
    d_resid, d_proj, resid_sums = run_resid(
        frames, frame_counts, d_pre, one_w, mods, resid, grad_out, proj
    )
    d_proj, one_parts = tie(d_proj, one_parts)
    one_parts = one_steps.send(one_parts)
    d_heads, head_sums = run_attention_back(frames, frame_counts, d_proj, parts, attn_w)
    d_heads, one_parts, two_parts, right_wholes[2] = tie(
        d_heads, one_parts, two_parts, right_wholes[2]
    )
    whole_two = two_steps.send(two_parts)
    attn_steps = sum_blocks(
        lambda left: fast_dot("jtd,jte->jde", left, d_heads),
        lambda first, size: jnp.stack(
            [lax.dynamic_slice_in_dim(left, first, size, 1) for left in (attn_in,) * 3 + (mixed,)]
        ),
        width,
        group,
    )
    attn_parts = list(next(attn_steps))
    d_heads, attn_parts[0], one_parts = tie(d_heads, attn_parts[0], one_parts)
    one_parts = one_steps.send(one_parts)
    input_grad, input_sums = run_input(d_heads, attn_w, mods, stream, d_resid)
    input_sums, attn_parts, one_parts = tie(input_sums, attn_parts, one_parts)
    attn_parts = attn_steps.send(attn_parts)
    whole_one = one_steps.send(one_parts)

    d_mods = jnp.stack(
        [
            input_sums[:, 0],
            input_sums[:, 1],
            resid_sums[:, 2],
            resid_sums[:, 0],
            resid_sums[:, 1],
            d_gate_two[:, 0],
        ],
        axis=1,
    )
    head_sums = jnp.sum(head_sums, axis=0)
    grad_bias = jnp.concatenate(
        [
            jnp.sum(d_mods, axis=0),
            head_sums[0:1],
            head_sums[2:3],
            jnp.sum(resid_sums[:, 3], axis=0)[None],
            d_pre_sums[:, 0],
            jnp.sum(d_branch_sums, axis=0),
        ]
    )
    to_ranks = jnp.concatenate(
        [
            d_mods.reshape(clip_count, mod_count, ranks, col_part)
            .transpose(2, 0, 1, 3)
            .reshape(ranks, mod_size),
            grad_bias.reshape(dp_count, ranks, bias_part)
            .transpose(1, 0, 2)
            .reshape(ranks, bias_size),
        ],
        axis=1,
    )
    rank_sums = jnp.sum(lax.all_to_all(to_ranks, "fsdp", 0, 0, tiled=True), axis=0)
    to_rows = jnp.concatenate(
        [
            jnp.broadcast_to(rank_sums[None, :mod_size], (dp_count, mod_size)),
            rank_sums[mod_size:].reshape(dp_count, bias_part),
        ],
        axis=1,
    )
    from_rows = lax.all_to_all(to_rows, "dp", 0, 0, tiled=True)
    products_two = owned_step(whole_two, left_rows[2], right_wholes[2], group)
    from_rows, products_two, attn_parts = tie(from_rows, products_two, attn_parts)
    attn_parts = attn_steps.send(attn_parts)
    back_two = shard_rows(products_two, group)
    bias_grad = jnp.sum(from_rows[:, mod_size:], axis=0)
    mod_grad_cols = from_rows[:, :mod_size].reshape(all_clips, mod_count, col_part)
    mod_grad = lax.all_gather(packed([mod_grad_cols], 8), "fsdp", axis=0, tiled=True)
    mod_grad = mod_grad.reshape(ranks, -1)[:, : mod_grad_cols.size]
    mod_grad = mod_grad.reshape(ranks, all_clips, mod_count, col_part).transpose(1, 2, 0, 3)
    mod_grad = mod_grad.reshape(all_clips, mod_count, width)

    mod_grad_rows = lax.dynamic_slice_in_dim(mod_grad, dp_at * row_part, row_part, 2)
    right_parts = jnp.einsum(
        "cjk,jke->cje", mod_grad_rows, right_roots[:mod_count], precision=precise
    )
    cond_wide = wide(cond_all)
    cond_row_wide = wide(cond_rows)
    mod_gram = jnp.einsum("cjk,bjk->jcb", mod_grad, mod_grad, precision=precise)
    cond_gram = jnp.einsum("ck,bk->cb", cond_wide, cond_wide, precision=precise)
    mod_side = jnp.einsum("jcb,be->jce", mod_gram, cond_cols, precision=precise)
    ada_left = jnp.einsum("cr,jce->jre", cond_row_wide, mod_side, precision=precise)
    cond_side = jnp.einsum("cb,bje->jce", cond_gram, mod_grad_cols, precision=precise)
    ada_right = jnp.einsum("cjr,jce->jre", mod_grad_rows, cond_side, precision=precise)

    products_one = owned_step(whole_one, left_rows[1], right_wholes[1], group)
    products_one, right_parts, attn_parts = tie(products_one, right_parts, attn_parts)
    whole_attn = attn_steps.send(attn_parts)
    back_one = shard_rows(products_one, group)
    right_parts = lax.all_gather(packed([right_parts], 8), "dp", axis=0, tiled=True)
    mod_right = jnp.sum(right_parts.reshape(dp_count, -1), axis=0)[: mod_grad_cols.size]
    mod_right = mod_right.reshape(all_clips, mod_count, col_part)
    ada_pre = jnp.einsum("jrc,cje->jre", left_cond, mod_right, precision=precise)
    back_attn = shard_rows(owned_step(whole_attn, left_rows[0], right_wholes[0], group), group)

    def joined(at, ada):
        span = slice(at * group, (at + 1) * group)
        return jnp.concatenate(
            [ada, wide(back_attn[span]), wide(back_one[span]), wide(back_two[span])]
        )

    precond = joined(0, ada_pre)
    left_new = stat_decay * left_stats + (1.0 - stat_decay) * joined(1, ada_left)
    right_new = stat_decay * right_stats + (1.0 - stat_decay) * joined(2, ada_right)
    momentum_new = moment_decay * momentum + precond
    weights_new = weights - weight_rate * momentum_new
    weights_copy = weights_new.astype(jnp.bfloat16)
    bias_second_new = stat_decay * bias_second + (1.0 - stat_decay) * bias_grad * bias_grad
    bias_moment_new = moment_decay * bias_moment + bias_grad * lax.rsqrt(
        bias_second_new + diag_epsilon
    )
    biases_new = biases - bias_rate * bias_moment_new
    return (
        block_out.reshape(tokens.shape),
        input_grad.reshape(tokens.shape),
        left_new,
        right_new,
        momentum_new,
        weights_new,
        weights_copy,
        bias_moment_new,
        bias_second_new,
        biases_new,
    )


def solution(mesh):
    placed = (
        P("dp", "fsdp", None, None),
        P("dp", None),
        P("dp"),
        P("dp", "fsdp", None, None),
        P(None, "dp", "fsdp"),
        P(("dp", "fsdp")),
        P(None, "dp", "fsdp"),
        P(None, "dp", "fsdp"),
        P(None, "dp", "fsdp"),
        P(None, "dp", "fsdp"),
        P(None, "dp", "fsdp"),
        P(("dp", "fsdp")),
        P(("dp", "fsdp")),
    )
    return jax.shard_map(
        per_device,
        mesh=mesh,
        in_specs=placed,
        out_specs=(
            P("dp", "fsdp", None, None),
            P("dp", "fsdp", None, None),
            P(None, "dp", "fsdp"),
            P(None, "dp", "fsdp"),
            P(None, "dp", "fsdp"),
            P(None, "dp", "fsdp"),
            P(None, "dp", "fsdp"),
            P(("dp", "fsdp")),
            P(("dp", "fsdp")),
            P(("dp", "fsdp")),
        ),
        check_vma=False,
    )
```

```python
import functools
import math

import jax
import jax.numpy as jnp
from jax import lax
from jax.experimental import pallas as pl
from jax.experimental.pallas import tpu as pltpu
from jax.sharding import PartitionSpec as P

HEADS = 16


precise = lax.Precision.HIGHEST
norm_epsilon = 1e-06
masked_score = -1e30
stat_decay = 0.5
moment_decay = 0.9
weight_rate = 0.7
bias_rate = 0.1
diag_epsilon = 1e-08
vmem_bytes = 50 * 2**20


def narrow(array):
    return array.astype(jnp.bfloat16)


def wide(array):
    return array.astype(jnp.float32)


def spec(shape, index_map, **keywords):
    return pl.BlockSpec(shape, index_map, **keywords)


def held(shape):
    return pl.BlockSpec(shape, lambda step: (0,) * len(shape), pipeline_mode=pl.Buffered(1))


def column_cuts(total):
    cuts, at = [], 0
    while at < total:
        cuts.append((at, min(total, at + 256)))
        at += 256
    return cuts


def dot_nn(left, right):
    return lax.dot_general(left, right, (((1,), (0,)), ((), ())), preferred_element_type=jnp.float32)


def dot_nt(left, right):
    return lax.dot_general(left, right, (((1,), (1,)), ((), ())), preferred_element_type=jnp.float32)


def dot_tn(left, right):
    return lax.dot_general(left, right, (((0,), (0,)), ((), ())), preferred_element_type=jnp.float32)


def split_high(values):
    high = narrow(values)
    return high, narrow(values - wide(high))


def valid_rows(count, rows, frames):
    at = lax.broadcasted_iota(jnp.int32, (rows, 1), 0)
    return (lax.rem(at, frames) < count).astype(jnp.float32)


def score_offset(count, size, frames, key_axis):
    first = lax.broadcasted_iota(jnp.int32, (size, size), 0)
    second = lax.broadcasted_iota(jnp.int32, (size, size), 1)
    key = second if key_axis == 1 else first
    met = (lax.div(first, frames) == lax.div(second, frames)) & (lax.rem(key, frames) < count)
    return jnp.where(met, 0.0, masked_score)


def head_windows(width):
    size = width // HEADS
    windows = []
    for head in range(HEADS):
        low, high = head * size, (head + 1) * size
        start = low // 128 * 128
        stop = min(width, -(-high // 128) * 128)
        windows.append((low - start, high - start, start, stop))
    return windows


def lane_mask(low, high, count, dtype):
    lanes = lax.broadcasted_iota(jnp.int32, (1, count), 1)
    return ((lanes >= low) & (lanes < high)).astype(jnp.float32).astype(dtype)


def norm_parts(values):
    centered = values - jnp.mean(values, axis=-1, keepdims=True)
    variance = jnp.mean(centered * centered, axis=-1, keepdims=True)
    inverse = lax.rsqrt(variance + norm_epsilon)
    return centered * inverse, inverse


def norm_back(grad, normed, inverse):
    first = jnp.mean(grad, axis=-1, keepdims=True)
    second = jnp.mean(grad * normed, axis=-1, keepdims=True)
    return (grad - first - normed * second) * inverse


def column_sum(values):
    return jnp.sum(values, axis=0, keepdims=True)


def attention_kernel(
    frames,
    counts,
    tokens,
    cotangent,
    mods,
    bias,
    blocks,
    attn_in,
    parts,
    mixed_low,
    proj_out,
    resid_out,
    mlp_in,
    d_branch,
    d_branch_sum,
    mixed,
):
    rows, width = tokens.shape
    tile = min(rows, 128)
    count = counts[pl.program_id(0)]
    shift_one, scale_one, gate_one = (mods[0, at : at + 1, :] for at in range(3))
    shift_two, scale_two, gate_two = (mods[0, at : at + 1, :] for at in range(3, 6))
    for first in range(0, rows, tile):
        span = slice(first, first + tile)
        normed, _ = norm_parts(wide(tokens[span]))
        attn_in[span] = narrow(normed * (1.0 + scale_one) + shift_one)
        branch_back = narrow(wide(cotangent[span]) * valid_rows(count, tile, frames) * gate_two)
        d_branch[span] = branch_back
        part_sum = column_sum(wide(branch_back))
        d_branch_sum[0] = part_sum if first == 0 else d_branch_sum[0] + part_sum
    scale = (width // HEADS) ** -0.5
    source = attn_in[...]
    for low, high in column_cuts(width):
        span = slice(low, high)
        query = (dot_nn(source, blocks[0, :, span]) + bias[0:1, span]) * scale
        parts[0, :, span], parts[1, :, span] = split_high(query)
        parts[2, :, span], parts[3, :, span] = split_high(dot_nn(source, blocks[1, :, span]))
        parts[4, :, span] = narrow(dot_nn(source, blocks[2, :, span]) + bias[2:3, span])
    offset = score_offset(count, tile, frames, 1)
    mixed[...] = jnp.zeros_like(mixed)
    for first in range(0, rows, tile):
        span = slice(first, first + tile)
        for low, high, start, stop in head_windows(width):
            lanes = slice(start, stop)
            mask = lane_mask(low, high, stop - start, jnp.bfloat16)
            key_high = parts[2, span, lanes]
            query_high = parts[0, span, lanes] * mask
            scores = dot_nt(query_high, key_high)
            scores += dot_nt(parts[1, span, lanes] * mask, key_high)
            scores += dot_nt(query_high, parts[3, span, lanes]) + offset
            expons = jnp.exp(scores - jnp.max(scores, axis=-1, keepdims=True))
            probs = expons * (1.0 / jnp.sum(expons, axis=-1, keepdims=True))
            out = dot_nn(narrow(probs), parts[4, span, lanes] * mask)
            mixed[span, lanes] += out
    mixed_low[...] = narrow(mixed[...])
    source = mixed_low[...]
    for low, high in column_cuts(width):
        span = slice(low, high)
        proj_out[:, span] = dot_nn(source, blocks[3, :, span]) + bias[3:4, span]
    for first in range(0, rows, tile):
        span = slice(first, first + tile)
        resid = wide(tokens[span]) + valid_rows(count, tile, frames) * gate_one * proj_out[span]
        resid_out[span] = resid
        normed, _ = norm_parts(resid)
        mlp_in[span] = narrow(normed * (1.0 + scale_two) + shift_two)


def run_attention(frames, counts, tokens, cotangent, mods, bias, blocks):
    total, width = tokens.shape
    clips = mods.shape[0]
    rows = total // clips
    clip_rows = spec((rows, width), lambda clip: (clip, 0))
    low = jax.ShapeDtypeStruct((total, width), jnp.bfloat16)
    full = jax.ShapeDtypeStruct((total, width), jnp.float32)
    return pl.pallas_call(
        functools.partial(attention_kernel, frames),
        grid=(clips,),
        in_specs=[
            pl.BlockSpec(memory_space=pltpu.SMEM),
            clip_rows,
            clip_rows,
            spec((1,) + mods.shape[1:], lambda clip: (clip, 0, 0)),
            held(bias.shape),
            held(blocks.shape),
        ],
        out_specs=[
            clip_rows,
            spec((5, rows, width), lambda clip: (0, clip, 0)),
            clip_rows,
            clip_rows,
            clip_rows,
            clip_rows,
            clip_rows,
            spec((1, 1, width), lambda clip: (clip, 0, 0)),
        ],
        out_shape=[
            low,
            jax.ShapeDtypeStruct((5, total, width), jnp.bfloat16),
            low,
            full,
            full,
            low,
            low,
            jax.ShapeDtypeStruct((clips, 1, width), jnp.float32),
        ],
        scratch_shapes=[pltpu.VMEM((rows, width), jnp.float32)],
        compiler_params=pltpu.CompilerParams(vmem_limit_bytes=vmem_bytes),
        cost_estimate=pl.CostEstimate(
            flops=12 * total * width * width, bytes_accessed=40 * total * width, transcendentals=0
        ),
    )(counts, tokens, cotangent, mods, bias, blocks)


def hidden_kernel(mlp_in, block, bias, hidden, slope):
    root = (2.0 / math.pi) ** 0.5
    source = mlp_in[...]
    for low, high in column_cuts(block.shape[-1]):
        span = slice(low, high)
        pre = dot_nn(source, block[0, :, span]) + bias[0, :, span]
        square = pre * pre
        bent = jnp.tanh(root * pre * (1.0 + 0.044715 * square))
        half = 0.5 + 0.5 * bent
        hidden[0, :, span] = narrow(pre * half)
        steep = (0.5 * root) * pre * (1.0 + 3 * 0.044715 * square)
        slope[0, :, span] = narrow(half + steep * (1.0 - bent * bent))


def run_hidden(mlp_in, blocks, bias):
    total, width = mlp_in.shape
    count = blocks.shape[0]
    per_block = spec((1, total, width), lambda at: (at, 0, 0))
    out = jax.ShapeDtypeStruct((count, total, width), jnp.bfloat16)
    return pl.pallas_call(
        hidden_kernel,
        grid=(count,),
        in_specs=[
            held(mlp_in.shape),
            spec((1, width, width), lambda at: (at, 0, 0)),
            spec((1, 1, width), lambda at: (at, 0, 0)),
        ],
        out_specs=[per_block, per_block],
        out_shape=[out, out],
        compiler_params=pltpu.CompilerParams(vmem_limit_bytes=vmem_bytes),
        cost_estimate=pl.CostEstimate(
            flops=8 * total * width * width, bytes_accessed=30 * total * width, transcendentals=0
        ),
    )(mlp_in, blocks, bias)


def branch_kernel(
    frames,
    counts,
    hidden,
    slope,
    block,
    d_branch,
    bias,
    gates,
    resid,
    cotangent,
    d_pre,
    d_pre_sum,
    block_out,
    d_gate,
    branch,
):
    step, steps = pl.program_id(0), pl.num_programs(0)
    total, width = resid.shape
    clips = gates.shape[0]
    rows = total // clips
    source, back = hidden[0], d_branch[...]

    @pl.when(step == 0)
    def _():
        branch[...] = jnp.zeros_like(branch)

    for low, high in column_cuts(width):
        span = slice(low, high)
        d_hidden = dot_nt(back, block[0, span, :])
        low_back = narrow(d_hidden * wide(slope[0, :, span]))
        d_pre[0, :, span] = low_back
        d_pre_sum[0, :, span] = column_sum(wide(low_back))
        branch[:, span] += dot_nn(source, block[0, :, span])

    @pl.when(step == steps - 1)
    def _():
        for clip in range(clips):
            span = slice(clip * rows, (clip + 1) * rows)
            kept = valid_rows(counts[clip], rows, frames) * (branch[span] + bias[...])
            block_out[span] = narrow(resid[span] + gates[clip] * kept)
            d_gate[clip] = column_sum(wide(cotangent[span]) * kept)


def run_branch(frames, counts, hidden, slope, blocks, d_branch, bias, gates, resid, cotangent):
    count, total, width = hidden.shape
    clips = gates.shape[0]
    per_block = spec((1, total, width), lambda at: (at, 0, 0))
    low = jax.ShapeDtypeStruct((total, width), jnp.bfloat16)
    return pl.pallas_call(
        functools.partial(branch_kernel, frames),
        grid=(count,),
        in_specs=[
            pl.BlockSpec(memory_space=pltpu.SMEM),
            per_block,
            per_block,
            spec((1, width, width), lambda at: (at, 0, 0)),
            held((total, width)),
            held(bias.shape),
            held(gates.shape),
            held((total, width)),
            held((total, width)),
        ],
        out_specs=[
            per_block,
            spec((1, 1, width), lambda at: (at, 0, 0)),
            held((total, width)),
            held((clips, 1, width)),
        ],
        out_shape=[
            jax.ShapeDtypeStruct((count, total, width), jnp.bfloat16),
            jax.ShapeDtypeStruct((count, 1, width), jnp.float32),
            low,
            jax.ShapeDtypeStruct((clips, 1, width), jnp.float32),
        ],
        scratch_shapes=[pltpu.VMEM((total, width), jnp.float32)],
        compiler_params=pltpu.CompilerParams(vmem_limit_bytes=vmem_bytes),
        cost_estimate=pl.CostEstimate(
            flops=16 * total * width * width, bytes_accessed=40 * total * width, transcendentals=0
        ),
    )(counts, hidden, slope, blocks, d_branch, bias, gates, resid, cotangent)


def resid_kernel(
    frames,
    counts,
    d_pre,
    block,
    mods,
    resid,
    cotangent,
    proj,
    d_resid_out,
    d_proj,
    sums,
    total_grad,
):
    step, steps = pl.program_id(0), pl.num_programs(0)
    total, width = resid.shape
    clips = mods.shape[0]
    rows = total // clips
    tile = min(rows, 128)
    source = d_pre[0]

    @pl.when(step == 0)
    def _():
        total_grad[...] = jnp.zeros_like(total_grad)

    for low, high in column_cuts(width):
        span = slice(low, high)
        total_grad[:, span] += dot_nt(source, block[0, span, :])

    @pl.when(step == steps - 1)
    def _():
        for clip in range(clips):
            gate_one, scale_two = mods[clip, 2:3, :], mods[clip, 4:5, :]
            found = [0.0] * 4
            for first in range(clip * rows, (clip + 1) * rows, tile):
                span = slice(first, first + tile)
                grad = total_grad[span]
                normed, inverse = norm_parts(resid[span])
                back = norm_back(grad * (1.0 + scale_two), normed, inverse)
                d_resid = wide(cotangent[span]) + back
                d_resid_out[span] = d_resid
                kept = valid_rows(counts[clip], tile, frames) * d_resid
                low_back = narrow(kept * gate_one)
                d_proj[span] = low_back
                terms = (grad, grad * normed, kept * proj[span], wide(low_back))
                found = [old + column_sum(term) for old, term in zip(found, terms)]
            for at in range(4):
                sums[clip, at : at + 1, :] = found[at]


def run_resid(frames, counts, d_pre, blocks, mods, resid, cotangent, proj):
    count, total, width = d_pre.shape
    clips = mods.shape[0]
    return pl.pallas_call(
        functools.partial(resid_kernel, frames),
        grid=(count,),
        in_specs=[
            pl.BlockSpec(memory_space=pltpu.SMEM),
            spec((1, total, width), lambda at: (at, 0, 0)),
            spec((1, width, width), lambda at: (at, 0, 0)),
            held(mods.shape),
            held((total, width)),
            held((total, width)),
            held((total, width)),
        ],
        out_specs=[held((total, width)), held((total, width)), held((clips, 4, width))],
        out_shape=[
            jax.ShapeDtypeStruct((total, width), jnp.float32),
            jax.ShapeDtypeStruct((total, width), jnp.bfloat16),
            jax.ShapeDtypeStruct((clips, 4, width), jnp.float32),
        ],
        scratch_shapes=[pltpu.VMEM((total, width), jnp.float32)],
        compiler_params=pltpu.CompilerParams(vmem_limit_bytes=vmem_bytes),
        cost_estimate=pl.CostEstimate(
            flops=8 * total * width * width, bytes_accessed=40 * total * width, transcendentals=0
        ),
    )(counts, d_pre, blocks, mods, resid, cotangent, proj)


def attention_back_kernel(
    frames, counts, d_proj, parts, block, d_qkv, sums, d_mixed, d_query, d_key, d_value
):
    rows, width = d_proj.shape
    tile = min(rows, 128)
    count = counts[pl.program_id(0)]
    source = d_proj[...]
    for low, high in column_cuts(width):
        d_mixed[:, low:high] = narrow(dot_nt(source, block[0, low:high, :]))
    scale = (width // HEADS) ** -0.5
    offset = score_offset(count, tile, frames, 0)
    for ref in (d_query, d_key, d_value):
        ref[...] = jnp.zeros_like(ref)
    for first in range(0, rows, tile):
        span = slice(first, first + tile)
        for low, high, start, stop in head_windows(width):
            lanes = slice(start, stop)
            mask = lane_mask(low, high, stop - start, jnp.bfloat16)
            query_high = parts[0, span, lanes] * mask
            key_high = parts[2, span, lanes] * mask
            back = d_mixed[span, lanes] * mask
            scores = dot_nt(key_high, query_high)
            scores += dot_nt(key_high, parts[1, span, lanes])
            scores += dot_nt(parts[3, span, lanes], query_high) + offset
            expons = jnp.exp(scores - jnp.max(scores, axis=0, keepdims=True))
            probs = expons * (1.0 / jnp.sum(expons, axis=0, keepdims=True))
            d_probs = dot_nt(parts[4, span, lanes], back)
            inner = jnp.sum(d_probs * probs, axis=0, keepdims=True)
            d_scores = narrow(probs * (d_probs - inner))
            d_value[span, lanes] += dot_nn(narrow(probs), back)
            d_key[span, lanes] += dot_nn(d_scores, query_high)
            d_query[span, lanes] += dot_tn(d_scores, key_high)
    for at, ref in enumerate((d_query, d_key, d_value)):
        low_back = narrow(ref[...] * scale) if at == 0 else narrow(ref[...])
        d_qkv[at] = low_back
        sums[0, at : at + 1, :] = column_sum(wide(low_back))
    d_qkv[3] = source


def run_attention_back(frames, counts, d_proj, parts, block):
    total, width = d_proj.shape
    clips = counts.shape[0]
    rows = total // clips
    return pl.pallas_call(
        functools.partial(attention_back_kernel, frames),
        grid=(clips,),
        in_specs=[
            pl.BlockSpec(memory_space=pltpu.SMEM),
            spec((rows, width), lambda clip: (clip, 0)),
            spec((5, rows, width), lambda clip: (0, clip, 0)),
            spec((1, width, width), lambda clip: (3, 0, 0), pipeline_mode=pl.Buffered(1)),
        ],
        out_specs=[
            spec((4, rows, width), lambda clip: (0, clip, 0)),
            spec((1, 3, width), lambda clip: (clip, 0, 0)),
        ],
        out_shape=[
            jax.ShapeDtypeStruct((4, total, width), jnp.bfloat16),
            jax.ShapeDtypeStruct((clips, 3, width), jnp.float32),
        ],
        scratch_shapes=[pltpu.VMEM((rows, width), jnp.bfloat16)]
        + [pltpu.VMEM((rows, width), jnp.float32)] * 3,
        compiler_params=pltpu.CompilerParams(vmem_limit_bytes=vmem_bytes),
        cost_estimate=pl.CostEstimate(
            flops=12 * total * width * width, bytes_accessed=20 * total * width, transcendentals=0
        ),
    )(counts, d_proj, parts, block)


def input_kernel(d_qkv, block, mods, tokens, d_resid, input_grad, sums, total_grad):
    step, steps = pl.program_id(0), pl.num_programs(0)
    total, width = tokens.shape
    clips = mods.shape[0]
    rows = total // clips
    tile = min(rows, 128)
    source = d_qkv[0]

    @pl.when(step == 0)
    def _():
        total_grad[...] = jnp.zeros_like(total_grad)

    for low, high in column_cuts(width):
        span = slice(low, high)
        total_grad[:, span] += dot_nt(source, block[0, span, :])

    @pl.when(step == steps - 1)
    def _():
        for clip in range(clips):
            scale_one = mods[clip, 1:2, :]
            found = [0.0] * 2
            for first in range(clip * rows, (clip + 1) * rows, tile):
                span = slice(first, first + tile)
                grad = total_grad[span]
                normed, inverse = norm_parts(wide(tokens[span]))
                back = norm_back(grad * (1.0 + scale_one), normed, inverse)
                input_grad[span] = narrow(d_resid[span] + back)
                terms = (grad, grad * normed)
                found = [old + column_sum(term) for old, term in zip(found, terms)]
            for at in range(2):
                sums[clip, at : at + 1, :] = found[at]


def run_input(d_qkv, blocks, mods, tokens, d_resid):
    total, width = tokens.shape
    clips = mods.shape[0]
    return pl.pallas_call(
        input_kernel,
        grid=(3,),
        in_specs=[
            spec((1, total, width), lambda at: (at, 0, 0)),
            spec((1, width, width), lambda at: (at, 0, 0)),
            held(mods.shape),
            held((total, width)),
            held((total, width)),
        ],
        out_specs=[held((total, width)), held((clips, 2, width))],
        out_shape=[
            jax.ShapeDtypeStruct((total, width), jnp.bfloat16),
            jax.ShapeDtypeStruct((clips, 2, width), jnp.float32),
        ],
        scratch_shapes=[pltpu.VMEM((total, width), jnp.float32)],
        compiler_params=pltpu.CompilerParams(vmem_limit_bytes=vmem_bytes),
        cost_estimate=pl.CostEstimate(
            flops=6 * total * width * width, bytes_accessed=30 * total * width, transcendentals=0
        ),
    )(d_qkv, blocks, mods, tokens, d_resid)


def tie(*values):
    return lax.optimization_barrier(values)


def packed(arrays, tile):
    flat = jnp.concatenate([array.reshape(-1) for array in arrays])
    return jnp.pad(flat, (0, -flat.shape[0] % (tile * 128))).reshape(-1, 128)


def core_swap(array):
    count = lax.axis_size("dp")
    return lax.ppermute(array, "dp", [(at, at ^ 1) for at in range(count)])


def chip_shift(array, step):
    count = lax.axis_size("dp")
    return lax.ppermute(array, "dp", [(at, (at + 2 * step) % count) for at in range(count)])


def rank_swap(array, bits):
    count = lax.axis_size("fsdp")
    return lax.ppermute(array, "fsdp", [(at, at ^ bits) for at in range(count)])


def entry(array, at, axis=0):
    return lax.dynamic_index_in_dim(array, at, axis, keepdims=False)


def place_kernel(count, at, *refs):
    parts, whole, held_rows, semaphores = refs[:count], refs[count], refs[count + 1], refs[count + 2]
    spans, loads, stores = [], [], []
    for index, part in enumerate(parts):
        first = pl.multiple_of(at[index] * 16, 16)
        spans.append(pl.ds(first, part.shape[0]))
        loads.append(
            pltpu.make_async_copy(part, held_rows.at[spans[index]], semaphores.at[0, index])
        )
        loads[index].start()
    for index in range(count):
        loads[index].wait()
        stores.append(
            pltpu.make_async_copy(
                held_rows.at[spans[index]], whole.at[spans[index]], semaphores.at[1, index]
            )
        )
        stores[index].start()
    for store in stores:
        store.wait()


def place(parts, starts, rows):
    width = parts[0].shape[-1]
    dtype = parts[0].dtype
    return pl.pallas_call(
        functools.partial(place_kernel, len(parts)),
        in_specs=[pl.BlockSpec(memory_space=pltpu.SMEM)]
        + [pl.BlockSpec(memory_space=pl.ANY)] * len(parts),
        out_specs=pl.BlockSpec(memory_space=pl.ANY),
        out_shape=jax.ShapeDtypeStruct((rows, width), dtype),
        scratch_shapes=[
            pltpu.VMEM((rows, width), dtype),
            pltpu.SemaphoreType.DMA((2, len(parts))),
        ],
        compiler_params=pltpu.CompilerParams(vmem_limit_bytes=vmem_bytes),
        cost_estimate=pl.CostEstimate(
            flops=0, bytes_accessed=4 * rows * width, transcendentals=0
        ),
    )(jnp.stack([jnp.asarray(start, jnp.int32) for start in starts]), *parts)


def own_rows(parts, group):
    ranks, at = lax.axis_size("fsdp"), lax.axis_index("fsdp")
    shares = ranks // group
    row_part, col_part = parts.shape[1:]
    chunk = row_part // shares
    split = parts.reshape(ranks, chunk, col_part)
    if shares > 1:
        moved = lax.all_to_all(split, "fsdp", 0, 0, tiled=True)
        return moved.transpose(1, 0, 2).reshape(chunk, ranks * col_part)
    panels = [entry(split, at)]
    panels += [rank_swap(entry(split, at ^ bits), bits) for bits in range(1, ranks)]
    placed = [
        lax.select_n(at, *[panels[panel ^ index] for index in range(ranks)])
        for panel in range(ranks)
    ]
    return jnp.concatenate(placed, axis=1)


def shard_rows(rows, group):
    ranks = lax.axis_size("fsdp")
    shares = ranks // group
    count, chunk, total = rows.shape
    col_part = total // ranks
    split = rows.reshape(count, chunk, ranks, col_part).transpose(2, 0, 1, 3)
    moved = lax.all_to_all(split, "fsdp", 0, 0, tiled=True)
    moved = moved.reshape(group, shares, count, chunk, col_part).transpose(2, 0, 1, 3, 4)
    return moved.reshape(count * group, shares * chunk, col_part)


def gather_blocks(rows, group):
    ranks, dp_count = lax.axis_size("fsdp"), lax.axis_size("dp")
    shares = ranks // group
    chunk, total = rows.shape
    all_rows = lax.all_gather(rows, ("fsdp", "dp"), axis=0, tiled=True)
    if shares > 1:
        all_rows = all_rows.reshape(group, shares, dp_count, chunk, total).transpose(0, 2, 1, 3, 4)
    return all_rows.reshape(group, total, total)


def gather_pieces(rows, group):
    ranks, at = lax.axis_size("fsdp"), lax.axis_index("fsdp")
    if ranks != group:
        blocks = gather_blocks(rows, group)
        (blocks,) = yield (blocks,)
        yield blocks
        return
    chips = lax.axis_size("dp") // 2
    core, chip = lax.axis_index("dp") % 2, lax.axis_index("dp") // 2
    chunk, total = rows.shape
    half = total // 2
    unit = chunk // 16
    found = [rows] + [chip_shift(rows, step) for step in range(1, chips)]
    line = place(found, [(chip - step) % chips * unit for step in range(chips)], half)
    other = core_swap(line)
    pairs = [part[step * chunk : (step + 1) * chunk] for part in (line, other) for step in range(chips)]
    starts = [(2 * step + side) * unit for side in (core, 1 - core) for step in range(chips)]
    own = place(pairs, starts, total)
    share = lax.dynamic_slice_in_dim(own, core * half, half, 0)
    mine = [rank_swap(share, bits) for bits in range(1, ranks)]
    own, *mine = yield (own, *mine)
    others = [core_swap(part) for part in mine]
    starts = [at * 2] + [
        (at ^ bits) * 2 + side for side in (core, 1 - core) for bits in range(1, ranks)
    ]
    starts = [start * (half // 16) for start in starts]
    yield place([own] + mine + others, starts, group * total).reshape(group, total, total)


def gather_own(rows, group):
    ranks = lax.axis_size("fsdp")
    shares = ranks // group
    chunk, total = rows.shape
    if shares > 1:
        sets = [[share + shares * block for share in range(shares)] for block in range(group)]
        rows = lax.all_gather(rows, "fsdp", axis=0, tiled=True, axis_index_groups=sets)
    return lax.all_gather(rows, "dp", axis=0, tiled=True)


def sum_blocks(product, cut, total, group):
    ranks, dp_count = lax.axis_size("fsdp"), lax.axis_size("dp")
    shares = ranks // group
    if shares > 1:
        blocks = narrow(product(cut(0, total)))
        chunk = total // (dp_count * shares)
        blocks = blocks.reshape(group, dp_count, shares, chunk, -1).transpose(0, 2, 1, 3, 4)
        rows = lax.psum_scatter(
            blocks.reshape(group * total, -1), ("fsdp", "dp"), scatter_dimension=0, tiled=True
        )
        for _ in range(3):
            (rows,) = yield (rows,)
        yield gather_own(rows, group)
        return
    chips, half = dp_count // 2, total // 2
    chunk = half // chips
    core, chip = lax.axis_index("dp") % 2, lax.axis_index("dp") // 2
    low_bit, high_bit = lax.axis_index("fsdp") % 2, lax.axis_index("fsdp") // 2
    away = narrow(product(cut((1 - core) * half, half)))
    here = product(cut(core * half, half))
    here = narrow(here + wide(core_swap(away)))
    here = here.reshape(2, 2, chips, chunk, -1)
    middle = chips // 2
    first, second = here[:, :, :middle], here[:, :, middle:]
    first_in = rank_swap(entry(first, 1 - low_bit, 1), 1)
    second_in = rank_swap(entry(second, 1 - high_bit, 0), 2)
    here, first_in, second_in = yield (here, first_in, second_in)
    first, second = here[:, :, :middle], here[:, :, middle:]
    first = narrow(wide(entry(first, low_bit, 1)) + wide(first_in))
    second = narrow(wide(entry(second, high_bit, 0)) + wide(second_in))
    first_in = rank_swap(entry(first, 1 - high_bit), 2)
    second_in = rank_swap(entry(second, 1 - low_bit), 1)
    first, second, first_in, second_in = yield (first, second, first_in, second_in)
    first = narrow(wide(entry(first, high_bit)) + wide(first_in))
    second = narrow(wide(entry(second, low_bit)) + wide(second_in))
    line = jnp.concatenate([first, second])
    parts = [entry(line, chip)]
    parts += [chip_shift(entry(line, (chip + step) % chips), step) for step in range(1, chips)]
    parts = yield tuple(parts)
    rows = sum(wide(part) for part in parts)
    found = lax.all_gather(narrow(rows), "dp", axis=0, tiled=True)
    yield found.reshape(chips, 2, chunk, -1).transpose(1, 0, 2, 3).reshape(total, -1)


def fast_dot(subscripts, left, right):
    return jnp.einsum(subscripts, left, right, preferred_element_type=jnp.float32)


def owned_step(whole, left_root, right_root, group):
    chunk = left_root.shape[0]
    shares = lax.axis_size("fsdp") // group
    first = lax.axis_index("dp") * (chunk * shares) + lax.axis_index("fsdp") % shares * chunk
    grad_rows = lax.dynamic_slice_in_dim(whole, first, chunk, 0)
    own_columns = lax.dynamic_slice_in_dim(whole, first, chunk, 1)
    outer = fast_dot("rk,jk->rj", grad_rows, whole)
    inner = fast_dot("kr,kj->rj", own_columns, whole)
    side = fast_dot("rk,kj->rj", left_root, whole)
    side_high = narrow(side)
    side_low = narrow(side - wide(side_high))
    precond = fast_dot("rk,kj->rj", side_high, right_root) + fast_dot(
        "rk,kj->rj", side_low, right_root
    )
    return narrow(jnp.stack([precond, outer, inner]))


def per_device(
    tokens,
    conditioning,
    frame_counts,
    cotangent,
    weights,
    biases,
    momentum,
    left_stats,
    right_stats,
    left_roots,
    right_roots,
    bias_moment,
    bias_second,
):
    group = 4
    mod_count = 6
    clip_count, pos_count, frames, width = tokens.shape
    token_count = clip_count * pos_count * frames
    block_count, row_part, col_part = weights.shape
    dp_count, ranks = lax.axis_size("dp"), lax.axis_size("fsdp")
    dp_at, rank_at = lax.axis_index("dp"), lax.axis_index("fsdp")
    all_clips = clip_count * dp_count
    bias_part = biases.shape[0]
    stream = tokens.reshape(token_count, width)
    grad_out = cotangent.reshape(token_count, width)
    pieces = [slice(mod_count + group * piece, mod_count + group * (piece + 1)) for piece in range(3)]

    attn_rows = own_rows(narrow(weights[pieces[0]]), group)
    cond_low = narrow(jax.nn.silu(conditioning))
    attn_rows, one_shard, two_shard, cond_low = tie(
        attn_rows, weights[pieces[1]], weights[pieces[2]], cond_low
    )
    attn_w = gather_blocks(attn_rows, group)
    two_w = gather_blocks(own_rows(narrow(two_shard), group), group)
    one_steps = gather_pieces(own_rows(narrow(one_shard), group), group)
    one_parts = next(one_steps)

    first_parts = lax.all_gather(
        packed([cond_low, narrow(biases)], 16), "dp", axis=0, tiled=True
    ).reshape(dp_count, -1)
    cond_all = first_parts[:, : clip_count * width].reshape(all_clips, width)
    bias_rows = wide(first_parts[:, clip_count * width : clip_count * width + bias_part])
    cond_rows = lax.dynamic_slice_in_dim(cond_all, dp_at * row_part, row_part, 1)
    cond_cols = wide(lax.dynamic_slice_in_dim(cond_all, rank_at * col_part, col_part, 1))
    mod_parts = fast_dot("cr,jre->cje", cond_rows, narrow(weights[:mod_count]))
    mod_parts = lax.all_to_all(mod_parts, "dp", 0, 0, tiled=True)
    mod_cols = jnp.sum(mod_parts.reshape(dp_count, clip_count, mod_count, col_part), axis=0)
    left_cond = jnp.einsum("jrk,ck->jrc", left_roots[:mod_count], cond_cols, precision=precise)
    mod_size, bias_size = mod_cols.size, dp_count * bias_part
    second_parts = lax.all_gather(
        packed([mod_cols, bias_rows, left_cond], 8), "fsdp", axis=0, tiled=True
    ).reshape(ranks, -1)
    mods = second_parts[:, :mod_size].reshape(ranks, clip_count, mod_count, col_part)
    mods = mods.transpose(1, 2, 0, 3).reshape(clip_count, mod_count, width)
    bias_all = second_parts[:, mod_size : mod_size + bias_size].reshape(ranks, dp_count, bias_part)
    bias_all = bias_all.transpose(1, 0, 2).reshape(-1, width)
    left_size = mod_size + bias_size + left_cond.size
    left_cond = jnp.sum(second_parts[:, mod_size + bias_size : left_size], axis=0)
    left_cond = left_cond.reshape(mod_count, row_part, all_clips)
    mods = mods + bias_all[:mod_count]
    bias_table = jnp.concatenate(
        [bias_all[6:7], jnp.zeros((1, width), jnp.float32), bias_all[7:14]]
    )

    attn_in, parts, mixed, proj, resid, mlp_in, d_branch, d_branch_sums = run_attention(
        frames, frame_counts, stream, grad_out, mods, bias_table, attn_w
    )
    left_rows = [own_rows(narrow(left_roots[piece]), group) for piece in pieces]
    right_wholes = [gather_own(own_rows(narrow(right_roots[piece]), group), group) for piece in pieces]
    mlp_in, one_parts = tie(mlp_in, one_parts)
    one_w = one_steps.send(one_parts)
    hidden, slope = run_hidden(mlp_in, one_w, bias_table[4:8, None])
    two_steps = sum_blocks(
        lambda left: fast_dot("jtd,te->jde", left, d_branch),
        lambda first, size: lax.dynamic_slice_in_dim(hidden, first, size, 2),
        width,
        group,
    )
    two_parts = list(next(two_steps))
    hidden, two_parts[0] = tie(hidden, two_parts[0])

    d_pre, d_pre_sums, block_out, d_gate_two = run_branch(
        frames,
        frame_counts,
        hidden,
        slope,
        two_w,
        d_branch,
        bias_table[8:9],
        mods[:, 5:6],
        resid,
        grad_out,
    )
    d_pre, two_parts = tie(d_pre, two_parts)
    two_parts = list(two_steps.send(two_parts))
    one_steps = sum_blocks(
        lambda left: fast_dot("td,jte->jde", left, d_pre),
        lambda first, size: lax.dynamic_slice_in_dim(mlp_in, first, size, 1),
        width,
        group,
    )
    one_parts = list(next(one_steps))
    d_pre, one_parts[0], two_parts = tie(d_pre, one_parts[0], two_parts)
    two_parts = two_steps.send(two_parts)
    d_resid, d_proj, resid_sums = run_resid(
        frames, frame_counts, d_pre, one_w, mods, resid, grad_out, proj
    )
    d_proj, one_parts = tie(d_proj, one_parts)
    one_parts = one_steps.send(one_parts)
    d_heads, head_sums = run_attention_back(frames, frame_counts, d_proj, parts, attn_w)
    d_heads, one_parts, two_parts, right_wholes[2] = tie(
        d_heads, one_parts, two_parts, right_wholes[2]
    )
    whole_two = two_steps.send(two_parts)
    attn_steps = sum_blocks(
        lambda left: fast_dot("jtd,jte->jde", left, d_heads),
        lambda first, size: jnp.stack(
            [lax.dynamic_slice_in_dim(left, first, size, 1) for left in (attn_in,) * 3 + (mixed,)]
        ),
        width,
        group,
    )
    attn_parts = list(next(attn_steps))
    d_heads, attn_parts[0], one_parts = tie(d_heads, attn_parts[0], one_parts)
    one_parts = one_steps.send(one_parts)
    input_grad, input_sums = run_input(d_heads, attn_w, mods, stream, d_resid)
    input_sums, attn_parts, one_parts = tie(input_sums, attn_parts, one_parts)
    attn_parts = attn_steps.send(attn_parts)
    whole_one = one_steps.send(one_parts)

    d_mods = jnp.stack(
        [
            input_sums[:, 0],
            input_sums[:, 1],
            resid_sums[:, 2],
            resid_sums[:, 0],
            resid_sums[:, 1],
            d_gate_two[:, 0],
        ],
        axis=1,
    )
    head_sums = jnp.sum(head_sums, axis=0)
    grad_bias = jnp.concatenate(
        [
            jnp.sum(d_mods, axis=0),
            head_sums[0:1],
            head_sums[2:3],
            jnp.sum(resid_sums[:, 3], axis=0)[None],
            d_pre_sums[:, 0],
            jnp.sum(d_branch_sums, axis=0),
        ]
    )
    to_ranks = jnp.concatenate(
        [
            d_mods.reshape(clip_count, mod_count, ranks, col_part)
            .transpose(2, 0, 1, 3)
            .reshape(ranks, mod_size),
            grad_bias.reshape(dp_count, ranks, bias_part)
            .transpose(1, 0, 2)
            .reshape(ranks, bias_size),
        ],
        axis=1,
    )
    rank_sums = jnp.sum(lax.all_to_all(to_ranks, "fsdp", 0, 0, tiled=True), axis=0)
    to_rows = jnp.concatenate(
        [
            jnp.broadcast_to(rank_sums[None, :mod_size], (dp_count, mod_size)),
            rank_sums[mod_size:].reshape(dp_count, bias_part),
        ],
        axis=1,
    )
    from_rows = lax.all_to_all(to_rows, "dp", 0, 0, tiled=True)
    products_two = owned_step(whole_two, left_rows[2], right_wholes[2], group)
    from_rows, products_two, attn_parts = tie(from_rows, products_two, attn_parts)
    attn_parts = attn_steps.send(attn_parts)
    back_two = shard_rows(products_two, group)
    bias_grad = jnp.sum(from_rows[:, mod_size:], axis=0)
    mod_grad_cols = from_rows[:, :mod_size].reshape(all_clips, mod_count, col_part)
    mod_grad = lax.all_gather(packed([mod_grad_cols], 8), "fsdp", axis=0, tiled=True)
    mod_grad = mod_grad.reshape(ranks, -1)[:, : mod_grad_cols.size]
    mod_grad = mod_grad.reshape(ranks, all_clips, mod_count, col_part).transpose(1, 2, 0, 3)
    mod_grad = mod_grad.reshape(all_clips, mod_count, width)

    mod_grad_rows = lax.dynamic_slice_in_dim(mod_grad, dp_at * row_part, row_part, 2)
    right_parts = jnp.einsum(
        "cjk,jke->cje", mod_grad_rows, right_roots[:mod_count], precision=precise
    )
    cond_wide = wide(cond_all)
    cond_row_wide = wide(cond_rows)
    mod_gram = jnp.einsum("cjk,bjk->jcb", mod_grad, mod_grad, precision=precise)
    cond_gram = jnp.einsum("ck,bk->cb", cond_wide, cond_wide, precision=precise)
    mod_side = jnp.einsum("jcb,be->jce", mod_gram, cond_cols, precision=precise)
    ada_left = jnp.einsum("cr,jce->jre", cond_row_wide, mod_side, precision=precise)
    cond_side = jnp.einsum("cb,bje->jce", cond_gram, mod_grad_cols, precision=precise)
    ada_right = jnp.einsum("cjr,jce->jre", mod_grad_rows, cond_side, precision=precise)

    products_one = owned_step(whole_one, left_rows[1], right_wholes[1], group)
    products_one, right_parts, attn_parts = tie(products_one, right_parts, attn_parts)
    whole_attn = attn_steps.send(attn_parts)
    back_one = shard_rows(products_one, group)
    right_parts = lax.all_gather(packed([right_parts], 8), "dp", axis=0, tiled=True)
    mod_right = jnp.sum(right_parts.reshape(dp_count, -1), axis=0)[: mod_grad_cols.size]
    mod_right = mod_right.reshape(all_clips, mod_count, col_part)
    ada_pre = jnp.einsum("jrc,cje->jre", left_cond, mod_right, precision=precise)
    back_attn = shard_rows(owned_step(whole_attn, left_rows[0], right_wholes[0], group), group)

    def joined(at, ada):
        span = slice(at * group, (at + 1) * group)
        return jnp.concatenate(
            [ada, wide(back_attn[span]), wide(back_one[span]), wide(back_two[span])]
        )

    precond = joined(0, ada_pre)
    left_new = stat_decay * left_stats + (1.0 - stat_decay) * joined(1, ada_left)
    right_new = stat_decay * right_stats + (1.0 - stat_decay) * joined(2, ada_right)
    momentum_new = moment_decay * momentum + precond
    weights_new = weights - weight_rate * momentum_new
    weights_copy = weights_new.astype(jnp.bfloat16)
    bias_second_new = stat_decay * bias_second + (1.0 - stat_decay) * bias_grad * bias_grad
    bias_moment_new = moment_decay * bias_moment + bias_grad * lax.rsqrt(
        bias_second_new + diag_epsilon
    )
    biases_new = biases - bias_rate * bias_moment_new
    return (
        block_out.reshape(tokens.shape),
        input_grad.reshape(tokens.shape),
        left_new,
        right_new,
        momentum_new,
        weights_new,
        weights_copy,
        bias_moment_new,
        bias_second_new,
        biases_new,
    )


def solution(mesh):
    placed = (
        P("dp", "fsdp", None, None),
        P("dp", None),
        P("dp"),
        P("dp", "fsdp", None, None),
        P(None, "dp", "fsdp"),
        P(("dp", "fsdp")),
        P(None, "dp", "fsdp"),
        P(None, "dp", "fsdp"),
        P(None, "dp", "fsdp"),
        P(None, "dp", "fsdp"),
        P(None, "dp", "fsdp"),
        P(("dp", "fsdp")),
        P(("dp", "fsdp")),
    )
    return jax.shard_map(
        per_device,
        mesh=mesh,
        in_specs=placed,
        out_specs=(
            P("dp", "fsdp", None, None),
            P("dp", "fsdp", None, None),
            P(None, "dp", "fsdp"),
            P(None, "dp", "fsdp"),
            P(None, "dp", "fsdp"),
            P(None, "dp", "fsdp"),
            P(None, "dp", "fsdp"),
            P(("dp", "fsdp")),
            P(("dp", "fsdp")),
            P(("dp", "fsdp")),
        ),
        check_vma=False,
    )
```

```python
import functools
import math

import jax
import jax.numpy as jnp
from jax import lax
from jax.experimental import pallas as pl
from jax.experimental.pallas import tpu as pltpu
from jax.sharding import PartitionSpec as P

HEADS = 16


precise = lax.Precision.HIGHEST
norm_epsilon = 1e-06
masked_score = -1e30
stat_decay = 0.5
moment_decay = 0.9
weight_rate = 0.7
bias_rate = 0.1
diag_epsilon = 1e-08
vmem_bytes = 50 * 2**20


def narrow(array):
    return array.astype(jnp.bfloat16)


def wide(array):
    return array.astype(jnp.float32)


def spec(shape, index_map, **keywords):
    return pl.BlockSpec(shape, index_map, **keywords)


def held(shape):
    return pl.BlockSpec(shape, lambda step: (0,) * len(shape), pipeline_mode=pl.Buffered(1))


def column_cuts(total):
    cuts, at = [], 0
    while at < total:
        cuts.append((at, min(total, at + 256)))
        at += 256
    return cuts


def dot_nn(left, right):
    return lax.dot_general(left, right, (((1,), (0,)), ((), ())), preferred_element_type=jnp.float32)


def dot_nt(left, right):
    return lax.dot_general(left, right, (((1,), (1,)), ((), ())), preferred_element_type=jnp.float32)


def dot_tn(left, right):
    return lax.dot_general(left, right, (((0,), (0,)), ((), ())), preferred_element_type=jnp.float32)


def split_high(values):
    high = narrow(values)
    return high, narrow(values - wide(high))


def valid_rows(count, rows, frames):
    at = lax.broadcasted_iota(jnp.int32, (rows, 1), 0)
    return (lax.rem(at, frames) < count).astype(jnp.float32)


def score_offset(count, size, frames, key_axis):
    first = lax.broadcasted_iota(jnp.int32, (size, size), 0)
    second = lax.broadcasted_iota(jnp.int32, (size, size), 1)
    key = second if key_axis == 1 else first
    met = (lax.div(first, frames) == lax.div(second, frames)) & (lax.rem(key, frames) < count)
    return jnp.where(met, 0.0, masked_score)


def head_windows(width):
    size = width // HEADS
    windows = []
    for head in range(HEADS):
        low, high = head * size, (head + 1) * size
        start = low // 128 * 128
        stop = min(width, -(-high // 128) * 128)
        windows.append((low - start, high - start, start, stop))
    return windows


def lane_mask(low, high, count, dtype):
    lanes = lax.broadcasted_iota(jnp.int32, (1, count), 1)
    return ((lanes >= low) & (lanes < high)).astype(jnp.float32).astype(dtype)


def norm_parts(values):
    centered = values - jnp.mean(values, axis=-1, keepdims=True)
    variance = jnp.mean(centered * centered, axis=-1, keepdims=True)
    inverse = lax.rsqrt(variance + norm_epsilon)
    return centered * inverse, inverse


def norm_back(grad, normed, inverse):
    first = jnp.mean(grad, axis=-1, keepdims=True)
    second = jnp.mean(grad * normed, axis=-1, keepdims=True)
    return (grad - first - normed * second) * inverse


def column_sum(values):
    return jnp.sum(values, axis=0, keepdims=True)


def attention_kernel(
    frames,
    counts,
    tokens,
    cotangent,
    mods,
    bias,
    blocks,
    attn_in,
    parts,
    mixed_low,
    proj_out,
    resid_out,
    mlp_in,
    d_branch,
    d_branch_sum,
    mixed,
):
    rows, width = tokens.shape
    tile = min(rows, 128)
    count = counts[pl.program_id(0)]
    shift_one, scale_one, gate_one = (mods[0, at : at + 1, :] for at in range(3))
    shift_two, scale_two, gate_two = (mods[0, at : at + 1, :] for at in range(3, 6))
    for first in range(0, rows, tile):
        span = slice(first, first + tile)
        normed, _ = norm_parts(wide(tokens[span]))
        attn_in[span] = narrow(normed * (1.0 + scale_one) + shift_one)
        branch_back = narrow(wide(cotangent[span]) * valid_rows(count, tile, frames) * gate_two)
        d_branch[span] = branch_back
        part_sum = column_sum(wide(branch_back))
        d_branch_sum[0] = part_sum if first == 0 else d_branch_sum[0] + part_sum
    scale = (width // HEADS) ** -0.5
    source = attn_in[...]
    for low, high in column_cuts(width):
        span = slice(low, high)
        query = (dot_nn(source, blocks[0, :, span]) + bias[0:1, span]) * scale
        parts[0, :, span], parts[1, :, span] = split_high(query)
        parts[2, :, span], parts[3, :, span] = split_high(dot_nn(source, blocks[1, :, span]))
        parts[4, :, span] = narrow(dot_nn(source, blocks[2, :, span]) + bias[2:3, span])
    offset = score_offset(count, tile, frames, 1)
    mixed[...] = jnp.zeros_like(mixed)
    for first in range(0, rows, tile):
        span = slice(first, first + tile)
        for low, high, start, stop in head_windows(width):
            lanes = slice(start, stop)
            mask = lane_mask(low, high, stop - start, jnp.bfloat16)
            key_high = parts[2, span, lanes]
            query_high = parts[0, span, lanes] * mask
            scores = dot_nt(query_high, key_high)
            scores += dot_nt(parts[1, span, lanes] * mask, key_high)
            scores += dot_nt(query_high, parts[3, span, lanes]) + offset
            expons = jnp.exp(scores - jnp.max(scores, axis=-1, keepdims=True))
            probs = expons * (1.0 / jnp.sum(expons, axis=-1, keepdims=True))
            out = dot_nn(narrow(probs), parts[4, span, lanes] * mask)
            mixed[span, lanes] += out
    mixed_low[...] = narrow(mixed[...])
    source = mixed_low[...]
    for low, high in column_cuts(width):
        span = slice(low, high)
        proj_out[:, span] = dot_nn(source, blocks[3, :, span]) + bias[3:4, span]
    for first in range(0, rows, tile):
        span = slice(first, first + tile)
        resid = wide(tokens[span]) + valid_rows(count, tile, frames) * gate_one * proj_out[span]
        resid_out[span] = resid
        normed, _ = norm_parts(resid)
        mlp_in[span] = narrow(normed * (1.0 + scale_two) + shift_two)


def run_attention(frames, counts, tokens, cotangent, mods, bias, blocks):
    total, width = tokens.shape
    clips = mods.shape[0]
    rows = total // clips
    clip_rows = spec((rows, width), lambda clip: (clip, 0))
    low = jax.ShapeDtypeStruct((total, width), jnp.bfloat16)
    full = jax.ShapeDtypeStruct((total, width), jnp.float32)
    return pl.pallas_call(
        functools.partial(attention_kernel, frames),
        grid=(clips,),
        in_specs=[
            pl.BlockSpec(memory_space=pltpu.SMEM),
            clip_rows,
            clip_rows,
            spec((1,) + mods.shape[1:], lambda clip: (clip, 0, 0)),
            held(bias.shape),
            held(blocks.shape),
        ],
        out_specs=[
            clip_rows,
            spec((5, rows, width), lambda clip: (0, clip, 0)),
            clip_rows,
            clip_rows,
            clip_rows,
            clip_rows,
            clip_rows,
            spec((1, 1, width), lambda clip: (clip, 0, 0)),
        ],
        out_shape=[
            low,
            jax.ShapeDtypeStruct((5, total, width), jnp.bfloat16),
            low,
            full,
            full,
            low,
            low,
            jax.ShapeDtypeStruct((clips, 1, width), jnp.float32),
        ],
        scratch_shapes=[pltpu.VMEM((rows, width), jnp.float32)],
        compiler_params=pltpu.CompilerParams(vmem_limit_bytes=vmem_bytes),
        cost_estimate=pl.CostEstimate(
            flops=12 * total * width * width, bytes_accessed=40 * total * width, transcendentals=0
        ),
    )(counts, tokens, cotangent, mods, bias, blocks)


def hidden_kernel(mlp_in, block, bias, hidden, slope):
    root = (2.0 / math.pi) ** 0.5
    source = mlp_in[...]
    for low, high in column_cuts(block.shape[-1]):
        span = slice(low, high)
        pre = dot_nn(source, block[0, :, span]) + bias[0, :, span]
        square = pre * pre
        bent = jnp.tanh(root * pre * (1.0 + 0.044715 * square))
        half = 0.5 + 0.5 * bent
        hidden[0, :, span] = narrow(pre * half)
        steep = (0.5 * root) * pre * (1.0 + 3 * 0.044715 * square)
        slope[0, :, span] = narrow(half + steep * (1.0 - bent * bent))


def run_hidden(mlp_in, blocks, bias):
    total, width = mlp_in.shape
    count = blocks.shape[0]
    per_block = spec((1, total, width), lambda at: (at, 0, 0))
    out = jax.ShapeDtypeStruct((count, total, width), jnp.bfloat16)
    return pl.pallas_call(
        hidden_kernel,
        grid=(count,),
        in_specs=[
            held(mlp_in.shape),
            spec((1, width, width), lambda at: (at, 0, 0)),
            spec((1, 1, width), lambda at: (at, 0, 0)),
        ],
        out_specs=[per_block, per_block],
        out_shape=[out, out],
        compiler_params=pltpu.CompilerParams(vmem_limit_bytes=vmem_bytes),
        cost_estimate=pl.CostEstimate(
            flops=8 * total * width * width, bytes_accessed=30 * total * width, transcendentals=0
        ),
    )(mlp_in, blocks, bias)


def branch_kernel(
    frames,
    counts,
    hidden,
    slope,
    block,
    d_branch,
    bias,
    gates,
    resid,
    cotangent,
    d_pre,
    d_pre_sum,
    block_out,
    d_gate,
    branch,
):
    step, steps = pl.program_id(0), pl.num_programs(0)
    total, width = resid.shape
    clips = gates.shape[0]
    rows = total // clips
    source, back = hidden[0], d_branch[...]

    @pl.when(step == 0)
    def _():
        branch[...] = jnp.zeros_like(branch)

    for low, high in column_cuts(width):
        span = slice(low, high)
        d_hidden = dot_nt(back, block[0, span, :])
        low_back = narrow(d_hidden * wide(slope[0, :, span]))
        d_pre[0, :, span] = low_back
        d_pre_sum[0, :, span] = column_sum(wide(low_back))
        branch[:, span] += dot_nn(source, block[0, :, span])

    @pl.when(step == steps - 1)
    def _():
        for clip in range(clips):
            span = slice(clip * rows, (clip + 1) * rows)
            kept = valid_rows(counts[clip], rows, frames) * (branch[span] + bias[...])
            block_out[span] = narrow(resid[span] + gates[clip] * kept)
            d_gate[clip] = column_sum(wide(cotangent[span]) * kept)


def run_branch(frames, counts, hidden, slope, blocks, d_branch, bias, gates, resid, cotangent):
    count, total, width = hidden.shape
    clips = gates.shape[0]
    per_block = spec((1, total, width), lambda at: (at, 0, 0))
    low = jax.ShapeDtypeStruct((total, width), jnp.bfloat16)
    return pl.pallas_call(
        functools.partial(branch_kernel, frames),
        grid=(count,),
        in_specs=[
            pl.BlockSpec(memory_space=pltpu.SMEM),
            per_block,
            per_block,
            spec((1, width, width), lambda at: (at, 0, 0)),
            held((total, width)),
            held(bias.shape),
            held(gates.shape),
            held((total, width)),
            held((total, width)),
        ],
        out_specs=[
            per_block,
            spec((1, 1, width), lambda at: (at, 0, 0)),
            held((total, width)),
            held((clips, 1, width)),
        ],
        out_shape=[
            jax.ShapeDtypeStruct((count, total, width), jnp.bfloat16),
            jax.ShapeDtypeStruct((count, 1, width), jnp.float32),
            low,
            jax.ShapeDtypeStruct((clips, 1, width), jnp.float32),
        ],
        scratch_shapes=[pltpu.VMEM((total, width), jnp.float32)],
        compiler_params=pltpu.CompilerParams(vmem_limit_bytes=vmem_bytes),
        cost_estimate=pl.CostEstimate(
            flops=16 * total * width * width, bytes_accessed=40 * total * width, transcendentals=0
        ),
    )(counts, hidden, slope, blocks, d_branch, bias, gates, resid, cotangent)


def resid_kernel(
    frames,
    counts,
    d_pre,
    block,
    mods,
    resid,
    cotangent,
    proj,
    d_resid_out,
    d_proj,
    sums,
    total_grad,
):
    step, steps = pl.program_id(0), pl.num_programs(0)
    total, width = resid.shape
    clips = mods.shape[0]
    rows = total // clips
    tile = min(rows, 128)
    source = d_pre[0]

    @pl.when(step == 0)
    def _():
        total_grad[...] = jnp.zeros_like(total_grad)

    for low, high in column_cuts(width):
        span = slice(low, high)
        total_grad[:, span] += dot_nt(source, block[0, span, :])

    @pl.when(step == steps - 1)
    def _():
        for clip in range(clips):
            gate_one, scale_two = mods[clip, 2:3, :], mods[clip, 4:5, :]
            found = [0.0] * 4
            for first in range(clip * rows, (clip + 1) * rows, tile):
                span = slice(first, first + tile)
                grad = total_grad[span]
                normed, inverse = norm_parts(resid[span])
                back = norm_back(grad * (1.0 + scale_two), normed, inverse)
                d_resid = wide(cotangent[span]) + back
                d_resid_out[span] = d_resid
                kept = valid_rows(counts[clip], tile, frames) * d_resid
                low_back = narrow(kept * gate_one)
                d_proj[span] = low_back
                terms = (grad, grad * normed, kept * proj[span], wide(low_back))
                found = [old + column_sum(term) for old, term in zip(found, terms)]
            for at in range(4):
                sums[clip, at : at + 1, :] = found[at]


def run_resid(frames, counts, d_pre, blocks, mods, resid, cotangent, proj):
    count, total, width = d_pre.shape
    clips = mods.shape[0]
    return pl.pallas_call(
        functools.partial(resid_kernel, frames),
        grid=(count,),
        in_specs=[
            pl.BlockSpec(memory_space=pltpu.SMEM),
            spec((1, total, width), lambda at: (at, 0, 0)),
            spec((1, width, width), lambda at: (at, 0, 0)),
            held(mods.shape),
            held((total, width)),
            held((total, width)),
            held((total, width)),
        ],
        out_specs=[held((total, width)), held((total, width)), held((clips, 4, width))],
        out_shape=[
            jax.ShapeDtypeStruct((total, width), jnp.float32),
            jax.ShapeDtypeStruct((total, width), jnp.bfloat16),
            jax.ShapeDtypeStruct((clips, 4, width), jnp.float32),
        ],
        scratch_shapes=[pltpu.VMEM((total, width), jnp.float32)],
        compiler_params=pltpu.CompilerParams(vmem_limit_bytes=vmem_bytes),
        cost_estimate=pl.CostEstimate(
            flops=8 * total * width * width, bytes_accessed=40 * total * width, transcendentals=0
        ),
    )(counts, d_pre, blocks, mods, resid, cotangent, proj)


def attention_back_kernel(
    frames, counts, d_proj, parts, block, d_qkv, sums, d_mixed, d_query, d_key, d_value
):
    rows, width = d_proj.shape
    tile = min(rows, 128)
    count = counts[pl.program_id(0)]
    source = d_proj[...]
    for low, high in column_cuts(width):
        d_mixed[:, low:high] = narrow(dot_nt(source, block[0, low:high, :]))
    scale = (width // HEADS) ** -0.5
    offset = score_offset(count, tile, frames, 0)
    for ref in (d_query, d_key, d_value):
        ref[...] = jnp.zeros_like(ref)
    for first in range(0, rows, tile):
        span = slice(first, first + tile)
        for low, high, start, stop in head_windows(width):
            lanes = slice(start, stop)
            mask = lane_mask(low, high, stop - start, jnp.bfloat16)
            query_high = parts[0, span, lanes] * mask
            key_high = parts[2, span, lanes] * mask
            back = d_mixed[span, lanes] * mask
            scores = dot_nt(key_high, query_high)
            scores += dot_nt(key_high, parts[1, span, lanes])
            scores += dot_nt(parts[3, span, lanes], query_high) + offset
            expons = jnp.exp(scores - jnp.max(scores, axis=0, keepdims=True))
            probs = expons * (1.0 / jnp.sum(expons, axis=0, keepdims=True))
            d_probs = dot_nt(parts[4, span, lanes], back)
            inner = jnp.sum(d_probs * probs, axis=0, keepdims=True)
            d_scores = narrow(probs * (d_probs - inner))
            d_value[span, lanes] += dot_nn(narrow(probs), back)
            d_key[span, lanes] += dot_nn(d_scores, query_high)
            d_query[span, lanes] += dot_tn(d_scores, key_high)
    for at, ref in enumerate((d_query, d_key, d_value)):
        low_back = narrow(ref[...] * scale) if at == 0 else narrow(ref[...])
        d_qkv[at] = low_back
        sums[0, at : at + 1, :] = column_sum(wide(low_back))
    d_qkv[3] = source


def run_attention_back(frames, counts, d_proj, parts, block):
    total, width = d_proj.shape
    clips = counts.shape[0]
    rows = total // clips
    return pl.pallas_call(
        functools.partial(attention_back_kernel, frames),
        grid=(clips,),
        in_specs=[
            pl.BlockSpec(memory_space=pltpu.SMEM),
            spec((rows, width), lambda clip: (clip, 0)),
            spec((5, rows, width), lambda clip: (0, clip, 0)),
            spec((1, width, width), lambda clip: (3, 0, 0), pipeline_mode=pl.Buffered(1)),
        ],
        out_specs=[
            spec((4, rows, width), lambda clip: (0, clip, 0)),
            spec((1, 3, width), lambda clip: (clip, 0, 0)),
        ],
        out_shape=[
            jax.ShapeDtypeStruct((4, total, width), jnp.bfloat16),
            jax.ShapeDtypeStruct((clips, 3, width), jnp.float32),
        ],
        scratch_shapes=[pltpu.VMEM((rows, width), jnp.bfloat16)]
        + [pltpu.VMEM((rows, width), jnp.float32)] * 3,
        compiler_params=pltpu.CompilerParams(vmem_limit_bytes=vmem_bytes),
        cost_estimate=pl.CostEstimate(
            flops=12 * total * width * width, bytes_accessed=20 * total * width, transcendentals=0
        ),
    )(counts, d_proj, parts, block)


def input_kernel(d_qkv, block, mods, tokens, d_resid, input_grad, sums, total_grad):
    step, steps = pl.program_id(0), pl.num_programs(0)
    total, width = tokens.shape
    clips = mods.shape[0]
    rows = total // clips
    tile = min(rows, 128)
    source = d_qkv[0]

    @pl.when(step == 0)
    def _():
        total_grad[...] = jnp.zeros_like(total_grad)

    for low, high in column_cuts(width):
        span = slice(low, high)
        total_grad[:, span] += dot_nt(source, block[0, span, :])

    @pl.when(step == steps - 1)
    def _():
        for clip in range(clips):
            scale_one = mods[clip, 1:2, :]
            found = [0.0] * 2
            for first in range(clip * rows, (clip + 1) * rows, tile):
                span = slice(first, first + tile)
                grad = total_grad[span]
                normed, inverse = norm_parts(wide(tokens[span]))
                back = norm_back(grad * (1.0 + scale_one), normed, inverse)
                input_grad[span] = narrow(d_resid[span] + back)
                terms = (grad, grad * normed)
                found = [old + column_sum(term) for old, term in zip(found, terms)]
            for at in range(2):
                sums[clip, at : at + 1, :] = found[at]


def run_input(d_qkv, blocks, mods, tokens, d_resid):
    total, width = tokens.shape
    clips = mods.shape[0]
    return pl.pallas_call(
        input_kernel,
        grid=(3,),
        in_specs=[
            spec((1, total, width), lambda at: (at, 0, 0)),
            spec((1, width, width), lambda at: (at, 0, 0)),
            held(mods.shape),
            held((total, width)),
            held((total, width)),
        ],
        out_specs=[held((total, width)), held((clips, 2, width))],
        out_shape=[
            jax.ShapeDtypeStruct((total, width), jnp.bfloat16),
            jax.ShapeDtypeStruct((clips, 2, width), jnp.float32),
        ],
        scratch_shapes=[pltpu.VMEM((total, width), jnp.float32)],
        compiler_params=pltpu.CompilerParams(vmem_limit_bytes=vmem_bytes),
        cost_estimate=pl.CostEstimate(
            flops=6 * total * width * width, bytes_accessed=30 * total * width, transcendentals=0
        ),
    )(d_qkv, blocks, mods, tokens, d_resid)


def tie(*values):
    return lax.optimization_barrier(values)


def packed(arrays, tile):
    flat = jnp.concatenate([array.reshape(-1) for array in arrays])
    return jnp.pad(flat, (0, -flat.shape[0] % (tile * 128))).reshape(-1, 128)


def core_swap(array):
    count = lax.axis_size("dp")
    return lax.ppermute(array, "dp", [(at, at ^ 1) for at in range(count)])


def chip_shift(array, step):
    count = lax.axis_size("dp")
    return lax.ppermute(array, "dp", [(at, (at + 2 * step) % count) for at in range(count)])


def rank_swap(array, bits):
    count = lax.axis_size("fsdp")
    return lax.ppermute(array, "fsdp", [(at, at ^ bits) for at in range(count)])


def entry(array, at, axis=0):
    return lax.dynamic_index_in_dim(array, at, axis, keepdims=False)


def place_kernel(cuts, at, *refs):
    parts, whole, held_rows, semaphores = refs[:-3], refs[-3], refs[-2], refs[-1]
    spans, loads, stores = [], [], []
    for index, (part, first, rows) in enumerate(cuts):
        spans.append(pl.ds(pl.multiple_of(at[index] * 16, 16), rows))
        source = parts[part].at[pl.ds(first, rows)]
        loads.append(
            pltpu.make_async_copy(source, held_rows.at[spans[index]], semaphores.at[0, index])
        )
        loads[index].start()
    for index, span in enumerate(spans):
        loads[index].wait()
        stores.append(
            pltpu.make_async_copy(held_rows.at[span], whole.at[span], semaphores.at[1, index])
        )
        stores[index].start()
    for store in stores:
        store.wait()


def place(parts, cuts, starts, rows):
    width = parts[0].shape[-1]
    dtype = parts[0].dtype
    return pl.pallas_call(
        functools.partial(place_kernel, cuts),
        in_specs=[pl.BlockSpec(memory_space=pltpu.SMEM)]
        + [pl.BlockSpec(memory_space=pl.ANY)] * len(parts),
        out_specs=pl.BlockSpec(memory_space=pl.ANY),
        out_shape=jax.ShapeDtypeStruct((rows, width), dtype),
        scratch_shapes=[
            pltpu.VMEM((rows, width), dtype),
            pltpu.SemaphoreType.DMA((2, len(cuts))),
        ],
        compiler_params=pltpu.CompilerParams(vmem_limit_bytes=vmem_bytes),
        cost_estimate=pl.CostEstimate(
            flops=0, bytes_accessed=4 * rows * width, transcendentals=0
        ),
    )(jnp.stack([jnp.asarray(start, jnp.int32) for start in starts]), *parts)


def own_rows(parts, group):
    ranks, at = lax.axis_size("fsdp"), lax.axis_index("fsdp")
    shares = ranks // group
    count, _, row_part, col_part = parts.shape
    chunk = row_part // shares
    split = parts.reshape(count, group, shares, chunk, col_part).transpose(1, 2, 0, 3, 4)
    split = split.reshape(ranks, count, chunk, col_part)
    if shares > 1:
        moved = lax.all_to_all(split, "fsdp", 0, 0, tiled=True)
        (moved,) = yield (moved,)
        yield moved.transpose(1, 2, 0, 3).reshape(count, chunk, ranks * col_part)
        return
    panels = [entry(split, at)]
    panels += [rank_swap(entry(split, at ^ bits), bits) for bits in range(1, ranks)]
    panels = yield tuple(panels)
    placed = [
        lax.select_n(at, *[panels[panel ^ index] for index in range(ranks)])
        for panel in range(ranks)
    ]
    yield jnp.concatenate(placed, axis=2)


def shard_rows(rows, group):
    ranks = lax.axis_size("fsdp")
    shares = ranks // group
    count, chunk, total = rows.shape
    col_part = total // ranks
    split = rows.reshape(count, chunk, ranks, col_part).transpose(2, 0, 1, 3)
    moved = lax.all_to_all(split, "fsdp", 0, 0, tiled=True)
    moved = moved.reshape(group, shares, count, chunk, col_part).transpose(2, 0, 1, 3, 4)
    return moved.reshape(count * group, shares * chunk, col_part)


def gather_blocks(rows, group):
    ranks, dp_count = lax.axis_size("fsdp"), lax.axis_size("dp")
    shares = ranks // group
    chunk, total = rows.shape
    all_rows = lax.all_gather(rows, ("fsdp", "dp"), axis=0, tiled=True)
    if shares > 1:
        all_rows = all_rows.reshape(group, shares, dp_count, chunk, total).transpose(0, 2, 1, 3, 4)
    return all_rows.reshape(group, total, total)


def gather_pieces(rows, group):
    ranks, at = lax.axis_size("fsdp"), lax.axis_index("fsdp")
    if ranks != group:
        blocks = gather_blocks(rows, group)
        (blocks,) = yield (blocks,)
        yield blocks
        return
    chips = lax.axis_size("dp") // 2
    core, chip = lax.axis_index("dp") % 2, lax.axis_index("dp") // 2
    chunk, total = rows.shape
    half = total // 2
    unit = chunk // 16
    found = [rows] + [chip_shift(rows, step) for step in range(1, chips)]
    starts = [(chip - step) % chips * unit for step in range(chips)]
    line = place(found, [(step, 0, chunk) for step in range(chips)], starts, half)
    cuts = [(side, step * chunk, chunk) for side in range(2) for step in range(chips)]
    starts = [(2 * step + side) * unit for side in (core, 1 - core) for step in range(chips)]
    own = place([line, core_swap(line)], cuts, starts, total)
    share = lax.dynamic_slice_in_dim(own, core * half, half, 0)
    mine = [rank_swap(share, bits) for bits in range(1, ranks)]
    own, *mine = yield (own, *mine)
    others = [core_swap(part) for part in mine]
    starts = [at * 2] + [
        (at ^ bits) * 2 + side for side in (core, 1 - core) for bits in range(1, ranks)
    ]
    starts = [start * (half // 16) for start in starts]
    cuts = [(0, 0, total)] + [(1 + index, 0, half) for index in range(2 * ranks - 2)]
    found = place([own] + mine + others, cuts, starts, group * total)
    yield found.reshape(group, total, total)


def gather_own(rows, group):
    ranks = lax.axis_size("fsdp")
    shares = ranks // group
    if shares > 1:
        sets = [[share + shares * block for share in range(shares)] for block in range(group)]
        rows = lax.all_gather(rows, "fsdp", axis=1, tiled=True, axis_index_groups=sets)
    return lax.all_gather(rows, "dp", axis=1, tiled=True)


def sum_blocks(product, cut, total, group):
    ranks, dp_count = lax.axis_size("fsdp"), lax.axis_size("dp")
    shares = ranks // group
    if shares > 1:
        blocks = narrow(product(cut(0, total)))
        chunk = total // (dp_count * shares)
        blocks = blocks.reshape(group, dp_count, shares, chunk, -1).transpose(0, 2, 1, 3, 4)
        rows = lax.psum_scatter(
            blocks.reshape(group * total, -1), ("fsdp", "dp"), scatter_dimension=0, tiled=True
        )
        for _ in range(3):
            (rows,) = yield (rows,)
        yield gather_own(rows[None], group)[0]
        return
    chips, half = dp_count // 2, total // 2
    chunk = half // chips
    core, chip = lax.axis_index("dp") % 2, lax.axis_index("dp") // 2
    low_bit, high_bit = lax.axis_index("fsdp") % 2, lax.axis_index("fsdp") // 2
    away = narrow(product(cut((1 - core) * half, half)))
    here = product(cut(core * half, half))
    here = narrow(here + wide(core_swap(away)))
    here = here.reshape(2, 2, chips, chunk, -1)
    middle = chips // 2
    first, second = here[:, :, :middle], here[:, :, middle:]
    first_in = rank_swap(entry(first, 1 - low_bit, 1), 1)
    second_in = rank_swap(entry(second, 1 - high_bit, 0), 2)
    here, first_in, second_in = yield (here, first_in, second_in)
    first, second = here[:, :, :middle], here[:, :, middle:]
    first = narrow(wide(entry(first, low_bit, 1)) + wide(first_in))
    second = narrow(wide(entry(second, high_bit, 0)) + wide(second_in))
    first_in = rank_swap(entry(first, 1 - high_bit), 2)
    second_in = rank_swap(entry(second, 1 - low_bit), 1)
    first, second, first_in, second_in = yield (first, second, first_in, second_in)
    first = narrow(wide(entry(first, high_bit)) + wide(first_in))
    second = narrow(wide(entry(second, low_bit)) + wide(second_in))
    line = jnp.concatenate([first, second])
    parts = [entry(line, chip)]
    parts += [chip_shift(entry(line, (chip + step) % chips), step) for step in range(1, chips)]
    parts = yield tuple(parts)
    rows = sum(wide(part) for part in parts)
    found = lax.all_gather(narrow(rows), "dp", axis=0, tiled=True)
    yield found.reshape(chips, 2, chunk, -1).transpose(1, 0, 2, 3).reshape(total, -1)


def fast_dot(subscripts, left, right):
    return jnp.einsum(subscripts, left, right, preferred_element_type=jnp.float32)


def owned_step(whole, left_root, right_root, group):
    chunk = left_root.shape[0]
    shares = lax.axis_size("fsdp") // group
    first = lax.axis_index("dp") * (chunk * shares) + lax.axis_index("fsdp") % shares * chunk
    grad_rows = lax.dynamic_slice_in_dim(whole, first, chunk, 0)
    own_columns = lax.dynamic_slice_in_dim(whole, first, chunk, 1)
    outer = fast_dot("rk,jk->rj", grad_rows, whole)
    inner = fast_dot("kr,kj->rj", own_columns, whole)
    side = fast_dot("rk,kj->rj", left_root, whole)
    side_high = narrow(side)
    side_low = narrow(side - wide(side_high))
    precond = fast_dot("rk,kj->rj", side_high, right_root) + fast_dot(
        "rk,kj->rj", side_low, right_root
    )
    return narrow(jnp.stack([precond, outer, inner]))


def per_device(
    tokens,
    conditioning,
    frame_counts,
    cotangent,
    weights,
    biases,
    momentum,
    left_stats,
    right_stats,
    left_roots,
    right_roots,
    bias_moment,
    bias_second,
):
    group = 4
    mod_count = 6
    clip_count, pos_count, frames, width = tokens.shape
    token_count = clip_count * pos_count * frames
    block_count, row_part, col_part = weights.shape
    dp_count, ranks = lax.axis_size("dp"), lax.axis_size("fsdp")
    dp_at, rank_at = lax.axis_index("dp"), lax.axis_index("fsdp")
    all_clips = clip_count * dp_count
    bias_part = biases.shape[0]
    stream = tokens.reshape(token_count, width)
    grad_out = cotangent.reshape(token_count, width)
    low_weights = narrow(weights).reshape(block_count, row_part, col_part)
    shards = low_weights[mod_count:].reshape(-1, group, row_part, col_part)

    attn_rows, cond_low = own_rows(shards[:1], group), narrow(jax.nn.silu(conditioning))
    attn_panels = next(attn_rows)
    first_parts = lax.all_gather(packed([cond_low, narrow(biases)], 16), "dp", axis=0, tiled=True)
    attn_panels, first_parts, other_shards = tie(attn_panels, first_parts, shards[1:])
    attn_w = gather_blocks(attn_rows.send(attn_panels)[0], group)
    other_rows = own_rows(other_shards, group)
    other_rows = other_rows.send(next(other_rows))
    one_steps = gather_pieces(other_rows[0], group)
    one_parts = next(one_steps)
    two_w = gather_blocks(other_rows[1], group)

    first_parts = first_parts.reshape(dp_count, -1)
    cond_all = first_parts[:, : clip_count * width].reshape(all_clips, width)
    bias_rows = wide(first_parts[:, clip_count * width : clip_count * width + bias_part])
    cond_rows = lax.dynamic_slice_in_dim(cond_all, dp_at * row_part, row_part, 1)
    cond_cols = wide(lax.dynamic_slice_in_dim(cond_all, rank_at * col_part, col_part, 1))
    mod_parts = fast_dot("cr,jre->cje", cond_rows, low_weights[:mod_count])
    mod_parts = lax.all_to_all(mod_parts, "dp", 0, 0, tiled=True)
    mod_cols = jnp.sum(mod_parts.reshape(dp_count, clip_count, mod_count, col_part), axis=0)
    left_cond = jnp.einsum("jrk,ck->jrc", left_roots[:mod_count], cond_cols, precision=precise)
    mod_size, bias_size = mod_cols.size, dp_count * bias_part
    second_parts = lax.all_gather(
        packed([mod_cols, bias_rows, left_cond], 8), "fsdp", axis=0, tiled=True
    ).reshape(ranks, -1)
    mods = second_parts[:, :mod_size].reshape(ranks, clip_count, mod_count, col_part)
    mods = mods.transpose(1, 2, 0, 3).reshape(clip_count, mod_count, width)
    bias_all = second_parts[:, mod_size : mod_size + bias_size].reshape(ranks, dp_count, bias_part)
    bias_all = bias_all.transpose(1, 0, 2).reshape(-1, width)
    left_size = mod_size + bias_size + left_cond.size
    left_cond = jnp.sum(second_parts[:, mod_size + bias_size : left_size], axis=0)
    left_cond = left_cond.reshape(mod_count, row_part, all_clips)
    mods = mods + bias_all[:mod_count]
    bias_table = jnp.concatenate(
        [bias_all[6:7], jnp.zeros((1, width), jnp.float32), bias_all[7:14]]
    )

    attn_in, parts, mixed, proj, resid, mlp_in, d_branch, d_branch_sums = run_attention(
        frames, frame_counts, stream, grad_out, mods, bias_table, attn_w
    )
    roots = jnp.stack([narrow(left_roots[mod_count:]), narrow(right_roots[mod_count:])])
    mlp_in, one_parts, roots = tie(mlp_in, one_parts, roots)
    root_rows = own_rows(roots.reshape(-1, group, row_part, col_part), group)
    root_panels = next(root_rows)
    one_w = one_steps.send(one_parts)
    hidden, slope = run_hidden(mlp_in, one_w, bias_table[4:8, None])
    two_steps = sum_blocks(
        lambda left: fast_dot("jtd,te->jde", left, d_branch),
        lambda first, size: lax.dynamic_slice_in_dim(hidden, first, size, 2),
        width,
        group,
    )
    two_parts = list(next(two_steps))
    hidden, two_parts[0] = tie(hidden, two_parts[0])

    d_pre, d_pre_sums, block_out, d_gate_two = run_branch(
        frames,
        frame_counts,
        hidden,
        slope,
        two_w,
        d_branch,
        bias_table[8:9],
        mods[:, 5:6],
        resid,
        grad_out,
    )
    d_pre, two_parts, root_panels = tie(d_pre, two_parts, root_panels)
    two_parts = list(two_steps.send(two_parts))
    left_rows, right_rows = jnp.split(root_rows.send(root_panels), 2)
    right_wholes = gather_own(right_rows, group)
    one_steps = sum_blocks(
        lambda left: fast_dot("td,jte->jde", left, d_pre),
        lambda first, size: lax.dynamic_slice_in_dim(mlp_in, first, size, 1),
        width,
        group,
    )
    one_parts = list(next(one_steps))
    d_pre, one_parts[0], two_parts = tie(d_pre, one_parts[0], two_parts)
    two_parts = two_steps.send(two_parts)
    d_resid, d_proj, resid_sums = run_resid(
        frames, frame_counts, d_pre, one_w, mods, resid, grad_out, proj
    )
    d_proj, one_parts = tie(d_proj, one_parts)
    one_parts = one_steps.send(one_parts)
    d_heads, head_sums = run_attention_back(frames, frame_counts, d_proj, parts, attn_w)
    d_heads, one_parts, two_parts = tie(d_heads, one_parts, two_parts)
    whole_two = two_steps.send(two_parts)
    attn_steps = sum_blocks(
        lambda left: fast_dot("jtd,jte->jde", left, d_heads),
        lambda first, size: jnp.stack(
            [lax.dynamic_slice_in_dim(left, first, size, 1) for left in (attn_in,) * 3 + (mixed,)]
        ),
        width,
        group,
    )
    attn_parts = list(next(attn_steps))
    d_heads, attn_parts[0], one_parts = tie(d_heads, attn_parts[0], one_parts)
    one_parts = one_steps.send(one_parts)
    input_grad, input_sums = run_input(d_heads, attn_w, mods, stream, d_resid)
    input_sums, attn_parts, one_parts, right_wholes = tie(
        input_sums, attn_parts, one_parts, right_wholes
    )
    attn_parts = attn_steps.send(attn_parts)
    whole_one = one_steps.send(one_parts)

    d_mods = jnp.stack(
        [
            input_sums[:, 0],
            input_sums[:, 1],
            resid_sums[:, 2],
            resid_sums[:, 0],
            resid_sums[:, 1],
            d_gate_two[:, 0],
        ],
        axis=1,
    )
    head_sums = jnp.sum(head_sums, axis=0)
    grad_bias = jnp.concatenate(
        [
            jnp.sum(d_mods, axis=0),
            head_sums[0:1],
            head_sums[2:3],
            jnp.sum(resid_sums[:, 3], axis=0)[None],
            d_pre_sums[:, 0],
            jnp.sum(d_branch_sums, axis=0),
        ]
    )
    to_ranks = jnp.concatenate(
        [
            d_mods.reshape(clip_count, mod_count, ranks, col_part)
            .transpose(2, 0, 1, 3)
            .reshape(ranks, mod_size),
            grad_bias.reshape(dp_count, ranks, bias_part)
            .transpose(1, 0, 2)
            .reshape(ranks, bias_size),
        ],
        axis=1,
    )
    rank_sums = jnp.sum(lax.all_to_all(to_ranks, "fsdp", 0, 0, tiled=True), axis=0)
    to_rows = jnp.concatenate(
        [
            jnp.broadcast_to(rank_sums[None, :mod_size], (dp_count, mod_size)),
            rank_sums[mod_size:].reshape(dp_count, bias_part),
        ],
        axis=1,
    )
    to_rows, attn_parts = tie(to_rows, attn_parts)
    attn_parts = attn_steps.send(attn_parts)
    from_rows = lax.all_to_all(to_rows, "dp", 0, 0, tiled=True)
    products_two = owned_step(whole_two, left_rows[2], right_wholes[2], group)
    bias_grad = jnp.sum(from_rows[:, mod_size:], axis=0)
    mod_grad_cols = from_rows[:, :mod_size].reshape(all_clips, mod_count, col_part)
    mod_grad = lax.all_gather(packed([mod_grad_cols], 8), "fsdp", axis=0, tiled=True)
    mod_grad = mod_grad.reshape(ranks, -1)[:, : mod_grad_cols.size]
    mod_grad = mod_grad.reshape(ranks, all_clips, mod_count, col_part).transpose(1, 2, 0, 3)
    mod_grad = mod_grad.reshape(all_clips, mod_count, width)

    mod_grad_rows = lax.dynamic_slice_in_dim(mod_grad, dp_at * row_part, row_part, 2)
    right_parts = jnp.einsum(
        "cjk,jke->cje", mod_grad_rows, right_roots[:mod_count], precision=precise
    )
    cond_wide = wide(cond_all)
    cond_row_wide = wide(cond_rows)
    mod_gram = jnp.einsum("cjk,bjk->jcb", mod_grad, mod_grad, precision=precise)
    cond_gram = jnp.einsum("ck,bk->cb", cond_wide, cond_wide, precision=precise)
    mod_side = jnp.einsum("jcb,be->jce", mod_gram, cond_cols, precision=precise)
    ada_left = jnp.einsum("cr,jce->jre", cond_row_wide, mod_side, precision=precise)
    cond_side = jnp.einsum("cb,bje->jce", cond_gram, mod_grad_cols, precision=precise)
    ada_right = jnp.einsum("cjr,jce->jre", mod_grad_rows, cond_side, precision=precise)

    products_two, right_parts, attn_parts = tie(products_two, right_parts, attn_parts)
    whole_attn = attn_steps.send(attn_parts)
    back_two = shard_rows(products_two, group)
    back_one = shard_rows(owned_step(whole_one, left_rows[1], right_wholes[1], group), group)
    right_parts = lax.all_gather(packed([right_parts], 8), "dp", axis=0, tiled=True)
    mod_right = jnp.sum(right_parts.reshape(dp_count, -1), axis=0)[: mod_grad_cols.size]
    mod_right = mod_right.reshape(all_clips, mod_count, col_part)
    ada_pre = jnp.einsum("jrc,cje->jre", left_cond, mod_right, precision=precise)
    back_attn = shard_rows(owned_step(whole_attn, left_rows[0], right_wholes[0], group), group)

    def joined(at, ada):
        span = slice(at * group, (at + 1) * group)
        return jnp.concatenate(
            [ada, wide(back_attn[span]), wide(back_one[span]), wide(back_two[span])]
        )

    precond = joined(0, ada_pre)
    left_new = stat_decay * left_stats + (1.0 - stat_decay) * joined(1, ada_left)
    right_new = stat_decay * right_stats + (1.0 - stat_decay) * joined(2, ada_right)
    momentum_new = moment_decay * momentum + precond
    weights_new = weights - weight_rate * momentum_new
    weights_copy = weights_new.astype(jnp.bfloat16)
    bias_second_new = stat_decay * bias_second + (1.0 - stat_decay) * bias_grad * bias_grad
    bias_moment_new = moment_decay * bias_moment + bias_grad * lax.rsqrt(
        bias_second_new + diag_epsilon
    )
    biases_new = biases - bias_rate * bias_moment_new
    return (
        block_out.reshape(tokens.shape),
        input_grad.reshape(tokens.shape),
        left_new,
        right_new,
        momentum_new,
        weights_new,
        weights_copy,
        bias_moment_new,
        bias_second_new,
        biases_new,
    )


def solution(mesh):
    placed = (
        P("dp", "fsdp", None, None),
        P("dp", None),
        P("dp"),
        P("dp", "fsdp", None, None),
        P(None, "dp", "fsdp"),
        P(("dp", "fsdp")),
        P(None, "dp", "fsdp"),
        P(None, "dp", "fsdp"),
        P(None, "dp", "fsdp"),
        P(None, "dp", "fsdp"),
        P(None, "dp", "fsdp"),
        P(("dp", "fsdp")),
        P(("dp", "fsdp")),
    )
    return jax.shard_map(
        per_device,
        mesh=mesh,
        in_specs=placed,
        out_specs=(
            P("dp", "fsdp", None, None),
            P("dp", "fsdp", None, None),
            P(None, "dp", "fsdp"),
            P(None, "dp", "fsdp"),
            P(None, "dp", "fsdp"),
            P(None, "dp", "fsdp"),
            P(None, "dp", "fsdp"),
            P(("dp", "fsdp")),
            P(("dp", "fsdp")),
            P(("dp", "fsdp")),
        ),
        check_vma=False,
    )
```

```python
import functools
import math

import jax
import jax.numpy as jnp
from jax import lax
from jax.experimental import pallas as pl
from jax.experimental.pallas import tpu as pltpu
from jax.sharding import PartitionSpec as P

HEADS = 16


precise = lax.Precision.HIGHEST
norm_epsilon = 1e-06
masked_score = -1e30
stat_decay = 0.5
moment_decay = 0.9
weight_rate = 0.7
bias_rate = 0.1
diag_epsilon = 1e-08
vmem_bytes = 50 * 2**20


def narrow(array):
    return array.astype(jnp.bfloat16)


def wide(array):
    return array.astype(jnp.float32)


def spec(shape, index_map, **keywords):
    return pl.BlockSpec(shape, index_map, **keywords)


def held(shape):
    return pl.BlockSpec(shape, lambda step: (0,) * len(shape), pipeline_mode=pl.Buffered(1))


def column_cuts(total):
    cuts, at = [], 0
    while at < total:
        cuts.append((at, min(total, at + 256)))
        at += 256
    return cuts


def dot_nn(left, right):
    return lax.dot_general(left, right, (((1,), (0,)), ((), ())), preferred_element_type=jnp.float32)


def dot_nt(left, right):
    return lax.dot_general(left, right, (((1,), (1,)), ((), ())), preferred_element_type=jnp.float32)


def dot_tn(left, right):
    return lax.dot_general(left, right, (((0,), (0,)), ((), ())), preferred_element_type=jnp.float32)


def split_high(values):
    high = narrow(values)
    return high, narrow(values - wide(high))


def valid_rows(count, rows, frames):
    at = lax.broadcasted_iota(jnp.int32, (rows, 1), 0)
    return (lax.rem(at, frames) < count).astype(jnp.float32)


def score_offset(count, size, frames, key_axis):
    first = lax.broadcasted_iota(jnp.int32, (size, size), 0)
    second = lax.broadcasted_iota(jnp.int32, (size, size), 1)
    key = second if key_axis == 1 else first
    met = (lax.div(first, frames) == lax.div(second, frames)) & (lax.rem(key, frames) < count)
    return jnp.where(met, 0.0, masked_score)


def head_windows(width):
    size = width // HEADS
    windows = []
    for head in range(HEADS):
        low, high = head * size, (head + 1) * size
        start = low // 128 * 128
        stop = min(width, -(-high // 128) * 128)
        windows.append((low - start, high - start, start, stop))
    return windows


def lane_mask(low, high, count, dtype):
    lanes = lax.broadcasted_iota(jnp.int32, (1, count), 1)
    return ((lanes >= low) & (lanes < high)).astype(jnp.float32).astype(dtype)


def norm_parts(values):
    centered = values - jnp.mean(values, axis=-1, keepdims=True)
    variance = jnp.mean(centered * centered, axis=-1, keepdims=True)
    inverse = lax.rsqrt(variance + norm_epsilon)
    return centered * inverse, inverse


def norm_back(grad, normed, inverse):
    first = jnp.mean(grad, axis=-1, keepdims=True)
    second = jnp.mean(grad * normed, axis=-1, keepdims=True)
    return (grad - first - normed * second) * inverse


def column_sum(values):
    return jnp.sum(values, axis=0, keepdims=True)


def attention_kernel(
    frames,
    counts,
    tokens,
    cotangent,
    mods,
    bias,
    blocks,
    attn_in,
    parts,
    mixed_low,
    proj_out,
    resid_out,
    mlp_in,
    d_branch,
    d_branch_sum,
    mixed,
):
    rows, width = tokens.shape
    tile = min(rows, 128)
    count = counts[pl.program_id(0)]
    shift_one, scale_one, gate_one = (mods[0, at : at + 1, :] for at in range(3))
    shift_two, scale_two, gate_two = (mods[0, at : at + 1, :] for at in range(3, 6))
    for first in range(0, rows, tile):
        span = slice(first, first + tile)
        normed, _ = norm_parts(wide(tokens[span]))
        attn_in[span] = narrow(normed * (1.0 + scale_one) + shift_one)
        branch_back = narrow(wide(cotangent[span]) * valid_rows(count, tile, frames) * gate_two)
        d_branch[span] = branch_back
        part_sum = column_sum(wide(branch_back))
        d_branch_sum[0] = part_sum if first == 0 else d_branch_sum[0] + part_sum
    scale = (width // HEADS) ** -0.5
    source = attn_in[...]
    for low, high in column_cuts(width):
        span = slice(low, high)
        query = (dot_nn(source, blocks[0, :, span]) + bias[0:1, span]) * scale
        parts[0, :, span], parts[1, :, span] = split_high(query)
        parts[2, :, span], parts[3, :, span] = split_high(dot_nn(source, blocks[1, :, span]))
        parts[4, :, span] = narrow(dot_nn(source, blocks[2, :, span]) + bias[2:3, span])
    offset = score_offset(count, tile, frames, 1)
    mixed[...] = jnp.zeros_like(mixed)
    for first in range(0, rows, tile):
        span = slice(first, first + tile)
        for low, high, start, stop in head_windows(width):
            lanes = slice(start, stop)
            mask = lane_mask(low, high, stop - start, jnp.bfloat16)
            key_high = parts[2, span, lanes]
            query_high = parts[0, span, lanes] * mask
            scores = dot_nt(query_high, key_high)
            scores += dot_nt(parts[1, span, lanes] * mask, key_high)
            scores += dot_nt(query_high, parts[3, span, lanes]) + offset
            expons = jnp.exp(scores - jnp.max(scores, axis=-1, keepdims=True))
            probs = expons * (1.0 / jnp.sum(expons, axis=-1, keepdims=True))
            out = dot_nn(narrow(probs), parts[4, span, lanes] * mask)
            mixed[span, lanes] += out
    mixed_low[...] = narrow(mixed[...])
    source = mixed_low[...]
    for low, high in column_cuts(width):
        span = slice(low, high)
        proj_out[:, span] = dot_nn(source, blocks[3, :, span]) + bias[3:4, span]
    for first in range(0, rows, tile):
        span = slice(first, first + tile)
        resid = wide(tokens[span]) + valid_rows(count, tile, frames) * gate_one * proj_out[span]
        resid_out[span] = resid
        normed, _ = norm_parts(resid)
        mlp_in[span] = narrow(normed * (1.0 + scale_two) + shift_two)


def run_attention(frames, counts, tokens, cotangent, mods, bias, blocks):
    total, width = tokens.shape
    clips = mods.shape[0]
    rows = total // clips
    clip_rows = spec((rows, width), lambda clip: (clip, 0))
    low = jax.ShapeDtypeStruct((total, width), jnp.bfloat16)
    full = jax.ShapeDtypeStruct((total, width), jnp.float32)
    return pl.pallas_call(
        functools.partial(attention_kernel, frames),
        grid=(clips,),
        in_specs=[
            pl.BlockSpec(memory_space=pltpu.SMEM),
            clip_rows,
            clip_rows,
            spec((1,) + mods.shape[1:], lambda clip: (clip, 0, 0)),
            held(bias.shape),
            held(blocks.shape),
        ],
        out_specs=[
            clip_rows,
            spec((5, rows, width), lambda clip: (0, clip, 0)),
            clip_rows,
            clip_rows,
            clip_rows,
            clip_rows,
            clip_rows,
            spec((1, 1, width), lambda clip: (clip, 0, 0)),
        ],
        out_shape=[
            low,
            jax.ShapeDtypeStruct((5, total, width), jnp.bfloat16),
            low,
            full,
            full,
            low,
            low,
            jax.ShapeDtypeStruct((clips, 1, width), jnp.float32),
        ],
        scratch_shapes=[pltpu.VMEM((rows, width), jnp.float32)],
        compiler_params=pltpu.CompilerParams(vmem_limit_bytes=vmem_bytes),
        cost_estimate=pl.CostEstimate(
            flops=12 * total * width * width, bytes_accessed=40 * total * width, transcendentals=0
        ),
    )(counts, tokens, cotangent, mods, bias, blocks)


def hidden_kernel(mlp_in, block, bias, hidden, slope):
    root = (2.0 / math.pi) ** 0.5
    source = mlp_in[...]
    for low, high in column_cuts(block.shape[-1]):
        span = slice(low, high)
        pre = dot_nn(source, block[0, :, span]) + bias[0, :, span]
        square = pre * pre
        bent = jnp.tanh(root * pre * (1.0 + 0.044715 * square))
        half = 0.5 + 0.5 * bent
        hidden[0, :, span] = narrow(pre * half)
        steep = (0.5 * root) * pre * (1.0 + 3 * 0.044715 * square)
        slope[0, :, span] = narrow(half + steep * (1.0 - bent * bent))


def run_hidden(mlp_in, blocks, bias):
    total, width = mlp_in.shape
    count = blocks.shape[0]
    per_block = spec((1, total, width), lambda at: (at, 0, 0))
    out = jax.ShapeDtypeStruct((count, total, width), jnp.bfloat16)
    return pl.pallas_call(
        hidden_kernel,
        grid=(count,),
        in_specs=[
            held(mlp_in.shape),
            spec((1, width, width), lambda at: (at, 0, 0)),
            spec((1, 1, width), lambda at: (at, 0, 0)),
        ],
        out_specs=[per_block, per_block],
        out_shape=[out, out],
        compiler_params=pltpu.CompilerParams(vmem_limit_bytes=vmem_bytes),
        cost_estimate=pl.CostEstimate(
            flops=8 * total * width * width, bytes_accessed=30 * total * width, transcendentals=0
        ),
    )(mlp_in, blocks, bias)


def branch_kernel(
    frames,
    counts,
    hidden,
    slope,
    block,
    d_branch,
    bias,
    gates,
    resid,
    cotangent,
    d_pre,
    d_pre_sum,
    block_out,
    d_gate,
    branch,
):
    step, steps = pl.program_id(0), pl.num_programs(0)
    total, width = resid.shape
    clips = gates.shape[0]
    rows = total // clips
    source, back = hidden[0], d_branch[...]

    @pl.when(step == 0)
    def _():
        branch[...] = jnp.zeros_like(branch)

    for low, high in column_cuts(width):
        span = slice(low, high)
        d_hidden = dot_nt(back, block[0, span, :])
        low_back = narrow(d_hidden * wide(slope[0, :, span]))
        d_pre[0, :, span] = low_back
        d_pre_sum[0, :, span] = column_sum(wide(low_back))
        branch[:, span] += dot_nn(source, block[0, :, span])

    @pl.when(step == steps - 1)
    def _():
        for clip in range(clips):
            span = slice(clip * rows, (clip + 1) * rows)
            kept = valid_rows(counts[clip], rows, frames) * (branch[span] + bias[...])
            block_out[span] = narrow(resid[span] + gates[clip] * kept)
            d_gate[clip] = column_sum(wide(cotangent[span]) * kept)


def run_branch(frames, counts, hidden, slope, blocks, d_branch, bias, gates, resid, cotangent):
    count, total, width = hidden.shape
    clips = gates.shape[0]
    per_block = spec((1, total, width), lambda at: (at, 0, 0))
    low = jax.ShapeDtypeStruct((total, width), jnp.bfloat16)
    return pl.pallas_call(
        functools.partial(branch_kernel, frames),
        grid=(count,),
        in_specs=[
            pl.BlockSpec(memory_space=pltpu.SMEM),
            per_block,
            per_block,
            spec((1, width, width), lambda at: (at, 0, 0)),
            held((total, width)),
            held(bias.shape),
            held(gates.shape),
            held((total, width)),
            held((total, width)),
        ],
        out_specs=[
            per_block,
            spec((1, 1, width), lambda at: (at, 0, 0)),
            held((total, width)),
            held((clips, 1, width)),
        ],
        out_shape=[
            jax.ShapeDtypeStruct((count, total, width), jnp.bfloat16),
            jax.ShapeDtypeStruct((count, 1, width), jnp.float32),
            low,
            jax.ShapeDtypeStruct((clips, 1, width), jnp.float32),
        ],
        scratch_shapes=[pltpu.VMEM((total, width), jnp.float32)],
        compiler_params=pltpu.CompilerParams(vmem_limit_bytes=vmem_bytes),
        cost_estimate=pl.CostEstimate(
            flops=16 * total * width * width, bytes_accessed=40 * total * width, transcendentals=0
        ),
    )(counts, hidden, slope, blocks, d_branch, bias, gates, resid, cotangent)


def resid_kernel(
    frames,
    counts,
    d_pre,
    block,
    mods,
    resid,
    cotangent,
    proj,
    d_resid_out,
    d_proj,
    sums,
    total_grad,
):
    step, steps = pl.program_id(0), pl.num_programs(0)
    total, width = resid.shape
    clips = mods.shape[0]
    rows = total // clips
    tile = min(rows, 128)
    source = d_pre[0]

    @pl.when(step == 0)
    def _():
        total_grad[...] = jnp.zeros_like(total_grad)

    for low, high in column_cuts(width):
        span = slice(low, high)
        total_grad[:, span] += dot_nt(source, block[0, span, :])

    @pl.when(step == steps - 1)
    def _():
        for clip in range(clips):
            gate_one, scale_two = mods[clip, 2:3, :], mods[clip, 4:5, :]
            found = [0.0] * 4
            for first in range(clip * rows, (clip + 1) * rows, tile):
                span = slice(first, first + tile)
                grad = total_grad[span]
                normed, inverse = norm_parts(resid[span])
                back = norm_back(grad * (1.0 + scale_two), normed, inverse)
                d_resid = wide(cotangent[span]) + back
                d_resid_out[span] = d_resid
                kept = valid_rows(counts[clip], tile, frames) * d_resid
                low_back = narrow(kept * gate_one)
                d_proj[span] = low_back
                terms = (grad, grad * normed, kept * proj[span], wide(low_back))
                found = [old + column_sum(term) for old, term in zip(found, terms)]
            for at in range(4):
                sums[clip, at : at + 1, :] = found[at]


def run_resid(frames, counts, d_pre, blocks, mods, resid, cotangent, proj):
    count, total, width = d_pre.shape
    clips = mods.shape[0]
    return pl.pallas_call(
        functools.partial(resid_kernel, frames),
        grid=(count,),
        in_specs=[
            pl.BlockSpec(memory_space=pltpu.SMEM),
            spec((1, total, width), lambda at: (at, 0, 0)),
            spec((1, width, width), lambda at: (at, 0, 0)),
            held(mods.shape),
            held((total, width)),
            held((total, width)),
            held((total, width)),
        ],
        out_specs=[held((total, width)), held((total, width)), held((clips, 4, width))],
        out_shape=[
            jax.ShapeDtypeStruct((total, width), jnp.float32),
            jax.ShapeDtypeStruct((total, width), jnp.bfloat16),
            jax.ShapeDtypeStruct((clips, 4, width), jnp.float32),
        ],
        scratch_shapes=[pltpu.VMEM((total, width), jnp.float32)],
        compiler_params=pltpu.CompilerParams(vmem_limit_bytes=vmem_bytes),
        cost_estimate=pl.CostEstimate(
            flops=8 * total * width * width, bytes_accessed=40 * total * width, transcendentals=0
        ),
    )(counts, d_pre, blocks, mods, resid, cotangent, proj)


def attention_back_kernel(
    frames, counts, d_proj, parts, block, d_qkv, sums, d_mixed, d_query, d_key, d_value
):
    rows, width = d_proj.shape
    tile = min(rows, 128)
    count = counts[pl.program_id(0)]
    source = d_proj[...]
    for low, high in column_cuts(width):
        d_mixed[:, low:high] = narrow(dot_nt(source, block[0, low:high, :]))
    scale = (width // HEADS) ** -0.5
    offset = score_offset(count, tile, frames, 0)
    for ref in (d_query, d_key, d_value):
        ref[...] = jnp.zeros_like(ref)
    for first in range(0, rows, tile):
        span = slice(first, first + tile)
        for low, high, start, stop in head_windows(width):
            lanes = slice(start, stop)
            mask = lane_mask(low, high, stop - start, jnp.bfloat16)
            query_high = parts[0, span, lanes] * mask
            key_high = parts[2, span, lanes] * mask
            back = d_mixed[span, lanes] * mask
            scores = dot_nt(key_high, query_high)
            scores += dot_nt(key_high, parts[1, span, lanes])
            scores += dot_nt(parts[3, span, lanes], query_high) + offset
            expons = jnp.exp(scores - jnp.max(scores, axis=0, keepdims=True))
            probs = expons * (1.0 / jnp.sum(expons, axis=0, keepdims=True))
            d_probs = dot_nt(parts[4, span, lanes], back)
            inner = jnp.sum(d_probs * probs, axis=0, keepdims=True)
            d_scores = narrow(probs * (d_probs - inner))
            d_value[span, lanes] += dot_nn(narrow(probs), back)
            d_key[span, lanes] += dot_nn(d_scores, query_high)
            d_query[span, lanes] += dot_tn(d_scores, key_high)
    for at, ref in enumerate((d_query, d_key, d_value)):
        low_back = narrow(ref[...] * scale) if at == 0 else narrow(ref[...])
        d_qkv[at] = low_back
        sums[0, at : at + 1, :] = column_sum(wide(low_back))
    d_qkv[3] = source


def run_attention_back(frames, counts, d_proj, parts, block):
    total, width = d_proj.shape
    clips = counts.shape[0]
    rows = total // clips
    return pl.pallas_call(
        functools.partial(attention_back_kernel, frames),
        grid=(clips,),
        in_specs=[
            pl.BlockSpec(memory_space=pltpu.SMEM),
            spec((rows, width), lambda clip: (clip, 0)),
            spec((5, rows, width), lambda clip: (0, clip, 0)),
            spec((1, width, width), lambda clip: (3, 0, 0), pipeline_mode=pl.Buffered(1)),
        ],
        out_specs=[
            spec((4, rows, width), lambda clip: (0, clip, 0)),
            spec((1, 3, width), lambda clip: (clip, 0, 0)),
        ],
        out_shape=[
            jax.ShapeDtypeStruct((4, total, width), jnp.bfloat16),
            jax.ShapeDtypeStruct((clips, 3, width), jnp.float32),
        ],
        scratch_shapes=[pltpu.VMEM((rows, width), jnp.bfloat16)]
        + [pltpu.VMEM((rows, width), jnp.float32)] * 3,
        compiler_params=pltpu.CompilerParams(vmem_limit_bytes=vmem_bytes),
        cost_estimate=pl.CostEstimate(
            flops=12 * total * width * width, bytes_accessed=20 * total * width, transcendentals=0
        ),
    )(counts, d_proj, parts, block)


def input_kernel(d_qkv, block, mods, tokens, d_resid, input_grad, sums, total_grad):
    step, steps = pl.program_id(0), pl.num_programs(0)
    total, width = tokens.shape
    clips = mods.shape[0]
    rows = total // clips
    tile = min(rows, 128)
    source = d_qkv[0]

    @pl.when(step == 0)
    def _():
        total_grad[...] = jnp.zeros_like(total_grad)

    for low, high in column_cuts(width):
        span = slice(low, high)
        total_grad[:, span] += dot_nt(source, block[0, span, :])

    @pl.when(step == steps - 1)
    def _():
        for clip in range(clips):
            scale_one = mods[clip, 1:2, :]
            found = [0.0] * 2
            for first in range(clip * rows, (clip + 1) * rows, tile):
                span = slice(first, first + tile)
                grad = total_grad[span]
                normed, inverse = norm_parts(wide(tokens[span]))
                back = norm_back(grad * (1.0 + scale_one), normed, inverse)
                input_grad[span] = narrow(d_resid[span] + back)
                terms = (grad, grad * normed)
                found = [old + column_sum(term) for old, term in zip(found, terms)]
            for at in range(2):
                sums[clip, at : at + 1, :] = found[at]


def run_input(d_qkv, blocks, mods, tokens, d_resid):
    total, width = tokens.shape
    clips = mods.shape[0]
    return pl.pallas_call(
        input_kernel,
        grid=(3,),
        in_specs=[
            spec((1, total, width), lambda at: (at, 0, 0)),
            spec((1, width, width), lambda at: (at, 0, 0)),
            held(mods.shape),
            held((total, width)),
            held((total, width)),
        ],
        out_specs=[held((total, width)), held((clips, 2, width))],
        out_shape=[
            jax.ShapeDtypeStruct((total, width), jnp.bfloat16),
            jax.ShapeDtypeStruct((clips, 2, width), jnp.float32),
        ],
        scratch_shapes=[pltpu.VMEM((total, width), jnp.float32)],
        compiler_params=pltpu.CompilerParams(vmem_limit_bytes=vmem_bytes),
        cost_estimate=pl.CostEstimate(
            flops=6 * total * width * width, bytes_accessed=30 * total * width, transcendentals=0
        ),
    )(d_qkv, blocks, mods, tokens, d_resid)


def tie(*values):
    return lax.optimization_barrier(values)


def packed(arrays, tile):
    flat = jnp.concatenate([array.reshape(-1) for array in arrays])
    return jnp.pad(flat, (0, -flat.shape[0] % (tile * 128))).reshape(-1, 128)


def core_swap(array):
    count = lax.axis_size("dp")
    return lax.ppermute(array, "dp", [(at, at ^ 1) for at in range(count)])


def chip_shift(array, step):
    count = lax.axis_size("dp")
    return lax.ppermute(array, "dp", [(at, (at + 2 * step) % count) for at in range(count)])


def rank_swap(array, bits):
    count = lax.axis_size("fsdp")
    return lax.ppermute(array, "fsdp", [(at, at ^ bits) for at in range(count)])


def entry(array, at, axis=0):
    return lax.dynamic_index_in_dim(array, at, axis, keepdims=False)


def place_kernel(cuts, at, *refs):
    parts, whole, held_rows, semaphores = refs[:-3], refs[-3], refs[-2], refs[-1]
    spans, loads, stores = [], [], []
    for index, (part, first, rows) in enumerate(cuts):
        spans.append(pl.ds(pl.multiple_of(at[index] * 16, 16), rows))
        source = parts[part].at[pl.ds(first, rows)]
        loads.append(
            pltpu.make_async_copy(source, held_rows.at[spans[index]], semaphores.at[0, index])
        )
        loads[index].start()
    for index, span in enumerate(spans):
        loads[index].wait()
        stores.append(
            pltpu.make_async_copy(held_rows.at[span], whole.at[span], semaphores.at[1, index])
        )
        stores[index].start()
    for store in stores:
        store.wait()


def place(parts, cuts, starts, rows):
    width = parts[0].shape[-1]
    dtype = parts[0].dtype
    return pl.pallas_call(
        functools.partial(place_kernel, cuts),
        in_specs=[pl.BlockSpec(memory_space=pltpu.SMEM)]
        + [pl.BlockSpec(memory_space=pl.ANY)] * len(parts),
        out_specs=pl.BlockSpec(memory_space=pl.ANY),
        out_shape=jax.ShapeDtypeStruct((rows, width), dtype),
        scratch_shapes=[
            pltpu.VMEM((rows, width), dtype),
            pltpu.SemaphoreType.DMA((2, len(cuts))),
        ],
        compiler_params=pltpu.CompilerParams(vmem_limit_bytes=vmem_bytes),
        cost_estimate=pl.CostEstimate(
            flops=0, bytes_accessed=4 * rows * width, transcendentals=0
        ),
    )(jnp.stack([jnp.asarray(start, jnp.int32) for start in starts]), *parts)


def own_rows(parts, group):
    ranks, at = lax.axis_size("fsdp"), lax.axis_index("fsdp")
    shares = ranks // group
    count, _, row_part, col_part = parts.shape
    chunk = row_part // shares
    split = parts.reshape(count, group, shares, chunk, col_part).transpose(1, 2, 0, 3, 4)
    split = split.reshape(ranks, count, chunk, col_part)
    if shares > 1:
        moved = lax.all_to_all(split, "fsdp", 0, 0, tiled=True)
        (moved,) = yield (moved,)
        yield moved.transpose(1, 2, 0, 3).reshape(count, chunk, ranks * col_part)
        return
    panels = [entry(split, at)]
    panels += [rank_swap(entry(split, at ^ bits), bits) for bits in range(1, ranks)]
    panels = yield tuple(panels)
    placed = [
        lax.select_n(at, *[panels[panel ^ index] for index in range(ranks)])
        for panel in range(ranks)
    ]
    yield jnp.concatenate(placed, axis=2)


def shard_rows(split, group):
    ranks, count, chunk, col_part = split.shape
    shares = ranks // group
    moved = lax.all_to_all(split, "fsdp", 0, 0, tiled=True)
    moved = moved.reshape(group, shares, count, chunk, col_part).transpose(2, 0, 1, 3, 4)
    return moved.reshape(count, group, shares * chunk, col_part)


def gather_blocks(rows, group):
    ranks, dp_count = lax.axis_size("fsdp"), lax.axis_size("dp")
    shares = ranks // group
    chunk, total = rows.shape
    all_rows = lax.all_gather(rows, ("fsdp", "dp"), axis=0, tiled=True)
    if shares > 1:
        all_rows = all_rows.reshape(group, shares, dp_count, chunk, total).transpose(0, 2, 1, 3, 4)
    return all_rows.reshape(group, total, total)


def gather_pieces(rows, group):
    ranks, at = lax.axis_size("fsdp"), lax.axis_index("fsdp")
    if ranks != group:
        blocks = gather_blocks(rows, group)
        (blocks,) = yield (blocks,)
        (blocks,) = yield (blocks,)
        yield blocks
        return
    chips = lax.axis_size("dp") // 2
    core, chip = lax.axis_index("dp") % 2, lax.axis_index("dp") // 2
    chunk, total = rows.shape
    half = total // 2
    unit = chunk // 16
    found = [rows] + [chip_shift(rows, step) for step in range(1, chips)]
    starts = [(chip - step) % chips * unit for step in range(chips)]
    line = place(found, [(step, 0, chunk) for step in range(chips)], starts, half)
    cuts = [(side, step * chunk, chunk) for side in range(2) for step in range(chips)]
    starts = [(2 * step + side) * unit for side in (core, 1 - core) for step in range(chips)]
    own = place([line, core_swap(line)], cuts, starts, total)
    (own,) = yield (own,)
    share = lax.dynamic_slice_in_dim(own, core * half, half, 0)
    mine = [rank_swap(share, bits) for bits in range(1, ranks)]
    own, *mine = yield (own, *mine)
    others = [core_swap(part) for part in mine]
    starts = [at * 2] + [
        (at ^ bits) * 2 + side for side in (core, 1 - core) for bits in range(1, ranks)
    ]
    starts = [start * (half // 16) for start in starts]
    cuts = [(0, 0, total)] + [(1 + index, 0, half) for index in range(2 * ranks - 2)]
    found = place([own] + mine + others, cuts, starts, group * total)
    yield found.reshape(group, total, total)


def gather_own(rows, group):
    ranks = lax.axis_size("fsdp")
    shares = ranks // group
    if shares > 1:
        sets = [[share + shares * block for share in range(shares)] for block in range(group)]
        rows = lax.all_gather(rows, "fsdp", axis=1, tiled=True, axis_index_groups=sets)
    return lax.all_gather(rows, "dp", axis=1, tiled=True)


def sum_blocks(product, cut, total, group):
    ranks, dp_count = lax.axis_size("fsdp"), lax.axis_size("dp")
    shares = ranks // group
    if shares > 1:
        blocks = narrow(product(cut(0, total)))
        chunk = total // (dp_count * shares)
        blocks = blocks.reshape(group, dp_count, shares, chunk, -1).transpose(0, 2, 1, 3, 4)
        rows = lax.psum_scatter(
            blocks.reshape(group * total, -1), ("fsdp", "dp"), scatter_dimension=0, tiled=True
        )
        for _ in range(3):
            (rows,) = yield (rows,)
        yield gather_own(rows[None], group)[0]
        return
    chips, half = dp_count // 2, total // 2
    chunk = half // chips
    core, chip = lax.axis_index("dp") % 2, lax.axis_index("dp") // 2
    low_bit, high_bit = lax.axis_index("fsdp") % 2, lax.axis_index("fsdp") // 2
    away = narrow(product(cut((1 - core) * half, half)))
    here = product(cut(core * half, half))
    here = narrow(here + wide(core_swap(away)))
    here = here.reshape(2, 2, chips, chunk, -1)
    middle = chips // 2
    first, second = here[:, :, :middle], here[:, :, middle:]
    first_in = rank_swap(entry(first, 1 - low_bit, 1), 1)
    second_in = rank_swap(entry(second, 1 - high_bit, 0), 2)
    first_in, second_in = yield (first_in, second_in)
    first = narrow(wide(entry(first, low_bit, 1)) + wide(first_in))
    second = narrow(wide(entry(second, high_bit, 0)) + wide(second_in))
    first_in = rank_swap(entry(first, 1 - high_bit), 2)
    second_in = rank_swap(entry(second, 1 - low_bit), 1)
    first_in, second_in = yield (first_in, second_in)
    first = narrow(wide(entry(first, high_bit)) + wide(first_in))
    second = narrow(wide(entry(second, low_bit)) + wide(second_in))
    line = jnp.concatenate([first, second])
    parts = [chip_shift(entry(line, (chip + step) % chips), step) for step in range(1, chips)]
    parts = yield tuple(parts)
    rows = sum([wide(part) for part in parts], wide(entry(line, chip)))
    yield lax.all_gather(narrow(rows), "dp", axis=0, tiled=True)


def fast_dot(subscripts, left, right):
    return jnp.einsum(subscripts, left, right, preferred_element_type=jnp.float32)


def products_kernel(chips, at, gathered, left_root, right_root, out, whole, semaphores):
    chunk, width = left_root.shape
    ranks = out.shape[0]
    copies = []
    for index in range(2 * chips):
        first = (index % 2 * chips + index // 2) * chunk
        copies.append(
            pltpu.make_async_copy(
                gathered.at[pl.ds(index * chunk, chunk)],
                whole.at[pl.ds(first, chunk)],
                semaphores.at[index],
            )
        )
        copies[-1].start()
    for copy in copies:
        copy.wait()
    first = at[0] * 16
    grad = whole[...]
    picked = lax.broadcasted_iota(jnp.int32, (width, chunk), 0) - first
    picked = picked == lax.broadcasted_iota(jnp.int32, (width, chunk), 1)
    own_columns = narrow(dot_nn(grad, narrow(picked.astype(jnp.float32))))
    side_high, side_low = split_high(dot_nn(left_root[...], grad))
    right = right_root[...]
    precond = dot_nn(side_high, right) + dot_nn(side_low, right)
    outer = dot_nt(whole[pl.ds(pl.multiple_of(first, 16), chunk), :], grad)
    inner = dot_tn(own_columns, grad)
    for at_out, product in enumerate((precond, outer, inner)):
        low = narrow(product)
        for rank in range(ranks):
            span = slice(rank * (width // ranks), (rank + 1) * (width // ranks))
            out[rank, at_out] = low[:, span]


def owned_step(whole, left_root, right_root, group):
    ranks, dp_count = lax.axis_size("fsdp"), lax.axis_size("dp")
    shares = ranks // group
    chunk, total = left_root.shape
    col_part = total // ranks
    first = lax.axis_index("dp") * (chunk * shares) + lax.axis_index("fsdp") % shares * chunk
    if shares == 1:
        return pl.pallas_call(
            functools.partial(products_kernel, dp_count // 2),
            in_specs=[
                pl.BlockSpec(memory_space=pltpu.SMEM),
                pl.BlockSpec(memory_space=pl.ANY),
                pl.BlockSpec(memory_space=pltpu.VMEM),
                pl.BlockSpec(memory_space=pltpu.VMEM),
            ],
            out_specs=pl.BlockSpec(memory_space=pltpu.VMEM),
            out_shape=jax.ShapeDtypeStruct((ranks, 3, chunk, col_part), jnp.bfloat16),
            scratch_shapes=[
                pltpu.VMEM((total, total), jnp.bfloat16),
                pltpu.SemaphoreType.DMA((dp_count,)),
            ],
            compiler_params=pltpu.CompilerParams(vmem_limit_bytes=vmem_bytes),
            cost_estimate=pl.CostEstimate(
                flops=12 * chunk * total * total, bytes_accessed=6 * total * total, transcendentals=0
            ),
        )((first // 16)[None], whole, left_root, right_root)
    grad_rows = lax.dynamic_slice_in_dim(whole, first, chunk, 0)
    own_columns = lax.dynamic_slice_in_dim(whole, first, chunk, 1)
    outer = fast_dot("rk,jk->rj", grad_rows, whole)
    inner = fast_dot("kr,kj->rj", own_columns, whole)
    side_high, side_low = split_high(fast_dot("rk,kj->rj", left_root, whole))
    precond = fast_dot("rk,kj->rj", side_high, right_root) + fast_dot(
        "rk,kj->rj", side_low, right_root
    )
    products = narrow(jnp.stack([precond, outer, inner]))
    return products.reshape(3, chunk, ranks, col_part).transpose(2, 0, 1, 3)


def per_device(
    tokens,
    conditioning,
    frame_counts,
    cotangent,
    weights,
    biases,
    momentum,
    left_stats,
    right_stats,
    left_roots,
    right_roots,
    bias_moment,
    bias_second,
):
    group = 4
    mod_count = 6
    clip_count, pos_count, frames, width = tokens.shape
    token_count = clip_count * pos_count * frames
    block_count, row_part, col_part = weights.shape
    dp_count, ranks = lax.axis_size("dp"), lax.axis_size("fsdp")
    dp_at, rank_at = lax.axis_index("dp"), lax.axis_index("fsdp")
    all_clips = clip_count * dp_count
    bias_part = biases.shape[0]
    stream = tokens.reshape(token_count, width)
    grad_out = cotangent.reshape(token_count, width)
    low_weights = narrow(weights).reshape(block_count, row_part, col_part)
    shards = low_weights[mod_count:].reshape(-1, group, row_part, col_part)

    attn_rows, cond_low = own_rows(shards[:1], group), narrow(jax.nn.silu(conditioning))
    attn_panels = next(attn_rows)
    first_parts = lax.all_gather(packed([cond_low, narrow(biases)], 16), "dp", axis=0, tiled=True)
    attn_panels, first_parts, other_shards = tie(attn_panels, first_parts, shards[1:])
    attn_w = gather_blocks(attn_rows.send(attn_panels)[0], group)
    other_rows = own_rows(other_shards, group)
    other_rows = other_rows.send(next(other_rows))
    one_steps = gather_pieces(other_rows[0], group)
    one_parts, first_parts = tie(next(one_steps), first_parts)
    one_parts = one_steps.send(one_parts)
    two_w = gather_blocks(other_rows[1], group)
    roots = jnp.stack([narrow(left_roots[mod_count:]), narrow(right_roots[mod_count:])])
    roots, first_parts = tie(roots, first_parts)
    root_rows = own_rows(roots.reshape(-1, group, row_part, col_part), group)
    root_panels = next(root_rows)

    first_parts = first_parts.reshape(dp_count, -1)
    cond_all = first_parts[:, : clip_count * width].reshape(all_clips, width)
    bias_rows = wide(first_parts[:, clip_count * width : clip_count * width + bias_part])
    cond_rows = lax.dynamic_slice_in_dim(cond_all, dp_at * row_part, row_part, 1)
    cond_cols = wide(lax.dynamic_slice_in_dim(cond_all, rank_at * col_part, col_part, 1))
    mod_parts = fast_dot("cr,jre->cje", cond_rows, low_weights[:mod_count])
    mod_parts = lax.all_to_all(mod_parts, "dp", 0, 0, tiled=True)
    mod_cols = jnp.sum(mod_parts.reshape(dp_count, clip_count, mod_count, col_part), axis=0)
    left_cond = jnp.einsum("jrk,ck->jrc", left_roots[:mod_count], cond_cols, precision=precise)
    mod_size, bias_size = mod_cols.size, dp_count * bias_part
    second_parts = lax.all_gather(
        packed([mod_cols, bias_rows, left_cond], 8), "fsdp", axis=0, tiled=True
    ).reshape(ranks, -1)
    mods = second_parts[:, :mod_size].reshape(ranks, clip_count, mod_count, col_part)
    mods = mods.transpose(1, 2, 0, 3).reshape(clip_count, mod_count, width)
    bias_all = second_parts[:, mod_size : mod_size + bias_size].reshape(ranks, dp_count, bias_part)
    bias_all = bias_all.transpose(1, 0, 2).reshape(-1, width)
    left_size = mod_size + bias_size + left_cond.size
    left_cond = jnp.sum(second_parts[:, mod_size + bias_size : left_size], axis=0)
    left_cond = left_cond.reshape(mod_count, row_part, all_clips)
    mods = mods + bias_all[:mod_count]
    bias_table = jnp.concatenate(
        [bias_all[6:7], jnp.zeros((1, width), jnp.float32), bias_all[7:14]]
    )

    attn_in, parts, mixed, proj, resid, mlp_in, d_branch, d_branch_sums = run_attention(
        frames, frame_counts, stream, grad_out, mods, bias_table, attn_w
    )
    mlp_in, one_parts, root_panels = tie(mlp_in, one_parts, root_panels)
    one_w = one_steps.send(one_parts)
    hidden, slope = run_hidden(mlp_in, one_w, bias_table[4:8, None])
    two_steps = sum_blocks(
        lambda left: fast_dot("jtd,te->jde", left, d_branch),
        lambda first, size: lax.dynamic_slice_in_dim(hidden, first, size, 2),
        width,
        group,
    )
    two_parts = list(next(two_steps))
    root_rows = root_rows.send(root_panels)
    hidden, two_parts[0], root_rows = tie(hidden, two_parts[0], root_rows)
    left_rows, right_rows = jnp.split(root_rows, 2)
    right_wholes = [gather_own(rows[None], group)[0] for rows in right_rows]

    d_pre, d_pre_sums, block_out, d_gate_two = run_branch(
        frames,
        frame_counts,
        hidden,
        slope,
        two_w,
        d_branch,
        bias_table[8:9],
        mods[:, 5:6],
        resid,
        grad_out,
    )
    d_pre, two_parts = tie(d_pre, two_parts)
    two_parts = list(two_steps.send(two_parts))
    one_steps = sum_blocks(
        lambda left: fast_dot("td,jte->jde", left, d_pre),
        lambda first, size: lax.dynamic_slice_in_dim(mlp_in, first, size, 1),
        width,
        group,
    )
    one_parts = list(next(one_steps))
    d_pre, one_parts[0], two_parts = tie(d_pre, one_parts[0], two_parts)
    two_parts = two_steps.send(two_parts)
    d_resid, d_proj, resid_sums = run_resid(
        frames, frame_counts, d_pre, one_w, mods, resid, grad_out, proj
    )
    d_proj, one_parts = tie(d_proj, one_parts)
    one_parts = one_steps.send(one_parts)
    d_heads, head_sums = run_attention_back(frames, frame_counts, d_proj, parts, attn_w)
    d_heads, one_parts, two_parts = tie(d_heads, one_parts, two_parts)
    whole_two = two_steps.send(two_parts)
    attn_steps = sum_blocks(
        lambda left: fast_dot("jtd,jte->jde", left, d_heads),
        lambda first, size: jnp.stack(
            [lax.dynamic_slice_in_dim(left, first, size, 1) for left in (attn_in,) * 3 + (mixed,)]
        ),
        width,
        group,
    )
    attn_parts = list(next(attn_steps))
    d_heads, attn_parts[0], one_parts = tie(d_heads, attn_parts[0], one_parts)
    one_parts = one_steps.send(one_parts)
    input_grad, input_sums = run_input(d_heads, attn_w, mods, stream, d_resid)
    products_two = owned_step(whole_two, left_rows[2], right_wholes[2], group)
    input_sums, attn_parts, one_parts, products_two = tie(
        input_sums, attn_parts, one_parts, products_two
    )
    attn_parts = attn_steps.send(attn_parts)
    whole_one = one_steps.send(one_parts)

    d_mods = jnp.stack(
        [
            input_sums[:, 0],
            input_sums[:, 1],
            resid_sums[:, 2],
            resid_sums[:, 0],
            resid_sums[:, 1],
            d_gate_two[:, 0],
        ],
        axis=1,
    )
    head_sums = jnp.sum(head_sums, axis=0)
    grad_bias = jnp.concatenate(
        [
            jnp.sum(d_mods, axis=0),
            head_sums[0:1],
            head_sums[2:3],
            jnp.sum(resid_sums[:, 3], axis=0)[None],
            d_pre_sums[:, 0],
            jnp.sum(d_branch_sums, axis=0),
        ]
    )
    to_ranks = jnp.concatenate(
        [
            d_mods.reshape(clip_count, mod_count, ranks, col_part)
            .transpose(2, 0, 1, 3)
            .reshape(ranks, mod_size),
            grad_bias.reshape(dp_count, ranks, bias_part)
            .transpose(1, 0, 2)
            .reshape(ranks, bias_size),
        ],
        axis=1,
    )
    rank_sums = jnp.sum(lax.all_to_all(to_ranks, "fsdp", 0, 0, tiled=True), axis=0)
    to_rows = jnp.concatenate(
        [
            jnp.broadcast_to(rank_sums[None, :mod_size], (dp_count, mod_size)),
            rank_sums[mod_size:].reshape(dp_count, bias_part),
        ],
        axis=1,
    )
    to_rows, attn_parts = tie(to_rows, attn_parts)
    attn_parts = attn_steps.send(attn_parts)
    from_rows = lax.all_to_all(to_rows, "dp", 0, 0, tiled=True)
    back_two = shard_rows(products_two, group)
    bias_grad = jnp.sum(from_rows[:, mod_size:], axis=0)
    mod_grad_cols = from_rows[:, :mod_size].reshape(all_clips, mod_count, col_part)
    mod_grad = lax.all_gather(packed([mod_grad_cols], 8), "fsdp", axis=0, tiled=True)
    mod_grad = mod_grad.reshape(ranks, -1)[:, : mod_grad_cols.size]
    mod_grad = mod_grad.reshape(ranks, all_clips, mod_count, col_part).transpose(1, 2, 0, 3)
    mod_grad = mod_grad.reshape(all_clips, mod_count, width)

    mod_grad_rows = lax.dynamic_slice_in_dim(mod_grad, dp_at * row_part, row_part, 2)
    right_parts = jnp.einsum(
        "cjk,jke->cje", mod_grad_rows, right_roots[:mod_count], precision=precise
    )
    cond_wide = wide(cond_all)
    cond_row_wide = wide(cond_rows)
    mod_gram = jnp.einsum("cjk,bjk->jcb", mod_grad, mod_grad, precision=precise)
    cond_gram = jnp.einsum("ck,bk->cb", cond_wide, cond_wide, precision=precise)
    mod_side = jnp.einsum("jcb,be->jce", mod_gram, cond_cols, precision=precise)
    ada_left = jnp.einsum("cr,jce->jre", cond_row_wide, mod_side, precision=precise)
    cond_side = jnp.einsum("cb,bje->jce", cond_gram, mod_grad_cols, precision=precise)
    ada_right = jnp.einsum("cjr,jce->jre", mod_grad_rows, cond_side, precision=precise)

    products_one = owned_step(whole_one, left_rows[1], right_wholes[1], group)
    back_two, products_one, right_parts, attn_parts = tie(
        back_two, products_one, right_parts, attn_parts
    )
    whole_attn = attn_steps.send(attn_parts)
    back_one = shard_rows(products_one, group)
    right_parts = lax.all_gather(packed([right_parts], 8), "dp", axis=0, tiled=True)
    mod_right = jnp.sum(right_parts.reshape(dp_count, -1), axis=0)[: mod_grad_cols.size]
    mod_right = mod_right.reshape(all_clips, mod_count, col_part)
    ada_pre = jnp.einsum("jrc,cje->jre", left_cond, mod_right, precision=precise)
    whole_attn, back_one, ada_pre, ada_left, ada_right = tie(
        whole_attn, back_one, ada_pre, ada_left, ada_right
    )
    back_attn = shard_rows(owned_step(whole_attn, left_rows[0], right_wholes[0], group), group)

    def joined(at, ada):
        return jnp.concatenate([ada, wide(back_attn[at]), wide(back_one[at]), wide(back_two[at])])

    precond = joined(0, ada_pre)
    left_new = stat_decay * left_stats + (1.0 - stat_decay) * joined(1, ada_left)
    right_new = stat_decay * right_stats + (1.0 - stat_decay) * joined(2, ada_right)
    momentum_new = moment_decay * momentum + precond
    weights_new = weights - weight_rate * momentum_new
    weights_copy = weights_new.astype(jnp.bfloat16)
    bias_second_new = stat_decay * bias_second + (1.0 - stat_decay) * bias_grad * bias_grad
    bias_moment_new = moment_decay * bias_moment + bias_grad * lax.rsqrt(
        bias_second_new + diag_epsilon
    )
    biases_new = biases - bias_rate * bias_moment_new
    return (
        block_out.reshape(tokens.shape),
        input_grad.reshape(tokens.shape),
        left_new,
        right_new,
        momentum_new,
        weights_new,
        weights_copy,
        bias_moment_new,
        bias_second_new,
        biases_new,
    )


def solution(mesh):
    placed = (
        P("dp", "fsdp", None, None),
        P("dp", None),
        P("dp"),
        P("dp", "fsdp", None, None),
        P(None, "dp", "fsdp"),
        P(("dp", "fsdp")),
        P(None, "dp", "fsdp"),
        P(None, "dp", "fsdp"),
        P(None, "dp", "fsdp"),
        P(None, "dp", "fsdp"),
        P(None, "dp", "fsdp"),
        P(("dp", "fsdp")),
        P(("dp", "fsdp")),
    )
    return jax.shard_map(
        per_device,
        mesh=mesh,
        in_specs=placed,
        out_specs=(
            P("dp", "fsdp", None, None),
            P("dp", "fsdp", None, None),
            P(None, "dp", "fsdp"),
            P(None, "dp", "fsdp"),
            P(None, "dp", "fsdp"),
            P(None, "dp", "fsdp"),
            P(None, "dp", "fsdp"),
            P(("dp", "fsdp")),
            P(("dp", "fsdp")),
            P(("dp", "fsdp")),
        ),
        check_vma=False,
    )
```

```python
import functools
import math

import jax
import jax.numpy as jnp
from jax import lax
from jax.experimental import pallas as pl
from jax.experimental.pallas import tpu as pltpu
from jax.sharding import PartitionSpec as P

HEADS = 16


precise = lax.Precision.HIGHEST
norm_epsilon = 1e-06
masked_score = -1e30
stat_decay = 0.5
moment_decay = 0.9
weight_rate = 0.7
bias_rate = 0.1
diag_epsilon = 1e-08
vmem_bytes = 50 * 2**20


def narrow(array):
    return array.astype(jnp.bfloat16)


def wide(array):
    return array.astype(jnp.float32)


def spec(shape, index_map, **keywords):
    return pl.BlockSpec(shape, index_map, **keywords)


def held(shape):
    return pl.BlockSpec(shape, lambda step: (0,) * len(shape), pipeline_mode=pl.Buffered(1))


def column_cuts(total):
    cuts, at = [], 0
    while at < total:
        cuts.append((at, min(total, at + 256)))
        at += 256
    return cuts


def dot_nn(left, right):
    return lax.dot_general(left, right, (((1,), (0,)), ((), ())), preferred_element_type=jnp.float32)


def dot_nt(left, right):
    return lax.dot_general(left, right, (((1,), (1,)), ((), ())), preferred_element_type=jnp.float32)


def dot_tn(left, right):
    return lax.dot_general(left, right, (((0,), (0,)), ((), ())), preferred_element_type=jnp.float32)


def split_high(values):
    high = narrow(values)
    return high, narrow(values - wide(high))


def valid_rows(count, rows, frames):
    at = lax.broadcasted_iota(jnp.int32, (rows, 1), 0)
    return (lax.rem(at, frames) < count).astype(jnp.float32)


def score_offset(count, size, frames, key_axis):
    first = lax.broadcasted_iota(jnp.int32, (size, size), 0)
    second = lax.broadcasted_iota(jnp.int32, (size, size), 1)
    key = second if key_axis == 1 else first
    met = (lax.div(first, frames) == lax.div(second, frames)) & (lax.rem(key, frames) < count)
    return jnp.where(met, 0.0, masked_score)


def head_windows(width):
    size = width // HEADS
    windows = []
    for head in range(HEADS):
        low, high = head * size, (head + 1) * size
        start = low // 128 * 128
        stop = min(width, -(-high // 128) * 128)
        windows.append((low - start, high - start, start, stop))
    return windows


def lane_mask(low, high, count, dtype):
    lanes = lax.broadcasted_iota(jnp.int32, (1, count), 1)
    return ((lanes >= low) & (lanes < high)).astype(jnp.float32).astype(dtype)


def norm_parts(values):
    centered = values - jnp.mean(values, axis=-1, keepdims=True)
    variance = jnp.mean(centered * centered, axis=-1, keepdims=True)
    inverse = lax.rsqrt(variance + norm_epsilon)
    return centered * inverse, inverse


def norm_back(grad, normed, inverse):
    first = jnp.mean(grad, axis=-1, keepdims=True)
    second = jnp.mean(grad * normed, axis=-1, keepdims=True)
    return (grad - first - normed * second) * inverse


def column_sum(values):
    return jnp.sum(values, axis=0, keepdims=True)


def start_loads(cuts, at, parts, whole, semaphores, first_index=0):
    loads = []
    for index, (part, first, rows) in enumerate(cuts, first_index):
        span = pl.ds(pl.multiple_of(at[index] * 16, 16), rows)
        source = parts[part].at[pl.ds(first, rows)]
        loads.append(pltpu.make_async_copy(source, whole.at[span], semaphores.at[index]))
        loads[-1].start()
    return loads


def attention_kernel(
    frames,
    cuts,
    counts,
    starts,
    tokens,
    cotangent,
    mods,
    bias,
    *refs,
):
    whole_out, attn_in, parts, mixed_low, proj_out, resid_out, mlp_in, d_branch, d_branch_sum = refs[
        -13:-4
    ]
    mixed, whole, semaphores, store_semaphore = refs[-4:]
    pieces = refs[:-13]
    rows, width = tokens.shape
    clip, clips = pl.program_id(0), pl.num_programs(0)
    blocks = [whole.at[pl.ds(index * width, width)] for index in range(4)]
    store = pltpu.make_async_copy(whole, whole_out, store_semaphore)

    @pl.when(clip == 0)
    def _():
        start_loads(cuts, starts, pieces, whole, semaphores)
    tile = min(rows, 128)
    count = counts[pl.program_id(0)]
    shift_one, scale_one, gate_one = (mods[0, at : at + 1, :] for at in range(3))
    shift_two, scale_two, gate_two = (mods[0, at : at + 1, :] for at in range(3, 6))
    for first in range(0, rows, tile):
        span = slice(first, first + tile)
        normed, _ = norm_parts(wide(tokens[span]))
        attn_in[span] = narrow(normed * (1.0 + scale_one) + shift_one)
        branch_back = narrow(wide(cotangent[span]) * valid_rows(count, tile, frames) * gate_two)
        d_branch[span] = branch_back
        part_sum = column_sum(wide(branch_back))
        d_branch_sum[0] = part_sum if first == 0 else d_branch_sum[0] + part_sum

    @pl.when(clip == 0)
    def _():
        for index, (part, first, size) in enumerate(cuts):
            span = pl.ds(pl.multiple_of(starts[index] * 16, 16), size)
            source = pieces[part].at[pl.ds(first, size)]
            pltpu.make_async_copy(source, whole.at[span], semaphores.at[index]).wait()
        store.start()

    scale = (width // HEADS) ** -0.5
    source = attn_in[...]
    for low, high in column_cuts(width):
        span = slice(low, high)
        query = (dot_nn(source, blocks[0][:, span]) + bias[0:1, span]) * scale
        parts[0, :, span], parts[1, :, span] = split_high(query)
        parts[2, :, span], parts[3, :, span] = split_high(dot_nn(source, blocks[1][:, span]))
        parts[4, :, span] = narrow(dot_nn(source, blocks[2][:, span]) + bias[2:3, span])
    offset = score_offset(count, tile, frames, 1)
    mixed[...] = jnp.zeros_like(mixed)
    for first in range(0, rows, tile):
        span = slice(first, first + tile)
        for low, high, start, stop in head_windows(width):
            lanes = slice(start, stop)
            mask = lane_mask(low, high, stop - start, jnp.bfloat16)
            key_high = parts[2, span, lanes]
            query_high = parts[0, span, lanes] * mask
            scores = dot_nt(query_high, key_high)
            scores += dot_nt(parts[1, span, lanes] * mask, key_high)
            scores += dot_nt(query_high, parts[3, span, lanes]) + offset
            expons = jnp.exp(scores - jnp.max(scores, axis=-1, keepdims=True))
            probs = expons * (1.0 / jnp.sum(expons, axis=-1, keepdims=True))
            out = dot_nn(narrow(probs), parts[4, span, lanes] * mask)
            mixed[span, lanes] += out
    mixed_low[...] = narrow(mixed[...])
    source = mixed_low[...]
    for low, high in column_cuts(width):
        span = slice(low, high)
        proj_out[:, span] = dot_nn(source, blocks[3][:, span]) + bias[3:4, span]
    for first in range(0, rows, tile):
        span = slice(first, first + tile)
        resid = wide(tokens[span]) + valid_rows(count, tile, frames) * gate_one * proj_out[span]
        resid_out[span] = resid
        normed, _ = norm_parts(resid)
        mlp_in[span] = narrow(normed * (1.0 + scale_two) + shift_two)

    @pl.when(clip == clips - 1)
    def _():
        store.wait()


def run_attention(frames, counts, tokens, cotangent, mods, bias, gathered):
    pieces, cuts, starts = gathered
    total, width = tokens.shape
    clips = mods.shape[0]
    rows = total // clips
    clip_rows = spec((rows, width), lambda clip: (clip, 0))
    low = jax.ShapeDtypeStruct((total, width), jnp.bfloat16)
    full = jax.ShapeDtypeStruct((total, width), jnp.float32)
    return pl.pallas_call(
        functools.partial(attention_kernel, frames, cuts),
        grid=(clips,),
        in_specs=[
            pl.BlockSpec(memory_space=pltpu.SMEM),
            pl.BlockSpec(memory_space=pltpu.SMEM),
            clip_rows,
            clip_rows,
            spec((1,) + mods.shape[1:], lambda clip: (clip, 0, 0)),
            held(bias.shape),
        ]
        + [pl.BlockSpec(memory_space=pl.ANY)] * len(pieces),
        out_specs=[
            pl.BlockSpec(memory_space=pl.ANY),
            clip_rows,
            spec((5, rows, width), lambda clip: (0, clip, 0)),
            clip_rows,
            clip_rows,
            clip_rows,
            clip_rows,
            clip_rows,
            spec((1, 1, width), lambda clip: (clip, 0, 0)),
        ],
        out_shape=[
            jax.ShapeDtypeStruct((4 * width, width), jnp.bfloat16),
            low,
            jax.ShapeDtypeStruct((5, total, width), jnp.bfloat16),
            low,
            full,
            full,
            low,
            low,
            jax.ShapeDtypeStruct((clips, 1, width), jnp.float32),
        ],
        scratch_shapes=[
            pltpu.VMEM((rows, width), jnp.float32),
            pltpu.VMEM((4 * width, width), jnp.bfloat16),
            pltpu.SemaphoreType.DMA((len(cuts),)),
            pltpu.SemaphoreType.DMA,
        ],
        compiler_params=pltpu.CompilerParams(vmem_limit_bytes=vmem_bytes),
        cost_estimate=pl.CostEstimate(
            flops=16 * total * width * width, bytes_accessed=100 * total * width, transcendentals=0
        ),
    )(counts, stacked(starts), tokens, cotangent, mods, bias, *pieces)


def stacked(numbers):
    return jnp.stack([jnp.asarray(number, jnp.int32) for number in numbers])


def hidden_kernel(cuts, order, starts, mlp_in, bias, *refs):
    whole_out, hidden, slope, whole, semaphores, store_semaphores = refs[-6:]
    pieces = refs[:-6]
    step, steps = pl.program_id(0), pl.num_programs(0)
    width = mlp_in.shape[-1]
    flat = [cut for group in cuts for cut in group]
    span = pl.ds(pl.multiple_of(order[step] * width, width), width)

    @pl.when(step == 0)
    def _():
        start_loads(flat, starts, pieces, whole, semaphores)

    index = 0
    for at, group in enumerate(cuts):
        first_index = index
        index += len(group)

        @pl.when(step == at)
        def _(group=group, first_index=first_index):
            for offset, (part, first, size) in enumerate(group):
                target = pl.ds(pl.multiple_of(starts[first_index + offset] * 16, 16), size)
                pltpu.make_async_copy(
                    pieces[part].at[pl.ds(first, size)],
                    whole.at[target],
                    semaphores.at[first_index + offset],
                ).wait()

    pltpu.make_async_copy(whole.at[span], whole_out.at[span], store_semaphores.at[step]).start()
    root = (2.0 / math.pi) ** 0.5
    source = mlp_in[...]
    block = whole.at[span]
    for low, high in column_cuts(width):
        lanes = slice(low, high)
        pre = dot_nn(source, block[:, lanes]) + bias[0, :, lanes]
        square = pre * pre
        bent = jnp.tanh(root * pre * (1.0 + 0.044715 * square))
        half = 0.5 + 0.5 * bent
        hidden[0, :, lanes] = narrow(pre * half)
        steep = (0.5 * root) * pre * (1.0 + 3 * 0.044715 * square)
        slope[0, :, lanes] = narrow(half + steep * (1.0 - bent * bent))

    @pl.when(step == steps - 1)
    def _():
        for at in range(len(cuts)):
            rows = pl.ds(pl.multiple_of(order[at] * width, width), width)
            pltpu.make_async_copy(
                whole.at[rows], whole_out.at[rows], store_semaphores.at[at]
            ).wait()


def run_hidden(mlp_in, gathered, bias):
    pieces, cuts, starts, order = gathered
    total, width = mlp_in.shape
    count = len(cuts)
    per_block = pl.BlockSpec((1, total, width), lambda at, order, starts: (order[at], 0, 0))
    out = jax.ShapeDtypeStruct((count, total, width), jnp.bfloat16)
    return pl.pallas_call(
        functools.partial(hidden_kernel, cuts),
        grid_spec=pltpu.PrefetchScalarGridSpec(
            num_scalar_prefetch=2,
            grid=(count,),
            in_specs=[
                pl.BlockSpec((total, width), lambda at, order, starts: (0, 0)),
                pl.BlockSpec((1, 1, width), lambda at, order, starts: (order[at], 0, 0)),
            ]
            + [pl.BlockSpec(memory_space=pl.ANY)] * len(pieces),
            out_specs=[pl.BlockSpec(memory_space=pl.ANY), per_block, per_block],
            scratch_shapes=[
                pltpu.VMEM((count * width, width), jnp.bfloat16),
                pltpu.SemaphoreType.DMA((len(starts),)),
                pltpu.SemaphoreType.DMA((count,)),
            ],
        ),
        out_shape=[jax.ShapeDtypeStruct((count * width, width), jnp.bfloat16), out, out],
        compiler_params=pltpu.CompilerParams(vmem_limit_bytes=vmem_bytes),
        cost_estimate=pl.CostEstimate(
            flops=8 * total * width * width, bytes_accessed=50 * total * width, transcendentals=0
        ),
    )(stacked(order), stacked(starts), mlp_in, bias, *pieces)


def branch_kernel(
    frames,
    counts,
    hidden,
    slope,
    block,
    d_branch,
    bias,
    gates,
    resid,
    cotangent,
    d_pre,
    d_pre_sum,
    block_out,
    d_gate,
    branch,
):
    step, steps = pl.program_id(0), pl.num_programs(0)
    total, width = resid.shape
    clips = gates.shape[0]
    rows = total // clips
    source, back = hidden[0], d_branch[...]

    @pl.when(step == 0)
    def _():
        branch[...] = jnp.zeros_like(branch)

    for low, high in column_cuts(width):
        span = slice(low, high)
        d_hidden = dot_nt(back, block[0, span, :])
        low_back = narrow(d_hidden * wide(slope[0, :, span]))
        d_pre[0, :, span] = low_back
        d_pre_sum[0, :, span] = column_sum(wide(low_back))
        branch[:, span] += dot_nn(source, block[0, :, span])

    @pl.when(step == steps - 1)
    def _():
        for clip in range(clips):
            span = slice(clip * rows, (clip + 1) * rows)
            kept = valid_rows(counts[clip], rows, frames) * (branch[span] + bias[...])
            block_out[span] = narrow(resid[span] + gates[clip] * kept)
            d_gate[clip] = column_sum(wide(cotangent[span]) * kept)


def run_branch(frames, counts, hidden, slope, blocks, d_branch, bias, gates, resid, cotangent):
    count, total, width = hidden.shape
    clips = gates.shape[0]
    per_block = spec((1, total, width), lambda at: (at, 0, 0))
    low = jax.ShapeDtypeStruct((total, width), jnp.bfloat16)
    return pl.pallas_call(
        functools.partial(branch_kernel, frames),
        grid=(count,),
        in_specs=[
            pl.BlockSpec(memory_space=pltpu.SMEM),
            per_block,
            per_block,
            spec((1, width, width), lambda at: (at, 0, 0)),
            held((total, width)),
            held(bias.shape),
            held(gates.shape),
            held((total, width)),
            held((total, width)),
        ],
        out_specs=[
            per_block,
            spec((1, 1, width), lambda at: (at, 0, 0)),
            held((total, width)),
            held((clips, 1, width)),
        ],
        out_shape=[
            jax.ShapeDtypeStruct((count, total, width), jnp.bfloat16),
            jax.ShapeDtypeStruct((count, 1, width), jnp.float32),
            low,
            jax.ShapeDtypeStruct((clips, 1, width), jnp.float32),
        ],
        scratch_shapes=[pltpu.VMEM((total, width), jnp.float32)],
        compiler_params=pltpu.CompilerParams(vmem_limit_bytes=vmem_bytes),
        cost_estimate=pl.CostEstimate(
            flops=16 * total * width * width, bytes_accessed=40 * total * width, transcendentals=0
        ),
    )(counts, hidden, slope, blocks, d_branch, bias, gates, resid, cotangent)


def resid_kernel(
    frames,
    counts,
    d_pre,
    block,
    mods,
    resid,
    cotangent,
    proj,
    d_resid_out,
    d_proj,
    sums,
    total_grad,
):
    step, steps = pl.program_id(0), pl.num_programs(0)
    total, width = resid.shape
    clips = mods.shape[0]
    rows = total // clips
    tile = min(rows, 128)
    source = d_pre[0]

    @pl.when(step == 0)
    def _():
        total_grad[...] = jnp.zeros_like(total_grad)

    for low, high in column_cuts(width):
        span = slice(low, high)
        total_grad[:, span] += dot_nt(source, block[0, span, :])

    @pl.when(step == steps - 1)
    def _():
        for clip in range(clips):
            gate_one, scale_two = mods[clip, 2:3, :], mods[clip, 4:5, :]
            found = [0.0] * 4
            for first in range(clip * rows, (clip + 1) * rows, tile):
                span = slice(first, first + tile)
                grad = total_grad[span]
                normed, inverse = norm_parts(resid[span])
                back = norm_back(grad * (1.0 + scale_two), normed, inverse)
                d_resid = wide(cotangent[span]) + back
                d_resid_out[span] = d_resid
                kept = valid_rows(counts[clip], tile, frames) * d_resid
                low_back = narrow(kept * gate_one)
                d_proj[span] = low_back
                terms = (grad, grad * normed, kept * proj[span], wide(low_back))
                found = [old + column_sum(term) for old, term in zip(found, terms)]
            for at in range(4):
                sums[clip, at : at + 1, :] = found[at]


def run_resid(frames, counts, d_pre, blocks, mods, resid, cotangent, proj):
    count, total, width = d_pre.shape
    clips = mods.shape[0]
    return pl.pallas_call(
        functools.partial(resid_kernel, frames),
        grid=(count,),
        in_specs=[
            pl.BlockSpec(memory_space=pltpu.SMEM),
            spec((1, total, width), lambda at: (at, 0, 0)),
            spec((1, width, width), lambda at: (at, 0, 0)),
            held(mods.shape),
            held((total, width)),
            held((total, width)),
            held((total, width)),
        ],
        out_specs=[held((total, width)), held((total, width)), held((clips, 4, width))],
        out_shape=[
            jax.ShapeDtypeStruct((total, width), jnp.float32),
            jax.ShapeDtypeStruct((total, width), jnp.bfloat16),
            jax.ShapeDtypeStruct((clips, 4, width), jnp.float32),
        ],
        scratch_shapes=[pltpu.VMEM((total, width), jnp.float32)],
        compiler_params=pltpu.CompilerParams(vmem_limit_bytes=vmem_bytes),
        cost_estimate=pl.CostEstimate(
            flops=8 * total * width * width, bytes_accessed=40 * total * width, transcendentals=0
        ),
    )(counts, d_pre, blocks, mods, resid, cotangent, proj)


def attention_back_kernel(
    frames, counts, d_proj, parts, block, d_qkv, sums, d_mixed, d_query, d_key, d_value
):
    rows, width = d_proj.shape
    tile = min(rows, 128)
    count = counts[pl.program_id(0)]
    source = d_proj[...]
    for low, high in column_cuts(width):
        d_mixed[:, low:high] = narrow(dot_nt(source, block[0, low:high, :]))
    scale = (width // HEADS) ** -0.5
    offset = score_offset(count, tile, frames, 0)
    for ref in (d_query, d_key, d_value):
        ref[...] = jnp.zeros_like(ref)
    for first in range(0, rows, tile):
        span = slice(first, first + tile)
        for low, high, start, stop in head_windows(width):
            lanes = slice(start, stop)
            mask = lane_mask(low, high, stop - start, jnp.bfloat16)
            query_high = parts[0, span, lanes] * mask
            key_high = parts[2, span, lanes] * mask
            back = d_mixed[span, lanes] * mask
            scores = dot_nt(key_high, query_high)
            scores += dot_nt(key_high, parts[1, span, lanes])
            scores += dot_nt(parts[3, span, lanes], query_high) + offset
            expons = jnp.exp(scores - jnp.max(scores, axis=0, keepdims=True))
            probs = expons * (1.0 / jnp.sum(expons, axis=0, keepdims=True))
            d_probs = dot_nt(parts[4, span, lanes], back)
            inner = jnp.sum(d_probs * probs, axis=0, keepdims=True)
            d_scores = narrow(probs * (d_probs - inner))
            d_value[span, lanes] += dot_nn(narrow(probs), back)
            d_key[span, lanes] += dot_nn(d_scores, query_high)
            d_query[span, lanes] += dot_tn(d_scores, key_high)
    for at, ref in enumerate((d_query, d_key, d_value)):
        low_back = narrow(ref[...] * scale) if at == 0 else narrow(ref[...])
        d_qkv[at] = low_back
        sums[0, at : at + 1, :] = column_sum(wide(low_back))
    d_qkv[3] = source


def run_attention_back(frames, counts, d_proj, parts, block):
    total, width = d_proj.shape
    clips = counts.shape[0]
    rows = total // clips
    return pl.pallas_call(
        functools.partial(attention_back_kernel, frames),
        grid=(clips,),
        in_specs=[
            pl.BlockSpec(memory_space=pltpu.SMEM),
            spec((rows, width), lambda clip: (clip, 0)),
            spec((5, rows, width), lambda clip: (0, clip, 0)),
            spec((1, width, width), lambda clip: (3, 0, 0), pipeline_mode=pl.Buffered(1)),
        ],
        out_specs=[
            spec((4, rows, width), lambda clip: (0, clip, 0)),
            spec((1, 3, width), lambda clip: (clip, 0, 0)),
        ],
        out_shape=[
            jax.ShapeDtypeStruct((4, total, width), jnp.bfloat16),
            jax.ShapeDtypeStruct((clips, 3, width), jnp.float32),
        ],
        scratch_shapes=[pltpu.VMEM((rows, width), jnp.bfloat16)]
        + [pltpu.VMEM((rows, width), jnp.float32)] * 3,
        compiler_params=pltpu.CompilerParams(vmem_limit_bytes=vmem_bytes),
        cost_estimate=pl.CostEstimate(
            flops=12 * total * width * width, bytes_accessed=20 * total * width, transcendentals=0
        ),
    )(counts, d_proj, parts, block)


def input_kernel(d_qkv, block, mods, tokens, d_resid, input_grad, sums, total_grad):
    step, steps = pl.program_id(0), pl.num_programs(0)
    total, width = tokens.shape
    clips = mods.shape[0]
    rows = total // clips
    tile = min(rows, 128)
    source = d_qkv[0]

    @pl.when(step == 0)
    def _():
        total_grad[...] = jnp.zeros_like(total_grad)

    for low, high in column_cuts(width):
        span = slice(low, high)
        total_grad[:, span] += dot_nt(source, block[0, span, :])

    @pl.when(step == steps - 1)
    def _():
        for clip in range(clips):
            scale_one = mods[clip, 1:2, :]
            found = [0.0] * 2
            for first in range(clip * rows, (clip + 1) * rows, tile):
                span = slice(first, first + tile)
                grad = total_grad[span]
                normed, inverse = norm_parts(wide(tokens[span]))
                back = norm_back(grad * (1.0 + scale_one), normed, inverse)
                input_grad[span] = narrow(d_resid[span] + back)
                terms = (grad, grad * normed)
                found = [old + column_sum(term) for old, term in zip(found, terms)]
            for at in range(2):
                sums[clip, at : at + 1, :] = found[at]


def run_input(d_qkv, blocks, mods, tokens, d_resid):
    total, width = tokens.shape
    clips = mods.shape[0]
    return pl.pallas_call(
        input_kernel,
        grid=(3,),
        in_specs=[
            spec((1, total, width), lambda at: (at, 0, 0)),
            spec((1, width, width), lambda at: (at, 0, 0)),
            held(mods.shape),
            held((total, width)),
            held((total, width)),
        ],
        out_specs=[held((total, width)), held((clips, 2, width))],
        out_shape=[
            jax.ShapeDtypeStruct((total, width), jnp.bfloat16),
            jax.ShapeDtypeStruct((clips, 2, width), jnp.float32),
        ],
        scratch_shapes=[pltpu.VMEM((total, width), jnp.float32)],
        compiler_params=pltpu.CompilerParams(vmem_limit_bytes=vmem_bytes),
        cost_estimate=pl.CostEstimate(
            flops=6 * total * width * width, bytes_accessed=30 * total * width, transcendentals=0
        ),
    )(d_qkv, blocks, mods, tokens, d_resid)


def tie(*values):
    return lax.optimization_barrier(values)


def packed(arrays, tile):
    flat = jnp.concatenate([array.reshape(-1) for array in arrays])
    return jnp.pad(flat, (0, -flat.shape[0] % (tile * 128))).reshape(-1, 128)


def core_swap(array):
    count = lax.axis_size("dp")
    return lax.ppermute(array, "dp", [(at, at ^ 1) for at in range(count)])


def chip_shift(array, step):
    count = lax.axis_size("dp")
    return lax.ppermute(array, "dp", [(at, (at + 2 * step) % count) for at in range(count)])


def rank_swap(array, bits):
    count = lax.axis_size("fsdp")
    return lax.ppermute(array, "fsdp", [(at, at ^ bits) for at in range(count)])


def entry(array, at, axis=0):
    return lax.dynamic_index_in_dim(array, at, axis, keepdims=False)


def place_kernel(cuts, at, *refs):
    parts, whole, held_rows, semaphores = refs[:-3], refs[-3], refs[-2], refs[-1]
    spans, loads, stores = [], [], []
    for index, (part, first, rows) in enumerate(cuts):
        spans.append(pl.ds(pl.multiple_of(at[index] * 16, 16), rows))
        source = parts[part].at[pl.ds(first, rows)]
        loads.append(
            pltpu.make_async_copy(source, held_rows.at[spans[index]], semaphores.at[0, index])
        )
        loads[index].start()
    for index, span in enumerate(spans):
        loads[index].wait()
        stores.append(
            pltpu.make_async_copy(held_rows.at[span], whole.at[span], semaphores.at[1, index])
        )
        stores[index].start()
    for store in stores:
        store.wait()


def place(parts, cuts, starts, rows):
    width = parts[0].shape[-1]
    dtype = parts[0].dtype
    return pl.pallas_call(
        functools.partial(place_kernel, cuts),
        in_specs=[pl.BlockSpec(memory_space=pltpu.SMEM)]
        + [pl.BlockSpec(memory_space=pl.ANY)] * len(parts),
        out_specs=pl.BlockSpec(memory_space=pl.ANY),
        out_shape=jax.ShapeDtypeStruct((rows, width), dtype),
        scratch_shapes=[
            pltpu.VMEM((rows, width), dtype),
            pltpu.SemaphoreType.DMA((2, len(cuts))),
        ],
        compiler_params=pltpu.CompilerParams(vmem_limit_bytes=vmem_bytes),
        cost_estimate=pl.CostEstimate(
            flops=0, bytes_accessed=4 * rows * width, transcendentals=0
        ),
    )(stacked(starts), *parts)


def own_rows(parts, group):
    ranks, at = lax.axis_size("fsdp"), lax.axis_index("fsdp")
    shares = ranks // group
    count, _, row_part, col_part = parts.shape
    chunk = row_part // shares
    split = parts.reshape(count, group, shares, chunk, col_part).transpose(1, 2, 0, 3, 4)
    split = split.reshape(ranks, count, chunk, col_part)
    if shares > 1:
        moved = lax.all_to_all(split, "fsdp", 0, 0, tiled=True)
        (moved,) = yield (moved,)
        yield moved.transpose(1, 2, 0, 3).reshape(count, chunk, ranks * col_part)
        return
    panels = [entry(split, at)]
    panels += [rank_swap(entry(split, at ^ bits), bits) for bits in range(1, ranks)]
    panels = yield tuple(panels)
    placed = [
        lax.select_n(at, *[panels[panel ^ index] for index in range(ranks)])
        for panel in range(ranks)
    ]
    yield jnp.concatenate(placed, axis=2)


def shard_rows(split, group):
    ranks, count, chunk, col_part = split.shape
    shares = ranks // group
    moved = lax.all_to_all(split, "fsdp", 0, 0, tiled=True)
    moved = moved.reshape(group, shares, count, chunk, col_part).transpose(2, 0, 1, 3, 4)
    return moved.reshape(count, group, shares * chunk, col_part)


def gather_blocks(rows, group):
    ranks, dp_count = lax.axis_size("fsdp"), lax.axis_size("dp")
    shares = ranks // group
    chunk, total = rows.shape
    all_rows = lax.all_gather(rows, ("fsdp", "dp"), axis=0, tiled=True)
    if shares > 1:
        all_rows = all_rows.reshape(group, shares, dp_count, chunk, total).transpose(0, 2, 1, 3, 4)
    return all_rows.reshape(group, total, total)


def join_line(rows):
    chips, chip = lax.axis_size("dp") // 2, lax.axis_index("dp") // 2
    chunk = rows.shape[0]
    found = [rows] + [chip_shift(rows, step) for step in range(1, chips)]
    starts = [(chip - step) % chips * (chunk // 16) for step in range(chips)]
    return place(found, [(step, 0, chunk) for step in range(chips)], starts, chips * chunk)


def gather_first(rows, group):
    ranks, at = lax.axis_size("fsdp"), lax.axis_index("fsdp")
    total = rows.shape[-1]
    if ranks != group:
        blocks = gather_blocks(rows, group).reshape(group * total, total)
        for _ in range(3):
            (blocks,) = yield (blocks,)
        yield [blocks], [(0, 0, group * total)], [0]
        return
    chips = lax.axis_size("dp") // 2
    core = lax.axis_index("dp") % 2
    chunk = rows.shape[0]
    (line,) = yield (join_line(rows),)
    low_in, high_in = yield (rank_swap(line, 1), rank_swap(line, 2))
    half = total // 4
    parts = [line, low_in, high_in]
    parts += [rank_swap(high_in[:half], 1), rank_swap(low_in[half:], 2)]
    others = [core_swap(part) for part in parts[:3]]
    parts[3:] = yield tuple(parts[3:])
    others += [core_swap(part) for part in parts[3:]]
    cuts, starts = [], []
    for side, found in ((core, parts), (1 - core, others)):
        for index, part in enumerate(found):
            bits, first_chip = ((0, 0), (1, 0), (2, 0), (3, 0), (3, chips // 2))[index]
            for step in range(part.shape[0] // chunk):
                cuts.append((len(parts) * (found is others) + index, step * chunk, chunk))
                row = (at ^ bits) * (2 * chips) + 2 * (first_chip + step) + side
                starts.append(row * (chunk // 16))
    yield parts + others, cuts, starts


def gather_second(rows, group):
    ranks, at = lax.axis_size("fsdp"), lax.axis_index("fsdp")
    total = rows.shape[-1]
    if ranks != group:
        blocks = gather_blocks(rows, group).reshape(group * total, total)
        for _ in range(2):
            (blocks,) = yield (blocks,)
        cuts = [[(0, index * total, total)] for index in range(group)]
        yield [blocks], cuts, [index * (total // 16) for index in range(group)], range(group)
        return
    chips = lax.axis_size("dp") // 2
    core = lax.axis_index("dp") % 2
    chunk, half = rows.shape[0], total // 2
    line = join_line(rows)
    cuts = [(side, step * chunk, chunk) for side in range(2) for step in range(chips)]
    starts = [
        (2 * step + side) * (chunk // 16) for side in (core, 1 - core) for step in range(chips)
    ]
    (own,) = yield (place([line, core_swap(line)], cuts, starts, total),)
    share = lax.dynamic_slice_in_dim(own, core * half, half, 0)
    mine = yield tuple(rank_swap(share, bits) for bits in range(1, ranks))
    parts, cuts, starts = [own], [[(0, 0, total)]], [at * (total // 16)]
    for bits in range(1, ranks):
        parts += [mine[bits - 1], core_swap(mine[bits - 1])]
        cuts.append([(2 * bits - 1, 0, half), (2 * bits, 0, half)])
        starts += [((at ^ bits) * 2 + side) * (half // 16) for side in (core, 1 - core)]
    yield parts, cuts, starts, [at ^ bits for bits in range(ranks)]


def gather_own(rows, group):
    ranks = lax.axis_size("fsdp")
    shares = ranks // group
    if shares > 1:
        sets = [[share + shares * block for share in range(shares)] for block in range(group)]
        rows = lax.all_gather(rows, "fsdp", axis=1, tiled=True, axis_index_groups=sets)
    return lax.all_gather(rows, "dp", axis=1, tiled=True)


def sum_blocks(product, cut, total, group):
    ranks, dp_count = lax.axis_size("fsdp"), lax.axis_size("dp")
    shares = ranks // group
    if shares > 1:
        blocks = narrow(product(cut(0, total)))
        chunk = total // (dp_count * shares)
        blocks = blocks.reshape(group, dp_count, shares, chunk, -1).transpose(0, 2, 1, 3, 4)
        rows = lax.psum_scatter(
            blocks.reshape(group * total, -1), ("fsdp", "dp"), scatter_dimension=0, tiled=True
        )
        for _ in range(6):
            (rows,) = yield (rows,)
        yield gather_own(rows[None], group)[0]
        return
    chips, half = dp_count // 2, total // 2
    chunk = half // chips
    core, chip = lax.axis_index("dp") % 2, lax.axis_index("dp") // 2
    low_bit, high_bit = lax.axis_index("fsdp") % 2, lax.axis_index("fsdp") // 2
    (away,) = yield (narrow(product(cut((1 - core) * half, half))),)
    (away_in,) = yield (core_swap(away),)
    here = product(cut(core * half, half))
    here = narrow(here + wide(away_in))
    here = here.reshape(2, 2, chips, chunk, -1)
    middle = chips // 2
    first, second = here[:, :, :middle], here[:, :, middle:]
    first_out, second_out = yield (entry(first, 1 - low_bit, 1), entry(second, 1 - high_bit, 0))
    first_in, second_in = yield (rank_swap(first_out, 1), rank_swap(second_out, 2))
    first = narrow(wide(entry(first, low_bit, 1)) + wide(first_in))
    second = narrow(wide(entry(second, high_bit, 0)) + wide(second_in))
    first_in = rank_swap(entry(first, 1 - high_bit), 2)
    second_in = rank_swap(entry(second, 1 - low_bit), 1)
    first_in, second_in = yield (first_in, second_in)
    first = narrow(wide(entry(first, high_bit)) + wide(first_in))
    second = narrow(wide(entry(second, low_bit)) + wide(second_in))
    line = jnp.concatenate([first, second])
    parts = [chip_shift(entry(line, (chip + step) % chips), step) for step in range(1, chips)]
    parts = yield tuple(parts)
    rows = sum([wide(part) for part in parts], wide(entry(line, chip)))
    yield lax.all_gather(narrow(rows), "dp", axis=0, tiled=True)


def fast_dot(subscripts, left, right):
    return jnp.einsum(subscripts, left, right, preferred_element_type=jnp.float32)


def products_kernel(chips, at, gathered, left_root, right_root, out, whole, semaphores):
    chunk, width = left_root.shape
    ranks = out.shape[0]
    copies = []
    for index in range(2 * chips):
        first = (index % 2 * chips + index // 2) * chunk
        copies.append(
            pltpu.make_async_copy(
                gathered.at[pl.ds(index * chunk, chunk)],
                whole.at[pl.ds(first, chunk)],
                semaphores.at[index],
            )
        )
        copies[-1].start()
    for copy in copies:
        copy.wait()
    first = at[0] * 16
    grad = whole[...]
    picked = lax.broadcasted_iota(jnp.int32, (width, chunk), 0) - first
    picked = picked == lax.broadcasted_iota(jnp.int32, (width, chunk), 1)
    own_columns = narrow(dot_nn(grad, narrow(picked.astype(jnp.float32))))
    side_high, side_low = split_high(dot_nn(left_root[...], grad))
    right = right_root[...]
    precond = dot_nn(side_high, right) + dot_nn(side_low, right)
    outer = dot_nt(whole[pl.ds(pl.multiple_of(first, 16), chunk), :], grad)
    inner = dot_tn(own_columns, grad)
    for at_out, product in enumerate((precond, outer, inner)):
        low = narrow(product)
        for rank in range(ranks):
            span = slice(rank * (width // ranks), (rank + 1) * (width // ranks))
            out[rank, at_out] = low[:, span]


def owned_step(whole, left_root, right_root, group):
    ranks, dp_count = lax.axis_size("fsdp"), lax.axis_size("dp")
    shares = ranks // group
    chunk, total = left_root.shape
    col_part = total // ranks
    first = lax.axis_index("dp") * (chunk * shares) + lax.axis_index("fsdp") % shares * chunk
    if shares == 1:
        return pl.pallas_call(
            functools.partial(products_kernel, dp_count // 2),
            in_specs=[
                pl.BlockSpec(memory_space=pltpu.SMEM),
                pl.BlockSpec(memory_space=pl.ANY),
                pl.BlockSpec(memory_space=pltpu.VMEM),
                pl.BlockSpec(memory_space=pltpu.VMEM),
            ],
            out_specs=pl.BlockSpec(memory_space=pltpu.VMEM),
            out_shape=jax.ShapeDtypeStruct((ranks, 3, chunk, col_part), jnp.bfloat16),
            scratch_shapes=[
                pltpu.VMEM((total, total), jnp.bfloat16),
                pltpu.SemaphoreType.DMA((dp_count,)),
            ],
            compiler_params=pltpu.CompilerParams(vmem_limit_bytes=vmem_bytes),
            cost_estimate=pl.CostEstimate(
                flops=12 * chunk * total * total, bytes_accessed=6 * total * total, transcendentals=0
            ),
        )((first // 16)[None], whole, left_root, right_root)
    grad_rows = lax.dynamic_slice_in_dim(whole, first, chunk, 0)
    own_columns = lax.dynamic_slice_in_dim(whole, first, chunk, 1)
    outer = fast_dot("rk,jk->rj", grad_rows, whole)
    inner = fast_dot("kr,kj->rj", own_columns, whole)
    side_high, side_low = split_high(fast_dot("rk,kj->rj", left_root, whole))
    precond = fast_dot("rk,kj->rj", side_high, right_root) + fast_dot(
        "rk,kj->rj", side_low, right_root
    )
    products = narrow(jnp.stack([precond, outer, inner]))
    return products.reshape(3, chunk, ranks, col_part).transpose(2, 0, 1, 3)


def per_device(
    tokens,
    conditioning,
    frame_counts,
    cotangent,
    weights,
    biases,
    momentum,
    left_stats,
    right_stats,
    left_roots,
    right_roots,
    bias_moment,
    bias_second,
):
    group = 4
    mod_count = 6
    clip_count, pos_count, frames, width = tokens.shape
    token_count = clip_count * pos_count * frames
    block_count, row_part, col_part = weights.shape
    dp_count, ranks = lax.axis_size("dp"), lax.axis_size("fsdp")
    dp_at, rank_at = lax.axis_index("dp"), lax.axis_index("fsdp")
    all_clips = clip_count * dp_count
    bias_part = biases.shape[0]
    stream = tokens.reshape(token_count, width)
    grad_out = cotangent.reshape(token_count, width)
    low_weights = narrow(weights).reshape(block_count, row_part, col_part)
    shards = low_weights[mod_count:].reshape(-1, group, row_part, col_part)

    attn_rows, cond_low = own_rows(shards[:1], group), narrow(jax.nn.silu(conditioning))
    attn_panels = next(attn_rows)
    first_parts = lax.all_gather(packed([cond_low, narrow(biases)], 16), "dp", axis=0, tiled=True)
    attn_panels, first_parts, other_shards = tie(attn_panels, first_parts, shards[1:])
    attn_rows = attn_rows.send(attn_panels)[0]
    other_rows = own_rows(other_shards, group)
    other_panels = next(other_rows)
    attn_steps = gather_first(attn_rows, group)
    attn_parts = next(attn_steps)
    one_rows, two_rows = other_rows.send(other_panels)

    first_parts = first_parts.reshape(dp_count, -1)
    cond_all = first_parts[:, : clip_count * width].reshape(all_clips, width)
    bias_rows = wide(first_parts[:, clip_count * width : clip_count * width + bias_part])
    cond_rows = lax.dynamic_slice_in_dim(cond_all, dp_at * row_part, row_part, 1)
    cond_cols = wide(lax.dynamic_slice_in_dim(cond_all, rank_at * col_part, col_part, 1))
    mod_parts = fast_dot("cr,jre->cje", cond_rows, low_weights[:mod_count])
    mod_parts, attn_parts = tie(mod_parts, attn_parts)
    attn_parts = attn_steps.send(attn_parts)
    mod_parts = lax.all_to_all(mod_parts, "dp", 0, 0, tiled=True)
    mod_parts, one_rows = tie(mod_parts, one_rows)
    one_steps = gather_second(one_rows, group)
    one_parts = next(one_steps)
    mod_cols = jnp.sum(mod_parts.reshape(dp_count, clip_count, mod_count, col_part), axis=0)
    left_cond = jnp.einsum("jrk,ck->jrc", left_roots[:mod_count], cond_cols, precision=precise)
    mod_size, bias_size = mod_cols.size, dp_count * bias_part
    second_parts, attn_parts = tie(packed([mod_cols, bias_rows, left_cond], 8), attn_parts)
    attn_parts = attn_steps.send(attn_parts)
    second_parts = lax.all_gather(second_parts, "fsdp", axis=0, tiled=True)
    second_parts, one_parts, attn_parts = tie(second_parts, one_parts, attn_parts)
    one_parts = one_steps.send(one_parts)
    gathered = attn_steps.send(attn_parts)
    attn_parts, two_rows = tie(attn_parts, two_rows)
    two_w = gather_blocks(two_rows, group)
    second_parts = second_parts.reshape(ranks, -1)
    mods = second_parts[:, :mod_size].reshape(ranks, clip_count, mod_count, col_part)
    mods = mods.transpose(1, 2, 0, 3).reshape(clip_count, mod_count, width)
    bias_all = second_parts[:, mod_size : mod_size + bias_size].reshape(ranks, dp_count, bias_part)
    bias_all = bias_all.transpose(1, 0, 2).reshape(-1, width)
    left_size = mod_size + bias_size + left_cond.size
    left_cond = jnp.sum(second_parts[:, mod_size + bias_size : left_size], axis=0)
    left_cond = left_cond.reshape(mod_count, row_part, all_clips)
    mods = mods + bias_all[:mod_count]
    bias_table = jnp.concatenate(
        [bias_all[6:7], jnp.zeros((1, width), jnp.float32), bias_all[7:14]]
    )

    attn_w, attn_in, parts, mixed, proj, resid, mlp_in, d_branch, d_branch_sums = run_attention(
        frames, frame_counts, stream, grad_out, mods, bias_table, gathered
    )
    attn_w = attn_w.reshape(group, width, width)
    roots = jnp.stack([narrow(left_roots[mod_count:]), narrow(right_roots[mod_count:])])
    mlp_in, one_parts, roots = tie(mlp_in, one_parts, roots)
    root_rows = own_rows(roots.reshape(-1, group, row_part, col_part), group)
    root_panels = next(root_rows)
    one_w, hidden, slope = run_hidden(mlp_in, one_steps.send(one_parts), bias_table[4:8, None])
    one_w = one_w.reshape(group, width, width)

    two_steps = sum_blocks(
        lambda left: fast_dot("jtd,te->jde", left, d_branch),
        lambda first, size: lax.dynamic_slice_in_dim(hidden, first, size, 2),
        width,
        group,
    )
    two_parts = next(two_steps)
    hidden, two_parts = tie(hidden, two_parts)
    two_parts = two_steps.send(two_parts)
    d_pre, d_pre_sums, block_out, d_gate_two = run_branch(
        frames,
        frame_counts,
        hidden,
        slope,
        two_w,
        d_branch,
        bias_table[8:9],
        mods[:, 5:6],
        resid,
        grad_out,
    )
    d_pre, two_parts, root_panels = tie(d_pre, two_parts, root_panels)
    two_parts = two_steps.send(two_parts)
    d_pre, two_parts = tie(d_pre, two_parts)
    two_parts = two_steps.send(two_parts)
    left_rows, right_rows = jnp.split(root_rows.send(root_panels), 2)
    right_wholes = [gather_own(rows[None], group)[0] for rows in right_rows]
    one_steps = sum_blocks(
        lambda left: fast_dot("td,jte->jde", left, d_pre),
        lambda first, size: lax.dynamic_slice_in_dim(mlp_in, first, size, 1),
        width,
        group,
    )
    one_parts = next(one_steps)
    d_pre, one_parts = tie(d_pre, one_parts)
    one_parts = one_steps.send(one_parts)
    d_resid, d_proj, resid_sums = run_resid(
        frames, frame_counts, d_pre, one_w, mods, resid, grad_out, proj
    )
    d_proj, one_parts, two_parts = tie(d_proj, one_parts, two_parts)
    two_parts = two_steps.send(two_parts)
    one_parts = one_steps.send(one_parts)
    d_proj, one_parts = tie(d_proj, one_parts)
    one_parts = one_steps.send(one_parts)
    d_heads, head_sums = run_attention_back(frames, frame_counts, d_proj, parts, attn_w)
    d_heads, two_parts = tie(d_heads, two_parts)
    two_parts = two_steps.send(two_parts)
    attn_steps = sum_blocks(
        lambda left: fast_dot("jtd,jte->jde", left, d_heads),
        lambda first, size: jnp.stack(
            [lax.dynamic_slice_in_dim(left, first, size, 1) for left in (attn_in,) * 3 + (mixed,)]
        ),
        width,
        group,
    )
    attn_parts = next(attn_steps)
    d_heads, attn_parts = tie(d_heads, attn_parts)
    attn_parts = attn_steps.send(attn_parts)
    d_heads, attn_parts, one_parts = tie(d_heads, attn_parts, one_parts)
    one_parts = one_steps.send(one_parts)
    attn_parts = attn_steps.send(attn_parts)
    d_heads, attn_parts = tie(d_heads, attn_parts)
    attn_parts = attn_steps.send(attn_parts)
    input_grad, input_sums = run_input(d_heads, attn_w, mods, stream, d_resid)
    input_sums, one_parts, two_parts = tie(input_sums, one_parts, two_parts)
    whole_two = two_steps.send(two_parts)
    one_parts = one_steps.send(one_parts)
    input_sums, attn_parts = tie(input_sums, attn_parts)
    attn_parts = attn_steps.send(attn_parts)

    d_mods = jnp.stack(
        [
            input_sums[:, 0],
            input_sums[:, 1],
            resid_sums[:, 2],
            resid_sums[:, 0],
            resid_sums[:, 1],
            d_gate_two[:, 0],
        ],
        axis=1,
    )
    head_sums = jnp.sum(head_sums, axis=0)
    grad_bias = jnp.concatenate(
        [
            jnp.sum(d_mods, axis=0),
            head_sums[0:1],
            head_sums[2:3],
            jnp.sum(resid_sums[:, 3], axis=0)[None],
            d_pre_sums[:, 0],
            jnp.sum(d_branch_sums, axis=0),
        ]
    )
    to_ranks = jnp.concatenate(
        [
            d_mods.reshape(clip_count, mod_count, ranks, col_part)
            .transpose(2, 0, 1, 3)
            .reshape(ranks, mod_size),
            grad_bias.reshape(dp_count, ranks, bias_part)
            .transpose(1, 0, 2)
            .reshape(ranks, bias_size),
        ],
        axis=1,
    )
    rank_sums = jnp.sum(lax.all_to_all(to_ranks, "fsdp", 0, 0, tiled=True), axis=0)
    rank_sums, attn_parts = tie(rank_sums, attn_parts)
    attn_parts = attn_steps.send(attn_parts)
    to_rows = jnp.concatenate(
        [
            jnp.broadcast_to(rank_sums[None, :mod_size], (dp_count, mod_size)),
            rank_sums[mod_size:].reshape(dp_count, bias_part),
        ],
        axis=1,
    )
    from_rows = lax.all_to_all(to_rows, "dp", 0, 0, tiled=True)
    from_rows, one_parts = tie(from_rows, one_parts)
    whole_one = one_steps.send(one_parts)
    bias_grad = jnp.sum(from_rows[:, mod_size:], axis=0)
    mod_grad_cols = from_rows[:, :mod_size].reshape(all_clips, mod_count, col_part)
    mod_grad = lax.all_gather(packed([mod_grad_cols], 8), "fsdp", axis=0, tiled=True)
    mod_grad = mod_grad.reshape(ranks, -1)[:, : mod_grad_cols.size]
    mod_grad = mod_grad.reshape(ranks, all_clips, mod_count, col_part).transpose(1, 2, 0, 3)
    mod_grad = mod_grad.reshape(all_clips, mod_count, width)

    mod_grad_rows = lax.dynamic_slice_in_dim(mod_grad, dp_at * row_part, row_part, 2)
    right_parts = jnp.einsum(
        "cjk,jke->cje", mod_grad_rows, right_roots[:mod_count], precision=precise
    )
    cond_wide = wide(cond_all)
    cond_row_wide = wide(cond_rows)
    mod_gram = jnp.einsum("cjk,bjk->jcb", mod_grad, mod_grad, precision=precise)
    cond_gram = jnp.einsum("ck,bk->cb", cond_wide, cond_wide, precision=precise)
    mod_side = jnp.einsum("jcb,be->jce", mod_gram, cond_cols, precision=precise)
    ada_left = jnp.einsum("cr,jce->jre", cond_row_wide, mod_side, precision=precise)
    cond_side = jnp.einsum("cb,bje->jce", cond_gram, mod_grad_cols, precision=precise)
    ada_right = jnp.einsum("cjr,jce->jre", mod_grad_rows, cond_side, precision=precise)

    products_two = owned_step(whole_two, left_rows[2], right_wholes[2], group)
    products_two, right_parts, attn_parts = tie(products_two, right_parts, attn_parts)
    whole_attn = attn_steps.send(attn_parts)
    back_two = shard_rows(products_two, group)
    products_one = owned_step(whole_one, left_rows[1], right_wholes[1], group)
    back_one = shard_rows(products_one, group)
    right_parts = lax.all_gather(packed([right_parts], 8), "dp", axis=0, tiled=True)
    mod_right = jnp.sum(right_parts.reshape(dp_count, -1), axis=0)[: mod_grad_cols.size]
    mod_right = mod_right.reshape(all_clips, mod_count, col_part)
    ada_pre = jnp.einsum("jrc,cje->jre", left_cond, mod_right, precision=precise)
    whole_attn, back_one, back_two, ada_pre, ada_left, ada_right = tie(
        whole_attn, back_one, back_two, ada_pre, ada_left, ada_right
    )
    back_attn = shard_rows(owned_step(whole_attn, left_rows[0], right_wholes[0], group), group)

    def joined(at, ada):
        return jnp.concatenate([ada, wide(back_attn[at]), wide(back_one[at]), wide(back_two[at])])

    precond = joined(0, ada_pre)
    left_new = stat_decay * left_stats + (1.0 - stat_decay) * joined(1, ada_left)
    right_new = stat_decay * right_stats + (1.0 - stat_decay) * joined(2, ada_right)
    momentum_new = moment_decay * momentum + precond
    weights_new = weights - weight_rate * momentum_new
    weights_copy = weights_new.astype(jnp.bfloat16)
    bias_second_new = stat_decay * bias_second + (1.0 - stat_decay) * bias_grad * bias_grad
    bias_moment_new = moment_decay * bias_moment + bias_grad * lax.rsqrt(
        bias_second_new + diag_epsilon
    )
    biases_new = biases - bias_rate * bias_moment_new
    return (
        block_out.reshape(tokens.shape),
        input_grad.reshape(tokens.shape),
        left_new,
        right_new,
        momentum_new,
        weights_new,
        weights_copy,
        bias_moment_new,
        bias_second_new,
        biases_new,
    )


def solution(mesh):
    placed = (
        P("dp", "fsdp", None, None),
        P("dp", None),
        P("dp"),
        P("dp", "fsdp", None, None),
        P(None, "dp", "fsdp"),
        P(("dp", "fsdp")),
        P(None, "dp", "fsdp"),
        P(None, "dp", "fsdp"),
        P(None, "dp", "fsdp"),
        P(None, "dp", "fsdp"),
        P(None, "dp", "fsdp"),
        P(("dp", "fsdp")),
        P(("dp", "fsdp")),
    )
    return jax.shard_map(
        per_device,
        mesh=mesh,
        in_specs=placed,
        out_specs=(
            P("dp", "fsdp", None, None),
            P("dp", "fsdp", None, None),
            P(None, "dp", "fsdp"),
            P(None, "dp", "fsdp"),
            P(None, "dp", "fsdp"),
            P(None, "dp", "fsdp"),
            P(None, "dp", "fsdp"),
            P(("dp", "fsdp")),
            P(("dp", "fsdp")),
            P(("dp", "fsdp")),
        ),
        check_vma=False,
    )
```

```python
import functools
import math

import jax
import jax.numpy as jnp
from jax import lax
from jax.experimental import pallas as pl
from jax.experimental.pallas import tpu as pltpu
from jax.sharding import PartitionSpec as P

HEADS = 16


precise = lax.Precision.HIGHEST
norm_epsilon = 1e-06
masked_score = -1e30
stat_decay = 0.5
moment_decay = 0.9
weight_rate = 0.7
bias_rate = 0.1
diag_epsilon = 1e-08
vmem_bytes = 50 * 2**20


def narrow(array):
    return array.astype(jnp.bfloat16)


def wide(array):
    return array.astype(jnp.float32)


def spec(shape, index_map, **keywords):
    return pl.BlockSpec(shape, index_map, **keywords)


def held(shape):
    return pl.BlockSpec(shape, lambda step: (0,) * len(shape), pipeline_mode=pl.Buffered(1))


def column_cuts(total):
    cuts, at = [], 0
    while at < total:
        cuts.append((at, min(total, at + 256)))
        at += 256
    return cuts


def dot_nn(left, right):
    return lax.dot_general(left, right, (((1,), (0,)), ((), ())), preferred_element_type=jnp.float32)


def dot_nt(left, right):
    return lax.dot_general(left, right, (((1,), (1,)), ((), ())), preferred_element_type=jnp.float32)


def dot_tn(left, right):
    return lax.dot_general(left, right, (((0,), (0,)), ((), ())), preferred_element_type=jnp.float32)


def split_high(values):
    high = narrow(values)
    return high, narrow(values - wide(high))


def valid_rows(count, rows, frames):
    at = lax.broadcasted_iota(jnp.int32, (rows, 1), 0)
    return (lax.rem(at, frames) < count).astype(jnp.float32)


def score_offset(count, size, frames, key_axis):
    first = lax.broadcasted_iota(jnp.int32, (size, size), 0)
    second = lax.broadcasted_iota(jnp.int32, (size, size), 1)
    key = second if key_axis == 1 else first
    met = (lax.div(first, frames) == lax.div(second, frames)) & (lax.rem(key, frames) < count)
    return jnp.where(met, 0.0, masked_score)


def head_windows(width):
    size = width // HEADS
    windows = []
    for head in range(HEADS):
        low, high = head * size, (head + 1) * size
        start = low // 128 * 128
        stop = min(width, -(-high // 128) * 128)
        windows.append((low - start, high - start, start, stop))
    return windows


def lane_mask(low, high, count, dtype):
    lanes = lax.broadcasted_iota(jnp.int32, (1, count), 1)
    return ((lanes >= low) & (lanes < high)).astype(jnp.float32).astype(dtype)


def norm_parts(values):
    centered = values - jnp.mean(values, axis=-1, keepdims=True)
    variance = jnp.mean(centered * centered, axis=-1, keepdims=True)
    inverse = lax.rsqrt(variance + norm_epsilon)
    return centered * inverse, inverse


def norm_back(grad, normed, inverse):
    first = jnp.mean(grad, axis=-1, keepdims=True)
    second = jnp.mean(grad * normed, axis=-1, keepdims=True)
    return (grad - first - normed * second) * inverse


def column_sum(values):
    return jnp.sum(values, axis=0, keepdims=True)


def start_loads(cuts, at, parts, whole, semaphores, first_index=0):
    loads = []
    for index, (part, first, rows) in enumerate(cuts, first_index):
        span = pl.ds(pl.multiple_of(at[index] * 16, 16), rows)
        source = parts[part].at[pl.ds(first, rows)]
        loads.append(pltpu.make_async_copy(source, whole.at[span], semaphores.at[index]))
        loads[-1].start()
    return loads


def attention_kernel(
    frames,
    counts,
    tokens,
    cotangent,
    mods,
    bias,
    blocks,
    attn_in,
    parts,
    mixed_low,
    proj_out,
    resid_out,
    mlp_in,
    d_branch,
    d_branch_sum,
    mixed,
    whole,
    semaphores,
):
    rows, width = tokens.shape
    clip = pl.program_id(0)
    loads = [
        pltpu.make_async_copy(blocks.at[at], whole.at[at], semaphores.at[at]) for at in range(4)
    ]

    @pl.when(clip == 0)
    def _():
        for load in loads:
            load.start()

    tile = min(rows, 128)
    count = counts[clip]
    shift_one, scale_one, gate_one = (mods[0, at : at + 1, :] for at in range(3))
    shift_two, scale_two, gate_two = (mods[0, at : at + 1, :] for at in range(3, 6))
    for first in range(0, rows, tile):
        span = slice(first, first + tile)
        normed, _ = norm_parts(wide(tokens[span]))
        attn_in[span] = narrow(normed * (1.0 + scale_one) + shift_one)
        branch_back = narrow(wide(cotangent[span]) * valid_rows(count, tile, frames) * gate_two)
        d_branch[span] = branch_back
        part_sum = column_sum(wide(branch_back))
        d_branch_sum[0] = part_sum if first == 0 else d_branch_sum[0] + part_sum

    @pl.when(clip == 0)
    def _():
        for load in loads:
            load.wait()

    scale = (width // HEADS) ** -0.5
    source = attn_in[...]
    for low, high in column_cuts(width):
        span = slice(low, high)
        query = (dot_nn(source, whole[0, :, span]) + bias[0:1, span]) * scale
        parts[0, :, span], parts[1, :, span] = split_high(query)
        parts[2, :, span], parts[3, :, span] = split_high(dot_nn(source, whole[1, :, span]))
        parts[4, :, span] = narrow(dot_nn(source, whole[2, :, span]) + bias[2:3, span])
    offset = score_offset(count, tile, frames, 1)
    mixed[...] = jnp.zeros_like(mixed)
    for first in range(0, rows, tile):
        span = slice(first, first + tile)
        for low, high, start, stop in head_windows(width):
            lanes = slice(start, stop)
            mask = lane_mask(low, high, stop - start, jnp.bfloat16)
            key_high = parts[2, span, lanes]
            query_high = parts[0, span, lanes] * mask
            scores = dot_nt(query_high, key_high)
            scores += dot_nt(parts[1, span, lanes] * mask, key_high)
            scores += dot_nt(query_high, parts[3, span, lanes]) + offset
            expons = jnp.exp(scores - jnp.max(scores, axis=-1, keepdims=True))
            probs = expons * (1.0 / jnp.sum(expons, axis=-1, keepdims=True))
            out = dot_nn(narrow(probs), parts[4, span, lanes] * mask)
            mixed[span, lanes] += out
    mixed_low[...] = narrow(mixed[...])
    source = mixed_low[...]
    for low, high in column_cuts(width):
        span = slice(low, high)
        proj_out[:, span] = dot_nn(source, whole[3, :, span]) + bias[3:4, span]
    for first in range(0, rows, tile):
        span = slice(first, first + tile)
        resid = wide(tokens[span]) + valid_rows(count, tile, frames) * gate_one * proj_out[span]
        resid_out[span] = resid
        normed, _ = norm_parts(resid)
        mlp_in[span] = narrow(normed * (1.0 + scale_two) + shift_two)


def run_attention(frames, counts, tokens, cotangent, mods, bias, blocks):
    total, width = tokens.shape
    clips = mods.shape[0]
    rows = total // clips
    clip_rows = spec((rows, width), lambda clip: (clip, 0))
    low = jax.ShapeDtypeStruct((total, width), jnp.bfloat16)
    full = jax.ShapeDtypeStruct((total, width), jnp.float32)
    return pl.pallas_call(
        functools.partial(attention_kernel, frames),
        grid=(clips,),
        in_specs=[
            pl.BlockSpec(memory_space=pltpu.SMEM),
            clip_rows,
            clip_rows,
            spec((1,) + mods.shape[1:], lambda clip: (clip, 0, 0)),
            held(bias.shape),
            pl.BlockSpec(memory_space=pl.ANY),
        ],
        out_specs=[
            clip_rows,
            spec((5, rows, width), lambda clip: (0, clip, 0)),
            clip_rows,
            clip_rows,
            clip_rows,
            clip_rows,
            clip_rows,
            spec((1, 1, width), lambda clip: (clip, 0, 0)),
        ],
        out_shape=[
            low,
            jax.ShapeDtypeStruct((5, total, width), jnp.bfloat16),
            low,
            full,
            full,
            low,
            low,
            jax.ShapeDtypeStruct((clips, 1, width), jnp.float32),
        ],
        scratch_shapes=[
            pltpu.VMEM((rows, width), jnp.float32),
            pltpu.VMEM(blocks.shape, jnp.bfloat16),
            pltpu.SemaphoreType.DMA((4,)),
        ],
        compiler_params=pltpu.CompilerParams(vmem_limit_bytes=vmem_bytes),
        cost_estimate=pl.CostEstimate(
            flops=16 * total * width * width, bytes_accessed=100 * total * width, transcendentals=0
        ),
    )(counts, tokens, cotangent, mods, bias, blocks)


def stacked(numbers):
    return jnp.stack([jnp.asarray(number, jnp.int32) for number in numbers])


def hidden_kernel(cuts, order, starts, mlp_in, bias, *refs):
    whole_out, hidden, slope, whole, semaphores, store_semaphores = refs[-6:]
    pieces = refs[:-6]
    step, steps = pl.program_id(0), pl.num_programs(0)
    width = mlp_in.shape[-1]
    flat = [cut for group in cuts for cut in group]
    span = pl.ds(pl.multiple_of(order[step] * width, width), width)

    @pl.when(step == 0)
    def _():
        start_loads(flat, starts, pieces, whole, semaphores)

    index = 0
    for at, group in enumerate(cuts):
        first_index = index
        index += len(group)

        @pl.when(step == at)
        def _(group=group, first_index=first_index):
            for offset, (part, first, size) in enumerate(group):
                target = pl.ds(pl.multiple_of(starts[first_index + offset] * 16, 16), size)
                pltpu.make_async_copy(
                    pieces[part].at[pl.ds(first, size)],
                    whole.at[target],
                    semaphores.at[first_index + offset],
                ).wait()

    pltpu.make_async_copy(whole.at[span], whole_out.at[span], store_semaphores.at[step]).start()
    root = (2.0 / math.pi) ** 0.5
    source = mlp_in[...]
    block = whole.at[span]
    for low, high in column_cuts(width):
        lanes = slice(low, high)
        pre = dot_nn(source, block[:, lanes]) + bias[0, :, lanes]
        square = pre * pre
        bent = jnp.tanh(root * pre * (1.0 + 0.044715 * square))
        half = 0.5 + 0.5 * bent
        hidden[0, :, lanes] = narrow(pre * half)
        steep = (0.5 * root) * pre * (1.0 + 3 * 0.044715 * square)
        slope[0, :, lanes] = narrow(half + steep * (1.0 - bent * bent))

    @pl.when(step == steps - 1)
    def _():
        for at in range(len(cuts)):
            rows = pl.ds(pl.multiple_of(order[at] * width, width), width)
            pltpu.make_async_copy(
                whole.at[rows], whole_out.at[rows], store_semaphores.at[at]
            ).wait()


def run_hidden(mlp_in, gathered, bias):
    pieces, cuts, starts, order = gathered
    total, width = mlp_in.shape
    count = len(cuts)
    per_block = pl.BlockSpec((1, total, width), lambda at, order, starts: (order[at], 0, 0))
    out = jax.ShapeDtypeStruct((count, total, width), jnp.bfloat16)
    return pl.pallas_call(
        functools.partial(hidden_kernel, cuts),
        grid_spec=pltpu.PrefetchScalarGridSpec(
            num_scalar_prefetch=2,
            grid=(count,),
            in_specs=[
                pl.BlockSpec((total, width), lambda at, order, starts: (0, 0)),
                pl.BlockSpec((1, 1, width), lambda at, order, starts: (order[at], 0, 0)),
            ]
            + [pl.BlockSpec(memory_space=pl.ANY)] * len(pieces),
            out_specs=[pl.BlockSpec(memory_space=pl.ANY), per_block, per_block],
            scratch_shapes=[
                pltpu.VMEM((count * width, width), jnp.bfloat16),
                pltpu.SemaphoreType.DMA((len(starts),)),
                pltpu.SemaphoreType.DMA((count,)),
            ],
        ),
        out_shape=[jax.ShapeDtypeStruct((count * width, width), jnp.bfloat16), out, out],
        compiler_params=pltpu.CompilerParams(vmem_limit_bytes=vmem_bytes),
        cost_estimate=pl.CostEstimate(
            flops=8 * total * width * width, bytes_accessed=50 * total * width, transcendentals=0
        ),
    )(stacked(order), stacked(starts), mlp_in, bias, *pieces)


def branch_kernel(
    frames,
    counts,
    hidden,
    slope,
    block,
    d_branch,
    bias,
    gates,
    resid,
    cotangent,
    d_pre,
    d_pre_sum,
    block_out,
    d_gate,
    branch,
):
    step, steps = pl.program_id(0), pl.num_programs(0)
    total, width = resid.shape
    clips = gates.shape[0]
    rows = total // clips
    source, back = hidden[0], d_branch[...]

    @pl.when(step == 0)
    def _():
        branch[...] = jnp.zeros_like(branch)

    for low, high in column_cuts(width):
        span = slice(low, high)
        d_hidden = dot_nt(back, block[0, span, :])
        low_back = narrow(d_hidden * wide(slope[0, :, span]))
        d_pre[0, :, span] = low_back
        d_pre_sum[0, :, span] = column_sum(wide(low_back))
        branch[:, span] += dot_nn(source, block[0, :, span])

    @pl.when(step == steps - 1)
    def _():
        for clip in range(clips):
            span = slice(clip * rows, (clip + 1) * rows)
            kept = valid_rows(counts[clip], rows, frames) * (branch[span] + bias[...])
            block_out[span] = narrow(resid[span] + gates[clip] * kept)
            d_gate[clip] = column_sum(wide(cotangent[span]) * kept)


def run_branch(frames, counts, hidden, slope, blocks, d_branch, bias, gates, resid, cotangent):
    count, total, width = hidden.shape
    clips = gates.shape[0]
    per_block = spec((1, total, width), lambda at: (at, 0, 0))
    low = jax.ShapeDtypeStruct((total, width), jnp.bfloat16)
    return pl.pallas_call(
        functools.partial(branch_kernel, frames),
        grid=(count,),
        in_specs=[
            pl.BlockSpec(memory_space=pltpu.SMEM),
            per_block,
            per_block,
            spec((1, width, width), lambda at: (at, 0, 0)),
            held((total, width)),
            held(bias.shape),
            held(gates.shape),
            held((total, width)),
            held((total, width)),
        ],
        out_specs=[
            per_block,
            spec((1, 1, width), lambda at: (at, 0, 0)),
            held((total, width)),
            held((clips, 1, width)),
        ],
        out_shape=[
            jax.ShapeDtypeStruct((count, total, width), jnp.bfloat16),
            jax.ShapeDtypeStruct((count, 1, width), jnp.float32),
            low,
            jax.ShapeDtypeStruct((clips, 1, width), jnp.float32),
        ],
        scratch_shapes=[pltpu.VMEM((total, width), jnp.float32)],
        compiler_params=pltpu.CompilerParams(vmem_limit_bytes=vmem_bytes),
        cost_estimate=pl.CostEstimate(
            flops=16 * total * width * width, bytes_accessed=40 * total * width, transcendentals=0
        ),
    )(counts, hidden, slope, blocks, d_branch, bias, gates, resid, cotangent)


def resid_kernel(
    frames,
    counts,
    d_pre,
    block,
    mods,
    resid,
    cotangent,
    proj,
    d_resid_out,
    d_proj,
    sums,
    total_grad,
):
    step, steps = pl.program_id(0), pl.num_programs(0)
    total, width = resid.shape
    clips = mods.shape[0]
    rows = total // clips
    tile = min(rows, 128)
    source = d_pre[0]

    @pl.when(step == 0)
    def _():
        total_grad[...] = jnp.zeros_like(total_grad)

    for low, high in column_cuts(width):
        span = slice(low, high)
        total_grad[:, span] += dot_nt(source, block[0, span, :])

    @pl.when(step == steps - 1)
    def _():
        for clip in range(clips):
            gate_one, scale_two = mods[clip, 2:3, :], mods[clip, 4:5, :]
            found = [0.0] * 4
            for first in range(clip * rows, (clip + 1) * rows, tile):
                span = slice(first, first + tile)
                grad = total_grad[span]
                normed, inverse = norm_parts(resid[span])
                back = norm_back(grad * (1.0 + scale_two), normed, inverse)
                d_resid = wide(cotangent[span]) + back
                d_resid_out[span] = d_resid
                kept = valid_rows(counts[clip], tile, frames) * d_resid
                low_back = narrow(kept * gate_one)
                d_proj[span] = low_back
                terms = (grad, grad * normed, kept * proj[span], wide(low_back))
                found = [old + column_sum(term) for old, term in zip(found, terms)]
            for at in range(4):
                sums[clip, at : at + 1, :] = found[at]


def run_resid(frames, counts, d_pre, blocks, mods, resid, cotangent, proj):
    count, total, width = d_pre.shape
    clips = mods.shape[0]
    return pl.pallas_call(
        functools.partial(resid_kernel, frames),
        grid=(count,),
        in_specs=[
            pl.BlockSpec(memory_space=pltpu.SMEM),
            spec((1, total, width), lambda at: (at, 0, 0)),
            spec((1, width, width), lambda at: (at, 0, 0)),
            held(mods.shape),
            held((total, width)),
            held((total, width)),
            held((total, width)),
        ],
        out_specs=[held((total, width)), held((total, width)), held((clips, 4, width))],
        out_shape=[
            jax.ShapeDtypeStruct((total, width), jnp.float32),
            jax.ShapeDtypeStruct((total, width), jnp.bfloat16),
            jax.ShapeDtypeStruct((clips, 4, width), jnp.float32),
        ],
        scratch_shapes=[pltpu.VMEM((total, width), jnp.float32)],
        compiler_params=pltpu.CompilerParams(vmem_limit_bytes=vmem_bytes),
        cost_estimate=pl.CostEstimate(
            flops=8 * total * width * width, bytes_accessed=40 * total * width, transcendentals=0
        ),
    )(counts, d_pre, blocks, mods, resid, cotangent, proj)


def attention_back_kernel(
    frames, counts, d_proj, parts, block, d_qkv, sums, d_mixed, d_query, d_key, d_value
):
    rows, width = d_proj.shape
    tile = min(rows, 128)
    count = counts[pl.program_id(0)]
    source = d_proj[...]
    for low, high in column_cuts(width):
        d_mixed[:, low:high] = narrow(dot_nt(source, block[0, low:high, :]))
    scale = (width // HEADS) ** -0.5
    offset = score_offset(count, tile, frames, 0)
    for ref in (d_query, d_key, d_value):
        ref[...] = jnp.zeros_like(ref)
    for first in range(0, rows, tile):
        span = slice(first, first + tile)
        for low, high, start, stop in head_windows(width):
            lanes = slice(start, stop)
            mask = lane_mask(low, high, stop - start, jnp.bfloat16)
            query_high = parts[0, span, lanes] * mask
            key_high = parts[2, span, lanes] * mask
            back = d_mixed[span, lanes] * mask
            scores = dot_nt(key_high, query_high)
            scores += dot_nt(key_high, parts[1, span, lanes])
            scores += dot_nt(parts[3, span, lanes], query_high) + offset
            expons = jnp.exp(scores - jnp.max(scores, axis=0, keepdims=True))
            probs = expons * (1.0 / jnp.sum(expons, axis=0, keepdims=True))
            d_probs = dot_nt(parts[4, span, lanes], back)
            inner = jnp.sum(d_probs * probs, axis=0, keepdims=True)
            d_scores = narrow(probs * (d_probs - inner))
            d_value[span, lanes] += dot_nn(narrow(probs), back)
            d_key[span, lanes] += dot_nn(d_scores, query_high)
            d_query[span, lanes] += dot_tn(d_scores, key_high)
    for at, ref in enumerate((d_query, d_key, d_value)):
        low_back = narrow(ref[...] * scale) if at == 0 else narrow(ref[...])
        d_qkv[at] = low_back
        sums[0, at : at + 1, :] = column_sum(wide(low_back))
    d_qkv[3] = source


def run_attention_back(frames, counts, d_proj, parts, block):
    total, width = d_proj.shape
    clips = counts.shape[0]
    rows = total // clips
    return pl.pallas_call(
        functools.partial(attention_back_kernel, frames),
        grid=(clips,),
        in_specs=[
            pl.BlockSpec(memory_space=pltpu.SMEM),
            spec((rows, width), lambda clip: (clip, 0)),
            spec((5, rows, width), lambda clip: (0, clip, 0)),
            spec((1, width, width), lambda clip: (3, 0, 0), pipeline_mode=pl.Buffered(1)),
        ],
        out_specs=[
            spec((4, rows, width), lambda clip: (0, clip, 0)),
            spec((1, 3, width), lambda clip: (clip, 0, 0)),
        ],
        out_shape=[
            jax.ShapeDtypeStruct((4, total, width), jnp.bfloat16),
            jax.ShapeDtypeStruct((clips, 3, width), jnp.float32),
        ],
        scratch_shapes=[pltpu.VMEM((rows, width), jnp.bfloat16)]
        + [pltpu.VMEM((rows, width), jnp.float32)] * 3,
        compiler_params=pltpu.CompilerParams(vmem_limit_bytes=vmem_bytes),
        cost_estimate=pl.CostEstimate(
            flops=12 * total * width * width, bytes_accessed=20 * total * width, transcendentals=0
        ),
    )(counts, d_proj, parts, block)


def input_kernel(d_qkv, block, mods, tokens, d_resid, input_grad, sums, total_grad):
    step, steps = pl.program_id(0), pl.num_programs(0)
    total, width = tokens.shape
    clips = mods.shape[0]
    rows = total // clips
    tile = min(rows, 128)
    source = d_qkv[0]

    @pl.when(step == 0)
    def _():
        total_grad[...] = jnp.zeros_like(total_grad)

    for low, high in column_cuts(width):
        span = slice(low, high)
        total_grad[:, span] += dot_nt(source, block[0, span, :])

    @pl.when(step == steps - 1)
    def _():
        for clip in range(clips):
            scale_one = mods[clip, 1:2, :]
            found = [0.0] * 2
            for first in range(clip * rows, (clip + 1) * rows, tile):
                span = slice(first, first + tile)
                grad = total_grad[span]
                normed, inverse = norm_parts(wide(tokens[span]))
                back = norm_back(grad * (1.0 + scale_one), normed, inverse)
                input_grad[span] = narrow(d_resid[span] + back)
                terms = (grad, grad * normed)
                found = [old + column_sum(term) for old, term in zip(found, terms)]
            for at in range(2):
                sums[clip, at : at + 1, :] = found[at]


def run_input(d_qkv, blocks, mods, tokens, d_resid):
    total, width = tokens.shape
    clips = mods.shape[0]
    return pl.pallas_call(
        input_kernel,
        grid=(3,),
        in_specs=[
            spec((1, total, width), lambda at: (at, 0, 0)),
            spec((1, width, width), lambda at: (at, 0, 0)),
            held(mods.shape),
            held((total, width)),
            held((total, width)),
        ],
        out_specs=[held((total, width)), held((clips, 2, width))],
        out_shape=[
            jax.ShapeDtypeStruct((total, width), jnp.bfloat16),
            jax.ShapeDtypeStruct((clips, 2, width), jnp.float32),
        ],
        scratch_shapes=[pltpu.VMEM((total, width), jnp.float32)],
        compiler_params=pltpu.CompilerParams(vmem_limit_bytes=vmem_bytes),
        cost_estimate=pl.CostEstimate(
            flops=6 * total * width * width, bytes_accessed=30 * total * width, transcendentals=0
        ),
    )(d_qkv, blocks, mods, tokens, d_resid)


def tie(*values):
    return lax.optimization_barrier(values)


def packed(arrays, tile):
    flat = jnp.concatenate([array.reshape(-1) for array in arrays])
    return jnp.pad(flat, (0, -flat.shape[0] % (tile * 128))).reshape(-1, 128)


def core_swap(array):
    count = lax.axis_size("dp")
    return lax.ppermute(array, "dp", [(at, at ^ 1) for at in range(count)])


def chip_shift(array, step):
    count = lax.axis_size("dp")
    return lax.ppermute(array, "dp", [(at, (at + 2 * step) % count) for at in range(count)])


def chip_swap(array, bits):
    count = lax.axis_size("dp")
    return lax.ppermute(array, "dp", [(at, at ^ (2 * bits)) for at in range(count)])


def rank_swap(array, bits):
    count = lax.axis_size("fsdp")
    return lax.ppermute(array, "fsdp", [(at, at ^ bits) for at in range(count)])


def entry(array, at, axis=0):
    return lax.dynamic_index_in_dim(array, at, axis, keepdims=False)


def place_kernel(cuts, at, *refs):
    parts, whole, held_rows, semaphores = refs[:-3], refs[-3], refs[-2], refs[-1]
    spans, loads, stores = [], [], []
    for index, (part, first, rows) in enumerate(cuts):
        spans.append(pl.ds(pl.multiple_of(at[index] * 16, 16), rows))
        source = parts[part].at[pl.ds(first, rows)]
        loads.append(
            pltpu.make_async_copy(source, held_rows.at[spans[index]], semaphores.at[0, index])
        )
        loads[index].start()
    for index, span in enumerate(spans):
        loads[index].wait()
        stores.append(
            pltpu.make_async_copy(held_rows.at[span], whole.at[span], semaphores.at[1, index])
        )
        stores[index].start()
    for store in stores:
        store.wait()


def place(parts, cuts, starts, rows):
    width = parts[0].shape[-1]
    dtype = parts[0].dtype
    return pl.pallas_call(
        functools.partial(place_kernel, cuts),
        in_specs=[pl.BlockSpec(memory_space=pltpu.SMEM)]
        + [pl.BlockSpec(memory_space=pl.ANY)] * len(parts),
        out_specs=pl.BlockSpec(memory_space=pl.ANY),
        out_shape=jax.ShapeDtypeStruct((rows, width), dtype),
        scratch_shapes=[
            pltpu.VMEM((rows, width), dtype),
            pltpu.SemaphoreType.DMA((2, len(cuts))),
        ],
        compiler_params=pltpu.CompilerParams(vmem_limit_bytes=vmem_bytes),
        cost_estimate=pl.CostEstimate(
            flops=0, bytes_accessed=4 * rows * width, transcendentals=0
        ),
    )(stacked(starts), *parts)


def own_rows(parts, group):
    ranks, at = lax.axis_size("fsdp"), lax.axis_index("fsdp")
    shares = ranks // group
    count, _, row_part, col_part = parts.shape
    chunk = row_part // shares
    split = parts.reshape(count, group, shares, chunk, col_part).transpose(1, 2, 0, 3, 4)
    split = split.reshape(ranks, count, chunk, col_part)
    if shares > 1:
        moved = lax.all_to_all(split, "fsdp", 0, 0, tiled=True)
        (moved,) = yield (moved,)
        yield moved.transpose(1, 2, 0, 3).reshape(count, chunk, ranks * col_part)
        return
    panels = [entry(split, at)]
    panels += [rank_swap(entry(split, at ^ bits), bits) for bits in range(1, ranks)]
    panels = yield tuple(panels)
    placed = [
        lax.select_n(at, *[panels[panel ^ index] for index in range(ranks)])
        for panel in range(ranks)
    ]
    yield jnp.concatenate(placed, axis=2)


def shard_rows(split, group):
    ranks, count, chunk, col_part = split.shape
    shares = ranks // group
    moved = lax.all_to_all(split, "fsdp", 0, 0, tiled=True)
    moved = moved.reshape(group, shares, count, chunk, col_part).transpose(2, 0, 1, 3, 4)
    return moved.reshape(count, group, shares * chunk, col_part)


def gather_blocks(rows, group):
    ranks, dp_count = lax.axis_size("fsdp"), lax.axis_size("dp")
    shares = ranks // group
    chunk, total = rows.shape
    all_rows = lax.all_gather(rows, ("fsdp", "dp"), axis=0, tiled=True)
    if shares > 1:
        all_rows = all_rows.reshape(group, shares, dp_count, chunk, total).transpose(0, 2, 1, 3, 4)
    return all_rows.reshape(group, total, total)


def join_line(rows):
    chips, chip = lax.axis_size("dp") // 2, lax.axis_index("dp") // 2
    chunk = rows.shape[0]
    found = [rows] + [chip_shift(rows, step) for step in range(1, chips)]
    starts = [(chip - step) % chips * (chunk // 16) for step in range(chips)]
    return place(found, [(step, 0, chunk) for step in range(chips)], starts, chips * chunk)


def gather_second(rows, group):
    ranks, at = lax.axis_size("fsdp"), lax.axis_index("fsdp")
    total = rows.shape[-1]
    if ranks != group:
        blocks = gather_blocks(rows, group).reshape(group * total, total)
        for _ in range(2):
            (blocks,) = yield (blocks,)
        cuts = [[(0, index * total, total)] for index in range(group)]
        yield [blocks], cuts, [index * (total // 16) for index in range(group)], range(group)
        return
    chips = lax.axis_size("dp") // 2
    core = lax.axis_index("dp") % 2
    chunk, half = rows.shape[0], total // 2
    line = join_line(rows)
    cuts = [(side, step * chunk, chunk) for side in range(2) for step in range(chips)]
    starts = [
        (2 * step + side) * (chunk // 16) for side in (core, 1 - core) for step in range(chips)
    ]
    (own,) = yield (place([line, core_swap(line)], cuts, starts, total),)
    share = lax.dynamic_slice_in_dim(own, core * half, half, 0)
    mine = yield tuple(rank_swap(share, bits) for bits in range(1, ranks))
    parts, cuts, starts = [own], [[(0, 0, total)]], [at * (total // 16)]
    for bits in range(1, ranks):
        parts += [mine[bits - 1], core_swap(mine[bits - 1])]
        cuts.append([(2 * bits - 1, 0, half), (2 * bits, 0, half)])
        starts += [((at ^ bits) * 2 + side) * (half // 16) for side in (core, 1 - core)]
    yield parts, cuts, starts, [at ^ bits for bits in range(ranks)]


def gather_own(rows, group):
    ranks = lax.axis_size("fsdp")
    shares = ranks // group
    if shares > 1:
        sets = [[share + shares * block for share in range(shares)] for block in range(group)]
        rows = lax.all_gather(rows, "fsdp", axis=1, tiled=True, axis_index_groups=sets)
    return lax.all_gather(rows, "dp", axis=1, tiled=True)


def sum_blocks(product, cut, total, group):
    ranks, dp_count = lax.axis_size("fsdp"), lax.axis_size("dp")
    shares = ranks // group
    if shares > 1:
        blocks = narrow(product(cut(0, total)))
        chunk = total // (dp_count * shares)
        blocks = blocks.reshape(group, dp_count, shares, chunk, -1).transpose(0, 2, 1, 3, 4)
        rows = lax.psum_scatter(
            blocks.reshape(group * total, -1), ("fsdp", "dp"), scatter_dimension=0, tiled=True
        )
        for _ in range(7):
            (rows,) = yield (rows,)
        yield gather_own(rows[None], group)[0]
        return
    chips, half = dp_count // 2, total // 2
    chunk = half // chips
    core, chip = lax.axis_index("dp") % 2, lax.axis_index("dp") // 2
    low_bit, high_bit = lax.axis_index("fsdp") % 2, lax.axis_index("fsdp") // 2
    (away,) = yield (narrow(product(cut((1 - core) * half, half))),)
    (away_in,) = yield (core_swap(away),)
    here = product(cut(core * half, half))
    here = narrow(here + wide(away_in))
    here = here.reshape(2, 2, chips, chunk, -1)
    middle = chips // 2
    first, second = here[:, :, :middle], here[:, :, middle:]
    first_out, second_out = yield (entry(first, 1 - low_bit, 1), entry(second, 1 - high_bit, 0))
    first_in, second_in = yield (rank_swap(first_out, 1), rank_swap(second_out, 2))
    first = narrow(wide(entry(first, low_bit, 1)) + wide(first_in))
    second = narrow(wide(entry(second, high_bit, 0)) + wide(second_in))
    first_in = rank_swap(entry(first, 1 - high_bit), 2)
    second_in = rank_swap(entry(second, 1 - low_bit), 1)
    first_in, second_in = yield (first_in, second_in)
    first = narrow(wide(entry(first, high_bit)) + wide(first_in))
    second = narrow(wide(entry(second, low_bit)) + wide(second_in))
    line = jnp.concatenate([first, second])
    step = 1
    while step < chips:
        bit = chip // step % 2
        line = line.reshape(-1, 2, *line.shape[1:])
        (line_in,) = yield (chip_swap(entry(line, 1 - bit, 1), step),)
        line = narrow(wide(entry(line, bit, 1)) + wide(line_in))
        step *= 2
    yield lax.all_gather(line[0], "dp", axis=0, tiled=True)


def fast_dot(subscripts, left, right):
    return jnp.einsum(subscripts, left, right, preferred_element_type=jnp.float32)


def products_kernel(chips, at, gathered, left_root, right_root, out, whole, semaphores):
    chunk, width = left_root.shape
    ranks = out.shape[0]
    copies = []
    for index in range(2 * chips):
        first = (index % 2 * chips + index // 2) * chunk
        copies.append(
            pltpu.make_async_copy(
                gathered.at[pl.ds(index * chunk, chunk)],
                whole.at[pl.ds(first, chunk)],
                semaphores.at[index],
            )
        )
        copies[-1].start()
    for copy in copies:
        copy.wait()
    first = at[0] * 16
    grad = whole[...]
    picked = lax.broadcasted_iota(jnp.int32, (width, chunk), 0) - first
    picked = picked == lax.broadcasted_iota(jnp.int32, (width, chunk), 1)
    own_columns = narrow(dot_nn(grad, narrow(picked.astype(jnp.float32))))
    side_high, side_low = split_high(dot_nn(left_root[...], grad))
    right = right_root[...]
    precond = dot_nn(side_high, right) + dot_nn(side_low, right)
    outer = dot_nt(whole[pl.ds(pl.multiple_of(first, 16), chunk), :], grad)
    inner = dot_tn(own_columns, grad)
    for at_out, product in enumerate((precond, outer, inner)):
        low = narrow(product)
        for rank in range(ranks):
            span = slice(rank * (width // ranks), (rank + 1) * (width // ranks))
            out[rank, at_out] = low[:, span]


def owned_step(whole, left_root, right_root, group):
    ranks, dp_count = lax.axis_size("fsdp"), lax.axis_size("dp")
    shares = ranks // group
    chunk, total = left_root.shape
    col_part = total // ranks
    first = lax.axis_index("dp") * (chunk * shares) + lax.axis_index("fsdp") % shares * chunk
    if shares == 1:
        return pl.pallas_call(
            functools.partial(products_kernel, dp_count // 2),
            in_specs=[
                pl.BlockSpec(memory_space=pltpu.SMEM),
                pl.BlockSpec(memory_space=pl.ANY),
                pl.BlockSpec(memory_space=pltpu.VMEM),
                pl.BlockSpec(memory_space=pltpu.VMEM),
            ],
            out_specs=pl.BlockSpec(memory_space=pltpu.VMEM),
            out_shape=jax.ShapeDtypeStruct((ranks, 3, chunk, col_part), jnp.bfloat16),
            scratch_shapes=[
                pltpu.VMEM((total, total), jnp.bfloat16),
                pltpu.SemaphoreType.DMA((dp_count,)),
            ],
            compiler_params=pltpu.CompilerParams(vmem_limit_bytes=vmem_bytes),
            cost_estimate=pl.CostEstimate(
                flops=12 * chunk * total * total, bytes_accessed=6 * total * total, transcendentals=0
            ),
        )((first // 16)[None], whole, left_root, right_root)
    grad_rows = lax.dynamic_slice_in_dim(whole, first, chunk, 0)
    own_columns = lax.dynamic_slice_in_dim(whole, first, chunk, 1)
    outer = fast_dot("rk,jk->rj", grad_rows, whole)
    inner = fast_dot("kr,kj->rj", own_columns, whole)
    side_high, side_low = split_high(fast_dot("rk,kj->rj", left_root, whole))
    precond = fast_dot("rk,kj->rj", side_high, right_root) + fast_dot(
        "rk,kj->rj", side_low, right_root
    )
    products = narrow(jnp.stack([precond, outer, inner]))
    return products.reshape(3, chunk, ranks, col_part).transpose(2, 0, 1, 3)


def per_device(
    tokens,
    conditioning,
    frame_counts,
    cotangent,
    weights,
    biases,
    momentum,
    left_stats,
    right_stats,
    left_roots,
    right_roots,
    bias_moment,
    bias_second,
):
    group = 4
    mod_count = 6
    clip_count, pos_count, frames, width = tokens.shape
    token_count = clip_count * pos_count * frames
    block_count, row_part, col_part = weights.shape
    dp_count, ranks = lax.axis_size("dp"), lax.axis_size("fsdp")
    dp_at, rank_at = lax.axis_index("dp"), lax.axis_index("fsdp")
    all_clips = clip_count * dp_count
    bias_part = biases.shape[0]
    stream = tokens.reshape(token_count, width)
    grad_out = cotangent.reshape(token_count, width)
    low_weights = narrow(weights).reshape(block_count, row_part, col_part)
    shards = low_weights[mod_count:].reshape(-1, group, row_part, col_part)

    attn_rows, cond_low = own_rows(shards[:1], group), narrow(jax.nn.silu(conditioning))
    attn_panels = next(attn_rows)
    first_parts = lax.all_gather(packed([cond_low, narrow(biases)], 16), "dp", axis=0, tiled=True)
    attn_panels, first_parts, other_shards = tie(attn_panels, first_parts, shards[1:])
    attn_rows = attn_rows.send(attn_panels)[0]
    other_rows = own_rows(other_shards, group)
    other_panels = next(other_rows)
    attn_w = gather_blocks(attn_rows, group)
    one_rows, two_rows = other_rows.send(other_panels)
    two_w = gather_blocks(two_rows, group)

    first_parts = first_parts.reshape(dp_count, -1)
    cond_all = first_parts[:, : clip_count * width].reshape(all_clips, width)
    bias_rows = wide(first_parts[:, clip_count * width : clip_count * width + bias_part])
    cond_rows = lax.dynamic_slice_in_dim(cond_all, dp_at * row_part, row_part, 1)
    cond_cols = wide(lax.dynamic_slice_in_dim(cond_all, rank_at * col_part, col_part, 1))
    mod_parts = fast_dot("cr,jre->cje", cond_rows, low_weights[:mod_count])
    mod_parts = lax.all_to_all(mod_parts, "dp", 0, 0, tiled=True)
    mod_parts, one_rows = tie(mod_parts, one_rows)
    one_steps = gather_second(one_rows, group)
    one_parts = next(one_steps)
    mod_cols = jnp.sum(mod_parts.reshape(dp_count, clip_count, mod_count, col_part), axis=0)
    left_cond = jnp.einsum("jrk,ck->jrc", left_roots[:mod_count], cond_cols, precision=precise)
    mod_size, bias_size = mod_cols.size, dp_count * bias_part
    second_parts = lax.all_gather(
        packed([mod_cols, bias_rows, left_cond], 8), "fsdp", axis=0, tiled=True
    )
    second_parts, one_parts = tie(second_parts, one_parts)
    one_parts = one_steps.send(one_parts)
    second_parts = second_parts.reshape(ranks, -1)
    mods = second_parts[:, :mod_size].reshape(ranks, clip_count, mod_count, col_part)
    mods = mods.transpose(1, 2, 0, 3).reshape(clip_count, mod_count, width)
    bias_all = second_parts[:, mod_size : mod_size + bias_size].reshape(ranks, dp_count, bias_part)
    bias_all = bias_all.transpose(1, 0, 2).reshape(-1, width)
    left_size = mod_size + bias_size + left_cond.size
    left_cond = jnp.sum(second_parts[:, mod_size + bias_size : left_size], axis=0)
    left_cond = left_cond.reshape(mod_count, row_part, all_clips)
    mods = mods + bias_all[:mod_count]
    bias_table = jnp.concatenate(
        [bias_all[6:7], jnp.zeros((1, width), jnp.float32), bias_all[7:14]]
    )

    roots = jnp.stack([narrow(left_roots[mod_count:]), narrow(right_roots[mod_count:])])
    mods, roots = tie(mods, roots)
    root_rows = own_rows(roots.reshape(-1, group, row_part, col_part), group)
    root_panels = next(root_rows)
    attn_in, parts, mixed, proj, resid, mlp_in, d_branch, d_branch_sums = run_attention(
        frames, frame_counts, stream, grad_out, mods, bias_table, attn_w
    )
    mlp_in, one_parts = tie(mlp_in, one_parts)
    one_w, hidden, slope = run_hidden(mlp_in, one_steps.send(one_parts), bias_table[4:8, None])
    one_w = one_w.reshape(group, width, width)

    two_steps = sum_blocks(
        lambda left: fast_dot("jtd,te->jde", left, d_branch),
        lambda first, size: lax.dynamic_slice_in_dim(hidden, first, size, 2),
        width,
        group,
    )
    two_parts = next(two_steps)
    hidden, two_parts, root_panels = tie(hidden, two_parts, root_panels)
    two_parts = two_steps.send(two_parts)
    root_rows = root_rows.send(root_panels)
    hidden, root_rows = tie(hidden, root_rows)
    left_rows, right_rows = jnp.split(root_rows, 2)
    right_wholes = [gather_own(rows[None], group)[0] for rows in right_rows]
    d_pre, d_pre_sums, block_out, d_gate_two = run_branch(
        frames,
        frame_counts,
        hidden,
        slope,
        two_w,
        d_branch,
        bias_table[8:9],
        mods[:, 5:6],
        resid,
        grad_out,
    )
    d_pre, two_parts = tie(d_pre, two_parts)
    two_parts = two_steps.send(two_parts)
    d_pre, two_parts = tie(d_pre, two_parts)
    two_parts = two_steps.send(two_parts)
    one_steps = sum_blocks(
        lambda left: fast_dot("td,jte->jde", left, d_pre),
        lambda first, size: lax.dynamic_slice_in_dim(mlp_in, first, size, 1),
        width,
        group,
    )
    one_parts = next(one_steps)
    d_pre, one_parts = tie(d_pre, one_parts)
    one_parts = one_steps.send(one_parts)
    d_resid, d_proj, resid_sums = run_resid(
        frames, frame_counts, d_pre, one_w, mods, resid, grad_out, proj
    )
    d_proj, one_parts, two_parts = tie(d_proj, one_parts, two_parts)
    two_parts = two_steps.send(two_parts)
    one_parts = one_steps.send(one_parts)
    d_proj, one_parts = tie(d_proj, one_parts)
    one_parts = one_steps.send(one_parts)
    d_heads, head_sums = run_attention_back(frames, frame_counts, d_proj, parts, attn_w)
    d_heads, two_parts = tie(d_heads, two_parts)
    two_parts = two_steps.send(two_parts)
    attn_steps = sum_blocks(
        lambda left: fast_dot("jtd,jte->jde", left, d_heads),
        lambda first, size: jnp.stack(
            [lax.dynamic_slice_in_dim(left, first, size, 1) for left in (attn_in,) * 3 + (mixed,)]
        ),
        width,
        group,
    )
    attn_parts = next(attn_steps)
    d_heads, attn_parts = tie(d_heads, attn_parts)
    attn_parts = attn_steps.send(attn_parts)
    d_heads, attn_parts, one_parts, two_parts = tie(d_heads, attn_parts, one_parts, two_parts)
    two_parts = two_steps.send(two_parts)
    one_parts = one_steps.send(one_parts)
    attn_parts = attn_steps.send(attn_parts)
    d_heads, attn_parts = tie(d_heads, attn_parts)
    attn_parts = attn_steps.send(attn_parts)
    input_grad, input_sums = run_input(d_heads, attn_w, mods, stream, d_resid)
    input_sums, one_parts, two_parts = tie(input_sums, one_parts, two_parts)
    whole_two = two_steps.send(two_parts)
    one_parts = one_steps.send(one_parts)
    input_sums, attn_parts, one_parts = tie(input_sums, attn_parts, one_parts)
    attn_parts = attn_steps.send(attn_parts)
    one_parts = one_steps.send(one_parts)

    d_mods = jnp.stack(
        [
            input_sums[:, 0],
            input_sums[:, 1],
            resid_sums[:, 2],
            resid_sums[:, 0],
            resid_sums[:, 1],
            d_gate_two[:, 0],
        ],
        axis=1,
    )
    head_sums = jnp.sum(head_sums, axis=0)
    grad_bias = jnp.concatenate(
        [
            jnp.sum(d_mods, axis=0),
            head_sums[0:1],
            head_sums[2:3],
            jnp.sum(resid_sums[:, 3], axis=0)[None],
            d_pre_sums[:, 0],
            jnp.sum(d_branch_sums, axis=0),
        ]
    )
    to_ranks = jnp.concatenate(
        [
            d_mods.reshape(clip_count, mod_count, ranks, col_part)
            .transpose(2, 0, 1, 3)
            .reshape(ranks, mod_size),
            grad_bias.reshape(dp_count, ranks, bias_part)
            .transpose(1, 0, 2)
            .reshape(ranks, bias_size),
        ],
        axis=1,
    )
    rank_sums = jnp.sum(lax.all_to_all(to_ranks, "fsdp", 0, 0, tiled=True), axis=0)
    rank_sums, attn_parts, one_parts = tie(rank_sums, attn_parts, one_parts)
    attn_parts = attn_steps.send(attn_parts)
    whole_one = one_steps.send(one_parts)
    to_rows = jnp.concatenate(
        [
            jnp.broadcast_to(rank_sums[None, :mod_size], (dp_count, mod_size)),
            rank_sums[mod_size:].reshape(dp_count, bias_part),
        ],
        axis=1,
    )
    from_rows = lax.all_to_all(to_rows, "dp", 0, 0, tiled=True)
    from_rows, attn_parts = tie(from_rows, attn_parts)
    attn_parts = attn_steps.send(attn_parts)
    bias_grad = jnp.sum(from_rows[:, mod_size:], axis=0)
    mod_grad_cols = from_rows[:, :mod_size].reshape(all_clips, mod_count, col_part)
    mod_grad = lax.all_gather(packed([mod_grad_cols], 8), "fsdp", axis=0, tiled=True)
    mod_grad = mod_grad.reshape(ranks, -1)[:, : mod_grad_cols.size]
    mod_grad = mod_grad.reshape(ranks, all_clips, mod_count, col_part).transpose(1, 2, 0, 3)
    mod_grad = mod_grad.reshape(all_clips, mod_count, width)

    mod_grad_rows = lax.dynamic_slice_in_dim(mod_grad, dp_at * row_part, row_part, 2)
    right_parts = jnp.einsum(
        "cjk,jke->cje", mod_grad_rows, right_roots[:mod_count], precision=precise
    )
    cond_wide = wide(cond_all)
    cond_row_wide = wide(cond_rows)
    mod_gram = jnp.einsum("cjk,bjk->jcb", mod_grad, mod_grad, precision=precise)
    cond_gram = jnp.einsum("ck,bk->cb", cond_wide, cond_wide, precision=precise)
    mod_side = jnp.einsum("jcb,be->jce", mod_gram, cond_cols, precision=precise)
    ada_left = jnp.einsum("cr,jce->jre", cond_row_wide, mod_side, precision=precise)
    cond_side = jnp.einsum("cb,bje->jce", cond_gram, mod_grad_cols, precision=precise)
    ada_right = jnp.einsum("cjr,jce->jre", mod_grad_rows, cond_side, precision=precise)

    products_two = owned_step(whole_two, left_rows[2], right_wholes[2], group)
    products_two, right_parts, attn_parts = tie(products_two, right_parts, attn_parts)
    whole_attn = attn_steps.send(attn_parts)
    back_two = shard_rows(products_two, group)
    products_one = owned_step(whole_one, left_rows[1], right_wholes[1], group)
    back_one = shard_rows(products_one, group)
    right_parts = lax.all_gather(packed([right_parts], 8), "dp", axis=0, tiled=True)
    mod_right = jnp.sum(right_parts.reshape(dp_count, -1), axis=0)[: mod_grad_cols.size]
    mod_right = mod_right.reshape(all_clips, mod_count, col_part)
    ada_pre = jnp.einsum("jrc,cje->jre", left_cond, mod_right, precision=precise)
    whole_attn, back_one, back_two, ada_pre, ada_left, ada_right = tie(
        whole_attn, back_one, back_two, ada_pre, ada_left, ada_right
    )
    back_attn = shard_rows(owned_step(whole_attn, left_rows[0], right_wholes[0], group), group)

    def joined(at, ada):
        return jnp.concatenate([ada, wide(back_attn[at]), wide(back_one[at]), wide(back_two[at])])

    precond = joined(0, ada_pre)
    left_new = stat_decay * left_stats + (1.0 - stat_decay) * joined(1, ada_left)
    right_new = stat_decay * right_stats + (1.0 - stat_decay) * joined(2, ada_right)
    momentum_new = moment_decay * momentum + precond
    weights_new = weights - weight_rate * momentum_new
    weights_copy = weights_new.astype(jnp.bfloat16)
    bias_second_new = stat_decay * bias_second + (1.0 - stat_decay) * bias_grad * bias_grad
    bias_moment_new = moment_decay * bias_moment + bias_grad * lax.rsqrt(
        bias_second_new + diag_epsilon
    )
    biases_new = biases - bias_rate * bias_moment_new
    return (
        block_out.reshape(tokens.shape),
        input_grad.reshape(tokens.shape),
        left_new,
        right_new,
        momentum_new,
        weights_new,
        weights_copy,
        bias_moment_new,
        bias_second_new,
        biases_new,
    )


def solution(mesh):
    placed = (
        P("dp", "fsdp", None, None),
        P("dp", None),
        P("dp"),
        P("dp", "fsdp", None, None),
        P(None, "dp", "fsdp"),
        P(("dp", "fsdp")),
        P(None, "dp", "fsdp"),
        P(None, "dp", "fsdp"),
        P(None, "dp", "fsdp"),
        P(None, "dp", "fsdp"),
        P(None, "dp", "fsdp"),
        P(("dp", "fsdp")),
        P(("dp", "fsdp")),
    )
    return jax.shard_map(
        per_device,
        mesh=mesh,
        in_specs=placed,
        out_specs=(
            P("dp", "fsdp", None, None),
            P("dp", "fsdp", None, None),
            P(None, "dp", "fsdp"),
            P(None, "dp", "fsdp"),
            P(None, "dp", "fsdp"),
            P(None, "dp", "fsdp"),
            P(None, "dp", "fsdp"),
            P(("dp", "fsdp")),
            P(("dp", "fsdp")),
            P(("dp", "fsdp")),
        ),
        check_vma=False,
    )
```

```python
import functools
import math

import jax
import jax.numpy as jnp
from jax import lax
from jax.experimental import pallas as pl
from jax.experimental.pallas import tpu as pltpu
from jax.sharding import PartitionSpec as P

HEADS = 16


precise = lax.Precision.HIGHEST
norm_epsilon = 1e-06
masked_score = -1e30
stat_decay = 0.5
moment_decay = 0.9
weight_rate = 0.7
bias_rate = 0.1
diag_epsilon = 1e-08
vmem_bytes = 50 * 2**20
little_cost = pl.CostEstimate(flops=1024, bytes_accessed=1024, transcendentals=0)


def narrow(array):
    return array.astype(jnp.bfloat16)


def wide(array):
    return array.astype(jnp.float32)


def spec(shape, index_map, **keywords):
    return pl.BlockSpec(shape, index_map, **keywords)


def held(shape):
    return pl.BlockSpec(shape, lambda step: (0,) * len(shape), pipeline_mode=pl.Buffered(1))


def column_cuts(total):
    cuts, at = [], 0
    while at < total:
        cuts.append((at, min(total, at + 256)))
        at += 256
    return cuts


def dot_nn(left, right):
    return lax.dot_general(left, right, (((1,), (0,)), ((), ())), preferred_element_type=jnp.float32)


def dot_nt(left, right):
    return lax.dot_general(left, right, (((1,), (1,)), ((), ())), preferred_element_type=jnp.float32)


def dot_tn(left, right):
    return lax.dot_general(left, right, (((0,), (0,)), ((), ())), preferred_element_type=jnp.float32)


def split_high(values):
    high = narrow(values)
    return high, narrow(values - wide(high))


def valid_rows(count, rows, frames):
    at = lax.broadcasted_iota(jnp.int32, (rows, 1), 0)
    return (lax.rem(at, frames) < count).astype(jnp.float32)


def score_offset(count, size, frames, key_axis):
    first = lax.broadcasted_iota(jnp.int32, (size, size), 0)
    second = lax.broadcasted_iota(jnp.int32, (size, size), 1)
    key = second if key_axis == 1 else first
    met = (lax.div(first, frames) == lax.div(second, frames)) & (lax.rem(key, frames) < count)
    return jnp.where(met, 0.0, masked_score)


def head_windows(width):
    size = width // HEADS
    windows = []
    for head in range(HEADS):
        low, high = head * size, (head + 1) * size
        start = low // 128 * 128
        stop = min(width, -(-high // 128) * 128)
        windows.append((low - start, high - start, start, stop))
    return windows


def lane_mask(low, high, count, dtype):
    lanes = lax.broadcasted_iota(jnp.int32, (1, count), 1)
    return ((lanes >= low) & (lanes < high)).astype(jnp.float32).astype(dtype)


def norm_parts(values):
    centered = values - jnp.mean(values, axis=-1, keepdims=True)
    variance = jnp.mean(centered * centered, axis=-1, keepdims=True)
    inverse = lax.rsqrt(variance + norm_epsilon)
    return centered * inverse, inverse


def norm_back(grad, normed, inverse):
    first = jnp.mean(grad, axis=-1, keepdims=True)
    second = jnp.mean(grad * normed, axis=-1, keepdims=True)
    return (grad - first - normed * second) * inverse


def column_sum(values):
    return jnp.sum(values, axis=0, keepdims=True)


def start_loads(cuts, at, parts, whole, semaphores, first_index=0):
    loads = []
    for index, (part, first, rows) in enumerate(cuts, first_index):
        span = pl.ds(pl.multiple_of(at[index] * 16, 16), rows)
        source = parts[part].at[pl.ds(first, rows)]
        loads.append(pltpu.make_async_copy(source, whole.at[span], semaphores.at[index]))
        loads[-1].start()
    return loads


def attention_kernel(
    frames,
    counts,
    tokens,
    cotangent,
    mods,
    bias,
    blocks,
    attn_in,
    parts,
    mixed_low,
    proj_out,
    resid_out,
    mlp_in,
    d_branch,
    d_branch_sum,
    mixed,
    whole,
    semaphores,
):
    rows, width = tokens.shape
    clip = pl.program_id(0)
    loads = [
        pltpu.make_async_copy(blocks.at[at], whole.at[at], semaphores.at[at]) for at in range(4)
    ]

    @pl.when(clip == 0)
    def _():
        for load in loads:
            load.start()

    tile = min(rows, 128)
    count = counts[clip]
    shift_one, scale_one, gate_one = (mods[0, at : at + 1, :] for at in range(3))
    shift_two, scale_two, gate_two = (mods[0, at : at + 1, :] for at in range(3, 6))
    for first in range(0, rows, tile):
        span = slice(first, first + tile)
        normed, _ = norm_parts(wide(tokens[span]))
        attn_in[span] = narrow(normed * (1.0 + scale_one) + shift_one)
        branch_back = narrow(wide(cotangent[span]) * valid_rows(count, tile, frames) * gate_two)
        d_branch[span] = branch_back
        part_sum = column_sum(wide(branch_back))
        d_branch_sum[0] = part_sum if first == 0 else d_branch_sum[0] + part_sum

    @pl.when(clip == 0)
    def _():
        for load in loads:
            load.wait()

    scale = (width // HEADS) ** -0.5
    source = attn_in[...]
    for low, high in column_cuts(width):
        span = slice(low, high)
        query = (dot_nn(source, whole[0, :, span]) + bias[0:1, span]) * scale
        parts[0, :, span], parts[1, :, span] = split_high(query)
        parts[2, :, span], parts[3, :, span] = split_high(dot_nn(source, whole[1, :, span]))
        parts[4, :, span] = narrow(dot_nn(source, whole[2, :, span]) + bias[2:3, span])
    offset = score_offset(count, tile, frames, 1)
    mixed[...] = jnp.zeros_like(mixed)
    for first in range(0, rows, tile):
        span = slice(first, first + tile)
        for low, high, start, stop in head_windows(width):
            lanes = slice(start, stop)
            mask = lane_mask(low, high, stop - start, jnp.bfloat16)
            key_high = parts[2, span, lanes]
            query_high = parts[0, span, lanes] * mask
            scores = dot_nt(query_high, key_high)
            scores += dot_nt(parts[1, span, lanes] * mask, key_high)
            scores += dot_nt(query_high, parts[3, span, lanes]) + offset
            expons = jnp.exp(scores - jnp.max(scores, axis=-1, keepdims=True))
            probs = expons * (1.0 / jnp.sum(expons, axis=-1, keepdims=True))
            out = dot_nn(narrow(probs), parts[4, span, lanes] * mask)
            mixed[span, lanes] += out
    mixed_low[...] = narrow(mixed[...])
    source = mixed_low[...]
    for low, high in column_cuts(width):
        span = slice(low, high)
        proj_out[:, span] = dot_nn(source, whole[3, :, span]) + bias[3:4, span]
    for first in range(0, rows, tile):
        span = slice(first, first + tile)
        resid = wide(tokens[span]) + valid_rows(count, tile, frames) * gate_one * proj_out[span]
        resid_out[span] = resid
        normed, _ = norm_parts(resid)
        mlp_in[span] = narrow(normed * (1.0 + scale_two) + shift_two)


def run_attention(frames, counts, tokens, cotangent, mods, bias, blocks):
    total, width = tokens.shape
    clips = mods.shape[0]
    rows = total // clips
    clip_rows = spec((rows, width), lambda clip: (clip, 0))
    low = jax.ShapeDtypeStruct((total, width), jnp.bfloat16)
    full = jax.ShapeDtypeStruct((total, width), jnp.float32)
    return pl.pallas_call(
        functools.partial(attention_kernel, frames),
        grid=(clips,),
        in_specs=[
            pl.BlockSpec(memory_space=pltpu.SMEM),
            clip_rows,
            clip_rows,
            spec((1,) + mods.shape[1:], lambda clip: (clip, 0, 0)),
            held(bias.shape),
            pl.BlockSpec(memory_space=pl.ANY),
        ],
        out_specs=[
            clip_rows,
            spec((5, rows, width), lambda clip: (0, clip, 0)),
            clip_rows,
            clip_rows,
            clip_rows,
            clip_rows,
            clip_rows,
            spec((1, 1, width), lambda clip: (clip, 0, 0)),
        ],
        out_shape=[
            low,
            jax.ShapeDtypeStruct((5, total, width), jnp.bfloat16),
            low,
            full,
            full,
            low,
            low,
            jax.ShapeDtypeStruct((clips, 1, width), jnp.float32),
        ],
        scratch_shapes=[
            pltpu.VMEM((rows, width), jnp.float32),
            pltpu.VMEM(blocks.shape, jnp.bfloat16),
            pltpu.SemaphoreType.DMA((4,)),
        ],
        compiler_params=pltpu.CompilerParams(vmem_limit_bytes=vmem_bytes),
        cost_estimate=little_cost,
    )(counts, tokens, cotangent, mods, bias, blocks)


def stacked(numbers):
    return jnp.stack([jnp.asarray(number, jnp.int32) for number in numbers])


def start_loads(cuts, at, parts, whole, semaphores):
    for index, (part, first, rows) in enumerate(cuts):
        span = pl.ds(pl.multiple_of(at[index] * 16, 16), rows)
        source = parts[part].at[pl.ds(first, rows)]
        pltpu.make_async_copy(source, whole.at[span], semaphores.at[index]).start()


def wait_loads(groups, at, parts, whole, semaphores):
    index = 0
    for step, cuts in enumerate(groups):
        base = index
        index += len(cuts)

        @pl.when(pl.program_id(0) == step)
        def _(cuts=cuts, base=base):
            for offset, (part, first, rows) in enumerate(cuts):
                span = pl.ds(pl.multiple_of(at[base + offset] * 16, 16), rows)
                source = parts[part].at[pl.ds(first, rows)]
                semaphore = semaphores.at[base + offset]
                pltpu.make_async_copy(source, whole.at[span], semaphore).wait()


def hidden_kernel(cuts, order, starts, mlp_in, bias, *refs):
    whole_out, hidden, slope, whole, semaphores, store_semaphores = refs[-6:]
    pieces = refs[:-6]
    step, steps = pl.program_id(0), pl.num_programs(0)
    width = mlp_in.shape[-1]
    span = pl.ds(pl.multiple_of(order[step] * width, width), width)

    @pl.when(step == 0)
    def _():
        start_loads([cut for group in cuts for cut in group], starts, pieces, whole, semaphores)

    wait_loads(cuts, starts, pieces, whole, semaphores)
    pltpu.make_async_copy(whole.at[span], whole_out.at[span], store_semaphores.at[step]).start()
    root = (2.0 / math.pi) ** 0.5
    source = mlp_in[...]
    block = whole.at[span]
    for low, high in column_cuts(width):
        lanes = slice(low, high)
        pre = dot_nn(source, block[:, lanes]) + bias[0, :, lanes]
        square = pre * pre
        bent = jnp.tanh(root * pre * (1.0 + 0.044715 * square))
        half = 0.5 + 0.5 * bent
        hidden[0, :, lanes] = narrow(pre * half)
        steep = (0.5 * root) * pre * (1.0 + 3 * 0.044715 * square)
        slope[0, :, lanes] = narrow(half + steep * (1.0 - bent * bent))

    @pl.when(step == steps - 1)
    def _():
        for at in range(len(cuts)):
            rows = pl.ds(pl.multiple_of(order[at] * width, width), width)
            pltpu.make_async_copy(
                whole.at[rows], whole_out.at[rows], store_semaphores.at[at]
            ).wait()


def run_hidden(mlp_in, gathered, bias):
    pieces, cuts, starts, order = gathered
    total, width = mlp_in.shape
    count = len(cuts)
    per_block = pl.BlockSpec((1, total, width), lambda at, order, starts: (order[at], 0, 0))
    out = jax.ShapeDtypeStruct((count, total, width), jnp.bfloat16)
    return pl.pallas_call(
        functools.partial(hidden_kernel, cuts),
        grid_spec=pltpu.PrefetchScalarGridSpec(
            num_scalar_prefetch=2,
            grid=(count,),
            in_specs=[
                pl.BlockSpec((total, width), lambda at, order, starts: (0, 0)),
                pl.BlockSpec((1, 1, width), lambda at, order, starts: (order[at], 0, 0)),
            ]
            + [pl.BlockSpec(memory_space=pl.ANY)] * len(pieces),
            out_specs=[pl.BlockSpec(memory_space=pl.ANY), per_block, per_block],
            scratch_shapes=[
                pltpu.VMEM((count * width, width), jnp.bfloat16),
                pltpu.SemaphoreType.DMA((len(starts),)),
                pltpu.SemaphoreType.DMA((count,)),
            ],
        ),
        out_shape=[jax.ShapeDtypeStruct((count * width, width), jnp.bfloat16), out, out],
        compiler_params=pltpu.CompilerParams(vmem_limit_bytes=vmem_bytes),
        cost_estimate=little_cost,
    )(stacked(order), stacked(starts), mlp_in, bias, *pieces)


def branch_kernel(
    frames,
    cuts,
    order,
    starts,
    counts,
    hidden,
    slope,
    d_branch,
    bias,
    gates,
    resid,
    cotangent,
    *refs,
):
    d_pre, d_pre_sum, block_out, d_gate, branch, whole, semaphores = refs[-7:]
    pieces = refs[:-7]
    step, steps = pl.program_id(0), pl.num_programs(0)
    total, width = resid.shape
    clips = gates.shape[0]
    rows = total // clips
    source, back = hidden[0], d_branch[...]

    @pl.when(step == 0)
    def _():
        start_loads([cut for group in cuts for cut in group], starts, pieces, whole, semaphores)
        branch[...] = jnp.zeros_like(branch)

    wait_loads(cuts, starts, pieces, whole, semaphores)
    block = whole.at[pl.ds(pl.multiple_of(order[step] * width, width), width)]
    for low, high in column_cuts(width):
        span = slice(low, high)
        d_hidden = dot_nt(back, block[span, :])
        low_back = narrow(d_hidden * wide(slope[0, :, span]))
        d_pre[0, :, span] = low_back
        d_pre_sum[0, :, span] = column_sum(wide(low_back))
        branch[:, span] += dot_nn(source, block[:, span])

    @pl.when(step == steps - 1)
    def _():
        for clip in range(clips):
            span = slice(clip * rows, (clip + 1) * rows)
            kept = valid_rows(counts[clip], rows, frames) * (branch[span] + bias[...])
            block_out[span] = narrow(resid[span] + gates[clip] * kept)
            d_gate[clip] = column_sum(wide(cotangent[span]) * kept)


def run_branch(frames, counts, hidden, slope, gathered, d_branch, bias, gates, resid, cotangent):
    pieces, cuts, starts, order = gathered
    count, total, width = hidden.shape
    clips = gates.shape[0]

    def all_of(*shape):
        return pl.BlockSpec(shape, lambda at, order, starts: (0,) * len(shape))

    per_block = pl.BlockSpec((1, total, width), lambda at, order, starts: (order[at], 0, 0))
    low = jax.ShapeDtypeStruct((total, width), jnp.bfloat16)
    return pl.pallas_call(
        functools.partial(branch_kernel, frames, cuts),
        grid_spec=pltpu.PrefetchScalarGridSpec(
            num_scalar_prefetch=2,
            grid=(count,),
            in_specs=[
                pl.BlockSpec(memory_space=pltpu.SMEM),
                per_block,
                per_block,
                all_of(total, width),
                all_of(*bias.shape),
                all_of(*gates.shape),
                all_of(total, width),
                all_of(total, width),
            ]
            + [pl.BlockSpec(memory_space=pl.ANY)] * len(pieces),
            out_specs=[
                per_block,
                pl.BlockSpec((1, 1, width), lambda at, order, starts: (order[at], 0, 0)),
                all_of(total, width),
                all_of(clips, 1, width),
            ],
            scratch_shapes=[
                pltpu.VMEM((total, width), jnp.float32),
                pltpu.VMEM((count * width, width), jnp.bfloat16),
                pltpu.SemaphoreType.DMA((len(starts),)),
            ],
        ),
        out_shape=[
            jax.ShapeDtypeStruct((count, total, width), jnp.bfloat16),
            jax.ShapeDtypeStruct((count, 1, width), jnp.float32),
            low,
            jax.ShapeDtypeStruct((clips, 1, width), jnp.float32),
        ],
        compiler_params=pltpu.CompilerParams(vmem_limit_bytes=vmem_bytes),
        cost_estimate=little_cost,
    )(stacked(order), stacked(starts), counts, hidden, slope, d_branch, bias, gates, resid, cotangent, *pieces)


def resid_kernel(
    frames,
    counts,
    d_pre,
    block,
    mods,
    resid,
    cotangent,
    proj,
    d_resid_out,
    d_proj,
    sums,
    total_grad,
):
    step, steps = pl.program_id(0), pl.num_programs(0)
    total, width = resid.shape
    clips = mods.shape[0]
    rows = total // clips
    tile = min(rows, 128)
    source = d_pre[0]

    @pl.when(step == 0)
    def _():
        total_grad[...] = jnp.zeros_like(total_grad)

    for low, high in column_cuts(width):
        span = slice(low, high)
        total_grad[:, span] += dot_nt(source, block[0, span, :])

    @pl.when(step == steps - 1)
    def _():
        for clip in range(clips):
            gate_one, scale_two = mods[clip, 2:3, :], mods[clip, 4:5, :]
            found = [0.0] * 4
            for first in range(clip * rows, (clip + 1) * rows, tile):
                span = slice(first, first + tile)
                grad = total_grad[span]
                normed, inverse = norm_parts(resid[span])
                back = norm_back(grad * (1.0 + scale_two), normed, inverse)
                d_resid = wide(cotangent[span]) + back
                d_resid_out[span] = d_resid
                kept = valid_rows(counts[clip], tile, frames) * d_resid
                low_back = narrow(kept * gate_one)
                d_proj[span] = low_back
                terms = (grad, grad * normed, kept * proj[span], wide(low_back))
                found = [old + column_sum(term) for old, term in zip(found, terms)]
            for at in range(4):
                sums[clip, at : at + 1, :] = found[at]


def run_resid(frames, counts, d_pre, blocks, mods, resid, cotangent, proj):
    count, total, width = d_pre.shape
    clips = mods.shape[0]
    return pl.pallas_call(
        functools.partial(resid_kernel, frames),
        grid=(count,),
        in_specs=[
            pl.BlockSpec(memory_space=pltpu.SMEM),
            spec((1, total, width), lambda at: (at, 0, 0)),
            spec((1, width, width), lambda at: (at, 0, 0)),
            held(mods.shape),
            held((total, width)),
            held((total, width)),
            held((total, width)),
        ],
        out_specs=[held((total, width)), held((total, width)), held((clips, 4, width))],
        out_shape=[
            jax.ShapeDtypeStruct((total, width), jnp.float32),
            jax.ShapeDtypeStruct((total, width), jnp.bfloat16),
            jax.ShapeDtypeStruct((clips, 4, width), jnp.float32),
        ],
        scratch_shapes=[pltpu.VMEM((total, width), jnp.float32)],
        compiler_params=pltpu.CompilerParams(vmem_limit_bytes=vmem_bytes),
        cost_estimate=little_cost,
    )(counts, d_pre, blocks, mods, resid, cotangent, proj)


def attention_back_kernel(
    frames, counts, d_proj, parts, block, d_qkv, sums, d_mixed, d_query, d_key, d_value
):
    rows, width = d_proj.shape
    tile = min(rows, 128)
    count = counts[pl.program_id(0)]
    source = d_proj[...]
    for low, high in column_cuts(width):
        d_mixed[:, low:high] = narrow(dot_nt(source, block[0, low:high, :]))
    scale = (width // HEADS) ** -0.5
    offset = score_offset(count, tile, frames, 0)
    for ref in (d_query, d_key, d_value):
        ref[...] = jnp.zeros_like(ref)
    for first in range(0, rows, tile):
        span = slice(first, first + tile)
        for low, high, start, stop in head_windows(width):
            lanes = slice(start, stop)
            mask = lane_mask(low, high, stop - start, jnp.bfloat16)
            query_high = parts[0, span, lanes] * mask
            key_high = parts[2, span, lanes] * mask
            back = d_mixed[span, lanes] * mask
            scores = dot_nt(key_high, query_high)
            scores += dot_nt(key_high, parts[1, span, lanes])
            scores += dot_nt(parts[3, span, lanes], query_high) + offset
            expons = jnp.exp(scores - jnp.max(scores, axis=0, keepdims=True))
            probs = expons * (1.0 / jnp.sum(expons, axis=0, keepdims=True))
            d_probs = dot_nt(parts[4, span, lanes], back)
            inner = jnp.sum(d_probs * probs, axis=0, keepdims=True)
            d_scores = narrow(probs * (d_probs - inner))
            d_value[span, lanes] += dot_nn(narrow(probs), back)
            d_key[span, lanes] += dot_nn(d_scores, query_high)
            d_query[span, lanes] += dot_tn(d_scores, key_high)
    for at, ref in enumerate((d_query, d_key, d_value)):
        low_back = narrow(ref[...] * scale) if at == 0 else narrow(ref[...])
        d_qkv[at] = low_back
        sums[0, at : at + 1, :] = column_sum(wide(low_back))
    d_qkv[3] = source


def run_attention_back(frames, counts, d_proj, parts, block):
    total, width = d_proj.shape
    clips = counts.shape[0]
    rows = total // clips
    return pl.pallas_call(
        functools.partial(attention_back_kernel, frames),
        grid=(clips,),
        in_specs=[
            pl.BlockSpec(memory_space=pltpu.SMEM),
            spec((rows, width), lambda clip: (clip, 0)),
            spec((5, rows, width), lambda clip: (0, clip, 0)),
            spec((1, width, width), lambda clip: (3, 0, 0), pipeline_mode=pl.Buffered(1)),
        ],
        out_specs=[
            spec((4, rows, width), lambda clip: (0, clip, 0)),
            spec((1, 3, width), lambda clip: (clip, 0, 0)),
        ],
        out_shape=[
            jax.ShapeDtypeStruct((4, total, width), jnp.bfloat16),
            jax.ShapeDtypeStruct((clips, 3, width), jnp.float32),
        ],
        scratch_shapes=[pltpu.VMEM((rows, width), jnp.bfloat16)]
        + [pltpu.VMEM((rows, width), jnp.float32)] * 3,
        compiler_params=pltpu.CompilerParams(vmem_limit_bytes=vmem_bytes),
        cost_estimate=little_cost,
    )(counts, d_proj, parts, block)


def input_kernel(d_qkv, block, mods, tokens, d_resid, input_grad, sums, total_grad):
    step, steps = pl.program_id(0), pl.num_programs(0)
    total, width = tokens.shape
    clips = mods.shape[0]
    rows = total // clips
    tile = min(rows, 128)
    source = d_qkv[0]

    @pl.when(step == 0)
    def _():
        total_grad[...] = jnp.zeros_like(total_grad)

    for low, high in column_cuts(width):
        span = slice(low, high)
        total_grad[:, span] += dot_nt(source, block[0, span, :])

    @pl.when(step == steps - 1)
    def _():
        for clip in range(clips):
            scale_one = mods[clip, 1:2, :]
            found = [0.0] * 2
            for first in range(clip * rows, (clip + 1) * rows, tile):
                span = slice(first, first + tile)
                grad = total_grad[span]
                normed, inverse = norm_parts(wide(tokens[span]))
                back = norm_back(grad * (1.0 + scale_one), normed, inverse)
                input_grad[span] = narrow(d_resid[span] + back)
                terms = (grad, grad * normed)
                found = [old + column_sum(term) for old, term in zip(found, terms)]
            for at in range(2):
                sums[clip, at : at + 1, :] = found[at]


def run_input(d_qkv, blocks, mods, tokens, d_resid):
    total, width = tokens.shape
    clips = mods.shape[0]
    return pl.pallas_call(
        input_kernel,
        grid=(3,),
        in_specs=[
            spec((1, total, width), lambda at: (at, 0, 0)),
            spec((1, width, width), lambda at: (at, 0, 0)),
            held(mods.shape),
            held((total, width)),
            held((total, width)),
        ],
        out_specs=[held((total, width)), held((clips, 2, width))],
        out_shape=[
            jax.ShapeDtypeStruct((total, width), jnp.bfloat16),
            jax.ShapeDtypeStruct((clips, 2, width), jnp.float32),
        ],
        scratch_shapes=[pltpu.VMEM((total, width), jnp.float32)],
        compiler_params=pltpu.CompilerParams(vmem_limit_bytes=vmem_bytes),
        cost_estimate=little_cost,
    )(d_qkv, blocks, mods, tokens, d_resid)


def tie(*values):
    return lax.optimization_barrier(values)


def packed(arrays, tile):
    flat = jnp.concatenate([array.reshape(-1) for array in arrays])
    return jnp.pad(flat, (0, -flat.shape[0] % (tile * 128))).reshape(-1, 128)


def core_swap(array):
    count = lax.axis_size("dp")
    return lax.ppermute(array, "dp", [(at, at ^ 1) for at in range(count)])


def chip_shift(array, step):
    count = lax.axis_size("dp")
    return lax.ppermute(array, "dp", [(at, (at + 2 * step) % count) for at in range(count)])


def chip_swap(array, bits):
    count = lax.axis_size("dp")
    return lax.ppermute(array, "dp", [(at, at ^ (2 * bits)) for at in range(count)])


def rank_swap(array, bits):
    count = lax.axis_size("fsdp")
    return lax.ppermute(array, "fsdp", [(at, at ^ bits) for at in range(count)])


def entry(array, at, axis=0):
    return lax.dynamic_index_in_dim(array, at, axis, keepdims=False)


def place_kernel(cuts, at, *refs):
    parts, whole, held_rows, semaphores = refs[:-3], refs[-3], refs[-2], refs[-1]
    spans, loads, stores = [], [], []
    for index, (part, first, rows) in enumerate(cuts):
        spans.append(pl.ds(pl.multiple_of(at[index] * 16, 16), rows))
        source = parts[part].at[pl.ds(first, rows)]
        loads.append(
            pltpu.make_async_copy(source, held_rows.at[spans[index]], semaphores.at[0, index])
        )
        loads[index].start()
    for index, span in enumerate(spans):
        loads[index].wait()
        stores.append(
            pltpu.make_async_copy(held_rows.at[span], whole.at[span], semaphores.at[1, index])
        )
        stores[index].start()
    for store in stores:
        store.wait()


def place(parts, cuts, starts, rows):
    width = parts[0].shape[-1]
    dtype = parts[0].dtype
    return pl.pallas_call(
        functools.partial(place_kernel, cuts),
        in_specs=[pl.BlockSpec(memory_space=pltpu.SMEM)]
        + [pl.BlockSpec(memory_space=pl.ANY)] * len(parts),
        out_specs=pl.BlockSpec(memory_space=pl.ANY),
        out_shape=jax.ShapeDtypeStruct((rows, width), dtype),
        scratch_shapes=[
            pltpu.VMEM((rows, width), dtype),
            pltpu.SemaphoreType.DMA((2, len(cuts))),
        ],
        compiler_params=pltpu.CompilerParams(vmem_limit_bytes=vmem_bytes),
        cost_estimate=little_cost,
    )(stacked(starts), *parts)


def own_rows(parts, group):
    ranks, at = lax.axis_size("fsdp"), lax.axis_index("fsdp")
    shares = ranks // group
    count, _, row_part, col_part = parts.shape
    chunk = row_part // shares
    split = parts.reshape(count, group, shares, chunk, col_part).transpose(1, 2, 0, 3, 4)
    split = split.reshape(ranks, count, chunk, col_part)
    if shares > 1:
        moved = lax.all_to_all(split, "fsdp", 0, 0, tiled=True)
        (moved,) = yield (moved,)
        yield moved.transpose(1, 2, 0, 3).reshape(count, chunk, ranks * col_part)
        return
    panels = [entry(split, at)]
    panels += [rank_swap(entry(split, at ^ bits), bits) for bits in range(1, ranks)]
    panels = yield tuple(panels)
    placed = [
        lax.select_n(at, *[panels[panel ^ index] for index in range(ranks)])
        for panel in range(ranks)
    ]
    yield jnp.concatenate(placed, axis=2)


def shard_rows(split, group):
    ranks, count, chunk, col_part = split.shape
    shares = ranks // group
    moved = lax.all_to_all(split, "fsdp", 0, 0, tiled=True)
    moved = moved.reshape(group, shares, count, chunk, col_part).transpose(2, 0, 1, 3, 4)
    return moved.reshape(count, group, shares * chunk, col_part)


def gather_blocks(rows, group):
    ranks, dp_count = lax.axis_size("fsdp"), lax.axis_size("dp")
    shares = ranks // group
    chunk, total = rows.shape
    all_rows = lax.all_gather(rows, ("fsdp", "dp"), axis=0, tiled=True)
    if shares > 1:
        all_rows = all_rows.reshape(group, shares, dp_count, chunk, total).transpose(0, 2, 1, 3, 4)
    return all_rows.reshape(group, total, total)


def join_line(found):
    chips, chip = lax.axis_size("dp") // 2, lax.axis_index("dp") // 2
    chunk = found[0].shape[0]
    starts = [(chip - step) % chips * (chunk // 16) for step in range(chips)]
    return place(found, [(step, 0, chunk) for step in range(chips)], starts, chips * chunk)


def gather_second(rows, group):
    ranks, at = lax.axis_size("fsdp"), lax.axis_index("fsdp")
    total = rows.shape[-1]
    if ranks != group:
        blocks = gather_blocks(rows, group).reshape(group * total, total)
        for _ in range(3):
            (blocks,) = yield (blocks,)
        cuts = [[(0, index * total, total)] for index in range(group)]
        yield [blocks], cuts, [index * (total // 16) for index in range(group)], range(group)
        return
    chips = lax.axis_size("dp") // 2
    core = lax.axis_index("dp") % 2
    chunk, half = rows.shape[0], total // 2
    others = yield tuple(chip_shift(rows, step) for step in range(1, chips))
    line = join_line([rows, *others])
    cuts = [(side, step * chunk, chunk) for side in range(2) for step in range(chips)]
    starts = [
        (2 * step + side) * (chunk // 16) for side in (core, 1 - core) for step in range(chips)
    ]
    (own,) = yield (place([line, core_swap(line)], cuts, starts, total),)
    share = lax.dynamic_slice_in_dim(own, core * half, half, 0)
    mine = yield tuple(rank_swap(share, bits) for bits in range(1, ranks))
    parts, cuts, starts = [own], [[(0, 0, total)]], [at * (total // 16)]
    for bits in range(1, ranks):
        parts += [mine[bits - 1], core_swap(mine[bits - 1])]
        cuts.append([(2 * bits - 1, 0, half), (2 * bits, 0, half)])
        starts += [((at ^ bits) * 2 + side) * (half // 16) for side in (core, 1 - core)]
    yield parts, cuts, starts, [at ^ bits for bits in range(ranks)]


def gather_own(rows, group):
    ranks = lax.axis_size("fsdp")
    shares = ranks // group
    if shares > 1:
        sets = [[share + shares * block for share in range(shares)] for block in range(group)]
        rows = lax.all_gather(rows, "fsdp", axis=1, tiled=True, axis_index_groups=sets)
    return lax.all_gather(rows, "dp", axis=1, tiled=True)


def sum_blocks(product, cut, total, group):
    ranks, dp_count = lax.axis_size("fsdp"), lax.axis_size("dp")
    shares = ranks // group
    if shares > 1:
        blocks = narrow(product(cut(0, total)))
        chunk = total // (dp_count * shares)
        blocks = blocks.reshape(group, dp_count, shares, chunk, -1).transpose(0, 2, 1, 3, 4)
        rows = lax.psum_scatter(
            blocks.reshape(group * total, -1), ("fsdp", "dp"), scatter_dimension=0, tiled=True
        )
        for _ in range(7):
            (rows,) = yield (rows,)
        yield gather_own(rows[None], group)[0]
        return
    chips, half = dp_count // 2, total // 2
    chunk = half // chips
    core, chip = lax.axis_index("dp") % 2, lax.axis_index("dp") // 2
    low_bit, high_bit = lax.axis_index("fsdp") % 2, lax.axis_index("fsdp") // 2
    (away,) = yield (narrow(product(cut((1 - core) * half, half))),)
    (away_in,) = yield (core_swap(away),)
    here = product(cut(core * half, half))
    here = narrow(here + wide(away_in))
    here = here.reshape(2, 2, chips, chunk, -1)
    middle = chips // 2
    first, second = here[:, :, :middle], here[:, :, middle:]
    first_out, second_out = yield (entry(first, 1 - low_bit, 1), entry(second, 1 - high_bit, 0))
    first_in, second_in = yield (rank_swap(first_out, 1), rank_swap(second_out, 2))
    first = narrow(wide(entry(first, low_bit, 1)) + wide(first_in))
    second = narrow(wide(entry(second, high_bit, 0)) + wide(second_in))
    first_in = rank_swap(entry(first, 1 - high_bit), 2)
    second_in = rank_swap(entry(second, 1 - low_bit), 1)
    first_in, second_in = yield (first_in, second_in)
    first = narrow(wide(entry(first, high_bit)) + wide(first_in))
    second = narrow(wide(entry(second, low_bit)) + wide(second_in))
    line = jnp.concatenate([first, second])
    step = 1
    while step < chips:
        bit = chip // step % 2
        line = line.reshape(-1, 2, *line.shape[1:])
        (line_in,) = yield (chip_swap(entry(line, 1 - bit, 1), step),)
        line = narrow(wide(entry(line, bit, 1)) + wide(line_in))
        step *= 2
    yield lax.all_gather(line[0], "dp", axis=0, tiled=True)


def fast_dot(subscripts, left, right):
    return jnp.einsum(subscripts, left, right, preferred_element_type=jnp.float32)


def products_kernel(chips, at, gathered, left_root, right_root, out, whole, semaphores):
    chunk, width = left_root.shape
    ranks = out.shape[0]
    copies = []
    for index in range(2 * chips):
        first = (index % 2 * chips + index // 2) * chunk
        copies.append(
            pltpu.make_async_copy(
                gathered.at[pl.ds(index * chunk, chunk)],
                whole.at[pl.ds(first, chunk)],
                semaphores.at[index],
            )
        )
        copies[-1].start()
    for copy in copies:
        copy.wait()
    first = at[0] * 16
    grad = whole[...]
    picked = lax.broadcasted_iota(jnp.int32, (width, chunk), 0) - first
    picked = picked == lax.broadcasted_iota(jnp.int32, (width, chunk), 1)
    own_columns = narrow(dot_nn(grad, narrow(picked.astype(jnp.float32))))
    side_high, side_low = split_high(dot_nn(left_root[...], grad))
    right = right_root[...]
    precond = dot_nn(side_high, right) + dot_nn(side_low, right)
    outer = dot_nt(whole[pl.ds(pl.multiple_of(first, 16), chunk), :], grad)
    inner = dot_tn(own_columns, grad)
    for at_out, product in enumerate((precond, outer, inner)):
        low = narrow(product)
        for rank in range(ranks):
            span = slice(rank * (width // ranks), (rank + 1) * (width // ranks))
            out[rank, at_out] = low[:, span]


def owned_step(whole, left_root, right_root, group):
    ranks, dp_count = lax.axis_size("fsdp"), lax.axis_size("dp")
    shares = ranks // group
    chunk, total = left_root.shape
    col_part = total // ranks
    first = lax.axis_index("dp") * (chunk * shares) + lax.axis_index("fsdp") % shares * chunk
    if shares == 1:
        return pl.pallas_call(
            functools.partial(products_kernel, dp_count // 2),
            in_specs=[
                pl.BlockSpec(memory_space=pltpu.SMEM),
                pl.BlockSpec(memory_space=pl.ANY),
                pl.BlockSpec(memory_space=pltpu.VMEM),
                pl.BlockSpec(memory_space=pltpu.VMEM),
            ],
            out_specs=pl.BlockSpec(memory_space=pltpu.VMEM),
            out_shape=jax.ShapeDtypeStruct((ranks, 3, chunk, col_part), jnp.bfloat16),
            scratch_shapes=[
                pltpu.VMEM((total, total), jnp.bfloat16),
                pltpu.SemaphoreType.DMA((dp_count,)),
            ],
            compiler_params=pltpu.CompilerParams(vmem_limit_bytes=vmem_bytes),
            cost_estimate=little_cost,
        )((first // 16)[None], whole, left_root, right_root)
    grad_rows = lax.dynamic_slice_in_dim(whole, first, chunk, 0)
    own_columns = lax.dynamic_slice_in_dim(whole, first, chunk, 1)
    outer = fast_dot("rk,jk->rj", grad_rows, whole)
    inner = fast_dot("kr,kj->rj", own_columns, whole)
    side_high, side_low = split_high(fast_dot("rk,kj->rj", left_root, whole))
    precond = fast_dot("rk,kj->rj", side_high, right_root) + fast_dot(
        "rk,kj->rj", side_low, right_root
    )
    products = narrow(jnp.stack([precond, outer, inner]))
    return products.reshape(3, chunk, ranks, col_part).transpose(2, 0, 1, 3)


def per_device(
    tokens,
    conditioning,
    frame_counts,
    cotangent,
    weights,
    biases,
    momentum,
    left_stats,
    right_stats,
    left_roots,
    right_roots,
    bias_moment,
    bias_second,
):
    group = 4
    mod_count = 6
    clip_count, pos_count, frames, width = tokens.shape
    token_count = clip_count * pos_count * frames
    block_count, row_part, col_part = weights.shape
    dp_count, ranks = lax.axis_size("dp"), lax.axis_size("fsdp")
    dp_at, rank_at = lax.axis_index("dp"), lax.axis_index("fsdp")
    all_clips = clip_count * dp_count
    bias_part = biases.shape[0]
    stream = tokens.reshape(token_count, width)
    grad_out = cotangent.reshape(token_count, width)
    low_weights = narrow(weights).reshape(block_count, row_part, col_part)
    shards = low_weights[mod_count:].reshape(-1, group, row_part, col_part)

    weight_rows = own_rows(shards, group)
    weight_panels = next(weight_rows)
    cond_low = narrow(jax.nn.silu(conditioning))
    first_parts = lax.all_gather(packed([cond_low, narrow(biases)], 16), "dp", axis=0, tiled=True)
    weight_panels, first_parts = tie(weight_panels, first_parts)
    attn_rows, one_rows, two_rows = weight_rows.send(weight_panels)
    attn_w = gather_blocks(attn_rows, group)

    first_parts = first_parts.reshape(dp_count, -1)
    cond_all = first_parts[:, : clip_count * width].reshape(all_clips, width)
    bias_rows = wide(first_parts[:, clip_count * width : clip_count * width + bias_part])
    cond_rows = lax.dynamic_slice_in_dim(cond_all, dp_at * row_part, row_part, 1)
    cond_cols = wide(lax.dynamic_slice_in_dim(cond_all, rank_at * col_part, col_part, 1))
    mod_parts = fast_dot("cr,jre->cje", cond_rows, low_weights[:mod_count])
    mod_parts = lax.all_to_all(mod_parts, "dp", 0, 0, tiled=True)
    mod_parts, one_rows = tie(mod_parts, one_rows)
    one_steps = gather_second(one_rows, group)
    one_parts = next(one_steps)
    mod_cols = jnp.sum(mod_parts.reshape(dp_count, clip_count, mod_count, col_part), axis=0)
    left_cond = jnp.einsum("jrk,ck->jrc", left_roots[:mod_count], cond_cols, precision=precise)
    mod_size, bias_size = mod_cols.size, dp_count * bias_part
    second_parts = lax.all_gather(
        packed([mod_cols, bias_rows, left_cond], 8), "fsdp", axis=0, tiled=True
    )
    second_parts, one_parts, two_rows = tie(second_parts, one_parts, two_rows)
    two_steps = gather_second(two_rows, group)
    two_parts = next(two_steps)
    one_parts = one_steps.send(one_steps.send(one_parts))
    two_parts = two_steps.send(two_parts)
    second_parts = second_parts.reshape(ranks, -1)
    mods = second_parts[:, :mod_size].reshape(ranks, clip_count, mod_count, col_part)
    mods = mods.transpose(1, 2, 0, 3).reshape(clip_count, mod_count, width)
    bias_all = second_parts[:, mod_size : mod_size + bias_size].reshape(ranks, dp_count, bias_part)
    bias_all = bias_all.transpose(1, 0, 2).reshape(-1, width)
    left_size = mod_size + bias_size + left_cond.size
    left_cond = jnp.sum(second_parts[:, mod_size + bias_size : left_size], axis=0)
    left_cond = left_cond.reshape(mod_count, row_part, all_clips)
    mods = mods + bias_all[:mod_count]
    bias_table = jnp.concatenate(
        [bias_all[6:7], jnp.zeros((1, width), jnp.float32), bias_all[7:14]]
    )

    roots = jnp.stack([narrow(left_roots[mod_count:]), narrow(right_roots[mod_count:])])
    mods, roots, two_parts = tie(mods, roots, two_parts)
    two_parts = two_steps.send(two_parts)
    root_rows = own_rows(roots.reshape(-1, group, row_part, col_part), group)
    root_panels = next(root_rows)
    attn_in, parts, mixed, proj, resid, mlp_in, d_branch, d_branch_sums = run_attention(
        frames, frame_counts, stream, grad_out, mods, bias_table, attn_w
    )
    mlp_in, one_parts = tie(mlp_in, one_parts)
    one_w, hidden, slope = run_hidden(mlp_in, one_steps.send(one_parts), bias_table[4:8, None])
    one_w = one_w.reshape(group, width, width)

    weight_steps, two_w_parts = two_steps, two_parts
    two_steps = sum_blocks(
        lambda left: fast_dot("jtd,te->jde", left, d_branch),
        lambda first, size: lax.dynamic_slice_in_dim(hidden, first, size, 2),
        width,
        group,
    )
    two_parts = next(two_steps)
    hidden, two_parts, root_panels = tie(hidden, two_parts, root_panels)
    two_parts = two_steps.send(two_parts)
    root_rows = root_rows.send(root_panels)
    gathered = weight_steps.send(two_w_parts)
    hidden, root_rows = tie(hidden, root_rows)
    left_rows, right_rows = jnp.split(root_rows, 2)
    right_wholes = [gather_own(rows[None], group)[0] for rows in right_rows]
    d_pre, d_pre_sums, block_out, d_gate_two = run_branch(
        frames,
        frame_counts,
        hidden,
        slope,
        gathered,
        d_branch,
        bias_table[8:9],
        mods[:, 5:6],
        resid,
        grad_out,
    )
    d_pre, two_parts = tie(d_pre, two_parts)
    two_parts = two_steps.send(two_parts)
    d_pre, two_parts = tie(d_pre, two_parts)
    two_parts = two_steps.send(two_parts)
    one_steps = sum_blocks(
        lambda left: fast_dot("td,jte->jde", left, d_pre),
        lambda first, size: lax.dynamic_slice_in_dim(mlp_in, first, size, 1),
        width,
        group,
    )
    one_parts = next(one_steps)
    d_pre, one_parts = tie(d_pre, one_parts)
    one_parts = one_steps.send(one_parts)
    d_resid, d_proj, resid_sums = run_resid(
        frames, frame_counts, d_pre, one_w, mods, resid, grad_out, proj
    )
    d_proj, one_parts, two_parts, right_wholes[2] = tie(
        d_proj, one_parts, two_parts, right_wholes[2]
    )
    two_parts = two_steps.send(two_parts)
    one_parts = one_steps.send(one_parts)
    d_proj, one_parts = tie(d_proj, one_parts)
    one_parts = one_steps.send(one_parts)
    d_heads, head_sums = run_attention_back(frames, frame_counts, d_proj, parts, attn_w)
    d_heads, two_parts, right_wholes[1] = tie(d_heads, two_parts, right_wholes[1])
    two_parts = two_steps.send(two_parts)
    attn_steps = sum_blocks(
        lambda left: fast_dot("jtd,jte->jde", left, d_heads),
        lambda first, size: jnp.stack(
            [lax.dynamic_slice_in_dim(left, first, size, 1) for left in (attn_in,) * 3 + (mixed,)]
        ),
        width,
        group,
    )
    attn_parts = next(attn_steps)
    d_heads, attn_parts = tie(d_heads, attn_parts)
    attn_parts = attn_steps.send(attn_parts)
    d_heads, attn_parts, one_parts, two_parts = tie(d_heads, attn_parts, one_parts, two_parts)
    two_parts = two_steps.send(two_parts)
    one_parts = one_steps.send(one_parts)
    attn_parts = attn_steps.send(attn_parts)
    d_heads, attn_parts = tie(d_heads, attn_parts)
    attn_parts = attn_steps.send(attn_parts)
    input_grad, input_sums = run_input(d_heads, attn_w, mods, stream, d_resid)
    input_sums, one_parts, two_parts, right_wholes[0] = tie(
        input_sums, one_parts, two_parts, right_wholes[0]
    )
    whole_two = two_steps.send(two_parts)
    one_parts = one_steps.send(one_parts)
    input_sums, attn_parts, one_parts = tie(input_sums, attn_parts, one_parts)
    attn_parts = attn_steps.send(attn_parts)
    one_parts = one_steps.send(one_parts)

    d_mods = jnp.stack(
        [
            input_sums[:, 0],
            input_sums[:, 1],
            resid_sums[:, 2],
            resid_sums[:, 0],
            resid_sums[:, 1],
            d_gate_two[:, 0],
        ],
        axis=1,
    )
    head_sums = jnp.sum(head_sums, axis=0)
    grad_bias = jnp.concatenate(
        [
            jnp.sum(d_mods, axis=0),
            head_sums[0:1],
            head_sums[2:3],
            jnp.sum(resid_sums[:, 3], axis=0)[None],
            d_pre_sums[:, 0],
            jnp.sum(d_branch_sums, axis=0),
        ]
    )
    to_ranks = jnp.concatenate(
        [
            d_mods.reshape(clip_count, mod_count, ranks, col_part)
            .transpose(2, 0, 1, 3)
            .reshape(ranks, mod_size),
            grad_bias.reshape(dp_count, ranks, bias_part)
            .transpose(1, 0, 2)
            .reshape(ranks, bias_size),
        ],
        axis=1,
    )
    rank_sums = jnp.sum(lax.all_to_all(to_ranks, "fsdp", 0, 0, tiled=True), axis=0)
    rank_sums, attn_parts, one_parts = tie(rank_sums, attn_parts, one_parts)
    attn_parts = attn_steps.send(attn_parts)
    whole_one = one_steps.send(one_parts)
    to_rows = jnp.concatenate(
        [
            jnp.broadcast_to(rank_sums[None, :mod_size], (dp_count, mod_size)),
            rank_sums[mod_size:].reshape(dp_count, bias_part),
        ],
        axis=1,
    )
    from_rows = lax.all_to_all(to_rows, "dp", 0, 0, tiled=True)
    from_rows, attn_parts = tie(from_rows, attn_parts)
    attn_parts = attn_steps.send(attn_parts)
    bias_grad = jnp.sum(from_rows[:, mod_size:], axis=0)
    mod_grad_cols = from_rows[:, :mod_size].reshape(all_clips, mod_count, col_part)
    mod_grad = lax.all_gather(packed([mod_grad_cols], 8), "fsdp", axis=0, tiled=True)
    mod_grad = mod_grad.reshape(ranks, -1)[:, : mod_grad_cols.size]
    mod_grad = mod_grad.reshape(ranks, all_clips, mod_count, col_part).transpose(1, 2, 0, 3)
    mod_grad = mod_grad.reshape(all_clips, mod_count, width)

    mod_grad_rows = lax.dynamic_slice_in_dim(mod_grad, dp_at * row_part, row_part, 2)
    right_parts = jnp.einsum(
        "cjk,jke->cje", mod_grad_rows, right_roots[:mod_count], precision=precise
    )
    cond_wide = wide(cond_all)
    cond_row_wide = wide(cond_rows)
    mod_gram = jnp.einsum("cjk,bjk->jcb", mod_grad, mod_grad, precision=precise)
    cond_gram = jnp.einsum("ck,bk->cb", cond_wide, cond_wide, precision=precise)
    mod_side = jnp.einsum("jcb,be->jce", mod_gram, cond_cols, precision=precise)
    ada_left = jnp.einsum("cr,jce->jre", cond_row_wide, mod_side, precision=precise)
    cond_side = jnp.einsum("cb,bje->jce", cond_gram, mod_grad_cols, precision=precise)
    ada_right = jnp.einsum("cjr,jce->jre", mod_grad_rows, cond_side, precision=precise)

    products_two = owned_step(whole_two, left_rows[2], right_wholes[2], group)
    products_two, right_parts, attn_parts = tie(products_two, right_parts, attn_parts)
    whole_attn = attn_steps.send(attn_parts)
    back_two = shard_rows(products_two, group)
    products_one = owned_step(whole_one, left_rows[1], right_wholes[1], group)
    back_one = shard_rows(products_one, group)
    right_parts = lax.all_gather(packed([right_parts], 8), "dp", axis=0, tiled=True)
    mod_right = jnp.sum(right_parts.reshape(dp_count, -1), axis=0)[: mod_grad_cols.size]
    mod_right = mod_right.reshape(all_clips, mod_count, col_part)
    ada_pre = jnp.einsum("jrc,cje->jre", left_cond, mod_right, precision=precise)
    whole_attn, back_one, back_two, ada_pre, ada_left, ada_right = tie(
        whole_attn, back_one, back_two, ada_pre, ada_left, ada_right
    )
    back_attn = shard_rows(owned_step(whole_attn, left_rows[0], right_wholes[0], group), group)

    def joined(at, ada):
        return jnp.concatenate([ada, wide(back_attn[at]), wide(back_one[at]), wide(back_two[at])])

    precond = joined(0, ada_pre)
    left_new = stat_decay * left_stats + (1.0 - stat_decay) * joined(1, ada_left)
    right_new = stat_decay * right_stats + (1.0 - stat_decay) * joined(2, ada_right)
    momentum_new = moment_decay * momentum + precond
    weights_new = weights - weight_rate * momentum_new
    weights_copy = weights_new.astype(jnp.bfloat16)
    bias_second_new = stat_decay * bias_second + (1.0 - stat_decay) * bias_grad * bias_grad
    bias_moment_new = moment_decay * bias_moment + bias_grad * lax.rsqrt(
        bias_second_new + diag_epsilon
    )
    biases_new = biases - bias_rate * bias_moment_new
    return (
        block_out.reshape(tokens.shape),
        input_grad.reshape(tokens.shape),
        left_new,
        right_new,
        momentum_new,
        weights_new,
        weights_copy,
        bias_moment_new,
        bias_second_new,
        biases_new,
    )


def solution(mesh):
    placed = (
        P("dp", "fsdp", None, None),
        P("dp", None),
        P("dp"),
        P("dp", "fsdp", None, None),
        P(None, "dp", "fsdp"),
        P(("dp", "fsdp")),
        P(None, "dp", "fsdp"),
        P(None, "dp", "fsdp"),
        P(None, "dp", "fsdp"),
        P(None, "dp", "fsdp"),
        P(None, "dp", "fsdp"),
        P(("dp", "fsdp")),
        P(("dp", "fsdp")),
    )
    return jax.shard_map(
        per_device,
        mesh=mesh,
        in_specs=placed,
        out_specs=(
            P("dp", "fsdp", None, None),
            P("dp", "fsdp", None, None),
            P(None, "dp", "fsdp"),
            P(None, "dp", "fsdp"),
            P(None, "dp", "fsdp"),
            P(None, "dp", "fsdp"),
            P(None, "dp", "fsdp"),
            P(("dp", "fsdp")),
            P(("dp", "fsdp")),
            P(("dp", "fsdp")),
        ),
        check_vma=False,
    )
```

```python
import functools
import math

import jax
import jax.numpy as jnp
from jax import lax
from jax.experimental import pallas as pl
from jax.experimental.pallas import tpu as pltpu
from jax.sharding import PartitionSpec as P

HEADS = 16


precise = lax.Precision.HIGHEST
norm_epsilon = 1e-06
masked_score = -1e30
stat_decay = 0.5
moment_decay = 0.9
weight_rate = 0.7
bias_rate = 0.1
diag_epsilon = 1e-08
vmem_bytes = 50 * 2**20
little_cost = pl.CostEstimate(flops=1024, bytes_accessed=1024, transcendentals=0)


def narrow(array):
    return array.astype(jnp.bfloat16)


def wide(array):
    return array.astype(jnp.float32)


def spec(shape, index_map, **keywords):
    return pl.BlockSpec(shape, index_map, **keywords)


def held(shape):
    return pl.BlockSpec(shape, lambda step: (0,) * len(shape), pipeline_mode=pl.Buffered(1))


def column_cuts(total):
    cuts, at = [], 0
    while at < total:
        cuts.append((at, min(total, at + 256)))
        at += 256
    return cuts


def dot_nn(left, right):
    return lax.dot_general(left, right, (((1,), (0,)), ((), ())), preferred_element_type=jnp.float32)


def dot_nt(left, right):
    return lax.dot_general(left, right, (((1,), (1,)), ((), ())), preferred_element_type=jnp.float32)


def dot_tn(left, right):
    return lax.dot_general(left, right, (((0,), (0,)), ((), ())), preferred_element_type=jnp.float32)


def split_high(values):
    high = narrow(values)
    return high, narrow(values - wide(high))


def valid_rows(count, rows, frames):
    at = lax.broadcasted_iota(jnp.int32, (rows, 1), 0)
    return (lax.rem(at, frames) < count).astype(jnp.float32)


def score_offset(count, size, frames, key_axis):
    first = lax.broadcasted_iota(jnp.int32, (size, size), 0)
    second = lax.broadcasted_iota(jnp.int32, (size, size), 1)
    key = second if key_axis == 1 else first
    met = (lax.div(first, frames) == lax.div(second, frames)) & (lax.rem(key, frames) < count)
    return jnp.where(met, 0.0, masked_score)


def head_windows(width):
    size = width // HEADS
    windows = []
    for head in range(HEADS):
        low, high = head * size, (head + 1) * size
        start = low // 128 * 128
        stop = min(width, -(-high // 128) * 128)
        windows.append((low - start, high - start, start, stop))
    return windows


def lane_mask(low, high, count, dtype):
    lanes = lax.broadcasted_iota(jnp.int32, (1, count), 1)
    return ((lanes >= low) & (lanes < high)).astype(jnp.float32).astype(dtype)


def norm_parts(values):
    centered = values - jnp.mean(values, axis=-1, keepdims=True)
    variance = jnp.mean(centered * centered, axis=-1, keepdims=True)
    inverse = lax.rsqrt(variance + norm_epsilon)
    return centered * inverse, inverse


def norm_back(grad, normed, inverse):
    first = jnp.mean(grad, axis=-1, keepdims=True)
    second = jnp.mean(grad * normed, axis=-1, keepdims=True)
    return (grad - first - normed * second) * inverse


def column_sum(values):
    return jnp.sum(values, axis=0, keepdims=True)


def start_loads(cuts, at, parts, whole, semaphores, first_index=0):
    loads = []
    for index, (part, first, rows) in enumerate(cuts, first_index):
        span = pl.ds(pl.multiple_of(at[index] * 16, 16), rows)
        source = parts[part].at[pl.ds(first, rows)]
        loads.append(pltpu.make_async_copy(source, whole.at[span], semaphores.at[index]))
        loads[-1].start()
    return loads


def attention_kernel(
    frames,
    cuts,
    counts,
    starts,
    tokens,
    cotangent,
    mods,
    bias,
    *refs,
):
    whole_out, attn_in, parts, mixed_low, proj_out, resid_out, mlp_in = refs[-13:-6]
    d_branch, d_branch_sum, mixed, whole, semaphores, store_semaphore = refs[-6:]
    pieces = refs[:-13]
    rows, width = tokens.shape
    clip, clips = pl.program_id(0), pl.num_programs(0)
    store = pltpu.make_async_copy(whole, whole_out, store_semaphore)

    @pl.when(clip == 0)
    def _():
        start_loads(cuts, starts, pieces, whole, semaphores)

    tile = min(rows, 128)
    count = counts[clip]
    shift_one, scale_one, gate_one = (mods[0, at : at + 1, :] for at in range(3))
    shift_two, scale_two, gate_two = (mods[0, at : at + 1, :] for at in range(3, 6))
    for first in range(0, rows, tile):
        span = slice(first, first + tile)
        normed, _ = norm_parts(wide(tokens[span]))
        attn_in[span] = narrow(normed * (1.0 + scale_one) + shift_one)
        branch_back = narrow(wide(cotangent[span]) * valid_rows(count, tile, frames) * gate_two)
        d_branch[span] = branch_back
        part_sum = column_sum(wide(branch_back))
        d_branch_sum[0] = part_sum if first == 0 else d_branch_sum[0] + part_sum

    wait_loads([cuts], starts, pieces, whole, semaphores)

    @pl.when(clip == 0)
    def _():
        store.start()

    scale = (width // HEADS) ** -0.5
    source = attn_in[...]
    for low, high in column_cuts(width):
        span = slice(low, high)
        query = (dot_nn(source, whole[0 * width : 1 * width, span]) + bias[0:1, span]) * scale
        parts[0, :, span], parts[1, :, span] = split_high(query)
        parts[2, :, span], parts[3, :, span] = split_high(dot_nn(source, whole[1 * width : 2 * width, span]))
        parts[4, :, span] = narrow(dot_nn(source, whole[2 * width : 3 * width, span]) + bias[2:3, span])
    offset = score_offset(count, tile, frames, 1)
    mixed[...] = jnp.zeros_like(mixed)
    for first in range(0, rows, tile):
        span = slice(first, first + tile)
        for low, high, start, stop in head_windows(width):
            lanes = slice(start, stop)
            mask = lane_mask(low, high, stop - start, jnp.bfloat16)
            key_high = parts[2, span, lanes]
            query_high = parts[0, span, lanes] * mask
            scores = dot_nt(query_high, key_high)
            scores += dot_nt(parts[1, span, lanes] * mask, key_high)
            scores += dot_nt(query_high, parts[3, span, lanes]) + offset
            expons = jnp.exp(scores - jnp.max(scores, axis=-1, keepdims=True))
            probs = expons * (1.0 / jnp.sum(expons, axis=-1, keepdims=True))
            out = dot_nn(narrow(probs), parts[4, span, lanes] * mask)
            mixed[span, lanes] += out
    mixed_low[...] = narrow(mixed[...])
    source = mixed_low[...]
    for low, high in column_cuts(width):
        span = slice(low, high)
        proj_out[:, span] = dot_nn(source, whole[3 * width : 4 * width, span]) + bias[3:4, span]
    for first in range(0, rows, tile):
        span = slice(first, first + tile)
        resid = wide(tokens[span]) + valid_rows(count, tile, frames) * gate_one * proj_out[span]
        resid_out[span] = resid
        normed, _ = norm_parts(resid)
        mlp_in[span] = narrow(normed * (1.0 + scale_two) + shift_two)

    @pl.when(clip == clips - 1)
    def _():
        store.wait()


def run_attention(frames, counts, tokens, cotangent, mods, bias, gathered):
    pieces, cuts, starts = gathered
    total, width = tokens.shape
    clips = mods.shape[0]
    rows = total // clips
    clip_rows = spec((rows, width), lambda clip: (clip, 0))
    low = jax.ShapeDtypeStruct((total, width), jnp.bfloat16)
    full = jax.ShapeDtypeStruct((total, width), jnp.float32)
    return pl.pallas_call(
        functools.partial(attention_kernel, frames, cuts),
        grid=(clips,),
        in_specs=[
            pl.BlockSpec(memory_space=pltpu.SMEM),
            pl.BlockSpec(memory_space=pltpu.SMEM),
            clip_rows,
            clip_rows,
            spec((1,) + mods.shape[1:], lambda clip: (clip, 0, 0)),
            held(bias.shape),
        ]
        + [pl.BlockSpec(memory_space=pl.ANY)] * len(pieces),
        out_specs=[
            pl.BlockSpec(memory_space=pl.ANY),
            clip_rows,
            spec((5, rows, width), lambda clip: (0, clip, 0)),
            clip_rows,
            clip_rows,
            clip_rows,
            clip_rows,
            clip_rows,
            spec((1, 1, width), lambda clip: (clip, 0, 0)),
        ],
        out_shape=[
            jax.ShapeDtypeStruct((4 * width, width), jnp.bfloat16),
            low,
            jax.ShapeDtypeStruct((5, total, width), jnp.bfloat16),
            low,
            full,
            full,
            low,
            low,
            jax.ShapeDtypeStruct((clips, 1, width), jnp.float32),
        ],
        scratch_shapes=[
            pltpu.VMEM((rows, width), jnp.float32),
            pltpu.VMEM((4 * width, width), jnp.bfloat16),
            pltpu.SemaphoreType.DMA((len(cuts),)),
            pltpu.SemaphoreType.DMA,
        ],
        compiler_params=pltpu.CompilerParams(vmem_limit_bytes=vmem_bytes),
        cost_estimate=little_cost,
    )(counts, stacked(starts), tokens, cotangent, mods, bias, *pieces)


def stacked(numbers):
    return jnp.stack([jnp.asarray(number, jnp.int32) for number in numbers])


def start_loads(cuts, at, parts, whole, semaphores):
    for index, (part, first, rows) in enumerate(cuts):
        span = pl.ds(pl.multiple_of(at[index] * 16, 16), rows)
        source = parts[part].at[pl.ds(first, rows)]
        pltpu.make_async_copy(source, whole.at[span], semaphores.at[index]).start()


def wait_loads(groups, at, parts, whole, semaphores):
    index = 0
    for step, cuts in enumerate(groups):
        base = index
        index += len(cuts)

        @pl.when(pl.program_id(0) == step)
        def _(cuts=cuts, base=base):
            for offset, (part, first, rows) in enumerate(cuts):
                span = pl.ds(pl.multiple_of(at[base + offset] * 16, 16), rows)
                source = parts[part].at[pl.ds(first, rows)]
                semaphore = semaphores.at[base + offset]
                pltpu.make_async_copy(source, whole.at[span], semaphore).wait()


def hidden_kernel(cuts, order, starts, mlp_in, bias, *refs):
    whole_out, hidden, slope, whole, semaphores, store_semaphores = refs[-6:]
    pieces = refs[:-6]
    step, steps = pl.program_id(0), pl.num_programs(0)
    width = mlp_in.shape[-1]
    span = pl.ds(pl.multiple_of(order[step] * width, width), width)

    @pl.when(step == 0)
    def _():
        start_loads([cut for group in cuts for cut in group], starts, pieces, whole, semaphores)

    wait_loads(cuts, starts, pieces, whole, semaphores)
    pltpu.make_async_copy(whole.at[span], whole_out.at[span], store_semaphores.at[step]).start()
    root = (2.0 / math.pi) ** 0.5
    source = mlp_in[...]
    block = whole.at[span]
    for low, high in column_cuts(width):
        lanes = slice(low, high)
        pre = dot_nn(source, block[:, lanes]) + bias[0, :, lanes]
        square = pre * pre
        bent = jnp.tanh(root * pre * (1.0 + 0.044715 * square))
        half = 0.5 + 0.5 * bent
        hidden[0, :, lanes] = narrow(pre * half)
        steep = (0.5 * root) * pre * (1.0 + 3 * 0.044715 * square)
        slope[0, :, lanes] = narrow(half + steep * (1.0 - bent * bent))

    @pl.when(step == steps - 1)
    def _():
        for at in range(len(cuts)):
            rows = pl.ds(pl.multiple_of(order[at] * width, width), width)
            pltpu.make_async_copy(
                whole.at[rows], whole_out.at[rows], store_semaphores.at[at]
            ).wait()


def run_hidden(mlp_in, gathered, bias):
    pieces, cuts, starts, order = gathered
    total, width = mlp_in.shape
    count = len(cuts)
    per_block = pl.BlockSpec((1, total, width), lambda at, order, starts: (order[at], 0, 0))
    out = jax.ShapeDtypeStruct((count, total, width), jnp.bfloat16)
    return pl.pallas_call(
        functools.partial(hidden_kernel, cuts),
        grid_spec=pltpu.PrefetchScalarGridSpec(
            num_scalar_prefetch=2,
            grid=(count,),
            in_specs=[
                pl.BlockSpec((total, width), lambda at, order, starts: (0, 0)),
                pl.BlockSpec((1, 1, width), lambda at, order, starts: (order[at], 0, 0)),
            ]
            + [pl.BlockSpec(memory_space=pl.ANY)] * len(pieces),
            out_specs=[pl.BlockSpec(memory_space=pl.ANY), per_block, per_block],
            scratch_shapes=[
                pltpu.VMEM((count * width, width), jnp.bfloat16),
                pltpu.SemaphoreType.DMA((len(starts),)),
                pltpu.SemaphoreType.DMA((count,)),
            ],
        ),
        out_shape=[jax.ShapeDtypeStruct((count * width, width), jnp.bfloat16), out, out],
        compiler_params=pltpu.CompilerParams(vmem_limit_bytes=vmem_bytes),
        cost_estimate=little_cost,
    )(stacked(order), stacked(starts), mlp_in, bias, *pieces)


def branch_kernel(
    frames,
    cuts,
    order,
    starts,
    counts,
    hidden,
    slope,
    d_branch,
    bias,
    gates,
    resid,
    cotangent,
    *refs,
):
    d_pre, d_pre_sum, block_out, d_gate, branch, whole, semaphores = refs[-7:]
    pieces = refs[:-7]
    step, steps = pl.program_id(0), pl.num_programs(0)
    total, width = resid.shape
    clips = gates.shape[0]
    rows = total // clips
    source, back = hidden[0], d_branch[...]

    @pl.when(step == 0)
    def _():
        start_loads([cut for group in cuts for cut in group], starts, pieces, whole, semaphores)
        branch[...] = jnp.zeros_like(branch)

    wait_loads(cuts, starts, pieces, whole, semaphores)
    block = whole.at[pl.ds(pl.multiple_of(order[step] * width, width), width)]
    for low, high in column_cuts(width):
        span = slice(low, high)
        d_hidden = dot_nt(back, block[span, :])
        low_back = narrow(d_hidden * wide(slope[0, :, span]))
        d_pre[0, :, span] = low_back
        d_pre_sum[0, :, span] = column_sum(wide(low_back))
        branch[:, span] += dot_nn(source, block[:, span])

    @pl.when(step == steps - 1)
    def _():
        for clip in range(clips):
            span = slice(clip * rows, (clip + 1) * rows)
            kept = valid_rows(counts[clip], rows, frames) * (branch[span] + bias[...])
            block_out[span] = narrow(resid[span] + gates[clip] * kept)
            d_gate[clip] = column_sum(wide(cotangent[span]) * kept)


def run_branch(frames, counts, hidden, slope, gathered, d_branch, bias, gates, resid, cotangent):
    pieces, cuts, starts, order = gathered
    count, total, width = hidden.shape
    clips = gates.shape[0]

    def all_of(*shape):
        return pl.BlockSpec(shape, lambda at, order, starts: (0,) * len(shape))

    per_block = pl.BlockSpec((1, total, width), lambda at, order, starts: (order[at], 0, 0))
    low = jax.ShapeDtypeStruct((total, width), jnp.bfloat16)
    return pl.pallas_call(
        functools.partial(branch_kernel, frames, cuts),
        grid_spec=pltpu.PrefetchScalarGridSpec(
            num_scalar_prefetch=2,
            grid=(count,),
            in_specs=[
                pl.BlockSpec(memory_space=pltpu.SMEM),
                per_block,
                per_block,
                all_of(total, width),
                all_of(*bias.shape),
                all_of(*gates.shape),
                all_of(total, width),
                all_of(total, width),
            ]
            + [pl.BlockSpec(memory_space=pl.ANY)] * len(pieces),
            out_specs=[
                per_block,
                pl.BlockSpec((1, 1, width), lambda at, order, starts: (order[at], 0, 0)),
                all_of(total, width),
                all_of(clips, 1, width),
            ],
            scratch_shapes=[
                pltpu.VMEM((total, width), jnp.float32),
                pltpu.VMEM((count * width, width), jnp.bfloat16),
                pltpu.SemaphoreType.DMA((len(starts),)),
            ],
        ),
        out_shape=[
            jax.ShapeDtypeStruct((count, total, width), jnp.bfloat16),
            jax.ShapeDtypeStruct((count, 1, width), jnp.float32),
            low,
            jax.ShapeDtypeStruct((clips, 1, width), jnp.float32),
        ],
        compiler_params=pltpu.CompilerParams(vmem_limit_bytes=vmem_bytes),
        cost_estimate=little_cost,
    )(stacked(order), stacked(starts), counts, hidden, slope, d_branch, bias, gates, resid, cotangent, *pieces)


def resid_kernel(
    frames,
    counts,
    d_pre,
    block,
    mods,
    resid,
    cotangent,
    proj,
    d_resid_out,
    d_proj,
    sums,
    total_grad,
):
    step, steps = pl.program_id(0), pl.num_programs(0)
    total, width = resid.shape
    clips = mods.shape[0]
    rows = total // clips
    tile = min(rows, 128)
    source = d_pre[0]

    @pl.when(step == 0)
    def _():
        total_grad[...] = jnp.zeros_like(total_grad)

    for low, high in column_cuts(width):
        span = slice(low, high)
        total_grad[:, span] += dot_nt(source, block[0, span, :])

    @pl.when(step == steps - 1)
    def _():
        for clip in range(clips):
            gate_one, scale_two = mods[clip, 2:3, :], mods[clip, 4:5, :]
            found = [0.0] * 4
            for first in range(clip * rows, (clip + 1) * rows, tile):
                span = slice(first, first + tile)
                grad = total_grad[span]
                normed, inverse = norm_parts(resid[span])
                back = norm_back(grad * (1.0 + scale_two), normed, inverse)
                d_resid = wide(cotangent[span]) + back
                d_resid_out[span] = d_resid
                kept = valid_rows(counts[clip], tile, frames) * d_resid
                low_back = narrow(kept * gate_one)
                d_proj[span] = low_back
                terms = (grad, grad * normed, kept * proj[span], wide(low_back))
                found = [old + column_sum(term) for old, term in zip(found, terms)]
            for at in range(4):
                sums[clip, at : at + 1, :] = found[at]


def run_resid(frames, counts, d_pre, blocks, mods, resid, cotangent, proj):
    count, total, width = d_pre.shape
    clips = mods.shape[0]
    return pl.pallas_call(
        functools.partial(resid_kernel, frames),
        grid=(count,),
        in_specs=[
            pl.BlockSpec(memory_space=pltpu.SMEM),
            spec((1, total, width), lambda at: (at, 0, 0)),
            spec((1, width, width), lambda at: (at, 0, 0)),
            held(mods.shape),
            held((total, width)),
            held((total, width)),
            held((total, width)),
        ],
        out_specs=[held((total, width)), held((total, width)), held((clips, 4, width))],
        out_shape=[
            jax.ShapeDtypeStruct((total, width), jnp.float32),
            jax.ShapeDtypeStruct((total, width), jnp.bfloat16),
            jax.ShapeDtypeStruct((clips, 4, width), jnp.float32),
        ],
        scratch_shapes=[pltpu.VMEM((total, width), jnp.float32)],
        compiler_params=pltpu.CompilerParams(vmem_limit_bytes=vmem_bytes),
        cost_estimate=little_cost,
    )(counts, d_pre, blocks, mods, resid, cotangent, proj)


def attention_back_kernel(
    frames, counts, d_proj, parts, block, d_qkv, sums, d_mixed, d_query, d_key, d_value
):
    rows, width = d_proj.shape
    tile = min(rows, 128)
    count = counts[pl.program_id(0)]
    source = d_proj[...]
    for low, high in column_cuts(width):
        d_mixed[:, low:high] = narrow(dot_nt(source, block[0, low:high, :]))
    scale = (width // HEADS) ** -0.5
    offset = score_offset(count, tile, frames, 0)
    for ref in (d_query, d_key, d_value):
        ref[...] = jnp.zeros_like(ref)
    for first in range(0, rows, tile):
        span = slice(first, first + tile)
        for low, high, start, stop in head_windows(width):
            lanes = slice(start, stop)
            mask = lane_mask(low, high, stop - start, jnp.bfloat16)
            query_high = parts[0, span, lanes] * mask
            key_high = parts[2, span, lanes] * mask
            back = d_mixed[span, lanes] * mask
            scores = dot_nt(key_high, query_high)
            scores += dot_nt(key_high, parts[1, span, lanes])
            scores += dot_nt(parts[3, span, lanes], query_high) + offset
            expons = jnp.exp(scores - jnp.max(scores, axis=0, keepdims=True))
            probs = expons * (1.0 / jnp.sum(expons, axis=0, keepdims=True))
            d_probs = dot_nt(parts[4, span, lanes], back)
            inner = jnp.sum(d_probs * probs, axis=0, keepdims=True)
            d_scores = narrow(probs * (d_probs - inner))
            d_value[span, lanes] += dot_nn(narrow(probs), back)
            d_key[span, lanes] += dot_nn(d_scores, query_high)
            d_query[span, lanes] += dot_tn(d_scores, key_high)
    for at, ref in enumerate((d_query, d_key, d_value)):
        low_back = narrow(ref[...] * scale) if at == 0 else narrow(ref[...])
        d_qkv[at] = low_back
        sums[0, at : at + 1, :] = column_sum(wide(low_back))
    d_qkv[3] = source


def run_attention_back(frames, counts, d_proj, parts, block):
    total, width = d_proj.shape
    clips = counts.shape[0]
    rows = total // clips
    return pl.pallas_call(
        functools.partial(attention_back_kernel, frames),
        grid=(clips,),
        in_specs=[
            pl.BlockSpec(memory_space=pltpu.SMEM),
            spec((rows, width), lambda clip: (clip, 0)),
            spec((5, rows, width), lambda clip: (0, clip, 0)),
            spec((1, width, width), lambda clip: (3, 0, 0), pipeline_mode=pl.Buffered(1)),
        ],
        out_specs=[
            spec((4, rows, width), lambda clip: (0, clip, 0)),
            spec((1, 3, width), lambda clip: (clip, 0, 0)),
        ],
        out_shape=[
            jax.ShapeDtypeStruct((4, total, width), jnp.bfloat16),
            jax.ShapeDtypeStruct((clips, 3, width), jnp.float32),
        ],
        scratch_shapes=[pltpu.VMEM((rows, width), jnp.bfloat16)]
        + [pltpu.VMEM((rows, width), jnp.float32)] * 3,
        compiler_params=pltpu.CompilerParams(vmem_limit_bytes=vmem_bytes),
        cost_estimate=little_cost,
    )(counts, d_proj, parts, block)


def input_kernel(d_qkv, block, mods, tokens, d_resid, input_grad, sums, total_grad):
    step, steps = pl.program_id(0), pl.num_programs(0)
    total, width = tokens.shape
    clips = mods.shape[0]
    rows = total // clips
    tile = min(rows, 128)
    source = d_qkv[0]

    @pl.when(step == 0)
    def _():
        total_grad[...] = jnp.zeros_like(total_grad)

    for low, high in column_cuts(width):
        span = slice(low, high)
        total_grad[:, span] += dot_nt(source, block[0, span, :])

    @pl.when(step == steps - 1)
    def _():
        for clip in range(clips):
            scale_one = mods[clip, 1:2, :]
            found = [0.0] * 2
            for first in range(clip * rows, (clip + 1) * rows, tile):
                span = slice(first, first + tile)
                grad = total_grad[span]
                normed, inverse = norm_parts(wide(tokens[span]))
                back = norm_back(grad * (1.0 + scale_one), normed, inverse)
                input_grad[span] = narrow(d_resid[span] + back)
                terms = (grad, grad * normed)
                found = [old + column_sum(term) for old, term in zip(found, terms)]
            for at in range(2):
                sums[clip, at : at + 1, :] = found[at]


def run_input(d_qkv, blocks, mods, tokens, d_resid):
    total, width = tokens.shape
    clips = mods.shape[0]
    return pl.pallas_call(
        input_kernel,
        grid=(3,),
        in_specs=[
            spec((1, total, width), lambda at: (at, 0, 0)),
            spec((1, width, width), lambda at: (at, 0, 0)),
            held(mods.shape),
            held((total, width)),
            held((total, width)),
        ],
        out_specs=[held((total, width)), held((clips, 2, width))],
        out_shape=[
            jax.ShapeDtypeStruct((total, width), jnp.bfloat16),
            jax.ShapeDtypeStruct((clips, 2, width), jnp.float32),
        ],
        scratch_shapes=[pltpu.VMEM((total, width), jnp.float32)],
        compiler_params=pltpu.CompilerParams(vmem_limit_bytes=vmem_bytes),
        cost_estimate=little_cost,
    )(d_qkv, blocks, mods, tokens, d_resid)


def tie(*values):
    return lax.optimization_barrier(values)


def packed(arrays, tile):
    flat = jnp.concatenate([array.reshape(-1) for array in arrays])
    return jnp.pad(flat, (0, -flat.shape[0] % (tile * 128))).reshape(-1, 128)


def core_swap(array):
    count = lax.axis_size("dp")
    return lax.ppermute(array, "dp", [(at, at ^ 1) for at in range(count)])


def chip_shift(array, step):
    count = lax.axis_size("dp")
    return lax.ppermute(array, "dp", [(at, (at + 2 * step) % count) for at in range(count)])


def chip_swap(array, bits):
    count = lax.axis_size("dp")
    return lax.ppermute(array, "dp", [(at, at ^ (2 * bits)) for at in range(count)])


def rank_swap(array, bits):
    count = lax.axis_size("fsdp")
    return lax.ppermute(array, "fsdp", [(at, at ^ bits) for at in range(count)])


def entry(array, at, axis=0):
    return lax.dynamic_index_in_dim(array, at, axis, keepdims=False)


def place_kernel(cuts, at, *refs):
    parts, whole, held_rows, semaphores = refs[:-3], refs[-3], refs[-2], refs[-1]
    spans, loads, stores = [], [], []
    for index, (part, first, rows) in enumerate(cuts):
        spans.append(pl.ds(pl.multiple_of(at[index] * 16, 16), rows))
        source = parts[part].at[pl.ds(first, rows)]
        loads.append(
            pltpu.make_async_copy(source, held_rows.at[spans[index]], semaphores.at[0, index])
        )
        loads[index].start()
    for index, span in enumerate(spans):
        loads[index].wait()
        stores.append(
            pltpu.make_async_copy(held_rows.at[span], whole.at[span], semaphores.at[1, index])
        )
        stores[index].start()
    for store in stores:
        store.wait()


def place(parts, cuts, starts, rows):
    width = parts[0].shape[-1]
    dtype = parts[0].dtype
    return pl.pallas_call(
        functools.partial(place_kernel, cuts),
        in_specs=[pl.BlockSpec(memory_space=pltpu.SMEM)]
        + [pl.BlockSpec(memory_space=pl.ANY)] * len(parts),
        out_specs=pl.BlockSpec(memory_space=pl.ANY),
        out_shape=jax.ShapeDtypeStruct((rows, width), dtype),
        scratch_shapes=[
            pltpu.VMEM((rows, width), dtype),
            pltpu.SemaphoreType.DMA((2, len(cuts))),
        ],
        compiler_params=pltpu.CompilerParams(vmem_limit_bytes=vmem_bytes),
        cost_estimate=little_cost,
    )(stacked(starts), *parts)


def own_rows(parts, group):
    ranks, at = lax.axis_size("fsdp"), lax.axis_index("fsdp")
    shares = ranks // group
    count, _, row_part, col_part = parts.shape
    chunk = row_part // shares
    split = parts.reshape(count, group, shares, chunk, col_part).transpose(1, 2, 0, 3, 4)
    split = split.reshape(ranks, count, chunk, col_part)
    if shares > 1:
        moved = lax.all_to_all(split, "fsdp", 0, 0, tiled=True)
        (moved,) = yield (moved,)
        yield moved.transpose(1, 2, 0, 3).reshape(count, chunk, ranks * col_part)
        return
    panels = [entry(split, at)]
    panels += [rank_swap(entry(split, at ^ bits), bits) for bits in range(1, ranks)]
    panels = yield tuple(panels)
    placed = [
        lax.select_n(at, *[panels[panel ^ index] for index in range(ranks)])
        for panel in range(ranks)
    ]
    yield jnp.concatenate(placed, axis=2)


def shard_rows(split, group):
    ranks, count, chunk, col_part = split.shape
    shares = ranks // group
    moved = lax.all_to_all(split, "fsdp", 0, 0, tiled=True)
    moved = moved.reshape(group, shares, count, chunk, col_part).transpose(2, 0, 1, 3, 4)
    return moved.reshape(count, group, shares * chunk, col_part)


def gather_blocks(rows, group):
    ranks, dp_count = lax.axis_size("fsdp"), lax.axis_size("dp")
    shares = ranks // group
    chunk, total = rows.shape
    all_rows = lax.all_gather(rows, ("fsdp", "dp"), axis=0, tiled=True)
    if shares > 1:
        all_rows = all_rows.reshape(group, shares, dp_count, chunk, total).transpose(0, 2, 1, 3, 4)
    return all_rows.reshape(group, total, total)


def join_line(found):
    chips, chip = lax.axis_size("dp") // 2, lax.axis_index("dp") // 2
    chunk = found[0].shape[0]
    starts = [(chip - step) % chips * (chunk // 16) for step in range(chips)]
    return place(found, [(step, 0, chunk) for step in range(chips)], starts, chips * chunk)


def gather_first(rows, group):
    ranks, at = lax.axis_size("fsdp"), lax.axis_index("fsdp")
    total = rows.shape[-1]
    if ranks != group:
        blocks = gather_blocks(rows, group).reshape(group * total, total)
        for _ in range(3):
            (blocks,) = yield (blocks,)
        yield [blocks], [(0, 0, group * total)], [0]
        return
    chips = lax.axis_size("dp") // 2
    core = lax.axis_index("dp") % 2
    chunk = rows.shape[0]
    found = yield tuple(chip_shift(rows, step) for step in range(1, chips))
    line = join_line([rows, *found])
    low_in, high_in = yield (rank_swap(line, 1), rank_swap(line, 2))
    half = total // 4
    parts = [line, low_in, high_in]
    others = [core_swap(part) for part in parts]
    parts += yield (rank_swap(high_in[:half], 1), rank_swap(low_in[half:], 2))
    others += [core_swap(part) for part in parts[3:]]
    cuts, starts = [], []
    for side, family in ((core, 0), (1 - core, len(parts))):
        for index, part in enumerate(parts):
            bits, first_chip = ((0, 0), (1, 0), (2, 0), (3, 0), (3, chips // 2))[index]
            for step in range(part.shape[0] // chunk):
                cuts.append((family + index, step * chunk, chunk))
                row = (at ^ bits) * (2 * chips) + 2 * (first_chip + step) + side
                starts.append(row * (chunk // 16))
    yield parts + others, cuts, starts


def gather_second(rows, group):
    ranks, at = lax.axis_size("fsdp"), lax.axis_index("fsdp")
    total = rows.shape[-1]
    if ranks != group:
        blocks = gather_blocks(rows, group).reshape(group * total, total)
        for _ in range(3):
            (blocks,) = yield (blocks,)
        cuts = [[(0, index * total, total)] for index in range(group)]
        yield [blocks], cuts, [index * (total // 16) for index in range(group)], range(group)
        return
    chips = lax.axis_size("dp") // 2
    core = lax.axis_index("dp") % 2
    chunk, half = rows.shape[0], total // 2
    others = yield tuple(chip_shift(rows, step) for step in range(1, chips))
    line = join_line([rows, *others])
    cuts = [(side, step * chunk, chunk) for side in range(2) for step in range(chips)]
    starts = [
        (2 * step + side) * (chunk // 16) for side in (core, 1 - core) for step in range(chips)
    ]
    (own,) = yield (place([line, core_swap(line)], cuts, starts, total),)
    share = lax.dynamic_slice_in_dim(own, core * half, half, 0)
    mine = yield tuple(rank_swap(share, bits) for bits in range(1, ranks))
    parts, cuts, starts = [own], [[(0, 0, total)]], [at * (total // 16)]
    for bits in range(1, ranks):
        parts += [mine[bits - 1], core_swap(mine[bits - 1])]
        cuts.append([(2 * bits - 1, 0, half), (2 * bits, 0, half)])
        starts += [((at ^ bits) * 2 + side) * (half // 16) for side in (core, 1 - core)]
    yield parts, cuts, starts, [at ^ bits for bits in range(ranks)]


def gather_own(rows, group):
    ranks = lax.axis_size("fsdp")
    shares = ranks // group
    if shares > 1:
        sets = [[share + shares * block for share in range(shares)] for block in range(group)]
        rows = lax.all_gather(rows, "fsdp", axis=1, tiled=True, axis_index_groups=sets)
    return lax.all_gather(rows, "dp", axis=1, tiled=True)


def sum_blocks(product, cut, total, group):
    ranks, dp_count = lax.axis_size("fsdp"), lax.axis_size("dp")
    shares = ranks // group
    if shares > 1:
        blocks = narrow(product(cut(0, total)))
        chunk = total // (dp_count * shares)
        blocks = blocks.reshape(group, dp_count, shares, chunk, -1).transpose(0, 2, 1, 3, 4)
        rows = lax.psum_scatter(
            blocks.reshape(group * total, -1), ("fsdp", "dp"), scatter_dimension=0, tiled=True
        )
        for _ in range(7):
            (rows,) = yield (rows,)
        yield gather_own(rows[None], group)[0]
        return
    chips, half = dp_count // 2, total // 2
    chunk = half // chips
    core, chip = lax.axis_index("dp") % 2, lax.axis_index("dp") // 2
    low_bit, high_bit = lax.axis_index("fsdp") % 2, lax.axis_index("fsdp") // 2
    (away,) = yield (narrow(product(cut((1 - core) * half, half))),)
    (away_in,) = yield (core_swap(away),)
    here = product(cut(core * half, half))
    here = narrow(here + wide(away_in))
    here = here.reshape(2, 2, chips, chunk, -1)
    middle = chips // 2
    first, second = here[:, :, :middle], here[:, :, middle:]
    first_out, second_out = yield (entry(first, 1 - low_bit, 1), entry(second, 1 - high_bit, 0))
    first_in, second_in = yield (rank_swap(first_out, 1), rank_swap(second_out, 2))
    first = narrow(wide(entry(first, low_bit, 1)) + wide(first_in))
    second = narrow(wide(entry(second, high_bit, 0)) + wide(second_in))
    first_in = rank_swap(entry(first, 1 - high_bit), 2)
    second_in = rank_swap(entry(second, 1 - low_bit), 1)
    first_in, second_in = yield (first_in, second_in)
    first = narrow(wide(entry(first, high_bit)) + wide(first_in))
    second = narrow(wide(entry(second, low_bit)) + wide(second_in))
    line = jnp.concatenate([first, second])
    step = 1
    while step < chips:
        bit = chip // step % 2
        line = line.reshape(-1, 2, *line.shape[1:])
        (line_in,) = yield (chip_swap(entry(line, 1 - bit, 1), step),)
        line = narrow(wide(entry(line, bit, 1)) + wide(line_in))
        step *= 2
    yield lax.all_gather(line[0], "dp", axis=0, tiled=True)


def fast_dot(subscripts, left, right):
    return jnp.einsum(subscripts, left, right, preferred_element_type=jnp.float32)


def products_kernel(chips, at, gathered, left_root, right_root, out, whole, semaphores):
    chunk, width = left_root.shape
    ranks = out.shape[0]
    copies = []
    for index in range(2 * chips):
        first = (index % 2 * chips + index // 2) * chunk
        copies.append(
            pltpu.make_async_copy(
                gathered.at[pl.ds(index * chunk, chunk)],
                whole.at[pl.ds(first, chunk)],
                semaphores.at[index],
            )
        )
        copies[-1].start()
    for copy in copies:
        copy.wait()
    first = at[0] * 16
    grad = whole[...]
    picked = lax.broadcasted_iota(jnp.int32, (width, chunk), 0) - first
    picked = picked == lax.broadcasted_iota(jnp.int32, (width, chunk), 1)
    own_columns = narrow(dot_nn(grad, narrow(picked.astype(jnp.float32))))
    side_high, side_low = split_high(dot_nn(left_root[...], grad))
    right = right_root[...]
    precond = dot_nn(side_high, right) + dot_nn(side_low, right)
    outer = dot_nt(whole[pl.ds(pl.multiple_of(first, 16), chunk), :], grad)
    inner = dot_tn(own_columns, grad)
    for at_out, product in enumerate((precond, outer, inner)):
        low = narrow(product)
        for rank in range(ranks):
            span = slice(rank * (width // ranks), (rank + 1) * (width // ranks))
            out[rank, at_out] = low[:, span]


def owned_step(whole, left_root, right_root, group):
    ranks, dp_count = lax.axis_size("fsdp"), lax.axis_size("dp")
    shares = ranks // group
    chunk, total = left_root.shape
    col_part = total // ranks
    first = lax.axis_index("dp") * (chunk * shares) + lax.axis_index("fsdp") % shares * chunk
    if shares == 1:
        return pl.pallas_call(
            functools.partial(products_kernel, dp_count // 2),
            in_specs=[
                pl.BlockSpec(memory_space=pltpu.SMEM),
                pl.BlockSpec(memory_space=pl.ANY),
                pl.BlockSpec(memory_space=pltpu.VMEM),
                pl.BlockSpec(memory_space=pltpu.VMEM),
            ],
            out_specs=pl.BlockSpec(memory_space=pltpu.VMEM),
            out_shape=jax.ShapeDtypeStruct((ranks, 3, chunk, col_part), jnp.bfloat16),
            scratch_shapes=[
                pltpu.VMEM((total, total), jnp.bfloat16),
                pltpu.SemaphoreType.DMA((dp_count,)),
            ],
            compiler_params=pltpu.CompilerParams(vmem_limit_bytes=vmem_bytes),
            cost_estimate=little_cost,
        )((first // 16)[None], whole, left_root, right_root)
    grad_rows = lax.dynamic_slice_in_dim(whole, first, chunk, 0)
    own_columns = lax.dynamic_slice_in_dim(whole, first, chunk, 1)
    outer = fast_dot("rk,jk->rj", grad_rows, whole)
    inner = fast_dot("kr,kj->rj", own_columns, whole)
    side_high, side_low = split_high(fast_dot("rk,kj->rj", left_root, whole))
    precond = fast_dot("rk,kj->rj", side_high, right_root) + fast_dot(
        "rk,kj->rj", side_low, right_root
    )
    products = narrow(jnp.stack([precond, outer, inner]))
    return products.reshape(3, chunk, ranks, col_part).transpose(2, 0, 1, 3)


def per_device(
    tokens,
    conditioning,
    frame_counts,
    cotangent,
    weights,
    biases,
    momentum,
    left_stats,
    right_stats,
    left_roots,
    right_roots,
    bias_moment,
    bias_second,
):
    group = 4
    mod_count = 6
    clip_count, pos_count, frames, width = tokens.shape
    token_count = clip_count * pos_count * frames
    block_count, row_part, col_part = weights.shape
    dp_count, ranks = lax.axis_size("dp"), lax.axis_size("fsdp")
    dp_at, rank_at = lax.axis_index("dp"), lax.axis_index("fsdp")
    all_clips = clip_count * dp_count
    bias_part = biases.shape[0]
    stream = tokens.reshape(token_count, width)
    grad_out = cotangent.reshape(token_count, width)
    low_weights = narrow(weights).reshape(block_count, row_part, col_part)
    shards = low_weights[mod_count:].reshape(-1, group, row_part, col_part)

    weight_rows = own_rows(shards, group)
    weight_panels = next(weight_rows)
    cond_low = narrow(jax.nn.silu(conditioning))
    first_parts = lax.all_gather(packed([cond_low, narrow(biases)], 16), "dp", axis=0, tiled=True)
    weight_panels, first_parts = tie(weight_panels, first_parts)
    attn_rows, one_rows, two_rows = weight_rows.send(weight_panels)

    first_parts = first_parts.reshape(dp_count, -1)
    cond_all = first_parts[:, : clip_count * width].reshape(all_clips, width)
    bias_rows = wide(first_parts[:, clip_count * width : clip_count * width + bias_part])
    cond_rows = lax.dynamic_slice_in_dim(cond_all, dp_at * row_part, row_part, 1)
    cond_cols = wide(lax.dynamic_slice_in_dim(cond_all, rank_at * col_part, col_part, 1))
    mod_parts = fast_dot("cr,jre->cje", cond_rows, low_weights[:mod_count])
    mod_parts = lax.all_to_all(mod_parts, "dp", 0, 0, tiled=True)
    roots = jnp.stack([narrow(left_roots[mod_count:]), narrow(right_roots[mod_count:])])
    mod_parts, attn_rows, roots = tie(mod_parts, attn_rows, roots)
    attn_steps = gather_first(attn_rows, group)
    attn_parts = next(attn_steps)
    root_rows = own_rows(roots.reshape(-1, group, row_part, col_part), group)
    root_panels = next(root_rows)
    mod_cols = jnp.sum(mod_parts.reshape(dp_count, clip_count, mod_count, col_part), axis=0)
    left_cond = jnp.einsum("jrk,ck->jrc", left_roots[:mod_count], cond_cols, precision=precise)
    mod_size, bias_size = mod_cols.size, dp_count * bias_part
    second_parts = lax.all_gather(
        packed([mod_cols, bias_rows, left_cond], 8), "fsdp", axis=0, tiled=True
    )
    second_parts, attn_parts, one_rows = tie(second_parts, attn_parts, one_rows)
    attn_parts = attn_steps.send(attn_parts)
    one_steps = gather_second(one_rows, group)
    one_parts = next(one_steps)
    root_rows = root_rows.send(root_panels)
    attn_parts, root_rows = tie(attn_parts, root_rows)
    attn_parts = attn_steps.send(attn_parts)
    one_parts = one_steps.send(one_parts)
    attn_parts, one_parts, two_rows = tie(attn_parts, one_parts, two_rows)
    one_parts = one_steps.send(one_parts)
    weight_steps = gather_second(two_rows, group)
    two_w_parts = next(weight_steps)
    gathered = attn_steps.send(attn_parts)
    left_rows, right_rows = jnp.split(root_rows, 2)
    right_wholes = [gather_own(rows[None], group)[0] for rows in right_rows]
    second_parts = second_parts.reshape(ranks, -1)
    mods = second_parts[:, :mod_size].reshape(ranks, clip_count, mod_count, col_part)
    mods = mods.transpose(1, 2, 0, 3).reshape(clip_count, mod_count, width)
    bias_all = second_parts[:, mod_size : mod_size + bias_size].reshape(ranks, dp_count, bias_part)
    bias_all = bias_all.transpose(1, 0, 2).reshape(-1, width)
    left_size = mod_size + bias_size + left_cond.size
    left_cond = jnp.sum(second_parts[:, mod_size + bias_size : left_size], axis=0)
    left_cond = left_cond.reshape(mod_count, row_part, all_clips)
    mods = mods + bias_all[:mod_count]
    bias_table = jnp.concatenate(
        [bias_all[6:7], jnp.zeros((1, width), jnp.float32), bias_all[7:14]]
    )

    attn_w, attn_in, parts, mixed, proj, resid, mlp_in, d_branch, d_branch_sums = run_attention(
        frames, frame_counts, stream, grad_out, mods, bias_table, gathered
    )
    attn_w = attn_w.reshape(group, width, width)
    mlp_in, two_w_parts = tie(mlp_in, two_w_parts)
    two_w_parts = weight_steps.send(two_w_parts)
    mlp_in, two_w_parts = tie(mlp_in, two_w_parts)
    two_w_parts = weight_steps.send(two_w_parts)
    one_w, hidden, slope = run_hidden(mlp_in, one_steps.send(one_parts), bias_table[4:8, None])
    one_w = one_w.reshape(group, width, width)

    two_steps = sum_blocks(
        lambda left: fast_dot("jtd,te->jde", left, d_branch),
        lambda first, size: lax.dynamic_slice_in_dim(hidden, first, size, 2),
        width,
        group,
    )
    two_parts = next(two_steps)
    hidden, two_parts, right_wholes[2] = tie(hidden, two_parts, right_wholes[2])
    two_parts = two_steps.send(two_parts)
    gathered = weight_steps.send(two_w_parts)
    d_pre, d_pre_sums, block_out, d_gate_two = run_branch(
        frames,
        frame_counts,
        hidden,
        slope,
        gathered,
        d_branch,
        bias_table[8:9],
        mods[:, 5:6],
        resid,
        grad_out,
    )
    d_pre, two_parts, right_wholes[1] = tie(d_pre, two_parts, right_wholes[1])
    two_parts = two_steps.send(two_parts)
    d_pre, two_parts = tie(d_pre, two_parts)
    two_parts = two_steps.send(two_parts)
    one_steps = sum_blocks(
        lambda left: fast_dot("td,jte->jde", left, d_pre),
        lambda first, size: lax.dynamic_slice_in_dim(mlp_in, first, size, 1),
        width,
        group,
    )
    one_parts = next(one_steps)
    d_pre, one_parts = tie(d_pre, one_parts)
    one_parts = one_steps.send(one_parts)
    d_resid, d_proj, resid_sums = run_resid(
        frames, frame_counts, d_pre, one_w, mods, resid, grad_out, proj
    )
    d_proj, one_parts, two_parts, right_wholes[0] = tie(
        d_proj, one_parts, two_parts, right_wholes[0]
    )
    two_parts = two_steps.send(two_parts)
    one_parts = one_steps.send(one_parts)
    d_proj, one_parts = tie(d_proj, one_parts)
    one_parts = one_steps.send(one_parts)
    d_heads, head_sums = run_attention_back(frames, frame_counts, d_proj, parts, attn_w)
    d_heads, two_parts, one_parts = tie(d_heads, two_parts, one_parts)
    two_parts = two_steps.send(two_parts)
    one_parts = one_steps.send(one_parts)
    attn_steps = sum_blocks(
        lambda left: fast_dot("jtd,jte->jde", left, d_heads),
        lambda first, size: jnp.stack(
            [lax.dynamic_slice_in_dim(left, first, size, 1) for left in (attn_in,) * 3 + (mixed,)]
        ),
        width,
        group,
    )
    attn_parts = next(attn_steps)
    d_heads, attn_parts = tie(d_heads, attn_parts)
    attn_parts = attn_steps.send(attn_parts)
    d_heads, attn_parts, two_parts = tie(d_heads, attn_parts, two_parts)
    two_parts = two_steps.send(two_parts)
    attn_parts = attn_steps.send(attn_parts)
    d_heads, attn_parts = tie(d_heads, attn_parts)
    attn_parts = attn_steps.send(attn_parts)
    input_grad, input_sums = run_input(d_heads, attn_w, mods, stream, d_resid)
    input_sums, one_parts, two_parts = tie(input_sums, one_parts, two_parts)
    whole_two = two_steps.send(two_parts)
    one_parts = one_steps.send(one_parts)
    input_sums, attn_parts, one_parts = tie(input_sums, attn_parts, one_parts)
    attn_parts = attn_steps.send(attn_parts)
    one_parts = one_steps.send(one_parts)

    d_mods = jnp.stack(
        [
            input_sums[:, 0],
            input_sums[:, 1],
            resid_sums[:, 2],
            resid_sums[:, 0],
            resid_sums[:, 1],
            d_gate_two[:, 0],
        ],
        axis=1,
    )
    head_sums = jnp.sum(head_sums, axis=0)
    grad_bias = jnp.concatenate(
        [
            jnp.sum(d_mods, axis=0),
            head_sums[0:1],
            head_sums[2:3],
            jnp.sum(resid_sums[:, 3], axis=0)[None],
            d_pre_sums[:, 0],
            jnp.sum(d_branch_sums, axis=0),
        ]
    )
    to_ranks = jnp.concatenate(
        [
            d_mods.reshape(clip_count, mod_count, ranks, col_part)
            .transpose(2, 0, 1, 3)
            .reshape(ranks, mod_size),
            grad_bias.reshape(dp_count, ranks, bias_part)
            .transpose(1, 0, 2)
            .reshape(ranks, bias_size),
        ],
        axis=1,
    )
    rank_sums = jnp.sum(lax.all_to_all(to_ranks, "fsdp", 0, 0, tiled=True), axis=0)
    rank_sums, attn_parts, one_parts = tie(rank_sums, attn_parts, one_parts)
    attn_parts = attn_steps.send(attn_parts)
    whole_one = one_steps.send(one_parts)
    to_rows = jnp.concatenate(
        [
            jnp.broadcast_to(rank_sums[None, :mod_size], (dp_count, mod_size)),
            rank_sums[mod_size:].reshape(dp_count, bias_part),
        ],
        axis=1,
    )
    from_rows = lax.all_to_all(to_rows, "dp", 0, 0, tiled=True)
    from_rows, attn_parts = tie(from_rows, attn_parts)
    attn_parts = attn_steps.send(attn_parts)
    bias_grad = jnp.sum(from_rows[:, mod_size:], axis=0)
    mod_grad_cols = from_rows[:, :mod_size].reshape(all_clips, mod_count, col_part)
    mod_grad = lax.all_gather(packed([mod_grad_cols], 8), "fsdp", axis=0, tiled=True)
    mod_grad = mod_grad.reshape(ranks, -1)[:, : mod_grad_cols.size]
    mod_grad = mod_grad.reshape(ranks, all_clips, mod_count, col_part).transpose(1, 2, 0, 3)
    mod_grad = mod_grad.reshape(all_clips, mod_count, width)

    mod_grad_rows = lax.dynamic_slice_in_dim(mod_grad, dp_at * row_part, row_part, 2)
    right_parts = jnp.einsum(
        "cjk,jke->cje", mod_grad_rows, right_roots[:mod_count], precision=precise
    )
    cond_wide = wide(cond_all)
    cond_row_wide = wide(cond_rows)
    mod_gram = jnp.einsum("cjk,bjk->jcb", mod_grad, mod_grad, precision=precise)
    cond_gram = jnp.einsum("ck,bk->cb", cond_wide, cond_wide, precision=precise)
    mod_side = jnp.einsum("jcb,be->jce", mod_gram, cond_cols, precision=precise)
    ada_left = jnp.einsum("cr,jce->jre", cond_row_wide, mod_side, precision=precise)
    cond_side = jnp.einsum("cb,bje->jce", cond_gram, mod_grad_cols, precision=precise)
    ada_right = jnp.einsum("cjr,jce->jre", mod_grad_rows, cond_side, precision=precise)

    products_two = owned_step(whole_two, left_rows[2], right_wholes[2], group)
    products_two, right_parts, attn_parts = tie(products_two, right_parts, attn_parts)
    whole_attn = attn_steps.send(attn_parts)
    back_two = shard_rows(products_two, group)
    products_one = owned_step(whole_one, left_rows[1], right_wholes[1], group)
    back_one = shard_rows(products_one, group)
    right_parts = lax.all_gather(packed([right_parts], 8), "dp", axis=0, tiled=True)
    mod_right = jnp.sum(right_parts.reshape(dp_count, -1), axis=0)[: mod_grad_cols.size]
    mod_right = mod_right.reshape(all_clips, mod_count, col_part)
    ada_pre = jnp.einsum("jrc,cje->jre", left_cond, mod_right, precision=precise)
    whole_attn, back_one, back_two, ada_pre, ada_left, ada_right = tie(
        whole_attn, back_one, back_two, ada_pre, ada_left, ada_right
    )
    back_attn = shard_rows(owned_step(whole_attn, left_rows[0], right_wholes[0], group), group)

    def joined(at, ada):
        return jnp.concatenate([ada, wide(back_attn[at]), wide(back_one[at]), wide(back_two[at])])

    precond = joined(0, ada_pre)
    left_new = stat_decay * left_stats + (1.0 - stat_decay) * joined(1, ada_left)
    right_new = stat_decay * right_stats + (1.0 - stat_decay) * joined(2, ada_right)
    momentum_new = moment_decay * momentum + precond
    weights_new = weights - weight_rate * momentum_new
    weights_copy = weights_new.astype(jnp.bfloat16)
    bias_second_new = stat_decay * bias_second + (1.0 - stat_decay) * bias_grad * bias_grad
    bias_moment_new = moment_decay * bias_moment + bias_grad * lax.rsqrt(
        bias_second_new + diag_epsilon
    )
    biases_new = biases - bias_rate * bias_moment_new
    return (
        block_out.reshape(tokens.shape),
        input_grad.reshape(tokens.shape),
        left_new,
        right_new,
        momentum_new,
        weights_new,
        weights_copy,
        bias_moment_new,
        bias_second_new,
        biases_new,
    )


def solution(mesh):
    placed = (
        P("dp", "fsdp", None, None),
        P("dp", None),
        P("dp"),
        P("dp", "fsdp", None, None),
        P(None, "dp", "fsdp"),
        P(("dp", "fsdp")),
        P(None, "dp", "fsdp"),
        P(None, "dp", "fsdp"),
        P(None, "dp", "fsdp"),
        P(None, "dp", "fsdp"),
        P(None, "dp", "fsdp"),
        P(("dp", "fsdp")),
        P(("dp", "fsdp")),
    )
    return jax.shard_map(
        per_device,
        mesh=mesh,
        in_specs=placed,
        out_specs=(
            P("dp", "fsdp", None, None),
            P("dp", "fsdp", None, None),
            P(None, "dp", "fsdp"),
            P(None, "dp", "fsdp"),
            P(None, "dp", "fsdp"),
            P(None, "dp", "fsdp"),
            P(None, "dp", "fsdp"),
            P(("dp", "fsdp")),
            P(("dp", "fsdp")),
            P(("dp", "fsdp")),
        ),
        check_vma=False,
    )
```

```python
import functools
import math

import jax
import jax.numpy as jnp
from jax import lax
from jax.experimental import pallas as pl
from jax.experimental.pallas import tpu as pltpu
from jax.sharding import PartitionSpec as P

HEADS = 16


precise = lax.Precision.HIGHEST
norm_epsilon = 1e-06
masked_score = -1e30
stat_decay = 0.5
moment_decay = 0.9
weight_rate = 0.7
bias_rate = 0.1
diag_epsilon = 1e-08
vmem_bytes = 50 * 2**20
little_cost = pl.CostEstimate(flops=1024, bytes_accessed=1024, transcendentals=0)


def narrow(array):
    return array.astype(jnp.bfloat16)


def wide(array):
    return array.astype(jnp.float32)


def spec(shape, index_map, **keywords):
    return pl.BlockSpec(shape, index_map, **keywords)


def held(shape):
    return pl.BlockSpec(shape, lambda step: (0,) * len(shape), pipeline_mode=pl.Buffered(1))


def column_cuts(total):
    cuts, at = [], 0
    while at < total:
        cuts.append((at, min(total, at + 256)))
        at += 256
    return cuts


def dot_nn(left, right):
    return lax.dot_general(left, right, (((1,), (0,)), ((), ())), preferred_element_type=jnp.float32)


def dot_nt(left, right):
    return lax.dot_general(left, right, (((1,), (1,)), ((), ())), preferred_element_type=jnp.float32)


def dot_tn(left, right):
    return lax.dot_general(left, right, (((0,), (0,)), ((), ())), preferred_element_type=jnp.float32)


def split_high(values):
    high = narrow(values)
    return high, narrow(values - wide(high))


def valid_rows(count, rows, frames):
    at = lax.broadcasted_iota(jnp.int32, (rows, 1), 0)
    return (lax.rem(at, frames) < count).astype(jnp.float32)


def score_offset(count, size, frames, key_axis):
    first = lax.broadcasted_iota(jnp.int32, (size, size), 0)
    second = lax.broadcasted_iota(jnp.int32, (size, size), 1)
    key = second if key_axis == 1 else first
    met = (lax.div(first, frames) == lax.div(second, frames)) & (lax.rem(key, frames) < count)
    return jnp.where(met, 0.0, masked_score)


def head_windows(width):
    size = width // HEADS
    windows = []
    for head in range(HEADS):
        low, high = head * size, (head + 1) * size
        start = low // 128 * 128
        stop = min(width, -(-high // 128) * 128)
        windows.append((low - start, high - start, start, stop))
    return windows


def lane_mask(low, high, count, dtype):
    lanes = lax.broadcasted_iota(jnp.int32, (1, count), 1)
    return ((lanes >= low) & (lanes < high)).astype(jnp.float32).astype(dtype)


def norm_parts(values):
    centered = values - jnp.mean(values, axis=-1, keepdims=True)
    variance = jnp.mean(centered * centered, axis=-1, keepdims=True)
    inverse = lax.rsqrt(variance + norm_epsilon)
    return centered * inverse, inverse


def norm_back(grad, normed, inverse):
    first = jnp.mean(grad, axis=-1, keepdims=True)
    second = jnp.mean(grad * normed, axis=-1, keepdims=True)
    return (grad - first - normed * second) * inverse


def column_sum(values):
    return jnp.sum(values, axis=0, keepdims=True)


def start_loads(cuts, at, parts, whole, semaphores, first_index=0):
    loads = []
    for index, (part, first, rows) in enumerate(cuts, first_index):
        span = pl.ds(pl.multiple_of(at[index] * 16, 16), rows)
        source = parts[part].at[pl.ds(first, rows)]
        loads.append(pltpu.make_async_copy(source, whole.at[span], semaphores.at[index]))
        loads[-1].start()
    return loads


def attention_kernel(
    frames,
    counts,
    tokens,
    cotangent,
    mods,
    bias,
    blocks,
    attn_in,
    parts,
    mixed_low,
    proj_out,
    resid_out,
    mlp_in,
    d_branch,
    d_branch_sum,
    mixed,
    whole,
    semaphores,
):
    rows, width = tokens.shape
    clip = pl.program_id(0)
    loads = [
        pltpu.make_async_copy(blocks.at[at], whole.at[at], semaphores.at[at]) for at in range(4)
    ]

    @pl.when(clip == 0)
    def _():
        for load in loads:
            load.start()

    tile = min(rows, 128)
    count = counts[clip]
    shift_one, scale_one, gate_one = (mods[0, at : at + 1, :] for at in range(3))
    shift_two, scale_two, gate_two = (mods[0, at : at + 1, :] for at in range(3, 6))
    for first in range(0, rows, tile):
        span = slice(first, first + tile)
        normed, _ = norm_parts(wide(tokens[span]))
        attn_in[span] = narrow(normed * (1.0 + scale_one) + shift_one)
        branch_back = narrow(wide(cotangent[span]) * valid_rows(count, tile, frames) * gate_two)
        d_branch[span] = branch_back
        part_sum = column_sum(wide(branch_back))
        d_branch_sum[0] = part_sum if first == 0 else d_branch_sum[0] + part_sum

    @pl.when(clip == 0)
    def _():
        for load in loads:
            load.wait()

    scale = (width // HEADS) ** -0.5
    source = attn_in[...]
    for low, high in column_cuts(width):
        span = slice(low, high)
        query = (dot_nn(source, whole[0, :, span]) + bias[0:1, span]) * scale
        parts[0, :, span], parts[1, :, span] = split_high(query)
        parts[2, :, span], parts[3, :, span] = split_high(dot_nn(source, whole[1, :, span]))
        parts[4, :, span] = narrow(dot_nn(source, whole[2, :, span]) + bias[2:3, span])
    offset = score_offset(count, tile, frames, 1)
    mixed[...] = jnp.zeros_like(mixed)
    for first in range(0, rows, tile):
        span = slice(first, first + tile)
        for low, high, start, stop in head_windows(width):
            lanes = slice(start, stop)
            mask = lane_mask(low, high, stop - start, jnp.bfloat16)
            key_high = parts[2, span, lanes]
            query_high = parts[0, span, lanes] * mask
            scores = dot_nt(query_high, key_high)
            scores += dot_nt(parts[1, span, lanes] * mask, key_high)
            scores += dot_nt(query_high, parts[3, span, lanes]) + offset
            expons = jnp.exp(scores - jnp.max(scores, axis=-1, keepdims=True))
            probs = expons * (1.0 / jnp.sum(expons, axis=-1, keepdims=True))
            out = dot_nn(narrow(probs), parts[4, span, lanes] * mask)
            mixed[span, lanes] += out
    mixed_low[...] = narrow(mixed[...])
    source = mixed_low[...]
    for low, high in column_cuts(width):
        span = slice(low, high)
        proj_out[:, span] = dot_nn(source, whole[3, :, span]) + bias[3:4, span]
    for first in range(0, rows, tile):
        span = slice(first, first + tile)
        resid = wide(tokens[span]) + valid_rows(count, tile, frames) * gate_one * proj_out[span]
        resid_out[span] = resid
        normed, _ = norm_parts(resid)
        mlp_in[span] = narrow(normed * (1.0 + scale_two) + shift_two)


def run_attention(frames, counts, tokens, cotangent, mods, bias, blocks):
    total, width = tokens.shape
    clips = mods.shape[0]
    rows = total // clips
    clip_rows = spec((rows, width), lambda clip: (clip, 0))
    low = jax.ShapeDtypeStruct((total, width), jnp.bfloat16)
    full = jax.ShapeDtypeStruct((total, width), jnp.float32)
    return pl.pallas_call(
        functools.partial(attention_kernel, frames),
        grid=(clips,),
        in_specs=[
            pl.BlockSpec(memory_space=pltpu.SMEM),
            clip_rows,
            clip_rows,
            spec((1,) + mods.shape[1:], lambda clip: (clip, 0, 0)),
            held(bias.shape),
            pl.BlockSpec(memory_space=pl.ANY),
        ],
        out_specs=[
            clip_rows,
            spec((5, rows, width), lambda clip: (0, clip, 0)),
            clip_rows,
            clip_rows,
            clip_rows,
            clip_rows,
            clip_rows,
            spec((1, 1, width), lambda clip: (clip, 0, 0)),
        ],
        out_shape=[
            low,
            jax.ShapeDtypeStruct((5, total, width), jnp.bfloat16),
            low,
            full,
            full,
            low,
            low,
            jax.ShapeDtypeStruct((clips, 1, width), jnp.float32),
        ],
        scratch_shapes=[
            pltpu.VMEM((rows, width), jnp.float32),
            pltpu.VMEM(blocks.shape, jnp.bfloat16),
            pltpu.SemaphoreType.DMA((4,)),
        ],
        compiler_params=pltpu.CompilerParams(vmem_limit_bytes=vmem_bytes),
        cost_estimate=little_cost,
    )(counts, tokens, cotangent, mods, bias, blocks)


def stacked(numbers):
    return jnp.stack([jnp.asarray(number, jnp.int32) for number in numbers])


def start_loads(cuts, at, parts, whole, semaphores):
    for index, (part, first, rows) in enumerate(cuts):
        span = pl.ds(pl.multiple_of(at[index] * 16, 16), rows)
        source = parts[part].at[pl.ds(first, rows)]
        pltpu.make_async_copy(source, whole.at[span], semaphores.at[index]).start()


def wait_loads(groups, at, parts, whole, semaphores):
    index = 0
    for step, cuts in enumerate(groups):
        base = index
        index += len(cuts)

        @pl.when(pl.program_id(0) == step)
        def _(cuts=cuts, base=base):
            for offset, (part, first, rows) in enumerate(cuts):
                span = pl.ds(pl.multiple_of(at[base + offset] * 16, 16), rows)
                source = parts[part].at[pl.ds(first, rows)]
                semaphore = semaphores.at[base + offset]
                pltpu.make_async_copy(source, whole.at[span], semaphore).wait()


def hidden_kernel(cuts, order, starts, mlp_in, bias, *refs):
    whole_out, hidden, slope, whole, semaphores, store_semaphores = refs[-6:]
    pieces = refs[:-6]
    step, steps = pl.program_id(0), pl.num_programs(0)
    width = mlp_in.shape[-1]
    span = pl.ds(pl.multiple_of(order[step] * width, width), width)

    @pl.when(step == 0)
    def _():
        start_loads([cut for group in cuts for cut in group], starts, pieces, whole, semaphores)

    wait_loads(cuts, starts, pieces, whole, semaphores)
    pltpu.make_async_copy(whole.at[span], whole_out.at[span], store_semaphores.at[step]).start()
    root = (2.0 / math.pi) ** 0.5
    source = mlp_in[...]
    block = whole.at[span]
    for low, high in column_cuts(width):
        lanes = slice(low, high)
        pre = dot_nn(source, block[:, lanes]) + bias[0, :, lanes]
        square = pre * pre
        bent = jnp.tanh(root * pre * (1.0 + 0.044715 * square))
        half = 0.5 + 0.5 * bent
        hidden[0, :, lanes] = narrow(pre * half)
        steep = (0.5 * root) * pre * (1.0 + 3 * 0.044715 * square)
        slope[0, :, lanes] = narrow(half + steep * (1.0 - bent * bent))

    @pl.when(step == steps - 1)
    def _():
        for at in range(len(cuts)):
            rows = pl.ds(pl.multiple_of(order[at] * width, width), width)
            pltpu.make_async_copy(
                whole.at[rows], whole_out.at[rows], store_semaphores.at[at]
            ).wait()


def run_hidden(mlp_in, gathered, bias):
    pieces, cuts, starts, order = gathered
    total, width = mlp_in.shape
    count = len(cuts)
    per_block = pl.BlockSpec((1, total, width), lambda at, order, starts: (order[at], 0, 0))
    out = jax.ShapeDtypeStruct((count, total, width), jnp.bfloat16)
    return pl.pallas_call(
        functools.partial(hidden_kernel, cuts),
        grid_spec=pltpu.PrefetchScalarGridSpec(
            num_scalar_prefetch=2,
            grid=(count,),
            in_specs=[
                pl.BlockSpec((total, width), lambda at, order, starts: (0, 0)),
                pl.BlockSpec((1, 1, width), lambda at, order, starts: (order[at], 0, 0)),
            ]
            + [pl.BlockSpec(memory_space=pl.ANY)] * len(pieces),
            out_specs=[pl.BlockSpec(memory_space=pl.ANY), per_block, per_block],
            scratch_shapes=[
                pltpu.VMEM((count * width, width), jnp.bfloat16),
                pltpu.SemaphoreType.DMA((len(starts),)),
                pltpu.SemaphoreType.DMA((count,)),
            ],
        ),
        out_shape=[jax.ShapeDtypeStruct((count * width, width), jnp.bfloat16), out, out],
        compiler_params=pltpu.CompilerParams(vmem_limit_bytes=vmem_bytes),
        cost_estimate=little_cost,
    )(stacked(order), stacked(starts), mlp_in, bias, *pieces)


def branch_kernel(
    frames,
    cuts,
    order,
    starts,
    counts,
    hidden,
    slope,
    d_branch,
    bias,
    gates,
    resid,
    cotangent,
    *refs,
):
    d_pre, d_pre_sum, block_out, d_gate, branch, whole, semaphores = refs[-7:]
    pieces = refs[:-7]
    step, steps = pl.program_id(0), pl.num_programs(0)
    total, width = resid.shape
    clips = gates.shape[0]
    rows = total // clips
    source, back = hidden[0], d_branch[...]

    @pl.when(step == 0)
    def _():
        start_loads([cut for group in cuts for cut in group], starts, pieces, whole, semaphores)
        branch[...] = jnp.zeros_like(branch)

    wait_loads(cuts, starts, pieces, whole, semaphores)
    block = whole.at[pl.ds(pl.multiple_of(order[step] * width, width), width)]
    for low, high in column_cuts(width):
        span = slice(low, high)
        d_hidden = dot_nt(back, block[span, :])
        low_back = narrow(d_hidden * wide(slope[0, :, span]))
        d_pre[0, :, span] = low_back
        d_pre_sum[0, :, span] = column_sum(wide(low_back))
        branch[:, span] += dot_nn(source, block[:, span])

    @pl.when(step == steps - 1)
    def _():
        for clip in range(clips):
            span = slice(clip * rows, (clip + 1) * rows)
            kept = valid_rows(counts[clip], rows, frames) * (branch[span] + bias[...])
            block_out[span] = narrow(resid[span] + gates[clip] * kept)
            d_gate[clip] = column_sum(wide(cotangent[span]) * kept)


def run_branch(frames, counts, hidden, slope, gathered, d_branch, bias, gates, resid, cotangent):
    pieces, cuts, starts, order = gathered
    count, total, width = hidden.shape
    clips = gates.shape[0]

    def all_of(*shape):
        return pl.BlockSpec(shape, lambda at, order, starts: (0,) * len(shape))

    per_block = pl.BlockSpec((1, total, width), lambda at, order, starts: (order[at], 0, 0))
    low = jax.ShapeDtypeStruct((total, width), jnp.bfloat16)
    return pl.pallas_call(
        functools.partial(branch_kernel, frames, cuts),
        grid_spec=pltpu.PrefetchScalarGridSpec(
            num_scalar_prefetch=2,
            grid=(count,),
            in_specs=[
                pl.BlockSpec(memory_space=pltpu.SMEM),
                per_block,
                per_block,
                all_of(total, width),
                all_of(*bias.shape),
                all_of(*gates.shape),
                all_of(total, width),
                all_of(total, width),
            ]
            + [pl.BlockSpec(memory_space=pl.ANY)] * len(pieces),
            out_specs=[
                per_block,
                pl.BlockSpec((1, 1, width), lambda at, order, starts: (order[at], 0, 0)),
                all_of(total, width),
                all_of(clips, 1, width),
            ],
            scratch_shapes=[
                pltpu.VMEM((total, width), jnp.float32),
                pltpu.VMEM((count * width, width), jnp.bfloat16),
                pltpu.SemaphoreType.DMA((len(starts),)),
            ],
        ),
        out_shape=[
            jax.ShapeDtypeStruct((count, total, width), jnp.bfloat16),
            jax.ShapeDtypeStruct((count, 1, width), jnp.float32),
            low,
            jax.ShapeDtypeStruct((clips, 1, width), jnp.float32),
        ],
        compiler_params=pltpu.CompilerParams(vmem_limit_bytes=vmem_bytes),
        cost_estimate=little_cost,
    )(stacked(order), stacked(starts), counts, hidden, slope, d_branch, bias, gates, resid, cotangent, *pieces)


def resid_kernel(
    frames,
    counts,
    d_pre,
    block,
    mods,
    resid,
    cotangent,
    proj,
    d_resid_out,
    d_proj,
    sums,
    total_grad,
):
    step, steps = pl.program_id(0), pl.num_programs(0)
    total, width = resid.shape
    clips = mods.shape[0]
    rows = total // clips
    tile = min(rows, 128)
    source = d_pre[0]

    @pl.when(step == 0)
    def _():
        total_grad[...] = jnp.zeros_like(total_grad)

    for low, high in column_cuts(width):
        span = slice(low, high)
        total_grad[:, span] += dot_nt(source, block[0, span, :])

    @pl.when(step == steps - 1)
    def _():
        for clip in range(clips):
            gate_one, scale_two = mods[clip, 2:3, :], mods[clip, 4:5, :]
            found = [0.0] * 4
            for first in range(clip * rows, (clip + 1) * rows, tile):
                span = slice(first, first + tile)
                grad = total_grad[span]
                normed, inverse = norm_parts(resid[span])
                back = norm_back(grad * (1.0 + scale_two), normed, inverse)
                d_resid = wide(cotangent[span]) + back
                d_resid_out[span] = d_resid
                kept = valid_rows(counts[clip], tile, frames) * d_resid
                low_back = narrow(kept * gate_one)
                d_proj[span] = low_back
                terms = (grad, grad * normed, kept * proj[span], wide(low_back))
                found = [old + column_sum(term) for old, term in zip(found, terms)]
            for at in range(4):
                sums[clip, at : at + 1, :] = found[at]


def run_resid(frames, counts, d_pre, blocks, mods, resid, cotangent, proj):
    count, total, width = d_pre.shape
    clips = mods.shape[0]
    return pl.pallas_call(
        functools.partial(resid_kernel, frames),
        grid=(count,),
        in_specs=[
            pl.BlockSpec(memory_space=pltpu.SMEM),
            spec((1, total, width), lambda at: (at, 0, 0)),
            spec((1, width, width), lambda at: (at, 0, 0)),
            held(mods.shape),
            held((total, width)),
            held((total, width)),
            held((total, width)),
        ],
        out_specs=[held((total, width)), held((total, width)), held((clips, 4, width))],
        out_shape=[
            jax.ShapeDtypeStruct((total, width), jnp.float32),
            jax.ShapeDtypeStruct((total, width), jnp.bfloat16),
            jax.ShapeDtypeStruct((clips, 4, width), jnp.float32),
        ],
        scratch_shapes=[pltpu.VMEM((total, width), jnp.float32)],
        compiler_params=pltpu.CompilerParams(vmem_limit_bytes=vmem_bytes),
        cost_estimate=little_cost,
    )(counts, d_pre, blocks, mods, resid, cotangent, proj)


def attention_back_kernel(
    frames, counts, d_proj, parts, block, d_qkv, sums, d_mixed, d_query, d_key, d_value
):
    rows, width = d_proj.shape
    tile = min(rows, 128)
    count = counts[pl.program_id(0)]
    source = d_proj[...]
    for low, high in column_cuts(width):
        d_mixed[:, low:high] = narrow(dot_nt(source, block[0, low:high, :]))
    scale = (width // HEADS) ** -0.5
    offset = score_offset(count, tile, frames, 0)
    for ref in (d_query, d_key, d_value):
        ref[...] = jnp.zeros_like(ref)
    for first in range(0, rows, tile):
        span = slice(first, first + tile)
        for low, high, start, stop in head_windows(width):
            lanes = slice(start, stop)
            mask = lane_mask(low, high, stop - start, jnp.bfloat16)
            query_high = parts[0, span, lanes] * mask
            key_high = parts[2, span, lanes] * mask
            back = d_mixed[span, lanes] * mask
            scores = dot_nt(key_high, query_high)
            scores += dot_nt(key_high, parts[1, span, lanes])
            scores += dot_nt(parts[3, span, lanes], query_high) + offset
            expons = jnp.exp(scores - jnp.max(scores, axis=0, keepdims=True))
            probs = expons * (1.0 / jnp.sum(expons, axis=0, keepdims=True))
            d_probs = dot_nt(parts[4, span, lanes], back)
            inner = jnp.sum(d_probs * probs, axis=0, keepdims=True)
            d_scores = narrow(probs * (d_probs - inner))
            d_value[span, lanes] += dot_nn(narrow(probs), back)
            d_key[span, lanes] += dot_nn(d_scores, query_high)
            d_query[span, lanes] += dot_tn(d_scores, key_high)
    for at, ref in enumerate((d_query, d_key, d_value)):
        low_back = narrow(ref[...] * scale) if at == 0 else narrow(ref[...])
        d_qkv[at] = low_back
        sums[0, at : at + 1, :] = column_sum(wide(low_back))
    d_qkv[3] = source


def run_attention_back(frames, counts, d_proj, parts, block):
    total, width = d_proj.shape
    clips = counts.shape[0]
    rows = total // clips
    return pl.pallas_call(
        functools.partial(attention_back_kernel, frames),
        grid=(clips,),
        in_specs=[
            pl.BlockSpec(memory_space=pltpu.SMEM),
            spec((rows, width), lambda clip: (clip, 0)),
            spec((5, rows, width), lambda clip: (0, clip, 0)),
            spec((1, width, width), lambda clip: (3, 0, 0), pipeline_mode=pl.Buffered(1)),
        ],
        out_specs=[
            spec((4, rows, width), lambda clip: (0, clip, 0)),
            spec((1, 3, width), lambda clip: (clip, 0, 0)),
        ],
        out_shape=[
            jax.ShapeDtypeStruct((4, total, width), jnp.bfloat16),
            jax.ShapeDtypeStruct((clips, 3, width), jnp.float32),
        ],
        scratch_shapes=[pltpu.VMEM((rows, width), jnp.bfloat16)]
        + [pltpu.VMEM((rows, width), jnp.float32)] * 3,
        compiler_params=pltpu.CompilerParams(vmem_limit_bytes=vmem_bytes),
        cost_estimate=little_cost,
    )(counts, d_proj, parts, block)


def input_kernel(d_qkv, block, mods, tokens, d_resid, input_grad, sums, total_grad):
    step, steps = pl.program_id(0), pl.num_programs(0)
    total, width = tokens.shape
    clips = mods.shape[0]
    rows = total // clips
    tile = min(rows, 128)
    source = d_qkv[0]

    @pl.when(step == 0)
    def _():
        total_grad[...] = jnp.zeros_like(total_grad)

    for low, high in column_cuts(width):
        span = slice(low, high)
        total_grad[:, span] += dot_nt(source, block[0, span, :])

    @pl.when(step == steps - 1)
    def _():
        for clip in range(clips):
            scale_one = mods[clip, 1:2, :]
            found = [0.0] * 2
            for first in range(clip * rows, (clip + 1) * rows, tile):
                span = slice(first, first + tile)
                grad = total_grad[span]
                normed, inverse = norm_parts(wide(tokens[span]))
                back = norm_back(grad * (1.0 + scale_one), normed, inverse)
                input_grad[span] = narrow(d_resid[span] + back)
                terms = (grad, grad * normed)
                found = [old + column_sum(term) for old, term in zip(found, terms)]
            for at in range(2):
                sums[clip, at : at + 1, :] = found[at]


def run_input(d_qkv, blocks, mods, tokens, d_resid):
    total, width = tokens.shape
    clips = mods.shape[0]
    return pl.pallas_call(
        input_kernel,
        grid=(3,),
        in_specs=[
            spec((1, total, width), lambda at: (at, 0, 0)),
            spec((1, width, width), lambda at: (at, 0, 0)),
            held(mods.shape),
            held((total, width)),
            held((total, width)),
        ],
        out_specs=[held((total, width)), held((clips, 2, width))],
        out_shape=[
            jax.ShapeDtypeStruct((total, width), jnp.bfloat16),
            jax.ShapeDtypeStruct((clips, 2, width), jnp.float32),
        ],
        scratch_shapes=[pltpu.VMEM((total, width), jnp.float32)],
        compiler_params=pltpu.CompilerParams(vmem_limit_bytes=vmem_bytes),
        cost_estimate=little_cost,
    )(d_qkv, blocks, mods, tokens, d_resid)


def tie(*values):
    return lax.optimization_barrier(values)


def packed(arrays, tile):
    flat = jnp.concatenate([array.reshape(-1) for array in arrays])
    return jnp.pad(flat, (0, -flat.shape[0] % (tile * 128))).reshape(-1, 128)


def core_swap(array):
    count = lax.axis_size("dp")
    return lax.ppermute(array, "dp", [(at, at ^ 1) for at in range(count)])


def chip_shift(array, step):
    count = lax.axis_size("dp")
    return lax.ppermute(array, "dp", [(at, (at + 2 * step) % count) for at in range(count)])


def chip_swap(array, bits):
    count = lax.axis_size("dp")
    return lax.ppermute(array, "dp", [(at, at ^ (2 * bits)) for at in range(count)])


def rank_swap(array, bits):
    count = lax.axis_size("fsdp")
    return lax.ppermute(array, "fsdp", [(at, at ^ bits) for at in range(count)])


def entry(array, at, axis=0):
    return lax.dynamic_index_in_dim(array, at, axis, keepdims=False)


def place_kernel(cuts, at, *refs):
    parts, whole, held_rows, semaphores = refs[:-3], refs[-3], refs[-2], refs[-1]
    spans, loads, stores = [], [], []
    for index, (part, first, rows) in enumerate(cuts):
        spans.append(pl.ds(pl.multiple_of(at[index] * 16, 16), rows))
        source = parts[part].at[pl.ds(first, rows)]
        loads.append(
            pltpu.make_async_copy(source, held_rows.at[spans[index]], semaphores.at[0, index])
        )
        loads[index].start()
    for index, span in enumerate(spans):
        loads[index].wait()
        stores.append(
            pltpu.make_async_copy(held_rows.at[span], whole.at[span], semaphores.at[1, index])
        )
        stores[index].start()
    for store in stores:
        store.wait()


def place(parts, cuts, starts, rows):
    width = parts[0].shape[-1]
    dtype = parts[0].dtype
    return pl.pallas_call(
        functools.partial(place_kernel, cuts),
        in_specs=[pl.BlockSpec(memory_space=pltpu.SMEM)]
        + [pl.BlockSpec(memory_space=pl.ANY)] * len(parts),
        out_specs=pl.BlockSpec(memory_space=pl.ANY),
        out_shape=jax.ShapeDtypeStruct((rows, width), dtype),
        scratch_shapes=[
            pltpu.VMEM((rows, width), dtype),
            pltpu.SemaphoreType.DMA((2, len(cuts))),
        ],
        compiler_params=pltpu.CompilerParams(vmem_limit_bytes=vmem_bytes),
        cost_estimate=little_cost,
    )(stacked(starts), *parts)


def own_rows(parts, group):
    ranks, at = lax.axis_size("fsdp"), lax.axis_index("fsdp")
    shares = ranks // group
    count, _, row_part, col_part = parts.shape
    chunk = row_part // shares
    split = parts.reshape(count, group, shares, chunk, col_part).transpose(1, 2, 0, 3, 4)
    split = split.reshape(ranks, count, chunk, col_part)
    if shares > 1:
        moved = lax.all_to_all(split, "fsdp", 0, 0, tiled=True)
        (moved,) = yield (moved,)
        yield moved.transpose(1, 2, 0, 3).reshape(count, chunk, ranks * col_part)
        return
    panels = [entry(split, at)]
    panels += [rank_swap(entry(split, at ^ bits), bits) for bits in range(1, ranks)]
    panels = yield tuple(panels)
    placed = [
        lax.select_n(at, *[panels[panel ^ index] for index in range(ranks)])
        for panel in range(ranks)
    ]
    yield jnp.concatenate(placed, axis=2)


def shard_rows(split, group):
    ranks, count, chunk, col_part = split.shape
    shares = ranks // group
    moved = lax.all_to_all(split, "fsdp", 0, 0, tiled=True)
    moved = moved.reshape(group, shares, count, chunk, col_part).transpose(2, 0, 1, 3, 4)
    return moved.reshape(count, group, shares * chunk, col_part)


def gather_blocks(rows, group):
    ranks, dp_count = lax.axis_size("fsdp"), lax.axis_size("dp")
    shares = ranks // group
    chunk, total = rows.shape
    all_rows = lax.all_gather(rows, ("fsdp", "dp"), axis=0, tiled=True)
    if shares > 1:
        all_rows = all_rows.reshape(group, shares, dp_count, chunk, total).transpose(0, 2, 1, 3, 4)
    return all_rows.reshape(group, total, total)


def join_line(found):
    chips, chip = lax.axis_size("dp") // 2, lax.axis_index("dp") // 2
    chunk = found[0].shape[0]
    starts = [(chip - step) % chips * (chunk // 16) for step in range(chips)]
    return place(found, [(step, 0, chunk) for step in range(chips)], starts, chips * chunk)


def gather_second(rows, group):
    ranks, at = lax.axis_size("fsdp"), lax.axis_index("fsdp")
    total = rows.shape[-1]
    if ranks != group:
        blocks = gather_blocks(rows, group).reshape(group * total, total)
        for _ in range(3):
            (blocks,) = yield (blocks,)
        cuts = [[(0, index * total, total)] for index in range(group)]
        yield [blocks], cuts, [index * (total // 16) for index in range(group)], range(group)
        return
    chips = lax.axis_size("dp") // 2
    core = lax.axis_index("dp") % 2
    chunk, half = rows.shape[0], total // 2
    others = yield tuple(chip_shift(rows, step) for step in range(1, chips))
    line = join_line([rows, *others])
    cuts = [(side, step * chunk, chunk) for side in range(2) for step in range(chips)]
    starts = [
        (2 * step + side) * (chunk // 16) for side in (core, 1 - core) for step in range(chips)
    ]
    (own,) = yield (place([line, core_swap(line)], cuts, starts, total),)
    share = lax.dynamic_slice_in_dim(own, core * half, half, 0)
    mine = yield tuple(rank_swap(share, bits) for bits in range(1, ranks))
    parts, cuts, starts = [own], [[(0, 0, total)]], [at * (total // 16)]
    for bits in range(1, ranks):
        parts += [mine[bits - 1], core_swap(mine[bits - 1])]
        cuts.append([(2 * bits - 1, 0, half), (2 * bits, 0, half)])
        starts += [((at ^ bits) * 2 + side) * (half // 16) for side in (core, 1 - core)]
    yield parts, cuts, starts, [at ^ bits for bits in range(ranks)]


def gather_own(rows, group):
    ranks = lax.axis_size("fsdp")
    shares = ranks // group
    if shares > 1:
        sets = [[share + shares * block for share in range(shares)] for block in range(group)]
        rows = lax.all_gather(rows, "fsdp", axis=1, tiled=True, axis_index_groups=sets)
    return lax.all_gather(rows, "dp", axis=1, tiled=True)


def sum_blocks(product, cut, total, group):
    ranks, dp_count = lax.axis_size("fsdp"), lax.axis_size("dp")
    shares = ranks // group
    if shares > 1:
        blocks = narrow(product(cut(0, total)))
        chunk = total // (dp_count * shares)
        blocks = blocks.reshape(group, dp_count, shares, chunk, -1).transpose(0, 2, 1, 3, 4)
        rows = lax.psum_scatter(
            blocks.reshape(group * total, -1), ("fsdp", "dp"), scatter_dimension=0, tiled=True
        )
        for _ in range(7):
            (rows,) = yield (rows,)
        yield gather_own(rows[None], group)[0]
        return
    chips, half = dp_count // 2, total // 2
    chunk = half // chips
    core, chip = lax.axis_index("dp") % 2, lax.axis_index("dp") // 2
    low_bit, high_bit = lax.axis_index("fsdp") % 2, lax.axis_index("fsdp") // 2
    (away,) = yield (narrow(product(cut((1 - core) * half, half))),)
    (away_in,) = yield (core_swap(away),)
    here = product(cut(core * half, half))
    here = narrow(here + wide(away_in))
    here = here.reshape(2, 2, chips, chunk, -1)
    middle = chips // 2
    first, second = here[:, :, :middle], here[:, :, middle:]
    first_out, second_out = yield (entry(first, 1 - low_bit, 1), entry(second, 1 - high_bit, 0))
    first_in, second_in = yield (rank_swap(first_out, 1), rank_swap(second_out, 2))
    first = narrow(wide(entry(first, low_bit, 1)) + wide(first_in))
    second = narrow(wide(entry(second, high_bit, 0)) + wide(second_in))
    first_in = rank_swap(entry(first, 1 - high_bit), 2)
    second_in = rank_swap(entry(second, 1 - low_bit), 1)
    first_in, second_in = yield (first_in, second_in)
    first = narrow(wide(entry(first, high_bit)) + wide(first_in))
    second = narrow(wide(entry(second, low_bit)) + wide(second_in))
    line = jnp.concatenate([first, second])
    step = 1
    while step < chips:
        bit = chip // step % 2
        line = line.reshape(-1, 2, *line.shape[1:])
        (line_in,) = yield (chip_swap(entry(line, 1 - bit, 1), step),)
        line = narrow(wide(entry(line, bit, 1)) + wide(line_in))
        step *= 2
    yield lax.all_gather(line[0], "dp", axis=0, tiled=True)


def fast_dot(subscripts, left, right):
    return jnp.einsum(subscripts, left, right, preferred_element_type=jnp.float32)


def products_kernel(chips, at, gathered, left_root, right_root, out, whole, semaphores):
    chunk, width = left_root.shape
    ranks = out.shape[0]
    copies = []
    for index in range(2 * chips):
        first = (index % 2 * chips + index // 2) * chunk
        copies.append(
            pltpu.make_async_copy(
                gathered.at[pl.ds(index * chunk, chunk)],
                whole.at[pl.ds(first, chunk)],
                semaphores.at[index],
            )
        )
        copies[-1].start()
    for copy in copies:
        copy.wait()
    first = at[0] * 16
    grad = whole[...]
    picked = lax.broadcasted_iota(jnp.int32, (width, chunk), 0) - first
    picked = picked == lax.broadcasted_iota(jnp.int32, (width, chunk), 1)
    own_columns = narrow(dot_nn(grad, narrow(picked.astype(jnp.float32))))
    side_high, side_low = split_high(dot_nn(left_root[...], grad))
    right = right_root[...]
    precond = dot_nn(side_high, right) + dot_nn(side_low, right)
    outer = dot_nt(whole[pl.ds(pl.multiple_of(first, 16), chunk), :], grad)
    inner = dot_tn(own_columns, grad)
    for at_out, product in enumerate((precond, outer, inner)):
        low = narrow(product)
        for rank in range(ranks):
            span = slice(rank * (width // ranks), (rank + 1) * (width // ranks))
            out[rank, at_out] = low[:, span]


def owned_step(whole, left_root, right_root, group):
    ranks, dp_count = lax.axis_size("fsdp"), lax.axis_size("dp")
    shares = ranks // group
    chunk, total = left_root.shape
    col_part = total // ranks
    first = lax.axis_index("dp") * (chunk * shares) + lax.axis_index("fsdp") % shares * chunk
    if shares == 1:
        return pl.pallas_call(
            functools.partial(products_kernel, dp_count // 2),
            in_specs=[
                pl.BlockSpec(memory_space=pltpu.SMEM),
                pl.BlockSpec(memory_space=pl.ANY),
                pl.BlockSpec(memory_space=pltpu.VMEM),
                pl.BlockSpec(memory_space=pltpu.VMEM),
            ],
            out_specs=pl.BlockSpec(memory_space=pltpu.VMEM),
            out_shape=jax.ShapeDtypeStruct((ranks, 3, chunk, col_part), jnp.bfloat16),
            scratch_shapes=[
                pltpu.VMEM((total, total), jnp.bfloat16),
                pltpu.SemaphoreType.DMA((dp_count,)),
            ],
            compiler_params=pltpu.CompilerParams(vmem_limit_bytes=vmem_bytes),
            cost_estimate=little_cost,
        )((first // 16)[None], whole, left_root, right_root)
    grad_rows = lax.dynamic_slice_in_dim(whole, first, chunk, 0)
    own_columns = lax.dynamic_slice_in_dim(whole, first, chunk, 1)
    outer = fast_dot("rk,jk->rj", grad_rows, whole)
    inner = fast_dot("kr,kj->rj", own_columns, whole)
    side_high, side_low = split_high(fast_dot("rk,kj->rj", left_root, whole))
    precond = fast_dot("rk,kj->rj", side_high, right_root) + fast_dot(
        "rk,kj->rj", side_low, right_root
    )
    products = narrow(jnp.stack([precond, outer, inner]))
    return products.reshape(3, chunk, ranks, col_part).transpose(2, 0, 1, 3)


def per_device(
    tokens,
    conditioning,
    frame_counts,
    cotangent,
    weights,
    biases,
    momentum,
    left_stats,
    right_stats,
    left_roots,
    right_roots,
    bias_moment,
    bias_second,
):
    group = 4
    mod_count = 6
    clip_count, pos_count, frames, width = tokens.shape
    token_count = clip_count * pos_count * frames
    block_count, row_part, col_part = weights.shape
    dp_count, ranks = lax.axis_size("dp"), lax.axis_size("fsdp")
    dp_at, rank_at = lax.axis_index("dp"), lax.axis_index("fsdp")
    all_clips = clip_count * dp_count
    bias_part = biases.shape[0]
    stream = tokens.reshape(token_count, width)
    grad_out = cotangent.reshape(token_count, width)
    low_weights = narrow(weights).reshape(block_count, row_part, col_part)
    shards = low_weights[mod_count:].reshape(-1, group, row_part, col_part)

    weight_rows = own_rows(shards, group)
    weight_panels = next(weight_rows)
    cond_low = narrow(jax.nn.silu(conditioning))
    first_parts = lax.all_gather(packed([cond_low, narrow(biases)], 16), "dp", axis=0, tiled=True)
    weight_panels, first_parts = tie(weight_panels, first_parts)
    attn_rows, one_rows, two_rows = weight_rows.send(weight_panels)
    attn_w = gather_blocks(attn_rows, group)
    two_w = gather_blocks(two_rows, group).reshape(group * width, width)
    two_gathered = (
        [two_w],
        [[(0, index * width, width)] for index in range(group)],
        [index * (width // 16) for index in range(group)],
        range(group),
    )

    first_parts = first_parts.reshape(dp_count, -1)
    cond_all = first_parts[:, : clip_count * width].reshape(all_clips, width)
    bias_rows = wide(first_parts[:, clip_count * width : clip_count * width + bias_part])
    cond_rows = lax.dynamic_slice_in_dim(cond_all, dp_at * row_part, row_part, 1)
    cond_cols = wide(lax.dynamic_slice_in_dim(cond_all, rank_at * col_part, col_part, 1))
    mod_parts = fast_dot("cr,jre->cje", cond_rows, low_weights[:mod_count])
    mod_parts = lax.all_to_all(mod_parts, "dp", 0, 0, tiled=True)
    mod_parts, one_rows = tie(mod_parts, one_rows)
    one_steps = gather_second(one_rows, group)
    one_parts = next(one_steps)
    mod_cols = jnp.sum(mod_parts.reshape(dp_count, clip_count, mod_count, col_part), axis=0)
    left_cond = jnp.einsum("jrk,ck->jrc", left_roots[:mod_count], cond_cols, precision=precise)
    mod_size, bias_size = mod_cols.size, dp_count * bias_part
    second_parts = lax.all_gather(
        packed([mod_cols, bias_rows, left_cond], 8), "fsdp", axis=0, tiled=True
    )
    second_parts, one_parts = tie(second_parts, one_parts)
    one_parts = one_steps.send(one_steps.send(one_parts))
    second_parts = second_parts.reshape(ranks, -1)
    mods = second_parts[:, :mod_size].reshape(ranks, clip_count, mod_count, col_part)
    mods = mods.transpose(1, 2, 0, 3).reshape(clip_count, mod_count, width)
    bias_all = second_parts[:, mod_size : mod_size + bias_size].reshape(ranks, dp_count, bias_part)
    bias_all = bias_all.transpose(1, 0, 2).reshape(-1, width)
    left_size = mod_size + bias_size + left_cond.size
    left_cond = jnp.sum(second_parts[:, mod_size + bias_size : left_size], axis=0)
    left_cond = left_cond.reshape(mod_count, row_part, all_clips)
    mods = mods + bias_all[:mod_count]
    bias_table = jnp.concatenate(
        [bias_all[6:7], jnp.zeros((1, width), jnp.float32), bias_all[7:14]]
    )

    roots = jnp.stack([narrow(left_roots[mod_count:]), narrow(right_roots[mod_count:])])
    mods, roots = tie(mods, roots)
    root_rows = own_rows(roots.reshape(-1, group, row_part, col_part), group)
    root_panels = next(root_rows)
    attn_in, parts, mixed, proj, resid, mlp_in, d_branch, d_branch_sums = run_attention(
        frames, frame_counts, stream, grad_out, mods, bias_table, attn_w
    )
    mlp_in, one_parts = tie(mlp_in, one_parts)
    one_w, hidden, slope = run_hidden(mlp_in, one_steps.send(one_parts), bias_table[4:8, None])
    one_w = one_w.reshape(group, width, width)

    two_steps = sum_blocks(
        lambda left: fast_dot("jtd,te->jde", left, d_branch),
        lambda first, size: lax.dynamic_slice_in_dim(hidden, first, size, 2),
        width,
        group,
    )
    two_parts = next(two_steps)
    hidden, two_parts, root_panels = tie(hidden, two_parts, root_panels)
    two_parts = two_steps.send(two_parts)
    root_rows = root_rows.send(root_panels)
    hidden, root_rows = tie(hidden, root_rows)
    left_rows, right_rows = jnp.split(root_rows, 2)
    right_wholes = [gather_own(rows[None], group)[0] for rows in right_rows]
    d_pre, d_pre_sums, block_out, d_gate_two = run_branch(
        frames,
        frame_counts,
        hidden,
        slope,
        two_gathered,
        d_branch,
        bias_table[8:9],
        mods[:, 5:6],
        resid,
        grad_out,
    )
    d_pre, two_parts, right_wholes[2] = tie(d_pre, two_parts, right_wholes[2])
    two_parts = two_steps.send(two_parts)
    d_pre, two_parts = tie(d_pre, two_parts)
    two_parts = two_steps.send(two_parts)
    one_steps = sum_blocks(
        lambda left: fast_dot("td,jte->jde", left, d_pre),
        lambda first, size: lax.dynamic_slice_in_dim(mlp_in, first, size, 1),
        width,
        group,
    )
    one_parts = next(one_steps)
    d_pre, one_parts = tie(d_pre, one_parts)
    one_parts = one_steps.send(one_parts)
    d_resid, d_proj, resid_sums = run_resid(
        frames, frame_counts, d_pre, one_w, mods, resid, grad_out, proj
    )
    d_proj, one_parts, two_parts, right_wholes[1] = tie(
        d_proj, one_parts, two_parts, right_wholes[1]
    )
    two_parts = two_steps.send(two_parts)
    one_parts = one_steps.send(one_parts)
    d_proj, one_parts = tie(d_proj, one_parts)
    one_parts = one_steps.send(one_parts)
    d_heads, head_sums = run_attention_back(frames, frame_counts, d_proj, parts, attn_w)
    d_heads, two_parts, one_parts, right_wholes[0] = tie(
        d_heads, two_parts, one_parts, right_wholes[0]
    )
    two_parts = two_steps.send(two_parts)
    one_parts = one_steps.send(one_parts)
    attn_steps = sum_blocks(
        lambda left: fast_dot("jtd,jte->jde", left, d_heads),
        lambda first, size: jnp.stack(
            [lax.dynamic_slice_in_dim(left, first, size, 1) for left in (attn_in,) * 3 + (mixed,)]
        ),
        width,
        group,
    )
    attn_parts = next(attn_steps)
    d_heads, attn_parts = tie(d_heads, attn_parts)
    attn_parts = attn_steps.send(attn_parts)
    d_heads, attn_parts, two_parts = tie(d_heads, attn_parts, two_parts)
    two_parts = two_steps.send(two_parts)
    attn_parts = attn_steps.send(attn_parts)
    d_heads, attn_parts = tie(d_heads, attn_parts)
    attn_parts = attn_steps.send(attn_parts)
    input_grad, input_sums = run_input(d_heads, attn_w, mods, stream, d_resid)
    input_sums, one_parts, two_parts = tie(input_sums, one_parts, two_parts)
    whole_two = two_steps.send(two_parts)
    one_parts = one_steps.send(one_parts)
    input_sums, attn_parts, one_parts = tie(input_sums, attn_parts, one_parts)
    attn_parts = attn_steps.send(attn_parts)
    one_parts = one_steps.send(one_parts)

    d_mods = jnp.stack(
        [
            input_sums[:, 0],
            input_sums[:, 1],
            resid_sums[:, 2],
            resid_sums[:, 0],
            resid_sums[:, 1],
            d_gate_two[:, 0],
        ],
        axis=1,
    )
    head_sums = jnp.sum(head_sums, axis=0)
    grad_bias = jnp.concatenate(
        [
            jnp.sum(d_mods, axis=0),
            head_sums[0:1],
            head_sums[2:3],
            jnp.sum(resid_sums[:, 3], axis=0)[None],
            d_pre_sums[:, 0],
            jnp.sum(d_branch_sums, axis=0),
        ]
    )
    to_ranks = jnp.concatenate(
        [
            d_mods.reshape(clip_count, mod_count, ranks, col_part)
            .transpose(2, 0, 1, 3)
            .reshape(ranks, mod_size),
            grad_bias.reshape(dp_count, ranks, bias_part)
            .transpose(1, 0, 2)
            .reshape(ranks, bias_size),
        ],
        axis=1,
    )
    rank_sums = jnp.sum(lax.all_to_all(to_ranks, "fsdp", 0, 0, tiled=True), axis=0)
    rank_sums, attn_parts, one_parts = tie(rank_sums, attn_parts, one_parts)
    attn_parts = attn_steps.send(attn_parts)
    whole_one = one_steps.send(one_parts)
    to_rows = jnp.concatenate(
        [
            jnp.broadcast_to(rank_sums[None, :mod_size], (dp_count, mod_size)),
            rank_sums[mod_size:].reshape(dp_count, bias_part),
        ],
        axis=1,
    )
    from_rows = lax.all_to_all(to_rows, "dp", 0, 0, tiled=True)
    from_rows, attn_parts = tie(from_rows, attn_parts)
    attn_parts = attn_steps.send(attn_parts)
    bias_grad = jnp.sum(from_rows[:, mod_size:], axis=0)
    mod_grad_cols = from_rows[:, :mod_size].reshape(all_clips, mod_count, col_part)
    mod_grad = lax.all_gather(packed([mod_grad_cols], 8), "fsdp", axis=0, tiled=True)
    mod_grad = mod_grad.reshape(ranks, -1)[:, : mod_grad_cols.size]
    mod_grad = mod_grad.reshape(ranks, all_clips, mod_count, col_part).transpose(1, 2, 0, 3)
    mod_grad = mod_grad.reshape(all_clips, mod_count, width)

    mod_grad_rows = lax.dynamic_slice_in_dim(mod_grad, dp_at * row_part, row_part, 2)
    right_parts = jnp.einsum(
        "cjk,jke->cje", mod_grad_rows, right_roots[:mod_count], precision=precise
    )
    cond_wide = wide(cond_all)
    cond_row_wide = wide(cond_rows)
    mod_gram = jnp.einsum("cjk,bjk->jcb", mod_grad, mod_grad, precision=precise)
    cond_gram = jnp.einsum("ck,bk->cb", cond_wide, cond_wide, precision=precise)
    mod_side = jnp.einsum("jcb,be->jce", mod_gram, cond_cols, precision=precise)
    ada_left = jnp.einsum("cr,jce->jre", cond_row_wide, mod_side, precision=precise)
    cond_side = jnp.einsum("cb,bje->jce", cond_gram, mod_grad_cols, precision=precise)
    ada_right = jnp.einsum("cjr,jce->jre", mod_grad_rows, cond_side, precision=precise)

    products_two = owned_step(whole_two, left_rows[2], right_wholes[2], group)
    products_two, right_parts, attn_parts = tie(products_two, right_parts, attn_parts)
    whole_attn = attn_steps.send(attn_parts)
    back_two = shard_rows(products_two, group)
    products_one = owned_step(whole_one, left_rows[1], right_wholes[1], group)
    back_one = shard_rows(products_one, group)
    right_parts = lax.all_gather(packed([right_parts], 8), "dp", axis=0, tiled=True)
    mod_right = jnp.sum(right_parts.reshape(dp_count, -1), axis=0)[: mod_grad_cols.size]
    mod_right = mod_right.reshape(all_clips, mod_count, col_part)
    ada_pre = jnp.einsum("jrc,cje->jre", left_cond, mod_right, precision=precise)
    whole_attn, back_one, back_two, ada_pre, ada_left, ada_right = tie(
        whole_attn, back_one, back_two, ada_pre, ada_left, ada_right
    )
    back_attn = shard_rows(owned_step(whole_attn, left_rows[0], right_wholes[0], group), group)

    def joined(at, ada):
        return jnp.concatenate([ada, wide(back_attn[at]), wide(back_one[at]), wide(back_two[at])])

    precond = joined(0, ada_pre)
    left_new = stat_decay * left_stats + (1.0 - stat_decay) * joined(1, ada_left)
    right_new = stat_decay * right_stats + (1.0 - stat_decay) * joined(2, ada_right)
    momentum_new = moment_decay * momentum + precond
    weights_new = weights - weight_rate * momentum_new
    weights_copy = weights_new.astype(jnp.bfloat16)
    bias_second_new = stat_decay * bias_second + (1.0 - stat_decay) * bias_grad * bias_grad
    bias_moment_new = moment_decay * bias_moment + bias_grad * lax.rsqrt(
        bias_second_new + diag_epsilon
    )
    biases_new = biases - bias_rate * bias_moment_new
    return (
        block_out.reshape(tokens.shape),
        input_grad.reshape(tokens.shape),
        left_new,
        right_new,
        momentum_new,
        weights_new,
        weights_copy,
        bias_moment_new,
        bias_second_new,
        biases_new,
    )


def solution(mesh):
    placed = (
        P("dp", "fsdp", None, None),
        P("dp", None),
        P("dp"),
        P("dp", "fsdp", None, None),
        P(None, "dp", "fsdp"),
        P(("dp", "fsdp")),
        P(None, "dp", "fsdp"),
        P(None, "dp", "fsdp"),
        P(None, "dp", "fsdp"),
        P(None, "dp", "fsdp"),
        P(None, "dp", "fsdp"),
        P(("dp", "fsdp")),
        P(("dp", "fsdp")),
    )
    return jax.shard_map(
        per_device,
        mesh=mesh,
        in_specs=placed,
        out_specs=(
            P("dp", "fsdp", None, None),
            P("dp", "fsdp", None, None),
            P(None, "dp", "fsdp"),
            P(None, "dp", "fsdp"),
            P(None, "dp", "fsdp"),
            P(None, "dp", "fsdp"),
            P(None, "dp", "fsdp"),
            P(("dp", "fsdp")),
            P(("dp", "fsdp")),
            P(("dp", "fsdp")),
        ),
        check_vma=False,
    )
```

```python
import functools
import math

import jax
import jax.numpy as jnp
from jax import lax
from jax.experimental import pallas as pl
from jax.experimental.pallas import tpu as pltpu
from jax.sharding import PartitionSpec as P

HEADS = 16


precise = lax.Precision.HIGHEST
norm_epsilon = 1e-06
masked_score = -1e30
stat_decay = 0.5
moment_decay = 0.9
weight_rate = 0.7
bias_rate = 0.1
diag_epsilon = 1e-08
vmem_bytes = 50 * 2**20
little_cost = pl.CostEstimate(flops=1024, bytes_accessed=1024, transcendentals=0)


def narrow(array):
    return array.astype(jnp.bfloat16)


def wide(array):
    return array.astype(jnp.float32)


def spec(shape, index_map, **keywords):
    return pl.BlockSpec(shape, index_map, **keywords)


def held(shape):
    return pl.BlockSpec(shape, lambda step: (0,) * len(shape), pipeline_mode=pl.Buffered(1))


def column_cuts(total):
    cuts, at = [], 0
    while at < total:
        cuts.append((at, min(total, at + 256)))
        at += 256
    return cuts


def dot_nn(left, right):
    return lax.dot_general(left, right, (((1,), (0,)), ((), ())), preferred_element_type=jnp.float32)


def dot_nt(left, right):
    return lax.dot_general(left, right, (((1,), (1,)), ((), ())), preferred_element_type=jnp.float32)


def dot_tn(left, right):
    return lax.dot_general(left, right, (((0,), (0,)), ((), ())), preferred_element_type=jnp.float32)


def split_high(values):
    high = narrow(values)
    return high, narrow(values - wide(high))


def valid_rows(count, rows, frames):
    at = lax.broadcasted_iota(jnp.int32, (rows, 1), 0)
    return (lax.rem(at, frames) < count).astype(jnp.float32)


def score_offset(count, size, frames, key_axis):
    first = lax.broadcasted_iota(jnp.int32, (size, size), 0)
    second = lax.broadcasted_iota(jnp.int32, (size, size), 1)
    key = second if key_axis == 1 else first
    met = (lax.div(first, frames) == lax.div(second, frames)) & (lax.rem(key, frames) < count)
    return jnp.where(met, 0.0, masked_score)


def head_windows(width):
    size = width // HEADS
    windows = []
    for head in range(HEADS):
        low, high = head * size, (head + 1) * size
        start = low // 128 * 128
        stop = min(width, -(-high // 128) * 128)
        windows.append((low - start, high - start, start, stop))
    return windows


def lane_mask(low, high, count, dtype):
    lanes = lax.broadcasted_iota(jnp.int32, (1, count), 1)
    return ((lanes >= low) & (lanes < high)).astype(jnp.float32).astype(dtype)


def norm_parts(values):
    centered = values - jnp.mean(values, axis=-1, keepdims=True)
    variance = jnp.mean(centered * centered, axis=-1, keepdims=True)
    inverse = lax.rsqrt(variance + norm_epsilon)
    return centered * inverse, inverse


def norm_back(grad, normed, inverse):
    first = jnp.mean(grad, axis=-1, keepdims=True)
    second = jnp.mean(grad * normed, axis=-1, keepdims=True)
    return (grad - first - normed * second) * inverse


def column_sum(values):
    return jnp.sum(values, axis=0, keepdims=True)


def start_loads(cuts, at, parts, whole, semaphores, first_index=0):
    loads = []
    for index, (part, first, rows) in enumerate(cuts, first_index):
        span = pl.ds(pl.multiple_of(at[index] * 16, 16), rows)
        source = parts[part].at[pl.ds(first, rows)]
        loads.append(pltpu.make_async_copy(source, whole.at[span], semaphores.at[index]))
        loads[-1].start()
    return loads


def attention_kernel(
    frames,
    counts,
    tokens,
    cotangent,
    mods,
    bias,
    blocks,
    attn_in,
    parts,
    mixed_low,
    proj_out,
    resid_out,
    mlp_in,
    d_branch,
    d_branch_sum,
    mixed,
    whole,
    semaphores,
):
    rows, width = tokens.shape
    clip = pl.program_id(0)
    loads = [
        pltpu.make_async_copy(blocks.at[at], whole.at[at], semaphores.at[at]) for at in range(4)
    ]

    @pl.when(clip == 0)
    def _():
        for load in loads:
            load.start()

    tile = min(rows, 128)
    count = counts[clip]
    shift_one, scale_one, gate_one = (mods[0, at : at + 1, :] for at in range(3))
    shift_two, scale_two, gate_two = (mods[0, at : at + 1, :] for at in range(3, 6))
    for first in range(0, rows, tile):
        span = slice(first, first + tile)
        normed, _ = norm_parts(wide(tokens[span]))
        attn_in[span] = narrow(normed * (1.0 + scale_one) + shift_one)
        branch_back = narrow(wide(cotangent[span]) * valid_rows(count, tile, frames) * gate_two)
        d_branch[span] = branch_back
        part_sum = column_sum(wide(branch_back))
        d_branch_sum[0] = part_sum if first == 0 else d_branch_sum[0] + part_sum

    @pl.when(clip == 0)
    def _():
        for load in loads:
            load.wait()

    scale = (width // HEADS) ** -0.5
    source = attn_in[...]
    for low, high in column_cuts(width):
        span = slice(low, high)
        query = (dot_nn(source, whole[0, :, span]) + bias[0:1, span]) * scale
        parts[0, :, span], parts[1, :, span] = split_high(query)
        parts[2, :, span], parts[3, :, span] = split_high(dot_nn(source, whole[1, :, span]))
        parts[4, :, span] = narrow(dot_nn(source, whole[2, :, span]) + bias[2:3, span])
    offset = score_offset(count, tile, frames, 1)
    mixed[...] = jnp.zeros_like(mixed)
    for first in range(0, rows, tile):
        span = slice(first, first + tile)
        for low, high, start, stop in head_windows(width):
            lanes = slice(start, stop)
            mask = lane_mask(low, high, stop - start, jnp.bfloat16)
            key_high = parts[2, span, lanes]
            query_high = parts[0, span, lanes] * mask
            scores = dot_nt(query_high, key_high)
            scores += dot_nt(parts[1, span, lanes] * mask, key_high)
            scores += dot_nt(query_high, parts[3, span, lanes]) + offset
            expons = jnp.exp(scores - jnp.max(scores, axis=-1, keepdims=True))
            probs = expons * (1.0 / jnp.sum(expons, axis=-1, keepdims=True))
            out = dot_nn(narrow(probs), parts[4, span, lanes] * mask)
            mixed[span, lanes] += out
    mixed_low[...] = narrow(mixed[...])
    source = mixed_low[...]
    for low, high in column_cuts(width):
        span = slice(low, high)
        proj_out[:, span] = dot_nn(source, whole[3, :, span]) + bias[3:4, span]
    for first in range(0, rows, tile):
        span = slice(first, first + tile)
        resid = wide(tokens[span]) + valid_rows(count, tile, frames) * gate_one * proj_out[span]
        resid_out[span] = resid
        normed, _ = norm_parts(resid)
        mlp_in[span] = narrow(normed * (1.0 + scale_two) + shift_two)


def run_attention(frames, counts, tokens, cotangent, mods, bias, blocks):
    total, width = tokens.shape
    clips = mods.shape[0]
    rows = total // clips
    clip_rows = spec((rows, width), lambda clip: (clip, 0))
    low = jax.ShapeDtypeStruct((total, width), jnp.bfloat16)
    full = jax.ShapeDtypeStruct((total, width), jnp.float32)
    return pl.pallas_call(
        functools.partial(attention_kernel, frames),
        grid=(clips,),
        in_specs=[
            pl.BlockSpec(memory_space=pltpu.SMEM),
            clip_rows,
            clip_rows,
            spec((1,) + mods.shape[1:], lambda clip: (clip, 0, 0)),
            held(bias.shape),
            pl.BlockSpec(memory_space=pl.ANY),
        ],
        out_specs=[
            clip_rows,
            spec((5, rows, width), lambda clip: (0, clip, 0)),
            clip_rows,
            clip_rows,
            clip_rows,
            clip_rows,
            clip_rows,
            spec((1, 1, width), lambda clip: (clip, 0, 0)),
        ],
        out_shape=[
            low,
            jax.ShapeDtypeStruct((5, total, width), jnp.bfloat16),
            low,
            full,
            full,
            low,
            low,
            jax.ShapeDtypeStruct((clips, 1, width), jnp.float32),
        ],
        scratch_shapes=[
            pltpu.VMEM((rows, width), jnp.float32),
            pltpu.VMEM(blocks.shape, jnp.bfloat16),
            pltpu.SemaphoreType.DMA((4,)),
        ],
        compiler_params=pltpu.CompilerParams(vmem_limit_bytes=vmem_bytes),
        cost_estimate=little_cost,
    )(counts, tokens, cotangent, mods, bias, blocks)


def stacked(numbers):
    return jnp.stack([jnp.asarray(number, jnp.int32) for number in numbers])


def start_loads(cuts, at, parts, whole, semaphores):
    for index, (part, first, rows) in enumerate(cuts):
        span = pl.ds(pl.multiple_of(at[index] * 16, 16), rows)
        source = parts[part].at[pl.ds(first, rows)]
        pltpu.make_async_copy(source, whole.at[span], semaphores.at[index]).start()


def wait_loads(groups, at, parts, whole, semaphores):
    index = 0
    for step, cuts in enumerate(groups):
        base = index
        index += len(cuts)

        @pl.when(pl.program_id(0) == step)
        def _(cuts=cuts, base=base):
            for offset, (part, first, rows) in enumerate(cuts):
                span = pl.ds(pl.multiple_of(at[base + offset] * 16, 16), rows)
                source = parts[part].at[pl.ds(first, rows)]
                semaphore = semaphores.at[base + offset]
                pltpu.make_async_copy(source, whole.at[span], semaphore).wait()


def hidden_kernel(cuts, order, starts, mlp_in, bias, *refs):
    whole_out, hidden, slope, whole, semaphores, store_semaphores = refs[-6:]
    pieces = refs[:-6]
    step, steps = pl.program_id(0), pl.num_programs(0)
    width = mlp_in.shape[-1]
    span = pl.ds(pl.multiple_of(order[step] * width, width), width)

    @pl.when(step == 0)
    def _():
        start_loads([cut for group in cuts for cut in group], starts, pieces, whole, semaphores)

    wait_loads(cuts, starts, pieces, whole, semaphores)
    pltpu.make_async_copy(whole.at[span], whole_out.at[span], store_semaphores.at[step]).start()
    root = (2.0 / math.pi) ** 0.5
    source = mlp_in[...]
    block = whole.at[span]
    for low, high in column_cuts(width):
        lanes = slice(low, high)
        pre = dot_nn(source, block[:, lanes]) + bias[0, :, lanes]
        square = pre * pre
        bent = jnp.tanh(root * pre * (1.0 + 0.044715 * square))
        half = 0.5 + 0.5 * bent
        hidden[0, :, lanes] = narrow(pre * half)
        steep = (0.5 * root) * pre * (1.0 + 3 * 0.044715 * square)
        slope[0, :, lanes] = narrow(half + steep * (1.0 - bent * bent))

    @pl.when(step == steps - 1)
    def _():
        for at in range(len(cuts)):
            rows = pl.ds(pl.multiple_of(order[at] * width, width), width)
            pltpu.make_async_copy(
                whole.at[rows], whole_out.at[rows], store_semaphores.at[at]
            ).wait()


def run_hidden(mlp_in, gathered, bias):
    pieces, cuts, starts, order = gathered
    total, width = mlp_in.shape
    count = len(cuts)
    per_block = pl.BlockSpec((1, total, width), lambda at, order, starts: (order[at], 0, 0))
    out = jax.ShapeDtypeStruct((count, total, width), jnp.bfloat16)
    return pl.pallas_call(
        functools.partial(hidden_kernel, cuts),
        grid_spec=pltpu.PrefetchScalarGridSpec(
            num_scalar_prefetch=2,
            grid=(count,),
            in_specs=[
                pl.BlockSpec((total, width), lambda at, order, starts: (0, 0)),
                pl.BlockSpec((1, 1, width), lambda at, order, starts: (order[at], 0, 0)),
            ]
            + [pl.BlockSpec(memory_space=pl.ANY)] * len(pieces),
            out_specs=[pl.BlockSpec(memory_space=pl.ANY), per_block, per_block],
            scratch_shapes=[
                pltpu.VMEM((count * width, width), jnp.bfloat16),
                pltpu.SemaphoreType.DMA((len(starts),)),
                pltpu.SemaphoreType.DMA((count,)),
            ],
        ),
        out_shape=[jax.ShapeDtypeStruct((count * width, width), jnp.bfloat16), out, out],
        compiler_params=pltpu.CompilerParams(vmem_limit_bytes=vmem_bytes),
        cost_estimate=little_cost,
    )(stacked(order), stacked(starts), mlp_in, bias, *pieces)


def branch_kernel(
    frames,
    cuts,
    order,
    starts,
    counts,
    hidden,
    slope,
    d_branch,
    bias,
    gates,
    resid,
    cotangent,
    *refs,
):
    d_pre, d_pre_sum, block_out, d_gate, branch, whole, semaphores = refs[-7:]
    pieces = refs[:-7]
    step, steps = pl.program_id(0), pl.num_programs(0)
    total, width = resid.shape
    clips = gates.shape[0]
    rows = total // clips
    source, back = hidden[0], d_branch[...]

    @pl.when(step == 0)
    def _():
        start_loads([cut for group in cuts for cut in group], starts, pieces, whole, semaphores)
        branch[...] = jnp.zeros_like(branch)

    wait_loads(cuts, starts, pieces, whole, semaphores)
    block = whole.at[pl.ds(pl.multiple_of(order[step] * width, width), width)]
    for low, high in column_cuts(width):
        span = slice(low, high)
        d_hidden = dot_nt(back, block[span, :])
        low_back = narrow(d_hidden * wide(slope[0, :, span]))
        d_pre[0, :, span] = low_back
        d_pre_sum[0, :, span] = column_sum(wide(low_back))
        branch[:, span] += dot_nn(source, block[:, span])

    @pl.when(step == steps - 1)
    def _():
        for clip in range(clips):
            span = slice(clip * rows, (clip + 1) * rows)
            kept = valid_rows(counts[clip], rows, frames) * (branch[span] + bias[...])
            block_out[span] = narrow(resid[span] + gates[clip] * kept)
            d_gate[clip] = column_sum(wide(cotangent[span]) * kept)


def run_branch(frames, counts, hidden, slope, gathered, d_branch, bias, gates, resid, cotangent):
    pieces, cuts, starts, order = gathered
    count, total, width = hidden.shape
    clips = gates.shape[0]

    def all_of(*shape):
        return pl.BlockSpec(shape, lambda at, order, starts: (0,) * len(shape))

    per_block = pl.BlockSpec((1, total, width), lambda at, order, starts: (order[at], 0, 0))
    low = jax.ShapeDtypeStruct((total, width), jnp.bfloat16)
    return pl.pallas_call(
        functools.partial(branch_kernel, frames, cuts),
        grid_spec=pltpu.PrefetchScalarGridSpec(
            num_scalar_prefetch=2,
            grid=(count,),
            in_specs=[
                pl.BlockSpec(memory_space=pltpu.SMEM),
                per_block,
                per_block,
                all_of(total, width),
                all_of(*bias.shape),
                all_of(*gates.shape),
                all_of(total, width),
                all_of(total, width),
            ]
            + [pl.BlockSpec(memory_space=pl.ANY)] * len(pieces),
            out_specs=[
                per_block,
                pl.BlockSpec((1, 1, width), lambda at, order, starts: (order[at], 0, 0)),
                all_of(total, width),
                all_of(clips, 1, width),
            ],
            scratch_shapes=[
                pltpu.VMEM((total, width), jnp.float32),
                pltpu.VMEM((count * width, width), jnp.bfloat16),
                pltpu.SemaphoreType.DMA((len(starts),)),
            ],
        ),
        out_shape=[
            jax.ShapeDtypeStruct((count, total, width), jnp.bfloat16),
            jax.ShapeDtypeStruct((count, 1, width), jnp.float32),
            low,
            jax.ShapeDtypeStruct((clips, 1, width), jnp.float32),
        ],
        compiler_params=pltpu.CompilerParams(vmem_limit_bytes=vmem_bytes),
        cost_estimate=little_cost,
    )(stacked(order), stacked(starts), counts, hidden, slope, d_branch, bias, gates, resid, cotangent, *pieces)


def resid_kernel(
    frames,
    counts,
    d_pre,
    block,
    mods,
    resid,
    cotangent,
    proj,
    d_resid_out,
    d_proj,
    sums,
    total_grad,
):
    step, steps = pl.program_id(0), pl.num_programs(0)
    total, width = resid.shape
    clips = mods.shape[0]
    rows = total // clips
    tile = min(rows, 128)
    source = d_pre[0]

    @pl.when(step == 0)
    def _():
        total_grad[...] = jnp.zeros_like(total_grad)

    for low, high in column_cuts(width):
        span = slice(low, high)
        total_grad[:, span] += dot_nt(source, block[0, span, :])

    @pl.when(step == steps - 1)
    def _():
        for clip in range(clips):
            gate_one, scale_two = mods[clip, 2:3, :], mods[clip, 4:5, :]
            found = [0.0] * 4
            for first in range(clip * rows, (clip + 1) * rows, tile):
                span = slice(first, first + tile)
                grad = total_grad[span]
                normed, inverse = norm_parts(resid[span])
                back = norm_back(grad * (1.0 + scale_two), normed, inverse)
                d_resid = wide(cotangent[span]) + back
                d_resid_out[span] = d_resid
                kept = valid_rows(counts[clip], tile, frames) * d_resid
                low_back = narrow(kept * gate_one)
                d_proj[span] = low_back
                terms = (grad, grad * normed, kept * proj[span], wide(low_back))
                found = [old + column_sum(term) for old, term in zip(found, terms)]
            for at in range(4):
                sums[clip, at : at + 1, :] = found[at]


def run_resid(frames, counts, d_pre, blocks, mods, resid, cotangent, proj):
    count, total, width = d_pre.shape
    clips = mods.shape[0]
    return pl.pallas_call(
        functools.partial(resid_kernel, frames),
        grid=(count,),
        in_specs=[
            pl.BlockSpec(memory_space=pltpu.SMEM),
            spec((1, total, width), lambda at: (at, 0, 0)),
            spec((1, width, width), lambda at: (at, 0, 0)),
            held(mods.shape),
            held((total, width)),
            held((total, width)),
            held((total, width)),
        ],
        out_specs=[held((total, width)), held((total, width)), held((clips, 4, width))],
        out_shape=[
            jax.ShapeDtypeStruct((total, width), jnp.float32),
            jax.ShapeDtypeStruct((total, width), jnp.bfloat16),
            jax.ShapeDtypeStruct((clips, 4, width), jnp.float32),
        ],
        scratch_shapes=[pltpu.VMEM((total, width), jnp.float32)],
        compiler_params=pltpu.CompilerParams(vmem_limit_bytes=vmem_bytes),
        cost_estimate=little_cost,
    )(counts, d_pre, blocks, mods, resid, cotangent, proj)


def attention_back_kernel(
    frames, counts, d_proj, parts, block, d_qkv, sums, d_mixed, d_query, d_key, d_value
):
    rows, width = d_proj.shape
    tile = min(rows, 128)
    count = counts[pl.program_id(0)]
    source = d_proj[...]
    for low, high in column_cuts(width):
        d_mixed[:, low:high] = narrow(dot_nt(source, block[0, low:high, :]))
    scale = (width // HEADS) ** -0.5
    offset = score_offset(count, tile, frames, 0)
    for ref in (d_query, d_key, d_value):
        ref[...] = jnp.zeros_like(ref)
    for first in range(0, rows, tile):
        span = slice(first, first + tile)
        for low, high, start, stop in head_windows(width):
            lanes = slice(start, stop)
            mask = lane_mask(low, high, stop - start, jnp.bfloat16)
            query_high = parts[0, span, lanes] * mask
            key_high = parts[2, span, lanes] * mask
            back = d_mixed[span, lanes] * mask
            scores = dot_nt(key_high, query_high)
            scores += dot_nt(key_high, parts[1, span, lanes])
            scores += dot_nt(parts[3, span, lanes], query_high) + offset
            expons = jnp.exp(scores - jnp.max(scores, axis=0, keepdims=True))
            probs = expons * (1.0 / jnp.sum(expons, axis=0, keepdims=True))
            d_probs = dot_nt(parts[4, span, lanes], back)
            inner = jnp.sum(d_probs * probs, axis=0, keepdims=True)
            d_scores = narrow(probs * (d_probs - inner))
            d_value[span, lanes] += dot_nn(narrow(probs), back)
            d_key[span, lanes] += dot_nn(d_scores, query_high)
            d_query[span, lanes] += dot_tn(d_scores, key_high)
    for at, ref in enumerate((d_query, d_key, d_value)):
        low_back = narrow(ref[...] * scale) if at == 0 else narrow(ref[...])
        d_qkv[at] = low_back
        sums[0, at : at + 1, :] = column_sum(wide(low_back))
    d_qkv[3] = source


def run_attention_back(frames, counts, d_proj, parts, block):
    total, width = d_proj.shape
    clips = counts.shape[0]
    rows = total // clips
    return pl.pallas_call(
        functools.partial(attention_back_kernel, frames),
        grid=(clips,),
        in_specs=[
            pl.BlockSpec(memory_space=pltpu.SMEM),
            spec((rows, width), lambda clip: (clip, 0)),
            spec((5, rows, width), lambda clip: (0, clip, 0)),
            spec((1, width, width), lambda clip: (3, 0, 0), pipeline_mode=pl.Buffered(1)),
        ],
        out_specs=[
            spec((4, rows, width), lambda clip: (0, clip, 0)),
            spec((1, 3, width), lambda clip: (clip, 0, 0)),
        ],
        out_shape=[
            jax.ShapeDtypeStruct((4, total, width), jnp.bfloat16),
            jax.ShapeDtypeStruct((clips, 3, width), jnp.float32),
        ],
        scratch_shapes=[pltpu.VMEM((rows, width), jnp.bfloat16)]
        + [pltpu.VMEM((rows, width), jnp.float32)] * 3,
        compiler_params=pltpu.CompilerParams(vmem_limit_bytes=vmem_bytes),
        cost_estimate=little_cost,
    )(counts, d_proj, parts, block)


def input_kernel(d_qkv, block, mods, tokens, d_resid, input_grad, sums, total_grad):
    step, steps = pl.program_id(0), pl.num_programs(0)
    total, width = tokens.shape
    clips = mods.shape[0]
    rows = total // clips
    tile = min(rows, 128)
    source = d_qkv[0]

    @pl.when(step == 0)
    def _():
        total_grad[...] = jnp.zeros_like(total_grad)

    for low, high in column_cuts(width):
        span = slice(low, high)
        total_grad[:, span] += dot_nt(source, block[0, span, :])

    @pl.when(step == steps - 1)
    def _():
        for clip in range(clips):
            scale_one = mods[clip, 1:2, :]
            found = [0.0] * 2
            for first in range(clip * rows, (clip + 1) * rows, tile):
                span = slice(first, first + tile)
                grad = total_grad[span]
                normed, inverse = norm_parts(wide(tokens[span]))
                back = norm_back(grad * (1.0 + scale_one), normed, inverse)
                input_grad[span] = narrow(d_resid[span] + back)
                terms = (grad, grad * normed)
                found = [old + column_sum(term) for old, term in zip(found, terms)]
            for at in range(2):
                sums[clip, at : at + 1, :] = found[at]


def run_input(d_qkv, blocks, mods, tokens, d_resid):
    total, width = tokens.shape
    clips = mods.shape[0]
    return pl.pallas_call(
        input_kernel,
        grid=(3,),
        in_specs=[
            spec((1, total, width), lambda at: (at, 0, 0)),
            spec((1, width, width), lambda at: (at, 0, 0)),
            held(mods.shape),
            held((total, width)),
            held((total, width)),
        ],
        out_specs=[held((total, width)), held((clips, 2, width))],
        out_shape=[
            jax.ShapeDtypeStruct((total, width), jnp.bfloat16),
            jax.ShapeDtypeStruct((clips, 2, width), jnp.float32),
        ],
        scratch_shapes=[pltpu.VMEM((total, width), jnp.float32)],
        compiler_params=pltpu.CompilerParams(vmem_limit_bytes=vmem_bytes),
        cost_estimate=little_cost,
    )(d_qkv, blocks, mods, tokens, d_resid)


def tie(*values):
    return lax.optimization_barrier(values)


def packed(arrays, tile):
    flat = jnp.concatenate([array.reshape(-1) for array in arrays])
    return jnp.pad(flat, (0, -flat.shape[0] % (tile * 128))).reshape(-1, 128)


def core_swap(array):
    count = lax.axis_size("dp")
    return lax.ppermute(array, "dp", [(at, at ^ 1) for at in range(count)])


def chip_shift(array, step):
    count = lax.axis_size("dp")
    return lax.ppermute(array, "dp", [(at, (at + 2 * step) % count) for at in range(count)])


def chip_swap(array, bits):
    count = lax.axis_size("dp")
    return lax.ppermute(array, "dp", [(at, at ^ (2 * bits)) for at in range(count)])


def rank_swap(array, bits):
    count = lax.axis_size("fsdp")
    return lax.ppermute(array, "fsdp", [(at, at ^ bits) for at in range(count)])


def entry(array, at, axis=0):
    return lax.dynamic_index_in_dim(array, at, axis, keepdims=False)


def place_kernel(cuts, at, *refs):
    parts, whole, held_rows, semaphores = refs[:-3], refs[-3], refs[-2], refs[-1]
    spans, loads, stores = [], [], []
    for index, (part, first, rows) in enumerate(cuts):
        spans.append(pl.ds(pl.multiple_of(at[index] * 16, 16), rows))
        source = parts[part].at[pl.ds(first, rows)]
        loads.append(
            pltpu.make_async_copy(source, held_rows.at[spans[index]], semaphores.at[0, index])
        )
        loads[index].start()
    for index, span in enumerate(spans):
        loads[index].wait()
        stores.append(
            pltpu.make_async_copy(held_rows.at[span], whole.at[span], semaphores.at[1, index])
        )
        stores[index].start()
    for store in stores:
        store.wait()


def place(parts, cuts, starts, rows):
    width = parts[0].shape[-1]
    dtype = parts[0].dtype
    return pl.pallas_call(
        functools.partial(place_kernel, cuts),
        in_specs=[pl.BlockSpec(memory_space=pltpu.SMEM)]
        + [pl.BlockSpec(memory_space=pl.ANY)] * len(parts),
        out_specs=pl.BlockSpec(memory_space=pl.ANY),
        out_shape=jax.ShapeDtypeStruct((rows, width), dtype),
        scratch_shapes=[
            pltpu.VMEM((rows, width), dtype),
            pltpu.SemaphoreType.DMA((2, len(cuts))),
        ],
        compiler_params=pltpu.CompilerParams(vmem_limit_bytes=vmem_bytes),
        cost_estimate=little_cost,
    )(stacked(starts), *parts)


def own_rows(parts, group):
    ranks, at = lax.axis_size("fsdp"), lax.axis_index("fsdp")
    shares = ranks // group
    count, _, row_part, col_part = parts.shape
    chunk = row_part // shares
    split = parts.reshape(count, group, shares, chunk, col_part).transpose(1, 2, 0, 3, 4)
    split = split.reshape(ranks, count, chunk, col_part)
    if shares > 1:
        moved = lax.all_to_all(split, "fsdp", 0, 0, tiled=True)
        (moved,) = yield (moved,)
        yield moved.transpose(1, 2, 0, 3).reshape(count, chunk, ranks * col_part)
        return
    panels = [entry(split, at)]
    panels += [rank_swap(entry(split, at ^ bits), bits) for bits in range(1, ranks)]
    panels = yield tuple(panels)
    placed = [
        lax.select_n(at, *[panels[panel ^ index] for index in range(ranks)])
        for panel in range(ranks)
    ]
    yield jnp.concatenate(placed, axis=2)


def shard_rows(split, group):
    ranks, count, chunk, col_part = split.shape
    shares = ranks // group
    moved = lax.all_to_all(split, "fsdp", 0, 0, tiled=True)
    moved = moved.reshape(group, shares, count, chunk, col_part).transpose(2, 0, 1, 3, 4)
    return moved.reshape(count, group, shares * chunk, col_part)


def gather_blocks(rows, group):
    ranks, dp_count = lax.axis_size("fsdp"), lax.axis_size("dp")
    shares = ranks // group
    chunk, total = rows.shape
    all_rows = lax.all_gather(rows, ("fsdp", "dp"), axis=0, tiled=True)
    if shares > 1:
        all_rows = all_rows.reshape(group, shares, dp_count, chunk, total).transpose(0, 2, 1, 3, 4)
    return all_rows.reshape(group, total, total)


def join_line(found):
    chips, chip = lax.axis_size("dp") // 2, lax.axis_index("dp") // 2
    chunk = found[0].shape[0]
    starts = [(chip - step) % chips * (chunk // 16) for step in range(chips)]
    return place(found, [(step, 0, chunk) for step in range(chips)], starts, chips * chunk)


def gather_second(rows, group):
    ranks, at = lax.axis_size("fsdp"), lax.axis_index("fsdp")
    total = rows.shape[-1]
    if ranks != group:
        blocks = gather_blocks(rows, group).reshape(group * total, total)
        for _ in range(3):
            (blocks,) = yield (blocks,)
        cuts = [[(0, index * total, total)] for index in range(group)]
        yield [blocks], cuts, [index * (total // 16) for index in range(group)], range(group)
        return
    chips = lax.axis_size("dp") // 2
    core = lax.axis_index("dp") % 2
    chunk, half = rows.shape[0], total // 2
    others = yield tuple(chip_shift(rows, step) for step in range(1, chips))
    line = join_line([rows, *others])
    cuts = [(side, step * chunk, chunk) for side in range(2) for step in range(chips)]
    starts = [
        (2 * step + side) * (chunk // 16) for side in (core, 1 - core) for step in range(chips)
    ]
    (own,) = yield (place([line, core_swap(line)], cuts, starts, total),)
    share = lax.dynamic_slice_in_dim(own, core * half, half, 0)
    mine = yield tuple(rank_swap(share, bits) for bits in range(1, ranks))
    parts, cuts, starts = [own], [[(0, 0, total)]], [at * (total // 16)]
    for bits in range(1, ranks):
        parts += [mine[bits - 1], core_swap(mine[bits - 1])]
        cuts.append([(2 * bits - 1, 0, half), (2 * bits, 0, half)])
        starts += [((at ^ bits) * 2 + side) * (half // 16) for side in (core, 1 - core)]
    yield parts, cuts, starts, [at ^ bits for bits in range(ranks)]


def gather_own(rows, group):
    ranks = lax.axis_size("fsdp")
    shares = ranks // group
    if shares > 1:
        sets = [[share + shares * block for share in range(shares)] for block in range(group)]
        rows = lax.all_gather(rows, "fsdp", axis=1, tiled=True, axis_index_groups=sets)
    return lax.all_gather(rows, "dp", axis=1, tiled=True)


def sum_blocks(product, cut, total, group):
    ranks, dp_count = lax.axis_size("fsdp"), lax.axis_size("dp")
    shares = ranks // group
    if shares > 1:
        blocks = narrow(product(cut(0, total)))
        chunk = total // (dp_count * shares)
        blocks = blocks.reshape(group, dp_count, shares, chunk, -1).transpose(0, 2, 1, 3, 4)
        rows = lax.psum_scatter(
            blocks.reshape(group * total, -1), ("fsdp", "dp"), scatter_dimension=0, tiled=True
        )
        for _ in range(7):
            (rows,) = yield (rows,)
        yield gather_own(rows[None], group)[0]
        return
    chips, half = dp_count // 2, total // 2
    chunk = half // chips
    core, chip = lax.axis_index("dp") % 2, lax.axis_index("dp") // 2
    low_bit, high_bit = lax.axis_index("fsdp") % 2, lax.axis_index("fsdp") // 2
    (away,) = yield (narrow(product(cut((1 - core) * half, half))),)
    (away_in,) = yield (core_swap(away),)
    here = product(cut(core * half, half))
    here = narrow(here + wide(away_in))
    here = here.reshape(2, 2, chips, chunk, -1)
    middle = chips // 2
    first, second = here[:, :, :middle], here[:, :, middle:]
    first_out, second_out = yield (entry(first, 1 - low_bit, 1), entry(second, 1 - high_bit, 0))
    first_in, second_in = yield (rank_swap(first_out, 1), rank_swap(second_out, 2))
    first = narrow(wide(entry(first, low_bit, 1)) + wide(first_in))
    second = narrow(wide(entry(second, high_bit, 0)) + wide(second_in))
    first_in = rank_swap(entry(first, 1 - high_bit), 2)
    second_in = rank_swap(entry(second, 1 - low_bit), 1)
    first_in, second_in = yield (first_in, second_in)
    first = narrow(wide(entry(first, high_bit)) + wide(first_in))
    second = narrow(wide(entry(second, low_bit)) + wide(second_in))
    line = jnp.concatenate([first, second])
    step = 1
    while step < chips:
        bit = chip // step % 2
        line = line.reshape(-1, 2, *line.shape[1:])
        (line_in,) = yield (chip_swap(entry(line, 1 - bit, 1), step),)
        line = narrow(wide(entry(line, bit, 1)) + wide(line_in))
        step *= 2
    yield lax.all_gather(line[0], "dp", axis=0, tiled=True)


def fast_dot(subscripts, left, right):
    return jnp.einsum(subscripts, left, right, preferred_element_type=jnp.float32)


def products_kernel(chips, at, gathered, left_root, right_root, out, whole, semaphores):
    chunk, width = left_root.shape
    ranks = out.shape[0]
    copies = []
    for index in range(2 * chips):
        first = (index % 2 * chips + index // 2) * chunk
        copies.append(
            pltpu.make_async_copy(
                gathered.at[pl.ds(index * chunk, chunk)],
                whole.at[pl.ds(first, chunk)],
                semaphores.at[index],
            )
        )
        copies[-1].start()
    for copy in copies:
        copy.wait()
    first = at[0] * 16
    grad = whole[...]
    picked = lax.broadcasted_iota(jnp.int32, (width, chunk), 0) - first
    picked = picked == lax.broadcasted_iota(jnp.int32, (width, chunk), 1)
    own_columns = narrow(dot_nn(grad, narrow(picked.astype(jnp.float32))))
    side_high, side_low = split_high(dot_nn(left_root[...], grad))
    right = right_root[...]
    precond = dot_nn(side_high, right) + dot_nn(side_low, right)
    outer = dot_nt(whole[pl.ds(pl.multiple_of(first, 16), chunk), :], grad)
    inner = dot_tn(own_columns, grad)
    for at_out, product in enumerate((precond, outer, inner)):
        low = narrow(product)
        for rank in range(ranks):
            span = slice(rank * (width // ranks), (rank + 1) * (width // ranks))
            out[rank, at_out] = low[:, span]


def owned_step(whole, left_root, right_root, group):
    ranks, dp_count = lax.axis_size("fsdp"), lax.axis_size("dp")
    shares = ranks // group
    chunk, total = left_root.shape
    col_part = total // ranks
    first = lax.axis_index("dp") * (chunk * shares) + lax.axis_index("fsdp") % shares * chunk
    if shares == 1:
        return pl.pallas_call(
            functools.partial(products_kernel, dp_count // 2),
            in_specs=[
                pl.BlockSpec(memory_space=pltpu.SMEM),
                pl.BlockSpec(memory_space=pl.ANY),
                pl.BlockSpec(memory_space=pltpu.VMEM),
                pl.BlockSpec(memory_space=pltpu.VMEM),
            ],
            out_specs=pl.BlockSpec(memory_space=pltpu.VMEM),
            out_shape=jax.ShapeDtypeStruct((ranks, 3, chunk, col_part), jnp.bfloat16),
            scratch_shapes=[
                pltpu.VMEM((total, total), jnp.bfloat16),
                pltpu.SemaphoreType.DMA((dp_count,)),
            ],
            compiler_params=pltpu.CompilerParams(vmem_limit_bytes=vmem_bytes),
            cost_estimate=little_cost,
        )((first // 16)[None], whole, left_root, right_root)
    grad_rows = lax.dynamic_slice_in_dim(whole, first, chunk, 0)
    own_columns = lax.dynamic_slice_in_dim(whole, first, chunk, 1)
    outer = fast_dot("rk,jk->rj", grad_rows, whole)
    inner = fast_dot("kr,kj->rj", own_columns, whole)
    side_high, side_low = split_high(fast_dot("rk,kj->rj", left_root, whole))
    precond = fast_dot("rk,kj->rj", side_high, right_root) + fast_dot(
        "rk,kj->rj", side_low, right_root
    )
    products = narrow(jnp.stack([precond, outer, inner]))
    return products.reshape(3, chunk, ranks, col_part).transpose(2, 0, 1, 3)


def per_device(
    tokens,
    conditioning,
    frame_counts,
    cotangent,
    weights,
    biases,
    momentum,
    left_stats,
    right_stats,
    left_roots,
    right_roots,
    bias_moment,
    bias_second,
):
    group = 4
    mod_count = 6
    clip_count, pos_count, frames, width = tokens.shape
    token_count = clip_count * pos_count * frames
    block_count, row_part, col_part = weights.shape
    dp_count, ranks = lax.axis_size("dp"), lax.axis_size("fsdp")
    dp_at, rank_at = lax.axis_index("dp"), lax.axis_index("fsdp")
    all_clips = clip_count * dp_count
    bias_part = biases.shape[0]
    stream = tokens.reshape(token_count, width)
    grad_out = cotangent.reshape(token_count, width)
    low_weights = narrow(weights).reshape(block_count, row_part, col_part)
    shards = low_weights[mod_count:].reshape(-1, group, row_part, col_part)

    weight_rows = own_rows(shards, group)
    weight_panels = next(weight_rows)
    cond_low = narrow(jax.nn.silu(conditioning))
    first_parts = lax.all_gather(packed([cond_low, narrow(biases)], 16), "dp", axis=0, tiled=True)
    weight_panels, first_parts = tie(weight_panels, first_parts)
    attn_rows, one_rows, two_rows = weight_rows.send(weight_panels)
    attn_w = gather_blocks(attn_rows, group)
    two_w = gather_blocks(two_rows, group).reshape(group * width, width)
    two_gathered = (
        [two_w],
        [[(0, index * width, width)] for index in range(group)],
        [index * (width // 16) for index in range(group)],
        range(group),
    )

    first_parts = first_parts.reshape(dp_count, -1)
    cond_all = first_parts[:, : clip_count * width].reshape(all_clips, width)
    bias_rows = wide(first_parts[:, clip_count * width : clip_count * width + bias_part])
    cond_rows = lax.dynamic_slice_in_dim(cond_all, dp_at * row_part, row_part, 1)
    cond_cols = wide(lax.dynamic_slice_in_dim(cond_all, rank_at * col_part, col_part, 1))
    mod_parts = fast_dot("cr,jre->cje", cond_rows, low_weights[:mod_count])
    mod_parts = lax.all_to_all(mod_parts, "dp", 0, 0, tiled=True)
    mod_parts, one_rows = tie(mod_parts, one_rows)
    one_steps = gather_second(one_rows, group)
    one_parts = next(one_steps)
    mod_cols = jnp.sum(mod_parts.reshape(dp_count, clip_count, mod_count, col_part), axis=0)
    left_cond = jnp.einsum("jrk,ck->jrc", left_roots[:mod_count], cond_cols, precision=precise)
    mod_size, bias_size = mod_cols.size, dp_count * bias_part
    second_parts = lax.all_gather(
        packed([mod_cols, bias_rows, left_cond], 8), "fsdp", axis=0, tiled=True
    )
    second_parts, one_parts = tie(second_parts, one_parts)
    one_parts, attn_w = tie(one_steps.send(one_parts), attn_w)
    one_parts = one_steps.send(one_parts)
    second_parts = second_parts.reshape(ranks, -1)
    mods = second_parts[:, :mod_size].reshape(ranks, clip_count, mod_count, col_part)
    mods = mods.transpose(1, 2, 0, 3).reshape(clip_count, mod_count, width)
    bias_all = second_parts[:, mod_size : mod_size + bias_size].reshape(ranks, dp_count, bias_part)
    bias_all = bias_all.transpose(1, 0, 2).reshape(-1, width)
    left_size = mod_size + bias_size + left_cond.size
    left_cond = jnp.sum(second_parts[:, mod_size + bias_size : left_size], axis=0)
    left_cond = left_cond.reshape(mod_count, row_part, all_clips)
    mods = mods + bias_all[:mod_count]
    bias_table = jnp.concatenate(
        [bias_all[6:7], jnp.zeros((1, width), jnp.float32), bias_all[7:14]]
    )

    attn_in, parts, mixed, proj, resid, mlp_in, d_branch, d_branch_sums = run_attention(
        frames, frame_counts, stream, grad_out, mods, bias_table, attn_w
    )
    mlp_in, one_parts = tie(mlp_in, one_parts)
    one_w, hidden, slope = run_hidden(mlp_in, one_steps.send(one_parts), bias_table[4:8, None])
    one_w = one_w.reshape(group, width, width)

    two_steps = sum_blocks(
        lambda left: fast_dot("jtd,te->jde", left, d_branch),
        lambda first, size: lax.dynamic_slice_in_dim(hidden, first, size, 2),
        width,
        group,
    )
    two_parts = next(two_steps)
    roots = jnp.stack([narrow(left_roots[mod_count:]), narrow(right_roots[mod_count:])])
    hidden, two_parts, roots = tie(hidden, two_parts, roots)
    two_parts = two_steps.send(two_parts)
    root_rows = own_rows(roots.reshape(-1, group, row_part, col_part), group)
    root_panels = next(root_rows)
    d_pre, d_pre_sums, block_out, d_gate_two = run_branch(
        frames,
        frame_counts,
        hidden,
        slope,
        two_gathered,
        d_branch,
        bias_table[8:9],
        mods[:, 5:6],
        resid,
        grad_out,
    )
    d_pre, two_parts, root_panels = tie(d_pre, two_parts, root_panels)
    two_parts = two_steps.send(two_parts)
    root_rows = root_rows.send(root_panels)
    d_pre, two_parts, root_rows = tie(d_pre, two_parts, root_rows)
    two_parts = two_steps.send(two_parts)
    left_rows, right_rows = jnp.split(root_rows, 2)
    right_wholes = [gather_own(rows[None], group)[0] for rows in right_rows]
    one_steps = sum_blocks(
        lambda left: fast_dot("td,jte->jde", left, d_pre),
        lambda first, size: lax.dynamic_slice_in_dim(mlp_in, first, size, 1),
        width,
        group,
    )
    one_parts = next(one_steps)
    d_pre, one_parts = tie(d_pre, one_parts)
    one_parts = one_steps.send(one_parts)
    d_resid, d_proj, resid_sums = run_resid(
        frames, frame_counts, d_pre, one_w, mods, resid, grad_out, proj
    )
    d_proj, one_parts, two_parts = tie(d_proj, one_parts, two_parts)
    two_parts = two_steps.send(two_parts)
    one_parts = one_steps.send(one_parts)
    d_proj, one_parts, right_wholes[2] = tie(d_proj, one_parts, right_wholes[2])
    one_parts = one_steps.send(one_parts)
    d_heads, head_sums = run_attention_back(frames, frame_counts, d_proj, parts, attn_w)
    d_heads, two_parts, one_parts, right_wholes[1] = tie(
        d_heads, two_parts, one_parts, right_wholes[1]
    )
    two_parts = two_steps.send(two_parts)
    one_parts = one_steps.send(one_parts)
    attn_steps = sum_blocks(
        lambda left: fast_dot("jtd,jte->jde", left, d_heads),
        lambda first, size: jnp.stack(
            [lax.dynamic_slice_in_dim(left, first, size, 1) for left in (attn_in,) * 3 + (mixed,)]
        ),
        width,
        group,
    )
    attn_parts = next(attn_steps)
    d_heads, attn_parts = tie(d_heads, attn_parts)
    attn_parts = attn_steps.send(attn_parts)
    d_heads, attn_parts, two_parts = tie(d_heads, attn_parts, two_parts)
    two_parts = two_steps.send(two_parts)
    attn_parts = attn_steps.send(attn_parts)
    d_heads, attn_parts = tie(d_heads, attn_parts)
    attn_parts = attn_steps.send(attn_parts)
    input_grad, input_sums = run_input(d_heads, attn_w, mods, stream, d_resid)
    input_sums, one_parts, two_parts, right_wholes[0] = tie(
        input_sums, one_parts, two_parts, right_wholes[0]
    )
    whole_two = two_steps.send(two_parts)
    one_parts = one_steps.send(one_parts)

    d_mods = jnp.stack(
        [
            input_sums[:, 0],
            input_sums[:, 1],
            resid_sums[:, 2],
            resid_sums[:, 0],
            resid_sums[:, 1],
            d_gate_two[:, 0],
        ],
        axis=1,
    )
    head_sums = jnp.sum(head_sums, axis=0)
    grad_bias = jnp.concatenate(
        [
            jnp.sum(d_mods, axis=0),
            head_sums[0:1],
            head_sums[2:3],
            jnp.sum(resid_sums[:, 3], axis=0)[None],
            d_pre_sums[:, 0],
            jnp.sum(d_branch_sums, axis=0),
        ]
    )
    to_ranks = jnp.concatenate(
        [
            d_mods.reshape(clip_count, mod_count, ranks, col_part)
            .transpose(2, 0, 1, 3)
            .reshape(ranks, mod_size),
            grad_bias.reshape(dp_count, ranks, bias_part)
            .transpose(1, 0, 2)
            .reshape(ranks, bias_size),
        ],
        axis=1,
    )
    rank_sums = lax.all_to_all(to_ranks, "fsdp", 0, 0, tiled=True)
    rank_sums, attn_parts, one_parts = tie(rank_sums, attn_parts, one_parts)
    attn_parts = attn_steps.send(attn_parts)
    one_parts = one_steps.send(one_parts)
    rank_sums = jnp.sum(rank_sums, axis=0)
    to_rows = jnp.concatenate(
        [
            jnp.broadcast_to(rank_sums[None, :mod_size], (dp_count, mod_size)),
            rank_sums[mod_size:].reshape(dp_count, bias_part),
        ],
        axis=1,
    )
    from_rows = lax.all_to_all(to_rows, "dp", 0, 0, tiled=True)
    from_rows, attn_parts, one_parts = tie(from_rows, attn_parts, one_parts)
    attn_parts = attn_steps.send(attn_parts)
    whole_one = one_steps.send(one_parts)
    bias_grad = jnp.sum(from_rows[:, mod_size:], axis=0)
    mod_grad_cols = from_rows[:, :mod_size].reshape(all_clips, mod_count, col_part)
    mod_grad = lax.all_gather(packed([mod_grad_cols], 8), "fsdp", axis=0, tiled=True)
    mod_grad, attn_parts = tie(mod_grad, attn_parts)
    attn_parts = attn_steps.send(attn_parts)
    mod_grad = mod_grad.reshape(ranks, -1)[:, : mod_grad_cols.size]
    mod_grad = mod_grad.reshape(ranks, all_clips, mod_count, col_part).transpose(1, 2, 0, 3)
    mod_grad = mod_grad.reshape(all_clips, mod_count, width)

    mod_grad_rows = lax.dynamic_slice_in_dim(mod_grad, dp_at * row_part, row_part, 2)
    right_parts = jnp.einsum(
        "cjk,jke->cje", mod_grad_rows, right_roots[:mod_count], precision=precise
    )
    cond_wide = wide(cond_all)
    cond_row_wide = wide(cond_rows)
    mod_gram = jnp.einsum("cjk,bjk->jcb", mod_grad, mod_grad, precision=precise)
    cond_gram = jnp.einsum("ck,bk->cb", cond_wide, cond_wide, precision=precise)
    mod_side = jnp.einsum("jcb,be->jce", mod_gram, cond_cols, precision=precise)
    ada_left = jnp.einsum("cr,jce->jre", cond_row_wide, mod_side, precision=precise)
    cond_side = jnp.einsum("cb,bje->jce", cond_gram, mod_grad_cols, precision=precise)
    ada_right = jnp.einsum("cjr,jce->jre", mod_grad_rows, cond_side, precision=precise)

    products_two = owned_step(whole_two, left_rows[2], right_wholes[2], group)
    products_two, right_parts, attn_parts = tie(products_two, right_parts, attn_parts)
    whole_attn = attn_steps.send(attn_parts)
    back_two = shard_rows(products_two, group)
    products_one = owned_step(whole_one, left_rows[1], right_wholes[1], group)
    back_one = shard_rows(products_one, group)
    right_parts = lax.all_gather(packed([right_parts], 8), "dp", axis=0, tiled=True)
    mod_right = jnp.sum(right_parts.reshape(dp_count, -1), axis=0)[: mod_grad_cols.size]
    mod_right = mod_right.reshape(all_clips, mod_count, col_part)
    ada_pre = jnp.einsum("jrc,cje->jre", left_cond, mod_right, precision=precise)
    whole_attn, back_one, back_two, ada_pre, ada_left, ada_right = tie(
        whole_attn, back_one, back_two, ada_pre, ada_left, ada_right
    )
    back_attn = shard_rows(owned_step(whole_attn, left_rows[0], right_wholes[0], group), group)

    def joined(at, ada):
        return jnp.concatenate([ada, wide(back_attn[at]), wide(back_one[at]), wide(back_two[at])])

    precond = joined(0, ada_pre)
    left_new = stat_decay * left_stats + (1.0 - stat_decay) * joined(1, ada_left)
    right_new = stat_decay * right_stats + (1.0 - stat_decay) * joined(2, ada_right)
    momentum_new = moment_decay * momentum + precond
    weights_new = weights - weight_rate * momentum_new
    weights_copy = weights_new.astype(jnp.bfloat16)
    bias_second_new = stat_decay * bias_second + (1.0 - stat_decay) * bias_grad * bias_grad
    bias_moment_new = moment_decay * bias_moment + bias_grad * lax.rsqrt(
        bias_second_new + diag_epsilon
    )
    biases_new = biases - bias_rate * bias_moment_new
    return (
        block_out.reshape(tokens.shape),
        input_grad.reshape(tokens.shape),
        left_new,
        right_new,
        momentum_new,
        weights_new,
        weights_copy,
        bias_moment_new,
        bias_second_new,
        biases_new,
    )


def solution(mesh):
    placed = (
        P("dp", "fsdp", None, None),
        P("dp", None),
        P("dp"),
        P("dp", "fsdp", None, None),
        P(None, "dp", "fsdp"),
        P(("dp", "fsdp")),
        P(None, "dp", "fsdp"),
        P(None, "dp", "fsdp"),
        P(None, "dp", "fsdp"),
        P(None, "dp", "fsdp"),
        P(None, "dp", "fsdp"),
        P(("dp", "fsdp")),
        P(("dp", "fsdp")),
    )
    return jax.shard_map(
        per_device,
        mesh=mesh,
        in_specs=placed,
        out_specs=(
            P("dp", "fsdp", None, None),
            P("dp", "fsdp", None, None),
            P(None, "dp", "fsdp"),
            P(None, "dp", "fsdp"),
            P(None, "dp", "fsdp"),
            P(None, "dp", "fsdp"),
            P(None, "dp", "fsdp"),
            P(("dp", "fsdp")),
            P(("dp", "fsdp")),
            P(("dp", "fsdp")),
        ),
        check_vma=False,
    )
```

```python
import functools
import math

import jax
import jax.numpy as jnp
from jax import lax
from jax.experimental import pallas as pl
from jax.experimental.pallas import tpu as pltpu
from jax.sharding import PartitionSpec as P

HEADS = 16


precise = lax.Precision.HIGHEST
norm_epsilon = 1e-06
masked_score = -1e30
stat_decay = 0.5
moment_decay = 0.9
weight_rate = 0.7
bias_rate = 0.1
diag_epsilon = 1e-08
vmem_bytes = 50 * 2**20
little_cost = pl.CostEstimate(flops=1024, bytes_accessed=1024, transcendentals=0)


def narrow(array):
    return array.astype(jnp.bfloat16)


def wide(array):
    return array.astype(jnp.float32)


def spec(shape, index_map, **keywords):
    return pl.BlockSpec(shape, index_map, **keywords)


def held(shape):
    return pl.BlockSpec(shape, lambda step: (0,) * len(shape), pipeline_mode=pl.Buffered(1))


def column_cuts(total):
    cuts, at = [], 0
    while at < total:
        cuts.append((at, min(total, at + 256)))
        at += 256
    return cuts


def dot_nn(left, right):
    return lax.dot_general(left, right, (((1,), (0,)), ((), ())), preferred_element_type=jnp.float32)


def dot_nt(left, right):
    return lax.dot_general(left, right, (((1,), (1,)), ((), ())), preferred_element_type=jnp.float32)


def dot_tn(left, right):
    return lax.dot_general(left, right, (((0,), (0,)), ((), ())), preferred_element_type=jnp.float32)


def split_high(values):
    high = narrow(values)
    return high, narrow(values - wide(high))


def valid_rows(count, rows, frames):
    at = lax.broadcasted_iota(jnp.int32, (rows, 1), 0)
    return (lax.rem(at, frames) < count).astype(jnp.float32)


def score_offset(count, size, frames, key_axis):
    first = lax.broadcasted_iota(jnp.int32, (size, size), 0)
    second = lax.broadcasted_iota(jnp.int32, (size, size), 1)
    key = second if key_axis == 1 else first
    met = (lax.div(first, frames) == lax.div(second, frames)) & (lax.rem(key, frames) < count)
    return jnp.where(met, 0.0, masked_score)


def head_windows(width):
    size = width // HEADS
    windows = []
    for head in range(HEADS):
        low, high = head * size, (head + 1) * size
        start = low // 128 * 128
        stop = min(width, -(-high // 128) * 128)
        windows.append((low - start, high - start, start, stop))
    return windows


def lane_mask(low, high, count, dtype):
    lanes = lax.broadcasted_iota(jnp.int32, (1, count), 1)
    return ((lanes >= low) & (lanes < high)).astype(jnp.float32).astype(dtype)


def norm_parts(values):
    centered = values - jnp.mean(values, axis=-1, keepdims=True)
    variance = jnp.mean(centered * centered, axis=-1, keepdims=True)
    inverse = lax.rsqrt(variance + norm_epsilon)
    return centered * inverse, inverse


def norm_back(grad, normed, inverse):
    first = jnp.mean(grad, axis=-1, keepdims=True)
    second = jnp.mean(grad * normed, axis=-1, keepdims=True)
    return (grad - first - normed * second) * inverse


def column_sum(values):
    return jnp.sum(values, axis=0, keepdims=True)


def start_loads(cuts, at, parts, whole, semaphores, first_index=0):
    loads = []
    for index, (part, first, rows) in enumerate(cuts, first_index):
        span = pl.ds(pl.multiple_of(at[index] * 16, 16), rows)
        source = parts[part].at[pl.ds(first, rows)]
        loads.append(pltpu.make_async_copy(source, whole.at[span], semaphores.at[index]))
        loads[-1].start()
    return loads


def attention_kernel(
    frames,
    counts,
    tokens,
    cotangent,
    mods,
    bias,
    blocks,
    attn_in,
    parts,
    mixed_low,
    proj_out,
    resid_out,
    mlp_in,
    d_branch,
    d_branch_sum,
    mixed,
    whole,
    semaphores,
):
    rows, width = tokens.shape
    clip = pl.program_id(0)
    loads = [
        pltpu.make_async_copy(blocks.at[at], whole.at[at], semaphores.at[at]) for at in range(4)
    ]

    @pl.when(clip == 0)
    def _():
        for load in loads:
            load.start()

    tile = min(rows, 128)
    count = counts[clip]
    shift_one, scale_one, gate_one = (mods[0, at : at + 1, :] for at in range(3))
    shift_two, scale_two, gate_two = (mods[0, at : at + 1, :] for at in range(3, 6))
    for first in range(0, rows, tile):
        span = slice(first, first + tile)
        normed, _ = norm_parts(wide(tokens[span]))
        attn_in[span] = narrow(normed * (1.0 + scale_one) + shift_one)
        branch_back = narrow(wide(cotangent[span]) * valid_rows(count, tile, frames) * gate_two)
        d_branch[span] = branch_back
        part_sum = column_sum(wide(branch_back))
        d_branch_sum[0] = part_sum if first == 0 else d_branch_sum[0] + part_sum

    @pl.when(clip == 0)
    def _():
        for load in loads:
            load.wait()

    scale = (width // HEADS) ** -0.5
    source = attn_in[...]
    for low, high in column_cuts(width):
        span = slice(low, high)
        query = (dot_nn(source, whole[0, :, span]) + bias[0:1, span]) * scale
        parts[0, :, span], parts[1, :, span] = split_high(query)
        parts[2, :, span], parts[3, :, span] = split_high(dot_nn(source, whole[1, :, span]))
        parts[4, :, span] = narrow(dot_nn(source, whole[2, :, span]) + bias[2:3, span])
    offset = score_offset(count, tile, frames, 1)
    mixed[...] = jnp.zeros_like(mixed)
    for first in range(0, rows, tile):
        span = slice(first, first + tile)
        for low, high, start, stop in head_windows(width):
            lanes = slice(start, stop)
            mask = lane_mask(low, high, stop - start, jnp.bfloat16)
            key_high = parts[2, span, lanes]
            query_high = parts[0, span, lanes] * mask
            scores = dot_nt(query_high, key_high)
            scores += dot_nt(parts[1, span, lanes] * mask, key_high)
            scores += dot_nt(query_high, parts[3, span, lanes]) + offset
            expons = jnp.exp(scores - jnp.max(scores, axis=-1, keepdims=True))
            probs = expons * (1.0 / jnp.sum(expons, axis=-1, keepdims=True))
            out = dot_nn(narrow(probs), parts[4, span, lanes] * mask)
            mixed[span, lanes] += out
    mixed_low[...] = narrow(mixed[...])
    source = mixed_low[...]
    for low, high in column_cuts(width):
        span = slice(low, high)
        proj_out[:, span] = dot_nn(source, whole[3, :, span]) + bias[3:4, span]
    for first in range(0, rows, tile):
        span = slice(first, first + tile)
        resid = wide(tokens[span]) + valid_rows(count, tile, frames) * gate_one * proj_out[span]
        resid_out[span] = resid
        normed, _ = norm_parts(resid)
        mlp_in[span] = narrow(normed * (1.0 + scale_two) + shift_two)


def run_attention(frames, counts, tokens, cotangent, mods, bias, blocks):
    total, width = tokens.shape
    clips = mods.shape[0]
    rows = total // clips
    clip_rows = spec((rows, width), lambda clip: (clip, 0))
    low = jax.ShapeDtypeStruct((total, width), jnp.bfloat16)
    full = jax.ShapeDtypeStruct((total, width), jnp.float32)
    return pl.pallas_call(
        functools.partial(attention_kernel, frames),
        grid=(clips,),
        in_specs=[
            pl.BlockSpec(memory_space=pltpu.SMEM),
            clip_rows,
            clip_rows,
            spec((1,) + mods.shape[1:], lambda clip: (clip, 0, 0)),
            held(bias.shape),
            pl.BlockSpec(memory_space=pl.ANY),
        ],
        out_specs=[
            clip_rows,
            spec((5, rows, width), lambda clip: (0, clip, 0)),
            clip_rows,
            clip_rows,
            clip_rows,
            clip_rows,
            clip_rows,
            spec((1, 1, width), lambda clip: (clip, 0, 0)),
        ],
        out_shape=[
            low,
            jax.ShapeDtypeStruct((5, total, width), jnp.bfloat16),
            low,
            full,
            full,
            low,
            low,
            jax.ShapeDtypeStruct((clips, 1, width), jnp.float32),
        ],
        scratch_shapes=[
            pltpu.VMEM((rows, width), jnp.float32),
            pltpu.VMEM(blocks.shape, jnp.bfloat16),
            pltpu.SemaphoreType.DMA((4,)),
        ],
        compiler_params=pltpu.CompilerParams(vmem_limit_bytes=vmem_bytes),
        cost_estimate=little_cost,
    )(counts, tokens, cotangent, mods, bias, blocks)


def stacked(numbers):
    return jnp.stack([jnp.asarray(number, jnp.int32) for number in numbers])


def start_loads(cuts, at, parts, whole, semaphores):
    for index, (part, first, rows) in enumerate(cuts):
        span = pl.ds(pl.multiple_of(at[index] * 16, 16), rows)
        source = parts[part].at[pl.ds(first, rows)]
        pltpu.make_async_copy(source, whole.at[span], semaphores.at[index]).start()


def wait_loads(groups, at, parts, whole, semaphores):
    index = 0
    for step, cuts in enumerate(groups):
        base = index
        index += len(cuts)

        @pl.when(pl.program_id(0) == step)
        def _(cuts=cuts, base=base):
            for offset, (part, first, rows) in enumerate(cuts):
                span = pl.ds(pl.multiple_of(at[base + offset] * 16, 16), rows)
                source = parts[part].at[pl.ds(first, rows)]
                semaphore = semaphores.at[base + offset]
                pltpu.make_async_copy(source, whole.at[span], semaphore).wait()


def hidden_kernel(cuts, order, starts, mlp_in, bias, *refs):
    whole_out, hidden, slope, whole, semaphores, store_semaphores = refs[-6:]
    pieces = refs[:-6]
    step, steps = pl.program_id(0), pl.num_programs(0)
    width = mlp_in.shape[-1]
    span = pl.ds(pl.multiple_of(order[step] * width, width), width)

    @pl.when(step == 0)
    def _():
        start_loads([cut for group in cuts for cut in group], starts, pieces, whole, semaphores)

    wait_loads(cuts, starts, pieces, whole, semaphores)
    pltpu.make_async_copy(whole.at[span], whole_out.at[span], store_semaphores.at[step]).start()
    root = (2.0 / math.pi) ** 0.5
    source = mlp_in[...]
    block = whole.at[span]
    for low, high in column_cuts(width):
        lanes = slice(low, high)
        pre = dot_nn(source, block[:, lanes]) + bias[0, :, lanes]
        square = pre * pre
        bent = jnp.tanh(root * pre * (1.0 + 0.044715 * square))
        half = 0.5 + 0.5 * bent
        hidden[0, :, lanes] = narrow(pre * half)
        steep = (0.5 * root) * pre * (1.0 + 3 * 0.044715 * square)
        slope[0, :, lanes] = narrow(half + steep * (1.0 - bent * bent))

    @pl.when(step == steps - 1)
    def _():
        for at in range(len(cuts)):
            rows = pl.ds(pl.multiple_of(order[at] * width, width), width)
            pltpu.make_async_copy(
                whole.at[rows], whole_out.at[rows], store_semaphores.at[at]
            ).wait()


def run_hidden(mlp_in, gathered, bias):
    pieces, cuts, starts, order = gathered
    total, width = mlp_in.shape
    count = len(cuts)
    per_block = pl.BlockSpec((1, total, width), lambda at, order, starts: (order[at], 0, 0))
    out = jax.ShapeDtypeStruct((count, total, width), jnp.bfloat16)
    return pl.pallas_call(
        functools.partial(hidden_kernel, cuts),
        grid_spec=pltpu.PrefetchScalarGridSpec(
            num_scalar_prefetch=2,
            grid=(count,),
            in_specs=[
                pl.BlockSpec((total, width), lambda at, order, starts: (0, 0)),
                pl.BlockSpec((1, 1, width), lambda at, order, starts: (order[at], 0, 0)),
            ]
            + [pl.BlockSpec(memory_space=pl.ANY)] * len(pieces),
            out_specs=[pl.BlockSpec(memory_space=pl.ANY), per_block, per_block],
            scratch_shapes=[
                pltpu.VMEM((count * width, width), jnp.bfloat16),
                pltpu.SemaphoreType.DMA((len(starts),)),
                pltpu.SemaphoreType.DMA((count,)),
            ],
        ),
        out_shape=[jax.ShapeDtypeStruct((count * width, width), jnp.bfloat16), out, out],
        compiler_params=pltpu.CompilerParams(vmem_limit_bytes=vmem_bytes),
        cost_estimate=little_cost,
    )(stacked(order), stacked(starts), mlp_in, bias, *pieces)


def branch_kernel(
    frames,
    cuts,
    order,
    starts,
    counts,
    hidden,
    slope,
    d_branch,
    bias,
    gates,
    resid,
    cotangent,
    *refs,
):
    d_pre, d_pre_sum, block_out, d_gate, branch, whole, semaphores = refs[-7:]
    pieces = refs[:-7]
    step, steps = pl.program_id(0), pl.num_programs(0)
    total, width = resid.shape
    clips = gates.shape[0]
    rows = total // clips
    source, back = hidden[0], d_branch[...]

    @pl.when(step == 0)
    def _():
        start_loads([cut for group in cuts for cut in group], starts, pieces, whole, semaphores)
        branch[...] = jnp.zeros_like(branch)

    wait_loads(cuts, starts, pieces, whole, semaphores)
    block = whole.at[pl.ds(pl.multiple_of(order[step] * width, width), width)]
    for low, high in column_cuts(width):
        span = slice(low, high)
        d_hidden = dot_nt(back, block[span, :])
        low_back = narrow(d_hidden * wide(slope[0, :, span]))
        d_pre[0, :, span] = low_back
        d_pre_sum[0, :, span] = column_sum(wide(low_back))
        branch[:, span] += dot_nn(source, block[:, span])

    @pl.when(step == steps - 1)
    def _():
        for clip in range(clips):
            span = slice(clip * rows, (clip + 1) * rows)
            kept = valid_rows(counts[clip], rows, frames) * (branch[span] + bias[...])
            block_out[span] = narrow(resid[span] + gates[clip] * kept)
            d_gate[clip] = column_sum(wide(cotangent[span]) * kept)


def run_branch(frames, counts, hidden, slope, gathered, d_branch, bias, gates, resid, cotangent):
    pieces, cuts, starts, order = gathered
    count, total, width = hidden.shape
    clips = gates.shape[0]

    def all_of(*shape):
        return pl.BlockSpec(shape, lambda at, order, starts: (0,) * len(shape))

    per_block = pl.BlockSpec((1, total, width), lambda at, order, starts: (order[at], 0, 0))
    low = jax.ShapeDtypeStruct((total, width), jnp.bfloat16)
    return pl.pallas_call(
        functools.partial(branch_kernel, frames, cuts),
        grid_spec=pltpu.PrefetchScalarGridSpec(
            num_scalar_prefetch=2,
            grid=(count,),
            in_specs=[
                pl.BlockSpec(memory_space=pltpu.SMEM),
                per_block,
                per_block,
                all_of(total, width),
                all_of(*bias.shape),
                all_of(*gates.shape),
                all_of(total, width),
                all_of(total, width),
            ]
            + [pl.BlockSpec(memory_space=pl.ANY)] * len(pieces),
            out_specs=[
                per_block,
                pl.BlockSpec((1, 1, width), lambda at, order, starts: (order[at], 0, 0)),
                all_of(total, width),
                all_of(clips, 1, width),
            ],
            scratch_shapes=[
                pltpu.VMEM((total, width), jnp.float32),
                pltpu.VMEM((count * width, width), jnp.bfloat16),
                pltpu.SemaphoreType.DMA((len(starts),)),
            ],
        ),
        out_shape=[
            jax.ShapeDtypeStruct((count, total, width), jnp.bfloat16),
            jax.ShapeDtypeStruct((count, 1, width), jnp.float32),
            low,
            jax.ShapeDtypeStruct((clips, 1, width), jnp.float32),
        ],
        compiler_params=pltpu.CompilerParams(vmem_limit_bytes=vmem_bytes),
        cost_estimate=little_cost,
    )(stacked(order), stacked(starts), counts, hidden, slope, d_branch, bias, gates, resid, cotangent, *pieces)


def resid_kernel(
    frames,
    counts,
    d_pre,
    block,
    mods,
    resid,
    cotangent,
    proj,
    d_resid_out,
    d_proj,
    sums,
    total_grad,
):
    step, steps = pl.program_id(0), pl.num_programs(0)
    total, width = resid.shape
    clips = mods.shape[0]
    rows = total // clips
    tile = min(rows, 128)
    source = d_pre[0]

    @pl.when(step == 0)
    def _():
        total_grad[...] = jnp.zeros_like(total_grad)

    for low, high in column_cuts(width):
        span = slice(low, high)
        total_grad[:, span] += dot_nt(source, block[0, span, :])

    @pl.when(step == steps - 1)
    def _():
        for clip in range(clips):
            gate_one, scale_two = mods[clip, 2:3, :], mods[clip, 4:5, :]
            found = [0.0] * 4
            for first in range(clip * rows, (clip + 1) * rows, tile):
                span = slice(first, first + tile)
                grad = total_grad[span]
                normed, inverse = norm_parts(resid[span])
                back = norm_back(grad * (1.0 + scale_two), normed, inverse)
                d_resid = wide(cotangent[span]) + back
                d_resid_out[span] = d_resid
                kept = valid_rows(counts[clip], tile, frames) * d_resid
                low_back = narrow(kept * gate_one)
                d_proj[span] = low_back
                terms = (grad, grad * normed, kept * proj[span], wide(low_back))
                found = [old + column_sum(term) for old, term in zip(found, terms)]
            for at in range(4):
                sums[clip, at : at + 1, :] = found[at]


def run_resid(frames, counts, d_pre, blocks, mods, resid, cotangent, proj):
    count, total, width = d_pre.shape
    clips = mods.shape[0]
    return pl.pallas_call(
        functools.partial(resid_kernel, frames),
        grid=(count,),
        in_specs=[
            pl.BlockSpec(memory_space=pltpu.SMEM),
            spec((1, total, width), lambda at: (at, 0, 0)),
            spec((1, width, width), lambda at: (at, 0, 0)),
            held(mods.shape),
            held((total, width)),
            held((total, width)),
            held((total, width)),
        ],
        out_specs=[held((total, width)), held((total, width)), held((clips, 4, width))],
        out_shape=[
            jax.ShapeDtypeStruct((total, width), jnp.float32),
            jax.ShapeDtypeStruct((total, width), jnp.bfloat16),
            jax.ShapeDtypeStruct((clips, 4, width), jnp.float32),
        ],
        scratch_shapes=[pltpu.VMEM((total, width), jnp.float32)],
        compiler_params=pltpu.CompilerParams(vmem_limit_bytes=vmem_bytes),
        cost_estimate=little_cost,
    )(counts, d_pre, blocks, mods, resid, cotangent, proj)


def attention_back_kernel(
    frames, counts, d_proj, parts, block, d_qkv, sums, d_mixed, d_query, d_key, d_value
):
    rows, width = d_proj.shape
    tile = min(rows, 128)
    count = counts[pl.program_id(0)]
    source = d_proj[...]
    for low, high in column_cuts(width):
        d_mixed[:, low:high] = narrow(dot_nt(source, block[0, low:high, :]))
    scale = (width // HEADS) ** -0.5
    offset = score_offset(count, tile, frames, 0)
    for ref in (d_query, d_key, d_value):
        ref[...] = jnp.zeros_like(ref)
    for first in range(0, rows, tile):
        span = slice(first, first + tile)
        for low, high, start, stop in head_windows(width):
            lanes = slice(start, stop)
            mask = lane_mask(low, high, stop - start, jnp.bfloat16)
            query_high = parts[0, span, lanes] * mask
            key_high = parts[2, span, lanes] * mask
            back = d_mixed[span, lanes] * mask
            scores = dot_nt(key_high, query_high)
            scores += dot_nt(key_high, parts[1, span, lanes])
            scores += dot_nt(parts[3, span, lanes], query_high) + offset
            expons = jnp.exp(scores - jnp.max(scores, axis=0, keepdims=True))
            probs = expons * (1.0 / jnp.sum(expons, axis=0, keepdims=True))
            d_probs = dot_nt(parts[4, span, lanes], back)
            inner = jnp.sum(d_probs * probs, axis=0, keepdims=True)
            d_scores = narrow(probs * (d_probs - inner))
            d_value[span, lanes] += dot_nn(narrow(probs), back)
            d_key[span, lanes] += dot_nn(d_scores, query_high)
            d_query[span, lanes] += dot_tn(d_scores, key_high)
    for at, ref in enumerate((d_query, d_key, d_value)):
        low_back = narrow(ref[...] * scale) if at == 0 else narrow(ref[...])
        d_qkv[at] = low_back
        sums[0, at : at + 1, :] = column_sum(wide(low_back))
    d_qkv[3] = source


def run_attention_back(frames, counts, d_proj, parts, block):
    total, width = d_proj.shape
    clips = counts.shape[0]
    rows = total // clips
    return pl.pallas_call(
        functools.partial(attention_back_kernel, frames),
        grid=(clips,),
        in_specs=[
            pl.BlockSpec(memory_space=pltpu.SMEM),
            spec((rows, width), lambda clip: (clip, 0)),
            spec((5, rows, width), lambda clip: (0, clip, 0)),
            spec((1, width, width), lambda clip: (3, 0, 0), pipeline_mode=pl.Buffered(1)),
        ],
        out_specs=[
            spec((4, rows, width), lambda clip: (0, clip, 0)),
            spec((1, 3, width), lambda clip: (clip, 0, 0)),
        ],
        out_shape=[
            jax.ShapeDtypeStruct((4, total, width), jnp.bfloat16),
            jax.ShapeDtypeStruct((clips, 3, width), jnp.float32),
        ],
        scratch_shapes=[pltpu.VMEM((rows, width), jnp.bfloat16)]
        + [pltpu.VMEM((rows, width), jnp.float32)] * 3,
        compiler_params=pltpu.CompilerParams(vmem_limit_bytes=vmem_bytes),
        cost_estimate=little_cost,
    )(counts, d_proj, parts, block)


def input_kernel(d_qkv, block, mods, tokens, d_resid, input_grad, sums, total_grad):
    step, steps = pl.program_id(0), pl.num_programs(0)
    total, width = tokens.shape
    clips = mods.shape[0]
    rows = total // clips
    tile = min(rows, 128)
    source = d_qkv[0]

    @pl.when(step == 0)
    def _():
        total_grad[...] = jnp.zeros_like(total_grad)

    for low, high in column_cuts(width):
        span = slice(low, high)
        total_grad[:, span] += dot_nt(source, block[0, span, :])

    @pl.when(step == steps - 1)
    def _():
        for clip in range(clips):
            scale_one = mods[clip, 1:2, :]
            found = [0.0] * 2
            for first in range(clip * rows, (clip + 1) * rows, tile):
                span = slice(first, first + tile)
                grad = total_grad[span]
                normed, inverse = norm_parts(wide(tokens[span]))
                back = norm_back(grad * (1.0 + scale_one), normed, inverse)
                input_grad[span] = narrow(d_resid[span] + back)
                terms = (grad, grad * normed)
                found = [old + column_sum(term) for old, term in zip(found, terms)]
            for at in range(2):
                sums[clip, at : at + 1, :] = found[at]


def run_input(d_qkv, blocks, mods, tokens, d_resid):
    total, width = tokens.shape
    clips = mods.shape[0]
    return pl.pallas_call(
        input_kernel,
        grid=(3,),
        in_specs=[
            spec((1, total, width), lambda at: (at, 0, 0)),
            spec((1, width, width), lambda at: (at, 0, 0)),
            held(mods.shape),
            held((total, width)),
            held((total, width)),
        ],
        out_specs=[held((total, width)), held((clips, 2, width))],
        out_shape=[
            jax.ShapeDtypeStruct((total, width), jnp.bfloat16),
            jax.ShapeDtypeStruct((clips, 2, width), jnp.float32),
        ],
        scratch_shapes=[pltpu.VMEM((total, width), jnp.float32)],
        compiler_params=pltpu.CompilerParams(vmem_limit_bytes=vmem_bytes),
        cost_estimate=little_cost,
    )(d_qkv, blocks, mods, tokens, d_resid)


def halves_kernel(left_of, adds, steps, order, side, *refs):
    lefts = refs[: max(left_of) + 1]
    right = refs[len(lefts)]
    turned, total_low = refs[-2:]
    if adds:
        incoming, first_keep, first_out, second_keep, second_out = refs[len(lefts) + 1 : -2]
    else:
        out = refs[-3]
    step = pl.program_id(0)
    block = order[step]
    width = lefts[0].shape[-1]
    half = width // 2

    def pick(left, at):
        lanes = slice(at * half, (at + 1) * half)
        turned[...] = (left[:, lanes] if left.ndim == 2 else left[0, :, lanes]).T

    fresh = (step == 0) | (lefts[0].ndim == 3) | (len(lefts) > 1)
    for at in range(2):
        for index, left in enumerate(lefts):
            of_left = [block == number for number, source in enumerate(left_of) if source == index]

            @pl.when(fresh & (side[0] == at) & functools.reduce(jnp.logical_or, of_left))
            def _(left=left, at=at):
                pick(left, at)

    found = dot_nn(turned[...], right[0] if right.ndim == 3 else right[...])
    if not adds:
        out[0] = narrow(found)
        return
    total_low[...] = narrow(found + wide(incoming[0]))
    for state, target, rows in (
        (steps[0][0], first_keep, slice(0, half // 2)),
        (steps[0][1], first_out, slice(0, half // 2)),
        (steps[1][0], second_keep, slice(half // 2, half)),
        (steps[1][1], second_out, slice(half // 2, half)),
    ):

        @pl.when(functools.reduce(jnp.logical_or, [step == at_step for at_step in state]))
        def _(target=target, rows=rows):
            target[0] = total_low[rows]


def run_halves(lefts, left_of, right, side, at, incoming=None):
    total, width = lefts[0].shape[-2:]
    half = width // 2
    low_bit, high_bit = at % 2, at // 2
    order = stacked([at ^ 3, at ^ 1, at, at ^ 2])
    places = {
        "first_keep": [high_bit, high_bit, high_bit, 1 - high_bit],
        "first_out": [1 - high_bit, high_bit, high_bit, high_bit],
        "second_keep": [1 - low_bit, 1 - low_bit, low_bit, low_bit],
        "second_out": [1 - low_bit, low_bit, low_bit, low_bit],
    }
    steps = (((2, 3), (0, 1)), ((1, 2), (0, 3)))
    adds = incoming is not None
    table = stacked([place for row in places.values() for place in row])

    def block_of(array, *rest):
        if array.ndim == 2:
            return pl.BlockSpec(array.shape, lambda step, order, side, table: (0, 0))
        return pl.BlockSpec((1,) + array.shape[1:], lambda step, order, side, table: (order[step], 0, 0))

    per_block = pl.BlockSpec((1, half, width), lambda step, order, side, table: (order[step], 0, 0))
    operands = list(lefts) + [right]
    in_specs = [block_of(array) for array in operands]
    if adds:
        operands.append(incoming)
        in_specs.append(per_block)
        out_specs = [
            pl.BlockSpec(
                (1, half // 2, width),
                functools.partial(lambda row, step, order, side, table: (table[row * 4 + step], 0, 0), row),
            )
            for row in range(4)
        ]
        out_shape = [jax.ShapeDtypeStruct((2, half // 2, width), jnp.bfloat16)] * 4
    else:
        out_specs = per_block
        out_shape = jax.ShapeDtypeStruct((4, half, width), jnp.bfloat16)

    def body(order, side, table, *refs):
        halves_kernel(left_of, adds, steps, order, side, *refs)

    return pl.pallas_call(
        body,
        grid_spec=pltpu.PrefetchScalarGridSpec(
            num_scalar_prefetch=3,
            grid=(4,),
            in_specs=in_specs,
            out_specs=out_specs,
            scratch_shapes=[
                pltpu.VMEM((half, total), jnp.bfloat16),
                pltpu.VMEM((half, width), jnp.bfloat16),
            ],
        ),
        out_shape=out_shape,
        compiler_params=pltpu.CompilerParams(vmem_limit_bytes=vmem_bytes),
        cost_estimate=little_cost,
    )(order, stacked([side]), table, *operands)


def tie(*values):
    return lax.optimization_barrier(values)


def packed(arrays, tile):
    flat = jnp.concatenate([array.reshape(-1) for array in arrays])
    return jnp.pad(flat, (0, -flat.shape[0] % (tile * 128))).reshape(-1, 128)


def core_swap(array):
    count = lax.axis_size("dp")
    return lax.ppermute(array, "dp", [(at, at ^ 1) for at in range(count)])


def chip_shift(array, step):
    count = lax.axis_size("dp")
    return lax.ppermute(array, "dp", [(at, (at + 2 * step) % count) for at in range(count)])


def chip_swap(array, bits):
    count = lax.axis_size("dp")
    return lax.ppermute(array, "dp", [(at, at ^ (2 * bits)) for at in range(count)])


def rank_swap(array, bits):
    count = lax.axis_size("fsdp")
    return lax.ppermute(array, "fsdp", [(at, at ^ bits) for at in range(count)])


def entry(array, at, axis=0):
    return lax.dynamic_index_in_dim(array, at, axis, keepdims=False)


def place_kernel(cuts, at, *refs):
    parts, whole, held_rows, semaphores = refs[:-3], refs[-3], refs[-2], refs[-1]
    spans, loads, stores = [], [], []
    for index, (part, first, rows) in enumerate(cuts):
        spans.append(pl.ds(pl.multiple_of(at[index] * 16, 16), rows))
        source = parts[part].at[pl.ds(first, rows)]
        loads.append(
            pltpu.make_async_copy(source, held_rows.at[spans[index]], semaphores.at[0, index])
        )
        loads[index].start()
    for index, span in enumerate(spans):
        loads[index].wait()
        stores.append(
            pltpu.make_async_copy(held_rows.at[span], whole.at[span], semaphores.at[1, index])
        )
        stores[index].start()
    for store in stores:
        store.wait()


def place(parts, cuts, starts, rows):
    width = parts[0].shape[-1]
    dtype = parts[0].dtype
    return pl.pallas_call(
        functools.partial(place_kernel, cuts),
        in_specs=[pl.BlockSpec(memory_space=pltpu.SMEM)]
        + [pl.BlockSpec(memory_space=pl.ANY)] * len(parts),
        out_specs=pl.BlockSpec(memory_space=pl.ANY),
        out_shape=jax.ShapeDtypeStruct((rows, width), dtype),
        scratch_shapes=[
            pltpu.VMEM((rows, width), dtype),
            pltpu.SemaphoreType.DMA((2, len(cuts))),
        ],
        compiler_params=pltpu.CompilerParams(vmem_limit_bytes=vmem_bytes),
        cost_estimate=little_cost,
    )(stacked(starts), *parts)


def own_rows(parts, group):
    ranks, at = lax.axis_size("fsdp"), lax.axis_index("fsdp")
    shares = ranks // group
    count, _, row_part, col_part = parts.shape
    chunk = row_part // shares
    split = parts.reshape(count, group, shares, chunk, col_part).transpose(1, 2, 0, 3, 4)
    split = split.reshape(ranks, count, chunk, col_part)
    if shares > 1:
        moved = lax.all_to_all(split, "fsdp", 0, 0, tiled=True)
        (moved,) = yield (moved,)
        yield moved.transpose(1, 2, 0, 3).reshape(count, chunk, ranks * col_part)
        return
    panels = [entry(split, at)]
    panels += [rank_swap(entry(split, at ^ bits), bits) for bits in range(1, ranks)]
    panels = yield tuple(panels)
    placed = [
        lax.select_n(at, *[panels[panel ^ index] for index in range(ranks)])
        for panel in range(ranks)
    ]
    yield jnp.concatenate(placed, axis=2)


def shard_rows(split, group):
    ranks, count, chunk, col_part = split.shape
    shares = ranks // group
    moved = lax.all_to_all(split, "fsdp", 0, 0, tiled=True)
    moved = moved.reshape(group, shares, count, chunk, col_part).transpose(2, 0, 1, 3, 4)
    return moved.reshape(count, group, shares * chunk, col_part)


def gather_blocks(rows, group):
    ranks, dp_count = lax.axis_size("fsdp"), lax.axis_size("dp")
    shares = ranks // group
    chunk, total = rows.shape
    all_rows = lax.all_gather(rows, ("fsdp", "dp"), axis=0, tiled=True)
    if shares > 1:
        all_rows = all_rows.reshape(group, shares, dp_count, chunk, total).transpose(0, 2, 1, 3, 4)
    return all_rows.reshape(group, total, total)


def join_line(found):
    chips, chip = lax.axis_size("dp") // 2, lax.axis_index("dp") // 2
    chunk = found[0].shape[0]
    starts = [(chip - step) % chips * (chunk // 16) for step in range(chips)]
    return place(found, [(step, 0, chunk) for step in range(chips)], starts, chips * chunk)


def gather_second(rows, group):
    ranks, at = lax.axis_size("fsdp"), lax.axis_index("fsdp")
    total = rows.shape[-1]
    if ranks != group:
        blocks = gather_blocks(rows, group).reshape(group * total, total)
        for _ in range(3):
            (blocks,) = yield (blocks,)
        cuts = [[(0, index * total, total)] for index in range(group)]
        yield [blocks], cuts, [index * (total // 16) for index in range(group)], range(group)
        return
    chips = lax.axis_size("dp") // 2
    core = lax.axis_index("dp") % 2
    chunk, half = rows.shape[0], total // 2
    others = yield tuple(chip_shift(rows, step) for step in range(1, chips))
    line = join_line([rows, *others])
    cuts = [(side, step * chunk, chunk) for side in range(2) for step in range(chips)]
    starts = [
        (2 * step + side) * (chunk // 16) for side in (core, 1 - core) for step in range(chips)
    ]
    (own,) = yield (place([line, core_swap(line)], cuts, starts, total),)
    share = lax.dynamic_slice_in_dim(own, core * half, half, 0)
    mine = yield tuple(rank_swap(share, bits) for bits in range(1, ranks))
    parts, cuts, starts = [own], [[(0, 0, total)]], [at * (total // 16)]
    for bits in range(1, ranks):
        parts += [mine[bits - 1], core_swap(mine[bits - 1])]
        cuts.append([(2 * bits - 1, 0, half), (2 * bits, 0, half)])
        starts += [((at ^ bits) * 2 + side) * (half // 16) for side in (core, 1 - core)]
    yield parts, cuts, starts, [at ^ bits for bits in range(ranks)]


def gather_own(rows, group):
    ranks = lax.axis_size("fsdp")
    shares = ranks // group
    if shares > 1:
        sets = [[share + shares * block for share in range(shares)] for block in range(group)]
        rows = lax.all_gather(rows, "fsdp", axis=1, tiled=True, axis_index_groups=sets)
    return lax.all_gather(rows, "dp", axis=1, tiled=True)


def sum_blocks(lefts, left_of, right, group):
    ranks, dp_count = lax.axis_size("fsdp"), lax.axis_size("dp")
    shares = ranks // group
    total = lefts[0].shape[-1]
    if shares > 1:
        blocks = jnp.stack(
            [
                narrow(
                    fast_dot(
                        "tr,te->re",
                        lefts[index] if lefts[index].ndim == 2 else lefts[index][block],
                        right if right.ndim == 2 else right[block],
                    )
                )
                for block, index in enumerate(left_of)
            ]
        )
        chunk = total // (dp_count * shares)
        blocks = blocks.reshape(group, dp_count, shares, chunk, -1).transpose(0, 2, 1, 3, 4)
        rows = lax.psum_scatter(
            blocks.reshape(group * total, -1), ("fsdp", "dp"), scatter_dimension=0, tiled=True
        )
        for _ in range(7):
            (rows,) = yield (rows,)
        yield gather_own(rows[None], group)[0]
        return
    chips, half = dp_count // 2, total // 2
    chunk = half // chips
    at = lax.axis_index("fsdp")
    core, chip = lax.axis_index("dp") % 2, lax.axis_index("dp") // 2
    low_bit, high_bit = at % 2, at // 2
    (away,) = yield (run_halves(lefts, left_of, right, 1 - core, at),)
    (away_in,) = yield (core_swap(away),)
    first, first_out, second, second_out = run_halves(lefts, left_of, right, core, at, away_in)
    first_out, second_out = yield (first_out, second_out)
    first_in, second_in = yield (rank_swap(first_out, 1), rank_swap(second_out, 2))
    first = narrow(wide(first) + wide(first_in)).reshape(2, chips // 2, chunk, -1)
    second = narrow(wide(second) + wide(second_in)).reshape(2, chips // 2, chunk, -1)
    first_in = rank_swap(entry(first, 1 - high_bit), 2)
    second_in = rank_swap(entry(second, 1 - low_bit), 1)
    first_in, second_in = yield (first_in, second_in)
    first = narrow(wide(entry(first, high_bit)) + wide(first_in))
    second = narrow(wide(entry(second, low_bit)) + wide(second_in))
    line = jnp.concatenate([first, second])
    step = 1
    while step < chips:
        bit = chip // step % 2
        line = line.reshape(-1, 2, *line.shape[1:])
        (line_in,) = yield (chip_swap(entry(line, 1 - bit, 1), step),)
        line = narrow(wide(entry(line, bit, 1)) + wide(line_in))
        step *= 2
    yield lax.all_gather(line[0], "dp", axis=0, tiled=True)


def fast_dot(subscripts, left, right):
    return jnp.einsum(subscripts, left, right, preferred_element_type=jnp.float32)


def products_kernel(chips, at, gathered, left_root, right_root, out, whole, semaphores):
    chunk, width = left_root.shape
    ranks = out.shape[0]
    copies = []
    for index in range(2 * chips):
        first = (index % 2 * chips + index // 2) * chunk
        copies.append(
            pltpu.make_async_copy(
                gathered.at[pl.ds(index * chunk, chunk)],
                whole.at[pl.ds(first, chunk)],
                semaphores.at[index],
            )
        )
        copies[-1].start()
    for copy in copies:
        copy.wait()
    first = at[0] * 16
    grad = whole[...]
    picked = lax.broadcasted_iota(jnp.int32, (width, chunk), 0) - first
    picked = picked == lax.broadcasted_iota(jnp.int32, (width, chunk), 1)
    own_columns = narrow(dot_nn(grad, narrow(picked.astype(jnp.float32))))
    side_high, side_low = split_high(dot_nn(left_root[...], grad))
    right = right_root[...]
    precond = dot_nn(side_high, right) + dot_nn(side_low, right)
    outer = dot_nt(whole[pl.ds(pl.multiple_of(first, 16), chunk), :], grad)
    inner = dot_tn(own_columns, grad)
    for at_out, product in enumerate((precond, outer, inner)):
        low = narrow(product)
        for rank in range(ranks):
            span = slice(rank * (width // ranks), (rank + 1) * (width // ranks))
            out[rank, at_out] = low[:, span]


def owned_step(whole, left_root, right_root, group):
    ranks, dp_count = lax.axis_size("fsdp"), lax.axis_size("dp")
    shares = ranks // group
    chunk, total = left_root.shape
    col_part = total // ranks
    first = lax.axis_index("dp") * (chunk * shares) + lax.axis_index("fsdp") % shares * chunk
    if shares == 1:
        return pl.pallas_call(
            functools.partial(products_kernel, dp_count // 2),
            in_specs=[
                pl.BlockSpec(memory_space=pltpu.SMEM),
                pl.BlockSpec(memory_space=pl.ANY),
                pl.BlockSpec(memory_space=pltpu.VMEM),
                pl.BlockSpec(memory_space=pltpu.VMEM),
            ],
            out_specs=pl.BlockSpec(memory_space=pltpu.VMEM),
            out_shape=jax.ShapeDtypeStruct((ranks, 3, chunk, col_part), jnp.bfloat16),
            scratch_shapes=[
                pltpu.VMEM((total, total), jnp.bfloat16),
                pltpu.SemaphoreType.DMA((dp_count,)),
            ],
            compiler_params=pltpu.CompilerParams(vmem_limit_bytes=vmem_bytes),
            cost_estimate=little_cost,
        )((first // 16)[None], whole, left_root, right_root)
    grad_rows = lax.dynamic_slice_in_dim(whole, first, chunk, 0)
    own_columns = lax.dynamic_slice_in_dim(whole, first, chunk, 1)
    outer = fast_dot("rk,jk->rj", grad_rows, whole)
    inner = fast_dot("kr,kj->rj", own_columns, whole)
    side_high, side_low = split_high(fast_dot("rk,kj->rj", left_root, whole))
    precond = fast_dot("rk,kj->rj", side_high, right_root) + fast_dot(
        "rk,kj->rj", side_low, right_root
    )
    products = narrow(jnp.stack([precond, outer, inner]))
    return products.reshape(3, chunk, ranks, col_part).transpose(2, 0, 1, 3)


def per_device(
    tokens,
    conditioning,
    frame_counts,
    cotangent,
    weights,
    biases,
    momentum,
    left_stats,
    right_stats,
    left_roots,
    right_roots,
    bias_moment,
    bias_second,
):
    group = 4
    mod_count = 6
    clip_count, pos_count, frames, width = tokens.shape
    token_count = clip_count * pos_count * frames
    block_count, row_part, col_part = weights.shape
    dp_count, ranks = lax.axis_size("dp"), lax.axis_size("fsdp")
    dp_at, rank_at = lax.axis_index("dp"), lax.axis_index("fsdp")
    all_clips = clip_count * dp_count
    bias_part = biases.shape[0]
    stream = tokens.reshape(token_count, width)
    grad_out = cotangent.reshape(token_count, width)
    low_weights = narrow(weights).reshape(block_count, row_part, col_part)
    shards = low_weights[mod_count:].reshape(-1, group, row_part, col_part)

    weight_rows = own_rows(shards, group)
    weight_panels = next(weight_rows)
    cond_low = narrow(jax.nn.silu(conditioning))
    first_parts = lax.all_gather(packed([cond_low, narrow(biases)], 16), "dp", axis=0, tiled=True)
    weight_panels, first_parts = tie(weight_panels, first_parts)
    attn_rows, one_rows, two_rows = weight_rows.send(weight_panels)
    attn_w = gather_blocks(attn_rows, group)
    two_w = gather_blocks(two_rows, group).reshape(group * width, width)
    two_gathered = (
        [two_w],
        [[(0, index * width, width)] for index in range(group)],
        [index * (width // 16) for index in range(group)],
        range(group),
    )

    first_parts = first_parts.reshape(dp_count, -1)
    cond_all = first_parts[:, : clip_count * width].reshape(all_clips, width)
    bias_rows = wide(first_parts[:, clip_count * width : clip_count * width + bias_part])
    cond_rows = lax.dynamic_slice_in_dim(cond_all, dp_at * row_part, row_part, 1)
    cond_cols = wide(lax.dynamic_slice_in_dim(cond_all, rank_at * col_part, col_part, 1))
    mod_parts = fast_dot("cr,jre->cje", cond_rows, low_weights[:mod_count])
    mod_parts = lax.all_to_all(mod_parts, "dp", 0, 0, tiled=True)
    mod_parts, one_rows = tie(mod_parts, one_rows)
    one_steps = gather_second(one_rows, group)
    one_parts = next(one_steps)
    mod_cols = jnp.sum(mod_parts.reshape(dp_count, clip_count, mod_count, col_part), axis=0)
    left_cond = jnp.einsum("jrk,ck->jrc", left_roots[:mod_count], cond_cols, precision=precise)
    mod_size, bias_size = mod_cols.size, dp_count * bias_part
    second_parts = lax.all_gather(
        packed([mod_cols, bias_rows, left_cond], 8), "fsdp", axis=0, tiled=True
    )
    second_parts, one_parts = tie(second_parts, one_parts)
    one_parts, attn_w = tie(one_steps.send(one_parts), attn_w)
    one_parts = one_steps.send(one_parts)
    second_parts = second_parts.reshape(ranks, -1)
    mods = second_parts[:, :mod_size].reshape(ranks, clip_count, mod_count, col_part)
    mods = mods.transpose(1, 2, 0, 3).reshape(clip_count, mod_count, width)
    bias_all = second_parts[:, mod_size : mod_size + bias_size].reshape(ranks, dp_count, bias_part)
    bias_all = bias_all.transpose(1, 0, 2).reshape(-1, width)
    left_size = mod_size + bias_size + left_cond.size
    left_cond = jnp.sum(second_parts[:, mod_size + bias_size : left_size], axis=0)
    left_cond = left_cond.reshape(mod_count, row_part, all_clips)
    mods = mods + bias_all[:mod_count]
    bias_table = jnp.concatenate(
        [bias_all[6:7], jnp.zeros((1, width), jnp.float32), bias_all[7:14]]
    )

    attn_in, parts, mixed, proj, resid, mlp_in, d_branch, d_branch_sums = run_attention(
        frames, frame_counts, stream, grad_out, mods, bias_table, attn_w
    )
    mlp_in, one_parts = tie(mlp_in, one_parts)
    one_w, hidden, slope = run_hidden(mlp_in, one_steps.send(one_parts), bias_table[4:8, None])
    one_w = one_w.reshape(group, width, width)

    two_steps = sum_blocks([hidden], [0] * group, d_branch, group)
    two_parts = next(two_steps)
    roots = jnp.stack([narrow(left_roots[mod_count:]), narrow(right_roots[mod_count:])])
    hidden, two_parts, roots = tie(hidden, two_parts, roots)
    two_parts = two_steps.send(two_parts)
    root_rows = own_rows(roots.reshape(-1, group, row_part, col_part), group)
    root_panels = next(root_rows)
    d_pre, d_pre_sums, block_out, d_gate_two = run_branch(
        frames,
        frame_counts,
        hidden,
        slope,
        two_gathered,
        d_branch,
        bias_table[8:9],
        mods[:, 5:6],
        resid,
        grad_out,
    )
    d_pre, root_panels = tie(d_pre, root_panels)
    root_rows = root_rows.send(root_panels)
    d_pre, two_parts, root_rows = tie(d_pre, two_parts, root_rows)
    two_parts = two_steps.send(two_parts)
    d_pre, two_parts = tie(d_pre, two_parts)
    two_parts = two_steps.send(two_parts)
    left_rows, right_rows = jnp.split(root_rows, 2)
    right_wholes = [gather_own(rows[None], group)[0] for rows in right_rows]
    one_steps = sum_blocks([mlp_in], [0] * group, d_pre, group)
    one_parts = next(one_steps)
    d_pre, one_parts = tie(d_pre, one_parts)
    one_parts = one_steps.send(one_parts)
    d_resid, d_proj, resid_sums = run_resid(
        frames, frame_counts, d_pre, one_w, mods, resid, grad_out, proj
    )
    d_proj, one_parts, two_parts = tie(d_proj, one_parts, two_parts)
    two_parts = two_steps.send(two_parts)
    one_parts = one_steps.send(one_parts)
    d_proj, one_parts, right_wholes[2] = tie(d_proj, one_parts, right_wholes[2])
    one_parts = one_steps.send(one_parts)
    d_heads, head_sums = run_attention_back(frames, frame_counts, d_proj, parts, attn_w)
    d_heads, two_parts, one_parts, right_wholes[1] = tie(
        d_heads, two_parts, one_parts, right_wholes[1]
    )
    two_parts = two_steps.send(two_parts)
    one_parts = one_steps.send(one_parts)
    attn_steps = sum_blocks([attn_in, mixed], [0, 0, 0, 1], d_heads, group)
    attn_parts = next(attn_steps)
    d_heads, attn_parts = tie(d_heads, attn_parts)
    attn_parts = attn_steps.send(attn_parts)
    d_heads, attn_parts, two_parts = tie(d_heads, attn_parts, two_parts)
    two_parts = two_steps.send(two_parts)
    attn_parts = attn_steps.send(attn_parts)
    d_heads, attn_parts = tie(d_heads, attn_parts)
    attn_parts = attn_steps.send(attn_parts)
    input_grad, input_sums = run_input(d_heads, attn_w, mods, stream, d_resid)
    input_sums, one_parts, two_parts, right_wholes[0] = tie(
        input_sums, one_parts, two_parts, right_wholes[0]
    )
    whole_two = two_steps.send(two_parts)
    one_parts = one_steps.send(one_parts)

    d_mods = jnp.stack(
        [
            input_sums[:, 0],
            input_sums[:, 1],
            resid_sums[:, 2],
            resid_sums[:, 0],
            resid_sums[:, 1],
            d_gate_two[:, 0],
        ],
        axis=1,
    )
    head_sums = jnp.sum(head_sums, axis=0)
    grad_bias = jnp.concatenate(
        [
            jnp.sum(d_mods, axis=0),
            head_sums[0:1],
            head_sums[2:3],
            jnp.sum(resid_sums[:, 3], axis=0)[None],
            d_pre_sums[:, 0],
            jnp.sum(d_branch_sums, axis=0),
        ]
    )
    to_ranks = jnp.concatenate(
        [
            d_mods.reshape(clip_count, mod_count, ranks, col_part)
            .transpose(2, 0, 1, 3)
            .reshape(ranks, mod_size),
            grad_bias.reshape(dp_count, ranks, bias_part)
            .transpose(1, 0, 2)
            .reshape(ranks, bias_size),
        ],
        axis=1,
    )
    rank_sums = lax.all_to_all(to_ranks, "fsdp", 0, 0, tiled=True)
    rank_sums, attn_parts, one_parts = tie(rank_sums, attn_parts, one_parts)
    attn_parts = attn_steps.send(attn_parts)
    one_parts = one_steps.send(one_parts)
    rank_sums = jnp.sum(rank_sums, axis=0)
    to_rows = jnp.concatenate(
        [
            jnp.broadcast_to(rank_sums[None, :mod_size], (dp_count, mod_size)),
            rank_sums[mod_size:].reshape(dp_count, bias_part),
        ],
        axis=1,
    )
    to_rows, attn_parts, one_parts = tie(to_rows, attn_parts, one_parts)
    attn_parts = attn_steps.send(attn_parts)
    whole_one = one_steps.send(one_parts)
    products_two = owned_step(whole_two, left_rows[2], right_wholes[2], group)
    products_two, attn_parts = tie(products_two, attn_parts)
    attn_parts = attn_steps.send(attn_parts)
    back_two = shard_rows(products_two, group)
    to_rows, back_two, attn_parts = tie(to_rows, back_two, attn_parts)
    whole_attn = attn_steps.send(attn_parts)
    from_rows = lax.all_to_all(to_rows, "dp", 0, 0, tiled=True)
    bias_grad = jnp.sum(from_rows[:, mod_size:], axis=0)
    mod_grad_cols = from_rows[:, :mod_size].reshape(all_clips, mod_count, col_part)
    mod_grad = lax.all_gather(packed([mod_grad_cols], 8), "fsdp", axis=0, tiled=True)
    mod_grad = mod_grad.reshape(ranks, -1)[:, : mod_grad_cols.size]
    mod_grad = mod_grad.reshape(ranks, all_clips, mod_count, col_part).transpose(1, 2, 0, 3)
    mod_grad = mod_grad.reshape(all_clips, mod_count, width)

    mod_grad_rows = lax.dynamic_slice_in_dim(mod_grad, dp_at * row_part, row_part, 2)
    right_parts = jnp.einsum(
        "cjk,jke->cje", mod_grad_rows, right_roots[:mod_count], precision=precise
    )
    cond_wide = wide(cond_all)
    cond_row_wide = wide(cond_rows)
    mod_gram = jnp.einsum("cjk,bjk->jcb", mod_grad, mod_grad, precision=precise)
    cond_gram = jnp.einsum("ck,bk->cb", cond_wide, cond_wide, precision=precise)
    mod_side = jnp.einsum("jcb,be->jce", mod_gram, cond_cols, precision=precise)
    ada_left = jnp.einsum("cr,jce->jre", cond_row_wide, mod_side, precision=precise)
    cond_side = jnp.einsum("cb,bje->jce", cond_gram, mod_grad_cols, precision=precise)
    ada_right = jnp.einsum("cjr,jce->jre", mod_grad_rows, cond_side, precision=precise)

    products_one = owned_step(whole_one, left_rows[1], right_wholes[1], group)
    back_one = shard_rows(products_one, group)
    right_parts = lax.all_gather(packed([right_parts], 8), "dp", axis=0, tiled=True)
    mod_right = jnp.sum(right_parts.reshape(dp_count, -1), axis=0)[: mod_grad_cols.size]
    mod_right = mod_right.reshape(all_clips, mod_count, col_part)
    ada_pre = jnp.einsum("jrc,cje->jre", left_cond, mod_right, precision=precise)
    whole_attn, right_parts = tie(whole_attn, right_parts)
    back_attn = shard_rows(owned_step(whole_attn, left_rows[0], right_wholes[0], group), group)

    def joined(at, ada):
        return jnp.concatenate([ada, wide(back_attn[at]), wide(back_one[at]), wide(back_two[at])])

    precond = joined(0, ada_pre)
    left_new = stat_decay * left_stats + (1.0 - stat_decay) * joined(1, ada_left)
    right_new = stat_decay * right_stats + (1.0 - stat_decay) * joined(2, ada_right)
    momentum_new = moment_decay * momentum + precond
    weights_new = weights - weight_rate * momentum_new
    weights_copy = weights_new.astype(jnp.bfloat16)
    bias_second_new = stat_decay * bias_second + (1.0 - stat_decay) * bias_grad * bias_grad
    bias_moment_new = moment_decay * bias_moment + bias_grad * lax.rsqrt(
        bias_second_new + diag_epsilon
    )
    biases_new = biases - bias_rate * bias_moment_new
    return (
        block_out.reshape(tokens.shape),
        input_grad.reshape(tokens.shape),
        left_new,
        right_new,
        momentum_new,
        weights_new,
        weights_copy,
        bias_moment_new,
        bias_second_new,
        biases_new,
    )


def solution(mesh):
    placed = (
        P("dp", "fsdp", None, None),
        P("dp", None),
        P("dp"),
        P("dp", "fsdp", None, None),
        P(None, "dp", "fsdp"),
        P(("dp", "fsdp")),
        P(None, "dp", "fsdp"),
        P(None, "dp", "fsdp"),
        P(None, "dp", "fsdp"),
        P(None, "dp", "fsdp"),
        P(None, "dp", "fsdp"),
        P(("dp", "fsdp")),
        P(("dp", "fsdp")),
    )
    return jax.shard_map(
        per_device,
        mesh=mesh,
        in_specs=placed,
        out_specs=(
            P("dp", "fsdp", None, None),
            P("dp", "fsdp", None, None),
            P(None, "dp", "fsdp"),
            P(None, "dp", "fsdp"),
            P(None, "dp", "fsdp"),
            P(None, "dp", "fsdp"),
            P(None, "dp", "fsdp"),
            P(("dp", "fsdp")),
            P(("dp", "fsdp")),
            P(("dp", "fsdp")),
        ),
        check_vma=False,
    )
```

```python
import functools
import math

import jax
import jax.numpy as jnp
from jax import lax
from jax.experimental import pallas as pl
from jax.experimental.pallas import tpu as pltpu
from jax.sharding import PartitionSpec as P

HEADS = 16


precise = lax.Precision.HIGHEST
norm_epsilon = 1e-06
masked_score = -1e30
stat_decay = 0.5
moment_decay = 0.9
weight_rate = 0.7
bias_rate = 0.1
diag_epsilon = 1e-08
vmem_bytes = 50 * 2**20
little_cost = pl.CostEstimate(flops=1024, bytes_accessed=1024, transcendentals=0)


def narrow(array):
    return array.astype(jnp.bfloat16)


def wide(array):
    return array.astype(jnp.float32)


def spec(shape, index_map, **keywords):
    return pl.BlockSpec(shape, index_map, **keywords)


def held(shape):
    return pl.BlockSpec(shape, lambda step: (0,) * len(shape), pipeline_mode=pl.Buffered(1))


def column_cuts(total):
    cuts, at = [], 0
    while at < total:
        cuts.append((at, min(total, at + 256)))
        at += 256
    return cuts


def dot_nn(left, right):
    return lax.dot_general(left, right, (((1,), (0,)), ((), ())), preferred_element_type=jnp.float32)


def dot_nt(left, right):
    return lax.dot_general(left, right, (((1,), (1,)), ((), ())), preferred_element_type=jnp.float32)


def dot_tn(left, right):
    return lax.dot_general(left, right, (((0,), (0,)), ((), ())), preferred_element_type=jnp.float32)


def split_high(values):
    high = narrow(values)
    return high, narrow(values - wide(high))


def valid_rows(count, rows, frames):
    at = lax.broadcasted_iota(jnp.int32, (rows, 1), 0)
    return (lax.rem(at, frames) < count).astype(jnp.float32)


def score_offset(count, size, frames, key_axis):
    first = lax.broadcasted_iota(jnp.int32, (size, size), 0)
    second = lax.broadcasted_iota(jnp.int32, (size, size), 1)
    key = second if key_axis == 1 else first
    met = (lax.div(first, frames) == lax.div(second, frames)) & (lax.rem(key, frames) < count)
    return jnp.where(met, 0.0, masked_score)


def head_windows(width):
    size = width // HEADS
    windows = []
    for head in range(HEADS):
        low, high = head * size, (head + 1) * size
        start = low // 128 * 128
        stop = min(width, -(-high // 128) * 128)
        windows.append((low - start, high - start, start, stop))
    return windows


def lane_mask(low, high, count, dtype):
    lanes = lax.broadcasted_iota(jnp.int32, (1, count), 1)
    return ((lanes >= low) & (lanes < high)).astype(jnp.float32).astype(dtype)


def norm_parts(values):
    centered = values - jnp.mean(values, axis=-1, keepdims=True)
    variance = jnp.mean(centered * centered, axis=-1, keepdims=True)
    inverse = lax.rsqrt(variance + norm_epsilon)
    return centered * inverse, inverse


def norm_back(grad, normed, inverse):
    first = jnp.mean(grad, axis=-1, keepdims=True)
    second = jnp.mean(grad * normed, axis=-1, keepdims=True)
    return (grad - first - normed * second) * inverse


def column_sum(values):
    return jnp.sum(values, axis=0, keepdims=True)


def start_loads(cuts, at, parts, whole, semaphores, first_index=0):
    loads = []
    for index, (part, first, rows) in enumerate(cuts, first_index):
        span = pl.ds(pl.multiple_of(at[index] * 16, 16), rows)
        source = parts[part].at[pl.ds(first, rows)]
        loads.append(pltpu.make_async_copy(source, whole.at[span], semaphores.at[index]))
        loads[-1].start()
    return loads


def attention_kernel(
    frames,
    counts,
    tokens,
    cotangent,
    mods,
    bias,
    blocks,
    attn_in,
    parts,
    mixed_low,
    proj_out,
    resid_out,
    mlp_in,
    d_branch,
    d_branch_sum,
    mixed,
    whole,
    semaphores,
):
    rows, width = tokens.shape
    clip = pl.program_id(0)
    loads = [
        pltpu.make_async_copy(blocks.at[at], whole.at[at], semaphores.at[at]) for at in range(4)
    ]

    @pl.when(clip == 0)
    def _():
        for load in loads:
            load.start()

    tile = min(rows, 128)
    count = counts[clip]
    shift_one, scale_one, gate_one = (mods[0, at : at + 1, :] for at in range(3))
    shift_two, scale_two, gate_two = (mods[0, at : at + 1, :] for at in range(3, 6))
    for first in range(0, rows, tile):
        span = slice(first, first + tile)
        normed, _ = norm_parts(wide(tokens[span]))
        attn_in[span] = narrow(normed * (1.0 + scale_one) + shift_one)
        branch_back = narrow(wide(cotangent[span]) * valid_rows(count, tile, frames) * gate_two)
        d_branch[span] = branch_back
        part_sum = column_sum(wide(branch_back))
        d_branch_sum[0] = part_sum if first == 0 else d_branch_sum[0] + part_sum

    @pl.when(clip == 0)
    def _():
        for load in loads:
            load.wait()

    scale = (width // HEADS) ** -0.5
    source = attn_in[...]
    for low, high in column_cuts(width):
        span = slice(low, high)
        query = (dot_nn(source, whole[0, :, span]) + bias[0:1, span]) * scale
        parts[0, :, span], parts[1, :, span] = split_high(query)
        parts[2, :, span], parts[3, :, span] = split_high(dot_nn(source, whole[1, :, span]))
        parts[4, :, span] = narrow(dot_nn(source, whole[2, :, span]) + bias[2:3, span])
    offset = score_offset(count, tile, frames, 1)
    mixed[...] = jnp.zeros_like(mixed)
    for first in range(0, rows, tile):
        span = slice(first, first + tile)
        for low, high, start, stop in head_windows(width):
            lanes = slice(start, stop)
            mask = lane_mask(low, high, stop - start, jnp.bfloat16)
            key_high = parts[2, span, lanes]
            query_high = parts[0, span, lanes] * mask
            scores = dot_nt(query_high, key_high)
            scores += dot_nt(parts[1, span, lanes] * mask, key_high)
            scores += dot_nt(query_high, parts[3, span, lanes]) + offset
            expons = jnp.exp(scores - jnp.max(scores, axis=-1, keepdims=True))
            probs = expons * (1.0 / jnp.sum(expons, axis=-1, keepdims=True))
            out = dot_nn(narrow(probs), parts[4, span, lanes] * mask)
            mixed[span, lanes] += out
    mixed_low[...] = narrow(mixed[...])
    source = mixed_low[...]
    for low, high in column_cuts(width):
        span = slice(low, high)
        proj_out[:, span] = dot_nn(source, whole[3, :, span]) + bias[3:4, span]
    for first in range(0, rows, tile):
        span = slice(first, first + tile)
        resid = wide(tokens[span]) + valid_rows(count, tile, frames) * gate_one * proj_out[span]
        resid_out[span] = resid
        normed, _ = norm_parts(resid)
        mlp_in[span] = narrow(normed * (1.0 + scale_two) + shift_two)


def run_attention(frames, counts, tokens, cotangent, mods, bias, blocks):
    total, width = tokens.shape
    clips = mods.shape[0]
    rows = total // clips
    clip_rows = spec((rows, width), lambda clip: (clip, 0))
    low = jax.ShapeDtypeStruct((total, width), jnp.bfloat16)
    full = jax.ShapeDtypeStruct((total, width), jnp.float32)
    return pl.pallas_call(
        functools.partial(attention_kernel, frames),
        grid=(clips,),
        in_specs=[
            pl.BlockSpec(memory_space=pltpu.SMEM),
            clip_rows,
            clip_rows,
            spec((1,) + mods.shape[1:], lambda clip: (clip, 0, 0)),
            held(bias.shape),
            pl.BlockSpec(memory_space=pl.ANY),
        ],
        out_specs=[
            clip_rows,
            spec((5, rows, width), lambda clip: (0, clip, 0)),
            clip_rows,
            clip_rows,
            clip_rows,
            clip_rows,
            clip_rows,
            spec((1, 1, width), lambda clip: (clip, 0, 0)),
        ],
        out_shape=[
            low,
            jax.ShapeDtypeStruct((5, total, width), jnp.bfloat16),
            low,
            full,
            full,
            low,
            low,
            jax.ShapeDtypeStruct((clips, 1, width), jnp.float32),
        ],
        scratch_shapes=[
            pltpu.VMEM((rows, width), jnp.float32),
            pltpu.VMEM(blocks.shape, jnp.bfloat16),
            pltpu.SemaphoreType.DMA((4,)),
        ],
        compiler_params=pltpu.CompilerParams(vmem_limit_bytes=vmem_bytes),
        cost_estimate=little_cost,
    )(counts, tokens, cotangent, mods, bias, blocks)


def stacked(numbers):
    return jnp.stack([jnp.asarray(number, jnp.int32) for number in numbers])


def start_loads(cuts, at, parts, whole, semaphores):
    for index, (part, first, rows) in enumerate(cuts):
        span = pl.ds(pl.multiple_of(at[index] * 16, 16), rows)
        source = parts[part].at[pl.ds(first, rows)]
        pltpu.make_async_copy(source, whole.at[span], semaphores.at[index]).start()


def wait_loads(groups, at, parts, whole, semaphores):
    index = 0
    for step, cuts in enumerate(groups):
        base = index
        index += len(cuts)

        @pl.when(pl.program_id(0) == step)
        def _(cuts=cuts, base=base):
            for offset, (part, first, rows) in enumerate(cuts):
                span = pl.ds(pl.multiple_of(at[base + offset] * 16, 16), rows)
                source = parts[part].at[pl.ds(first, rows)]
                semaphore = semaphores.at[base + offset]
                pltpu.make_async_copy(source, whole.at[span], semaphore).wait()


def hidden_kernel(cuts, order, starts, mlp_in, bias, *refs):
    whole_out, hidden, slope, whole, semaphores, store_semaphores = refs[-6:]
    pieces = refs[:-6]
    step, steps = pl.program_id(0), pl.num_programs(0)
    width = mlp_in.shape[-1]
    span = pl.ds(pl.multiple_of(order[step] * width, width), width)

    @pl.when(step == 0)
    def _():
        start_loads([cut for group in cuts for cut in group], starts, pieces, whole, semaphores)

    wait_loads(cuts, starts, pieces, whole, semaphores)
    pltpu.make_async_copy(whole.at[span], whole_out.at[span], store_semaphores.at[step]).start()
    root = (2.0 / math.pi) ** 0.5
    source = mlp_in[...]
    block = whole.at[span]
    for low, high in column_cuts(width):
        lanes = slice(low, high)
        pre = dot_nn(source, block[:, lanes]) + bias[0, :, lanes]
        square = pre * pre
        bent = jnp.tanh(root * pre * (1.0 + 0.044715 * square))
        half = 0.5 + 0.5 * bent
        hidden[0, :, lanes] = narrow(pre * half)
        steep = (0.5 * root) * pre * (1.0 + 3 * 0.044715 * square)
        slope[0, :, lanes] = narrow(half + steep * (1.0 - bent * bent))

    @pl.when(step == steps - 1)
    def _():
        for at in range(len(cuts)):
            rows = pl.ds(pl.multiple_of(order[at] * width, width), width)
            pltpu.make_async_copy(
                whole.at[rows], whole_out.at[rows], store_semaphores.at[at]
            ).wait()


def run_hidden(mlp_in, gathered, bias):
    pieces, cuts, starts, order = gathered
    total, width = mlp_in.shape
    count = len(cuts)
    per_block = pl.BlockSpec((1, total, width), lambda at, order, starts: (order[at], 0, 0))
    out = jax.ShapeDtypeStruct((count, total, width), jnp.bfloat16)
    return pl.pallas_call(
        functools.partial(hidden_kernel, cuts),
        grid_spec=pltpu.PrefetchScalarGridSpec(
            num_scalar_prefetch=2,
            grid=(count,),
            in_specs=[
                pl.BlockSpec((total, width), lambda at, order, starts: (0, 0)),
                pl.BlockSpec((1, 1, width), lambda at, order, starts: (order[at], 0, 0)),
            ]
            + [pl.BlockSpec(memory_space=pl.ANY)] * len(pieces),
            out_specs=[pl.BlockSpec(memory_space=pl.ANY), per_block, per_block],
            scratch_shapes=[
                pltpu.VMEM((count * width, width), jnp.bfloat16),
                pltpu.SemaphoreType.DMA((len(starts),)),
                pltpu.SemaphoreType.DMA((count,)),
            ],
        ),
        out_shape=[jax.ShapeDtypeStruct((count * width, width), jnp.bfloat16), out, out],
        compiler_params=pltpu.CompilerParams(vmem_limit_bytes=vmem_bytes),
        cost_estimate=little_cost,
    )(stacked(order), stacked(starts), mlp_in, bias, *pieces)


def branch_kernel(
    frames,
    cuts,
    order,
    starts,
    counts,
    hidden,
    slope,
    d_branch,
    bias,
    gates,
    resid,
    cotangent,
    *refs,
):
    d_pre, d_pre_sum, block_out, d_gate, branch, whole, semaphores = refs[-7:]
    pieces = refs[:-7]
    step, steps = pl.program_id(0), pl.num_programs(0)
    total, width = resid.shape
    clips = gates.shape[0]
    rows = total // clips
    source, back = hidden[0], d_branch[...]

    @pl.when(step == 0)
    def _():
        start_loads([cut for group in cuts for cut in group], starts, pieces, whole, semaphores)
        branch[...] = jnp.zeros_like(branch)

    wait_loads(cuts, starts, pieces, whole, semaphores)
    block = whole.at[pl.ds(pl.multiple_of(order[step] * width, width), width)]
    for low, high in column_cuts(width):
        span = slice(low, high)
        d_hidden = dot_nt(back, block[span, :])
        low_back = narrow(d_hidden * wide(slope[0, :, span]))
        d_pre[0, :, span] = low_back
        d_pre_sum[0, :, span] = column_sum(wide(low_back))
        branch[:, span] += dot_nn(source, block[:, span])

    @pl.when(step == steps - 1)
    def _():
        for clip in range(clips):
            span = slice(clip * rows, (clip + 1) * rows)
            kept = valid_rows(counts[clip], rows, frames) * (branch[span] + bias[...])
            block_out[span] = narrow(resid[span] + gates[clip] * kept)
            d_gate[clip] = column_sum(wide(cotangent[span]) * kept)


def run_branch(frames, counts, hidden, slope, gathered, d_branch, bias, gates, resid, cotangent):
    pieces, cuts, starts, order = gathered
    count, total, width = hidden.shape
    clips = gates.shape[0]

    def all_of(*shape):
        return pl.BlockSpec(shape, lambda at, order, starts: (0,) * len(shape))

    per_block = pl.BlockSpec((1, total, width), lambda at, order, starts: (order[at], 0, 0))
    low = jax.ShapeDtypeStruct((total, width), jnp.bfloat16)
    return pl.pallas_call(
        functools.partial(branch_kernel, frames, cuts),
        grid_spec=pltpu.PrefetchScalarGridSpec(
            num_scalar_prefetch=2,
            grid=(count,),
            in_specs=[
                pl.BlockSpec(memory_space=pltpu.SMEM),
                per_block,
                per_block,
                all_of(total, width),
                all_of(*bias.shape),
                all_of(*gates.shape),
                all_of(total, width),
                all_of(total, width),
            ]
            + [pl.BlockSpec(memory_space=pl.ANY)] * len(pieces),
            out_specs=[
                per_block,
                pl.BlockSpec((1, 1, width), lambda at, order, starts: (order[at], 0, 0)),
                all_of(total, width),
                all_of(clips, 1, width),
            ],
            scratch_shapes=[
                pltpu.VMEM((total, width), jnp.float32),
                pltpu.VMEM((count * width, width), jnp.bfloat16),
                pltpu.SemaphoreType.DMA((len(starts),)),
            ],
        ),
        out_shape=[
            jax.ShapeDtypeStruct((count, total, width), jnp.bfloat16),
            jax.ShapeDtypeStruct((count, 1, width), jnp.float32),
            low,
            jax.ShapeDtypeStruct((clips, 1, width), jnp.float32),
        ],
        compiler_params=pltpu.CompilerParams(vmem_limit_bytes=vmem_bytes),
        cost_estimate=little_cost,
    )(stacked(order), stacked(starts), counts, hidden, slope, d_branch, bias, gates, resid, cotangent, *pieces)


def resid_kernel(
    frames,
    counts,
    d_pre,
    block,
    mods,
    resid,
    cotangent,
    proj,
    d_resid_out,
    d_proj,
    sums,
    total_grad,
):
    step, steps = pl.program_id(0), pl.num_programs(0)
    total, width = resid.shape
    clips = mods.shape[0]
    rows = total // clips
    tile = min(rows, 128)
    source = d_pre[0]

    @pl.when(step == 0)
    def _():
        total_grad[...] = jnp.zeros_like(total_grad)

    for low, high in column_cuts(width):
        span = slice(low, high)
        total_grad[:, span] += dot_nt(source, block[0, span, :])

    @pl.when(step == steps - 1)
    def _():
        for clip in range(clips):
            gate_one, scale_two = mods[clip, 2:3, :], mods[clip, 4:5, :]
            found = [0.0] * 4
            for first in range(clip * rows, (clip + 1) * rows, tile):
                span = slice(first, first + tile)
                grad = total_grad[span]
                normed, inverse = norm_parts(resid[span])
                back = norm_back(grad * (1.0 + scale_two), normed, inverse)
                d_resid = wide(cotangent[span]) + back
                d_resid_out[span] = d_resid
                kept = valid_rows(counts[clip], tile, frames) * d_resid
                low_back = narrow(kept * gate_one)
                d_proj[span] = low_back
                terms = (grad, grad * normed, kept * proj[span], wide(low_back))
                found = [old + column_sum(term) for old, term in zip(found, terms)]
            for at in range(4):
                sums[clip, at : at + 1, :] = found[at]


def run_resid(frames, counts, d_pre, blocks, mods, resid, cotangent, proj):
    count, total, width = d_pre.shape
    clips = mods.shape[0]
    return pl.pallas_call(
        functools.partial(resid_kernel, frames),
        grid=(count,),
        in_specs=[
            pl.BlockSpec(memory_space=pltpu.SMEM),
            spec((1, total, width), lambda at: (at, 0, 0)),
            spec((1, width, width), lambda at: (at, 0, 0)),
            held(mods.shape),
            held((total, width)),
            held((total, width)),
            held((total, width)),
        ],
        out_specs=[held((total, width)), held((total, width)), held((clips, 4, width))],
        out_shape=[
            jax.ShapeDtypeStruct((total, width), jnp.float32),
            jax.ShapeDtypeStruct((total, width), jnp.bfloat16),
            jax.ShapeDtypeStruct((clips, 4, width), jnp.float32),
        ],
        scratch_shapes=[pltpu.VMEM((total, width), jnp.float32)],
        compiler_params=pltpu.CompilerParams(vmem_limit_bytes=vmem_bytes),
        cost_estimate=little_cost,
    )(counts, d_pre, blocks, mods, resid, cotangent, proj)


def attention_back_kernel(
    frames, counts, d_proj, parts, block, d_qkv, sums, d_mixed, d_query, d_key, d_value
):
    rows, width = d_proj.shape
    tile = min(rows, 128)
    count = counts[pl.program_id(0)]
    source = d_proj[...]
    for low, high in column_cuts(width):
        d_mixed[:, low:high] = narrow(dot_nt(source, block[0, low:high, :]))
    scale = (width // HEADS) ** -0.5
    offset = score_offset(count, tile, frames, 0)
    for ref in (d_query, d_key, d_value):
        ref[...] = jnp.zeros_like(ref)
    for first in range(0, rows, tile):
        span = slice(first, first + tile)
        for low, high, start, stop in head_windows(width):
            lanes = slice(start, stop)
            mask = lane_mask(low, high, stop - start, jnp.bfloat16)
            query_high = parts[0, span, lanes] * mask
            key_high = parts[2, span, lanes] * mask
            back = d_mixed[span, lanes] * mask
            scores = dot_nt(key_high, query_high)
            scores += dot_nt(key_high, parts[1, span, lanes])
            scores += dot_nt(parts[3, span, lanes], query_high) + offset
            expons = jnp.exp(scores - jnp.max(scores, axis=0, keepdims=True))
            probs = expons * (1.0 / jnp.sum(expons, axis=0, keepdims=True))
            d_probs = dot_nt(parts[4, span, lanes], back)
            inner = jnp.sum(d_probs * probs, axis=0, keepdims=True)
            d_scores = narrow(probs * (d_probs - inner))
            d_value[span, lanes] += dot_nn(narrow(probs), back)
            d_key[span, lanes] += dot_nn(d_scores, query_high)
            d_query[span, lanes] += dot_tn(d_scores, key_high)
    for at, ref in enumerate((d_query, d_key, d_value)):
        low_back = narrow(ref[...] * scale) if at == 0 else narrow(ref[...])
        d_qkv[at] = low_back
        sums[0, at : at + 1, :] = column_sum(wide(low_back))
    d_qkv[3] = source


def run_attention_back(frames, counts, d_proj, parts, block):
    total, width = d_proj.shape
    clips = counts.shape[0]
    rows = total // clips
    return pl.pallas_call(
        functools.partial(attention_back_kernel, frames),
        grid=(clips,),
        in_specs=[
            pl.BlockSpec(memory_space=pltpu.SMEM),
            spec((rows, width), lambda clip: (clip, 0)),
            spec((5, rows, width), lambda clip: (0, clip, 0)),
            spec((1, width, width), lambda clip: (3, 0, 0), pipeline_mode=pl.Buffered(1)),
        ],
        out_specs=[
            spec((4, rows, width), lambda clip: (0, clip, 0)),
            spec((1, 3, width), lambda clip: (clip, 0, 0)),
        ],
        out_shape=[
            jax.ShapeDtypeStruct((4, total, width), jnp.bfloat16),
            jax.ShapeDtypeStruct((clips, 3, width), jnp.float32),
        ],
        scratch_shapes=[pltpu.VMEM((rows, width), jnp.bfloat16)]
        + [pltpu.VMEM((rows, width), jnp.float32)] * 3,
        compiler_params=pltpu.CompilerParams(vmem_limit_bytes=vmem_bytes),
        cost_estimate=little_cost,
    )(counts, d_proj, parts, block)


def input_kernel(d_qkv, block, mods, tokens, d_resid, input_grad, sums, total_grad):
    step, steps = pl.program_id(0), pl.num_programs(0)
    total, width = tokens.shape
    clips = mods.shape[0]
    rows = total // clips
    tile = min(rows, 128)
    source = d_qkv[0]

    @pl.when(step == 0)
    def _():
        total_grad[...] = jnp.zeros_like(total_grad)

    for low, high in column_cuts(width):
        span = slice(low, high)
        total_grad[:, span] += dot_nt(source, block[0, span, :])

    @pl.when(step == steps - 1)
    def _():
        for clip in range(clips):
            scale_one = mods[clip, 1:2, :]
            found = [0.0] * 2
            for first in range(clip * rows, (clip + 1) * rows, tile):
                span = slice(first, first + tile)
                grad = total_grad[span]
                normed, inverse = norm_parts(wide(tokens[span]))
                back = norm_back(grad * (1.0 + scale_one), normed, inverse)
                input_grad[span] = narrow(d_resid[span] + back)
                terms = (grad, grad * normed)
                found = [old + column_sum(term) for old, term in zip(found, terms)]
            for at in range(2):
                sums[clip, at : at + 1, :] = found[at]


def run_input(d_qkv, blocks, mods, tokens, d_resid):
    total, width = tokens.shape
    clips = mods.shape[0]
    return pl.pallas_call(
        input_kernel,
        grid=(3,),
        in_specs=[
            spec((1, total, width), lambda at: (at, 0, 0)),
            spec((1, width, width), lambda at: (at, 0, 0)),
            held(mods.shape),
            held((total, width)),
            held((total, width)),
        ],
        out_specs=[held((total, width)), held((clips, 2, width))],
        out_shape=[
            jax.ShapeDtypeStruct((total, width), jnp.bfloat16),
            jax.ShapeDtypeStruct((clips, 2, width), jnp.float32),
        ],
        scratch_shapes=[pltpu.VMEM((total, width), jnp.float32)],
        compiler_params=pltpu.CompilerParams(vmem_limit_bytes=vmem_bytes),
        cost_estimate=little_cost,
    )(d_qkv, blocks, mods, tokens, d_resid)


def halves_kernel(left_of, adds, steps, order, side, *refs):
    lefts = refs[: max(left_of) + 1]
    right = refs[len(lefts)]
    turned, total_low = refs[-2:]
    if adds:
        incoming, first_keep, first_out, second_keep, second_out = refs[len(lefts) + 1 : -2]
    else:
        out = refs[-3]
    step = pl.program_id(0)
    block = order[step]
    width = lefts[0].shape[-1]
    half = width // 2

    def pick(left, at):
        lanes = slice(at * half, (at + 1) * half)
        turned[...] = (left[:, lanes] if left.ndim == 2 else left[0, :, lanes]).T

    fresh = (step == 0) | (lefts[0].ndim == 3) | (len(lefts) > 1)
    for at in range(2):
        for index, left in enumerate(lefts):
            of_left = [block == number for number, source in enumerate(left_of) if source == index]

            @pl.when(fresh & (side[0] == at) & functools.reduce(jnp.logical_or, of_left))
            def _(left=left, at=at):
                pick(left, at)

    found = dot_nn(turned[...], right[0] if right.ndim == 3 else right[...])
    if not adds:
        out[0] = narrow(found)
        return
    total_low[...] = narrow(found + wide(incoming[0]))
    for state, target, rows in (
        (steps[0][0], first_keep, slice(0, half // 2)),
        (steps[0][1], first_out, slice(0, half // 2)),
        (steps[1][0], second_keep, slice(half // 2, half)),
        (steps[1][1], second_out, slice(half // 2, half)),
    ):

        @pl.when(functools.reduce(jnp.logical_or, [step == at_step for at_step in state]))
        def _(target=target, rows=rows):
            target[0] = total_low[rows]


def run_halves(lefts, left_of, right, side, at, incoming=None):
    total, width = lefts[0].shape[-2:]
    half = width // 2
    low_bit, high_bit = at % 2, at // 2
    order = stacked([at ^ 3, at ^ 1, at, at ^ 2])
    places = {
        "first_keep": [high_bit, high_bit, high_bit, 1 - high_bit],
        "first_out": [1 - high_bit, high_bit, high_bit, high_bit],
        "second_keep": [1 - low_bit, 1 - low_bit, low_bit, low_bit],
        "second_out": [1 - low_bit, low_bit, low_bit, low_bit],
    }
    steps = (((2, 3), (0, 1)), ((1, 2), (0, 3)))
    adds = incoming is not None
    table = stacked([place for row in places.values() for place in row])

    def block_of(array, *rest):
        if array.ndim == 2:
            return pl.BlockSpec(array.shape, lambda step, order, side, table: (0, 0))
        return pl.BlockSpec((1,) + array.shape[1:], lambda step, order, side, table: (order[step], 0, 0))

    per_block = pl.BlockSpec((1, half, width), lambda step, order, side, table: (order[step], 0, 0))
    operands = list(lefts) + [right]
    in_specs = [block_of(array) for array in operands]
    if adds:
        operands.append(incoming)
        in_specs.append(per_block)
        out_specs = [
            pl.BlockSpec(
                (1, half // 2, width),
                functools.partial(lambda row, step, order, side, table: (table[row * 4 + step], 0, 0), row),
            )
            for row in range(4)
        ]
        out_shape = [jax.ShapeDtypeStruct((2, half // 2, width), jnp.bfloat16)] * 4
    else:
        out_specs = per_block
        out_shape = jax.ShapeDtypeStruct((4, half, width), jnp.bfloat16)

    def body(order, side, table, *refs):
        halves_kernel(left_of, adds, steps, order, side, *refs)

    return pl.pallas_call(
        body,
        grid_spec=pltpu.PrefetchScalarGridSpec(
            num_scalar_prefetch=3,
            grid=(4,),
            in_specs=in_specs,
            out_specs=out_specs,
            scratch_shapes=[
                pltpu.VMEM((half, total), jnp.bfloat16),
                pltpu.VMEM((half, width), jnp.bfloat16),
            ],
        ),
        out_shape=out_shape,
        compiler_params=pltpu.CompilerParams(vmem_limit_bytes=vmem_bytes),
        cost_estimate=little_cost,
    )(order, stacked([side]), table, *operands)


def tie(*values):
    return lax.optimization_barrier(values)


def packed(arrays, tile):
    flat = jnp.concatenate([array.reshape(-1) for array in arrays])
    return jnp.pad(flat, (0, -flat.shape[0] % (tile * 128))).reshape(-1, 128)


def core_swap(array):
    count = lax.axis_size("dp")
    return lax.ppermute(array, "dp", [(at, at ^ 1) for at in range(count)])


def chip_shift(array, step):
    count = lax.axis_size("dp")
    return lax.ppermute(array, "dp", [(at, (at + 2 * step) % count) for at in range(count)])


def chip_swap(array, bits):
    count = lax.axis_size("dp")
    return lax.ppermute(array, "dp", [(at, at ^ (2 * bits)) for at in range(count)])


def rank_swap(array, bits):
    count = lax.axis_size("fsdp")
    return lax.ppermute(array, "fsdp", [(at, at ^ bits) for at in range(count)])


def entry(array, at, axis=0):
    return lax.dynamic_index_in_dim(array, at, axis, keepdims=False)


def place_kernel(cuts, at, *refs):
    parts, whole, held_rows, semaphores = refs[:-3], refs[-3], refs[-2], refs[-1]
    spans, loads, stores = [], [], []
    for index, (part, first, rows) in enumerate(cuts):
        spans.append(pl.ds(pl.multiple_of(at[index] * 16, 16), rows))
        source = parts[part].at[pl.ds(first, rows)]
        loads.append(
            pltpu.make_async_copy(source, held_rows.at[spans[index]], semaphores.at[0, index])
        )
        loads[index].start()
    for index, span in enumerate(spans):
        loads[index].wait()
        stores.append(
            pltpu.make_async_copy(held_rows.at[span], whole.at[span], semaphores.at[1, index])
        )
        stores[index].start()
    for store in stores:
        store.wait()


def place(parts, cuts, starts, rows):
    width = parts[0].shape[-1]
    dtype = parts[0].dtype
    return pl.pallas_call(
        functools.partial(place_kernel, cuts),
        in_specs=[pl.BlockSpec(memory_space=pltpu.SMEM)]
        + [pl.BlockSpec(memory_space=pl.ANY)] * len(parts),
        out_specs=pl.BlockSpec(memory_space=pl.ANY),
        out_shape=jax.ShapeDtypeStruct((rows, width), dtype),
        scratch_shapes=[
            pltpu.VMEM((rows, width), dtype),
            pltpu.SemaphoreType.DMA((2, len(cuts))),
        ],
        compiler_params=pltpu.CompilerParams(vmem_limit_bytes=vmem_bytes),
        cost_estimate=little_cost,
    )(stacked(starts), *parts)


def own_rows(parts, group):
    ranks, at = lax.axis_size("fsdp"), lax.axis_index("fsdp")
    shares = ranks // group
    count, _, row_part, col_part = parts.shape
    chunk = row_part // shares
    split = parts.reshape(count, group, shares, chunk, col_part).transpose(1, 2, 0, 3, 4)
    split = split.reshape(ranks, count, chunk, col_part)
    if shares > 1:
        moved = lax.all_to_all(split, "fsdp", 0, 0, tiled=True)
        (moved,) = yield (moved,)
        yield moved.transpose(1, 2, 0, 3).reshape(count, chunk, ranks * col_part)
        return
    panels = [entry(split, at)]
    panels += [rank_swap(entry(split, at ^ bits), bits) for bits in range(1, ranks)]
    panels = yield tuple(panels)
    placed = [
        lax.select_n(at, *[panels[panel ^ index] for index in range(ranks)])
        for panel in range(ranks)
    ]
    yield jnp.concatenate(placed, axis=2)


def shard_rows(split, group):
    ranks, count, chunk, col_part = split.shape
    shares = ranks // group
    moved = lax.all_to_all(split, "fsdp", 0, 0, tiled=True)
    moved = moved.reshape(group, shares, count, chunk, col_part).transpose(2, 0, 1, 3, 4)
    return moved.reshape(count, group, shares * chunk, col_part)


def gather_blocks(rows, group):
    ranks, dp_count = lax.axis_size("fsdp"), lax.axis_size("dp")
    shares = ranks // group
    chunk, total = rows.shape
    all_rows = lax.all_gather(rows, ("fsdp", "dp"), axis=0, tiled=True)
    if shares > 1:
        all_rows = all_rows.reshape(group, shares, dp_count, chunk, total).transpose(0, 2, 1, 3, 4)
    return all_rows.reshape(group, total, total)


def join_line(found):
    chips, chip = lax.axis_size("dp") // 2, lax.axis_index("dp") // 2
    chunk = found[0].shape[0]
    starts = [(chip - step) % chips * (chunk // 16) for step in range(chips)]
    return place(found, [(step, 0, chunk) for step in range(chips)], starts, chips * chunk)


def gather_second(rows, group):
    ranks, at = lax.axis_size("fsdp"), lax.axis_index("fsdp")
    total = rows.shape[-1]
    if ranks != group:
        blocks = gather_blocks(rows, group).reshape(group * total, total)
        for _ in range(3):
            (blocks,) = yield (blocks,)
        cuts = [[(0, index * total, total)] for index in range(group)]
        yield [blocks], cuts, [index * (total // 16) for index in range(group)], range(group)
        return
    chips = lax.axis_size("dp") // 2
    core = lax.axis_index("dp") % 2
    chunk, half = rows.shape[0], total // 2
    others = yield tuple(chip_shift(rows, step) for step in range(1, chips))
    line = join_line([rows, *others])
    cuts = [(side, step * chunk, chunk) for side in range(2) for step in range(chips)]
    starts = [
        (2 * step + side) * (chunk // 16) for side in (core, 1 - core) for step in range(chips)
    ]
    (own,) = yield (place([line, core_swap(line)], cuts, starts, total),)
    share = lax.dynamic_slice_in_dim(own, core * half, half, 0)
    mine = yield tuple(rank_swap(share, bits) for bits in range(1, ranks))
    parts, cuts, starts = [own], [[(0, 0, total)]], [at * (total // 16)]
    for bits in range(1, ranks):
        parts += [mine[bits - 1], core_swap(mine[bits - 1])]
        cuts.append([(2 * bits - 1, 0, half), (2 * bits, 0, half)])
        starts += [((at ^ bits) * 2 + side) * (half // 16) for side in (core, 1 - core)]
    yield parts, cuts, starts, [at ^ bits for bits in range(ranks)]


def gather_own(rows, group):
    ranks = lax.axis_size("fsdp")
    shares = ranks // group
    if shares > 1:
        sets = [[share + shares * block for share in range(shares)] for block in range(group)]
        rows = lax.all_gather(rows, "fsdp", axis=1, tiled=True, axis_index_groups=sets)
    return lax.all_gather(rows, "dp", axis=1, tiled=True)


def sum_blocks(lefts, left_of, right, group):
    ranks, dp_count = lax.axis_size("fsdp"), lax.axis_size("dp")
    shares = ranks // group
    total = lefts[0].shape[-1]
    if shares > 1:
        blocks = jnp.stack(
            [
                narrow(
                    fast_dot(
                        "tr,te->re",
                        lefts[index] if lefts[index].ndim == 2 else lefts[index][block],
                        right if right.ndim == 2 else right[block],
                    )
                )
                for block, index in enumerate(left_of)
            ]
        )
        chunk = total // (dp_count * shares)
        blocks = blocks.reshape(group, dp_count, shares, chunk, -1).transpose(0, 2, 1, 3, 4)
        rows = lax.psum_scatter(
            blocks.reshape(group * total, -1), ("fsdp", "dp"), scatter_dimension=0, tiled=True
        )
        for _ in range(7):
            (rows,) = yield (rows,)
        yield gather_own(rows[None], group)[0]
        return
    chips, half = dp_count // 2, total // 2
    chunk = half // chips
    at = lax.axis_index("fsdp")
    core, chip = lax.axis_index("dp") % 2, lax.axis_index("dp") // 2
    low_bit, high_bit = at % 2, at // 2
    (away,) = yield (run_halves(lefts, left_of, right, 1 - core, at),)
    (away_in,) = yield (core_swap(away),)
    first, first_out, second, second_out = run_halves(lefts, left_of, right, core, at, away_in)
    first_out, second_out = yield (first_out, second_out)
    first_in, second_in = yield (rank_swap(first_out, 1), rank_swap(second_out, 2))
    first = narrow(wide(first) + wide(first_in)).reshape(2, chips // 2, chunk, -1)
    second = narrow(wide(second) + wide(second_in)).reshape(2, chips // 2, chunk, -1)
    first_in = rank_swap(entry(first, 1 - high_bit), 2)
    second_in = rank_swap(entry(second, 1 - low_bit), 1)
    first_in, second_in = yield (first_in, second_in)
    first = narrow(wide(entry(first, high_bit)) + wide(first_in))
    second = narrow(wide(entry(second, low_bit)) + wide(second_in))
    line = jnp.concatenate([first, second])
    step = 1
    while step < chips:
        bit = chip // step % 2
        line = line.reshape(-1, 2, *line.shape[1:])
        (line_in,) = yield (chip_swap(entry(line, 1 - bit, 1), step),)
        line = narrow(wide(entry(line, bit, 1)) + wide(line_in))
        step *= 2
    yield lax.all_gather(line[0], "dp", axis=0, tiled=True)


def fast_dot(subscripts, left, right):
    return jnp.einsum(subscripts, left, right, preferred_element_type=jnp.float32)


def products_kernel(chips, at, gathered, left_root, right_root, out, whole, semaphores):
    chunk, width = left_root.shape
    ranks = out.shape[0]
    copies = []
    for index in range(2 * chips):
        first = (index % 2 * chips + index // 2) * chunk
        copies.append(
            pltpu.make_async_copy(
                gathered.at[pl.ds(index * chunk, chunk)],
                whole.at[pl.ds(first, chunk)],
                semaphores.at[index],
            )
        )
        copies[-1].start()
    for copy in copies:
        copy.wait()
    first = at[0] * 16
    grad = whole[...]
    picked = lax.broadcasted_iota(jnp.int32, (width, chunk), 0) - first
    picked = picked == lax.broadcasted_iota(jnp.int32, (width, chunk), 1)
    own_columns = narrow(dot_nn(grad, narrow(picked.astype(jnp.float32))))
    side_high, side_low = split_high(dot_nn(left_root[...], grad))
    right = right_root[...]
    precond = dot_nn(side_high, right) + dot_nn(side_low, right)
    outer = dot_nt(whole[pl.ds(pl.multiple_of(first, 16), chunk), :], grad)
    inner = dot_tn(own_columns, grad)
    for at_out, product in enumerate((precond, outer, inner)):
        low = narrow(product)
        for rank in range(ranks):
            span = slice(rank * (width // ranks), (rank + 1) * (width // ranks))
            out[rank, at_out] = low[:, span]


def owned_step(whole, left_root, right_root, group):
    ranks, dp_count = lax.axis_size("fsdp"), lax.axis_size("dp")
    shares = ranks // group
    chunk, total = left_root.shape
    col_part = total // ranks
    first = lax.axis_index("dp") * (chunk * shares) + lax.axis_index("fsdp") % shares * chunk
    if shares == 1:
        return pl.pallas_call(
            functools.partial(products_kernel, dp_count // 2),
            in_specs=[
                pl.BlockSpec(memory_space=pltpu.SMEM),
                pl.BlockSpec(memory_space=pl.ANY),
                pl.BlockSpec(memory_space=pltpu.VMEM),
                pl.BlockSpec(memory_space=pltpu.VMEM),
            ],
            out_specs=pl.BlockSpec(memory_space=pltpu.VMEM),
            out_shape=jax.ShapeDtypeStruct((ranks, 3, chunk, col_part), jnp.bfloat16),
            scratch_shapes=[
                pltpu.VMEM((total, total), jnp.bfloat16),
                pltpu.SemaphoreType.DMA((dp_count,)),
            ],
            compiler_params=pltpu.CompilerParams(vmem_limit_bytes=vmem_bytes),
            cost_estimate=little_cost,
        )((first // 16)[None], whole, left_root, right_root)
    grad_rows = lax.dynamic_slice_in_dim(whole, first, chunk, 0)
    own_columns = lax.dynamic_slice_in_dim(whole, first, chunk, 1)
    outer = fast_dot("rk,jk->rj", grad_rows, whole)
    inner = fast_dot("kr,kj->rj", own_columns, whole)
    side_high, side_low = split_high(fast_dot("rk,kj->rj", left_root, whole))
    precond = fast_dot("rk,kj->rj", side_high, right_root) + fast_dot(
        "rk,kj->rj", side_low, right_root
    )
    products = narrow(jnp.stack([precond, outer, inner]))
    return products.reshape(3, chunk, ranks, col_part).transpose(2, 0, 1, 3)


def per_device(
    tokens,
    conditioning,
    frame_counts,
    cotangent,
    weights,
    biases,
    momentum,
    left_stats,
    right_stats,
    left_roots,
    right_roots,
    bias_moment,
    bias_second,
):
    group = 4
    mod_count = 6
    clip_count, pos_count, frames, width = tokens.shape
    token_count = clip_count * pos_count * frames
    block_count, row_part, col_part = weights.shape
    dp_count, ranks = lax.axis_size("dp"), lax.axis_size("fsdp")
    dp_at, rank_at = lax.axis_index("dp"), lax.axis_index("fsdp")
    all_clips = clip_count * dp_count
    bias_part = biases.shape[0]
    stream = tokens.reshape(token_count, width)
    grad_out = cotangent.reshape(token_count, width)
    low_weights = narrow(weights).reshape(block_count, row_part, col_part)
    shards = low_weights[mod_count:].reshape(-1, group, row_part, col_part)

    weight_rows = own_rows(shards, group)
    weight_panels = next(weight_rows)
    cond_low = narrow(jax.nn.silu(conditioning))
    first_parts = lax.all_gather(packed([cond_low, narrow(biases)], 16), "dp", axis=0, tiled=True)
    weight_panels, first_parts = tie(weight_panels, first_parts)
    attn_rows, one_rows, two_rows = weight_rows.send(weight_panels)
    attn_w = gather_blocks(attn_rows, group)
    two_w = gather_blocks(two_rows, group).reshape(group * width, width)
    two_gathered = (
        [two_w],
        [[(0, index * width, width)] for index in range(group)],
        [index * (width // 16) for index in range(group)],
        range(group),
    )

    first_parts = first_parts.reshape(dp_count, -1)
    cond_all = first_parts[:, : clip_count * width].reshape(all_clips, width)
    bias_rows = wide(first_parts[:, clip_count * width : clip_count * width + bias_part])
    cond_rows = lax.dynamic_slice_in_dim(cond_all, dp_at * row_part, row_part, 1)
    cond_cols = wide(lax.dynamic_slice_in_dim(cond_all, rank_at * col_part, col_part, 1))
    mod_parts = fast_dot("cr,jre->cje", cond_rows, low_weights[:mod_count])
    mod_parts = lax.all_to_all(mod_parts, "dp", 0, 0, tiled=True)
    mod_parts, one_rows = tie(mod_parts, one_rows)
    one_steps = gather_second(one_rows, group)
    one_parts = next(one_steps)
    mod_cols = jnp.sum(mod_parts.reshape(dp_count, clip_count, mod_count, col_part), axis=0)
    left_cond = jnp.einsum("jrk,ck->jrc", left_roots[:mod_count], cond_cols, precision=precise)
    mod_size, bias_size = mod_cols.size, dp_count * bias_part
    second_parts = lax.all_gather(
        packed([mod_cols, bias_rows, left_cond], 8), "fsdp", axis=0, tiled=True
    )
    second_parts, one_parts = tie(second_parts, one_parts)
    one_parts, attn_w = tie(one_steps.send(one_parts), attn_w)
    one_parts = one_steps.send(one_parts)
    second_parts = second_parts.reshape(ranks, -1)
    mods = second_parts[:, :mod_size].reshape(ranks, clip_count, mod_count, col_part)
    mods = mods.transpose(1, 2, 0, 3).reshape(clip_count, mod_count, width)
    bias_all = second_parts[:, mod_size : mod_size + bias_size].reshape(ranks, dp_count, bias_part)
    bias_all = bias_all.transpose(1, 0, 2).reshape(-1, width)
    left_size = mod_size + bias_size + left_cond.size
    left_cond = jnp.sum(second_parts[:, mod_size + bias_size : left_size], axis=0)
    left_cond = left_cond.reshape(mod_count, row_part, all_clips)
    mods = mods + bias_all[:mod_count]
    bias_table = jnp.concatenate(
        [bias_all[6:7], jnp.zeros((1, width), jnp.float32), bias_all[7:14]]
    )

    attn_in, parts, mixed, proj, resid, mlp_in, d_branch, d_branch_sums = run_attention(
        frames, frame_counts, stream, grad_out, mods, bias_table, attn_w
    )
    mlp_in, one_parts = tie(mlp_in, one_parts)
    one_w, hidden, slope = run_hidden(mlp_in, one_steps.send(one_parts), bias_table[4:8, None])
    one_w = one_w.reshape(group, width, width)

    two_steps = sum_blocks([hidden], [0] * group, d_branch, group)
    two_parts = next(two_steps)
    roots = jnp.stack([narrow(left_roots[mod_count:]), narrow(right_roots[mod_count:])])
    hidden, two_parts, roots = tie(hidden, two_parts, roots)
    two_parts = two_steps.send(two_parts)
    root_rows = own_rows(roots.reshape(-1, group, row_part, col_part), group)
    root_panels = next(root_rows)
    d_pre, d_pre_sums, block_out, d_gate_two = run_branch(
        frames,
        frame_counts,
        hidden,
        slope,
        two_gathered,
        d_branch,
        bias_table[8:9],
        mods[:, 5:6],
        resid,
        grad_out,
    )
    d_pre, root_panels = tie(d_pre, root_panels)
    root_rows = root_rows.send(root_panels)
    d_pre, two_parts, root_rows = tie(d_pre, two_parts, root_rows)
    two_parts = two_steps.send(two_parts)
    d_pre, two_parts = tie(d_pre, two_parts)
    two_parts = two_steps.send(two_parts)
    left_rows, right_rows = jnp.split(root_rows, 2)
    right_wholes = [gather_own(rows[None], group)[0] for rows in right_rows]
    one_steps = sum_blocks([mlp_in], [0] * group, d_pre, group)
    one_parts = next(one_steps)
    d_pre, one_parts = tie(d_pre, one_parts)
    one_parts = one_steps.send(one_parts)
    d_resid, d_proj, resid_sums = run_resid(
        frames, frame_counts, d_pre, one_w, mods, resid, grad_out, proj
    )
    d_proj, one_parts = tie(d_proj, one_parts)
    one_parts = one_steps.send(one_parts)
    d_proj, one_parts, two_parts, right_wholes[2] = tie(
        d_proj, one_parts, two_parts, right_wholes[2]
    )
    two_parts = two_steps.send(two_parts)
    one_parts = one_steps.send(one_parts)
    d_heads, head_sums = run_attention_back(frames, frame_counts, d_proj, parts, attn_w)
    d_heads, two_parts, one_parts, right_wholes[1], right_wholes[0] = tie(
        d_heads, two_parts, one_parts, right_wholes[1], right_wholes[0]
    )
    two_parts = two_steps.send(two_parts)
    one_parts = one_steps.send(one_parts)
    attn_steps = sum_blocks([attn_in, mixed], [0, 0, 0, 1], d_heads, group)
    attn_parts = next(attn_steps)
    d_heads, attn_parts = tie(d_heads, attn_parts)
    attn_parts = attn_steps.send(attn_parts)
    d_heads, attn_parts, two_parts, one_parts = tie(d_heads, attn_parts, two_parts, one_parts)
    two_parts = two_steps.send(two_parts)
    one_parts = one_steps.send(one_parts)
    attn_parts = attn_steps.send(attn_parts)
    d_heads, attn_parts = tie(d_heads, attn_parts)
    attn_parts = attn_steps.send(attn_parts)
    input_grad, input_sums = run_input(d_heads, attn_w, mods, stream, d_resid)
    input_sums, one_parts, two_parts = tie(input_sums, one_parts, two_parts)
    whole_two = two_steps.send(two_parts)
    one_parts = one_steps.send(one_parts)

    d_mods = jnp.stack(
        [
            input_sums[:, 0],
            input_sums[:, 1],
            resid_sums[:, 2],
            resid_sums[:, 0],
            resid_sums[:, 1],
            d_gate_two[:, 0],
        ],
        axis=1,
    )
    head_sums = jnp.sum(head_sums, axis=0)
    grad_bias = jnp.concatenate(
        [
            jnp.sum(d_mods, axis=0),
            head_sums[0:1],
            head_sums[2:3],
            jnp.sum(resid_sums[:, 3], axis=0)[None],
            d_pre_sums[:, 0],
            jnp.sum(d_branch_sums, axis=0),
        ]
    )
    to_ranks = jnp.concatenate(
        [
            d_mods.reshape(clip_count, mod_count, ranks, col_part)
            .transpose(2, 0, 1, 3)
            .reshape(ranks, mod_size),
            grad_bias.reshape(dp_count, ranks, bias_part)
            .transpose(1, 0, 2)
            .reshape(ranks, bias_size),
        ],
        axis=1,
    )
    rank_sums = lax.all_to_all(to_ranks, "fsdp", 0, 0, tiled=True)
    rank_sums, attn_parts, one_parts = tie(rank_sums, attn_parts, one_parts)
    attn_parts = attn_steps.send(attn_parts)
    whole_one = one_steps.send(one_parts)
    rank_sums = jnp.sum(rank_sums, axis=0)
    to_rows = jnp.concatenate(
        [
            jnp.broadcast_to(rank_sums[None, :mod_size], (dp_count, mod_size)),
            rank_sums[mod_size:].reshape(dp_count, bias_part),
        ],
        axis=1,
    )
    to_rows, attn_parts = tie(to_rows, attn_parts)
    attn_parts = attn_steps.send(attn_parts)
    products_two = owned_step(whole_two, left_rows[2], right_wholes[2], group)
    products_two, attn_parts = tie(products_two, attn_parts)
    attn_parts = attn_steps.send(attn_parts)
    back_two = shard_rows(products_two, group)
    products_one = owned_step(whole_one, left_rows[1], right_wholes[1], group)
    to_rows, back_two, products_one, attn_parts = tie(to_rows, back_two, products_one, attn_parts)
    whole_attn = attn_steps.send(attn_parts)
    back_one = shard_rows(products_one, group)
    from_rows = lax.all_to_all(to_rows, "dp", 0, 0, tiled=True)
    bias_grad = jnp.sum(from_rows[:, mod_size:], axis=0)
    mod_grad_cols = from_rows[:, :mod_size].reshape(all_clips, mod_count, col_part)
    mod_grad = lax.all_gather(packed([mod_grad_cols], 8), "fsdp", axis=0, tiled=True)
    mod_grad = mod_grad.reshape(ranks, -1)[:, : mod_grad_cols.size]
    mod_grad = mod_grad.reshape(ranks, all_clips, mod_count, col_part).transpose(1, 2, 0, 3)
    mod_grad = mod_grad.reshape(all_clips, mod_count, width)

    mod_grad_rows = lax.dynamic_slice_in_dim(mod_grad, dp_at * row_part, row_part, 2)
    right_parts = jnp.einsum(
        "cjk,jke->cje", mod_grad_rows, right_roots[:mod_count], precision=precise
    )
    cond_wide = wide(cond_all)
    cond_row_wide = wide(cond_rows)
    mod_gram = jnp.einsum("cjk,bjk->jcb", mod_grad, mod_grad, precision=precise)
    cond_gram = jnp.einsum("ck,bk->cb", cond_wide, cond_wide, precision=precise)
    mod_side = jnp.einsum("jcb,be->jce", mod_gram, cond_cols, precision=precise)
    ada_left = jnp.einsum("cr,jce->jre", cond_row_wide, mod_side, precision=precise)
    cond_side = jnp.einsum("cb,bje->jce", cond_gram, mod_grad_cols, precision=precise)
    ada_right = jnp.einsum("cjr,jce->jre", mod_grad_rows, cond_side, precision=precise)

    right_parts = lax.all_gather(packed([right_parts], 8), "dp", axis=0, tiled=True)
    mod_right = jnp.sum(right_parts.reshape(dp_count, -1), axis=0)[: mod_grad_cols.size]
    mod_right = mod_right.reshape(all_clips, mod_count, col_part)
    ada_pre = jnp.einsum("jrc,cje->jre", left_cond, mod_right, precision=precise)
    whole_attn, back_one = tie(whole_attn, back_one)
    back_attn = shard_rows(owned_step(whole_attn, left_rows[0], right_wholes[0], group), group)

    def joined(at, ada):
        return jnp.concatenate([ada, wide(back_attn[at]), wide(back_one[at]), wide(back_two[at])])

    precond = joined(0, ada_pre)
    left_new = stat_decay * left_stats + (1.0 - stat_decay) * joined(1, ada_left)
    right_new = stat_decay * right_stats + (1.0 - stat_decay) * joined(2, ada_right)
    momentum_new = moment_decay * momentum + precond
    weights_new = weights - weight_rate * momentum_new
    weights_copy = weights_new.astype(jnp.bfloat16)
    bias_second_new = stat_decay * bias_second + (1.0 - stat_decay) * bias_grad * bias_grad
    bias_moment_new = moment_decay * bias_moment + bias_grad * lax.rsqrt(
        bias_second_new + diag_epsilon
    )
    biases_new = biases - bias_rate * bias_moment_new
    return (
        block_out.reshape(tokens.shape),
        input_grad.reshape(tokens.shape),
        left_new,
        right_new,
        momentum_new,
        weights_new,
        weights_copy,
        bias_moment_new,
        bias_second_new,
        biases_new,
    )


def solution(mesh):
    placed = (
        P("dp", "fsdp", None, None),
        P("dp", None),
        P("dp"),
        P("dp", "fsdp", None, None),
        P(None, "dp", "fsdp"),
        P(("dp", "fsdp")),
        P(None, "dp", "fsdp"),
        P(None, "dp", "fsdp"),
        P(None, "dp", "fsdp"),
        P(None, "dp", "fsdp"),
        P(None, "dp", "fsdp"),
        P(("dp", "fsdp")),
        P(("dp", "fsdp")),
    )
    return jax.shard_map(
        per_device,
        mesh=mesh,
        in_specs=placed,
        out_specs=(
            P("dp", "fsdp", None, None),
            P("dp", "fsdp", None, None),
            P(None, "dp", "fsdp"),
            P(None, "dp", "fsdp"),
            P(None, "dp", "fsdp"),
            P(None, "dp", "fsdp"),
            P(None, "dp", "fsdp"),
            P(("dp", "fsdp")),
            P(("dp", "fsdp")),
            P(("dp", "fsdp")),
        ),
        check_vma=False,
    )
```

```python
import functools
import math

import jax
import jax.numpy as jnp
from jax import lax
from jax.experimental import pallas as pl
from jax.experimental.pallas import tpu as pltpu
from jax.sharding import PartitionSpec as P

HEADS = 16


precise = lax.Precision.HIGHEST
norm_epsilon = 1e-06
masked_score = -1e30
stat_decay = 0.5
moment_decay = 0.9
weight_rate = 0.7
bias_rate = 0.1
diag_epsilon = 1e-08
vmem_bytes = 50 * 2**20
little_cost = pl.CostEstimate(flops=1024, bytes_accessed=1024, transcendentals=0)


def narrow(array):
    return array.astype(jnp.bfloat16)


def wide(array):
    return array.astype(jnp.float32)


def spec(shape, index_map, **keywords):
    return pl.BlockSpec(shape, index_map, **keywords)


def held(shape):
    return pl.BlockSpec(shape, lambda step: (0,) * len(shape), pipeline_mode=pl.Buffered(1))


def column_cuts(total):
    cuts, at = [], 0
    while at < total:
        cuts.append((at, min(total, at + 256)))
        at += 256
    return cuts


def dot_nn(left, right):
    return lax.dot_general(left, right, (((1,), (0,)), ((), ())), preferred_element_type=jnp.float32)


def dot_nt(left, right):
    return lax.dot_general(left, right, (((1,), (1,)), ((), ())), preferred_element_type=jnp.float32)


def dot_tn(left, right):
    return lax.dot_general(left, right, (((0,), (0,)), ((), ())), preferred_element_type=jnp.float32)


def split_high(values):
    high = narrow(values)
    return high, narrow(values - wide(high))


def valid_rows(count, rows, frames):
    at = lax.broadcasted_iota(jnp.int32, (rows, 1), 0)
    return (lax.rem(at, frames) < count).astype(jnp.float32)


def score_offset(count, size, frames, key_axis):
    first = lax.broadcasted_iota(jnp.int32, (size, size), 0)
    second = lax.broadcasted_iota(jnp.int32, (size, size), 1)
    key = second if key_axis == 1 else first
    met = (lax.div(first, frames) == lax.div(second, frames)) & (lax.rem(key, frames) < count)
    return jnp.where(met, 0.0, masked_score)


def head_windows(width):
    size = width // HEADS
    windows = []
    for head in range(HEADS):
        low, high = head * size, (head + 1) * size
        start = low // 128 * 128
        stop = min(width, -(-high // 128) * 128)
        windows.append((low - start, high - start, start, stop))
    return windows


def lane_mask(low, high, count, dtype):
    lanes = lax.broadcasted_iota(jnp.int32, (1, count), 1)
    return ((lanes >= low) & (lanes < high)).astype(jnp.float32).astype(dtype)


def norm_parts(values):
    centered = values - jnp.mean(values, axis=-1, keepdims=True)
    variance = jnp.mean(centered * centered, axis=-1, keepdims=True)
    inverse = lax.rsqrt(variance + norm_epsilon)
    return centered * inverse, inverse


def norm_back(grad, normed, inverse):
    first = jnp.mean(grad, axis=-1, keepdims=True)
    second = jnp.mean(grad * normed, axis=-1, keepdims=True)
    return (grad - first - normed * second) * inverse


def column_sum(values):
    return jnp.sum(values, axis=0, keepdims=True)


def start_loads(cuts, at, parts, whole, semaphores, first_index=0):
    loads = []
    for index, (part, first, rows) in enumerate(cuts, first_index):
        span = pl.ds(pl.multiple_of(at[index] * 16, 16), rows)
        source = parts[part].at[pl.ds(first, rows)]
        loads.append(pltpu.make_async_copy(source, whole.at[span], semaphores.at[index]))
        loads[-1].start()
    return loads


def attention_kernel(
    frames,
    counts,
    tokens,
    cotangent,
    mods,
    bias,
    blocks,
    attn_in,
    parts,
    mixed_low,
    proj_out,
    resid_out,
    mlp_in,
    d_branch,
    d_branch_sum,
    mixed,
    whole,
    semaphores,
):
    rows, width = tokens.shape
    clip = pl.program_id(0)
    loads = [
        pltpu.make_async_copy(blocks.at[at], whole.at[at], semaphores.at[at]) for at in range(4)
    ]

    @pl.when(clip == 0)
    def _():
        for load in loads:
            load.start()

    tile = min(rows, 128)
    count = counts[clip]
    shift_one, scale_one, gate_one = (mods[0, at : at + 1, :] for at in range(3))
    shift_two, scale_two, gate_two = (mods[0, at : at + 1, :] for at in range(3, 6))
    for first in range(0, rows, tile):
        span = slice(first, first + tile)
        normed, _ = norm_parts(wide(tokens[span]))
        attn_in[span] = narrow(normed * (1.0 + scale_one) + shift_one)
        branch_back = narrow(wide(cotangent[span]) * valid_rows(count, tile, frames) * gate_two)
        d_branch[span] = branch_back
        part_sum = column_sum(wide(branch_back))
        d_branch_sum[0] = part_sum if first == 0 else d_branch_sum[0] + part_sum

    @pl.when(clip == 0)
    def _():
        for load in loads:
            load.wait()

    scale = (width // HEADS) ** -0.5
    source = attn_in[...]
    for low, high in column_cuts(width):
        span = slice(low, high)
        query = (dot_nn(source, whole[0, :, span]) + bias[0:1, span]) * scale
        parts[0, :, span], parts[1, :, span] = split_high(query)
        parts[2, :, span], parts[3, :, span] = split_high(dot_nn(source, whole[1, :, span]))
        parts[4, :, span] = narrow(dot_nn(source, whole[2, :, span]) + bias[2:3, span])
    offset = score_offset(count, tile, frames, 1)
    mixed[...] = jnp.zeros_like(mixed)
    for first in range(0, rows, tile):
        span = slice(first, first + tile)
        for low, high, start, stop in head_windows(width):
            lanes = slice(start, stop)
            mask = lane_mask(low, high, stop - start, jnp.bfloat16)
            key_high = parts[2, span, lanes]
            query_high = parts[0, span, lanes] * mask
            scores = dot_nt(query_high, key_high)
            scores += dot_nt(parts[1, span, lanes] * mask, key_high)
            scores += dot_nt(query_high, parts[3, span, lanes]) + offset
            expons = jnp.exp(scores - jnp.max(scores, axis=-1, keepdims=True))
            probs = expons * (1.0 / jnp.sum(expons, axis=-1, keepdims=True))
            out = dot_nn(narrow(probs), parts[4, span, lanes] * mask)
            mixed[span, lanes] += out
    mixed_low[...] = narrow(mixed[...])
    source = mixed_low[...]
    for low, high in column_cuts(width):
        span = slice(low, high)
        proj_out[:, span] = dot_nn(source, whole[3, :, span]) + bias[3:4, span]
    for first in range(0, rows, tile):
        span = slice(first, first + tile)
        resid = wide(tokens[span]) + valid_rows(count, tile, frames) * gate_one * proj_out[span]
        resid_out[span] = resid
        normed, _ = norm_parts(resid)
        mlp_in[span] = narrow(normed * (1.0 + scale_two) + shift_two)


def run_attention(frames, counts, tokens, cotangent, mods, bias, blocks):
    total, width = tokens.shape
    clips = mods.shape[0]
    rows = total // clips
    clip_rows = spec((rows, width), lambda clip: (clip, 0))
    low = jax.ShapeDtypeStruct((total, width), jnp.bfloat16)
    full = jax.ShapeDtypeStruct((total, width), jnp.float32)
    return pl.pallas_call(
        functools.partial(attention_kernel, frames),
        grid=(clips,),
        in_specs=[
            pl.BlockSpec(memory_space=pltpu.SMEM),
            clip_rows,
            clip_rows,
            spec((1,) + mods.shape[1:], lambda clip: (clip, 0, 0)),
            held(bias.shape),
            pl.BlockSpec(memory_space=pl.ANY),
        ],
        out_specs=[
            clip_rows,
            spec((5, rows, width), lambda clip: (0, clip, 0)),
            clip_rows,
            clip_rows,
            clip_rows,
            clip_rows,
            clip_rows,
            spec((1, 1, width), lambda clip: (clip, 0, 0)),
        ],
        out_shape=[
            low,
            jax.ShapeDtypeStruct((5, total, width), jnp.bfloat16),
            low,
            full,
            full,
            low,
            low,
            jax.ShapeDtypeStruct((clips, 1, width), jnp.float32),
        ],
        scratch_shapes=[
            pltpu.VMEM((rows, width), jnp.float32),
            pltpu.VMEM(blocks.shape, jnp.bfloat16),
            pltpu.SemaphoreType.DMA((4,)),
        ],
        compiler_params=pltpu.CompilerParams(vmem_limit_bytes=vmem_bytes),
        cost_estimate=little_cost,
    )(counts, tokens, cotangent, mods, bias, blocks)


def stacked(numbers):
    return jnp.stack([jnp.asarray(number, jnp.int32) for number in numbers])


def start_loads(cuts, at, parts, whole, semaphores):
    for index, (part, first, rows) in enumerate(cuts):
        span = pl.ds(pl.multiple_of(at[index] * 16, 16), rows)
        source = parts[part].at[pl.ds(first, rows)]
        pltpu.make_async_copy(source, whole.at[span], semaphores.at[index]).start()


def wait_loads(groups, at, parts, whole, semaphores):
    index = 0
    for step, cuts in enumerate(groups):
        base = index
        index += len(cuts)

        @pl.when(pl.program_id(0) == step)
        def _(cuts=cuts, base=base):
            for offset, (part, first, rows) in enumerate(cuts):
                span = pl.ds(pl.multiple_of(at[base + offset] * 16, 16), rows)
                source = parts[part].at[pl.ds(first, rows)]
                semaphore = semaphores.at[base + offset]
                pltpu.make_async_copy(source, whole.at[span], semaphore).wait()


def hidden_kernel(cuts, order, starts, mlp_in, bias, *refs):
    whole_out, hidden, slope, whole, semaphores, store_semaphores = refs[-6:]
    pieces = refs[:-6]
    step, steps = pl.program_id(0), pl.num_programs(0)
    width = mlp_in.shape[-1]
    span = pl.ds(pl.multiple_of(order[step] * width, width), width)

    @pl.when(step == 0)
    def _():
        start_loads([cut for group in cuts for cut in group], starts, pieces, whole, semaphores)

    wait_loads(cuts, starts, pieces, whole, semaphores)
    pltpu.make_async_copy(whole.at[span], whole_out.at[span], store_semaphores.at[step]).start()
    root = (2.0 / math.pi) ** 0.5
    source = mlp_in[...]
    block = whole.at[span]
    for low, high in column_cuts(width):
        lanes = slice(low, high)
        pre = dot_nn(source, block[:, lanes]) + bias[0, :, lanes]
        square = pre * pre
        bent = jnp.tanh(root * pre * (1.0 + 0.044715 * square))
        half = 0.5 + 0.5 * bent
        hidden[0, :, lanes] = narrow(pre * half)
        steep = (0.5 * root) * pre * (1.0 + 3 * 0.044715 * square)
        slope[0, :, lanes] = narrow(half + steep * (1.0 - bent * bent))

    @pl.when(step == steps - 1)
    def _():
        for at in range(len(cuts)):
            rows = pl.ds(pl.multiple_of(order[at] * width, width), width)
            pltpu.make_async_copy(
                whole.at[rows], whole_out.at[rows], store_semaphores.at[at]
            ).wait()


def run_hidden(mlp_in, gathered, bias):
    pieces, cuts, starts, order = gathered
    total, width = mlp_in.shape
    count = len(cuts)
    per_block = pl.BlockSpec((1, total, width), lambda at, order, starts: (order[at], 0, 0))
    out = jax.ShapeDtypeStruct((count, total, width), jnp.bfloat16)
    return pl.pallas_call(
        functools.partial(hidden_kernel, cuts),
        grid_spec=pltpu.PrefetchScalarGridSpec(
            num_scalar_prefetch=2,
            grid=(count,),
            in_specs=[
                pl.BlockSpec((total, width), lambda at, order, starts: (0, 0)),
                pl.BlockSpec((1, 1, width), lambda at, order, starts: (order[at], 0, 0)),
            ]
            + [pl.BlockSpec(memory_space=pl.ANY)] * len(pieces),
            out_specs=[pl.BlockSpec(memory_space=pl.ANY), per_block, per_block],
            scratch_shapes=[
                pltpu.VMEM((count * width, width), jnp.bfloat16),
                pltpu.SemaphoreType.DMA((len(starts),)),
                pltpu.SemaphoreType.DMA((count,)),
            ],
        ),
        out_shape=[jax.ShapeDtypeStruct((count * width, width), jnp.bfloat16), out, out],
        compiler_params=pltpu.CompilerParams(vmem_limit_bytes=vmem_bytes),
        cost_estimate=little_cost,
    )(stacked(order), stacked(starts), mlp_in, bias, *pieces)


def branch_kernel(
    frames,
    cuts,
    order,
    starts,
    counts,
    hidden,
    slope,
    d_branch,
    bias,
    gates,
    resid,
    cotangent,
    *refs,
):
    d_pre, d_pre_sum, block_out, d_gate, branch, whole, semaphores = refs[-7:]
    pieces = refs[:-7]
    step, steps = pl.program_id(0), pl.num_programs(0)
    total, width = resid.shape
    clips = gates.shape[0]
    rows = total // clips
    source, back = hidden[0], d_branch[...]

    @pl.when(step == 0)
    def _():
        start_loads([cut for group in cuts for cut in group], starts, pieces, whole, semaphores)
        branch[...] = jnp.zeros_like(branch)

    wait_loads(cuts, starts, pieces, whole, semaphores)
    block = whole.at[pl.ds(pl.multiple_of(order[step] * width, width), width)]
    for low, high in column_cuts(width):
        span = slice(low, high)
        d_hidden = dot_nt(back, block[span, :])
        low_back = narrow(d_hidden * wide(slope[0, :, span]))
        d_pre[0, :, span] = low_back
        d_pre_sum[0, :, span] = column_sum(wide(low_back))
        branch[:, span] += dot_nn(source, block[:, span])

    @pl.when(step == steps - 1)
    def _():
        for clip in range(clips):
            span = slice(clip * rows, (clip + 1) * rows)
            kept = valid_rows(counts[clip], rows, frames) * (branch[span] + bias[...])
            block_out[span] = narrow(resid[span] + gates[clip] * kept)
            d_gate[clip] = column_sum(wide(cotangent[span]) * kept)


def run_branch(frames, counts, hidden, slope, gathered, d_branch, bias, gates, resid, cotangent):
    pieces, cuts, starts, order = gathered
    count, total, width = hidden.shape
    clips = gates.shape[0]

    def all_of(*shape):
        return pl.BlockSpec(shape, lambda at, order, starts: (0,) * len(shape))

    per_block = pl.BlockSpec((1, total, width), lambda at, order, starts: (order[at], 0, 0))
    low = jax.ShapeDtypeStruct((total, width), jnp.bfloat16)
    return pl.pallas_call(
        functools.partial(branch_kernel, frames, cuts),
        grid_spec=pltpu.PrefetchScalarGridSpec(
            num_scalar_prefetch=2,
            grid=(count,),
            in_specs=[
                pl.BlockSpec(memory_space=pltpu.SMEM),
                per_block,
                per_block,
                all_of(total, width),
                all_of(*bias.shape),
                all_of(*gates.shape),
                all_of(total, width),
                all_of(total, width),
            ]
            + [pl.BlockSpec(memory_space=pl.ANY)] * len(pieces),
            out_specs=[
                per_block,
                pl.BlockSpec((1, 1, width), lambda at, order, starts: (order[at], 0, 0)),
                all_of(total, width),
                all_of(clips, 1, width),
            ],
            scratch_shapes=[
                pltpu.VMEM((total, width), jnp.float32),
                pltpu.VMEM((count * width, width), jnp.bfloat16),
                pltpu.SemaphoreType.DMA((len(starts),)),
            ],
        ),
        out_shape=[
            jax.ShapeDtypeStruct((count, total, width), jnp.bfloat16),
            jax.ShapeDtypeStruct((count, 1, width), jnp.float32),
            low,
            jax.ShapeDtypeStruct((clips, 1, width), jnp.float32),
        ],
        compiler_params=pltpu.CompilerParams(vmem_limit_bytes=vmem_bytes),
        cost_estimate=little_cost,
    )(stacked(order), stacked(starts), counts, hidden, slope, d_branch, bias, gates, resid, cotangent, *pieces)


def resid_kernel(
    frames,
    counts,
    d_pre,
    block,
    mods,
    resid,
    cotangent,
    proj,
    d_resid_out,
    d_proj,
    sums,
    total_grad,
):
    step, steps = pl.program_id(0), pl.num_programs(0)
    total, width = resid.shape
    clips = mods.shape[0]
    rows = total // clips
    tile = min(rows, 128)
    source = d_pre[0]

    @pl.when(step == 0)
    def _():
        total_grad[...] = jnp.zeros_like(total_grad)

    for low, high in column_cuts(width):
        span = slice(low, high)
        total_grad[:, span] += dot_nt(source, block[0, span, :])

    @pl.when(step == steps - 1)
    def _():
        for clip in range(clips):
            gate_one, scale_two = mods[clip, 2:3, :], mods[clip, 4:5, :]
            found = [0.0] * 4
            for first in range(clip * rows, (clip + 1) * rows, tile):
                span = slice(first, first + tile)
                grad = total_grad[span]
                normed, inverse = norm_parts(resid[span])
                back = norm_back(grad * (1.0 + scale_two), normed, inverse)
                d_resid = wide(cotangent[span]) + back
                d_resid_out[span] = d_resid
                kept = valid_rows(counts[clip], tile, frames) * d_resid
                low_back = narrow(kept * gate_one)
                d_proj[span] = low_back
                terms = (grad, grad * normed, kept * proj[span], wide(low_back))
                found = [old + column_sum(term) for old, term in zip(found, terms)]
            for at in range(4):
                sums[clip, at : at + 1, :] = found[at]


def run_resid(frames, counts, d_pre, blocks, mods, resid, cotangent, proj):
    count, total, width = d_pre.shape
    clips = mods.shape[0]
    return pl.pallas_call(
        functools.partial(resid_kernel, frames),
        grid=(count,),
        in_specs=[
            pl.BlockSpec(memory_space=pltpu.SMEM),
            spec((1, total, width), lambda at: (at, 0, 0)),
            spec((1, width, width), lambda at: (at, 0, 0)),
            held(mods.shape),
            held((total, width)),
            held((total, width)),
            held((total, width)),
        ],
        out_specs=[held((total, width)), held((total, width)), held((clips, 4, width))],
        out_shape=[
            jax.ShapeDtypeStruct((total, width), jnp.float32),
            jax.ShapeDtypeStruct((total, width), jnp.bfloat16),
            jax.ShapeDtypeStruct((clips, 4, width), jnp.float32),
        ],
        scratch_shapes=[pltpu.VMEM((total, width), jnp.float32)],
        compiler_params=pltpu.CompilerParams(vmem_limit_bytes=vmem_bytes),
        cost_estimate=little_cost,
    )(counts, d_pre, blocks, mods, resid, cotangent, proj)


def attention_back_kernel(
    frames, counts, d_proj, parts, block, d_qkv, sums, d_mixed, d_query, d_key, d_value
):
    rows, width = d_proj.shape
    tile = min(rows, 128)
    count = counts[pl.program_id(0)]
    source = d_proj[...]
    for low, high in column_cuts(width):
        d_mixed[:, low:high] = narrow(dot_nt(source, block[0, low:high, :]))
    scale = (width // HEADS) ** -0.5
    offset = score_offset(count, tile, frames, 0)
    for ref in (d_query, d_key, d_value):
        ref[...] = jnp.zeros_like(ref)
    for first in range(0, rows, tile):
        span = slice(first, first + tile)
        for low, high, start, stop in head_windows(width):
            lanes = slice(start, stop)
            mask = lane_mask(low, high, stop - start, jnp.bfloat16)
            query_high = parts[0, span, lanes] * mask
            key_high = parts[2, span, lanes] * mask
            back = d_mixed[span, lanes] * mask
            scores = dot_nt(key_high, query_high)
            scores += dot_nt(key_high, parts[1, span, lanes])
            scores += dot_nt(parts[3, span, lanes], query_high) + offset
            expons = jnp.exp(scores - jnp.max(scores, axis=0, keepdims=True))
            probs = expons * (1.0 / jnp.sum(expons, axis=0, keepdims=True))
            d_probs = dot_nt(parts[4, span, lanes], back)
            inner = jnp.sum(d_probs * probs, axis=0, keepdims=True)
            d_scores = narrow(probs * (d_probs - inner))
            d_value[span, lanes] += dot_nn(narrow(probs), back)
            d_key[span, lanes] += dot_nn(d_scores, query_high)
            d_query[span, lanes] += dot_tn(d_scores, key_high)
    for at, ref in enumerate((d_query, d_key, d_value)):
        low_back = narrow(ref[...] * scale) if at == 0 else narrow(ref[...])
        d_qkv[at] = low_back
        sums[0, at : at + 1, :] = column_sum(wide(low_back))
    d_qkv[3] = source


def run_attention_back(frames, counts, d_proj, parts, block):
    total, width = d_proj.shape
    clips = counts.shape[0]
    rows = total // clips
    return pl.pallas_call(
        functools.partial(attention_back_kernel, frames),
        grid=(clips,),
        in_specs=[
            pl.BlockSpec(memory_space=pltpu.SMEM),
            spec((rows, width), lambda clip: (clip, 0)),
            spec((5, rows, width), lambda clip: (0, clip, 0)),
            spec((1, width, width), lambda clip: (3, 0, 0), pipeline_mode=pl.Buffered(1)),
        ],
        out_specs=[
            spec((4, rows, width), lambda clip: (0, clip, 0)),
            spec((1, 3, width), lambda clip: (clip, 0, 0)),
        ],
        out_shape=[
            jax.ShapeDtypeStruct((4, total, width), jnp.bfloat16),
            jax.ShapeDtypeStruct((clips, 3, width), jnp.float32),
        ],
        scratch_shapes=[pltpu.VMEM((rows, width), jnp.bfloat16)]
        + [pltpu.VMEM((rows, width), jnp.float32)] * 3,
        compiler_params=pltpu.CompilerParams(vmem_limit_bytes=vmem_bytes),
        cost_estimate=little_cost,
    )(counts, d_proj, parts, block)


def input_kernel(d_qkv, block, mods, tokens, d_resid, input_grad, sums, total_grad):
    step, steps = pl.program_id(0), pl.num_programs(0)
    total, width = tokens.shape
    clips = mods.shape[0]
    rows = total // clips
    tile = min(rows, 128)
    source = d_qkv[0]

    @pl.when(step == 0)
    def _():
        total_grad[...] = jnp.zeros_like(total_grad)

    for low, high in column_cuts(width):
        span = slice(low, high)
        total_grad[:, span] += dot_nt(source, block[0, span, :])

    @pl.when(step == steps - 1)
    def _():
        for clip in range(clips):
            scale_one = mods[clip, 1:2, :]
            found = [0.0] * 2
            for first in range(clip * rows, (clip + 1) * rows, tile):
                span = slice(first, first + tile)
                grad = total_grad[span]
                normed, inverse = norm_parts(wide(tokens[span]))
                back = norm_back(grad * (1.0 + scale_one), normed, inverse)
                input_grad[span] = narrow(d_resid[span] + back)
                terms = (grad, grad * normed)
                found = [old + column_sum(term) for old, term in zip(found, terms)]
            for at in range(2):
                sums[clip, at : at + 1, :] = found[at]


def run_input(d_qkv, blocks, mods, tokens, d_resid):
    total, width = tokens.shape
    clips = mods.shape[0]
    return pl.pallas_call(
        input_kernel,
        grid=(3,),
        in_specs=[
            spec((1, total, width), lambda at: (at, 0, 0)),
            spec((1, width, width), lambda at: (at, 0, 0)),
            held(mods.shape),
            held((total, width)),
            held((total, width)),
        ],
        out_specs=[held((total, width)), held((clips, 2, width))],
        out_shape=[
            jax.ShapeDtypeStruct((total, width), jnp.bfloat16),
            jax.ShapeDtypeStruct((clips, 2, width), jnp.float32),
        ],
        scratch_shapes=[pltpu.VMEM((total, width), jnp.float32)],
        compiler_params=pltpu.CompilerParams(vmem_limit_bytes=vmem_bytes),
        cost_estimate=little_cost,
    )(d_qkv, blocks, mods, tokens, d_resid)


def halves_kernel(left_of, adds, steps, order, side, *refs):
    lefts = refs[: max(left_of) + 1]
    right = refs[len(lefts)]
    turned, total_low = refs[-2:]
    if adds:
        incoming, first_keep, first_out, second_keep, second_out = refs[len(lefts) + 1 : -2]
    else:
        out = refs[-3]
    step = pl.program_id(0)
    block = order[step]
    width = lefts[0].shape[-1]
    half = width // 2

    def pick(left, at):
        lanes = slice(at * half, (at + 1) * half)
        turned[...] = (left[:, lanes] if left.ndim == 2 else left[0, :, lanes]).T

    fresh = (step == 0) | (lefts[0].ndim == 3) | (len(lefts) > 1)
    for at in range(2):
        for index, left in enumerate(lefts):
            of_left = [block == number for number, source in enumerate(left_of) if source == index]

            @pl.when(fresh & (side[0] == at) & functools.reduce(jnp.logical_or, of_left))
            def _(left=left, at=at):
                pick(left, at)

    found = dot_nn(turned[...], right[0] if right.ndim == 3 else right[...])
    if not adds:
        out[0] = narrow(found)
        return
    total_low[...] = narrow(found + wide(incoming[0]))
    for state, target, rows in (
        (steps[0][0], first_keep, slice(0, half // 2)),
        (steps[0][1], first_out, slice(0, half // 2)),
        (steps[1][0], second_keep, slice(half // 2, half)),
        (steps[1][1], second_out, slice(half // 2, half)),
    ):

        @pl.when(functools.reduce(jnp.logical_or, [step == at_step for at_step in state]))
        def _(target=target, rows=rows):
            target[0] = total_low[rows]


def run_halves(lefts, left_of, right, side, at, incoming=None):
    total, width = lefts[0].shape[-2:]
    half = width // 2
    low_bit, high_bit = at % 2, at // 2
    order = stacked([at ^ 3, at ^ 1, at, at ^ 2])
    places = {
        "first_keep": [high_bit, high_bit, high_bit, 1 - high_bit],
        "first_out": [1 - high_bit, high_bit, high_bit, high_bit],
        "second_keep": [1 - low_bit, 1 - low_bit, low_bit, low_bit],
        "second_out": [1 - low_bit, low_bit, low_bit, low_bit],
    }
    steps = (((2, 3), (0, 1)), ((1, 2), (0, 3)))
    adds = incoming is not None
    table = stacked([place for row in places.values() for place in row])

    def block_of(array, *rest):
        if array.ndim == 2:
            return pl.BlockSpec(array.shape, lambda step, order, side, table: (0, 0))
        return pl.BlockSpec((1,) + array.shape[1:], lambda step, order, side, table: (order[step], 0, 0))

    per_block = pl.BlockSpec((1, half, width), lambda step, order, side, table: (order[step], 0, 0))
    operands = list(lefts) + [right]
    in_specs = [block_of(array) for array in operands]
    if adds:
        operands.append(incoming)
        in_specs.append(per_block)
        out_specs = [
            pl.BlockSpec(
                (1, half // 2, width),
                functools.partial(lambda row, step, order, side, table: (table[row * 4 + step], 0, 0), row),
            )
            for row in range(4)
        ]
        out_shape = [jax.ShapeDtypeStruct((2, half // 2, width), jnp.bfloat16)] * 4
    else:
        out_specs = per_block
        out_shape = jax.ShapeDtypeStruct((4, half, width), jnp.bfloat16)

    def body(order, side, table, *refs):
        halves_kernel(left_of, adds, steps, order, side, *refs)

    return pl.pallas_call(
        body,
        grid_spec=pltpu.PrefetchScalarGridSpec(
            num_scalar_prefetch=3,
            grid=(4,),
            in_specs=in_specs,
            out_specs=out_specs,
            scratch_shapes=[
                pltpu.VMEM((half, total), jnp.bfloat16),
                pltpu.VMEM((half, width), jnp.bfloat16),
            ],
        ),
        out_shape=out_shape,
        compiler_params=pltpu.CompilerParams(vmem_limit_bytes=vmem_bytes),
        cost_estimate=little_cost,
    )(order, stacked([side]), table, *operands)


def tie(*values):
    return lax.optimization_barrier(values)


def packed(arrays, tile):
    flat = jnp.concatenate([array.reshape(-1) for array in arrays])
    return jnp.pad(flat, (0, -flat.shape[0] % (tile * 128))).reshape(-1, 128)


def core_swap(array):
    count = lax.axis_size("dp")
    return lax.ppermute(array, "dp", [(at, at ^ 1) for at in range(count)])


def chip_shift(array, step):
    count = lax.axis_size("dp")
    return lax.ppermute(array, "dp", [(at, (at + 2 * step) % count) for at in range(count)])


def chip_swap(array, bits):
    count = lax.axis_size("dp")
    return lax.ppermute(array, "dp", [(at, at ^ (2 * bits)) for at in range(count)])


def rank_swap(array, bits):
    count = lax.axis_size("fsdp")
    return lax.ppermute(array, "fsdp", [(at, at ^ bits) for at in range(count)])


def entry(array, at, axis=0):
    return lax.dynamic_index_in_dim(array, at, axis, keepdims=False)


def place_kernel(cuts, at, *refs):
    parts, whole, held_rows, semaphores = refs[:-3], refs[-3], refs[-2], refs[-1]
    spans, loads, stores = [], [], []
    for index, (part, first, rows) in enumerate(cuts):
        spans.append(pl.ds(pl.multiple_of(at[index] * 16, 16), rows))
        source = parts[part].at[pl.ds(first, rows)]
        loads.append(
            pltpu.make_async_copy(source, held_rows.at[spans[index]], semaphores.at[0, index])
        )
        loads[index].start()
    for index, span in enumerate(spans):
        loads[index].wait()
        stores.append(
            pltpu.make_async_copy(held_rows.at[span], whole.at[span], semaphores.at[1, index])
        )
        stores[index].start()
    for store in stores:
        store.wait()


def place(parts, cuts, starts, rows):
    width = parts[0].shape[-1]
    dtype = parts[0].dtype
    return pl.pallas_call(
        functools.partial(place_kernel, cuts),
        in_specs=[pl.BlockSpec(memory_space=pltpu.SMEM)]
        + [pl.BlockSpec(memory_space=pl.ANY)] * len(parts),
        out_specs=pl.BlockSpec(memory_space=pl.ANY),
        out_shape=jax.ShapeDtypeStruct((rows, width), dtype),
        scratch_shapes=[
            pltpu.VMEM((rows, width), dtype),
            pltpu.SemaphoreType.DMA((2, len(cuts))),
        ],
        compiler_params=pltpu.CompilerParams(vmem_limit_bytes=vmem_bytes),
        cost_estimate=little_cost,
    )(stacked(starts), *parts)


def own_rows(parts, group):
    ranks, at = lax.axis_size("fsdp"), lax.axis_index("fsdp")
    shares = ranks // group
    count, _, row_part, col_part = parts.shape
    chunk = row_part // shares
    split = parts.reshape(count, group, shares, chunk, col_part).transpose(1, 2, 0, 3, 4)
    split = split.reshape(ranks, count, chunk, col_part)
    if shares > 1:
        moved = lax.all_to_all(split, "fsdp", 0, 0, tiled=True)
        (moved,) = yield (moved,)
        yield moved.transpose(1, 2, 0, 3).reshape(count, chunk, ranks * col_part)
        return
    panels = [entry(split, at)]
    panels += [rank_swap(entry(split, at ^ bits), bits) for bits in range(1, ranks)]
    panels = yield tuple(panels)
    placed = [
        lax.select_n(at, *[panels[panel ^ index] for index in range(ranks)])
        for panel in range(ranks)
    ]
    yield jnp.concatenate(placed, axis=2)


def shard_rows(split, group):
    ranks, count, chunk, col_part = split.shape
    shares = ranks // group
    moved = lax.all_to_all(split, "fsdp", 0, 0, tiled=True)
    moved = moved.reshape(group, shares, count, chunk, col_part).transpose(2, 0, 1, 3, 4)
    return moved.reshape(count, group, shares * chunk, col_part)


def gather_blocks(rows, group):
    ranks, dp_count = lax.axis_size("fsdp"), lax.axis_size("dp")
    shares = ranks // group
    chunk, total = rows.shape
    all_rows = lax.all_gather(rows, ("fsdp", "dp"), axis=0, tiled=True)
    if shares > 1:
        all_rows = all_rows.reshape(group, shares, dp_count, chunk, total).transpose(0, 2, 1, 3, 4)
    return all_rows.reshape(group, total, total)


def join_line(found):
    chips, chip = lax.axis_size("dp") // 2, lax.axis_index("dp") // 2
    chunk = found[0].shape[0]
    starts = [(chip - step) % chips * (chunk // 16) for step in range(chips)]
    return place(found, [(step, 0, chunk) for step in range(chips)], starts, chips * chunk)


def gather_second(rows, group):
    ranks, at = lax.axis_size("fsdp"), lax.axis_index("fsdp")
    total = rows.shape[-1]
    if ranks != group:
        blocks = gather_blocks(rows, group).reshape(group * total, total)
        for _ in range(3):
            (blocks,) = yield (blocks,)
        cuts = [[(0, index * total, total)] for index in range(group)]
        yield [blocks], cuts, [index * (total // 16) for index in range(group)], range(group)
        return
    chips = lax.axis_size("dp") // 2
    core = lax.axis_index("dp") % 2
    chunk, half = rows.shape[0], total // 2
    others = yield tuple(chip_shift(rows, step) for step in range(1, chips))
    line = join_line([rows, *others])
    cuts = [(side, step * chunk, chunk) for side in range(2) for step in range(chips)]
    starts = [
        (2 * step + side) * (chunk // 16) for side in (core, 1 - core) for step in range(chips)
    ]
    (own,) = yield (place([line, core_swap(line)], cuts, starts, total),)
    share = lax.dynamic_slice_in_dim(own, core * half, half, 0)
    mine = yield tuple(rank_swap(share, bits) for bits in range(1, ranks))
    parts, cuts, starts = [own], [[(0, 0, total)]], [at * (total // 16)]
    for bits in range(1, ranks):
        parts += [mine[bits - 1], core_swap(mine[bits - 1])]
        cuts.append([(2 * bits - 1, 0, half), (2 * bits, 0, half)])
        starts += [((at ^ bits) * 2 + side) * (half // 16) for side in (core, 1 - core)]
    yield parts, cuts, starts, [at ^ bits for bits in range(ranks)]


def gather_own(rows, group):
    ranks = lax.axis_size("fsdp")
    shares = ranks // group
    if shares > 1:
        sets = [[share + shares * block for share in range(shares)] for block in range(group)]
        rows = lax.all_gather(rows, "fsdp", axis=1, tiled=True, axis_index_groups=sets)
    return lax.all_gather(rows, "dp", axis=1, tiled=True)


def sum_blocks(lefts, left_of, right, group):
    ranks, dp_count = lax.axis_size("fsdp"), lax.axis_size("dp")
    shares = ranks // group
    total = lefts[0].shape[-1]
    if shares > 1:
        blocks = jnp.stack(
            [
                narrow(
                    fast_dot(
                        "tr,te->re",
                        lefts[index] if lefts[index].ndim == 2 else lefts[index][block],
                        right if right.ndim == 2 else right[block],
                    )
                )
                for block, index in enumerate(left_of)
            ]
        )
        chunk = total // (dp_count * shares)
        blocks = blocks.reshape(group, dp_count, shares, chunk, -1).transpose(0, 2, 1, 3, 4)
        rows = lax.psum_scatter(
            blocks.reshape(group * total, -1), ("fsdp", "dp"), scatter_dimension=0, tiled=True
        )
        for _ in range(7):
            (rows,) = yield (rows,)
        yield gather_own(rows[None], group)[0]
        return
    chips, half = dp_count // 2, total // 2
    chunk = half // chips
    at = lax.axis_index("fsdp")
    core, chip = lax.axis_index("dp") % 2, lax.axis_index("dp") // 2
    low_bit, high_bit = at % 2, at // 2
    (away,) = yield (run_halves(lefts, left_of, right, 1 - core, at),)
    (away_in,) = yield (core_swap(away),)
    first, first_out, second, second_out = run_halves(lefts, left_of, right, core, at, away_in)
    first_out, second_out = yield (first_out, second_out)
    first_in, second_in = yield (rank_swap(first_out, 1), rank_swap(second_out, 2))
    first = narrow(wide(first) + wide(first_in)).reshape(2, chips // 2, chunk, -1)
    second = narrow(wide(second) + wide(second_in)).reshape(2, chips // 2, chunk, -1)
    first_in = rank_swap(entry(first, 1 - high_bit), 2)
    second_in = rank_swap(entry(second, 1 - low_bit), 1)
    first_in, second_in = yield (first_in, second_in)
    first = narrow(wide(entry(first, high_bit)) + wide(first_in))
    second = narrow(wide(entry(second, low_bit)) + wide(second_in))
    line = jnp.concatenate([first, second])
    step = 1
    while step < chips:
        bit = chip // step % 2
        line = line.reshape(-1, 2, *line.shape[1:])
        (line_in,) = yield (chip_swap(entry(line, 1 - bit, 1), step),)
        line = narrow(wide(entry(line, bit, 1)) + wide(line_in))
        step *= 2
    yield lax.all_gather(line[0], "dp", axis=0, tiled=True)


def fast_dot(subscripts, left, right):
    return jnp.einsum(subscripts, left, right, preferred_element_type=jnp.float32)


def products_kernel(chips, at, gathered, left_root, right_root, out, whole, semaphores):
    chunk, width = left_root.shape[1:]
    ranks = out.shape[0]
    copies = []
    for index in range(2 * chips):
        first = (index % 2 * chips + index // 2) * chunk
        copies.append(
            pltpu.make_async_copy(
                gathered.at[pl.ds(index * chunk, chunk)],
                whole.at[pl.ds(first, chunk)],
                semaphores.at[index],
            )
        )
        copies[-1].start()
    for copy in copies:
        copy.wait()
    first = at[0] * 16
    grad = whole[...]
    picked = lax.broadcasted_iota(jnp.int32, (width, chunk), 0) - first
    picked = picked == lax.broadcasted_iota(jnp.int32, (width, chunk), 1)
    own_columns = narrow(dot_nn(grad, narrow(picked.astype(jnp.float32))))
    side_high, side_low = split_high(dot_nn(left_root[0], grad))
    right = right_root[0]
    precond = dot_nn(side_high, right) + dot_nn(side_low, right)
    outer = dot_nt(whole[pl.ds(pl.multiple_of(first, 16), chunk), :], grad)
    inner = dot_tn(own_columns, grad)
    for at_out, product in enumerate((precond, outer, inner)):
        low = narrow(product)
        for rank in range(ranks):
            span = slice(rank * (width // ranks), (rank + 1) * (width // ranks))
            out[rank, at_out] = low[:, span]


def owned_step(whole, left_roots, right_roots, index, group):
    ranks, dp_count = lax.axis_size("fsdp"), lax.axis_size("dp")
    shares = ranks // group
    chunk, total = left_roots.shape[1:]
    col_part = total // ranks
    first = lax.axis_index("dp") * (chunk * shares) + lax.axis_index("fsdp") % shares * chunk
    if shares == 1:
        return pl.pallas_call(
            functools.partial(products_kernel, dp_count // 2),
            in_specs=[
                pl.BlockSpec(memory_space=pltpu.SMEM),
                pl.BlockSpec(memory_space=pl.ANY),
                pl.BlockSpec((1, chunk, total), lambda step: (index, 0, 0)),
                pl.BlockSpec((1, total, total), lambda step: (index, 0, 0)),
            ],
            out_specs=pl.BlockSpec((ranks, 3, chunk, col_part), lambda step: (0, 0, 0, 0)),
            grid=(1,),
            out_shape=jax.ShapeDtypeStruct((ranks, 3, chunk, col_part), jnp.bfloat16),
            scratch_shapes=[
                pltpu.VMEM((total, total), jnp.bfloat16),
                pltpu.SemaphoreType.DMA((dp_count,)),
            ],
            compiler_params=pltpu.CompilerParams(vmem_limit_bytes=vmem_bytes),
            cost_estimate=little_cost,
        )((first // 16)[None], whole, left_roots, right_roots)
    left_root, right_root = left_roots[index], right_roots[index]
    grad_rows = lax.dynamic_slice_in_dim(whole, first, chunk, 0)
    own_columns = lax.dynamic_slice_in_dim(whole, first, chunk, 1)
    outer = fast_dot("rk,jk->rj", grad_rows, whole)
    inner = fast_dot("kr,kj->rj", own_columns, whole)
    side_high, side_low = split_high(fast_dot("rk,kj->rj", left_root, whole))
    precond = fast_dot("rk,kj->rj", side_high, right_root) + fast_dot(
        "rk,kj->rj", side_low, right_root
    )
    products = narrow(jnp.stack([precond, outer, inner]))
    return products.reshape(3, chunk, ranks, col_part).transpose(2, 0, 1, 3)


def per_device(
    tokens,
    conditioning,
    frame_counts,
    cotangent,
    weights,
    biases,
    momentum,
    left_stats,
    right_stats,
    left_roots,
    right_roots,
    bias_moment,
    bias_second,
):
    group = 4
    mod_count = 6
    clip_count, pos_count, frames, width = tokens.shape
    token_count = clip_count * pos_count * frames
    block_count, row_part, col_part = weights.shape
    dp_count, ranks = lax.axis_size("dp"), lax.axis_size("fsdp")
    dp_at, rank_at = lax.axis_index("dp"), lax.axis_index("fsdp")
    all_clips = clip_count * dp_count
    bias_part = biases.shape[0]
    stream = tokens.reshape(token_count, width)
    grad_out = cotangent.reshape(token_count, width)
    low_weights = narrow(weights).reshape(block_count, row_part, col_part)
    shards = low_weights[mod_count:].reshape(-1, group, row_part, col_part)

    weight_rows = own_rows(shards, group)
    weight_panels = next(weight_rows)
    cond_low = narrow(jax.nn.silu(conditioning))
    first_parts = lax.all_gather(packed([cond_low, narrow(biases)], 16), "dp", axis=0, tiled=True)
    weight_panels, first_parts = tie(weight_panels, first_parts)
    attn_rows, one_rows, two_rows = weight_rows.send(weight_panels)
    attn_w = gather_blocks(attn_rows, group)
    two_w = gather_blocks(two_rows, group).reshape(group * width, width)
    two_gathered = (
        [two_w],
        [[(0, index * width, width)] for index in range(group)],
        [index * (width // 16) for index in range(group)],
        range(group),
    )

    first_parts = first_parts.reshape(dp_count, -1)
    cond_all = first_parts[:, : clip_count * width].reshape(all_clips, width)
    bias_rows = wide(first_parts[:, clip_count * width : clip_count * width + bias_part])
    cond_rows = lax.dynamic_slice_in_dim(cond_all, dp_at * row_part, row_part, 1)
    cond_cols = wide(lax.dynamic_slice_in_dim(cond_all, rank_at * col_part, col_part, 1))
    mod_parts = fast_dot("cr,jre->cje", cond_rows, low_weights[:mod_count])
    mod_parts = lax.all_to_all(mod_parts, "dp", 0, 0, tiled=True)
    mod_parts, one_rows = tie(mod_parts, one_rows)
    one_steps = gather_second(one_rows, group)
    one_parts = next(one_steps)
    mod_cols = jnp.sum(mod_parts.reshape(dp_count, clip_count, mod_count, col_part), axis=0)
    left_cond = jnp.einsum("jrk,ck->jrc", left_roots[:mod_count], cond_cols, precision=precise)
    mod_size, bias_size = mod_cols.size, dp_count * bias_part
    second_parts = lax.all_gather(
        packed([mod_cols, bias_rows, left_cond], 8), "fsdp", axis=0, tiled=True
    )
    second_parts, one_parts = tie(second_parts, one_parts)
    one_parts, attn_w = tie(one_steps.send(one_parts), attn_w)
    one_parts = one_steps.send(one_parts)
    second_parts = second_parts.reshape(ranks, -1)
    mods = second_parts[:, :mod_size].reshape(ranks, clip_count, mod_count, col_part)
    mods = mods.transpose(1, 2, 0, 3).reshape(clip_count, mod_count, width)
    bias_all = second_parts[:, mod_size : mod_size + bias_size].reshape(ranks, dp_count, bias_part)
    bias_all = bias_all.transpose(1, 0, 2).reshape(-1, width)
    left_size = mod_size + bias_size + left_cond.size
    left_cond = jnp.sum(second_parts[:, mod_size + bias_size : left_size], axis=0)
    left_cond = left_cond.reshape(mod_count, row_part, all_clips)
    mods = mods + bias_all[:mod_count]
    bias_table = jnp.concatenate(
        [bias_all[6:7], jnp.zeros((1, width), jnp.float32), bias_all[7:14]]
    )

    attn_in, parts, mixed, proj, resid, mlp_in, d_branch, d_branch_sums = run_attention(
        frames, frame_counts, stream, grad_out, mods, bias_table, attn_w
    )
    mlp_in, one_parts = tie(mlp_in, one_parts)
    one_w, hidden, slope = run_hidden(mlp_in, one_steps.send(one_parts), bias_table[4:8, None])
    one_w = one_w.reshape(group, width, width)

    two_steps = sum_blocks([hidden], [0] * group, d_branch, group)
    two_parts = next(two_steps)
    roots = jnp.stack([narrow(left_roots[mod_count:]), narrow(right_roots[mod_count:])])
    hidden, two_parts, roots = tie(hidden, two_parts, roots)
    two_parts = two_steps.send(two_parts)
    root_rows = own_rows(roots.reshape(-1, group, row_part, col_part), group)
    root_panels = next(root_rows)
    d_pre, d_pre_sums, block_out, d_gate_two = run_branch(
        frames,
        frame_counts,
        hidden,
        slope,
        two_gathered,
        d_branch,
        bias_table[8:9],
        mods[:, 5:6],
        resid,
        grad_out,
    )
    d_pre, root_panels = tie(d_pre, root_panels)
    root_rows = root_rows.send(root_panels)
    d_pre, two_parts, root_rows = tie(d_pre, two_parts, root_rows)
    two_parts = two_steps.send(two_parts)
    d_pre, two_parts = tie(d_pre, two_parts)
    two_parts = two_steps.send(two_parts)
    right_wholes = gather_own(root_rows[3:], group)
    one_steps = sum_blocks([mlp_in], [0] * group, d_pre, group)
    one_parts = next(one_steps)
    d_pre, one_parts = tie(d_pre, one_parts)
    one_parts = one_steps.send(one_parts)
    d_resid, d_proj, resid_sums = run_resid(
        frames, frame_counts, d_pre, one_w, mods, resid, grad_out, proj
    )
    d_proj, one_parts = tie(d_proj, one_parts)
    one_parts = one_steps.send(one_parts)
    d_proj, one_parts, two_parts = tie(d_proj, one_parts, two_parts)
    two_parts = two_steps.send(two_parts)
    one_parts = one_steps.send(one_parts)
    d_heads, head_sums = run_attention_back(frames, frame_counts, d_proj, parts, attn_w)
    d_heads, two_parts, one_parts, right_wholes = tie(
        d_heads, two_parts, one_parts, right_wholes
    )
    two_parts = two_steps.send(two_parts)
    one_parts = one_steps.send(one_parts)
    attn_steps = sum_blocks([attn_in, mixed], [0, 0, 0, 1], d_heads, group)
    attn_parts = next(attn_steps)
    d_heads, attn_parts = tie(d_heads, attn_parts)
    attn_parts = attn_steps.send(attn_parts)
    input_grad, input_sums = run_input(d_heads, attn_w, mods, stream, d_resid)
    input_sums, attn_parts, two_parts, one_parts = tie(
        input_sums, attn_parts, two_parts, one_parts
    )
    two_parts = two_steps.send(two_parts)
    one_parts = one_steps.send(one_parts)

    d_mods = jnp.stack(
        [
            input_sums[:, 0],
            input_sums[:, 1],
            resid_sums[:, 2],
            resid_sums[:, 0],
            resid_sums[:, 1],
            d_gate_two[:, 0],
        ],
        axis=1,
    )
    head_sums = jnp.sum(head_sums, axis=0)
    grad_bias = jnp.concatenate(
        [
            jnp.sum(d_mods, axis=0),
            head_sums[0:1],
            head_sums[2:3],
            jnp.sum(resid_sums[:, 3], axis=0)[None],
            d_pre_sums[:, 0],
            jnp.sum(d_branch_sums, axis=0),
        ]
    )
    to_ranks = jnp.concatenate(
        [
            d_mods.reshape(clip_count, mod_count, ranks, col_part)
            .transpose(2, 0, 1, 3)
            .reshape(ranks, mod_size),
            grad_bias.reshape(dp_count, ranks, bias_part)
            .transpose(1, 0, 2)
            .reshape(ranks, bias_size),
        ],
        axis=1,
    )
    rank_sums = lax.all_to_all(to_ranks, "fsdp", 0, 0, tiled=True)
    rank_sums, attn_parts = tie(rank_sums, attn_parts)
    attn_parts = attn_steps.send(attn_parts)
    rank_sums = jnp.sum(rank_sums, axis=0)
    to_rows = jnp.concatenate(
        [
            jnp.broadcast_to(rank_sums[None, :mod_size], (dp_count, mod_size)),
            rank_sums[mod_size:].reshape(dp_count, bias_part),
        ],
        axis=1,
    )
    to_rows, attn_parts = tie(to_rows, attn_parts)
    attn_parts = attn_steps.send(attn_parts)
    from_rows = lax.all_to_all(to_rows, "dp", 0, 0, tiled=True)
    from_rows, two_parts, one_parts = tie(from_rows, two_parts, one_parts)
    whole_two = two_steps.send(two_parts)
    one_parts = one_steps.send(one_parts)
    from_rows, attn_parts, one_parts = tie(from_rows, attn_parts, one_parts)
    attn_parts = attn_steps.send(attn_parts)
    whole_one = one_steps.send(one_parts)
    bias_grad = jnp.sum(from_rows[:, mod_size:], axis=0)
    mod_grad_cols = from_rows[:, :mod_size].reshape(all_clips, mod_count, col_part)
    mod_grad = lax.all_gather(packed([mod_grad_cols], 8), "fsdp", axis=0, tiled=True)
    mod_grad, attn_parts = tie(mod_grad, attn_parts)
    attn_parts = attn_steps.send(attn_parts)
    products_two = owned_step(whole_two, root_rows, right_wholes, 2, group)
    products_two, attn_parts = tie(products_two, attn_parts)
    attn_parts = attn_steps.send(attn_parts)
    back_two = shard_rows(products_two, group)
    products_one = owned_step(whole_one, root_rows, right_wholes, 1, group)
    mod_grad, back_two, products_one, attn_parts = tie(
        mod_grad, back_two, products_one, attn_parts
    )
    whole_attn = attn_steps.send(attn_parts)
    back_one = shard_rows(products_one, group)
    mod_grad = mod_grad.reshape(ranks, -1)[:, : mod_grad_cols.size]
    mod_grad = mod_grad.reshape(ranks, all_clips, mod_count, col_part).transpose(1, 2, 0, 3)
    mod_grad = mod_grad.reshape(all_clips, mod_count, width)

    mod_grad_rows = lax.dynamic_slice_in_dim(mod_grad, dp_at * row_part, row_part, 2)
    right_parts = jnp.einsum(
        "cjk,jke->cje", mod_grad_rows, right_roots[:mod_count], precision=precise
    )
    cond_wide = wide(cond_all)
    cond_row_wide = wide(cond_rows)
    mod_gram = jnp.einsum("cjk,bjk->jcb", mod_grad, mod_grad, precision=precise)
    cond_gram = jnp.einsum("ck,bk->cb", cond_wide, cond_wide, precision=precise)
    mod_side = jnp.einsum("jcb,be->jce", mod_gram, cond_cols, precision=precise)
    ada_left = jnp.einsum("cr,jce->jre", cond_row_wide, mod_side, precision=precise)
    cond_side = jnp.einsum("cb,bje->jce", cond_gram, mod_grad_cols, precision=precise)
    ada_right = jnp.einsum("cjr,jce->jre", mod_grad_rows, cond_side, precision=precise)

    right_parts = lax.all_gather(packed([right_parts], 8), "dp", axis=0, tiled=True)
    mod_right = jnp.sum(right_parts.reshape(dp_count, -1), axis=0)[: mod_grad_cols.size]
    mod_right = mod_right.reshape(all_clips, mod_count, col_part)
    ada_pre = jnp.einsum("jrc,cje->jre", left_cond, mod_right, precision=precise)
    whole_attn, back_one = tie(whole_attn, back_one)
    back_attn = shard_rows(owned_step(whole_attn, root_rows, right_wholes, 0, group), group)

    def joined(at, ada):
        return jnp.concatenate([ada, wide(back_attn[at]), wide(back_one[at]), wide(back_two[at])])

    precond = joined(0, ada_pre)
    left_new = stat_decay * left_stats + (1.0 - stat_decay) * joined(1, ada_left)
    right_new = stat_decay * right_stats + (1.0 - stat_decay) * joined(2, ada_right)
    momentum_new = moment_decay * momentum + precond
    weights_new = weights - weight_rate * momentum_new
    weights_copy = weights_new.astype(jnp.bfloat16)
    bias_second_new = stat_decay * bias_second + (1.0 - stat_decay) * bias_grad * bias_grad
    bias_moment_new = moment_decay * bias_moment + bias_grad * lax.rsqrt(
        bias_second_new + diag_epsilon
    )
    biases_new = biases - bias_rate * bias_moment_new
    return (
        block_out.reshape(tokens.shape),
        input_grad.reshape(tokens.shape),
        left_new,
        right_new,
        momentum_new,
        weights_new,
        weights_copy,
        bias_moment_new,
        bias_second_new,
        biases_new,
    )


def solution(mesh):
    placed = (
        P("dp", "fsdp", None, None),
        P("dp", None),
        P("dp"),
        P("dp", "fsdp", None, None),
        P(None, "dp", "fsdp"),
        P(("dp", "fsdp")),
        P(None, "dp", "fsdp"),
        P(None, "dp", "fsdp"),
        P(None, "dp", "fsdp"),
        P(None, "dp", "fsdp"),
        P(None, "dp", "fsdp"),
        P(("dp", "fsdp")),
        P(("dp", "fsdp")),
    )
    return jax.shard_map(
        per_device,
        mesh=mesh,
        in_specs=placed,
        out_specs=(
            P("dp", "fsdp", None, None),
            P("dp", "fsdp", None, None),
            P(None, "dp", "fsdp"),
            P(None, "dp", "fsdp"),
            P(None, "dp", "fsdp"),
            P(None, "dp", "fsdp"),
            P(None, "dp", "fsdp"),
            P(("dp", "fsdp")),
            P(("dp", "fsdp")),
            P(("dp", "fsdp")),
        ),
        check_vma=False,
    )
```

```python
import functools
import math

import jax
import jax.numpy as jnp
from jax import lax
from jax.experimental import pallas as pl
from jax.experimental.pallas import tpu as pltpu
from jax.sharding import PartitionSpec as P

HEADS = 16


precise = lax.Precision.HIGHEST
norm_epsilon = 1e-06
masked_score = -1e30
stat_decay = 0.5
moment_decay = 0.9
weight_rate = 0.7
bias_rate = 0.1
diag_epsilon = 1e-08
vmem_bytes = 50 * 2**20
little_cost = pl.CostEstimate(flops=1024, bytes_accessed=1024, transcendentals=0)


def narrow(array):
    return array.astype(jnp.bfloat16)


def wide(array):
    return array.astype(jnp.float32)


def spec(shape, index_map, **keywords):
    return pl.BlockSpec(shape, index_map, **keywords)


def held(shape):
    return pl.BlockSpec(shape, lambda step: (0,) * len(shape), pipeline_mode=pl.Buffered(1))


def column_cuts(total):
    cuts, at = [], 0
    while at < total:
        cuts.append((at, min(total, at + 256)))
        at += 256
    return cuts


def dot_nn(left, right):
    return lax.dot_general(left, right, (((1,), (0,)), ((), ())), preferred_element_type=jnp.float32)


def dot_nt(left, right):
    return lax.dot_general(left, right, (((1,), (1,)), ((), ())), preferred_element_type=jnp.float32)


def dot_tn(left, right):
    return lax.dot_general(left, right, (((0,), (0,)), ((), ())), preferred_element_type=jnp.float32)


def split_high(values):
    high = narrow(values)
    return high, narrow(values - wide(high))


def valid_rows(count, rows, frames):
    at = lax.broadcasted_iota(jnp.int32, (rows, 1), 0)
    return (lax.rem(at, frames) < count).astype(jnp.float32)


def score_offset(count, size, frames, key_axis):
    first = lax.broadcasted_iota(jnp.int32, (size, size), 0)
    second = lax.broadcasted_iota(jnp.int32, (size, size), 1)
    key = second if key_axis == 1 else first
    met = (lax.div(first, frames) == lax.div(second, frames)) & (lax.rem(key, frames) < count)
    return jnp.where(met, 0.0, masked_score)


def head_windows(width):
    size = width // HEADS
    windows = []
    for head in range(HEADS):
        low, high = head * size, (head + 1) * size
        start = low // 128 * 128
        stop = min(width, -(-high // 128) * 128)
        windows.append((low - start, high - start, start, stop))
    return windows


def lane_mask(low, high, count, dtype):
    lanes = lax.broadcasted_iota(jnp.int32, (1, count), 1)
    return ((lanes >= low) & (lanes < high)).astype(jnp.float32).astype(dtype)


def norm_parts(values):
    centered = values - jnp.mean(values, axis=-1, keepdims=True)
    variance = jnp.mean(centered * centered, axis=-1, keepdims=True)
    inverse = lax.rsqrt(variance + norm_epsilon)
    return centered * inverse, inverse


def norm_back(grad, normed, inverse):
    first = jnp.mean(grad, axis=-1, keepdims=True)
    second = jnp.mean(grad * normed, axis=-1, keepdims=True)
    return (grad - first - normed * second) * inverse


def column_sum(values):
    return jnp.sum(values, axis=0, keepdims=True)


def start_loads(cuts, at, parts, whole, semaphores, first_index=0):
    loads = []
    for index, (part, first, rows) in enumerate(cuts, first_index):
        span = pl.ds(pl.multiple_of(at[index] * 16, 16), rows)
        source = parts[part].at[pl.ds(first, rows)]
        loads.append(pltpu.make_async_copy(source, whole.at[span], semaphores.at[index]))
        loads[-1].start()
    return loads


def attention_kernel(
    frames,
    counts,
    tokens,
    cotangent,
    mods,
    bias,
    blocks,
    attn_in,
    parts,
    mixed_low,
    proj_out,
    resid_out,
    mlp_in,
    d_branch,
    d_branch_sum,
    mixed,
    whole,
    semaphores,
):
    rows, width = tokens.shape
    clip = pl.program_id(0)
    loads = [
        pltpu.make_async_copy(blocks.at[at], whole.at[at], semaphores.at[at]) for at in range(4)
    ]

    @pl.when(clip == 0)
    def _():
        for load in loads:
            load.start()

    tile = min(rows, 128)
    count = counts[clip]
    shift_one, scale_one, gate_one = (mods[0, at : at + 1, :] for at in range(3))
    shift_two, scale_two, gate_two = (mods[0, at : at + 1, :] for at in range(3, 6))
    for first in range(0, rows, tile):
        span = slice(first, first + tile)
        normed, _ = norm_parts(wide(tokens[span]))
        attn_in[span] = narrow(normed * (1.0 + scale_one) + shift_one)
        branch_back = narrow(wide(cotangent[span]) * valid_rows(count, tile, frames) * gate_two)
        d_branch[span] = branch_back
        part_sum = column_sum(wide(branch_back))
        d_branch_sum[0] = part_sum if first == 0 else d_branch_sum[0] + part_sum

    @pl.when(clip == 0)
    def _():
        for load in loads:
            load.wait()

    scale = (width // HEADS) ** -0.5
    source = attn_in[...]
    for low, high in column_cuts(width):
        span = slice(low, high)
        query = (dot_nn(source, whole[0, :, span]) + bias[0:1, span]) * scale
        parts[0, :, span], parts[1, :, span] = split_high(query)
        parts[2, :, span], parts[3, :, span] = split_high(dot_nn(source, whole[1, :, span]))
        parts[4, :, span] = narrow(dot_nn(source, whole[2, :, span]) + bias[2:3, span])
    offset = score_offset(count, tile, frames, 1)
    mixed[...] = jnp.zeros_like(mixed)
    for first in range(0, rows, tile):
        span = slice(first, first + tile)
        for low, high, start, stop in head_windows(width):
            lanes = slice(start, stop)
            mask = lane_mask(low, high, stop - start, jnp.bfloat16)
            key_high = parts[2, span, lanes]
            query_high = parts[0, span, lanes] * mask
            scores = dot_nt(query_high, key_high)
            scores += dot_nt(parts[1, span, lanes] * mask, key_high)
            scores += dot_nt(query_high, parts[3, span, lanes]) + offset
            expons = jnp.exp(scores - jnp.max(scores, axis=-1, keepdims=True))
            probs = expons * (1.0 / jnp.sum(expons, axis=-1, keepdims=True))
            out = dot_nn(narrow(probs), parts[4, span, lanes] * mask)
            mixed[span, lanes] += out
    mixed_low[...] = narrow(mixed[...])
    source = mixed_low[...]
    for low, high in column_cuts(width):
        span = slice(low, high)
        proj_out[:, span] = dot_nn(source, whole[3, :, span]) + bias[3:4, span]
    for first in range(0, rows, tile):
        span = slice(first, first + tile)
        resid = wide(tokens[span]) + valid_rows(count, tile, frames) * gate_one * proj_out[span]
        resid_out[span] = resid
        normed, _ = norm_parts(resid)
        mlp_in[span] = narrow(normed * (1.0 + scale_two) + shift_two)


def run_attention(frames, counts, tokens, cotangent, mods, bias, blocks):
    total, width = tokens.shape
    clips = mods.shape[0]
    rows = total // clips
    clip_rows = spec((rows, width), lambda clip: (clip, 0))
    low = jax.ShapeDtypeStruct((total, width), jnp.bfloat16)
    full = jax.ShapeDtypeStruct((total, width), jnp.float32)
    return pl.pallas_call(
        functools.partial(attention_kernel, frames),
        grid=(clips,),
        in_specs=[
            pl.BlockSpec(memory_space=pltpu.SMEM),
            clip_rows,
            clip_rows,
            spec((1,) + mods.shape[1:], lambda clip: (clip, 0, 0)),
            held(bias.shape),
            pl.BlockSpec(memory_space=pl.ANY),
        ],
        out_specs=[
            clip_rows,
            spec((5, rows, width), lambda clip: (0, clip, 0)),
            clip_rows,
            clip_rows,
            clip_rows,
            clip_rows,
            clip_rows,
            spec((1, 1, width), lambda clip: (clip, 0, 0)),
        ],
        out_shape=[
            low,
            jax.ShapeDtypeStruct((5, total, width), jnp.bfloat16),
            low,
            full,
            full,
            low,
            low,
            jax.ShapeDtypeStruct((clips, 1, width), jnp.float32),
        ],
        scratch_shapes=[
            pltpu.VMEM((rows, width), jnp.float32),
            pltpu.VMEM(blocks.shape, jnp.bfloat16),
            pltpu.SemaphoreType.DMA((4,)),
        ],
        compiler_params=pltpu.CompilerParams(vmem_limit_bytes=vmem_bytes),
        cost_estimate=little_cost,
    )(counts, tokens, cotangent, mods, bias, blocks)


def stacked(numbers):
    return jnp.stack([jnp.asarray(number, jnp.int32) for number in numbers])


def start_loads(cuts, at, parts, whole, semaphores):
    for index, (part, first, rows) in enumerate(cuts):
        span = pl.ds(pl.multiple_of(at[index] * 16, 16), rows)
        source = parts[part].at[pl.ds(first, rows)]
        pltpu.make_async_copy(source, whole.at[span], semaphores.at[index]).start()


def wait_loads(groups, at, parts, whole, semaphores):
    index = 0
    for step, cuts in enumerate(groups):
        base = index
        index += len(cuts)

        @pl.when(pl.program_id(0) == step)
        def _(cuts=cuts, base=base):
            for offset, (part, first, rows) in enumerate(cuts):
                span = pl.ds(pl.multiple_of(at[base + offset] * 16, 16), rows)
                source = parts[part].at[pl.ds(first, rows)]
                semaphore = semaphores.at[base + offset]
                pltpu.make_async_copy(source, whole.at[span], semaphore).wait()


def hidden_kernel(cuts, order, starts, mlp_in, bias, *refs):
    whole_out, hidden, slope, whole, semaphores, store_semaphores = refs[-6:]
    pieces = refs[:-6]
    step, steps = pl.program_id(0), pl.num_programs(0)
    width = mlp_in.shape[-1]
    span = pl.ds(pl.multiple_of(order[step] * width, width), width)

    @pl.when(step == 0)
    def _():
        start_loads([cut for group in cuts for cut in group], starts, pieces, whole, semaphores)

    wait_loads(cuts, starts, pieces, whole, semaphores)
    pltpu.make_async_copy(whole.at[span], whole_out.at[span], store_semaphores.at[step]).start()
    root = (2.0 / math.pi) ** 0.5
    source = mlp_in[...]
    block = whole.at[span]
    for low, high in column_cuts(width):
        lanes = slice(low, high)
        pre = dot_nn(source, block[:, lanes]) + bias[0, :, lanes]
        square = pre * pre
        bent = jnp.tanh(root * pre * (1.0 + 0.044715 * square))
        half = 0.5 + 0.5 * bent
        hidden[0, :, lanes] = narrow(pre * half)
        steep = (0.5 * root) * pre * (1.0 + 3 * 0.044715 * square)
        slope[0, :, lanes] = narrow(half + steep * (1.0 - bent * bent))

    @pl.when(step == steps - 1)
    def _():
        for at in range(len(cuts)):
            rows = pl.ds(pl.multiple_of(order[at] * width, width), width)
            pltpu.make_async_copy(
                whole.at[rows], whole_out.at[rows], store_semaphores.at[at]
            ).wait()


def run_hidden(mlp_in, gathered, bias):
    pieces, cuts, starts, order = gathered
    total, width = mlp_in.shape
    count = len(cuts)
    per_block = pl.BlockSpec((1, total, width), lambda at, order, starts: (order[at], 0, 0))
    out = jax.ShapeDtypeStruct((count, total, width), jnp.bfloat16)
    return pl.pallas_call(
        functools.partial(hidden_kernel, cuts),
        grid_spec=pltpu.PrefetchScalarGridSpec(
            num_scalar_prefetch=2,
            grid=(count,),
            in_specs=[
                pl.BlockSpec((total, width), lambda at, order, starts: (0, 0)),
                pl.BlockSpec((1, 1, width), lambda at, order, starts: (order[at], 0, 0)),
            ]
            + [pl.BlockSpec(memory_space=pl.ANY)] * len(pieces),
            out_specs=[pl.BlockSpec(memory_space=pl.ANY), per_block, per_block],
            scratch_shapes=[
                pltpu.VMEM((count * width, width), jnp.bfloat16),
                pltpu.SemaphoreType.DMA((len(starts),)),
                pltpu.SemaphoreType.DMA((count,)),
            ],
        ),
        out_shape=[jax.ShapeDtypeStruct((count * width, width), jnp.bfloat16), out, out],
        compiler_params=pltpu.CompilerParams(vmem_limit_bytes=vmem_bytes),
        cost_estimate=little_cost,
    )(stacked(order), stacked(starts), mlp_in, bias, *pieces)


def branch_kernel(
    frames,
    cuts,
    order,
    starts,
    counts,
    hidden,
    slope,
    d_branch,
    bias,
    gates,
    resid,
    cotangent,
    *refs,
):
    d_pre, d_pre_sum, block_out, d_gate, branch, whole, semaphores = refs[-7:]
    pieces = refs[:-7]
    step, steps = pl.program_id(0), pl.num_programs(0)
    total, width = resid.shape
    clips = gates.shape[0]
    rows = total // clips
    source, back = hidden[0], d_branch[...]

    @pl.when(step == 0)
    def _():
        start_loads([cut for group in cuts for cut in group], starts, pieces, whole, semaphores)
        branch[...] = jnp.zeros_like(branch)

    wait_loads(cuts, starts, pieces, whole, semaphores)
    block = whole.at[pl.ds(pl.multiple_of(order[step] * width, width), width)]
    for low, high in column_cuts(width):
        span = slice(low, high)
        d_hidden = dot_nt(back, block[span, :])
        low_back = narrow(d_hidden * wide(slope[0, :, span]))
        d_pre[0, :, span] = low_back
        d_pre_sum[0, :, span] = column_sum(wide(low_back))
        branch[:, span] += dot_nn(source, block[:, span])

    @pl.when(step == steps - 1)
    def _():
        for clip in range(clips):
            span = slice(clip * rows, (clip + 1) * rows)
            kept = valid_rows(counts[clip], rows, frames) * (branch[span] + bias[...])
            block_out[span] = narrow(resid[span] + gates[clip] * kept)
            d_gate[clip] = column_sum(wide(cotangent[span]) * kept)


def run_branch(frames, counts, hidden, slope, gathered, d_branch, bias, gates, resid, cotangent):
    pieces, cuts, starts, order = gathered
    count, total, width = hidden.shape
    clips = gates.shape[0]

    def all_of(*shape):
        return pl.BlockSpec(shape, lambda at, order, starts: (0,) * len(shape))

    per_block = pl.BlockSpec((1, total, width), lambda at, order, starts: (order[at], 0, 0))
    low = jax.ShapeDtypeStruct((total, width), jnp.bfloat16)
    return pl.pallas_call(
        functools.partial(branch_kernel, frames, cuts),
        grid_spec=pltpu.PrefetchScalarGridSpec(
            num_scalar_prefetch=2,
            grid=(count,),
            in_specs=[
                pl.BlockSpec(memory_space=pltpu.SMEM),
                per_block,
                per_block,
                all_of(total, width),
                all_of(*bias.shape),
                all_of(*gates.shape),
                all_of(total, width),
                all_of(total, width),
            ]
            + [pl.BlockSpec(memory_space=pl.ANY)] * len(pieces),
            out_specs=[
                per_block,
                pl.BlockSpec((1, 1, width), lambda at, order, starts: (order[at], 0, 0)),
                all_of(total, width),
                all_of(clips, 1, width),
            ],
            scratch_shapes=[
                pltpu.VMEM((total, width), jnp.float32),
                pltpu.VMEM((count * width, width), jnp.bfloat16),
                pltpu.SemaphoreType.DMA((len(starts),)),
            ],
        ),
        out_shape=[
            jax.ShapeDtypeStruct((count, total, width), jnp.bfloat16),
            jax.ShapeDtypeStruct((count, 1, width), jnp.float32),
            low,
            jax.ShapeDtypeStruct((clips, 1, width), jnp.float32),
        ],
        compiler_params=pltpu.CompilerParams(vmem_limit_bytes=vmem_bytes),
        cost_estimate=little_cost,
    )(stacked(order), stacked(starts), counts, hidden, slope, d_branch, bias, gates, resid, cotangent, *pieces)


def resid_kernel(
    frames,
    counts,
    d_pre,
    block,
    mods,
    resid,
    cotangent,
    proj,
    d_resid_out,
    d_proj,
    sums,
    total_grad,
):
    step, steps = pl.program_id(0), pl.num_programs(0)
    total, width = resid.shape
    clips = mods.shape[0]
    rows = total // clips
    tile = min(rows, 128)
    source = d_pre[0]

    @pl.when(step == 0)
    def _():
        total_grad[...] = jnp.zeros_like(total_grad)

    for low, high in column_cuts(width):
        span = slice(low, high)
        total_grad[:, span] += dot_nt(source, block[0, span, :])

    @pl.when(step == steps - 1)
    def _():
        for clip in range(clips):
            gate_one, scale_two = mods[clip, 2:3, :], mods[clip, 4:5, :]
            found = [0.0] * 4
            for first in range(clip * rows, (clip + 1) * rows, tile):
                span = slice(first, first + tile)
                grad = total_grad[span]
                normed, inverse = norm_parts(resid[span])
                back = norm_back(grad * (1.0 + scale_two), normed, inverse)
                d_resid = wide(cotangent[span]) + back
                d_resid_out[span] = d_resid
                kept = valid_rows(counts[clip], tile, frames) * d_resid
                low_back = narrow(kept * gate_one)
                d_proj[span] = low_back
                terms = (grad, grad * normed, kept * proj[span], wide(low_back))
                found = [old + column_sum(term) for old, term in zip(found, terms)]
            for at in range(4):
                sums[clip, at : at + 1, :] = found[at]


def run_resid(frames, counts, d_pre, blocks, mods, resid, cotangent, proj):
    count, total, width = d_pre.shape
    clips = mods.shape[0]
    return pl.pallas_call(
        functools.partial(resid_kernel, frames),
        grid=(count,),
        in_specs=[
            pl.BlockSpec(memory_space=pltpu.SMEM),
            spec((1, total, width), lambda at: (at, 0, 0)),
            spec((1, width, width), lambda at: (at, 0, 0)),
            held(mods.shape),
            held((total, width)),
            held((total, width)),
            held((total, width)),
        ],
        out_specs=[held((total, width)), held((total, width)), held((clips, 4, width))],
        out_shape=[
            jax.ShapeDtypeStruct((total, width), jnp.float32),
            jax.ShapeDtypeStruct((total, width), jnp.bfloat16),
            jax.ShapeDtypeStruct((clips, 4, width), jnp.float32),
        ],
        scratch_shapes=[pltpu.VMEM((total, width), jnp.float32)],
        compiler_params=pltpu.CompilerParams(vmem_limit_bytes=vmem_bytes),
        cost_estimate=little_cost,
    )(counts, d_pre, blocks, mods, resid, cotangent, proj)


def attention_back_kernel(
    frames, counts, d_proj, parts, block, d_qkv, sums, d_mixed, d_query, d_key, d_value
):
    rows, width = d_proj.shape
    tile = min(rows, 128)
    count = counts[pl.program_id(0)]
    source = d_proj[...]
    for low, high in column_cuts(width):
        d_mixed[:, low:high] = narrow(dot_nt(source, block[0, low:high, :]))
    scale = (width // HEADS) ** -0.5
    offset = score_offset(count, tile, frames, 0)
    for ref in (d_query, d_key, d_value):
        ref[...] = jnp.zeros_like(ref)
    for first in range(0, rows, tile):
        span = slice(first, first + tile)
        for low, high, start, stop in head_windows(width):
            lanes = slice(start, stop)
            mask = lane_mask(low, high, stop - start, jnp.bfloat16)
            query_high = parts[0, span, lanes] * mask
            key_high = parts[2, span, lanes] * mask
            back = d_mixed[span, lanes] * mask
            scores = dot_nt(key_high, query_high)
            scores += dot_nt(key_high, parts[1, span, lanes])
            scores += dot_nt(parts[3, span, lanes], query_high) + offset
            expons = jnp.exp(scores - jnp.max(scores, axis=0, keepdims=True))
            probs = expons * (1.0 / jnp.sum(expons, axis=0, keepdims=True))
            d_probs = dot_nt(parts[4, span, lanes], back)
            inner = jnp.sum(d_probs * probs, axis=0, keepdims=True)
            d_scores = narrow(probs * (d_probs - inner))
            d_value[span, lanes] += dot_nn(narrow(probs), back)
            d_key[span, lanes] += dot_nn(d_scores, query_high)
            d_query[span, lanes] += dot_tn(d_scores, key_high)
    for at, ref in enumerate((d_query, d_key, d_value)):
        low_back = narrow(ref[...] * scale) if at == 0 else narrow(ref[...])
        d_qkv[at] = low_back
        sums[0, at : at + 1, :] = column_sum(wide(low_back))
    d_qkv[3] = source


def run_attention_back(frames, counts, d_proj, parts, block):
    total, width = d_proj.shape
    clips = counts.shape[0]
    rows = total // clips
    return pl.pallas_call(
        functools.partial(attention_back_kernel, frames),
        grid=(clips,),
        in_specs=[
            pl.BlockSpec(memory_space=pltpu.SMEM),
            spec((rows, width), lambda clip: (clip, 0)),
            spec((5, rows, width), lambda clip: (0, clip, 0)),
            spec((1, width, width), lambda clip: (3, 0, 0), pipeline_mode=pl.Buffered(1)),
        ],
        out_specs=[
            spec((4, rows, width), lambda clip: (0, clip, 0)),
            spec((1, 3, width), lambda clip: (clip, 0, 0)),
        ],
        out_shape=[
            jax.ShapeDtypeStruct((4, total, width), jnp.bfloat16),
            jax.ShapeDtypeStruct((clips, 3, width), jnp.float32),
        ],
        scratch_shapes=[pltpu.VMEM((rows, width), jnp.bfloat16)]
        + [pltpu.VMEM((rows, width), jnp.float32)] * 3,
        compiler_params=pltpu.CompilerParams(vmem_limit_bytes=vmem_bytes),
        cost_estimate=little_cost,
    )(counts, d_proj, parts, block)


def input_kernel(d_qkv, block, mods, tokens, d_resid, input_grad, sums, total_grad):
    step, steps = pl.program_id(0), pl.num_programs(0)
    total, width = tokens.shape
    clips = mods.shape[0]
    rows = total // clips
    tile = min(rows, 128)
    source = d_qkv[0]

    @pl.when(step == 0)
    def _():
        total_grad[...] = jnp.zeros_like(total_grad)

    for low, high in column_cuts(width):
        span = slice(low, high)
        total_grad[:, span] += dot_nt(source, block[0, span, :])

    @pl.when(step == steps - 1)
    def _():
        for clip in range(clips):
            scale_one = mods[clip, 1:2, :]
            found = [0.0] * 2
            for first in range(clip * rows, (clip + 1) * rows, tile):
                span = slice(first, first + tile)
                grad = total_grad[span]
                normed, inverse = norm_parts(wide(tokens[span]))
                back = norm_back(grad * (1.0 + scale_one), normed, inverse)
                input_grad[span] = narrow(d_resid[span] + back)
                terms = (grad, grad * normed)
                found = [old + column_sum(term) for old, term in zip(found, terms)]
            for at in range(2):
                sums[clip, at : at + 1, :] = found[at]


def run_input(d_qkv, blocks, mods, tokens, d_resid):
    total, width = tokens.shape
    clips = mods.shape[0]
    return pl.pallas_call(
        input_kernel,
        grid=(3,),
        in_specs=[
            spec((1, total, width), lambda at: (at, 0, 0)),
            spec((1, width, width), lambda at: (at, 0, 0)),
            held(mods.shape),
            held((total, width)),
            held((total, width)),
        ],
        out_specs=[held((total, width)), held((clips, 2, width))],
        out_shape=[
            jax.ShapeDtypeStruct((total, width), jnp.bfloat16),
            jax.ShapeDtypeStruct((clips, 2, width), jnp.float32),
        ],
        scratch_shapes=[pltpu.VMEM((total, width), jnp.float32)],
        compiler_params=pltpu.CompilerParams(vmem_limit_bytes=vmem_bytes),
        cost_estimate=little_cost,
    )(d_qkv, blocks, mods, tokens, d_resid)


def halves_kernel(left_of, adds, steps, order, side, *refs):
    lefts = refs[: max(left_of) + 1]
    right = refs[len(lefts)]
    turned, total_low = refs[-2:]
    if adds:
        incoming, first_keep, first_out, second_keep, second_out = refs[len(lefts) + 1 : -2]
    else:
        out = refs[-3]
    step = pl.program_id(0)
    block = order[step]
    width = lefts[0].shape[-1]
    half = width // 2

    def pick(left, at):
        lanes = slice(at * half, (at + 1) * half)
        turned[...] = (left[:, lanes] if left.ndim == 2 else left[0, :, lanes]).T

    fresh = (step == 0) | (lefts[0].ndim == 3) | (len(lefts) > 1)
    for at in range(2):
        for index, left in enumerate(lefts):
            of_left = [block == number for number, source in enumerate(left_of) if source == index]

            @pl.when(fresh & (side[0] == at) & functools.reduce(jnp.logical_or, of_left))
            def _(left=left, at=at):
                pick(left, at)

    found = dot_nn(turned[...], right[0] if right.ndim == 3 else right[...])
    if not adds:
        out[0] = narrow(found)
        return
    total_low[...] = narrow(found + wide(incoming[0]))
    for state, target, rows in (
        (steps[0][0], first_keep, slice(0, half // 2)),
        (steps[0][1], first_out, slice(0, half // 2)),
        (steps[1][0], second_keep, slice(half // 2, half)),
        (steps[1][1], second_out, slice(half // 2, half)),
    ):

        @pl.when(functools.reduce(jnp.logical_or, [step == at_step for at_step in state]))
        def _(target=target, rows=rows):
            target[0] = total_low[rows]


def run_halves(lefts, left_of, right, side, at, incoming=None):
    total, width = lefts[0].shape[-2:]
    half = width // 2
    low_bit, high_bit = at % 2, at // 2
    order = stacked([at ^ 3, at ^ 1, at, at ^ 2])
    places = {
        "first_keep": [high_bit, high_bit, high_bit, 1 - high_bit],
        "first_out": [1 - high_bit, high_bit, high_bit, high_bit],
        "second_keep": [1 - low_bit, 1 - low_bit, low_bit, low_bit],
        "second_out": [1 - low_bit, low_bit, low_bit, low_bit],
    }
    steps = (((2, 3), (0, 1)), ((1, 2), (0, 3)))
    adds = incoming is not None
    table = stacked([place for row in places.values() for place in row])

    def block_of(array, *rest):
        if array.ndim == 2:
            return pl.BlockSpec(array.shape, lambda step, order, side, table: (0, 0))
        return pl.BlockSpec((1,) + array.shape[1:], lambda step, order, side, table: (order[step], 0, 0))

    per_block = pl.BlockSpec((1, half, width), lambda step, order, side, table: (order[step], 0, 0))
    operands = list(lefts) + [right]
    in_specs = [block_of(array) for array in operands]
    if adds:
        operands.append(incoming)
        in_specs.append(per_block)
        out_specs = [
            pl.BlockSpec(
                (1, half // 2, width),
                functools.partial(lambda row, step, order, side, table: (table[row * 4 + step], 0, 0), row),
            )
            for row in range(4)
        ]
        out_shape = [jax.ShapeDtypeStruct((2, half // 2, width), jnp.bfloat16)] * 4
    else:
        out_specs = per_block
        out_shape = jax.ShapeDtypeStruct((4, half, width), jnp.bfloat16)

    def body(order, side, table, *refs):
        halves_kernel(left_of, adds, steps, order, side, *refs)

    return pl.pallas_call(
        body,
        grid_spec=pltpu.PrefetchScalarGridSpec(
            num_scalar_prefetch=3,
            grid=(4,),
            in_specs=in_specs,
            out_specs=out_specs,
            scratch_shapes=[
                pltpu.VMEM((half, total), jnp.bfloat16),
                pltpu.VMEM((half, width), jnp.bfloat16),
            ],
        ),
        out_shape=out_shape,
        compiler_params=pltpu.CompilerParams(vmem_limit_bytes=vmem_bytes),
        cost_estimate=little_cost,
    )(order, stacked([side]), table, *operands)


def tie(*values):
    return lax.optimization_barrier(values)


def packed(arrays, tile):
    flat = jnp.concatenate([array.reshape(-1) for array in arrays])
    return jnp.pad(flat, (0, -flat.shape[0] % (tile * 128))).reshape(-1, 128)


def core_swap(array):
    count = lax.axis_size("dp")
    return lax.ppermute(array, "dp", [(at, at ^ 1) for at in range(count)])


def chip_shift(array, step):
    count = lax.axis_size("dp")
    return lax.ppermute(array, "dp", [(at, (at + 2 * step) % count) for at in range(count)])


def chip_swap(array, bits):
    count = lax.axis_size("dp")
    return lax.ppermute(array, "dp", [(at, at ^ (2 * bits)) for at in range(count)])


def rank_swap(array, bits):
    count = lax.axis_size("fsdp")
    return lax.ppermute(array, "fsdp", [(at, at ^ bits) for at in range(count)])


def entry(array, at, axis=0):
    return lax.dynamic_index_in_dim(array, at, axis, keepdims=False)


def place_kernel(cuts, at, *refs):
    parts, whole, held_rows, semaphores = refs[:-3], refs[-3], refs[-2], refs[-1]
    spans, loads, stores = [], [], []
    for index, (part, first, rows) in enumerate(cuts):
        spans.append(pl.ds(pl.multiple_of(at[index] * 16, 16), rows))
        source = parts[part].at[pl.ds(first, rows)]
        loads.append(
            pltpu.make_async_copy(source, held_rows.at[spans[index]], semaphores.at[0, index])
        )
        loads[index].start()
    for index, span in enumerate(spans):
        loads[index].wait()
        stores.append(
            pltpu.make_async_copy(held_rows.at[span], whole.at[span], semaphores.at[1, index])
        )
        stores[index].start()
    for store in stores:
        store.wait()


def place(parts, cuts, starts, rows):
    width = parts[0].shape[-1]
    dtype = parts[0].dtype
    return pl.pallas_call(
        functools.partial(place_kernel, cuts),
        in_specs=[pl.BlockSpec(memory_space=pltpu.SMEM)]
        + [pl.BlockSpec(memory_space=pl.ANY)] * len(parts),
        out_specs=pl.BlockSpec(memory_space=pl.ANY),
        out_shape=jax.ShapeDtypeStruct((rows, width), dtype),
        scratch_shapes=[
            pltpu.VMEM((rows, width), dtype),
            pltpu.SemaphoreType.DMA((2, len(cuts))),
        ],
        compiler_params=pltpu.CompilerParams(vmem_limit_bytes=vmem_bytes),
        cost_estimate=little_cost,
    )(stacked(starts), *parts)


def own_rows(parts, group):
    ranks, at = lax.axis_size("fsdp"), lax.axis_index("fsdp")
    shares = ranks // group
    count, _, row_part, col_part = parts.shape
    chunk = row_part // shares
    split = parts.reshape(count, group, shares, chunk, col_part).transpose(1, 2, 0, 3, 4)
    split = split.reshape(ranks, count, chunk, col_part)
    if shares > 1:
        moved = lax.all_to_all(split, "fsdp", 0, 0, tiled=True)
        (moved,) = yield (moved,)
        yield moved.transpose(1, 2, 0, 3).reshape(count, chunk, ranks * col_part)
        return
    panels = [entry(split, at)]
    panels += [rank_swap(entry(split, at ^ bits), bits) for bits in range(1, ranks)]
    panels = yield tuple(panels)
    placed = [
        lax.select_n(at, *[panels[panel ^ index] for index in range(ranks)])
        for panel in range(ranks)
    ]
    yield jnp.concatenate(placed, axis=2)


def shard_rows(split, group):
    ranks, count, chunk, col_part = split.shape
    shares = ranks // group
    moved = lax.all_to_all(split, "fsdp", 0, 0, tiled=True)
    moved = moved.reshape(group, shares, count, chunk, col_part).transpose(2, 0, 1, 3, 4)
    return moved.reshape(count, group, shares * chunk, col_part)


def gather_blocks(rows, group):
    ranks, dp_count = lax.axis_size("fsdp"), lax.axis_size("dp")
    shares = ranks // group
    chunk, total = rows.shape
    all_rows = lax.all_gather(rows, ("fsdp", "dp"), axis=0, tiled=True)
    if shares > 1:
        all_rows = all_rows.reshape(group, shares, dp_count, chunk, total).transpose(0, 2, 1, 3, 4)
    return all_rows.reshape(group, total, total)


def join_line(found):
    chips, chip = lax.axis_size("dp") // 2, lax.axis_index("dp") // 2
    chunk = found[0].shape[0]
    starts = [(chip - step) % chips * (chunk // 16) for step in range(chips)]
    return place(found, [(step, 0, chunk) for step in range(chips)], starts, chips * chunk)


def gather_second(rows, group):
    ranks, at = lax.axis_size("fsdp"), lax.axis_index("fsdp")
    total = rows.shape[-1]
    if ranks != group:
        blocks = gather_blocks(rows, group).reshape(group * total, total)
        for _ in range(4):
            (blocks,) = yield (blocks,)
        cuts = [[(0, index * total, total)] for index in range(group)]
        yield [blocks], cuts, [index * (total // 16) for index in range(group)], range(group)
        return
    chips = lax.axis_size("dp") // 2
    core = lax.axis_index("dp") % 2
    chunk, half = rows.shape[0], total // 2
    others = yield tuple(chip_shift(rows, step) for step in range(1, chips))
    line = join_line([rows, *others])
    cuts = [(side, step * chunk, chunk) for side in range(2) for step in range(chips)]
    starts = [
        (2 * step + side) * (chunk // 16) for side in (core, 1 - core) for step in range(chips)
    ]
    (own,) = yield (place([line, core_swap(line)], cuts, starts, total),)
    share = lax.dynamic_slice_in_dim(own, core * half, half, 0)
    low, high = yield (rank_swap(share, 1), rank_swap(share, 2))
    quarter = half // 2
    low_other, high_other = core_swap(low), core_swap(high)
    last = yield (rank_swap(high[:quarter], 1), rank_swap(low[quarter:], 2))
    parts = [own, low, low_other, high, high_other, *last, *[core_swap(part) for part in last]]
    cuts = [[(0, 0, total)], [(1, 0, half), (2, 0, half)], [(3, 0, half), (4, 0, half)]]
    cuts.append([(5 + index, 0, quarter) for index in range(4)])
    starts = [at * (total // 16)]
    for bits in (1, 2):
        starts += [((at ^ bits) * 2 + side) * (half // 16) for side in (core, 1 - core)]
    for side in (core, 1 - core):
        first = ((at ^ 3) * 2 + side) * (half // 16)
        starts += [first, first + quarter // 16]
    yield parts, cuts, starts, [at ^ bits for bits in range(ranks)]


def gather_own(rows, group):
    ranks = lax.axis_size("fsdp")
    shares = ranks // group
    if shares > 1:
        sets = [[share + shares * block for share in range(shares)] for block in range(group)]
        rows = lax.all_gather(rows, "fsdp", axis=1, tiled=True, axis_index_groups=sets)
    return lax.all_gather(rows, "dp", axis=1, tiled=True)


def sum_blocks(lefts, left_of, right, group):
    ranks, dp_count = lax.axis_size("fsdp"), lax.axis_size("dp")
    shares = ranks // group
    total = lefts[0].shape[-1]
    if shares > 1:
        blocks = jnp.stack(
            [
                narrow(
                    fast_dot(
                        "tr,te->re",
                        lefts[index] if lefts[index].ndim == 2 else lefts[index][block],
                        right if right.ndim == 2 else right[block],
                    )
                )
                for block, index in enumerate(left_of)
            ]
        )
        chunk = total // (dp_count * shares)
        blocks = blocks.reshape(group, dp_count, shares, chunk, -1).transpose(0, 2, 1, 3, 4)
        rows = lax.psum_scatter(
            blocks.reshape(group * total, -1), ("fsdp", "dp"), scatter_dimension=0, tiled=True
        )
        for _ in range(7):
            (rows,) = yield (rows,)
        yield gather_own(rows[None], group)[0]
        return
    chips, half = dp_count // 2, total // 2
    chunk = half // chips
    at = lax.axis_index("fsdp")
    core, chip = lax.axis_index("dp") % 2, lax.axis_index("dp") // 2
    low_bit, high_bit = at % 2, at // 2
    (away,) = yield (run_halves(lefts, left_of, right, 1 - core, at),)
    (away_in,) = yield (core_swap(away),)
    first, first_out, second, second_out = run_halves(lefts, left_of, right, core, at, away_in)
    first_out, second_out = yield (first_out, second_out)
    first_in, second_in = yield (rank_swap(first_out, 1), rank_swap(second_out, 2))
    first = narrow(wide(first) + wide(first_in)).reshape(2, chips // 2, chunk, -1)
    second = narrow(wide(second) + wide(second_in)).reshape(2, chips // 2, chunk, -1)
    first_in = rank_swap(entry(first, 1 - high_bit), 2)
    second_in = rank_swap(entry(second, 1 - low_bit), 1)
    first_in, second_in = yield (first_in, second_in)
    first = narrow(wide(entry(first, high_bit)) + wide(first_in))
    second = narrow(wide(entry(second, low_bit)) + wide(second_in))
    line = jnp.concatenate([first, second])
    step = 1
    while step < chips:
        bit = chip // step % 2
        line = line.reshape(-1, 2, *line.shape[1:])
        (line_in,) = yield (chip_swap(entry(line, 1 - bit, 1), step),)
        line = narrow(wide(entry(line, bit, 1)) + wide(line_in))
        step *= 2
    yield lax.all_gather(line[0], "dp", axis=0, tiled=True)


def fast_dot(subscripts, left, right):
    return jnp.einsum(subscripts, left, right, preferred_element_type=jnp.float32)


def products_kernel(chips, at, gathered, left_root, right_root, out, whole, semaphores):
    chunk, width = left_root.shape[1:]
    ranks = out.shape[0]
    copies = []
    for index in range(2 * chips):
        first = (index % 2 * chips + index // 2) * chunk
        copies.append(
            pltpu.make_async_copy(
                gathered.at[pl.ds(index * chunk, chunk)],
                whole.at[pl.ds(first, chunk)],
                semaphores.at[index],
            )
        )
        copies[-1].start()
    for copy in copies:
        copy.wait()
    first = at[0] * 16
    grad = whole[...]
    picked = lax.broadcasted_iota(jnp.int32, (width, chunk), 0) - first
    picked = picked == lax.broadcasted_iota(jnp.int32, (width, chunk), 1)
    own_columns = narrow(dot_nn(grad, narrow(picked.astype(jnp.float32))))
    side_high, side_low = split_high(dot_nn(left_root[0], grad))
    right = right_root[0]
    precond = dot_nn(side_high, right) + dot_nn(side_low, right)
    outer = dot_nt(whole[pl.ds(pl.multiple_of(first, 16), chunk), :], grad)
    inner = dot_tn(own_columns, grad)
    for at_out, product in enumerate((precond, outer, inner)):
        low = narrow(product)
        for rank in range(ranks):
            span = slice(rank * (width // ranks), (rank + 1) * (width // ranks))
            out[rank, at_out] = low[:, span]


def owned_step(whole, left_roots, right_roots, index, group):
    ranks, dp_count = lax.axis_size("fsdp"), lax.axis_size("dp")
    shares = ranks // group
    chunk, total = left_roots.shape[1:]
    col_part = total // ranks
    first = lax.axis_index("dp") * (chunk * shares) + lax.axis_index("fsdp") % shares * chunk
    if shares == 1:
        return pl.pallas_call(
            functools.partial(products_kernel, dp_count // 2),
            in_specs=[
                pl.BlockSpec(memory_space=pltpu.SMEM),
                pl.BlockSpec(memory_space=pl.ANY),
                pl.BlockSpec((1, chunk, total), lambda step: (index, 0, 0)),
                pl.BlockSpec((1, total, total), lambda step: (index, 0, 0)),
            ],
            out_specs=pl.BlockSpec((ranks, 3, chunk, col_part), lambda step: (0, 0, 0, 0)),
            grid=(1,),
            out_shape=jax.ShapeDtypeStruct((ranks, 3, chunk, col_part), jnp.bfloat16),
            scratch_shapes=[
                pltpu.VMEM((total, total), jnp.bfloat16),
                pltpu.SemaphoreType.DMA((dp_count,)),
            ],
            compiler_params=pltpu.CompilerParams(vmem_limit_bytes=vmem_bytes),
            cost_estimate=little_cost,
        )((first // 16)[None], whole, left_roots, right_roots)
    left_root, right_root = left_roots[index], right_roots[index]
    grad_rows = lax.dynamic_slice_in_dim(whole, first, chunk, 0)
    own_columns = lax.dynamic_slice_in_dim(whole, first, chunk, 1)
    outer = fast_dot("rk,jk->rj", grad_rows, whole)
    inner = fast_dot("kr,kj->rj", own_columns, whole)
    side_high, side_low = split_high(fast_dot("rk,kj->rj", left_root, whole))
    precond = fast_dot("rk,kj->rj", side_high, right_root) + fast_dot(
        "rk,kj->rj", side_low, right_root
    )
    products = narrow(jnp.stack([precond, outer, inner]))
    return products.reshape(3, chunk, ranks, col_part).transpose(2, 0, 1, 3)


def per_device(
    tokens,
    conditioning,
    frame_counts,
    cotangent,
    weights,
    biases,
    momentum,
    left_stats,
    right_stats,
    left_roots,
    right_roots,
    bias_moment,
    bias_second,
):
    group = 4
    mod_count = 6
    clip_count, pos_count, frames, width = tokens.shape
    token_count = clip_count * pos_count * frames
    block_count, row_part, col_part = weights.shape
    dp_count, ranks = lax.axis_size("dp"), lax.axis_size("fsdp")
    dp_at, rank_at = lax.axis_index("dp"), lax.axis_index("fsdp")
    all_clips = clip_count * dp_count
    bias_part = biases.shape[0]
    stream = tokens.reshape(token_count, width)
    grad_out = cotangent.reshape(token_count, width)
    low_weights = narrow(weights).reshape(block_count, row_part, col_part)
    shards = low_weights[mod_count:].reshape(-1, group, row_part, col_part)

    weight_rows = own_rows(shards, group)
    weight_panels = next(weight_rows)
    cond_low = narrow(jax.nn.silu(conditioning))
    first_parts = lax.all_gather(packed([cond_low, narrow(biases)], 16), "dp", axis=0, tiled=True)
    weight_panels, first_parts = tie(weight_panels, first_parts)
    attn_rows, one_rows, two_rows = weight_rows.send(weight_panels)
    attn_w = gather_blocks(attn_rows, group)
    two_w = gather_blocks(two_rows, group).reshape(group * width, width)
    two_gathered = (
        [two_w],
        [[(0, index * width, width)] for index in range(group)],
        [index * (width // 16) for index in range(group)],
        range(group),
    )

    first_parts = first_parts.reshape(dp_count, -1)
    cond_all = first_parts[:, : clip_count * width].reshape(all_clips, width)
    bias_rows = wide(first_parts[:, clip_count * width : clip_count * width + bias_part])
    cond_rows = lax.dynamic_slice_in_dim(cond_all, dp_at * row_part, row_part, 1)
    cond_cols = wide(lax.dynamic_slice_in_dim(cond_all, rank_at * col_part, col_part, 1))
    mod_parts = fast_dot("cr,jre->cje", cond_rows, low_weights[:mod_count])
    mod_parts = lax.all_to_all(mod_parts, "dp", 0, 0, tiled=True)
    mod_parts, one_rows = tie(mod_parts, one_rows)
    one_steps = gather_second(one_rows, group)
    one_parts = next(one_steps)
    mod_cols = jnp.sum(mod_parts.reshape(dp_count, clip_count, mod_count, col_part), axis=0)
    left_cond = jnp.einsum("jrk,ck->jrc", left_roots[:mod_count], cond_cols, precision=precise)
    mod_size, bias_size = mod_cols.size, dp_count * bias_part
    second_parts = lax.all_gather(
        packed([mod_cols, bias_rows, left_cond], 8), "fsdp", axis=0, tiled=True
    )
    second_parts, one_parts = tie(second_parts, one_parts)
    roots = jnp.stack([narrow(left_roots[mod_count:]), narrow(right_roots[mod_count:])])
    one_parts, attn_w, roots = tie(one_steps.send(one_parts), attn_w, roots)
    one_parts = one_steps.send(one_parts)
    second_parts = second_parts.reshape(ranks, -1)
    mods = second_parts[:, :mod_size].reshape(ranks, clip_count, mod_count, col_part)
    mods = mods.transpose(1, 2, 0, 3).reshape(clip_count, mod_count, width)
    bias_all = second_parts[:, mod_size : mod_size + bias_size].reshape(ranks, dp_count, bias_part)
    bias_all = bias_all.transpose(1, 0, 2).reshape(-1, width)
    left_size = mod_size + bias_size + left_cond.size
    left_cond = jnp.sum(second_parts[:, mod_size + bias_size : left_size], axis=0)
    left_cond = left_cond.reshape(mod_count, row_part, all_clips)
    mods = mods + bias_all[:mod_count]
    bias_table = jnp.concatenate(
        [bias_all[6:7], jnp.zeros((1, width), jnp.float32), bias_all[7:14]]
    )

    attn_in, parts, mixed, proj, resid, mlp_in, d_branch, d_branch_sums = run_attention(
        frames, frame_counts, stream, grad_out, mods, bias_table, attn_w
    )
    mlp_in, one_parts = tie(mlp_in, one_parts)
    one_parts = one_steps.send(one_parts)
    one_w, hidden, slope = run_hidden(mlp_in, one_steps.send(one_parts), bias_table[4:8, None])
    one_w = one_w.reshape(group, width, width)

    two_steps = sum_blocks([hidden], [0] * group, d_branch, group)
    two_parts = next(two_steps)
    hidden, two_parts, roots = tie(hidden, two_parts, roots)
    two_parts = two_steps.send(two_parts)
    root_rows = own_rows(roots.reshape(-1, group, row_part, col_part), group)
    root_panels = next(root_rows)
    d_pre, d_pre_sums, block_out, d_gate_two = run_branch(
        frames,
        frame_counts,
        hidden,
        slope,
        two_gathered,
        d_branch,
        bias_table[8:9],
        mods[:, 5:6],
        resid,
        grad_out,
    )
    d_pre, root_panels = tie(d_pre, root_panels)
    root_rows = root_rows.send(root_panels)
    d_pre, two_parts, root_rows = tie(d_pre, two_parts, root_rows)
    two_parts = two_steps.send(two_parts)
    d_pre, two_parts = tie(d_pre, two_parts)
    two_parts = two_steps.send(two_parts)
    right_wholes = gather_own(root_rows[3:], group)
    one_steps = sum_blocks([mlp_in], [0] * group, d_pre, group)
    one_parts = next(one_steps)
    d_pre, one_parts = tie(d_pre, one_parts)
    one_parts = one_steps.send(one_parts)
    d_resid, d_proj, resid_sums = run_resid(
        frames, frame_counts, d_pre, one_w, mods, resid, grad_out, proj
    )
    d_proj, one_parts = tie(d_proj, one_parts)
    one_parts = one_steps.send(one_parts)
    d_proj, one_parts, two_parts = tie(d_proj, one_parts, two_parts)
    two_parts = two_steps.send(two_parts)
    one_parts = one_steps.send(one_parts)
    d_heads, head_sums = run_attention_back(frames, frame_counts, d_proj, parts, attn_w)
    d_heads, two_parts, one_parts, right_wholes = tie(
        d_heads, two_parts, one_parts, right_wholes
    )
    two_parts = two_steps.send(two_parts)
    one_parts = one_steps.send(one_parts)
    attn_steps = sum_blocks([attn_in, mixed], [0, 0, 0, 1], d_heads, group)
    attn_parts = next(attn_steps)
    d_heads, attn_parts = tie(d_heads, attn_parts)
    attn_parts = attn_steps.send(attn_parts)
    input_grad, input_sums = run_input(d_heads, attn_w, mods, stream, d_resid)
    input_sums, attn_parts, two_parts, one_parts = tie(
        input_sums, attn_parts, two_parts, one_parts
    )
    two_parts = two_steps.send(two_parts)
    one_parts = one_steps.send(one_parts)

    d_mods = jnp.stack(
        [
            input_sums[:, 0],
            input_sums[:, 1],
            resid_sums[:, 2],
            resid_sums[:, 0],
            resid_sums[:, 1],
            d_gate_two[:, 0],
        ],
        axis=1,
    )
    head_sums = jnp.sum(head_sums, axis=0)
    grad_bias = jnp.concatenate(
        [
            jnp.sum(d_mods, axis=0),
            head_sums[0:1],
            head_sums[2:3],
            jnp.sum(resid_sums[:, 3], axis=0)[None],
            d_pre_sums[:, 0],
            jnp.sum(d_branch_sums, axis=0),
        ]
    )
    to_ranks = jnp.concatenate(
        [
            d_mods.reshape(clip_count, mod_count, ranks, col_part)
            .transpose(2, 0, 1, 3)
            .reshape(ranks, mod_size),
            grad_bias.reshape(dp_count, ranks, bias_part)
            .transpose(1, 0, 2)
            .reshape(ranks, bias_size),
        ],
        axis=1,
    )
    rank_sums = lax.all_to_all(to_ranks, "fsdp", 0, 0, tiled=True)
    rank_sums, attn_parts = tie(rank_sums, attn_parts)
    attn_parts = attn_steps.send(attn_parts)
    rank_sums = jnp.sum(rank_sums, axis=0)
    to_rows = jnp.concatenate(
        [
            jnp.broadcast_to(rank_sums[None, :mod_size], (dp_count, mod_size)),
            rank_sums[mod_size:].reshape(dp_count, bias_part),
        ],
        axis=1,
    )
    to_rows, attn_parts = tie(to_rows, attn_parts)
    attn_parts = attn_steps.send(attn_parts)
    from_rows = lax.all_to_all(to_rows, "dp", 0, 0, tiled=True)
    from_rows, attn_parts, two_parts, one_parts = tie(from_rows, attn_parts, two_parts, one_parts)
    attn_parts = attn_steps.send(attn_parts)
    whole_two = two_steps.send(two_parts)
    one_parts = one_steps.send(one_parts)
    bias_grad = jnp.sum(from_rows[:, mod_size:], axis=0)
    mod_grad_cols = from_rows[:, :mod_size].reshape(all_clips, mod_count, col_part)
    mod_grad = lax.all_gather(packed([mod_grad_cols], 8), "fsdp", axis=0, tiled=True)
    mod_grad, attn_parts, one_parts = tie(mod_grad, attn_parts, one_parts)
    attn_parts = attn_steps.send(attn_parts)
    whole_one = one_steps.send(one_parts)
    products_two = owned_step(whole_two, root_rows, right_wholes, 2, group)
    products_two, attn_parts = tie(products_two, attn_parts)
    attn_parts = attn_steps.send(attn_parts)
    back_two = shard_rows(products_two, group)
    products_one = owned_step(whole_one, root_rows, right_wholes, 1, group)
    mod_grad, back_two, attn_parts = tie(mod_grad, back_two, attn_parts)
    whole_attn = attn_steps.send(attn_parts)
    back_one = shard_rows(products_one, group)
    mod_grad = mod_grad.reshape(ranks, -1)[:, : mod_grad_cols.size]
    mod_grad = mod_grad.reshape(ranks, all_clips, mod_count, col_part).transpose(1, 2, 0, 3)
    mod_grad = mod_grad.reshape(all_clips, mod_count, width)

    mod_grad_rows = lax.dynamic_slice_in_dim(mod_grad, dp_at * row_part, row_part, 2)
    right_parts = jnp.einsum(
        "cjk,jke->cje", mod_grad_rows, right_roots[:mod_count], precision=precise
    )
    cond_wide = wide(cond_all)
    cond_row_wide = wide(cond_rows)
    mod_gram = jnp.einsum("cjk,bjk->jcb", mod_grad, mod_grad, precision=precise)
    cond_gram = jnp.einsum("ck,bk->cb", cond_wide, cond_wide, precision=precise)
    mod_side = jnp.einsum("jcb,be->jce", mod_gram, cond_cols, precision=precise)
    ada_left = jnp.einsum("cr,jce->jre", cond_row_wide, mod_side, precision=precise)
    cond_side = jnp.einsum("cb,bje->jce", cond_gram, mod_grad_cols, precision=precise)
    ada_right = jnp.einsum("cjr,jce->jre", mod_grad_rows, cond_side, precision=precise)

    right_parts = lax.all_gather(packed([right_parts], 8), "dp", axis=0, tiled=True)
    mod_right = jnp.sum(right_parts.reshape(dp_count, -1), axis=0)[: mod_grad_cols.size]
    mod_right = mod_right.reshape(all_clips, mod_count, col_part)
    ada_pre = jnp.einsum("jrc,cje->jre", left_cond, mod_right, precision=precise)
    whole_attn, back_one = tie(whole_attn, back_one)
    back_attn = shard_rows(owned_step(whole_attn, root_rows, right_wholes, 0, group), group)

    def joined(at, ada):
        return jnp.concatenate([ada, wide(back_attn[at]), wide(back_one[at]), wide(back_two[at])])

    precond = joined(0, ada_pre)
    left_new = stat_decay * left_stats + (1.0 - stat_decay) * joined(1, ada_left)
    right_new = stat_decay * right_stats + (1.0 - stat_decay) * joined(2, ada_right)
    momentum_new = moment_decay * momentum + precond
    weights_new = weights - weight_rate * momentum_new
    weights_copy = weights_new.astype(jnp.bfloat16)
    bias_second_new = stat_decay * bias_second + (1.0 - stat_decay) * bias_grad * bias_grad
    bias_moment_new = moment_decay * bias_moment + bias_grad * lax.rsqrt(
        bias_second_new + diag_epsilon
    )
    biases_new = biases - bias_rate * bias_moment_new
    return (
        block_out.reshape(tokens.shape),
        input_grad.reshape(tokens.shape),
        left_new,
        right_new,
        momentum_new,
        weights_new,
        weights_copy,
        bias_moment_new,
        bias_second_new,
        biases_new,
    )


def solution(mesh):
    placed = (
        P("dp", "fsdp", None, None),
        P("dp", None),
        P("dp"),
        P("dp", "fsdp", None, None),
        P(None, "dp", "fsdp"),
        P(("dp", "fsdp")),
        P(None, "dp", "fsdp"),
        P(None, "dp", "fsdp"),
        P(None, "dp", "fsdp"),
        P(None, "dp", "fsdp"),
        P(None, "dp", "fsdp"),
        P(("dp", "fsdp")),
        P(("dp", "fsdp")),
    )
    return jax.shard_map(
        per_device,
        mesh=mesh,
        in_specs=placed,
        out_specs=(
            P("dp", "fsdp", None, None),
            P("dp", "fsdp", None, None),
            P(None, "dp", "fsdp"),
            P(None, "dp", "fsdp"),
            P(None, "dp", "fsdp"),
            P(None, "dp", "fsdp"),
            P(None, "dp", "fsdp"),
            P(("dp", "fsdp")),
            P(("dp", "fsdp")),
            P(("dp", "fsdp")),
        ),
        check_vma=False,
    )
```

```python
import functools
import math

import jax
import jax.numpy as jnp
from jax import lax
from jax.experimental import pallas as pl
from jax.experimental.pallas import tpu as pltpu
from jax.sharding import PartitionSpec as P

HEADS = 16


precise = lax.Precision.HIGHEST
norm_epsilon = 1e-06
masked_score = -1e30
stat_decay = 0.5
moment_decay = 0.9
weight_rate = 0.7
bias_rate = 0.1
diag_epsilon = 1e-08
vmem_bytes = 50 * 2**20
little_cost = pl.CostEstimate(flops=1024, bytes_accessed=1024, transcendentals=0)


def narrow(array):
    return array.astype(jnp.bfloat16)


def wide(array):
    return array.astype(jnp.float32)


def spec(shape, index_map, **keywords):
    return pl.BlockSpec(shape, index_map, **keywords)


def held(shape):
    return pl.BlockSpec(shape, lambda step: (0,) * len(shape), pipeline_mode=pl.Buffered(1))


def column_cuts(total):
    cuts, at = [], 0
    while at < total:
        cuts.append((at, min(total, at + 256)))
        at += 256
    return cuts


def dot_nn(left, right):
    return lax.dot_general(left, right, (((1,), (0,)), ((), ())), preferred_element_type=jnp.float32)


def dot_nt(left, right):
    return lax.dot_general(left, right, (((1,), (1,)), ((), ())), preferred_element_type=jnp.float32)


def dot_tn(left, right):
    return lax.dot_general(left, right, (((0,), (0,)), ((), ())), preferred_element_type=jnp.float32)


def split_high(values):
    high = narrow(values)
    return high, narrow(values - wide(high))


def valid_rows(count, rows, frames):
    at = lax.broadcasted_iota(jnp.int32, (rows, 1), 0)
    return (lax.rem(at, frames) < count).astype(jnp.float32)


def score_offset(count, size, frames, key_axis):
    first = lax.broadcasted_iota(jnp.int32, (size, size), 0)
    second = lax.broadcasted_iota(jnp.int32, (size, size), 1)
    key = second if key_axis == 1 else first
    met = (lax.div(first, frames) == lax.div(second, frames)) & (lax.rem(key, frames) < count)
    return jnp.where(met, 0.0, masked_score)


def head_windows(width):
    size = width // HEADS
    windows = []
    for head in range(HEADS):
        low, high = head * size, (head + 1) * size
        start = low // 128 * 128
        stop = min(width, -(-high // 128) * 128)
        windows.append((low - start, high - start, start, stop))
    return windows


def lane_mask(low, high, count, dtype):
    lanes = lax.broadcasted_iota(jnp.int32, (1, count), 1)
    return ((lanes >= low) & (lanes < high)).astype(jnp.float32).astype(dtype)


def norm_parts(values):
    centered = values - jnp.mean(values, axis=-1, keepdims=True)
    variance = jnp.mean(centered * centered, axis=-1, keepdims=True)
    inverse = lax.rsqrt(variance + norm_epsilon)
    return centered * inverse, inverse


def norm_back(grad, normed, inverse):
    first = jnp.mean(grad, axis=-1, keepdims=True)
    second = jnp.mean(grad * normed, axis=-1, keepdims=True)
    return (grad - first - normed * second) * inverse


def column_sum(values):
    return jnp.sum(values, axis=0, keepdims=True)


def start_loads(cuts, at, parts, whole, semaphores, first_index=0):
    loads = []
    for index, (part, first, rows) in enumerate(cuts, first_index):
        span = pl.ds(pl.multiple_of(at[index] * 16, 16), rows)
        source = parts[part].at[pl.ds(first, rows)]
        loads.append(pltpu.make_async_copy(source, whole.at[span], semaphores.at[index]))
        loads[-1].start()
    return loads


def attention_kernel(
    frames,
    counts,
    tokens,
    cotangent,
    mods,
    bias,
    blocks,
    attn_in,
    parts,
    mixed_low,
    proj_out,
    resid_out,
    mlp_in,
    d_branch,
    d_branch_sum,
    mixed,
    whole,
    semaphores,
):
    rows, width = tokens.shape
    clip = pl.program_id(0)
    loads = [
        pltpu.make_async_copy(blocks.at[at], whole.at[at], semaphores.at[at]) for at in range(4)
    ]

    @pl.when(clip == 0)
    def _():
        for load in loads:
            load.start()

    tile = min(rows, 128)
    count = counts[clip]
    shift_one, scale_one, gate_one = (mods[0, at : at + 1, :] for at in range(3))
    shift_two, scale_two, gate_two = (mods[0, at : at + 1, :] for at in range(3, 6))
    for first in range(0, rows, tile):
        span = slice(first, first + tile)
        normed, _ = norm_parts(wide(tokens[span]))
        attn_in[span] = narrow(normed * (1.0 + scale_one) + shift_one)
        branch_back = narrow(wide(cotangent[span]) * valid_rows(count, tile, frames) * gate_two)
        d_branch[span] = branch_back
        part_sum = column_sum(wide(branch_back))
        d_branch_sum[0] = part_sum if first == 0 else d_branch_sum[0] + part_sum

    @pl.when(clip == 0)
    def _():
        for load in loads:
            load.wait()

    scale = (width // HEADS) ** -0.5
    source = attn_in[...]
    for low, high in column_cuts(width):
        span = slice(low, high)
        query = (dot_nn(source, whole[0, :, span]) + bias[0:1, span]) * scale
        parts[0, :, span], parts[1, :, span] = split_high(query)
        parts[2, :, span], parts[3, :, span] = split_high(dot_nn(source, whole[1, :, span]))
        parts[4, :, span] = narrow(dot_nn(source, whole[2, :, span]) + bias[2:3, span])
    offset = score_offset(count, tile, frames, 1)
    mixed[...] = jnp.zeros_like(mixed)
    for first in range(0, rows, tile):
        span = slice(first, first + tile)
        for low, high, start, stop in head_windows(width):
            lanes = slice(start, stop)
            mask = lane_mask(low, high, stop - start, jnp.bfloat16)
            key_high = parts[2, span, lanes]
            query_high = parts[0, span, lanes] * mask
            scores = dot_nt(query_high, key_high)
            scores += dot_nt(parts[1, span, lanes] * mask, key_high)
            scores += dot_nt(query_high, parts[3, span, lanes]) + offset
            expons = jnp.exp(scores - jnp.max(scores, axis=-1, keepdims=True))
            probs = expons * (1.0 / jnp.sum(expons, axis=-1, keepdims=True))
            out = dot_nn(narrow(probs), parts[4, span, lanes] * mask)
            mixed[span, lanes] += out
    mixed_low[...] = narrow(mixed[...])
    source = mixed_low[...]
    for low, high in column_cuts(width):
        span = slice(low, high)
        proj_out[:, span] = dot_nn(source, whole[3, :, span]) + bias[3:4, span]
    for first in range(0, rows, tile):
        span = slice(first, first + tile)
        resid = wide(tokens[span]) + valid_rows(count, tile, frames) * gate_one * proj_out[span]
        resid_out[span] = resid
        normed, _ = norm_parts(resid)
        mlp_in[span] = narrow(normed * (1.0 + scale_two) + shift_two)


def run_attention(frames, counts, tokens, cotangent, mods, bias, blocks):
    total, width = tokens.shape
    clips = mods.shape[0]
    rows = total // clips
    clip_rows = spec((rows, width), lambda clip: (clip, 0))
    low = jax.ShapeDtypeStruct((total, width), jnp.bfloat16)
    full = jax.ShapeDtypeStruct((total, width), jnp.float32)
    return pl.pallas_call(
        functools.partial(attention_kernel, frames),
        grid=(clips,),
        in_specs=[
            pl.BlockSpec(memory_space=pltpu.SMEM),
            clip_rows,
            clip_rows,
            spec((1,) + mods.shape[1:], lambda clip: (clip, 0, 0)),
            held(bias.shape),
            pl.BlockSpec(memory_space=pl.ANY),
        ],
        out_specs=[
            clip_rows,
            spec((5, rows, width), lambda clip: (0, clip, 0)),
            clip_rows,
            clip_rows,
            clip_rows,
            clip_rows,
            clip_rows,
            spec((1, 1, width), lambda clip: (clip, 0, 0)),
        ],
        out_shape=[
            low,
            jax.ShapeDtypeStruct((5, total, width), jnp.bfloat16),
            low,
            full,
            full,
            low,
            low,
            jax.ShapeDtypeStruct((clips, 1, width), jnp.float32),
        ],
        scratch_shapes=[
            pltpu.VMEM((rows, width), jnp.float32),
            pltpu.VMEM(blocks.shape, jnp.bfloat16),
            pltpu.SemaphoreType.DMA((4,)),
        ],
        compiler_params=pltpu.CompilerParams(vmem_limit_bytes=vmem_bytes),
        cost_estimate=little_cost,
    )(counts, tokens, cotangent, mods, bias, blocks)


def stacked(numbers):
    return jnp.stack([jnp.asarray(number, jnp.int32) for number in numbers])


def start_loads(cuts, at, parts, whole, semaphores):
    for index, (part, first, rows) in enumerate(cuts):
        span = pl.ds(pl.multiple_of(at[index] * 16, 16), rows)
        source = parts[part].at[pl.ds(first, rows)]
        pltpu.make_async_copy(source, whole.at[span], semaphores.at[index]).start()


def wait_loads(groups, at, parts, whole, semaphores):
    index = 0
    for step, cuts in enumerate(groups):
        base = index
        index += len(cuts)

        @pl.when(pl.program_id(0) == step)
        def _(cuts=cuts, base=base):
            for offset, (part, first, rows) in enumerate(cuts):
                span = pl.ds(pl.multiple_of(at[base + offset] * 16, 16), rows)
                source = parts[part].at[pl.ds(first, rows)]
                semaphore = semaphores.at[base + offset]
                pltpu.make_async_copy(source, whole.at[span], semaphore).wait()


def hidden_kernel(cuts, order, starts, mlp_in, bias, *refs):
    whole_out, hidden, slope, whole, semaphores, store_semaphores = refs[-6:]
    pieces = refs[:-6]
    step, steps = pl.program_id(0), pl.num_programs(0)
    width = mlp_in.shape[-1]
    span = pl.ds(pl.multiple_of(order[step] * width, width), width)

    @pl.when(step == 0)
    def _():
        start_loads([cut for group in cuts for cut in group], starts, pieces, whole, semaphores)

    wait_loads(cuts, starts, pieces, whole, semaphores)
    pltpu.make_async_copy(whole.at[span], whole_out.at[span], store_semaphores.at[step]).start()
    root = (2.0 / math.pi) ** 0.5
    source = mlp_in[...]
    block = whole.at[span]
    for low, high in column_cuts(width):
        lanes = slice(low, high)
        pre = dot_nn(source, block[:, lanes]) + bias[0, :, lanes]
        square = pre * pre
        bent = jnp.tanh(root * pre * (1.0 + 0.044715 * square))
        half = 0.5 + 0.5 * bent
        hidden[0, :, lanes] = narrow(pre * half)
        steep = (0.5 * root) * pre * (1.0 + 3 * 0.044715 * square)
        slope[0, :, lanes] = narrow(half + steep * (1.0 - bent * bent))

    @pl.when(step == steps - 1)
    def _():
        for at in range(len(cuts)):
            rows = pl.ds(pl.multiple_of(order[at] * width, width), width)
            pltpu.make_async_copy(
                whole.at[rows], whole_out.at[rows], store_semaphores.at[at]
            ).wait()


def run_hidden(mlp_in, gathered, bias):
    pieces, cuts, starts, order = gathered
    total, width = mlp_in.shape
    count = len(cuts)
    per_block = pl.BlockSpec((1, total, width), lambda at, order, starts: (order[at], 0, 0))
    out = jax.ShapeDtypeStruct((count, total, width), jnp.bfloat16)
    return pl.pallas_call(
        functools.partial(hidden_kernel, cuts),
        grid_spec=pltpu.PrefetchScalarGridSpec(
            num_scalar_prefetch=2,
            grid=(count,),
            in_specs=[
                pl.BlockSpec((total, width), lambda at, order, starts: (0, 0)),
                pl.BlockSpec((1, 1, width), lambda at, order, starts: (order[at], 0, 0)),
            ]
            + [pl.BlockSpec(memory_space=pl.ANY)] * len(pieces),
            out_specs=[pl.BlockSpec(memory_space=pl.ANY), per_block, per_block],
            scratch_shapes=[
                pltpu.VMEM((count * width, width), jnp.bfloat16),
                pltpu.SemaphoreType.DMA((len(starts),)),
                pltpu.SemaphoreType.DMA((count,)),
            ],
        ),
        out_shape=[jax.ShapeDtypeStruct((count * width, width), jnp.bfloat16), out, out],
        compiler_params=pltpu.CompilerParams(vmem_limit_bytes=vmem_bytes),
        cost_estimate=little_cost,
    )(stacked(order), stacked(starts), mlp_in, bias, *pieces)


def branch_kernel(
    frames,
    cuts,
    order,
    starts,
    counts,
    hidden,
    slope,
    d_branch,
    bias,
    gates,
    resid,
    cotangent,
    *refs,
):
    d_pre, d_pre_sum, block_out, d_gate, branch, whole, semaphores = refs[-7:]
    pieces = refs[:-7]
    step, steps = pl.program_id(0), pl.num_programs(0)
    total, width = resid.shape
    clips = gates.shape[0]
    rows = total // clips
    source, back = hidden[0], d_branch[...]

    @pl.when(step == 0)
    def _():
        start_loads([cut for group in cuts for cut in group], starts, pieces, whole, semaphores)
        branch[...] = jnp.zeros_like(branch)

    wait_loads(cuts, starts, pieces, whole, semaphores)
    block = whole.at[pl.ds(pl.multiple_of(order[step] * width, width), width)]
    for low, high in column_cuts(width):
        span = slice(low, high)
        d_hidden = dot_nt(back, block[span, :])
        low_back = narrow(d_hidden * wide(slope[0, :, span]))
        d_pre[0, :, span] = low_back
        d_pre_sum[0, :, span] = column_sum(wide(low_back))
        branch[:, span] += dot_nn(source, block[:, span])

    @pl.when(step == steps - 1)
    def _():
        for clip in range(clips):
            span = slice(clip * rows, (clip + 1) * rows)
            kept = valid_rows(counts[clip], rows, frames) * (branch[span] + bias[...])
            block_out[span] = narrow(resid[span] + gates[clip] * kept)
            d_gate[clip] = column_sum(wide(cotangent[span]) * kept)


def run_branch(frames, counts, hidden, slope, gathered, d_branch, bias, gates, resid, cotangent):
    pieces, cuts, starts, order = gathered
    count, total, width = hidden.shape
    clips = gates.shape[0]

    def all_of(*shape):
        return pl.BlockSpec(shape, lambda at, order, starts: (0,) * len(shape))

    per_block = pl.BlockSpec((1, total, width), lambda at, order, starts: (order[at], 0, 0))
    low = jax.ShapeDtypeStruct((total, width), jnp.bfloat16)
    return pl.pallas_call(
        functools.partial(branch_kernel, frames, cuts),
        grid_spec=pltpu.PrefetchScalarGridSpec(
            num_scalar_prefetch=2,
            grid=(count,),
            in_specs=[
                pl.BlockSpec(memory_space=pltpu.SMEM),
                per_block,
                per_block,
                all_of(total, width),
                all_of(*bias.shape),
                all_of(*gates.shape),
                all_of(total, width),
                all_of(total, width),
            ]
            + [pl.BlockSpec(memory_space=pl.ANY)] * len(pieces),
            out_specs=[
                per_block,
                pl.BlockSpec((1, 1, width), lambda at, order, starts: (order[at], 0, 0)),
                all_of(total, width),
                all_of(clips, 1, width),
            ],
            scratch_shapes=[
                pltpu.VMEM((total, width), jnp.float32),
                pltpu.VMEM((count * width, width), jnp.bfloat16),
                pltpu.SemaphoreType.DMA((len(starts),)),
            ],
        ),
        out_shape=[
            jax.ShapeDtypeStruct((count, total, width), jnp.bfloat16),
            jax.ShapeDtypeStruct((count, 1, width), jnp.float32),
            low,
            jax.ShapeDtypeStruct((clips, 1, width), jnp.float32),
        ],
        compiler_params=pltpu.CompilerParams(vmem_limit_bytes=vmem_bytes),
        cost_estimate=little_cost,
    )(stacked(order), stacked(starts), counts, hidden, slope, d_branch, bias, gates, resid, cotangent, *pieces)


def resid_kernel(
    frames,
    counts,
    d_pre,
    block,
    mods,
    resid,
    cotangent,
    proj,
    d_resid_out,
    d_proj,
    sums,
    total_grad,
):
    step, steps = pl.program_id(0), pl.num_programs(0)
    total, width = resid.shape
    clips = mods.shape[0]
    rows = total // clips
    tile = min(rows, 128)
    source = d_pre[0]

    @pl.when(step == 0)
    def _():
        total_grad[...] = jnp.zeros_like(total_grad)

    for low, high in column_cuts(width):
        span = slice(low, high)
        total_grad[:, span] += dot_nt(source, block[0, span, :])

    @pl.when(step == steps - 1)
    def _():
        for clip in range(clips):
            gate_one, scale_two = mods[clip, 2:3, :], mods[clip, 4:5, :]
            found = [0.0] * 4
            for first in range(clip * rows, (clip + 1) * rows, tile):
                span = slice(first, first + tile)
                grad = total_grad[span]
                normed, inverse = norm_parts(resid[span])
                back = norm_back(grad * (1.0 + scale_two), normed, inverse)
                d_resid = wide(cotangent[span]) + back
                d_resid_out[span] = d_resid
                kept = valid_rows(counts[clip], tile, frames) * d_resid
                low_back = narrow(kept * gate_one)
                d_proj[span] = low_back
                terms = (grad, grad * normed, kept * proj[span], wide(low_back))
                found = [old + column_sum(term) for old, term in zip(found, terms)]
            for at in range(4):
                sums[clip, at : at + 1, :] = found[at]


def run_resid(frames, counts, d_pre, blocks, mods, resid, cotangent, proj):
    count, total, width = d_pre.shape
    clips = mods.shape[0]
    return pl.pallas_call(
        functools.partial(resid_kernel, frames),
        grid=(count,),
        in_specs=[
            pl.BlockSpec(memory_space=pltpu.SMEM),
            spec((1, total, width), lambda at: (at, 0, 0)),
            spec((1, width, width), lambda at: (at, 0, 0)),
            held(mods.shape),
            held((total, width)),
            held((total, width)),
            held((total, width)),
        ],
        out_specs=[held((total, width)), held((total, width)), held((clips, 4, width))],
        out_shape=[
            jax.ShapeDtypeStruct((total, width), jnp.float32),
            jax.ShapeDtypeStruct((total, width), jnp.bfloat16),
            jax.ShapeDtypeStruct((clips, 4, width), jnp.float32),
        ],
        scratch_shapes=[pltpu.VMEM((total, width), jnp.float32)],
        compiler_params=pltpu.CompilerParams(vmem_limit_bytes=vmem_bytes),
        cost_estimate=little_cost,
    )(counts, d_pre, blocks, mods, resid, cotangent, proj)


def attention_back_kernel(
    frames, counts, d_proj, parts, block, d_qkv, sums, d_mixed, d_query, d_key, d_value
):
    rows, width = d_proj.shape
    tile = min(rows, 128)
    count = counts[pl.program_id(0)]
    source = d_proj[...]
    for low, high in column_cuts(width):
        d_mixed[:, low:high] = narrow(dot_nt(source, block[0, low:high, :]))
    scale = (width // HEADS) ** -0.5
    offset = score_offset(count, tile, frames, 0)
    for ref in (d_query, d_key, d_value):
        ref[...] = jnp.zeros_like(ref)
    for first in range(0, rows, tile):
        span = slice(first, first + tile)
        for low, high, start, stop in head_windows(width):
            lanes = slice(start, stop)
            mask = lane_mask(low, high, stop - start, jnp.bfloat16)
            query_high = parts[0, span, lanes] * mask
            key_high = parts[2, span, lanes] * mask
            back = d_mixed[span, lanes] * mask
            scores = dot_nt(key_high, query_high)
            scores += dot_nt(key_high, parts[1, span, lanes])
            scores += dot_nt(parts[3, span, lanes], query_high) + offset
            expons = jnp.exp(scores - jnp.max(scores, axis=0, keepdims=True))
            probs = expons * (1.0 / jnp.sum(expons, axis=0, keepdims=True))
            d_probs = dot_nt(parts[4, span, lanes], back)
            inner = jnp.sum(d_probs * probs, axis=0, keepdims=True)
            d_scores = narrow(probs * (d_probs - inner))
            d_value[span, lanes] += dot_nn(narrow(probs), back)
            d_key[span, lanes] += dot_nn(d_scores, query_high)
            d_query[span, lanes] += dot_tn(d_scores, key_high)
    for at, ref in enumerate((d_query, d_key, d_value)):
        low_back = narrow(ref[...] * scale) if at == 0 else narrow(ref[...])
        d_qkv[at] = low_back
        sums[0, at : at + 1, :] = column_sum(wide(low_back))
    d_qkv[3] = source


def run_attention_back(frames, counts, d_proj, parts, block):
    total, width = d_proj.shape
    clips = counts.shape[0]
    rows = total // clips
    return pl.pallas_call(
        functools.partial(attention_back_kernel, frames),
        grid=(clips,),
        in_specs=[
            pl.BlockSpec(memory_space=pltpu.SMEM),
            spec((rows, width), lambda clip: (clip, 0)),
            spec((5, rows, width), lambda clip: (0, clip, 0)),
            spec((1, width, width), lambda clip: (3, 0, 0), pipeline_mode=pl.Buffered(1)),
        ],
        out_specs=[
            spec((4, rows, width), lambda clip: (0, clip, 0)),
            spec((1, 3, width), lambda clip: (clip, 0, 0)),
        ],
        out_shape=[
            jax.ShapeDtypeStruct((4, total, width), jnp.bfloat16),
            jax.ShapeDtypeStruct((clips, 3, width), jnp.float32),
        ],
        scratch_shapes=[pltpu.VMEM((rows, width), jnp.bfloat16)]
        + [pltpu.VMEM((rows, width), jnp.float32)] * 3,
        compiler_params=pltpu.CompilerParams(vmem_limit_bytes=vmem_bytes),
        cost_estimate=little_cost,
    )(counts, d_proj, parts, block)


def input_kernel(d_qkv, block, mods, tokens, d_resid, input_grad, sums, total_grad):
    step, steps = pl.program_id(0), pl.num_programs(0)
    total, width = tokens.shape
    clips = mods.shape[0]
    rows = total // clips
    tile = min(rows, 128)
    source = d_qkv[0]

    @pl.when(step == 0)
    def _():
        total_grad[...] = jnp.zeros_like(total_grad)

    for low, high in column_cuts(width):
        span = slice(low, high)
        total_grad[:, span] += dot_nt(source, block[0, span, :])

    @pl.when(step == steps - 1)
    def _():
        for clip in range(clips):
            scale_one = mods[clip, 1:2, :]
            found = [0.0] * 2
            for first in range(clip * rows, (clip + 1) * rows, tile):
                span = slice(first, first + tile)
                grad = total_grad[span]
                normed, inverse = norm_parts(wide(tokens[span]))
                back = norm_back(grad * (1.0 + scale_one), normed, inverse)
                input_grad[span] = narrow(d_resid[span] + back)
                terms = (grad, grad * normed)
                found = [old + column_sum(term) for old, term in zip(found, terms)]
            for at in range(2):
                sums[clip, at : at + 1, :] = found[at]


def run_input(d_qkv, blocks, mods, tokens, d_resid):
    total, width = tokens.shape
    clips = mods.shape[0]
    return pl.pallas_call(
        input_kernel,
        grid=(3,),
        in_specs=[
            spec((1, total, width), lambda at: (at, 0, 0)),
            spec((1, width, width), lambda at: (at, 0, 0)),
            held(mods.shape),
            held((total, width)),
            held((total, width)),
        ],
        out_specs=[held((total, width)), held((clips, 2, width))],
        out_shape=[
            jax.ShapeDtypeStruct((total, width), jnp.bfloat16),
            jax.ShapeDtypeStruct((clips, 2, width), jnp.float32),
        ],
        scratch_shapes=[pltpu.VMEM((total, width), jnp.float32)],
        compiler_params=pltpu.CompilerParams(vmem_limit_bytes=vmem_bytes),
        cost_estimate=little_cost,
    )(d_qkv, blocks, mods, tokens, d_resid)


def halves_kernel(left_of, adds, steps, order, side, *refs):
    lefts = refs[: max(left_of) + 1]
    right = refs[len(lefts)]
    turned, total_low = refs[-2:]
    if adds:
        incoming, first_keep, first_out, second_keep, second_out = refs[len(lefts) + 1 : -2]
    else:
        out = refs[-3]
    step = pl.program_id(0)
    block = order[step]
    width = lefts[0].shape[-1]
    half = width // 2

    def pick(left, at):
        lanes = slice(at * half, (at + 1) * half)
        turned[...] = (left[:, lanes] if left.ndim == 2 else left[0, :, lanes]).T

    fresh = (step == 0) | (lefts[0].ndim == 3) | (len(lefts) > 1)
    for at in range(2):
        for index, left in enumerate(lefts):
            of_left = [block == number for number, source in enumerate(left_of) if source == index]

            @pl.when(fresh & (side[0] == at) & functools.reduce(jnp.logical_or, of_left))
            def _(left=left, at=at):
                pick(left, at)

    found = dot_nn(turned[...], right[0] if right.ndim == 3 else right[...])
    if not adds:
        out[0] = narrow(found)
        return
    total_low[...] = narrow(found + wide(incoming[0]))
    for state, target, rows in (
        (steps[0][0], first_keep, slice(0, half // 2)),
        (steps[0][1], first_out, slice(0, half // 2)),
        (steps[1][0], second_keep, slice(half // 2, half)),
        (steps[1][1], second_out, slice(half // 2, half)),
    ):

        @pl.when(functools.reduce(jnp.logical_or, [step == at_step for at_step in state]))
        def _(target=target, rows=rows):
            target[0] = total_low[rows]


def run_halves(lefts, left_of, right, side, at, incoming=None):
    total, width = lefts[0].shape[-2:]
    half = width // 2
    low_bit, high_bit = at % 2, at // 2
    order = stacked([at ^ 3, at ^ 1, at, at ^ 2])
    places = {
        "first_keep": [high_bit, high_bit, high_bit, 1 - high_bit],
        "first_out": [1 - high_bit, high_bit, high_bit, high_bit],
        "second_keep": [1 - low_bit, 1 - low_bit, low_bit, low_bit],
        "second_out": [1 - low_bit, low_bit, low_bit, low_bit],
    }
    steps = (((2, 3), (0, 1)), ((1, 2), (0, 3)))
    adds = incoming is not None
    table = stacked([place for row in places.values() for place in row])

    def block_of(array, *rest):
        if array.ndim == 2:
            return pl.BlockSpec(array.shape, lambda step, order, side, table: (0, 0))
        return pl.BlockSpec((1,) + array.shape[1:], lambda step, order, side, table: (order[step], 0, 0))

    per_block = pl.BlockSpec((1, half, width), lambda step, order, side, table: (order[step], 0, 0))
    operands = list(lefts) + [right]
    in_specs = [block_of(array) for array in operands]
    if adds:
        operands.append(incoming)
        in_specs.append(per_block)
        out_specs = [
            pl.BlockSpec(
                (1, half // 2, width),
                functools.partial(lambda row, step, order, side, table: (table[row * 4 + step], 0, 0), row),
            )
            for row in range(4)
        ]
        out_shape = [jax.ShapeDtypeStruct((2, half // 2, width), jnp.bfloat16)] * 4
    else:
        out_specs = per_block
        out_shape = jax.ShapeDtypeStruct((4, half, width), jnp.bfloat16)

    def body(order, side, table, *refs):
        halves_kernel(left_of, adds, steps, order, side, *refs)

    return pl.pallas_call(
        body,
        grid_spec=pltpu.PrefetchScalarGridSpec(
            num_scalar_prefetch=3,
            grid=(4,),
            in_specs=in_specs,
            out_specs=out_specs,
            scratch_shapes=[
                pltpu.VMEM((half, total), jnp.bfloat16),
                pltpu.VMEM((half, width), jnp.bfloat16),
            ],
        ),
        out_shape=out_shape,
        compiler_params=pltpu.CompilerParams(vmem_limit_bytes=vmem_bytes),
        cost_estimate=little_cost,
    )(order, stacked([side]), table, *operands)


def tie(*values):
    return lax.optimization_barrier(values)


def packed(arrays, tile):
    flat = jnp.concatenate([array.reshape(-1) for array in arrays])
    return jnp.pad(flat, (0, -flat.shape[0] % (tile * 128))).reshape(-1, 128)


def core_swap(array):
    count = lax.axis_size("dp")
    return lax.ppermute(array, "dp", [(at, at ^ 1) for at in range(count)])


def chip_shift(array, step):
    count = lax.axis_size("dp")
    return lax.ppermute(array, "dp", [(at, (at + 2 * step) % count) for at in range(count)])


def chip_swap(array, bits):
    count = lax.axis_size("dp")
    return lax.ppermute(array, "dp", [(at, at ^ (2 * bits)) for at in range(count)])


def rank_swap(array, bits):
    count = lax.axis_size("fsdp")
    return lax.ppermute(array, "fsdp", [(at, at ^ bits) for at in range(count)])


def entry(array, at, axis=0):
    return lax.dynamic_index_in_dim(array, at, axis, keepdims=False)


def place_kernel(cuts, at, *refs):
    parts, whole, held_rows, semaphores = refs[:-3], refs[-3], refs[-2], refs[-1]
    spans, loads, stores = [], [], []
    for index, (part, first, rows) in enumerate(cuts):
        spans.append(pl.ds(pl.multiple_of(at[index] * 16, 16), rows))
        source = parts[part].at[pl.ds(first, rows)]
        loads.append(
            pltpu.make_async_copy(source, held_rows.at[spans[index]], semaphores.at[0, index])
        )
        loads[index].start()
    for index, span in enumerate(spans):
        loads[index].wait()
        stores.append(
            pltpu.make_async_copy(held_rows.at[span], whole.at[span], semaphores.at[1, index])
        )
        stores[index].start()
    for store in stores:
        store.wait()


def place(parts, cuts, starts, rows):
    width = parts[0].shape[-1]
    dtype = parts[0].dtype
    return pl.pallas_call(
        functools.partial(place_kernel, cuts),
        in_specs=[pl.BlockSpec(memory_space=pltpu.SMEM)]
        + [pl.BlockSpec(memory_space=pl.ANY)] * len(parts),
        out_specs=pl.BlockSpec(memory_space=pl.ANY),
        out_shape=jax.ShapeDtypeStruct((rows, width), dtype),
        scratch_shapes=[
            pltpu.VMEM((rows, width), dtype),
            pltpu.SemaphoreType.DMA((2, len(cuts))),
        ],
        compiler_params=pltpu.CompilerParams(vmem_limit_bytes=vmem_bytes),
        cost_estimate=little_cost,
    )(stacked(starts), *parts)


def own_rows(parts, group):
    ranks, at = lax.axis_size("fsdp"), lax.axis_index("fsdp")
    shares = ranks // group
    count, _, row_part, col_part = parts.shape
    chunk = row_part // shares
    split = parts.reshape(count, group, shares, chunk, col_part).transpose(1, 2, 0, 3, 4)
    split = split.reshape(ranks, count, chunk, col_part)
    if shares > 1:
        moved = lax.all_to_all(split, "fsdp", 0, 0, tiled=True)
        (moved,) = yield (moved,)
        yield moved.transpose(1, 2, 0, 3).reshape(count, chunk, ranks * col_part)
        return
    panels = [entry(split, at)]
    panels += [rank_swap(entry(split, at ^ bits), bits) for bits in range(1, ranks)]
    panels = yield tuple(panels)
    placed = [
        lax.select_n(at, *[panels[panel ^ index] for index in range(ranks)])
        for panel in range(ranks)
    ]
    yield jnp.concatenate(placed, axis=2)


def shard_rows(split, group):
    ranks, count, chunk, col_part = split.shape
    shares = ranks // group
    moved = lax.all_to_all(split, "fsdp", 0, 0, tiled=True)
    moved = moved.reshape(group, shares, count, chunk, col_part).transpose(2, 0, 1, 3, 4)
    return moved.reshape(count, group, shares * chunk, col_part)


def gather_blocks(rows, group):
    ranks, dp_count = lax.axis_size("fsdp"), lax.axis_size("dp")
    shares = ranks // group
    chunk, total = rows.shape
    all_rows = lax.all_gather(rows, ("fsdp", "dp"), axis=0, tiled=True)
    if shares > 1:
        all_rows = all_rows.reshape(group, shares, dp_count, chunk, total).transpose(0, 2, 1, 3, 4)
    return all_rows.reshape(group, total, total)


def join_line(found):
    chips, chip = lax.axis_size("dp") // 2, lax.axis_index("dp") // 2
    chunk = found[0].shape[0]
    starts = [(chip - step) % chips * (chunk // 16) for step in range(chips)]
    return place(found, [(step, 0, chunk) for step in range(chips)], starts, chips * chunk)


def gather_second(rows, group):
    ranks, at = lax.axis_size("fsdp"), lax.axis_index("fsdp")
    total = rows.shape[-1]
    if ranks != group:
        blocks = gather_blocks(rows, group).reshape(group * total, total)
        for _ in range(4):
            (blocks,) = yield (blocks,)
        cuts = [[(0, index * total, total)] for index in range(group)]
        yield [blocks], cuts, [index * (total // 16) for index in range(group)], range(group)
        return
    chips = lax.axis_size("dp") // 2
    core = lax.axis_index("dp") % 2
    chunk, half = rows.shape[0], total // 2
    others = yield tuple(chip_shift(rows, step) for step in range(1, chips))
    line = join_line([rows, *others])
    cuts = [(side, step * chunk, chunk) for side in range(2) for step in range(chips)]
    starts = [
        (2 * step + side) * (chunk // 16) for side in (core, 1 - core) for step in range(chips)
    ]
    (own,) = yield (place([line, core_swap(line)], cuts, starts, total),)
    share = lax.dynamic_slice_in_dim(own, core * half, half, 0)
    low, high = yield (rank_swap(share, 1), rank_swap(share, 2))
    quarter = half // 2
    low_other, high_other = core_swap(low), core_swap(high)
    last = yield (rank_swap(high[:quarter], 1), rank_swap(low[quarter:], 2))
    parts = [own, low, low_other, high, high_other, *last, *[core_swap(part) for part in last]]
    cuts = [[(0, 0, total)], [(1, 0, half), (2, 0, half)], [(3, 0, half), (4, 0, half)]]
    cuts.append([(5 + index, 0, quarter) for index in range(4)])
    starts = [at * (total // 16)]
    for bits in (1, 2):
        starts += [((at ^ bits) * 2 + side) * (half // 16) for side in (core, 1 - core)]
    for side in (core, 1 - core):
        first = ((at ^ 3) * 2 + side) * (half // 16)
        starts += [first, first + quarter // 16]
    yield parts, cuts, starts, [at ^ bits for bits in range(ranks)]


def gather_own(rows, group):
    ranks = lax.axis_size("fsdp")
    shares = ranks // group
    if shares > 1:
        sets = [[share + shares * block for share in range(shares)] for block in range(group)]
        rows = lax.all_gather(rows, "fsdp", axis=1, tiled=True, axis_index_groups=sets)
    return lax.all_gather(rows, "dp", axis=1, tiled=True)


def sum_blocks(lefts, left_of, right, group):
    ranks, dp_count = lax.axis_size("fsdp"), lax.axis_size("dp")
    shares = ranks // group
    total = lefts[0].shape[-1]
    if shares > 1:
        blocks = jnp.stack(
            [
                narrow(
                    fast_dot(
                        "tr,te->re",
                        lefts[index] if lefts[index].ndim == 2 else lefts[index][block],
                        right if right.ndim == 2 else right[block],
                    )
                )
                for block, index in enumerate(left_of)
            ]
        )
        chunk = total // (dp_count * shares)
        blocks = blocks.reshape(group, dp_count, shares, chunk, -1).transpose(0, 2, 1, 3, 4)
        rows = lax.psum_scatter(
            blocks.reshape(group * total, -1), ("fsdp", "dp"), scatter_dimension=0, tiled=True
        )
        for _ in range(7):
            (rows,) = yield (rows,)
        yield gather_own(rows[None], group)[0]
        return
    chips, half = dp_count // 2, total // 2
    chunk = half // chips
    at = lax.axis_index("fsdp")
    core, chip = lax.axis_index("dp") % 2, lax.axis_index("dp") // 2
    low_bit, high_bit = at % 2, at // 2
    (away,) = yield (run_halves(lefts, left_of, right, 1 - core, at),)
    (away_in,) = yield (core_swap(away),)
    first, first_out, second, second_out = run_halves(lefts, left_of, right, core, at, away_in)
    first_out, second_out = yield (first_out, second_out)
    first_in, second_in = yield (rank_swap(first_out, 1), rank_swap(second_out, 2))
    first = narrow(wide(first) + wide(first_in)).reshape(2, chips // 2, chunk, -1)
    second = narrow(wide(second) + wide(second_in)).reshape(2, chips // 2, chunk, -1)
    first_in = rank_swap(entry(first, 1 - high_bit), 2)
    second_in = rank_swap(entry(second, 1 - low_bit), 1)
    first_in, second_in = yield (first_in, second_in)
    first = narrow(wide(entry(first, high_bit)) + wide(first_in))
    second = narrow(wide(entry(second, low_bit)) + wide(second_in))
    line = jnp.concatenate([first, second])
    step = 1
    while step < chips:
        bit = chip // step % 2
        line = line.reshape(-1, 2, *line.shape[1:])
        (line_in,) = yield (chip_swap(entry(line, 1 - bit, 1), step),)
        line = narrow(wide(entry(line, bit, 1)) + wide(line_in))
        step *= 2
    yield lax.all_gather(line[0], "dp", axis=0, tiled=True)


def fast_dot(subscripts, left, right):
    return jnp.einsum(subscripts, left, right, preferred_element_type=jnp.float32)


def products_kernel(chips, at, gathered, left_root, right_root, out, whole, semaphores):
    chunk, width = left_root.shape[1:]
    ranks = out.shape[0]
    copies = []
    for index in range(2 * chips):
        first = (index % 2 * chips + index // 2) * chunk
        copies.append(
            pltpu.make_async_copy(
                gathered.at[pl.ds(index * chunk, chunk)],
                whole.at[pl.ds(first, chunk)],
                semaphores.at[index],
            )
        )
        copies[-1].start()
    for copy in copies:
        copy.wait()
    first = at[0] * 16
    grad = whole[...]
    picked = lax.broadcasted_iota(jnp.int32, (width, chunk), 0) - first
    picked = picked == lax.broadcasted_iota(jnp.int32, (width, chunk), 1)
    own_columns = narrow(dot_nn(grad, narrow(picked.astype(jnp.float32))))
    side_high, side_low = split_high(dot_nn(left_root[0], grad))
    right = right_root[0]
    precond = dot_nn(side_high, right) + dot_nn(side_low, right)
    outer = dot_nt(whole[pl.ds(pl.multiple_of(first, 16), chunk), :], grad)
    inner = dot_tn(own_columns, grad)
    for at_out, product in enumerate((precond, outer, inner)):
        low = narrow(product)
        for rank in range(ranks):
            span = slice(rank * (width // ranks), (rank + 1) * (width // ranks))
            out[rank, at_out] = low[:, span]


def owned_step(whole, left_roots, right_roots, index, group):
    ranks, dp_count = lax.axis_size("fsdp"), lax.axis_size("dp")
    shares = ranks // group
    chunk, total = left_roots.shape[1:]
    col_part = total // ranks
    first = lax.axis_index("dp") * (chunk * shares) + lax.axis_index("fsdp") % shares * chunk
    if shares == 1:
        return pl.pallas_call(
            functools.partial(products_kernel, dp_count // 2),
            in_specs=[
                pl.BlockSpec(memory_space=pltpu.SMEM),
                pl.BlockSpec(memory_space=pl.ANY),
                pl.BlockSpec((1, chunk, total), lambda step: (index, 0, 0)),
                pl.BlockSpec((1, total, total), lambda step: (index, 0, 0)),
            ],
            out_specs=pl.BlockSpec((ranks, 3, chunk, col_part), lambda step: (0, 0, 0, 0)),
            grid=(1,),
            out_shape=jax.ShapeDtypeStruct((ranks, 3, chunk, col_part), jnp.bfloat16),
            scratch_shapes=[
                pltpu.VMEM((total, total), jnp.bfloat16),
                pltpu.SemaphoreType.DMA((dp_count,)),
            ],
            compiler_params=pltpu.CompilerParams(vmem_limit_bytes=vmem_bytes),
            cost_estimate=little_cost,
        )((first // 16)[None], whole, left_roots, right_roots)
    left_root, right_root = left_roots[index], right_roots[index]
    grad_rows = lax.dynamic_slice_in_dim(whole, first, chunk, 0)
    own_columns = lax.dynamic_slice_in_dim(whole, first, chunk, 1)
    outer = fast_dot("rk,jk->rj", grad_rows, whole)
    inner = fast_dot("kr,kj->rj", own_columns, whole)
    side_high, side_low = split_high(fast_dot("rk,kj->rj", left_root, whole))
    precond = fast_dot("rk,kj->rj", side_high, right_root) + fast_dot(
        "rk,kj->rj", side_low, right_root
    )
    products = narrow(jnp.stack([precond, outer, inner]))
    return products.reshape(3, chunk, ranks, col_part).transpose(2, 0, 1, 3)


def per_device(
    tokens,
    conditioning,
    frame_counts,
    cotangent,
    weights,
    biases,
    momentum,
    left_stats,
    right_stats,
    left_roots,
    right_roots,
    bias_moment,
    bias_second,
):
    group = 4
    mod_count = 6
    clip_count, pos_count, frames, width = tokens.shape
    token_count = clip_count * pos_count * frames
    block_count, row_part, col_part = weights.shape
    dp_count, ranks = lax.axis_size("dp"), lax.axis_size("fsdp")
    dp_at, rank_at = lax.axis_index("dp"), lax.axis_index("fsdp")
    all_clips = clip_count * dp_count
    bias_part = biases.shape[0]
    stream = tokens.reshape(token_count, width)
    grad_out = cotangent.reshape(token_count, width)
    low_weights = narrow(weights).reshape(block_count, row_part, col_part)
    shards = low_weights[mod_count:].reshape(-1, group, row_part, col_part)

    weight_rows = own_rows(shards, group)
    weight_panels = next(weight_rows)
    cond_low = narrow(jax.nn.silu(conditioning))
    first_parts = lax.all_gather(packed([cond_low, narrow(biases)], 16), "dp", axis=0, tiled=True)
    weight_panels, first_parts = tie(weight_panels, first_parts)
    attn_rows, one_rows, two_rows = weight_rows.send(weight_panels)
    attn_w = gather_blocks(attn_rows, group)
    two_w = gather_blocks(two_rows, group).reshape(group * width, width)
    two_gathered = (
        [two_w],
        [[(0, index * width, width)] for index in range(group)],
        [index * (width // 16) for index in range(group)],
        range(group),
    )

    first_parts = first_parts.reshape(dp_count, -1)
    cond_all = first_parts[:, : clip_count * width].reshape(all_clips, width)
    bias_rows = wide(first_parts[:, clip_count * width : clip_count * width + bias_part])
    cond_rows = lax.dynamic_slice_in_dim(cond_all, dp_at * row_part, row_part, 1)
    cond_cols = wide(lax.dynamic_slice_in_dim(cond_all, rank_at * col_part, col_part, 1))
    mod_parts = fast_dot("cr,jre->cje", cond_rows, low_weights[:mod_count])
    mod_parts = lax.all_to_all(mod_parts, "dp", 0, 0, tiled=True)
    mod_parts, one_rows = tie(mod_parts, one_rows)
    one_steps = gather_second(one_rows, group)
    one_parts = next(one_steps)
    mod_cols = jnp.sum(mod_parts.reshape(dp_count, clip_count, mod_count, col_part), axis=0)
    left_cond = jnp.einsum("jrk,ck->jrc", left_roots[:mod_count], cond_cols, precision=precise)
    mod_size, bias_size = mod_cols.size, dp_count * bias_part
    second_parts = lax.all_gather(
        packed([mod_cols, bias_rows, left_cond], 8), "fsdp", axis=0, tiled=True
    )
    second_parts, one_parts = tie(second_parts, one_parts)
    roots = jnp.stack([narrow(left_roots[mod_count:]), narrow(right_roots[mod_count:])])
    one_parts, attn_w, roots = tie(one_steps.send(one_parts), attn_w, roots)
    one_parts = one_steps.send(one_parts)
    second_parts = second_parts.reshape(ranks, -1)
    mods = second_parts[:, :mod_size].reshape(ranks, clip_count, mod_count, col_part)
    mods = mods.transpose(1, 2, 0, 3).reshape(clip_count, mod_count, width)
    bias_all = second_parts[:, mod_size : mod_size + bias_size].reshape(ranks, dp_count, bias_part)
    bias_all = bias_all.transpose(1, 0, 2).reshape(-1, width)
    left_size = mod_size + bias_size + left_cond.size
    left_cond = jnp.sum(second_parts[:, mod_size + bias_size : left_size], axis=0)
    left_cond = left_cond.reshape(mod_count, row_part, all_clips)
    mods = mods + bias_all[:mod_count]
    bias_table = jnp.concatenate(
        [bias_all[6:7], jnp.zeros((1, width), jnp.float32), bias_all[7:14]]
    )

    attn_in, parts, mixed, proj, resid, mlp_in, d_branch, d_branch_sums = run_attention(
        frames, frame_counts, stream, grad_out, mods, bias_table, attn_w
    )
    mlp_in, one_parts = tie(mlp_in, one_parts)
    one_parts = one_steps.send(one_parts)
    one_w, hidden, slope = run_hidden(mlp_in, one_steps.send(one_parts), bias_table[4:8, None])
    one_w = one_w.reshape(group, width, width)

    two_steps = sum_blocks([hidden], [0] * group, d_branch, group)
    two_parts = next(two_steps)
    hidden, two_parts, roots = tie(hidden, two_parts, roots)
    two_parts = two_steps.send(two_parts)
    root_rows = own_rows(roots.reshape(-1, group, row_part, col_part), group)
    root_panels = next(root_rows)
    d_pre, d_pre_sums, block_out, d_gate_two = run_branch(
        frames,
        frame_counts,
        hidden,
        slope,
        two_gathered,
        d_branch,
        bias_table[8:9],
        mods[:, 5:6],
        resid,
        grad_out,
    )
    d_pre, root_panels = tie(d_pre, root_panels)
    root_rows = root_rows.send(root_panels)
    d_pre, two_parts, root_rows = tie(d_pre, two_parts, root_rows)
    two_parts = two_steps.send(two_parts)
    d_pre, two_parts = tie(d_pre, two_parts)
    two_parts = two_steps.send(two_parts)
    right_wholes = gather_own(root_rows[3:], group)
    one_steps = sum_blocks([mlp_in], [0] * group, d_pre, group)
    one_parts = next(one_steps)
    d_pre, one_parts = tie(d_pre, one_parts)
    one_parts = one_steps.send(one_parts)
    d_resid, d_proj, resid_sums = run_resid(
        frames, frame_counts, d_pre, one_w, mods, resid, grad_out, proj
    )
    d_proj, one_parts = tie(d_proj, one_parts)
    one_parts = one_steps.send(one_parts)
    d_proj, one_parts, two_parts = tie(d_proj, one_parts, two_parts)
    two_parts = two_steps.send(two_parts)
    one_parts = one_steps.send(one_parts)
    d_heads, head_sums = run_attention_back(frames, frame_counts, d_proj, parts, attn_w)
    d_heads, two_parts, one_parts, right_wholes = tie(
        d_heads, two_parts, one_parts, right_wholes
    )
    two_parts = two_steps.send(two_parts)
    one_parts = one_steps.send(one_parts)
    attn_steps = sum_blocks([attn_in, mixed], [0, 0, 0, 1], d_heads, group)
    attn_parts = next(attn_steps)
    d_heads, attn_parts = tie(d_heads, attn_parts)
    attn_parts = attn_steps.send(attn_parts)
    input_grad, input_sums = run_input(d_heads, attn_w, mods, stream, d_resid)
    input_sums, attn_parts, two_parts, one_parts = tie(
        input_sums, attn_parts, two_parts, one_parts
    )
    two_parts = two_steps.send(two_parts)
    one_parts = one_steps.send(one_parts)

    d_mods = jnp.stack(
        [
            input_sums[:, 0],
            input_sums[:, 1],
            resid_sums[:, 2],
            resid_sums[:, 0],
            resid_sums[:, 1],
            d_gate_two[:, 0],
        ],
        axis=1,
    )
    head_sums = jnp.sum(head_sums, axis=0)
    grad_bias = jnp.concatenate(
        [
            jnp.sum(d_mods, axis=0),
            head_sums[0:1],
            head_sums[2:3],
            jnp.sum(resid_sums[:, 3], axis=0)[None],
            d_pre_sums[:, 0],
            jnp.sum(d_branch_sums, axis=0),
        ]
    )
    to_ranks = jnp.concatenate(
        [
            d_mods.reshape(clip_count, mod_count, ranks, col_part)
            .transpose(2, 0, 1, 3)
            .reshape(ranks, mod_size),
            grad_bias.reshape(dp_count, ranks, bias_part)
            .transpose(1, 0, 2)
            .reshape(ranks, bias_size),
        ],
        axis=1,
    )
    rank_sums = lax.all_to_all(to_ranks, "fsdp", 0, 0, tiled=True)
    rank_sums, attn_parts, two_parts = tie(rank_sums, attn_parts, two_parts)
    whole_two = two_steps.send(two_parts)
    attn_parts = attn_steps.send(attn_parts)
    rank_sums = jnp.sum(rank_sums, axis=0)
    to_rows = jnp.concatenate(
        [
            jnp.broadcast_to(rank_sums[None, :mod_size], (dp_count, mod_size)),
            rank_sums[mod_size:].reshape(dp_count, bias_part),
        ],
        axis=1,
    )
    to_rows, attn_parts, one_parts = tie(to_rows, attn_parts, one_parts)
    attn_parts = attn_steps.send(attn_parts)
    one_parts = one_steps.send(one_parts)
    from_rows = lax.all_to_all(to_rows, "dp", 0, 0, tiled=True)
    from_rows, attn_parts, one_parts = tie(from_rows, attn_parts, one_parts)
    attn_parts = attn_steps.send(attn_parts)
    whole_one = one_steps.send(one_parts)
    bias_grad = jnp.sum(from_rows[:, mod_size:], axis=0)
    mod_grad_cols = from_rows[:, :mod_size].reshape(all_clips, mod_count, col_part)
    mod_grad = lax.all_gather(packed([mod_grad_cols], 8), "fsdp", axis=0, tiled=True)
    mod_grad, attn_parts = tie(mod_grad, attn_parts)
    attn_parts = attn_steps.send(attn_parts)
    products_two = owned_step(whole_two, root_rows, right_wholes, 2, group)
    products_two, attn_parts = tie(products_two, attn_parts)
    attn_parts = attn_steps.send(attn_parts)
    back_two = shard_rows(products_two, group)
    products_one = owned_step(whole_one, root_rows, right_wholes, 1, group)
    mod_grad, back_two, attn_parts = tie(mod_grad, back_two, attn_parts)
    whole_attn = attn_steps.send(attn_parts)
    back_one = shard_rows(products_one, group)
    mod_grad = mod_grad.reshape(ranks, -1)[:, : mod_grad_cols.size]
    mod_grad = mod_grad.reshape(ranks, all_clips, mod_count, col_part).transpose(1, 2, 0, 3)
    mod_grad = mod_grad.reshape(all_clips, mod_count, width)

    mod_grad_rows = lax.dynamic_slice_in_dim(mod_grad, dp_at * row_part, row_part, 2)
    right_parts = jnp.einsum(
        "cjk,jke->cje", mod_grad_rows, right_roots[:mod_count], precision=precise
    )
    cond_wide = wide(cond_all)
    cond_row_wide = wide(cond_rows)
    mod_gram = jnp.einsum("cjk,bjk->jcb", mod_grad, mod_grad, precision=precise)
    cond_gram = jnp.einsum("ck,bk->cb", cond_wide, cond_wide, precision=precise)
    mod_side = jnp.einsum("jcb,be->jce", mod_gram, cond_cols, precision=precise)
    ada_left = jnp.einsum("cr,jce->jre", cond_row_wide, mod_side, precision=precise)
    cond_side = jnp.einsum("cb,bje->jce", cond_gram, mod_grad_cols, precision=precise)
    ada_right = jnp.einsum("cjr,jce->jre", mod_grad_rows, cond_side, precision=precise)

    right_parts = lax.all_gather(packed([right_parts], 8), "dp", axis=0, tiled=True)
    mod_right = jnp.sum(right_parts.reshape(dp_count, -1), axis=0)[: mod_grad_cols.size]
    mod_right = mod_right.reshape(all_clips, mod_count, col_part)
    ada_pre = jnp.einsum("jrc,cje->jre", left_cond, mod_right, precision=precise)
    whole_attn, back_one = tie(whole_attn, back_one)
    back_attn = shard_rows(owned_step(whole_attn, root_rows, right_wholes, 0, group), group)

    def joined(at, ada):
        return jnp.concatenate([ada, wide(back_attn[at]), wide(back_one[at]), wide(back_two[at])])

    precond = joined(0, ada_pre)
    left_new = stat_decay * left_stats + (1.0 - stat_decay) * joined(1, ada_left)
    right_new = stat_decay * right_stats + (1.0 - stat_decay) * joined(2, ada_right)
    momentum_new = moment_decay * momentum + precond
    weights_new = weights - weight_rate * momentum_new
    weights_copy = weights_new.astype(jnp.bfloat16)
    bias_second_new = stat_decay * bias_second + (1.0 - stat_decay) * bias_grad * bias_grad
    bias_moment_new = moment_decay * bias_moment + bias_grad * lax.rsqrt(
        bias_second_new + diag_epsilon
    )
    biases_new = biases - bias_rate * bias_moment_new
    return (
        block_out.reshape(tokens.shape),
        input_grad.reshape(tokens.shape),
        left_new,
        right_new,
        momentum_new,
        weights_new,
        weights_copy,
        bias_moment_new,
        bias_second_new,
        biases_new,
    )


def solution(mesh):
    placed = (
        P("dp", "fsdp", None, None),
        P("dp", None),
        P("dp"),
        P("dp", "fsdp", None, None),
        P(None, "dp", "fsdp"),
        P(("dp", "fsdp")),
        P(None, "dp", "fsdp"),
        P(None, "dp", "fsdp"),
        P(None, "dp", "fsdp"),
        P(None, "dp", "fsdp"),
        P(None, "dp", "fsdp"),
        P(("dp", "fsdp")),
        P(("dp", "fsdp")),
    )
    return jax.shard_map(
        per_device,
        mesh=mesh,
        in_specs=placed,
        out_specs=(
            P("dp", "fsdp", None, None),
            P("dp", "fsdp", None, None),
            P(None, "dp", "fsdp"),
            P(None, "dp", "fsdp"),
            P(None, "dp", "fsdp"),
            P(None, "dp", "fsdp"),
            P(None, "dp", "fsdp"),
            P(("dp", "fsdp")),
            P(("dp", "fsdp")),
            P(("dp", "fsdp")),
        ),
        check_vma=False,
    )
```

```python
import functools
import math

import jax
import jax.numpy as jnp
from jax import lax
from jax.experimental import pallas as pl
from jax.experimental.pallas import tpu as pltpu
from jax.sharding import PartitionSpec as P

HEADS = 16


precise = lax.Precision.HIGHEST
norm_epsilon = 1e-06
masked_score = -1e30
stat_decay = 0.5
moment_decay = 0.9
weight_rate = 0.7
bias_rate = 0.1
diag_epsilon = 1e-08
vmem_bytes = 50 * 2**20
little_cost = pl.CostEstimate(flops=1024, bytes_accessed=1024, transcendentals=0)


def narrow(array):
    return array.astype(jnp.bfloat16)


def wide(array):
    return array.astype(jnp.float32)


def spec(shape, index_map, **keywords):
    return pl.BlockSpec(shape, index_map, **keywords)


def held(shape):
    return pl.BlockSpec(shape, lambda step: (0,) * len(shape), pipeline_mode=pl.Buffered(1))


def column_cuts(total):
    cuts, at = [], 0
    while at < total:
        cuts.append((at, min(total, at + 256)))
        at += 256
    return cuts


def dot_nn(left, right):
    return lax.dot_general(left, right, (((1,), (0,)), ((), ())), preferred_element_type=jnp.float32)


def dot_nt(left, right):
    return lax.dot_general(left, right, (((1,), (1,)), ((), ())), preferred_element_type=jnp.float32)


def dot_tn(left, right):
    return lax.dot_general(left, right, (((0,), (0,)), ((), ())), preferred_element_type=jnp.float32)


def split_high(values):
    high = narrow(values)
    return high, narrow(values - wide(high))


def valid_rows(count, rows, frames):
    at = lax.broadcasted_iota(jnp.int32, (rows, 1), 0)
    return (lax.rem(at, frames) < count).astype(jnp.float32)


def score_offset(count, size, frames, key_axis):
    first = lax.broadcasted_iota(jnp.int32, (size, size), 0)
    second = lax.broadcasted_iota(jnp.int32, (size, size), 1)
    key = second if key_axis == 1 else first
    met = (lax.div(first, frames) == lax.div(second, frames)) & (lax.rem(key, frames) < count)
    return jnp.where(met, 0.0, masked_score)


def head_windows(width):
    size = width // HEADS
    windows = []
    for head in range(HEADS):
        low, high = head * size, (head + 1) * size
        start = low // 128 * 128
        stop = min(width, -(-high // 128) * 128)
        windows.append((low - start, high - start, start, stop))
    return windows


def lane_mask(low, high, count, dtype):
    lanes = lax.broadcasted_iota(jnp.int32, (1, count), 1)
    return ((lanes >= low) & (lanes < high)).astype(jnp.float32).astype(dtype)


def norm_parts(values):
    centered = values - jnp.mean(values, axis=-1, keepdims=True)
    variance = jnp.mean(centered * centered, axis=-1, keepdims=True)
    inverse = lax.rsqrt(variance + norm_epsilon)
    return centered * inverse, inverse


def norm_back(grad, normed, inverse):
    first = jnp.mean(grad, axis=-1, keepdims=True)
    second = jnp.mean(grad * normed, axis=-1, keepdims=True)
    return (grad - first - normed * second) * inverse


def column_sum(values):
    return jnp.sum(values, axis=0, keepdims=True)


def start_loads(cuts, at, parts, whole, semaphores, first_index=0):
    loads = []
    for index, (part, first, rows) in enumerate(cuts, first_index):
        span = pl.ds(pl.multiple_of(at[index] * 16, 16), rows)
        source = parts[part].at[pl.ds(first, rows)]
        loads.append(pltpu.make_async_copy(source, whole.at[span], semaphores.at[index]))
        loads[-1].start()
    return loads


def attention_kernel(
    frames,
    counts,
    tokens,
    cotangent,
    mods,
    bias,
    blocks,
    attn_in,
    parts,
    mixed_low,
    proj_out,
    resid_out,
    mlp_in,
    d_branch,
    d_branch_sum,
    mixed,
    whole,
    semaphores,
):
    rows, width = tokens.shape
    clip = pl.program_id(0)
    loads = [
        pltpu.make_async_copy(blocks.at[at], whole.at[at], semaphores.at[at]) for at in range(4)
    ]

    @pl.when(clip == 0)
    def _():
        for load in loads:
            load.start()

    tile = min(rows, 128)
    count = counts[clip]
    shift_one, scale_one, gate_one = (mods[0, at : at + 1, :] for at in range(3))
    shift_two, scale_two, gate_two = (mods[0, at : at + 1, :] for at in range(3, 6))
    for first in range(0, rows, tile):
        span = slice(first, first + tile)
        normed, _ = norm_parts(wide(tokens[span]))
        attn_in[span] = narrow(normed * (1.0 + scale_one) + shift_one)
        branch_back = narrow(wide(cotangent[span]) * valid_rows(count, tile, frames) * gate_two)
        d_branch[span] = branch_back
        part_sum = column_sum(wide(branch_back))
        d_branch_sum[0] = part_sum if first == 0 else d_branch_sum[0] + part_sum

    @pl.when(clip == 0)
    def _():
        for load in loads:
            load.wait()

    scale = (width // HEADS) ** -0.5
    source = attn_in[...]
    for low, high in column_cuts(width):
        span = slice(low, high)
        query = (dot_nn(source, whole[0, :, span]) + bias[0:1, span]) * scale
        parts[0, :, span], parts[1, :, span] = split_high(query)
        parts[2, :, span], parts[3, :, span] = split_high(dot_nn(source, whole[1, :, span]))
        parts[4, :, span] = narrow(dot_nn(source, whole[2, :, span]) + bias[2:3, span])
    offset = score_offset(count, tile, frames, 1)
    mixed[...] = jnp.zeros_like(mixed)
    for first in range(0, rows, tile):
        span = slice(first, first + tile)
        for low, high, start, stop in head_windows(width):
            lanes = slice(start, stop)
            mask = lane_mask(low, high, stop - start, jnp.bfloat16)
            key_high = parts[2, span, lanes]
            query_high = parts[0, span, lanes] * mask
            scores = dot_nt(query_high, key_high)
            scores += dot_nt(parts[1, span, lanes] * mask, key_high)
            scores += dot_nt(query_high, parts[3, span, lanes]) + offset
            expons = jnp.exp(scores - jnp.max(scores, axis=-1, keepdims=True))
            probs = expons * (1.0 / jnp.sum(expons, axis=-1, keepdims=True))
            out = dot_nn(narrow(probs), parts[4, span, lanes] * mask)
            mixed[span, lanes] += out
    mixed_low[...] = narrow(mixed[...])
    source = mixed_low[...]
    for low, high in column_cuts(width):
        span = slice(low, high)
        proj_out[:, span] = dot_nn(source, whole[3, :, span]) + bias[3:4, span]
    for first in range(0, rows, tile):
        span = slice(first, first + tile)
        resid = wide(tokens[span]) + valid_rows(count, tile, frames) * gate_one * proj_out[span]
        resid_out[span] = resid
        normed, _ = norm_parts(resid)
        mlp_in[span] = narrow(normed * (1.0 + scale_two) + shift_two)


def run_attention(frames, counts, tokens, cotangent, mods, bias, blocks):
    total, width = tokens.shape
    clips = mods.shape[0]
    rows = total // clips
    clip_rows = spec((rows, width), lambda clip: (clip, 0))
    low = jax.ShapeDtypeStruct((total, width), jnp.bfloat16)
    full = jax.ShapeDtypeStruct((total, width), jnp.float32)
    return pl.pallas_call(
        functools.partial(attention_kernel, frames),
        grid=(clips,),
        in_specs=[
            pl.BlockSpec(memory_space=pltpu.SMEM),
            clip_rows,
            clip_rows,
            spec((1,) + mods.shape[1:], lambda clip: (clip, 0, 0)),
            held(bias.shape),
            pl.BlockSpec(memory_space=pl.ANY),
        ],
        out_specs=[
            clip_rows,
            spec((5, rows, width), lambda clip: (0, clip, 0)),
            clip_rows,
            clip_rows,
            clip_rows,
            clip_rows,
            clip_rows,
            spec((1, 1, width), lambda clip: (clip, 0, 0)),
        ],
        out_shape=[
            low,
            jax.ShapeDtypeStruct((5, total, width), jnp.bfloat16),
            low,
            full,
            full,
            low,
            low,
            jax.ShapeDtypeStruct((clips, 1, width), jnp.float32),
        ],
        scratch_shapes=[
            pltpu.VMEM((rows, width), jnp.float32),
            pltpu.VMEM(blocks.shape, jnp.bfloat16),
            pltpu.SemaphoreType.DMA((4,)),
        ],
        compiler_params=pltpu.CompilerParams(vmem_limit_bytes=vmem_bytes),
        cost_estimate=little_cost,
    )(counts, tokens, cotangent, mods, bias, blocks)


def stacked(numbers):
    return jnp.stack([jnp.asarray(number, jnp.int32) for number in numbers])


def start_loads(cuts, at, parts, whole, semaphores):
    for index, (part, first, rows) in enumerate(cuts):
        span = pl.ds(pl.multiple_of(at[index] * 16, 16), rows)
        source = parts[part].at[pl.ds(first, rows)]
        pltpu.make_async_copy(source, whole.at[span], semaphores.at[index]).start()


def wait_loads(groups, at, parts, whole, semaphores):
    index = 0
    for step, cuts in enumerate(groups):
        base = index
        index += len(cuts)

        @pl.when(pl.program_id(0) == step)
        def _(cuts=cuts, base=base):
            for offset, (part, first, rows) in enumerate(cuts):
                span = pl.ds(pl.multiple_of(at[base + offset] * 16, 16), rows)
                source = parts[part].at[pl.ds(first, rows)]
                semaphore = semaphores.at[base + offset]
                pltpu.make_async_copy(source, whole.at[span], semaphore).wait()


def hidden_kernel(cuts, order, starts, mlp_in, bias, *refs):
    whole_out, hidden, slope, whole, semaphores, store_semaphores = refs[-6:]
    pieces = refs[:-6]
    step, steps = pl.program_id(0), pl.num_programs(0)
    width = mlp_in.shape[-1]
    span = pl.ds(pl.multiple_of(order[step] * width, width), width)

    @pl.when(step == 0)
    def _():
        start_loads([cut for group in cuts for cut in group], starts, pieces, whole, semaphores)

    wait_loads(cuts, starts, pieces, whole, semaphores)
    pltpu.make_async_copy(whole.at[span], whole_out.at[span], store_semaphores.at[step]).start()
    root = (2.0 / math.pi) ** 0.5
    source = mlp_in[...]
    block = whole.at[span]
    for low, high in column_cuts(width):
        lanes = slice(low, high)
        pre = dot_nn(source, block[:, lanes]) + bias[0, :, lanes]
        square = pre * pre
        bent = jnp.tanh(root * pre * (1.0 + 0.044715 * square))
        half = 0.5 + 0.5 * bent
        hidden[0, :, lanes] = narrow(pre * half)
        steep = (0.5 * root) * pre * (1.0 + 3 * 0.044715 * square)
        slope[0, :, lanes] = narrow(half + steep * (1.0 - bent * bent))

    @pl.when(step == steps - 1)
    def _():
        for at in range(len(cuts)):
            rows = pl.ds(pl.multiple_of(order[at] * width, width), width)
            pltpu.make_async_copy(
                whole.at[rows], whole_out.at[rows], store_semaphores.at[at]
            ).wait()


def run_hidden(mlp_in, gathered, bias):
    pieces, cuts, starts, order = gathered
    total, width = mlp_in.shape
    count = len(cuts)
    per_block = pl.BlockSpec((1, total, width), lambda at, order, starts: (order[at], 0, 0))
    out = jax.ShapeDtypeStruct((count, total, width), jnp.bfloat16)
    return pl.pallas_call(
        functools.partial(hidden_kernel, cuts),
        grid_spec=pltpu.PrefetchScalarGridSpec(
            num_scalar_prefetch=2,
            grid=(count,),
            in_specs=[
                pl.BlockSpec((total, width), lambda at, order, starts: (0, 0)),
                pl.BlockSpec((1, 1, width), lambda at, order, starts: (order[at], 0, 0)),
            ]
            + [pl.BlockSpec(memory_space=pl.ANY)] * len(pieces),
            out_specs=[pl.BlockSpec(memory_space=pl.ANY), per_block, per_block],
            scratch_shapes=[
                pltpu.VMEM((count * width, width), jnp.bfloat16),
                pltpu.SemaphoreType.DMA((len(starts),)),
                pltpu.SemaphoreType.DMA((count,)),
            ],
        ),
        out_shape=[jax.ShapeDtypeStruct((count * width, width), jnp.bfloat16), out, out],
        compiler_params=pltpu.CompilerParams(vmem_limit_bytes=vmem_bytes),
        cost_estimate=little_cost,
    )(stacked(order), stacked(starts), mlp_in, bias, *pieces)


def branch_kernel(
    frames,
    cuts,
    order,
    starts,
    counts,
    hidden,
    slope,
    d_branch,
    bias,
    gates,
    resid,
    cotangent,
    *refs,
):
    d_pre, d_pre_sum, block_out, d_gate, branch, whole, semaphores = refs[-7:]
    pieces = refs[:-7]
    step, steps = pl.program_id(0), pl.num_programs(0)
    total, width = resid.shape
    clips = gates.shape[0]
    rows = total // clips
    source, back = hidden[0], d_branch[...]

    @pl.when(step == 0)
    def _():
        start_loads([cut for group in cuts for cut in group], starts, pieces, whole, semaphores)
        branch[...] = jnp.zeros_like(branch)

    wait_loads(cuts, starts, pieces, whole, semaphores)
    block = whole.at[pl.ds(pl.multiple_of(order[step] * width, width), width)]
    for low, high in column_cuts(width):
        span = slice(low, high)
        d_hidden = dot_nt(back, block[span, :])
        low_back = narrow(d_hidden * wide(slope[0, :, span]))
        d_pre[0, :, span] = low_back
        d_pre_sum[0, :, span] = column_sum(wide(low_back))
        branch[:, span] += dot_nn(source, block[:, span])

    @pl.when(step == steps - 1)
    def _():
        for clip in range(clips):
            span = slice(clip * rows, (clip + 1) * rows)
            kept = valid_rows(counts[clip], rows, frames) * (branch[span] + bias[...])
            block_out[span] = narrow(resid[span] + gates[clip] * kept)
            d_gate[clip] = column_sum(wide(cotangent[span]) * kept)


def run_branch(frames, counts, hidden, slope, gathered, d_branch, bias, gates, resid, cotangent):
    pieces, cuts, starts, order = gathered
    count, total, width = hidden.shape
    clips = gates.shape[0]

    def all_of(*shape):
        return pl.BlockSpec(shape, lambda at, order, starts: (0,) * len(shape))

    per_block = pl.BlockSpec((1, total, width), lambda at, order, starts: (order[at], 0, 0))
    low = jax.ShapeDtypeStruct((total, width), jnp.bfloat16)
    return pl.pallas_call(
        functools.partial(branch_kernel, frames, cuts),
        grid_spec=pltpu.PrefetchScalarGridSpec(
            num_scalar_prefetch=2,
            grid=(count,),
            in_specs=[
                pl.BlockSpec(memory_space=pltpu.SMEM),
                per_block,
                per_block,
                all_of(total, width),
                all_of(*bias.shape),
                all_of(*gates.shape),
                all_of(total, width),
                all_of(total, width),
            ]
            + [pl.BlockSpec(memory_space=pl.ANY)] * len(pieces),
            out_specs=[
                per_block,
                pl.BlockSpec((1, 1, width), lambda at, order, starts: (order[at], 0, 0)),
                all_of(total, width),
                all_of(clips, 1, width),
            ],
            scratch_shapes=[
                pltpu.VMEM((total, width), jnp.float32),
                pltpu.VMEM((count * width, width), jnp.bfloat16),
                pltpu.SemaphoreType.DMA((len(starts),)),
            ],
        ),
        out_shape=[
            jax.ShapeDtypeStruct((count, total, width), jnp.bfloat16),
            jax.ShapeDtypeStruct((count, 1, width), jnp.float32),
            low,
            jax.ShapeDtypeStruct((clips, 1, width), jnp.float32),
        ],
        compiler_params=pltpu.CompilerParams(vmem_limit_bytes=vmem_bytes),
        cost_estimate=little_cost,
    )(stacked(order), stacked(starts), counts, hidden, slope, d_branch, bias, gates, resid, cotangent, *pieces)


def resid_kernel(
    frames,
    counts,
    d_pre,
    block,
    mods,
    resid,
    cotangent,
    proj,
    d_resid_out,
    d_proj,
    sums,
    total_grad,
):
    step, steps = pl.program_id(0), pl.num_programs(0)
    total, width = resid.shape
    clips = mods.shape[0]
    rows = total // clips
    tile = min(rows, 128)
    source = d_pre[0]

    @pl.when(step == 0)
    def _():
        total_grad[...] = jnp.zeros_like(total_grad)

    for low, high in column_cuts(width):
        span = slice(low, high)
        total_grad[:, span] += dot_nt(source, block[0, span, :])

    @pl.when(step == steps - 1)
    def _():
        for clip in range(clips):
            gate_one, scale_two = mods[clip, 2:3, :], mods[clip, 4:5, :]
            found = [0.0] * 4
            for first in range(clip * rows, (clip + 1) * rows, tile):
                span = slice(first, first + tile)
                grad = total_grad[span]
                normed, inverse = norm_parts(resid[span])
                back = norm_back(grad * (1.0 + scale_two), normed, inverse)
                d_resid = wide(cotangent[span]) + back
                d_resid_out[span] = d_resid
                kept = valid_rows(counts[clip], tile, frames) * d_resid
                low_back = narrow(kept * gate_one)
                d_proj[span] = low_back
                terms = (grad, grad * normed, kept * proj[span], wide(low_back))
                found = [old + column_sum(term) for old, term in zip(found, terms)]
            for at in range(4):
                sums[clip, at : at + 1, :] = found[at]


def run_resid(frames, counts, d_pre, blocks, mods, resid, cotangent, proj):
    count, total, width = d_pre.shape
    clips = mods.shape[0]
    return pl.pallas_call(
        functools.partial(resid_kernel, frames),
        grid=(count,),
        in_specs=[
            pl.BlockSpec(memory_space=pltpu.SMEM),
            spec((1, total, width), lambda at: (at, 0, 0)),
            spec((1, width, width), lambda at: (at, 0, 0)),
            held(mods.shape),
            held((total, width)),
            held((total, width)),
            held((total, width)),
        ],
        out_specs=[held((total, width)), held((total, width)), held((clips, 4, width))],
        out_shape=[
            jax.ShapeDtypeStruct((total, width), jnp.float32),
            jax.ShapeDtypeStruct((total, width), jnp.bfloat16),
            jax.ShapeDtypeStruct((clips, 4, width), jnp.float32),
        ],
        scratch_shapes=[pltpu.VMEM((total, width), jnp.float32)],
        compiler_params=pltpu.CompilerParams(vmem_limit_bytes=vmem_bytes),
        cost_estimate=little_cost,
    )(counts, d_pre, blocks, mods, resid, cotangent, proj)


def attention_back_kernel(
    frames, counts, d_proj, parts, block, d_qkv, sums, d_mixed, d_query, d_key, d_value
):
    rows, width = d_proj.shape
    tile = min(rows, 128)
    count = counts[pl.program_id(0)]
    source = d_proj[...]
    for low, high in column_cuts(width):
        d_mixed[:, low:high] = narrow(dot_nt(source, block[0, low:high, :]))
    scale = (width // HEADS) ** -0.5
    offset = score_offset(count, tile, frames, 0)
    for ref in (d_query, d_key, d_value):
        ref[...] = jnp.zeros_like(ref)
    for first in range(0, rows, tile):
        span = slice(first, first + tile)
        for low, high, start, stop in head_windows(width):
            lanes = slice(start, stop)
            mask = lane_mask(low, high, stop - start, jnp.bfloat16)
            query_high = parts[0, span, lanes] * mask
            key_high = parts[2, span, lanes] * mask
            back = d_mixed[span, lanes] * mask
            scores = dot_nt(key_high, query_high)
            scores += dot_nt(key_high, parts[1, span, lanes])
            scores += dot_nt(parts[3, span, lanes], query_high) + offset
            expons = jnp.exp(scores - jnp.max(scores, axis=0, keepdims=True))
            probs = expons * (1.0 / jnp.sum(expons, axis=0, keepdims=True))
            d_probs = dot_nt(parts[4, span, lanes], back)
            inner = jnp.sum(d_probs * probs, axis=0, keepdims=True)
            d_scores = narrow(probs * (d_probs - inner))
            d_value[span, lanes] += dot_nn(narrow(probs), back)
            d_key[span, lanes] += dot_nn(d_scores, query_high)
            d_query[span, lanes] += dot_tn(d_scores, key_high)
    for at, ref in enumerate((d_query, d_key, d_value)):
        low_back = narrow(ref[...] * scale) if at == 0 else narrow(ref[...])
        d_qkv[at] = low_back
        sums[0, at : at + 1, :] = column_sum(wide(low_back))
    d_qkv[3] = source


def run_attention_back(frames, counts, d_proj, parts, block):
    total, width = d_proj.shape
    clips = counts.shape[0]
    rows = total // clips
    return pl.pallas_call(
        functools.partial(attention_back_kernel, frames),
        grid=(clips,),
        in_specs=[
            pl.BlockSpec(memory_space=pltpu.SMEM),
            spec((rows, width), lambda clip: (clip, 0)),
            spec((5, rows, width), lambda clip: (0, clip, 0)),
            spec((1, width, width), lambda clip: (3, 0, 0), pipeline_mode=pl.Buffered(1)),
        ],
        out_specs=[
            spec((4, rows, width), lambda clip: (0, clip, 0)),
            spec((1, 3, width), lambda clip: (clip, 0, 0)),
        ],
        out_shape=[
            jax.ShapeDtypeStruct((4, total, width), jnp.bfloat16),
            jax.ShapeDtypeStruct((clips, 3, width), jnp.float32),
        ],
        scratch_shapes=[pltpu.VMEM((rows, width), jnp.bfloat16)]
        + [pltpu.VMEM((rows, width), jnp.float32)] * 3,
        compiler_params=pltpu.CompilerParams(vmem_limit_bytes=vmem_bytes),
        cost_estimate=little_cost,
    )(counts, d_proj, parts, block)


def input_kernel(d_qkv, block, mods, tokens, d_resid, input_grad, sums, total_grad):
    step, steps = pl.program_id(0), pl.num_programs(0)
    total, width = tokens.shape
    clips = mods.shape[0]
    rows = total // clips
    tile = min(rows, 128)
    source = d_qkv[0]

    @pl.when(step == 0)
    def _():
        total_grad[...] = jnp.zeros_like(total_grad)

    for low, high in column_cuts(width):
        span = slice(low, high)
        total_grad[:, span] += dot_nt(source, block[0, span, :])

    @pl.when(step == steps - 1)
    def _():
        for clip in range(clips):
            scale_one = mods[clip, 1:2, :]
            found = [0.0] * 2
            for first in range(clip * rows, (clip + 1) * rows, tile):
                span = slice(first, first + tile)
                grad = total_grad[span]
                normed, inverse = norm_parts(wide(tokens[span]))
                back = norm_back(grad * (1.0 + scale_one), normed, inverse)
                input_grad[span] = narrow(d_resid[span] + back)
                terms = (grad, grad * normed)
                found = [old + column_sum(term) for old, term in zip(found, terms)]
            for at in range(2):
                sums[clip, at : at + 1, :] = found[at]


def run_input(d_qkv, blocks, mods, tokens, d_resid):
    total, width = tokens.shape
    clips = mods.shape[0]
    return pl.pallas_call(
        input_kernel,
        grid=(3,),
        in_specs=[
            spec((1, total, width), lambda at: (at, 0, 0)),
            spec((1, width, width), lambda at: (at, 0, 0)),
            held(mods.shape),
            held((total, width)),
            held((total, width)),
        ],
        out_specs=[held((total, width)), held((clips, 2, width))],
        out_shape=[
            jax.ShapeDtypeStruct((total, width), jnp.bfloat16),
            jax.ShapeDtypeStruct((clips, 2, width), jnp.float32),
        ],
        scratch_shapes=[pltpu.VMEM((total, width), jnp.float32)],
        compiler_params=pltpu.CompilerParams(vmem_limit_bytes=vmem_bytes),
        cost_estimate=little_cost,
    )(d_qkv, blocks, mods, tokens, d_resid)


def halves_kernel(left_of, adds, steps, order, side, *refs):
    lefts = refs[: max(left_of) + 1]
    right = refs[len(lefts)]
    turned, total_low = refs[-2:]
    if adds:
        incoming, first_keep, first_out, second_keep, second_out = refs[len(lefts) + 1 : -2]
    else:
        out = refs[-3]
    step = pl.program_id(0)
    block = order[step]
    width = lefts[0].shape[-1]
    half = width // 2

    def pick(left, at):
        lanes = slice(at * half, (at + 1) * half)
        turned[...] = (left[:, lanes] if left.ndim == 2 else left[0, :, lanes]).T

    fresh = (step == 0) | (lefts[0].ndim == 3) | (len(lefts) > 1)
    for at in range(2):
        for index, left in enumerate(lefts):
            of_left = [block == number for number, source in enumerate(left_of) if source == index]

            @pl.when(fresh & (side[0] == at) & functools.reduce(jnp.logical_or, of_left))
            def _(left=left, at=at):
                pick(left, at)

    found = dot_nn(turned[...], right[0] if right.ndim == 3 else right[...])
    if not adds:
        out[0] = narrow(found)
        return
    total_low[...] = narrow(found + wide(incoming[0]))
    for state, target, rows in (
        (steps[0][0], first_keep, slice(0, half // 2)),
        (steps[0][1], first_out, slice(0, half // 2)),
        (steps[1][0], second_keep, slice(half // 2, half)),
        (steps[1][1], second_out, slice(half // 2, half)),
    ):

        @pl.when(functools.reduce(jnp.logical_or, [step == at_step for at_step in state]))
        def _(target=target, rows=rows):
            target[0] = total_low[rows]


def run_halves(lefts, left_of, right, side, at, incoming=None):
    total, width = lefts[0].shape[-2:]
    half = width // 2
    low_bit, high_bit = at % 2, at // 2
    order = stacked([at ^ 3, at ^ 1, at, at ^ 2])
    places = {
        "first_keep": [high_bit, high_bit, high_bit, 1 - high_bit],
        "first_out": [1 - high_bit, high_bit, high_bit, high_bit],
        "second_keep": [1 - low_bit, 1 - low_bit, low_bit, low_bit],
        "second_out": [1 - low_bit, low_bit, low_bit, low_bit],
    }
    steps = (((2, 3), (0, 1)), ((1, 2), (0, 3)))
    adds = incoming is not None
    table = stacked([place for row in places.values() for place in row])

    def block_of(array, *rest):
        if array.ndim == 2:
            return pl.BlockSpec(array.shape, lambda step, order, side, table: (0, 0))
        return pl.BlockSpec((1,) + array.shape[1:], lambda step, order, side, table: (order[step], 0, 0))

    per_block = pl.BlockSpec((1, half, width), lambda step, order, side, table: (order[step], 0, 0))
    operands = list(lefts) + [right]
    in_specs = [block_of(array) for array in operands]
    if adds:
        operands.append(incoming)
        in_specs.append(per_block)
        out_specs = [
            pl.BlockSpec(
                (1, half // 2, width),
                functools.partial(lambda row, step, order, side, table: (table[row * 4 + step], 0, 0), row),
            )
            for row in range(4)
        ]
        out_shape = [jax.ShapeDtypeStruct((2, half // 2, width), jnp.bfloat16)] * 4
    else:
        out_specs = per_block
        out_shape = jax.ShapeDtypeStruct((4, half, width), jnp.bfloat16)

    def body(order, side, table, *refs):
        halves_kernel(left_of, adds, steps, order, side, *refs)

    return pl.pallas_call(
        body,
        grid_spec=pltpu.PrefetchScalarGridSpec(
            num_scalar_prefetch=3,
            grid=(4,),
            in_specs=in_specs,
            out_specs=out_specs,
            scratch_shapes=[
                pltpu.VMEM((half, total), jnp.bfloat16),
                pltpu.VMEM((half, width), jnp.bfloat16),
            ],
        ),
        out_shape=out_shape,
        compiler_params=pltpu.CompilerParams(vmem_limit_bytes=vmem_bytes),
        cost_estimate=little_cost,
    )(order, stacked([side]), table, *operands)


def tie(*values):
    return lax.optimization_barrier(values)


def packed(arrays, tile):
    flat = jnp.concatenate([array.reshape(-1) for array in arrays])
    return jnp.pad(flat, (0, -flat.shape[0] % (tile * 128))).reshape(-1, 128)


def core_swap(array):
    count = lax.axis_size("dp")
    return lax.ppermute(array, "dp", [(at, at ^ 1) for at in range(count)])


def chip_shift(array, step):
    count = lax.axis_size("dp")
    return lax.ppermute(array, "dp", [(at, (at + 2 * step) % count) for at in range(count)])


def chip_swap(array, bits):
    count = lax.axis_size("dp")
    return lax.ppermute(array, "dp", [(at, at ^ (2 * bits)) for at in range(count)])


def rank_swap(array, bits):
    count = lax.axis_size("fsdp")
    return lax.ppermute(array, "fsdp", [(at, at ^ bits) for at in range(count)])


def entry(array, at, axis=0):
    return lax.dynamic_index_in_dim(array, at, axis, keepdims=False)


def place_kernel(cuts, at, *refs):
    parts, whole, held_rows, semaphores = refs[:-3], refs[-3], refs[-2], refs[-1]
    spans, loads, stores = [], [], []
    for index, (part, first, rows) in enumerate(cuts):
        spans.append(pl.ds(pl.multiple_of(at[index] * 16, 16), rows))
        source = parts[part].at[pl.ds(first, rows)]
        loads.append(
            pltpu.make_async_copy(source, held_rows.at[spans[index]], semaphores.at[0, index])
        )
        loads[index].start()
    for index, span in enumerate(spans):
        loads[index].wait()
        stores.append(
            pltpu.make_async_copy(held_rows.at[span], whole.at[span], semaphores.at[1, index])
        )
        stores[index].start()
    for store in stores:
        store.wait()


def place(parts, cuts, starts, rows):
    width = parts[0].shape[-1]
    dtype = parts[0].dtype
    return pl.pallas_call(
        functools.partial(place_kernel, cuts),
        in_specs=[pl.BlockSpec(memory_space=pltpu.SMEM)]
        + [pl.BlockSpec(memory_space=pl.ANY)] * len(parts),
        out_specs=pl.BlockSpec(memory_space=pl.ANY),
        out_shape=jax.ShapeDtypeStruct((rows, width), dtype),
        scratch_shapes=[
            pltpu.VMEM((rows, width), dtype),
            pltpu.SemaphoreType.DMA((2, len(cuts))),
        ],
        compiler_params=pltpu.CompilerParams(vmem_limit_bytes=vmem_bytes),
        cost_estimate=little_cost,
    )(stacked(starts), *parts)


def own_rows(parts, group):
    ranks, at = lax.axis_size("fsdp"), lax.axis_index("fsdp")
    shares = ranks // group
    count, _, row_part, col_part = parts.shape
    chunk = row_part // shares
    split = parts.reshape(count, group, shares, chunk, col_part).transpose(1, 2, 0, 3, 4)
    split = split.reshape(ranks, count, chunk, col_part)
    if shares > 1:
        moved = lax.all_to_all(split, "fsdp", 0, 0, tiled=True)
        (moved,) = yield (moved,)
        yield moved.transpose(1, 2, 0, 3).reshape(count, chunk, ranks * col_part)
        return
    panels = [entry(split, at)]
    panels += [rank_swap(entry(split, at ^ bits), bits) for bits in range(1, ranks)]
    panels = yield tuple(panels)
    placed = [
        lax.select_n(at, *[panels[panel ^ index] for index in range(ranks)])
        for panel in range(ranks)
    ]
    yield jnp.concatenate(placed, axis=2)


def shard_rows(split, group):
    ranks, count, chunk, col_part = split.shape
    shares = ranks // group
    moved = lax.all_to_all(split, "fsdp", 0, 0, tiled=True)
    moved = moved.reshape(group, shares, count, chunk, col_part).transpose(2, 0, 1, 3, 4)
    return moved.reshape(count, group, shares * chunk, col_part)


def gather_blocks(rows, group):
    ranks, dp_count = lax.axis_size("fsdp"), lax.axis_size("dp")
    shares = ranks // group
    chunk, total = rows.shape
    all_rows = lax.all_gather(rows, ("fsdp", "dp"), axis=0, tiled=True)
    if shares > 1:
        all_rows = all_rows.reshape(group, shares, dp_count, chunk, total).transpose(0, 2, 1, 3, 4)
    return all_rows.reshape(group, total, total)


def join_line(found):
    chips, chip = lax.axis_size("dp") // 2, lax.axis_index("dp") // 2
    chunk = found[0].shape[0]
    starts = [(chip - step) % chips * (chunk // 16) for step in range(chips)]
    return place(found, [(step, 0, chunk) for step in range(chips)], starts, chips * chunk)


def gather_second(rows, group):
    ranks, at = lax.axis_size("fsdp"), lax.axis_index("fsdp")
    total = rows.shape[-1]
    if ranks != group:
        blocks = gather_blocks(rows, group).reshape(group * total, total)
        for _ in range(4):
            (blocks,) = yield (blocks,)
        cuts = [[(0, index * total, total)] for index in range(group)]
        yield [blocks], cuts, [index * (total // 16) for index in range(group)], range(group)
        return
    chips = lax.axis_size("dp") // 2
    core = lax.axis_index("dp") % 2
    chunk, half = rows.shape[0], total // 2
    others = yield tuple(chip_shift(rows, step) for step in range(1, chips))
    line = join_line([rows, *others])
    cuts = [(side, step * chunk, chunk) for side in range(2) for step in range(chips)]
    starts = [
        (2 * step + side) * (chunk // 16) for side in (core, 1 - core) for step in range(chips)
    ]
    (own,) = yield (place([line, core_swap(line)], cuts, starts, total),)
    share = lax.dynamic_slice_in_dim(own, core * half, half, 0)
    low, high = yield (rank_swap(share, 1), rank_swap(share, 2))
    quarter = half // 2
    low_other, high_other = core_swap(low), core_swap(high)
    last = yield (rank_swap(high[:quarter], 1), rank_swap(low[quarter:], 2))
    parts = [own, low, low_other, high, high_other, *last, *[core_swap(part) for part in last]]
    cuts = [[(0, 0, total)], [(1, 0, half), (2, 0, half)], [(3, 0, half), (4, 0, half)]]
    cuts.append([(5 + index, 0, quarter) for index in range(4)])
    starts = [at * (total // 16)]
    for bits in (1, 2):
        starts += [((at ^ bits) * 2 + side) * (half // 16) for side in (core, 1 - core)]
    for side in (core, 1 - core):
        first = ((at ^ 3) * 2 + side) * (half // 16)
        starts += [first, first + quarter // 16]
    yield parts, cuts, starts, [at ^ bits for bits in range(ranks)]


def gather_own(rows, group):
    ranks = lax.axis_size("fsdp")
    shares = ranks // group
    if shares > 1:
        sets = [[share + shares * block for share in range(shares)] for block in range(group)]
        rows = lax.all_gather(rows, "fsdp", axis=1, tiled=True, axis_index_groups=sets)
    return lax.all_gather(rows, "dp", axis=1, tiled=True)


def sum_blocks(lefts, left_of, right, group):
    ranks, dp_count = lax.axis_size("fsdp"), lax.axis_size("dp")
    shares = ranks // group
    total = lefts[0].shape[-1]
    if shares > 1:
        blocks = jnp.stack(
            [
                narrow(
                    fast_dot(
                        "tr,te->re",
                        lefts[index] if lefts[index].ndim == 2 else lefts[index][block],
                        right if right.ndim == 2 else right[block],
                    )
                )
                for block, index in enumerate(left_of)
            ]
        )
        chunk = total // (dp_count * shares)
        blocks = blocks.reshape(group, dp_count, shares, chunk, -1).transpose(0, 2, 1, 3, 4)
        rows = lax.psum_scatter(
            blocks.reshape(group * total, -1), ("fsdp", "dp"), scatter_dimension=0, tiled=True
        )
        for _ in range(7):
            (rows,) = yield (rows,)
        yield gather_own(rows[None], group)[0]
        return
    chips, half = dp_count // 2, total // 2
    chunk = half // chips
    at = lax.axis_index("fsdp")
    core, chip = lax.axis_index("dp") % 2, lax.axis_index("dp") // 2
    low_bit, high_bit = at % 2, at // 2
    (away,) = yield (run_halves(lefts, left_of, right, 1 - core, at),)
    (away_in,) = yield (core_swap(away),)
    first, first_out, second, second_out = run_halves(lefts, left_of, right, core, at, away_in)
    first_out, second_out = yield (first_out, second_out)
    first_in, second_in = yield (rank_swap(first_out, 1), rank_swap(second_out, 2))
    first = narrow(wide(first) + wide(first_in)).reshape(2, chips // 2, chunk, -1)
    second = narrow(wide(second) + wide(second_in)).reshape(2, chips // 2, chunk, -1)
    first_in = rank_swap(entry(first, 1 - high_bit), 2)
    second_in = rank_swap(entry(second, 1 - low_bit), 1)
    first_in, second_in = yield (first_in, second_in)
    first = narrow(wide(entry(first, high_bit)) + wide(first_in))
    second = narrow(wide(entry(second, low_bit)) + wide(second_in))
    line = jnp.concatenate([first, second])
    step = 1
    while step < chips:
        bit = chip // step % 2
        line = line.reshape(-1, 2, *line.shape[1:])
        (line_in,) = yield (chip_swap(entry(line, 1 - bit, 1), step),)
        line = narrow(wide(entry(line, bit, 1)) + wide(line_in))
        step *= 2
    yield lax.all_gather(line[0], "dp", axis=0, tiled=True)


def fast_dot(subscripts, left, right):
    return jnp.einsum(subscripts, left, right, preferred_element_type=jnp.float32)


def products_kernel(chips, at, gathered, left_root, right_root, out, whole, semaphores):
    chunk, width = left_root.shape[1:]
    ranks = out.shape[0]
    copies = []
    for index in range(2 * chips):
        first = (index % 2 * chips + index // 2) * chunk
        copies.append(
            pltpu.make_async_copy(
                gathered.at[pl.ds(index * chunk, chunk)],
                whole.at[pl.ds(first, chunk)],
                semaphores.at[index],
            )
        )
        copies[-1].start()
    for copy in copies:
        copy.wait()
    first = at[0] * 16
    grad = whole[...]
    picked = lax.broadcasted_iota(jnp.int32, (width, chunk), 0) - first
    picked = picked == lax.broadcasted_iota(jnp.int32, (width, chunk), 1)
    own_columns = narrow(dot_nn(grad, narrow(picked.astype(jnp.float32))))
    side_high, side_low = split_high(dot_nn(left_root[0], grad))
    right = right_root[0]
    precond = dot_nn(side_high, right) + dot_nn(side_low, right)
    outer = dot_nt(whole[pl.ds(pl.multiple_of(first, 16), chunk), :], grad)
    inner = dot_tn(own_columns, grad)
    for at_out, product in enumerate((precond, outer, inner)):
        low = narrow(product)
        for rank in range(ranks):
            span = slice(rank * (width // ranks), (rank + 1) * (width // ranks))
            out[rank, at_out] = low[:, span]


def owned_step(whole, left_roots, right_roots, index, group):
    ranks, dp_count = lax.axis_size("fsdp"), lax.axis_size("dp")
    shares = ranks // group
    chunk, total = left_roots.shape[1:]
    col_part = total // ranks
    first = lax.axis_index("dp") * (chunk * shares) + lax.axis_index("fsdp") % shares * chunk
    if shares == 1:
        return pl.pallas_call(
            functools.partial(products_kernel, dp_count // 2),
            in_specs=[
                pl.BlockSpec(memory_space=pltpu.SMEM),
                pl.BlockSpec(memory_space=pl.ANY),
                pl.BlockSpec((1, chunk, total), lambda step: (index, 0, 0)),
                pl.BlockSpec((1, total, total), lambda step: (index, 0, 0)),
            ],
            out_specs=pl.BlockSpec((ranks, 3, chunk, col_part), lambda step: (0, 0, 0, 0)),
            grid=(1,),
            out_shape=jax.ShapeDtypeStruct((ranks, 3, chunk, col_part), jnp.bfloat16),
            scratch_shapes=[
                pltpu.VMEM((total, total), jnp.bfloat16),
                pltpu.SemaphoreType.DMA((dp_count,)),
            ],
            compiler_params=pltpu.CompilerParams(vmem_limit_bytes=vmem_bytes),
            cost_estimate=little_cost,
        )((first // 16)[None], whole, left_roots, right_roots)
    left_root, right_root = left_roots[index], right_roots[index]
    grad_rows = lax.dynamic_slice_in_dim(whole, first, chunk, 0)
    own_columns = lax.dynamic_slice_in_dim(whole, first, chunk, 1)
    outer = fast_dot("rk,jk->rj", grad_rows, whole)
    inner = fast_dot("kr,kj->rj", own_columns, whole)
    side_high, side_low = split_high(fast_dot("rk,kj->rj", left_root, whole))
    precond = fast_dot("rk,kj->rj", side_high, right_root) + fast_dot(
        "rk,kj->rj", side_low, right_root
    )
    products = narrow(jnp.stack([precond, outer, inner]))
    return products.reshape(3, chunk, ranks, col_part).transpose(2, 0, 1, 3)


def per_device(
    tokens,
    conditioning,
    frame_counts,
    cotangent,
    weights,
    biases,
    momentum,
    left_stats,
    right_stats,
    left_roots,
    right_roots,
    bias_moment,
    bias_second,
):
    group = 4
    mod_count = 6
    clip_count, pos_count, frames, width = tokens.shape
    token_count = clip_count * pos_count * frames
    block_count, row_part, col_part = weights.shape
    dp_count, ranks = lax.axis_size("dp"), lax.axis_size("fsdp")
    dp_at, rank_at = lax.axis_index("dp"), lax.axis_index("fsdp")
    all_clips = clip_count * dp_count
    bias_part = biases.shape[0]
    stream = tokens.reshape(token_count, width)
    grad_out = cotangent.reshape(token_count, width)
    low_weights = narrow(weights).reshape(block_count, row_part, col_part)
    shards = low_weights[mod_count:].reshape(-1, group, row_part, col_part)

    weight_rows = own_rows(shards, group)
    weight_panels = next(weight_rows)
    cond_low = narrow(jax.nn.silu(conditioning))
    first_parts = lax.all_gather(packed([cond_low, narrow(biases)], 16), "dp", axis=0, tiled=True)
    weight_panels, first_parts = tie(weight_panels, first_parts)
    attn_rows, one_rows, two_rows = weight_rows.send(weight_panels)
    attn_w = gather_blocks(attn_rows, group)
    two_w = gather_blocks(two_rows, group).reshape(group * width, width)
    two_gathered = (
        [two_w],
        [[(0, index * width, width)] for index in range(group)],
        [index * (width // 16) for index in range(group)],
        range(group),
    )

    first_parts = first_parts.reshape(dp_count, -1)
    cond_all = first_parts[:, : clip_count * width].reshape(all_clips, width)
    bias_rows = wide(first_parts[:, clip_count * width : clip_count * width + bias_part])
    cond_rows = lax.dynamic_slice_in_dim(cond_all, dp_at * row_part, row_part, 1)
    cond_cols = wide(lax.dynamic_slice_in_dim(cond_all, rank_at * col_part, col_part, 1))
    mod_parts = fast_dot("cr,jre->cje", cond_rows, low_weights[:mod_count])
    mod_parts = lax.all_to_all(mod_parts, "dp", 0, 0, tiled=True)
    mod_parts, one_rows = tie(mod_parts, one_rows)
    one_steps = gather_second(one_rows, group)
    one_parts = next(one_steps)
    mod_cols = jnp.sum(mod_parts.reshape(dp_count, clip_count, mod_count, col_part), axis=0)
    left_cond = jnp.einsum("jrk,ck->jrc", left_roots[:mod_count], cond_cols, precision=precise)
    mod_size, bias_size = mod_cols.size, dp_count * bias_part
    second_parts = lax.all_gather(
        packed([mod_cols, bias_rows, left_cond], 8), "fsdp", axis=0, tiled=True
    )
    second_parts, one_parts = tie(second_parts, one_parts)
    roots = jnp.stack([narrow(left_roots[mod_count:]), narrow(right_roots[mod_count:])])
    one_parts, attn_w, roots = tie(one_steps.send(one_parts), attn_w, roots)
    one_parts = one_steps.send(one_parts)
    second_parts = second_parts.reshape(ranks, -1)
    mods = second_parts[:, :mod_size].reshape(ranks, clip_count, mod_count, col_part)
    mods = mods.transpose(1, 2, 0, 3).reshape(clip_count, mod_count, width)
    bias_all = second_parts[:, mod_size : mod_size + bias_size].reshape(ranks, dp_count, bias_part)
    bias_all = bias_all.transpose(1, 0, 2).reshape(-1, width)
    left_size = mod_size + bias_size + left_cond.size
    left_cond = jnp.sum(second_parts[:, mod_size + bias_size : left_size], axis=0)
    left_cond = left_cond.reshape(mod_count, row_part, all_clips)
    mods = mods + bias_all[:mod_count]
    bias_table = jnp.concatenate(
        [bias_all[6:7], jnp.zeros((1, width), jnp.float32), bias_all[7:14]]
    )

    attn_in, parts, mixed, proj, resid, mlp_in, d_branch, d_branch_sums = run_attention(
        frames, frame_counts, stream, grad_out, mods, bias_table, attn_w
    )
    mlp_in, one_parts = tie(mlp_in, one_parts)
    one_parts = one_steps.send(one_parts)
    one_w, hidden, slope = run_hidden(mlp_in, one_steps.send(one_parts), bias_table[4:8, None])
    one_w = one_w.reshape(group, width, width)

    two_steps = sum_blocks([hidden], [0] * group, d_branch, group)
    two_parts = next(two_steps)
    hidden, two_parts, roots = tie(hidden, two_parts, roots)
    two_parts = two_steps.send(two_parts)
    root_rows = own_rows(roots.reshape(-1, group, row_part, col_part), group)
    root_panels = next(root_rows)
    d_pre, d_pre_sums, block_out, d_gate_two = run_branch(
        frames,
        frame_counts,
        hidden,
        slope,
        two_gathered,
        d_branch,
        bias_table[8:9],
        mods[:, 5:6],
        resid,
        grad_out,
    )
    d_pre, root_panels = tie(d_pre, root_panels)
    root_rows = root_rows.send(root_panels)
    d_pre, two_parts, root_rows = tie(d_pre, two_parts, root_rows)
    two_parts = two_steps.send(two_parts)
    d_pre, two_parts = tie(d_pre, two_parts)
    two_parts = two_steps.send(two_parts)
    right_wholes = gather_own(root_rows[3:], group)
    one_steps = sum_blocks([mlp_in], [0] * group, d_pre, group)
    one_parts = next(one_steps)
    d_pre, one_parts = tie(d_pre, one_parts)
    one_parts = one_steps.send(one_parts)
    d_resid, d_proj, resid_sums = run_resid(
        frames, frame_counts, d_pre, one_w, mods, resid, grad_out, proj
    )
    d_proj, one_parts = tie(d_proj, one_parts)
    one_parts = one_steps.send(one_parts)
    d_proj, one_parts, two_parts = tie(d_proj, one_parts, two_parts)
    two_parts = two_steps.send(two_parts)
    one_parts = one_steps.send(one_parts)
    d_heads, head_sums = run_attention_back(frames, frame_counts, d_proj, parts, attn_w)
    d_heads, two_parts, one_parts, right_wholes = tie(
        d_heads, two_parts, one_parts, right_wholes
    )
    two_parts = two_steps.send(two_parts)
    one_parts = one_steps.send(one_parts)
    attn_steps = sum_blocks([attn_in, mixed], [0, 0, 0, 1], d_heads, group)
    attn_parts = next(attn_steps)
    d_heads, attn_parts = tie(d_heads, attn_parts)
    attn_parts = attn_steps.send(attn_parts)
    input_grad, input_sums = run_input(d_heads, attn_w, mods, stream, d_resid)
    input_sums, attn_parts, two_parts, one_parts = tie(
        input_sums, attn_parts, two_parts, one_parts
    )
    two_parts = two_steps.send(two_parts)
    one_parts = one_steps.send(one_parts)

    d_mods = jnp.stack(
        [
            input_sums[:, 0],
            input_sums[:, 1],
            resid_sums[:, 2],
            resid_sums[:, 0],
            resid_sums[:, 1],
            d_gate_two[:, 0],
        ],
        axis=1,
    )
    head_sums = jnp.sum(head_sums, axis=0)
    grad_bias = jnp.concatenate(
        [
            jnp.sum(d_mods, axis=0),
            head_sums[0:1],
            head_sums[2:3],
            jnp.sum(resid_sums[:, 3], axis=0)[None],
            d_pre_sums[:, 0],
            jnp.sum(d_branch_sums, axis=0),
        ]
    )
    to_ranks = jnp.concatenate(
        [
            d_mods.reshape(clip_count, mod_count, ranks, col_part)
            .transpose(2, 0, 1, 3)
            .reshape(ranks, mod_size),
            grad_bias.reshape(dp_count, ranks, bias_part)
            .transpose(1, 0, 2)
            .reshape(ranks, bias_size),
        ],
        axis=1,
    )
    rank_sums = lax.all_to_all(to_ranks, "fsdp", 0, 0, tiled=True)
    rank_sums, attn_parts, two_parts = tie(rank_sums, attn_parts, two_parts)
    whole_two = two_steps.send(two_parts)
    attn_parts = attn_steps.send(attn_parts)
    rank_sums = jnp.sum(rank_sums, axis=0)
    to_rows = jnp.concatenate(
        [
            jnp.broadcast_to(rank_sums[None, :mod_size], (dp_count, mod_size)),
            rank_sums[mod_size:].reshape(dp_count, bias_part),
        ],
        axis=1,
    )
    to_rows, attn_parts = tie(to_rows, attn_parts)
    attn_parts = attn_steps.send(attn_parts)
    from_rows = lax.all_to_all(to_rows, "dp", 0, 0, tiled=True)
    from_rows, attn_parts, one_parts = tie(from_rows, attn_parts, one_parts)
    attn_parts = attn_steps.send(attn_parts)
    one_parts = one_steps.send(one_parts)
    bias_grad = jnp.sum(from_rows[:, mod_size:], axis=0)
    mod_grad_cols = from_rows[:, :mod_size].reshape(all_clips, mod_count, col_part)
    mod_grad = lax.all_gather(packed([mod_grad_cols], 8), "fsdp", axis=0, tiled=True)
    mod_grad, attn_parts, one_parts = tie(mod_grad, attn_parts, one_parts)
    attn_parts = attn_steps.send(attn_parts)
    whole_one = one_steps.send(one_parts)
    products_two = owned_step(whole_two, root_rows, right_wholes, 2, group)
    products_two, attn_parts = tie(products_two, attn_parts)
    attn_parts = attn_steps.send(attn_parts)
    back_two = shard_rows(products_two, group)
    products_one = owned_step(whole_one, root_rows, right_wholes, 1, group)
    mod_grad, back_two, attn_parts = tie(mod_grad, back_two, attn_parts)
    whole_attn = attn_steps.send(attn_parts)
    back_one = shard_rows(products_one, group)
    mod_grad = mod_grad.reshape(ranks, -1)[:, : mod_grad_cols.size]
    mod_grad = mod_grad.reshape(ranks, all_clips, mod_count, col_part).transpose(1, 2, 0, 3)
    mod_grad = mod_grad.reshape(all_clips, mod_count, width)

    mod_grad_rows = lax.dynamic_slice_in_dim(mod_grad, dp_at * row_part, row_part, 2)
    right_parts = jnp.einsum(
        "cjk,jke->cje", mod_grad_rows, right_roots[:mod_count], precision=precise
    )
    cond_wide = wide(cond_all)
    cond_row_wide = wide(cond_rows)
    mod_gram = jnp.einsum("cjk,bjk->jcb", mod_grad, mod_grad, precision=precise)
    cond_gram = jnp.einsum("ck,bk->cb", cond_wide, cond_wide, precision=precise)
    mod_side = jnp.einsum("jcb,be->jce", mod_gram, cond_cols, precision=precise)
    ada_left = jnp.einsum("cr,jce->jre", cond_row_wide, mod_side, precision=precise)
    cond_side = jnp.einsum("cb,bje->jce", cond_gram, mod_grad_cols, precision=precise)
    ada_right = jnp.einsum("cjr,jce->jre", mod_grad_rows, cond_side, precision=precise)

    right_parts = lax.all_gather(packed([right_parts], 8), "dp", axis=0, tiled=True)
    mod_right = jnp.sum(right_parts.reshape(dp_count, -1), axis=0)[: mod_grad_cols.size]
    mod_right = mod_right.reshape(all_clips, mod_count, col_part)
    ada_pre = jnp.einsum("jrc,cje->jre", left_cond, mod_right, precision=precise)
    whole_attn, back_one = tie(whole_attn, back_one)
    back_attn = shard_rows(owned_step(whole_attn, root_rows, right_wholes, 0, group), group)

    def joined(at, ada):
        return jnp.concatenate([ada, wide(back_attn[at]), wide(back_one[at]), wide(back_two[at])])

    precond = joined(0, ada_pre)
    left_new = stat_decay * left_stats + (1.0 - stat_decay) * joined(1, ada_left)
    right_new = stat_decay * right_stats + (1.0 - stat_decay) * joined(2, ada_right)
    momentum_new = moment_decay * momentum + precond
    weights_new = weights - weight_rate * momentum_new
    weights_copy = weights_new.astype(jnp.bfloat16)
    bias_second_new = stat_decay * bias_second + (1.0 - stat_decay) * bias_grad * bias_grad
    bias_moment_new = moment_decay * bias_moment + bias_grad * lax.rsqrt(
        bias_second_new + diag_epsilon
    )
    biases_new = biases - bias_rate * bias_moment_new
    return (
        block_out.reshape(tokens.shape),
        input_grad.reshape(tokens.shape),
        left_new,
        right_new,
        momentum_new,
        weights_new,
        weights_copy,
        bias_moment_new,
        bias_second_new,
        biases_new,
    )


def solution(mesh):
    placed = (
        P("dp", "fsdp", None, None),
        P("dp", None),
        P("dp"),
        P("dp", "fsdp", None, None),
        P(None, "dp", "fsdp"),
        P(("dp", "fsdp")),
        P(None, "dp", "fsdp"),
        P(None, "dp", "fsdp"),
        P(None, "dp", "fsdp"),
        P(None, "dp", "fsdp"),
        P(None, "dp", "fsdp"),
        P(("dp", "fsdp")),
        P(("dp", "fsdp")),
    )
    return jax.shard_map(
        per_device,
        mesh=mesh,
        in_specs=placed,
        out_specs=(
            P("dp", "fsdp", None, None),
            P("dp", "fsdp", None, None),
            P(None, "dp", "fsdp"),
            P(None, "dp", "fsdp"),
            P(None, "dp", "fsdp"),
            P(None, "dp", "fsdp"),
            P(None, "dp", "fsdp"),
            P(("dp", "fsdp")),
            P(("dp", "fsdp")),
            P(("dp", "fsdp")),
        ),
        check_vma=False,
    )
```

```python
import functools
import math

import jax
import jax.numpy as jnp
from jax import lax
from jax.experimental import pallas as pl
from jax.experimental.pallas import tpu as pltpu
from jax.sharding import PartitionSpec as P

HEADS = 16


precise = lax.Precision.HIGHEST
norm_epsilon = 1e-06
masked_score = -1e30
stat_decay = 0.5
moment_decay = 0.9
weight_rate = 0.7
bias_rate = 0.1
diag_epsilon = 1e-08
vmem_bytes = 50 * 2**20
little_cost = pl.CostEstimate(flops=1024, bytes_accessed=1024, transcendentals=0)


def narrow(array):
    return array.astype(jnp.bfloat16)


def wide(array):
    return array.astype(jnp.float32)


def spec(shape, index_map, **keywords):
    return pl.BlockSpec(shape, index_map, **keywords)


def held(shape):
    return pl.BlockSpec(shape, lambda step: (0,) * len(shape), pipeline_mode=pl.Buffered(1))


def column_cuts(total):
    cuts, at = [], 0
    while at < total:
        cuts.append((at, min(total, at + 256)))
        at += 256
    return cuts


def dot_nn(left, right):
    return lax.dot_general(left, right, (((1,), (0,)), ((), ())), preferred_element_type=jnp.float32)


def dot_nt(left, right):
    return lax.dot_general(left, right, (((1,), (1,)), ((), ())), preferred_element_type=jnp.float32)


def dot_tn(left, right):
    return lax.dot_general(left, right, (((0,), (0,)), ((), ())), preferred_element_type=jnp.float32)


def split_high(values):
    high = narrow(values)
    return high, narrow(values - wide(high))


def valid_rows(count, rows, frames):
    at = lax.broadcasted_iota(jnp.int32, (rows, 1), 0)
    return (lax.rem(at, frames) < count).astype(jnp.float32)


def score_offset(count, size, frames, key_axis):
    first = lax.broadcasted_iota(jnp.int32, (size, size), 0)
    second = lax.broadcasted_iota(jnp.int32, (size, size), 1)
    key = second if key_axis == 1 else first
    met = (lax.div(first, frames) == lax.div(second, frames)) & (lax.rem(key, frames) < count)
    return jnp.where(met, 0.0, masked_score)


def head_windows(width):
    size = width // HEADS
    windows = []
    for head in range(HEADS):
        low, high = head * size, (head + 1) * size
        start = low // 128 * 128
        stop = min(width, -(-high // 128) * 128)
        windows.append((low - start, high - start, start, stop))
    return windows


def lane_mask(low, high, count, dtype):
    lanes = lax.broadcasted_iota(jnp.int32, (1, count), 1)
    return ((lanes >= low) & (lanes < high)).astype(jnp.float32).astype(dtype)


def norm_parts(values):
    centered = values - jnp.mean(values, axis=-1, keepdims=True)
    variance = jnp.mean(centered * centered, axis=-1, keepdims=True)
    inverse = lax.rsqrt(variance + norm_epsilon)
    return centered * inverse, inverse


def norm_back(grad, normed, inverse):
    first = jnp.mean(grad, axis=-1, keepdims=True)
    second = jnp.mean(grad * normed, axis=-1, keepdims=True)
    return (grad - first - normed * second) * inverse


def column_sum(values):
    return jnp.sum(values, axis=0, keepdims=True)


def start_loads(cuts, at, parts, whole, semaphores, first_index=0):
    loads = []
    for index, (part, first, rows) in enumerate(cuts, first_index):
        span = pl.ds(pl.multiple_of(at[index] * 16, 16), rows)
        source = parts[part].at[pl.ds(first, rows)]
        loads.append(pltpu.make_async_copy(source, whole.at[span], semaphores.at[index]))
        loads[-1].start()
    return loads


def attention_kernel(
    frames,
    counts,
    tokens,
    cotangent,
    mods,
    bias,
    blocks,
    attn_in,
    parts,
    mixed_low,
    proj_out,
    resid_out,
    mlp_in,
    d_branch,
    d_branch_sum,
    mixed,
    whole,
    semaphores,
):
    rows, width = tokens.shape
    clip = pl.program_id(0)
    loads = [
        pltpu.make_async_copy(blocks.at[at], whole.at[at], semaphores.at[at]) for at in range(4)
    ]

    @pl.when(clip == 0)
    def _():
        for load in loads:
            load.start()

    tile = min(rows, 128)
    count = counts[clip]
    shift_one, scale_one, gate_one = (mods[0, at : at + 1, :] for at in range(3))
    shift_two, scale_two, gate_two = (mods[0, at : at + 1, :] for at in range(3, 6))
    for first in range(0, rows, tile):
        span = slice(first, first + tile)
        normed, _ = norm_parts(wide(tokens[span]))
        attn_in[span] = narrow(normed * (1.0 + scale_one) + shift_one)
        branch_back = narrow(wide(cotangent[span]) * valid_rows(count, tile, frames) * gate_two)
        d_branch[span] = branch_back
        part_sum = column_sum(wide(branch_back))
        d_branch_sum[0] = part_sum if first == 0 else d_branch_sum[0] + part_sum

    @pl.when(clip == 0)
    def _():
        for load in loads:
            load.wait()

    scale = (width // HEADS) ** -0.5
    source = attn_in[...]
    for low, high in column_cuts(width):
        span = slice(low, high)
        query = (dot_nn(source, whole[0, :, span]) + bias[0:1, span]) * scale
        parts[0, :, span], parts[1, :, span] = split_high(query)
        parts[2, :, span], parts[3, :, span] = split_high(dot_nn(source, whole[1, :, span]))
        parts[4, :, span] = narrow(dot_nn(source, whole[2, :, span]) + bias[2:3, span])
    offset = score_offset(count, tile, frames, 1)
    mixed[...] = jnp.zeros_like(mixed)
    for first in range(0, rows, tile):
        span = slice(first, first + tile)
        for low, high, start, stop in head_windows(width):
            lanes = slice(start, stop)
            mask = lane_mask(low, high, stop - start, jnp.bfloat16)
            key_high = parts[2, span, lanes]
            query_high = parts[0, span, lanes] * mask
            scores = dot_nt(query_high, key_high)
            scores += dot_nt(parts[1, span, lanes] * mask, key_high)
            scores += dot_nt(query_high, parts[3, span, lanes]) + offset
            expons = jnp.exp(scores - jnp.max(scores, axis=-1, keepdims=True))
            probs = expons * (1.0 / jnp.sum(expons, axis=-1, keepdims=True))
            out = dot_nn(narrow(probs), parts[4, span, lanes] * mask)
            mixed[span, lanes] += out
    mixed_low[...] = narrow(mixed[...])
    source = mixed_low[...]
    for low, high in column_cuts(width):
        span = slice(low, high)
        proj_out[:, span] = dot_nn(source, whole[3, :, span]) + bias[3:4, span]
    for first in range(0, rows, tile):
        span = slice(first, first + tile)
        resid = wide(tokens[span]) + valid_rows(count, tile, frames) * gate_one * proj_out[span]
        resid_out[span] = resid
        normed, _ = norm_parts(resid)
        mlp_in[span] = narrow(normed * (1.0 + scale_two) + shift_two)


def run_attention(frames, counts, tokens, cotangent, mods, bias, blocks):
    total, width = tokens.shape
    clips = mods.shape[0]
    rows = total // clips
    clip_rows = spec((rows, width), lambda clip: (clip, 0))
    low = jax.ShapeDtypeStruct((total, width), jnp.bfloat16)
    full = jax.ShapeDtypeStruct((total, width), jnp.float32)
    return pl.pallas_call(
        functools.partial(attention_kernel, frames),
        grid=(clips,),
        in_specs=[
            pl.BlockSpec(memory_space=pltpu.SMEM),
            clip_rows,
            clip_rows,
            spec((1,) + mods.shape[1:], lambda clip: (clip, 0, 0)),
            held(bias.shape),
            pl.BlockSpec(memory_space=pl.ANY),
        ],
        out_specs=[
            clip_rows,
            spec((5, rows, width), lambda clip: (0, clip, 0)),
            clip_rows,
            clip_rows,
            clip_rows,
            clip_rows,
            clip_rows,
            spec((1, 1, width), lambda clip: (clip, 0, 0)),
        ],
        out_shape=[
            low,
            jax.ShapeDtypeStruct((5, total, width), jnp.bfloat16),
            low,
            full,
            full,
            low,
            low,
            jax.ShapeDtypeStruct((clips, 1, width), jnp.float32),
        ],
        scratch_shapes=[
            pltpu.VMEM((rows, width), jnp.float32),
            pltpu.VMEM(blocks.shape, jnp.bfloat16),
            pltpu.SemaphoreType.DMA((4,)),
        ],
        compiler_params=pltpu.CompilerParams(vmem_limit_bytes=vmem_bytes),
        cost_estimate=little_cost,
    )(counts, tokens, cotangent, mods, bias, blocks)


def stacked(numbers):
    return jnp.stack([jnp.asarray(number, jnp.int32) for number in numbers])


def start_loads(cuts, at, parts, whole, semaphores):
    for index, (part, first, rows) in enumerate(cuts):
        span = pl.ds(pl.multiple_of(at[index] * 16, 16), rows)
        source = parts[part].at[pl.ds(first, rows)]
        pltpu.make_async_copy(source, whole.at[span], semaphores.at[index]).start()


def wait_loads(groups, at, parts, whole, semaphores):
    index = 0
    for step, cuts in enumerate(groups):
        base = index
        index += len(cuts)

        @pl.when(pl.program_id(0) == step)
        def _(cuts=cuts, base=base):
            for offset, (part, first, rows) in enumerate(cuts):
                span = pl.ds(pl.multiple_of(at[base + offset] * 16, 16), rows)
                source = parts[part].at[pl.ds(first, rows)]
                semaphore = semaphores.at[base + offset]
                pltpu.make_async_copy(source, whole.at[span], semaphore).wait()


def hidden_kernel(cuts, order, starts, mlp_in, bias, *refs):
    whole_out, hidden, slope, whole, semaphores, store_semaphores = refs[-6:]
    pieces = refs[:-6]
    step, steps = pl.program_id(0), pl.num_programs(0)
    width = mlp_in.shape[-1]
    span = pl.ds(pl.multiple_of(order[step] * width, width), width)

    @pl.when(step == 0)
    def _():
        start_loads([cut for group in cuts for cut in group], starts, pieces, whole, semaphores)

    wait_loads(cuts, starts, pieces, whole, semaphores)
    pltpu.make_async_copy(whole.at[span], whole_out.at[span], store_semaphores.at[step]).start()
    root = (2.0 / math.pi) ** 0.5
    source = mlp_in[...]
    block = whole.at[span]
    for low, high in column_cuts(width):
        lanes = slice(low, high)
        pre = dot_nn(source, block[:, lanes]) + bias[0, :, lanes]
        square = pre * pre
        bent = jnp.tanh(root * pre * (1.0 + 0.044715 * square))
        half = 0.5 + 0.5 * bent
        hidden[0, :, lanes] = narrow(pre * half)
        steep = (0.5 * root) * pre * (1.0 + 3 * 0.044715 * square)
        slope[0, :, lanes] = narrow(half + steep * (1.0 - bent * bent))

    @pl.when(step == steps - 1)
    def _():
        for at in range(len(cuts)):
            rows = pl.ds(pl.multiple_of(order[at] * width, width), width)
            pltpu.make_async_copy(
                whole.at[rows], whole_out.at[rows], store_semaphores.at[at]
            ).wait()


def run_hidden(mlp_in, gathered, bias):
    pieces, cuts, starts, order = gathered
    total, width = mlp_in.shape
    count = len(cuts)
    per_block = pl.BlockSpec((1, total, width), lambda at, order, starts: (order[at], 0, 0))
    out = jax.ShapeDtypeStruct((count, total, width), jnp.bfloat16)
    return pl.pallas_call(
        functools.partial(hidden_kernel, cuts),
        grid_spec=pltpu.PrefetchScalarGridSpec(
            num_scalar_prefetch=2,
            grid=(count,),
            in_specs=[
                pl.BlockSpec((total, width), lambda at, order, starts: (0, 0)),
                pl.BlockSpec((1, 1, width), lambda at, order, starts: (order[at], 0, 0)),
            ]
            + [pl.BlockSpec(memory_space=pl.ANY)] * len(pieces),
            out_specs=[pl.BlockSpec(memory_space=pl.ANY), per_block, per_block],
            scratch_shapes=[
                pltpu.VMEM((count * width, width), jnp.bfloat16),
                pltpu.SemaphoreType.DMA((len(starts),)),
                pltpu.SemaphoreType.DMA((count,)),
            ],
        ),
        out_shape=[jax.ShapeDtypeStruct((count * width, width), jnp.bfloat16), out, out],
        compiler_params=pltpu.CompilerParams(vmem_limit_bytes=vmem_bytes),
        cost_estimate=little_cost,
    )(stacked(order), stacked(starts), mlp_in, bias, *pieces)


def branch_kernel(
    frames,
    cuts,
    order,
    starts,
    counts,
    hidden,
    slope,
    d_branch,
    bias,
    gates,
    resid,
    cotangent,
    *refs,
):
    d_pre, d_pre_sum, block_out, d_gate, branch, whole, semaphores = refs[-7:]
    pieces = refs[:-7]
    step, steps = pl.program_id(0), pl.num_programs(0)
    total, width = resid.shape
    clips = gates.shape[0]
    rows = total // clips
    source, back = hidden[0], d_branch[...]

    @pl.when(step == 0)
    def _():
        start_loads([cut for group in cuts for cut in group], starts, pieces, whole, semaphores)
        branch[...] = jnp.zeros_like(branch)

    wait_loads(cuts, starts, pieces, whole, semaphores)
    block = whole.at[pl.ds(pl.multiple_of(order[step] * width, width), width)]
    for low, high in column_cuts(width):
        span = slice(low, high)
        d_hidden = dot_nt(back, block[span, :])
        low_back = narrow(d_hidden * wide(slope[0, :, span]))
        d_pre[0, :, span] = low_back
        d_pre_sum[0, :, span] = column_sum(wide(low_back))
        branch[:, span] += dot_nn(source, block[:, span])

    @pl.when(step == steps - 1)
    def _():
        for clip in range(clips):
            span = slice(clip * rows, (clip + 1) * rows)
            kept = valid_rows(counts[clip], rows, frames) * (branch[span] + bias[...])
            block_out[span] = narrow(resid[span] + gates[clip] * kept)
            d_gate[clip] = column_sum(wide(cotangent[span]) * kept)


def run_branch(frames, counts, hidden, slope, gathered, d_branch, bias, gates, resid, cotangent):
    pieces, cuts, starts, order = gathered
    count, total, width = hidden.shape
    clips = gates.shape[0]

    def all_of(*shape):
        return pl.BlockSpec(shape, lambda at, order, starts: (0,) * len(shape))

    per_block = pl.BlockSpec((1, total, width), lambda at, order, starts: (order[at], 0, 0))
    low = jax.ShapeDtypeStruct((total, width), jnp.bfloat16)
    return pl.pallas_call(
        functools.partial(branch_kernel, frames, cuts),
        grid_spec=pltpu.PrefetchScalarGridSpec(
            num_scalar_prefetch=2,
            grid=(count,),
            in_specs=[
                pl.BlockSpec(memory_space=pltpu.SMEM),
                per_block,
                per_block,
                all_of(total, width),
                all_of(*bias.shape),
                all_of(*gates.shape),
                all_of(total, width),
                all_of(total, width),
            ]
            + [pl.BlockSpec(memory_space=pl.ANY)] * len(pieces),
            out_specs=[
                per_block,
                pl.BlockSpec((1, 1, width), lambda at, order, starts: (order[at], 0, 0)),
                all_of(total, width),
                all_of(clips, 1, width),
            ],
            scratch_shapes=[
                pltpu.VMEM((total, width), jnp.float32),
                pltpu.VMEM((count * width, width), jnp.bfloat16),
                pltpu.SemaphoreType.DMA((len(starts),)),
            ],
        ),
        out_shape=[
            jax.ShapeDtypeStruct((count, total, width), jnp.bfloat16),
            jax.ShapeDtypeStruct((count, 1, width), jnp.float32),
            low,
            jax.ShapeDtypeStruct((clips, 1, width), jnp.float32),
        ],
        compiler_params=pltpu.CompilerParams(vmem_limit_bytes=vmem_bytes),
        cost_estimate=little_cost,
    )(stacked(order), stacked(starts), counts, hidden, slope, d_branch, bias, gates, resid, cotangent, *pieces)


def resid_kernel(
    frames,
    counts,
    d_pre,
    block,
    mods,
    resid,
    cotangent,
    proj,
    d_resid_out,
    d_proj,
    sums,
    total_grad,
):
    step, steps = pl.program_id(0), pl.num_programs(0)
    total, width = resid.shape
    clips = mods.shape[0]
    rows = total // clips
    tile = min(rows, 128)
    source = d_pre[0]

    @pl.when(step == 0)
    def _():
        total_grad[...] = jnp.zeros_like(total_grad)

    for low, high in column_cuts(width):
        span = slice(low, high)
        total_grad[:, span] += dot_nt(source, block[0, span, :])

    @pl.when(step == steps - 1)
    def _():
        for clip in range(clips):
            gate_one, scale_two = mods[clip, 2:3, :], mods[clip, 4:5, :]
            found = [0.0] * 4
            for first in range(clip * rows, (clip + 1) * rows, tile):
                span = slice(first, first + tile)
                grad = total_grad[span]
                normed, inverse = norm_parts(resid[span])
                back = norm_back(grad * (1.0 + scale_two), normed, inverse)
                d_resid = wide(cotangent[span]) + back
                d_resid_out[span] = d_resid
                kept = valid_rows(counts[clip], tile, frames) * d_resid
                low_back = narrow(kept * gate_one)
                d_proj[span] = low_back
                terms = (grad, grad * normed, kept * proj[span], wide(low_back))
                found = [old + column_sum(term) for old, term in zip(found, terms)]
            for at in range(4):
                sums[clip, at : at + 1, :] = found[at]


def run_resid(frames, counts, d_pre, blocks, mods, resid, cotangent, proj):
    count, total, width = d_pre.shape
    clips = mods.shape[0]
    return pl.pallas_call(
        functools.partial(resid_kernel, frames),
        grid=(count,),
        in_specs=[
            pl.BlockSpec(memory_space=pltpu.SMEM),
            spec((1, total, width), lambda at: (at, 0, 0)),
            spec((1, width, width), lambda at: (at, 0, 0)),
            held(mods.shape),
            held((total, width)),
            held((total, width)),
            held((total, width)),
        ],
        out_specs=[held((total, width)), held((total, width)), held((clips, 4, width))],
        out_shape=[
            jax.ShapeDtypeStruct((total, width), jnp.float32),
            jax.ShapeDtypeStruct((total, width), jnp.bfloat16),
            jax.ShapeDtypeStruct((clips, 4, width), jnp.float32),
        ],
        scratch_shapes=[pltpu.VMEM((total, width), jnp.float32)],
        compiler_params=pltpu.CompilerParams(vmem_limit_bytes=vmem_bytes),
        cost_estimate=little_cost,
    )(counts, d_pre, blocks, mods, resid, cotangent, proj)


def attention_back_kernel(
    frames, counts, d_proj, parts, block, d_qkv, sums, d_mixed, d_query, d_key, d_value
):
    rows, width = d_proj.shape
    tile = min(rows, 128)
    count = counts[pl.program_id(0)]
    source = d_proj[...]
    for low, high in column_cuts(width):
        d_mixed[:, low:high] = narrow(dot_nt(source, block[0, low:high, :]))
    scale = (width // HEADS) ** -0.5
    offset = score_offset(count, tile, frames, 0)
    for ref in (d_query, d_key, d_value):
        ref[...] = jnp.zeros_like(ref)
    for first in range(0, rows, tile):
        span = slice(first, first + tile)
        for low, high, start, stop in head_windows(width):
            lanes = slice(start, stop)
            mask = lane_mask(low, high, stop - start, jnp.bfloat16)
            query_high = parts[0, span, lanes] * mask
            key_high = parts[2, span, lanes] * mask
            back = d_mixed[span, lanes] * mask
            scores = dot_nt(key_high, query_high)
            scores += dot_nt(key_high, parts[1, span, lanes])
            scores += dot_nt(parts[3, span, lanes], query_high) + offset
            expons = jnp.exp(scores - jnp.max(scores, axis=0, keepdims=True))
            probs = expons * (1.0 / jnp.sum(expons, axis=0, keepdims=True))
            d_probs = dot_nt(parts[4, span, lanes], back)
            inner = jnp.sum(d_probs * probs, axis=0, keepdims=True)
            d_scores = narrow(probs * (d_probs - inner))
            d_value[span, lanes] += dot_nn(narrow(probs), back)
            d_key[span, lanes] += dot_nn(d_scores, query_high)
            d_query[span, lanes] += dot_tn(d_scores, key_high)
    for at, ref in enumerate((d_query, d_key, d_value)):
        low_back = narrow(ref[...] * scale) if at == 0 else narrow(ref[...])
        d_qkv[at] = low_back
        sums[0, at : at + 1, :] = column_sum(wide(low_back))
    d_qkv[3] = source


def run_attention_back(frames, counts, d_proj, parts, block):
    total, width = d_proj.shape
    clips = counts.shape[0]
    rows = total // clips
    return pl.pallas_call(
        functools.partial(attention_back_kernel, frames),
        grid=(clips,),
        in_specs=[
            pl.BlockSpec(memory_space=pltpu.SMEM),
            spec((rows, width), lambda clip: (clip, 0)),
            spec((5, rows, width), lambda clip: (0, clip, 0)),
            spec((1, width, width), lambda clip: (3, 0, 0), pipeline_mode=pl.Buffered(1)),
        ],
        out_specs=[
            spec((4, rows, width), lambda clip: (0, clip, 0)),
            spec((1, 3, width), lambda clip: (clip, 0, 0)),
        ],
        out_shape=[
            jax.ShapeDtypeStruct((4, total, width), jnp.bfloat16),
            jax.ShapeDtypeStruct((clips, 3, width), jnp.float32),
        ],
        scratch_shapes=[pltpu.VMEM((rows, width), jnp.bfloat16)]
        + [pltpu.VMEM((rows, width), jnp.float32)] * 3,
        compiler_params=pltpu.CompilerParams(vmem_limit_bytes=vmem_bytes),
        cost_estimate=little_cost,
    )(counts, d_proj, parts, block)


def input_kernel(d_qkv, block, mods, tokens, d_resid, input_grad, sums, total_grad):
    step, steps = pl.program_id(0), pl.num_programs(0)
    total, width = tokens.shape
    clips = mods.shape[0]
    rows = total // clips
    tile = min(rows, 128)
    source = d_qkv[0]

    @pl.when(step == 0)
    def _():
        total_grad[...] = jnp.zeros_like(total_grad)

    for low, high in column_cuts(width):
        span = slice(low, high)
        total_grad[:, span] += dot_nt(source, block[0, span, :])

    @pl.when(step == steps - 1)
    def _():
        for clip in range(clips):
            scale_one = mods[clip, 1:2, :]
            found = [0.0] * 2
            for first in range(clip * rows, (clip + 1) * rows, tile):
                span = slice(first, first + tile)
                grad = total_grad[span]
                normed, inverse = norm_parts(wide(tokens[span]))
                back = norm_back(grad * (1.0 + scale_one), normed, inverse)
                input_grad[span] = narrow(d_resid[span] + back)
                terms = (grad, grad * normed)
                found = [old + column_sum(term) for old, term in zip(found, terms)]
            for at in range(2):
                sums[clip, at : at + 1, :] = found[at]


def run_input(d_qkv, blocks, mods, tokens, d_resid):
    total, width = tokens.shape
    clips = mods.shape[0]
    return pl.pallas_call(
        input_kernel,
        grid=(3,),
        in_specs=[
            spec((1, total, width), lambda at: (at, 0, 0)),
            spec((1, width, width), lambda at: (at, 0, 0)),
            held(mods.shape),
            held((total, width)),
            held((total, width)),
        ],
        out_specs=[held((total, width)), held((clips, 2, width))],
        out_shape=[
            jax.ShapeDtypeStruct((total, width), jnp.bfloat16),
            jax.ShapeDtypeStruct((clips, 2, width), jnp.float32),
        ],
        scratch_shapes=[pltpu.VMEM((total, width), jnp.float32)],
        compiler_params=pltpu.CompilerParams(vmem_limit_bytes=vmem_bytes),
        cost_estimate=little_cost,
    )(d_qkv, blocks, mods, tokens, d_resid)


def halves_kernel(left_of, adds, steps, order, side, *refs):
    lefts = refs[: max(left_of) + 1]
    right = refs[len(lefts)]
    turned, total_low = refs[-2:]
    if adds:
        incoming, first_keep, first_out, second_keep, second_out = refs[len(lefts) + 1 : -2]
    else:
        out = refs[-3]
    step = pl.program_id(0)
    block = order[step]
    width = lefts[0].shape[-1]
    half = width // 2

    def pick(left, at):
        lanes = slice(at * half, (at + 1) * half)
        turned[...] = (left[:, lanes] if left.ndim == 2 else left[0, :, lanes]).T

    fresh = (step == 0) | (lefts[0].ndim == 3) | (len(lefts) > 1)
    for at in range(2):
        for index, left in enumerate(lefts):
            of_left = [block == number for number, source in enumerate(left_of) if source == index]

            @pl.when(fresh & (side[0] == at) & functools.reduce(jnp.logical_or, of_left))
            def _(left=left, at=at):
                pick(left, at)

    found = dot_nn(turned[...], right[0] if right.ndim == 3 else right[...])
    if not adds:
        out[0] = narrow(found)
        return
    total_low[...] = narrow(found + wide(incoming[0]))
    for state, target, rows in (
        (steps[0][0], first_keep, slice(0, half // 2)),
        (steps[0][1], first_out, slice(0, half // 2)),
        (steps[1][0], second_keep, slice(half // 2, half)),
        (steps[1][1], second_out, slice(half // 2, half)),
    ):

        @pl.when(functools.reduce(jnp.logical_or, [step == at_step for at_step in state]))
        def _(target=target, rows=rows):
            target[0] = total_low[rows]


def run_halves(lefts, left_of, right, side, at, incoming=None):
    total, width = lefts[0].shape[-2:]
    half = width // 2
    low_bit, high_bit = at % 2, at // 2
    order = stacked([at ^ 3, at ^ 1, at, at ^ 2])
    places = {
        "first_keep": [high_bit, high_bit, high_bit, 1 - high_bit],
        "first_out": [1 - high_bit, high_bit, high_bit, high_bit],
        "second_keep": [1 - low_bit, 1 - low_bit, low_bit, low_bit],
        "second_out": [1 - low_bit, low_bit, low_bit, low_bit],
    }
    steps = (((2, 3), (0, 1)), ((1, 2), (0, 3)))
    adds = incoming is not None
    table = stacked([place for row in places.values() for place in row])

    def block_of(array, *rest):
        if array.ndim == 2:
            return pl.BlockSpec(array.shape, lambda step, order, side, table: (0, 0))
        return pl.BlockSpec((1,) + array.shape[1:], lambda step, order, side, table: (order[step], 0, 0))

    per_block = pl.BlockSpec((1, half, width), lambda step, order, side, table: (order[step], 0, 0))
    operands = list(lefts) + [right]
    in_specs = [block_of(array) for array in operands]
    if adds:
        operands.append(incoming)
        in_specs.append(per_block)
        out_specs = [
            pl.BlockSpec(
                (1, half // 2, width),
                functools.partial(lambda row, step, order, side, table: (table[row * 4 + step], 0, 0), row),
            )
            for row in range(4)
        ]
        out_shape = [jax.ShapeDtypeStruct((2, half // 2, width), jnp.bfloat16)] * 4
    else:
        out_specs = per_block
        out_shape = jax.ShapeDtypeStruct((4, half, width), jnp.bfloat16)

    def body(order, side, table, *refs):
        halves_kernel(left_of, adds, steps, order, side, *refs)

    return pl.pallas_call(
        body,
        grid_spec=pltpu.PrefetchScalarGridSpec(
            num_scalar_prefetch=3,
            grid=(4,),
            in_specs=in_specs,
            out_specs=out_specs,
            scratch_shapes=[
                pltpu.VMEM((half, total), jnp.bfloat16),
                pltpu.VMEM((half, width), jnp.bfloat16),
            ],
        ),
        out_shape=out_shape,
        compiler_params=pltpu.CompilerParams(vmem_limit_bytes=vmem_bytes),
        cost_estimate=little_cost,
    )(order, stacked([side]), table, *operands)


def tie(*values):
    return lax.optimization_barrier(values)


def packed(arrays, tile):
    flat = jnp.concatenate([array.reshape(-1) for array in arrays])
    return jnp.pad(flat, (0, -flat.shape[0] % (tile * 128))).reshape(-1, 128)


def core_swap(array):
    count = lax.axis_size("dp")
    return lax.ppermute(array, "dp", [(at, at ^ 1) for at in range(count)])


def chip_shift(array, step):
    count = lax.axis_size("dp")
    return lax.ppermute(array, "dp", [(at, (at + 2 * step) % count) for at in range(count)])


def chip_swap(array, bits):
    count = lax.axis_size("dp")
    return lax.ppermute(array, "dp", [(at, at ^ (2 * bits)) for at in range(count)])


def rank_swap(array, bits):
    count = lax.axis_size("fsdp")
    return lax.ppermute(array, "fsdp", [(at, at ^ bits) for at in range(count)])


def entry(array, at, axis=0):
    return lax.dynamic_index_in_dim(array, at, axis, keepdims=False)


def place_kernel(cuts, at, *refs):
    parts, whole, held_rows, semaphores = refs[:-3], refs[-3], refs[-2], refs[-1]
    spans, loads, stores = [], [], []
    for index, (part, first, rows) in enumerate(cuts):
        spans.append(pl.ds(pl.multiple_of(at[index] * 16, 16), rows))
        source = parts[part].at[pl.ds(first, rows)]
        loads.append(
            pltpu.make_async_copy(source, held_rows.at[spans[index]], semaphores.at[0, index])
        )
        loads[index].start()
    for index, span in enumerate(spans):
        loads[index].wait()
        stores.append(
            pltpu.make_async_copy(held_rows.at[span], whole.at[span], semaphores.at[1, index])
        )
        stores[index].start()
    for store in stores:
        store.wait()


def place(parts, cuts, starts, rows):
    width = parts[0].shape[-1]
    dtype = parts[0].dtype
    return pl.pallas_call(
        functools.partial(place_kernel, cuts),
        in_specs=[pl.BlockSpec(memory_space=pltpu.SMEM)]
        + [pl.BlockSpec(memory_space=pl.ANY)] * len(parts),
        out_specs=pl.BlockSpec(memory_space=pl.ANY),
        out_shape=jax.ShapeDtypeStruct((rows, width), dtype),
        scratch_shapes=[
            pltpu.VMEM((rows, width), dtype),
            pltpu.SemaphoreType.DMA((2, len(cuts))),
        ],
        compiler_params=pltpu.CompilerParams(vmem_limit_bytes=vmem_bytes),
        cost_estimate=little_cost,
    )(stacked(starts), *parts)


def own_rows(parts, group):
    ranks, at = lax.axis_size("fsdp"), lax.axis_index("fsdp")
    shares = ranks // group
    count, _, row_part, col_part = parts.shape
    chunk = row_part // shares
    split = parts.reshape(count, group, shares, chunk, col_part).transpose(1, 2, 0, 3, 4)
    split = split.reshape(ranks, count, chunk, col_part)
    if shares > 1:
        moved = lax.all_to_all(split, "fsdp", 0, 0, tiled=True)
        (moved,) = yield (moved,)
        yield moved.transpose(1, 2, 0, 3).reshape(count, chunk, ranks * col_part)
        return
    panels = [entry(split, at)]
    panels += [rank_swap(entry(split, at ^ bits), bits) for bits in range(1, ranks)]
    panels = yield tuple(panels)
    placed = [
        lax.select_n(at, *[panels[panel ^ index] for index in range(ranks)])
        for panel in range(ranks)
    ]
    yield jnp.concatenate(placed, axis=2)


def shard_rows(split, group):
    ranks, count, chunk, col_part = split.shape
    shares = ranks // group
    moved = lax.all_to_all(split, "fsdp", 0, 0, tiled=True)
    moved = moved.reshape(group, shares, count, chunk, col_part).transpose(2, 0, 1, 3, 4)
    return moved.reshape(count, group, shares * chunk, col_part)


def gather_blocks(rows, group):
    ranks, dp_count = lax.axis_size("fsdp"), lax.axis_size("dp")
    shares = ranks // group
    chunk, total = rows.shape
    all_rows = lax.all_gather(rows, ("fsdp", "dp"), axis=0, tiled=True)
    if shares > 1:
        all_rows = all_rows.reshape(group, shares, dp_count, chunk, total).transpose(0, 2, 1, 3, 4)
    return all_rows.reshape(group, total, total)


def join_line(found):
    chips, chip = lax.axis_size("dp") // 2, lax.axis_index("dp") // 2
    chunk = found[0].shape[0]
    starts = [(chip - step) % chips * (chunk // 16) for step in range(chips)]
    return place(found, [(step, 0, chunk) for step in range(chips)], starts, chips * chunk)


def gather_second(rows, group):
    ranks, at = lax.axis_size("fsdp"), lax.axis_index("fsdp")
    total = rows.shape[-1]
    if ranks != group:
        blocks = gather_blocks(rows, group).reshape(group * total, total)
        for _ in range(4):
            (blocks,) = yield (blocks,)
        cuts = [[(0, index * total, total)] for index in range(group)]
        yield [blocks], cuts, [index * (total // 16) for index in range(group)], range(group)
        return
    chips = lax.axis_size("dp") // 2
    core = lax.axis_index("dp") % 2
    chunk, half = rows.shape[0], total // 2
    others = yield tuple(chip_shift(rows, step) for step in range(1, chips))
    line = join_line([rows, *others])
    cuts = [(side, step * chunk, chunk) for side in range(2) for step in range(chips)]
    starts = [
        (2 * step + side) * (chunk // 16) for side in (core, 1 - core) for step in range(chips)
    ]
    (own,) = yield (place([line, core_swap(line)], cuts, starts, total),)
    share = lax.dynamic_slice_in_dim(own, core * half, half, 0)
    low, high = yield (rank_swap(share, 1), rank_swap(share, 2))
    quarter = half // 2
    low_other, high_other = core_swap(low), core_swap(high)
    last = yield (rank_swap(high[:quarter], 1), rank_swap(low[quarter:], 2))
    parts = [own, low, low_other, high, high_other, *last, *[core_swap(part) for part in last]]
    cuts = [[(0, 0, total)], [(1, 0, half), (2, 0, half)], [(3, 0, half), (4, 0, half)]]
    cuts.append([(5 + index, 0, quarter) for index in range(4)])
    starts = [at * (total // 16)]
    for bits in (1, 2):
        starts += [((at ^ bits) * 2 + side) * (half // 16) for side in (core, 1 - core)]
    for side in (core, 1 - core):
        first = ((at ^ 3) * 2 + side) * (half // 16)
        starts += [first, first + quarter // 16]
    yield parts, cuts, starts, [at ^ bits for bits in range(ranks)]


def gather_own(rows, group):
    ranks = lax.axis_size("fsdp")
    shares = ranks // group
    if shares > 1:
        sets = [[share + shares * block for share in range(shares)] for block in range(group)]
        rows = lax.all_gather(rows, "fsdp", axis=1, tiled=True, axis_index_groups=sets)
    return lax.all_gather(rows, "dp", axis=1, tiled=True)


def sum_blocks(lefts, left_of, right, group):
    ranks, dp_count = lax.axis_size("fsdp"), lax.axis_size("dp")
    shares = ranks // group
    total = lefts[0].shape[-1]
    if shares > 1:
        blocks = jnp.stack(
            [
                narrow(
                    fast_dot(
                        "tr,te->re",
                        lefts[index] if lefts[index].ndim == 2 else lefts[index][block],
                        right if right.ndim == 2 else right[block],
                    )
                )
                for block, index in enumerate(left_of)
            ]
        )
        chunk = total // (dp_count * shares)
        blocks = blocks.reshape(group, dp_count, shares, chunk, -1).transpose(0, 2, 1, 3, 4)
        rows = lax.psum_scatter(
            blocks.reshape(group * total, -1), ("fsdp", "dp"), scatter_dimension=0, tiled=True
        )
        for _ in range(7):
            (rows,) = yield (rows,)
        yield gather_own(rows[None], group)[0]
        return
    chips, half = dp_count // 2, total // 2
    chunk = half // chips
    at = lax.axis_index("fsdp")
    core, chip = lax.axis_index("dp") % 2, lax.axis_index("dp") // 2
    low_bit, high_bit = at % 2, at // 2
    (away,) = yield (run_halves(lefts, left_of, right, 1 - core, at),)
    (away_in,) = yield (core_swap(away),)
    first, first_out, second, second_out = run_halves(lefts, left_of, right, core, at, away_in)
    first_out, second_out = yield (first_out, second_out)
    first_in, second_in = yield (rank_swap(first_out, 1), rank_swap(second_out, 2))
    first = narrow(wide(first) + wide(first_in)).reshape(2, chips // 2, chunk, -1)
    second = narrow(wide(second) + wide(second_in)).reshape(2, chips // 2, chunk, -1)
    first_in = rank_swap(entry(first, 1 - high_bit), 2)
    second_in = rank_swap(entry(second, 1 - low_bit), 1)
    first_in, second_in = yield (first_in, second_in)
    first = narrow(wide(entry(first, high_bit)) + wide(first_in))
    second = narrow(wide(entry(second, low_bit)) + wide(second_in))
    line = jnp.concatenate([first, second])
    step = 1
    while step < chips:
        bit = chip // step % 2
        line = line.reshape(-1, 2, *line.shape[1:])
        (line_in,) = yield (chip_swap(entry(line, 1 - bit, 1), step),)
        line = narrow(wide(entry(line, bit, 1)) + wide(line_in))
        step *= 2
    yield lax.all_gather(line[0], "dp", axis=0, tiled=True)


def fast_dot(subscripts, left, right):
    return jnp.einsum(subscripts, left, right, preferred_element_type=jnp.float32)


def products_kernel(chips, at, gathered, left_root, right_root, out, whole, semaphores):
    chunk, width = left_root.shape[1:]
    ranks = out.shape[0]
    copies = []
    for index in range(2 * chips):
        first = (index % 2 * chips + index // 2) * chunk
        copies.append(
            pltpu.make_async_copy(
                gathered.at[pl.ds(index * chunk, chunk)],
                whole.at[pl.ds(first, chunk)],
                semaphores.at[index],
            )
        )
        copies[-1].start()
    for copy in copies:
        copy.wait()
    first = at[0] * 16
    grad = whole[...]
    picked = lax.broadcasted_iota(jnp.int32, (width, chunk), 0) - first
    picked = picked == lax.broadcasted_iota(jnp.int32, (width, chunk), 1)
    own_columns = narrow(dot_nn(grad, narrow(picked.astype(jnp.float32))))
    side_high, side_low = split_high(dot_nn(left_root[0], grad))
    right = right_root[0]
    precond = dot_nn(side_high, right) + dot_nn(side_low, right)
    outer = dot_nt(whole[pl.ds(pl.multiple_of(first, 16), chunk), :], grad)
    inner = dot_tn(own_columns, grad)
    for at_out, product in enumerate((precond, outer, inner)):
        low = narrow(product)
        for rank in range(ranks):
            span = slice(rank * (width // ranks), (rank + 1) * (width // ranks))
            out[rank, at_out] = low[:, span]


def owned_step(whole, left_roots, right_roots, index, group):
    ranks, dp_count = lax.axis_size("fsdp"), lax.axis_size("dp")
    shares = ranks // group
    chunk, total = left_roots.shape[1:]
    col_part = total // ranks
    first = lax.axis_index("dp") * (chunk * shares) + lax.axis_index("fsdp") % shares * chunk
    if shares == 1:
        return pl.pallas_call(
            functools.partial(products_kernel, dp_count // 2),
            in_specs=[
                pl.BlockSpec(memory_space=pltpu.SMEM),
                pl.BlockSpec(memory_space=pl.ANY),
                pl.BlockSpec((1, chunk, total), lambda step: (index, 0, 0)),
                pl.BlockSpec((1, total, total), lambda step: (index, 0, 0)),
            ],
            out_specs=pl.BlockSpec((ranks, 3, chunk, col_part), lambda step: (0, 0, 0, 0)),
            grid=(1,),
            out_shape=jax.ShapeDtypeStruct((ranks, 3, chunk, col_part), jnp.bfloat16),
            scratch_shapes=[
                pltpu.VMEM((total, total), jnp.bfloat16),
                pltpu.SemaphoreType.DMA((dp_count,)),
            ],
            compiler_params=pltpu.CompilerParams(vmem_limit_bytes=vmem_bytes),
            cost_estimate=little_cost,
        )((first // 16)[None], whole, left_roots, right_roots)
    left_root, right_root = left_roots[index], right_roots[index]
    grad_rows = lax.dynamic_slice_in_dim(whole, first, chunk, 0)
    own_columns = lax.dynamic_slice_in_dim(whole, first, chunk, 1)
    outer = fast_dot("rk,jk->rj", grad_rows, whole)
    inner = fast_dot("kr,kj->rj", own_columns, whole)
    side_high, side_low = split_high(fast_dot("rk,kj->rj", left_root, whole))
    precond = fast_dot("rk,kj->rj", side_high, right_root) + fast_dot(
        "rk,kj->rj", side_low, right_root
    )
    products = narrow(jnp.stack([precond, outer, inner]))
    return products.reshape(3, chunk, ranks, col_part).transpose(2, 0, 1, 3)


def per_device(
    tokens,
    conditioning,
    frame_counts,
    cotangent,
    weights,
    biases,
    momentum,
    left_stats,
    right_stats,
    left_roots,
    right_roots,
    bias_moment,
    bias_second,
):
    group = 4
    mod_count = 6
    clip_count, pos_count, frames, width = tokens.shape
    token_count = clip_count * pos_count * frames
    block_count, row_part, col_part = weights.shape
    dp_count, ranks = lax.axis_size("dp"), lax.axis_size("fsdp")
    dp_at, rank_at = lax.axis_index("dp"), lax.axis_index("fsdp")
    all_clips = clip_count * dp_count
    bias_part = biases.shape[0]
    stream = tokens.reshape(token_count, width)
    grad_out = cotangent.reshape(token_count, width)
    low_weights = narrow(weights).reshape(block_count, row_part, col_part)
    shards = low_weights[mod_count:].reshape(-1, group, row_part, col_part)

    weight_rows = own_rows(shards, group)
    weight_panels = next(weight_rows)
    cond_low = narrow(jax.nn.silu(conditioning))
    first_parts = lax.all_gather(packed([cond_low, narrow(biases)], 16), "dp", axis=0, tiled=True)
    weight_panels, first_parts = tie(weight_panels, first_parts)
    attn_rows, one_rows, two_rows = weight_rows.send(weight_panels)
    attn_w = gather_blocks(attn_rows, group)
    two_w = gather_blocks(two_rows, group).reshape(group * width, width)
    two_gathered = (
        [two_w],
        [[(0, index * width, width)] for index in range(group)],
        [index * (width // 16) for index in range(group)],
        range(group),
    )

    first_parts = first_parts.reshape(dp_count, -1)
    cond_all = first_parts[:, : clip_count * width].reshape(all_clips, width)
    bias_rows = wide(first_parts[:, clip_count * width : clip_count * width + bias_part])
    cond_rows = lax.dynamic_slice_in_dim(cond_all, dp_at * row_part, row_part, 1)
    cond_cols = wide(lax.dynamic_slice_in_dim(cond_all, rank_at * col_part, col_part, 1))
    mod_parts = fast_dot("cr,jre->cje", cond_rows, low_weights[:mod_count])
    mod_parts = lax.all_to_all(mod_parts, "dp", 0, 0, tiled=True)
    mod_parts, one_rows = tie(mod_parts, one_rows)
    one_steps = gather_second(one_rows, group)
    one_parts = next(one_steps)
    mod_cols = jnp.sum(mod_parts.reshape(dp_count, clip_count, mod_count, col_part), axis=0)
    left_cond = jnp.einsum("jrk,ck->jrc", left_roots[:mod_count], cond_cols, precision=precise)
    mod_size, bias_size = mod_cols.size, dp_count * bias_part
    second_parts = lax.all_gather(
        packed([mod_cols, bias_rows, left_cond], 8), "fsdp", axis=0, tiled=True
    )
    second_parts, one_parts = tie(second_parts, one_parts)
    roots = jnp.stack([narrow(left_roots[mod_count:]), narrow(right_roots[mod_count:])])
    one_parts, attn_w, roots = tie(one_steps.send(one_parts), attn_w, roots)
    one_parts = one_steps.send(one_parts)
    second_parts = second_parts.reshape(ranks, -1)
    mods = second_parts[:, :mod_size].reshape(ranks, clip_count, mod_count, col_part)
    mods = mods.transpose(1, 2, 0, 3).reshape(clip_count, mod_count, width)
    bias_all = second_parts[:, mod_size : mod_size + bias_size].reshape(ranks, dp_count, bias_part)
    bias_all = bias_all.transpose(1, 0, 2).reshape(-1, width)
    left_size = mod_size + bias_size + left_cond.size
    left_cond = jnp.sum(second_parts[:, mod_size + bias_size : left_size], axis=0)
    left_cond = left_cond.reshape(mod_count, row_part, all_clips)
    mods = mods + bias_all[:mod_count]
    bias_table = jnp.concatenate(
        [bias_all[6:7], jnp.zeros((1, width), jnp.float32), bias_all[7:14]]
    )

    attn_in, parts, mixed, proj, resid, mlp_in, d_branch, d_branch_sums = run_attention(
        frames, frame_counts, stream, grad_out, mods, bias_table, attn_w
    )
    mlp_in, one_parts = tie(mlp_in, one_parts)
    one_parts = one_steps.send(one_parts)
    one_w, hidden, slope = run_hidden(mlp_in, one_steps.send(one_parts), bias_table[4:8, None])
    one_w = one_w.reshape(group, width, width)

    two_steps = sum_blocks([hidden], [0] * group, d_branch, group)
    two_parts = next(two_steps)
    hidden, two_parts, roots = tie(hidden, two_parts, roots)
    two_parts = two_steps.send(two_parts)
    root_rows = own_rows(roots.reshape(-1, group, row_part, col_part), group)
    root_panels = next(root_rows)
    d_pre, d_pre_sums, block_out, d_gate_two = run_branch(
        frames,
        frame_counts,
        hidden,
        slope,
        two_gathered,
        d_branch,
        bias_table[8:9],
        mods[:, 5:6],
        resid,
        grad_out,
    )
    d_pre, root_panels = tie(d_pre, root_panels)
    root_rows = root_rows.send(root_panels)
    d_pre, two_parts, root_rows = tie(d_pre, two_parts, root_rows)
    two_parts = two_steps.send(two_parts)
    d_pre, two_parts = tie(d_pre, two_parts)
    two_parts = two_steps.send(two_parts)
    right_wholes = gather_own(root_rows[3:], group)
    one_steps = sum_blocks([mlp_in], [0] * group, d_pre, group)
    one_parts = next(one_steps)
    d_pre, one_parts = tie(d_pre, one_parts)
    one_parts = one_steps.send(one_parts)
    d_resid, d_proj, resid_sums = run_resid(
        frames, frame_counts, d_pre, one_w, mods, resid, grad_out, proj
    )
    d_proj, one_parts = tie(d_proj, one_parts)
    one_parts = one_steps.send(one_parts)
    d_proj, one_parts, two_parts = tie(d_proj, one_parts, two_parts)
    two_parts = two_steps.send(two_parts)
    one_parts = one_steps.send(one_parts)
    d_heads, head_sums = run_attention_back(frames, frame_counts, d_proj, parts, attn_w)
    d_heads, one_parts, right_wholes = tie(d_heads, one_parts, right_wholes)
    one_parts = one_steps.send(one_parts)
    attn_steps = sum_blocks([attn_in, mixed], [0, 0, 0, 1], d_heads, group)
    attn_parts = next(attn_steps)
    d_heads, attn_parts, two_parts = tie(d_heads, attn_parts, two_parts)
    two_parts = two_steps.send(two_parts)
    attn_parts = attn_steps.send(attn_parts)
    input_grad, input_sums = run_input(d_heads, attn_w, mods, stream, d_resid)
    input_sums, attn_parts, two_parts, one_parts = tie(
        input_sums, attn_parts, two_parts, one_parts
    )
    two_parts = two_steps.send(two_parts)
    one_parts = one_steps.send(one_parts)

    d_mods = jnp.stack(
        [
            input_sums[:, 0],
            input_sums[:, 1],
            resid_sums[:, 2],
            resid_sums[:, 0],
            resid_sums[:, 1],
            d_gate_two[:, 0],
        ],
        axis=1,
    )
    head_sums = jnp.sum(head_sums, axis=0)
    grad_bias = jnp.concatenate(
        [
            jnp.sum(d_mods, axis=0),
            head_sums[0:1],
            head_sums[2:3],
            jnp.sum(resid_sums[:, 3], axis=0)[None],
            d_pre_sums[:, 0],
            jnp.sum(d_branch_sums, axis=0),
        ]
    )
    to_ranks = jnp.concatenate(
        [
            d_mods.reshape(clip_count, mod_count, ranks, col_part)
            .transpose(2, 0, 1, 3)
            .reshape(ranks, mod_size),
            grad_bias.reshape(dp_count, ranks, bias_part)
            .transpose(1, 0, 2)
            .reshape(ranks, bias_size),
        ],
        axis=1,
    )
    rank_sums = lax.all_to_all(to_ranks, "fsdp", 0, 0, tiled=True)
    rank_sums, attn_parts = tie(rank_sums, attn_parts)
    attn_parts = attn_steps.send(attn_parts)
    rank_sums = jnp.sum(rank_sums, axis=0)
    to_rows = jnp.concatenate(
        [
            jnp.broadcast_to(rank_sums[None, :mod_size], (dp_count, mod_size)),
            rank_sums[mod_size:].reshape(dp_count, bias_part),
        ],
        axis=1,
    )
    to_rows, attn_parts = tie(to_rows, attn_parts)
    attn_parts = attn_steps.send(attn_parts)
    from_rows = lax.all_to_all(to_rows, "dp", 0, 0, tiled=True)
    from_rows, attn_parts, two_parts, one_parts = tie(from_rows, attn_parts, two_parts, one_parts)
    attn_parts = attn_steps.send(attn_parts)
    whole_two = two_steps.send(two_parts)
    one_parts = one_steps.send(one_parts)
    bias_grad = jnp.sum(from_rows[:, mod_size:], axis=0)
    mod_grad_cols = from_rows[:, :mod_size].reshape(all_clips, mod_count, col_part)
    mod_grad = lax.all_gather(packed([mod_grad_cols], 8), "fsdp", axis=0, tiled=True)
    mod_grad, attn_parts, one_parts = tie(mod_grad, attn_parts, one_parts)
    attn_parts = attn_steps.send(attn_parts)
    whole_one = one_steps.send(one_parts)
    products_two = owned_step(whole_two, root_rows, right_wholes, 2, group)
    products_two, attn_parts = tie(products_two, attn_parts)
    attn_parts = attn_steps.send(attn_parts)
    back_two = shard_rows(products_two, group)
    products_one = owned_step(whole_one, root_rows, right_wholes, 1, group)
    mod_grad, back_two, attn_parts = tie(mod_grad, back_two, attn_parts)
    whole_attn = attn_steps.send(attn_parts)
    back_one = shard_rows(products_one, group)
    mod_grad = mod_grad.reshape(ranks, -1)[:, : mod_grad_cols.size]
    mod_grad = mod_grad.reshape(ranks, all_clips, mod_count, col_part).transpose(1, 2, 0, 3)
    mod_grad = mod_grad.reshape(all_clips, mod_count, width)

    mod_grad_rows = lax.dynamic_slice_in_dim(mod_grad, dp_at * row_part, row_part, 2)
    right_parts = jnp.einsum(
        "cjk,jke->cje", mod_grad_rows, right_roots[:mod_count], precision=precise
    )
    cond_wide = wide(cond_all)
    cond_row_wide = wide(cond_rows)
    mod_gram = jnp.einsum("cjk,bjk->jcb", mod_grad, mod_grad, precision=precise)
    cond_gram = jnp.einsum("ck,bk->cb", cond_wide, cond_wide, precision=precise)
    mod_side = jnp.einsum("jcb,be->jce", mod_gram, cond_cols, precision=precise)
    ada_left = jnp.einsum("cr,jce->jre", cond_row_wide, mod_side, precision=precise)
    cond_side = jnp.einsum("cb,bje->jce", cond_gram, mod_grad_cols, precision=precise)
    ada_right = jnp.einsum("cjr,jce->jre", mod_grad_rows, cond_side, precision=precise)

    right_parts = lax.all_gather(packed([right_parts], 8), "dp", axis=0, tiled=True)
    mod_right = jnp.sum(right_parts.reshape(dp_count, -1), axis=0)[: mod_grad_cols.size]
    mod_right = mod_right.reshape(all_clips, mod_count, col_part)
    ada_pre = jnp.einsum("jrc,cje->jre", left_cond, mod_right, precision=precise)
    whole_attn, back_one = tie(whole_attn, back_one)
    back_attn = shard_rows(owned_step(whole_attn, root_rows, right_wholes, 0, group), group)

    def joined(at, ada):
        return jnp.concatenate([ada, wide(back_attn[at]), wide(back_one[at]), wide(back_two[at])])

    precond = joined(0, ada_pre)
    left_new = stat_decay * left_stats + (1.0 - stat_decay) * joined(1, ada_left)
    right_new = stat_decay * right_stats + (1.0 - stat_decay) * joined(2, ada_right)
    momentum_new = moment_decay * momentum + precond
    weights_new = weights - weight_rate * momentum_new
    weights_copy = weights_new.astype(jnp.bfloat16)
    bias_second_new = stat_decay * bias_second + (1.0 - stat_decay) * bias_grad * bias_grad
    bias_moment_new = moment_decay * bias_moment + bias_grad * lax.rsqrt(
        bias_second_new + diag_epsilon
    )
    biases_new = biases - bias_rate * bias_moment_new
    return (
        block_out.reshape(tokens.shape),
        input_grad.reshape(tokens.shape),
        left_new,
        right_new,
        momentum_new,
        weights_new,
        weights_copy,
        bias_moment_new,
        bias_second_new,
        biases_new,
    )


def solution(mesh):
    placed = (
        P("dp", "fsdp", None, None),
        P("dp", None),
        P("dp"),
        P("dp", "fsdp", None, None),
        P(None, "dp", "fsdp"),
        P(("dp", "fsdp")),
        P(None, "dp", "fsdp"),
        P(None, "dp", "fsdp"),
        P(None, "dp", "fsdp"),
        P(None, "dp", "fsdp"),
        P(None, "dp", "fsdp"),
        P(("dp", "fsdp")),
        P(("dp", "fsdp")),
    )
    return jax.shard_map(
        per_device,
        mesh=mesh,
        in_specs=placed,
        out_specs=(
            P("dp", "fsdp", None, None),
            P("dp", "fsdp", None, None),
            P(None, "dp", "fsdp"),
            P(None, "dp", "fsdp"),
            P(None, "dp", "fsdp"),
            P(None, "dp", "fsdp"),
            P(None, "dp", "fsdp"),
            P(("dp", "fsdp")),
            P(("dp", "fsdp")),
            P(("dp", "fsdp")),
        ),
        check_vma=False,
    )
```
